32 devices in a mesh: dp: 4 (over y, x), wide: 8 (over z, core).
Axes of the slice: x: 2, y: 2, z: 4, core: 2. Of those that a mesh axis runs over, the one named last changes fastest.
Arguments:
- tokens: bfloat16 [8192, 768], P(('dp', 'wide'))
- cluster_ids: int32 [8192, 12], P(('dp', 'wide')), may hold values from 0 to 127, as said below
- lengths: int32 [4], P('dp'), may hold values from 1793 to 2048, as said below
- top_keys: int32 [4, 12, 128, 32], P('dp', None, 'wide'), may hold values from 0 to 2047, as said below
- gain_one: float32 [768], replicated, may hold values from 0.25 to 1.75
- shift_one: float32 [768], replicated, may hold values from -1.8 to 1.8
- w_query: bfloat16 [768, 768], replicated, may hold values from -0.625 to 0.625
- w_keyval: bfloat16 [768, 1536], replicated, may hold values from -0.21875 to 0.21875
- w_out: bfloat16 [768, 768], replicated, may hold values from -6 to 6
- gain_two: float32 [768], replicated, may hold values from 0.25 to 1.75
- shift_two: float32 [768], replicated, may hold values from -1.8 to 1.8
- w_up: bfloat16 [768, 3072], replicated, may hold values from -0.21875 to 0.21875
- w_down: bfloat16 [3072, 768], replicated, may hold values from -0.109375 to 0.109375
- cotangent: bfloat16 [8192, 768], P(('dp', 'wide')), may hold values from -6 to 6
Outputs:
- output: bfloat16 [8192, 768], P(('dp', 'wide'))
- grad_tokens: bfloat16 [8192, 768], P(('dp', 'wide'))
- grad_query: float32 [768, 768], P('wide')
- grad_keyval: float32 [768, 1536], P('wide')
- grad_out: float32 [768, 768], P('wide')
- grad_up: float32 [768, 3072], P('wide')
- grad_down: float32 [3072, 768], P('wide')
- grad_gain_one: float32 [768], P('wide')
- grad_shift_one: float32 [768], P('wide')
- grad_gain_two: float32 [768], P('wide')
- grad_shift_two: float32 [768], P('wide')
The draws below stay inside these ranges and needn't reach their ends.
Inputs may be any that keep to these rules, and one draw needn't show every extreme that they name: `cluster_ids`: within each aligned block of 256 rows (the rows of one device) and each head, at most 4 rows name the same cluster; in each head one cluster is named by exactly 4 rows of every block. `lengths`: one sequence has the full length 2048. `top_keys`: the 32 positions of a cluster are distinct and below its sequence's length.
All inputs are finite; a program needn't handle non-finite values.
Results may differ from the reference program's by a relative error of at most 0.015.
Values may be sent and summed in bfloat16 or wider, within the bound.
No kernel may reach another device: no remote copies, remote signals or barrier semaphores. Data moves between devices by JAX's collectives and lax.ppermute only.
A program may use at most 640 MiB of HBM per device.

```python
from functools import partial
import jax
import jax.numpy as jnp
from jax import lax

D = 768
H = 12
HD = 64
FF = 3072
CL = 128
TOPK = 32
TOK_DEV = 256
CAP = 4
SEQ = 2048
TOKENS = 8192
N_DP = 4


def cluster_table(key):
    key = jax.random.fold_in(key, 101)
    rank_key, noise_key, order_key = jax.random.split(key, 3)
    blocks = TOKENS // TOK_DEV
    ranks = jnp.argsort(jax.random.randint(rank_key, (H, CL), 0, 2 ** 20) * CL + jnp.arange(CL)[None, :], axis=1)
    places = jnp.arange(CL * CAP)
    place_rank = ranks[:, places // CAP]
    noise = jax.random.randint(noise_key, (blocks, H, CL * CAP), 0, 65536)
    scores = jnp.where(place_rank[None] == 0, -1, noise + place_rank[None] * 256)
    chosen = jnp.argsort(scores * (CL * CAP) + places[None, None, :], axis=-1)[:, :, :TOK_DEV]
    order = jnp.argsort(jax.random.randint(order_key, (blocks, H, TOK_DEV), 0, 2 ** 20) * TOK_DEV + jnp.arange(TOK_DEV)[None, None, :], axis=-1)
    chosen = jnp.take_along_axis(chosen, order, axis=-1)
    return (chosen // CAP).transpose(0, 2, 1).reshape(TOKENS, H).astype(jnp.int32)


def length_table(key):
    key = jax.random.fold_in(key, 202)
    pad_key, full_key = jax.random.split(key)
    pads = jax.random.randint(pad_key, (N_DP,), 0, TOK_DEV)
    longest = jax.random.randint(full_key, (), 0, N_DP)
    pads = jnp.where(jnp.arange(N_DP) == longest, 0, pads)
    return (SEQ - pads).astype(jnp.int32)


def draw_cluster_ids(key, part):
    return cluster_table(key)


def draw_lengths(key, part):
    return length_table(key)


def draw_top_keys(key, part):
    sizes = length_table(key)
    key = jax.random.fold_in(key, 303)
    pick_key, window_key, start_key, phase_key, order_key = jax.random.split(key, 5)
    shape = (N_DP, H, CL, TOPK)
    total = sizes[:, None, None, None]
    span = 4 * TOK_DEV
    spread_pick = jax.random.randint(pick_key, shape, 0, 2 ** 30) % (total - TOPK + 1)
    window_pick = jax.random.randint(window_key, shape, 0, span - TOPK + 1)
    start = jax.random.randint(start_key, (N_DP, H, CL, 1), 0, 2 ** 30) % (total - span + 1)
    phase = jax.random.randint(phase_key, (N_DP, H, 1, 1), 0, 8)
    gathered = (jnp.arange(CL)[None, None, :, None] + phase) % 8 == 0
    picks = jnp.where(gathered, window_pick, spread_pick)
    base = jnp.where(gathered, start, 0)
    positions = base + jnp.sort(picks, axis=-1) + jnp.arange(TOPK)[None, None, None, :]
    order = jnp.argsort(jax.random.randint(order_key, shape, 0, 2 ** 20) * TOPK + jnp.arange(TOPK)[None, None, None, :], axis=-1)
    return jnp.take_along_axis(positions, order, axis=-1).astype(jnp.int32)


def draw_tokens(key, part):
    clusters = cluster_table(key)
    key = jax.random.fold_in(key, 404)
    center_key, noise_key = jax.random.split(key, 2)
    centers = jax.random.normal(center_key, (H, CL, D), jnp.float32) * 0.4
    noise = jax.random.normal(noise_key, (TOKENS, D), jnp.float32)
    values = noise
    for head_index in range(H):
        values = values + centers[head_index][clusters[:, head_index]]
    return values.astype(jnp.bfloat16)


def levels(own_key, shape, shards, low, largest):
    factor_of = 1.0
    for axis_at, blocks in shards:
        steps = jax.random.uniform(jax.random.fold_in(jax.random.fold_in(own_key, 6), axis_at), (blocks,), jnp.float32, low / len(shards), largest / len(shards))
        factor_of = factor_of * jnp.repeat(jnp.exp(steps), shape[axis_at] // blocks).reshape((-1,) + (1,) * (len(shape) - 1 - axis_at))
    return factor_of


def gaussian(own_key, dims, deviation, most, cuts=(), dtype=jnp.bfloat16):
    drawn = deviation * jax.random.normal(own_key, dims, jnp.float32)
    if cuts:
        drawn = drawn * levels(own_key, dims, cuts, -0.22, 0.18)
    return jnp.clip(drawn, -most, most).astype(dtype)


def setup_inputs(seed: int = 0) -> dict:
    key_list = jax.random.split(jax.random.key(seed), 15)
    tokens = draw_tokens(jax.random.fold_in(key_list[14], 71), 0)
    cluster_ids = draw_cluster_ids(jax.random.fold_in(key_list[14], 71), 0)
    lengths = draw_lengths(jax.random.fold_in(key_list[14], 71), 0)
    top_keys = draw_top_keys(jax.random.fold_in(key_list[14], 71), 0)
    gain_one = jnp.clip(1.0 + 0.15 * jax.random.normal(key_list[4], (D,), jnp.float32), 0.25, 1.75)
    shift_one = gaussian(key_list[5], (D,), 0.3, 1.8, (), jnp.float32)
    w_query = gaussian(key_list[6], (D, D), (D // 8) ** -0.5, 0.625)
    w_keyval = gaussian(key_list[7], (D, 2 * D), D ** -0.5, 0.21875)
    w_out = gaussian(key_list[8], (D, D), 1 ** -0.5, 6.0)
    gain_two = jnp.clip(1.0 + 0.15 * jax.random.normal(key_list[9], (D,), jnp.float32), 0.25, 1.75)
    shift_two = gaussian(key_list[10], (D,), 0.3, 1.8, (), jnp.float32)
    w_up = gaussian(key_list[11], (D, FF), D ** -0.5, 0.21875)
    w_down = gaussian(key_list[12], (FF, D), FF ** -0.5, 0.109375)
    cotangent = gaussian(key_list[13], (TOKENS, D), 1.0, 6.0, ((0, 32),))
    return {"tokens": tokens, "cluster_ids": cluster_ids, "lengths": lengths, "top_keys": top_keys, "gain_one": gain_one, "shift_one": shift_one, "w_query": w_query, "w_keyval": w_keyval, "w_out": w_out, "gain_two": gain_two, "shift_two": shift_two, "w_up": w_up, "w_down": w_down, "cotangent": cotangent}


@jax.custom_vjp
def low(v):
    return lax.optimization_barrier(v.astype(jnp.bfloat16)).astype(jnp.float32)

@jax.custom_vjp
def low_back(v):
    return v

def low_keep(v):
    return (low(v), None)

def low_pass(kept, grad):
    return (grad,)

def back_keep(v):
    return (v, None)

def back_low(kept, grad):
    return (low(grad),)
low.defvjp(low_keep, low_pass)
low_back.defvjp(back_keep, back_low)
EPSILON = 1e-05
NEGATIVE = -1e+30
HIGHEST = lax.Precision.HIGHEST

def matmul(left, right):
    return jnp.dot(left, right, precision=HIGHEST)

def normalize(values, gain, shift):
    centered = values - lax.optimization_barrier(jnp.mean(values, axis=-1, keepdims=True))
    variance = lax.optimization_barrier(jnp.mean(centered * centered, axis=-1, keepdims=True))
    return centered * lax.rsqrt(variance + EPSILON) * gain + shift

def forward(token_f, gain_one, shift_one, w_query, w_keyval, w_out, gain_two, shift_two, w_up, w_down, cluster=None, chosen=None, length=None):
    normed_one = low(normalize(token_f, gain_one, shift_one))
    queries = low(low_back(matmul(normed_one, w_query)))
    keyvals = low(low_back(matmul(normed_one, w_keyval)))
    query_h = queries.reshape(SEQ, H, HD)
    keys_h = keyvals[:, :D].reshape(SEQ, H, HD)
    values_h = keyvals[:, D:].reshape(SEQ, H, HD)
    validity = (jnp.arange(SEQ) < length).astype(jnp.float32)
    segment = (jnp.arange(H)[None, :] * CL + cluster).reshape(-1)
    sums = jax.ops.segment_sum((query_h * validity[:, None, None]).reshape(SEQ * H, HD), segment, H * CL).reshape(H, CL, HD)
    counts = jax.ops.segment_sum(jnp.broadcast_to(validity[:, None], (SEQ, H)).reshape(-1), segment, H * CL).reshape(H, CL)
    centroid = low(sums / jnp.maximum(counts, 1.0)[:, :, None])
    scores = low_back(jnp.einsum('hcd,shd->hcs', centroid, keys_h, precision=HIGHEST) * 0.125)
    masked = jnp.where(validity[None, None, :] > 0, scores, NEGATIVE)
    peak = lax.optimization_barrier(jnp.max(masked, axis=-1, keepdims=True))
    expo = jnp.exp(masked - peak)
    probs = expo / lax.optimization_barrier(jnp.sum(expo, axis=-1, keepdims=True))
    probs_low = low(probs)
    full = jnp.einsum('hcs,shd->hcd', probs_low, values_h, precision=HIGHEST)
    head_range = jnp.arange(H)[:, None, None]
    top_k = keys_h[chosen, head_range]
    top_v = values_h[chosen, head_range]
    top_mass = lax.optimization_barrier(jnp.sum(jnp.take_along_axis(probs, chosen, axis=2), axis=-1))
    top_low = jnp.take_along_axis(probs_low, chosen, axis=2)
    rest = low_back(full - jnp.einsum('hct,hctd->hcd', top_low, top_v, precision=HIGHEST))
    head_row = jnp.arange(H)[None, :]
    block = 512 if SEQ % 512 == 0 else SEQ

    def member_block(pieces):
        query_b, cluster_b, valid_b = pieces
        keys_b = top_k[head_row, cluster_b]
        values_b = top_v[head_row, cluster_b]
        member = low_back(jnp.einsum('bhd,bhtd->bht', query_b, keys_b, precision=HIGHEST) * 0.125)
        weights = jax.nn.softmax(member, axis=-1)
        mixed = low_back(jnp.einsum('bht,bhtd->bhd', low(weights), values_b, precision=HIGHEST))
        result = valid_b[:, None, None] * (top_mass[head_row, cluster_b][:, :, None] * mixed + rest[head_row, cluster_b])
        return low(low_back(result)).reshape(query_b.shape[0], D)
    blocks = SEQ // block
    attn = lax.map(jax.checkpoint(member_block), (query_h.reshape(blocks, block, H, HD), cluster.reshape(blocks, block, H), validity.reshape(blocks, block))).reshape(SEQ, D)
    resid = token_f + low_back(matmul(attn, w_out))
    normed_two = low(normalize(resid, gain_two, shift_two))
    up_pre = low_back(matmul(normed_two, w_up))
    act = low(jax.nn.gelu(up_pre, approximate=True))
    return resid + matmul(act, w_down)

def reference(tokens, cluster_ids, lengths, top_keys, gain_one, shift_one, w_query, w_keyval, w_out, gain_two, shift_two, w_up, w_down, cotangent):
    weights = tuple((item.astype(jnp.float32) for item in (gain_one, shift_one, w_query, w_keyval, w_out, gain_two, shift_two, w_up, w_down)))
    outputs = []
    grad_rows = []
    totals = tuple((jnp.zeros(item.shape, jnp.float32) for item in weights))
    for seq_index in range(N_DP):
        start = seq_index * SEQ
        token_f = tokens[start:start + SEQ].astype(jnp.float32)
        passes = partial(forward, cluster=cluster_ids[start:start + SEQ], chosen=top_keys[seq_index], length=lengths[seq_index])
        result, backward = jax.vjp(passes, token_f, *weights)
        grads = backward(cotangent[start:start + SEQ].astype(jnp.float32))
        outputs.append(result.astype(jnp.bfloat16))
        grad_rows.append(grads[0].astype(jnp.bfloat16))
        totals = tuple((total + grad for total, grad in zip(totals, grads[1:])))
    output = jnp.concatenate(outputs, axis=0)
    grad_tokens = jnp.concatenate(grad_rows, axis=0)
    return (output, grad_tokens, totals[2], totals[3], totals[4], totals[7], totals[8], totals[0], totals[1], totals[5], totals[6])
```

```python
import functools
import math

import jax
import jax.numpy as jnp
import numpy as np
from jax import lax
from jax.experimental import pallas as pl
from jax.experimental.pallas import tpu as pltpu
from jax.sharding import PartitionSpec as P

EPSILON = 1e-05
NEGATIVE = -1e30
EXCLUDED = -3e30
GELU_A = math.sqrt(2.0 / math.pi)
GELU_B = 0.044715
BF = jnp.bfloat16
F32 = jnp.float32


def nn(left, right):
    return lax.dot_general(left, right, (((1,), (0,)), ((), ())), preferred_element_type=F32)


def nt(left, right):
    return lax.dot_general(left, right, (((1,), (1,)), ((), ())), preferred_element_type=F32)


def tn(left, right):
    return lax.dot_general(left, right, (((0,), (0,)), ((), ())), preferred_element_type=F32)


def params(mib, dims):
    return pltpu.CompilerParams(
        vmem_limit_bytes=mib * 1024 * 1024, dimension_semantics=("arbitrary",) * dims
    )


def cost(flops, nbytes, trans=0):
    return pl.CostEstimate(flops=int(flops), bytes_accessed=int(nbytes), transcendentals=int(trans))


def split_low(values):
    high = values.astype(BF)
    return high, (values - high.astype(F32)).astype(BF)


def one_hot_t(ids_row, clusters):
    rows = lax.broadcasted_iota(jnp.int32, (clusters, ids_row.shape[1]), 0)
    return jnp.where(rows == ids_row, 1.0, 0.0).astype(BF)


def key_passes(total, size, score, weigh):
    if total == size:
        first = score(0)
        peak = jnp.max(first, axis=0, keepdims=True)
        expo = jnp.exp(first - peak)
        return peak, jnp.sum(expo, axis=0, keepdims=True), weigh(0, expo)

    def step(index, carry):
        peak, denom, sums = carry
        block = score(index)
        fresh = jnp.maximum(peak, jnp.max(block, axis=0, keepdims=True))
        expo = jnp.exp(block - fresh)
        fade = jnp.exp(peak - fresh)
        parts = weigh(index, expo)
        return (
            fresh,
            denom * fade + jnp.sum(expo, axis=0, keepdims=True),
            tuple(old * fade + new for old, new in zip(sums, parts)),
        )

    shapes = jax.eval_shape(lambda: (score(0), weigh(0, score(0))))
    lanes = shapes[0].shape[1]
    start = (
        jnp.full((1, lanes), NEGATIVE, F32),
        jnp.zeros((1, lanes), F32),
        tuple(jnp.zeros(item.shape, F32) for item in shapes[1]),
    )
    return lax.fori_loop(0, total // size, step, start)


def piece(ref, index, size, axis):
    if ref.shape[axis] == size:
        return ref[...]
    start = pl.multiple_of(index * size, size)
    if axis == 0:
        return ref[pl.ds(start, size), :]
    return ref[:, pl.ds(start, size)]


def bias_kernel(info, top_ref, bias_ref, *, groups, peers, rows):
    part = pl.program_id(0)
    owner = (
        lax.rem(info[0] + part // peers, groups) * peers + lax.rem(info[1] + part % peers, peers)
    )
    heads, picks, clusters = top_ref.shape
    place = owner * rows + lax.broadcasted_iota(jnp.int32, (rows, clusters), 0)
    outside = place >= info[2]
    for head in range(heads):
        top = top_ref[head]
        chosen = place == top[0:1, :]
        for pick in range(1, picks):
            chosen = chosen | (place == top[pick : pick + 1, :])
        value = jnp.where(chosen, 0.0, jnp.where(outside, EXCLUDED, NEGATIVE))
        bias_ref[head] = value.astype(BF)


def project_kernel(
    info, x_ref, gain_ref, shift_ref, wq_ref, wkv_ref, low_ref, qt_ref, kvt_ref, kv_ref, *, peers
):
    values = x_ref[...].astype(F32)
    centered = values - jnp.mean(values, axis=-1, keepdims=True)
    variance = jnp.mean(centered * centered, axis=-1, keepdims=True)
    normed = centered * lax.rsqrt(variance + EPSILON) * gain_ref[...] + shift_ref[...]
    low = normed.astype(BF)

    @pl.when(pl.program_id(1) == 0)
    def keep():
        low_ref[...] = low

    qt_ref[...] = (nt(wq_ref[0], low) * 0.125).astype(BF)
    pairs = nt(wkv_ref[0], low).astype(BF)
    kvt_ref[...] = pairs
    width = kv_ref.shape[2]
    for head in range(kv_ref.shape[0]):
        kv_ref[head] = pairs[head * width : (head + 1) * width].T


def forward_kernel(
    ids_all, ids_own, qt_all, qt_own, kvt, kv, bias, out, mix_ref, stat_ref, cen_ref, table, *, size
):
    hs = qt_own.shape[0]
    keys = kv.shape[1]
    clusters = bias.shape[2]
    kv_h, bias_h = kv.at[0], bias.at[0]

    @pl.when(pl.program_id(1) == 0)
    def centroid_stage():
        hot = one_hot_t(ids_all[0], clusters)
        ones = jnp.ones((16, keys), BF)
        sums = nt(jnp.concatenate([qt_all[...], ones], axis=0), hot)
        counts = sums[hs : hs + 1]
        centroid = (sums[:hs] / jnp.maximum(counts, 1.0)).astype(BF)
        padded = jnp.concatenate([centroid, jnp.zeros_like(centroid)], axis=0)

        def score(index):
            scores = nn(piece(kv_h, index, size, 0), padded)
            outside = piece(bias_h, index, size, 0).astype(F32) < 2.0 * NEGATIVE
            return jnp.where(outside, NEGATIVE, scores)

        def weigh(index, expo):
            top = piece(bias_h, index, size, 0).astype(F32) == 0.0
            mass = jnp.sum(jnp.where(top, expo, 0.0), axis=0, keepdims=True)
            other = jnp.where(top, 0.0, expo).astype(BF)
            return nn(piece(kvt, index, size, 1), other), mass

        peak, denom, (rest, mass) = key_passes(keys, size, score, weigh)
        rest = rest[hs:] / denom
        mass = mass / denom
        stats = jnp.concatenate(
            [
                rest,
                mass,
                peak + jnp.log(denom),
                counts,
                jnp.zeros((5, clusters), F32),
            ],
            axis=0,
        )
        stat_ref[0] = stats
        cen_ref[0] = centroid
        high, low = split_low(stats)
        table[...] = jnp.concatenate([high, low], axis=1)

    hot = one_hot_t(ids_own[0], clusters)
    queries = qt_own[...]
    side = jnp.concatenate([queries, jnp.zeros_like(queries), hot], axis=0)
    gathered = nn(table[...], jnp.concatenate([hot, hot], axis=0))

    def score(index):
        return nn(
            jnp.concatenate([piece(kv_h, index, size, 0), piece(bias_h, index, size, 0)], axis=1),
            side,
        )

    def weigh(index, expo):
        return (nn(piece(kvt, index, size, 1), expo.astype(BF)),)

    peak, denom, (mix,) = key_passes(keys, size, score, weigh)
    mix = mix[hs:] / denom
    out[0] = (gathered[hs : hs + 1] * mix + gathered[:hs]).astype(BF)
    mix_ref[0, 0] = jnp.concatenate(
        [mix, jnp.broadcast_to(peak + jnp.log(denom), (8, mix.shape[1]))], axis=0
    )


def sums_kernel(ids_own, grad, mix_ref, part_ref):
    hs = grad.shape[1]
    hot = one_hot_t(ids_own[0], part_ref.shape[2])
    rows = grad[0]
    along = jnp.sum(rows.astype(F32) * mix_ref[0, 0, :hs], axis=0, keepdims=True)
    high, low = split_low(along)
    pad = jnp.zeros((14, rows.shape[1]), BF)
    part = nt(jnp.concatenate([rows, high, low, pad], axis=0), hot)

    @pl.when(pl.program_id(1) == 0)
    def first():
        part_ref[0] = part

    @pl.when(pl.program_id(1) > 0)
    def later():
        part_ref[0] += part


def member_kernel(
    ids_own, qt_own, kvt, kv, bias, grad, mix_ref, stat_ref, dq_ref, own_ref, send_ref, total, *, size
):
    hs = qt_own.shape[0]
    keys = kv.shape[1]
    rows = grad.shape[2]
    clusters = bias.shape[2]
    block = pl.program_id(1)
    kv_h, bias_h = kv.at[0], bias.at[0]
    hot = one_hot_t(ids_own[0], clusters)
    queries = qt_own[...]
    blank = jnp.zeros_like(queries)
    side = jnp.concatenate([queries, blank, hot], axis=0)
    high, low = split_low(stat_ref[0, hs : hs + 8, :])
    mass = nn(jnp.concatenate([high, low], axis=1), jnp.concatenate([hot, hot], axis=0))[0:1]
    mix = mix_ref[0, 0, :hs]
    level = mix_ref[0, 0, hs : hs + 1]
    back = (mass * grad[0].astype(F32)).astype(BF)
    delta = jnp.sum(back.astype(F32) * mix, axis=0, keepdims=True)
    back_pad = jnp.concatenate([blank, back], axis=0)
    right = jnp.concatenate([jnp.concatenate([queries, blank], axis=0), back_pad], axis=1).T

    def step(index, dq):
        kv_c = piece(kv_h, index, size, 0)
        scores = nn(jnp.concatenate([kv_c, piece(bias_h, index, size, 0)], axis=1), side)
        weights = jnp.exp(scores - level)
        grad_w = nn(kv_c, back_pad)
        grad_s = (weights * (grad_w - delta)).astype(BF)
        both = nn(jnp.concatenate([grad_s, weights.astype(BF)], axis=1), right)
        spot = pl.ds(pl.multiple_of(index * size, size), size)

        @pl.when(block == 0)
        def first():
            total[spot, :] = both

        @pl.when(block > 0)
        def later():
            total[spot, :] += both

        return dq + nn(piece(kvt, index, size, 1), grad_s)

    dq = jnp.zeros((2 * hs, rows), F32)
    if keys == size:
        dq = step(0, dq)
    else:
        dq = lax.fori_loop(0, keys // size, step, dq)
    dq_ref[0] = dq[:hs] * 0.125

    @pl.when(block == pl.num_programs(1) - 1)
    def finish():
        blocks = pl.num_programs(1)
        groups = own_ref.shape[1] // rows
        peers = keys // own_ref.shape[1]
        for group in range(groups):
            base = group * peers * rows
            own_ref[0, group * rows : (group + 1) * rows, :] = total[base : base + rows, :]
            for peer in range(1, peers):
                spot = (peer - 1) * groups * rows + group * rows
                send_ref[0, spot : spot + rows, :] = total[
                    base + peer * rows : base + (peer + 1) * rows, :
                ].astype(BF)


def centroid_kernel(
    ids_own, kvt, kv, bias, part_ref, stat_ref, cen_ref, dqm_ref, own_ref, got_ref, dq_ref, dkv_ref, both, *, size
):
    hs = dq_ref.shape[1]
    keys = kv.shape[1]
    rows = dq_ref.shape[2]
    groups = dq_ref.shape[0]
    peers = keys // (groups * rows)
    clusters = bias.shape[2]
    kv_h, bias_h = kv.at[0], bias.at[0]
    stats = stat_ref[0]
    rest, mass = stats[:hs], stats[hs : hs + 1]
    level, counts = stats[hs + 1 : hs + 2], stats[hs + 2 : hs + 3]
    centroid = cen_ref[0]
    blank = jnp.zeros_like(centroid)
    part = part_ref[0]
    d_rest = part[:hs].astype(BF)
    d_mass = part[hs : hs + 1] + part[hs + 1 : hs + 2]
    delta = jnp.sum(d_rest.astype(F32) * rest, axis=0, keepdims=True) + d_mass * mass
    cen_pad = jnp.concatenate([centroid, blank], axis=0)
    rest_pad = jnp.concatenate([blank, d_rest], axis=0)
    right = jnp.concatenate([cen_pad, rest_pad], axis=1).T

    def step(index, total):
        kv_c = piece(kv_h, index, size, 0)
        marks = piece(bias_h, index, size, 0).astype(F32)
        scores = nn(kv_c, cen_pad)
        probs = jnp.where(marks < 2.0 * NEGATIVE, 0.0, jnp.exp(scores - level))
        top = marks == 0.0
        d_probs = jnp.where(top, d_mass, nn(kv_c, rest_pad))
        d_score = (probs * (d_probs - delta)).astype(BF)
        other = jnp.where(top, 0.0, probs).astype(BF)
        spot = pl.ds(pl.multiple_of(index * size, size), size)
        both[spot, :] = jnp.concatenate([d_score, other], axis=1)
        return total + nn(piece(kvt, index, size, 1), d_score)

    d_cen = jnp.zeros((2 * hs, clusters), F32)
    if keys == size:
        d_cen = step(0, d_cen)
    else:
        d_cen = lax.fori_loop(0, keys // size, step, d_cen)
    d_cen = d_cen[:hs] * 0.125 / jnp.maximum(counts, 1.0)
    high, low = split_low(d_cen)
    table = jnp.concatenate([high, low], axis=1)
    for group in range(groups):
        spot = group * peers * rows
        hot = one_hot_t(ids_own[0, :, spot : spot + rows], clusters)
        spread = nn(table, jnp.concatenate([hot, hot], axis=0))
        dq_ref[group] = (dqm_ref[group] + spread).astype(BF)
        own = nn(both[spot : spot + rows, :], right) + own_ref[0, group * rows : (group + 1) * rows, :]
        for peer in range(1, peers):
            at = (peer - 1) * groups * rows + group * rows
            own = own + got_ref[0, at : at + rows, :].astype(F32)
        dkv_ref[group] = own.astype(BF)


def block_kernel(info, *refs, groups, chunks):
    (attn, rest) = (refs[:groups], refs[groups:])
    x_ref, gain_ref, shift_ref, wo_ref, up_ref, down_ref, cot_ref = rest[:7]
    resid_ref, low_ref, act_ref, dup_ref, dres_ref, dbr_ref, dn_ref = rest[7:14]
    dat = rest[14 : 14 + groups]
    hat_ref, inv_ref, back = rest[14 + groups :]
    index = pl.program_id(0)

    @pl.when(index == 0)
    def before():
        resid = x_ref[...].astype(F32)
        for group in range(groups):
            owner = lax.rem(info[0] + groups - group, groups)
            resid = resid + tn(attn[group][...], wo_ref[owner])
        resid_ref[...] = resid
        centered = resid - jnp.mean(resid, axis=-1, keepdims=True)
        variance = jnp.mean(centered * centered, axis=-1, keepdims=True)
        inverse = lax.rsqrt(variance + EPSILON)
        hat = centered * inverse
        hat_ref[...] = hat
        inv_ref[...] = jnp.broadcast_to(inverse, inv_ref.shape)
        low_ref[...] = (hat * gain_ref[...] + shift_ref[...]).astype(BF)
        back[...] = jnp.zeros_like(back)

    up = nn(low_ref[...], up_ref[...])
    grad_act = nt(cot_ref[...], down_ref[...])
    square = up * up
    inner = GELU_A * (up + GELU_B * up * square)
    curve = jnp.tanh(inner)
    act_ref[...] = (0.5 * up * (1.0 + curve)).astype(BF)
    slope = 0.5 * (1.0 + curve) + 0.5 * up * (1.0 - curve * curve) * (
        GELU_A * (1.0 + 3.0 * GELU_B * square)
    )
    d_up = (grad_act * slope).astype(BF)
    dup_ref[...] = d_up
    back[...] += nt(d_up, up_ref[...])

    @pl.when(index == chunks - 1)
    def after():
        d_normed = back[...]
        hat = hat_ref[...]
        gain_part = jnp.sum(d_normed * hat, axis=0, keepdims=True)
        shift_part = jnp.sum(d_normed, axis=0, keepdims=True)
        dn_ref[...] = jnp.concatenate([gain_part, shift_part], axis=0)
        gy = d_normed * gain_ref[...]
        mean_one = jnp.mean(gy, axis=-1, keepdims=True)
        mean_two = jnp.mean(gy * hat, axis=-1, keepdims=True)
        d_resid = cot_ref[...].astype(F32) + inv_ref[:, 0:1] * (gy - mean_one - hat * mean_two)
        dres_ref[...] = d_resid
        branch = d_resid.astype(BF)
        dbr_ref[...] = branch
        for group in range(groups):
            owner = lax.rem(info[0] + groups - group, groups)
            dat[group][...] = nt(wo_ref[owner], branch).astype(BF)


def weights_kernel(resid_ref, low_ref, act_ref, dup_ref, down_ref, cot_ref, out_ref, gup_ref, gdown_ref, total, *, chunks):
    index = pl.program_id(0)

    @pl.when(index == 0)
    def first():
        total[...] = resid_ref[...]

    total[...] += nn(act_ref[...], down_ref[...])
    gup_ref[...] = tn(low_ref[...], dup_ref[...]).astype(BF)
    gdown_ref[...] = tn(act_ref[...], cot_ref[...]).astype(BF)

    @pl.when(index == chunks - 1)
    def last():
        out_ref[...] = total[...].astype(BF)


def final_kernel(info, *refs, groups):
    dqs, dkvs = refs[:groups], refs[groups : 2 * groups]
    x_ref, dres_ref, gain_ref, wq_ref, wkv_ref, out_ref = refs[2 * groups :]
    d_normed = jnp.zeros(dres_ref.shape, F32)
    for group in range(groups):
        owner = lax.rem(info[0] + groups - group, groups)
        d_normed = d_normed + tn(dqs[group][...], wq_ref[owner]) + nn(dkvs[group][...], wkv_ref[owner])
    values = x_ref[...].astype(F32)
    centered = values - jnp.mean(values, axis=-1, keepdims=True)
    variance = jnp.mean(centered * centered, axis=-1, keepdims=True)
    inverse = lax.rsqrt(variance + EPSILON)
    hat = centered * inverse
    gy = d_normed * gain_ref[...]
    mean_one = jnp.mean(gy, axis=-1, keepdims=True)
    mean_two = jnp.mean(gy * hat, axis=-1, keepdims=True)
    out_ref[...] = (dres_ref[...] + inverse * (gy - mean_one - hat * mean_two)).astype(BF)


def whole(shape):
    return pl.BlockSpec(shape, lambda *at: (0,) * len(shape))


def per_device(
    tokens,
    cluster_ids,
    lengths,
    top_keys,
    gain_one,
    shift_one,
    w_query,
    w_keyval,
    w_out,
    gain_two,
    shift_two,
    w_up,
    w_down,
    cotangent,
):
    rows, width = tokens.shape
    heads = cluster_ids.shape[1]
    hs = width // heads
    hidden = w_up.shape[1]
    wide = lax.axis_size("wide")
    n_dp = lax.axis_size("dp")
    groups = math.gcd(heads, wide)
    peers = wide // groups
    own_heads = heads // groups
    clusters = top_keys.shape[2] * wide
    picks = top_keys.shape[3]
    seq = rows * wide
    size = min(seq, 2048)
    feats = own_heads * hs
    me = lax.axis_index("wide")
    group_at, peer_at = me // peers, me % peers
    dp_at = lax.axis_index("dp")
    seq_len = lengths[0]
    info = jnp.stack([group_at, peer_at, seq_len]).astype(jnp.int32)

    def along_groups(values, hop):
        pairs = [
            (i, ((i // peers + hop) % groups) * peers + i % peers) for i in range(wide)
        ]
        return lax.ppermute(values, "wide", pairs)

    def along_peers(values, hop):
        pairs = [(i, (i // peers) * peers + (i % peers + hop) % peers) for i in range(wide)]
        return lax.ppermute(values, "wide", pairs)

    mine = [tokens] + [along_groups(tokens, -hop) for hop in range(1, groups)]
    blocks = []
    for item in mine:
        blocks.append(item)
        blocks += [along_peers(item, -hop) for hop in range(1, peers)]
    tokens_all = jnp.concatenate(blocks, axis=0)

    position = me * rows + jnp.arange(rows, dtype=jnp.int32)
    marked = jnp.where((position < seq_len)[:, None], cluster_ids, -1)
    packed = jnp.concatenate([marked.T.reshape(-1), top_keys[0].reshape(-1)])
    gathered = lax.all_gather(packed, "wide", axis=0, tiled=False)
    ids_all = gathered[:, : heads * rows].reshape(groups, peers, heads, rows)
    ids_all = lax.dynamic_slice_in_dim(ids_all, group_at * own_heads, own_heads, axis=2)
    ids_all = lax.dynamic_slice_in_dim(
        jnp.concatenate([ids_all, ids_all], axis=0), group_at, groups, axis=0
    )
    ids_all = lax.dynamic_slice_in_dim(
        jnp.concatenate([ids_all, ids_all], axis=1), peer_at, peers, axis=1
    )
    ids_all = ids_all.transpose(2, 0, 1, 3).reshape(own_heads, 1, seq)
    top_all = gathered[:, heads * rows :].reshape(wide, heads, clusters // wide, picks)
    top_all = lax.dynamic_slice_in_dim(top_all, group_at * own_heads, own_heads, axis=1)
    top_all = top_all.transpose(1, 3, 0, 2).reshape(own_heads, picks, clusters)

    bias = pl.pallas_call(
        functools.partial(bias_kernel, groups=groups, peers=peers, rows=rows),
        grid_spec=pltpu.PrefetchScalarGridSpec(
            num_scalar_prefetch=1,
            grid=(wide,),
            in_specs=[whole((own_heads, picks, clusters))],
            out_specs=pl.BlockSpec((own_heads, rows, clusters), lambda i, s: (0, i, 0)),
        ),
        out_shape=jax.ShapeDtypeStruct((own_heads, seq, clusters), BF),
        compiler_params=params(32, 1),
        cost_estimate=cost(own_heads * seq * clusters * picks * 8, own_heads * seq * clusters * 2),
        name="bias",
    )(info, top_all)

    wq_t = w_query.T.reshape(groups, feats, width)
    wkv_t = (
        w_keyval.T.reshape(2, heads, hs, width)
        .transpose(1, 0, 2, 3)
        .reshape(groups, 2 * feats, width)
    )
    gain_row, shift_row = gain_one[None, :], shift_one[None, :]

    normed_own, q_t, kv_t, kv = pl.pallas_call(
        functools.partial(project_kernel, peers=peers),
        grid_spec=pltpu.PrefetchScalarGridSpec(
            num_scalar_prefetch=1,
            grid=(groups, peers),
            in_specs=[
                pl.BlockSpec((rows, width), lambda g, p, s: (g * peers + p, 0)),
                whole((1, width)),
                whole((1, width)),
                pl.BlockSpec((1, feats, width), lambda g, p, s: (s[0], 0, 0)),
                pl.BlockSpec((1, 2 * feats, width), lambda g, p, s: (s[0], 0, 0)),
            ],
            out_specs=[
                pl.BlockSpec((rows, width), lambda g, p, s: (g, 0)),
                pl.BlockSpec((feats, rows), lambda g, p, s: (0, g * peers + p)),
                pl.BlockSpec((2 * feats, rows), lambda g, p, s: (0, g * peers + p)),
                pl.BlockSpec((own_heads, rows, 2 * hs), lambda g, p, s: (0, g * peers + p, 0)),
            ],
        ),
        out_shape=[
            jax.ShapeDtypeStruct((groups * rows, width), BF),
            jax.ShapeDtypeStruct((feats, seq), BF),
            jax.ShapeDtypeStruct((2 * feats, seq), BF),
            jax.ShapeDtypeStruct((own_heads, seq, 2 * hs), BF),
        ],
        compiler_params=params(32, 2),
        cost_estimate=cost(6 * seq * width * feats, seq * width * 4),
        name="project",
    )(info, tokens_all, gain_row, shift_row, wq_t, wkv_t)

    ids_full = pl.BlockSpec((1, 1, seq), lambda h, r: (h, 0, 0))
    ids_block = pl.BlockSpec((1, 1, rows), lambda h, r: (h, 0, r * peers))
    q_full = pl.BlockSpec((hs, seq), lambda h, r: (h, 0))
    q_block = pl.BlockSpec((hs, rows), lambda h, r: (h, r * peers))
    kvt_full = pl.BlockSpec((2 * hs, seq), lambda h, r: (h, 0))
    kv_full = pl.BlockSpec((1, seq, 2 * hs), lambda h, r: (h, 0, 0))
    bias_full = pl.BlockSpec((1, seq, clusters), lambda h, r: (h, 0, 0))
    head_out = pl.BlockSpec((1, hs, rows), lambda h, r: (r, h, 0))
    mix_spec = pl.BlockSpec((1, 1, hs + 8, rows), lambda h, r: (h, r, 0, 0))
    stat_spec = pl.BlockSpec((1, hs + 8, clusters), lambda h, r: (h, 0, 0))
    cen_spec = pl.BlockSpec((1, hs, clusters), lambda h, r: (h, 0, 0))
    part_spec = pl.BlockSpec((1, hs + 16, clusters), lambda h, r: (h, 0, 0))
    own_rows = groups * rows
    pair_flops = own_heads * own_rows * seq * 256

    attn_t, mixed, stats, centroid = pl.pallas_call(
        functools.partial(forward_kernel, size=size),
        grid=(own_heads, groups),
        in_specs=[ids_full, ids_block, q_full, q_block, kvt_full, kv_full, bias_full],
        out_specs=[head_out, mix_spec, stat_spec, cen_spec],
        out_shape=[
            jax.ShapeDtypeStruct((groups, feats, rows), BF),
            jax.ShapeDtypeStruct((own_heads, groups, hs + 8, rows), F32),
            jax.ShapeDtypeStruct((own_heads, hs + 8, clusters), F32),
            jax.ShapeDtypeStruct((own_heads, hs, clusters), BF),
        ],
        scratch_shapes=[pltpu.VMEM((hs + 8, 2 * clusters), BF)],
        compiler_params=params(56, 2),
        cost_estimate=cost(6 * pair_flops, 8e6, own_heads * own_rows * seq),
        name="attend",
    )(ids_all, ids_all, q_t, q_t, kv_t, kv, bias)

    arrived = [attn_t[0]] + [along_groups(attn_t[hop], hop) for hop in range(1, groups)]

    chunks = 6 if hidden % 768 == 0 else 1
    part = hidden // chunks
    w_out_g = w_out.reshape(groups, feats, width)
    gain_row2, shift_row2 = gain_two[None, :], shift_two[None, :]
    square = whole((rows, width))
    results = pl.pallas_call(
        functools.partial(block_kernel, groups=groups, chunks=chunks),
        grid_spec=pltpu.PrefetchScalarGridSpec(
            num_scalar_prefetch=1,
            grid=(chunks,),
            in_specs=[whole((feats, rows))] * groups
            + [
                square,
                whole((1, width)),
                whole((1, width)),
                whole((groups, feats, width)),
                pl.BlockSpec((width, part), lambda i, s: (0, i)),
                pl.BlockSpec((part, width), lambda i, s: (i, 0)),
                square,
            ],
            out_specs=[
                square,
                square,
                pl.BlockSpec((rows, part), lambda i, s: (0, i)),
                pl.BlockSpec((rows, part), lambda i, s: (0, i)),
                square,
                square,
                whole((2, width)),
            ]
            + [whole((feats, rows))] * groups,
            scratch_shapes=[
                pltpu.VMEM((rows, width), F32),
                pltpu.VMEM((rows, 128), F32),
                pltpu.VMEM((rows, width), F32),
            ],
        ),
        out_shape=[
            jax.ShapeDtypeStruct((rows, width), F32),
            jax.ShapeDtypeStruct((rows, width), BF),
            jax.ShapeDtypeStruct((rows, hidden), BF),
            jax.ShapeDtypeStruct((rows, hidden), BF),
            jax.ShapeDtypeStruct((rows, width), F32),
            jax.ShapeDtypeStruct((rows, width), BF),
            jax.ShapeDtypeStruct((2, width), F32),
        ]
        + [jax.ShapeDtypeStruct((feats, rows), BF)] * groups,
        compiler_params=params(48, 1),
        cost_estimate=cost(6 * rows * width * hidden, 4 * width * hidden, rows * hidden),
        name="feed",
    )(info, *arrived, tokens, gain_row2, shift_row2, w_out_g, w_up, w_down, cotangent)
    resid, normed_two, act, d_up, d_resid, d_branch, norm_two = results[:7]
    d_attn = results[7:]
    grads = [d_attn[0]] + [along_groups(d_attn[hop], -hop) for hop in range(1, groups)]
    grad_own = jnp.stack(grads)

    output, grad_up, grad_down = pl.pallas_call(
        functools.partial(weights_kernel, chunks=chunks),
        grid=(chunks,),
        in_specs=[
            square,
            square,
            pl.BlockSpec((rows, part), lambda i: (0, i)),
            pl.BlockSpec((rows, part), lambda i: (0, i)),
            pl.BlockSpec((part, width), lambda i: (i, 0)),
            square,
        ],
        out_specs=[
            square,
            pl.BlockSpec((width, part), lambda i: (0, i)),
            pl.BlockSpec((part, width), lambda i: (i, 0)),
        ],
        out_shape=[
            jax.ShapeDtypeStruct((rows, width), BF),
            jax.ShapeDtypeStruct((width, hidden), BF),
            jax.ShapeDtypeStruct((hidden, width), BF),
        ],
        scratch_shapes=[pltpu.VMEM((rows, width), F32)],
        compiler_params=params(48, 1),
        cost_estimate=cost(6 * rows * width * hidden, 6 * width * hidden),
        name="weights",
    )(resid, normed_two, act, d_up, w_down, cotangent)
    grad_out = jnp.concatenate([nn(item, d_branch).astype(BF)[None] for item in arrived], axis=0)
    grad_out = jnp.stack(
        [
            lax.dynamic_index_in_dim(grad_out, (group_at + groups - g) % groups, keepdims=False)
            for g in range(groups)
        ]
    ).reshape(width, width)

    def reduce_rows(partial, masks, axis):
        blocks = partial.reshape(groups, peers, partial.shape[0] // wide, partial.shape[1])

        def of_peer(hop):
            return lax.dynamic_index_in_dim(
                blocks, (peer_at + hop) % peers, axis=1, keepdims=False
            )

        total = of_peer(0).astype(F32)
        for hop in range(1, peers):
            total = total + along_peers(of_peer(hop), hop).astype(F32)
        total = total.astype(BF)
        for mask in masks:
            bit = (dp_at // mask) % 2
            half = total.shape[axis] // 2
            keep = lax.dynamic_slice_in_dim(total, bit * half, half, axis=axis)
            send = lax.dynamic_slice_in_dim(total, (1 - bit) * half, half, axis=axis)
            got = lax.ppermute(send, "dp", [(i, i ^ mask) for i in range(n_dp)])
            total = (keep.astype(F32) + got.astype(F32)).astype(BF)

        def of_group(hop):
            return lax.dynamic_index_in_dim(total, (group_at + hop) % groups, keepdims=False)

        done = of_group(0).astype(F32)
        for hop in range(1, groups):
            done = done + along_groups(of_group(hop), hop).astype(F32)
        return spread_dp(done.astype(BF), masks, axis - 1)

    def spread_dp(done, masks, axis):
        for mask in reversed(masks):
            bit = (dp_at // mask) % 2
            got = lax.ppermute(done, "dp", [(i, i ^ mask) for i in range(n_dp)])
            done = jnp.where(
                bit == 0,
                jnp.concatenate([done, got], axis=axis),
                jnp.concatenate([got, done], axis=axis),
            )
        return done

    masks = [1 << k for k in range(n_dp.bit_length() - 1)]
    total_up = reduce_rows(grad_up, masks, 2).astype(F32)
    total_down = reduce_rows(grad_down, masks[::-1], 2).astype(F32)
    total_out = reduce_rows(grad_out, masks, 2).astype(F32)
    norms = lax.psum(norm_two, ("dp", "wide"))

    part = pl.pallas_call(
        sums_kernel,
        grid=(own_heads, groups),
        in_specs=[ids_block, head_out, mix_spec],
        out_specs=part_spec,
        out_shape=jax.ShapeDtypeStruct((own_heads, hs + 16, clusters), F32),
        compiler_params=params(32, 2),
        cost_estimate=cost(own_heads * own_rows * clusters * 160, 2e6),
        name="sums",
    )(ids_all, grad_own, mixed)
    part_total = part
    for hop in range(1, peers):
        part_total = part_total + along_peers(part, hop)

    dq_member, dkv_own, dkv_send = pl.pallas_call(
        functools.partial(member_kernel, size=size),
        grid=(own_heads, groups),
        in_specs=[
            ids_block,
            q_block,
            kvt_full,
            kv_full,
            bias_full,
            head_out,
            mix_spec,
            stat_spec,
        ],
        out_specs=[
            head_out,
            pl.BlockSpec((1, own_rows, 2 * hs), lambda h, r: (h, 0, 0)),
            pl.BlockSpec((1, max(peers - 1, 1) * own_rows, 2 * hs), lambda h, r: (h, 0, 0)),
        ],
        out_shape=[
            jax.ShapeDtypeStruct((groups, feats, rows), F32),
            jax.ShapeDtypeStruct((own_heads, own_rows, 2 * hs), F32),
            jax.ShapeDtypeStruct((own_heads, max(peers - 1, 1) * own_rows, 2 * hs), BF),
        ],
        scratch_shapes=[pltpu.VMEM((seq, 2 * hs), F32)],
        compiler_params=params(56, 2),
        cost_estimate=cost(12 * pair_flops, 10e6, own_heads * own_rows * seq),
        name="member",
    )(ids_all, q_t, kv_t, kv, bias, grad_own, mixed, stats)
    dkv_got = [
        along_peers(dkv_send[:, (hop - 1) * own_rows : hop * own_rows], hop)
        for hop in range(1, peers)
    ]
    dkv_got = jnp.concatenate(dkv_got, axis=1) if dkv_got else jnp.zeros_like(dkv_send)

    one = [
        pl.BlockSpec(spec.block_shape, functools.partial(lambda h, f: f(h, 0), f=spec.index_map))
        for spec in (ids_full, kvt_full, kv_full, bias_full, part_spec, stat_spec, cen_spec)
    ]
    all_groups = pl.BlockSpec((groups, hs, rows), lambda h: (0, h, 0))
    d_q, d_kv = pl.pallas_call(
        functools.partial(centroid_kernel, size=size),
        grid=(own_heads,),
        in_specs=one
        + [
            all_groups,
            pl.BlockSpec((1, own_rows, 2 * hs), lambda h: (h, 0, 0)),
            pl.BlockSpec((1, max(peers - 1, 1) * own_rows, 2 * hs), lambda h: (h, 0, 0)),
        ],
        out_specs=[
            all_groups,
            pl.BlockSpec((groups, rows, 2 * hs), lambda h: (0, 0, h)),
        ],
        out_shape=[
            jax.ShapeDtypeStruct((groups, feats, rows), BF),
            jax.ShapeDtypeStruct((groups, rows, 2 * feats), BF),
        ],
        scratch_shapes=[pltpu.VMEM((seq, 2 * clusters), BF)],
        compiler_params=params(56, 1),
        cost_estimate=cost(own_heads * clusters * seq * 1024, 8e6, own_heads * clusters * seq),
        name="centroid",
    )(ids_all, kv_t, kv, bias, part_total, stats, centroid, dq_member, dkv_own, dkv_got)

    dqs = [d_q[0]] + [along_groups(d_q[hop], hop) for hop in range(1, groups)]
    dkvs = [d_kv[0]] + [along_groups(d_kv[hop], hop) for hop in range(1, groups)]

    grad_tokens = pl.pallas_call(
        functools.partial(final_kernel, groups=groups),
        grid_spec=pltpu.PrefetchScalarGridSpec(
            num_scalar_prefetch=1,
            grid=(1,),
            in_specs=[whole((feats, rows))] * groups
            + [whole((rows, 2 * feats))] * groups
            + [
                square,
                square,
                whole((1, width)),
                whole((groups, feats, width)),
                whole((groups, 2 * feats, width)),
            ],
            out_specs=square,
        ),
        out_shape=jax.ShapeDtypeStruct((rows, width), BF),
        compiler_params=params(48, 1),
        cost_estimate=cost(6 * rows * width * width, 6 * width * width),
        name="final",
    )(info, *dqs, *dkvs, tokens, d_resid, gain_row, wq_t, wkv_t)

    flat_kv = d_kv.reshape(own_rows, 2 * feats)
    grad_q = jnp.einsum("grk,gfr->kf", normed_own.reshape(groups, rows, width), d_q, preferred_element_type=F32)
    grad_kv = tn(normed_own, flat_kv)
    grad_kv = grad_kv.reshape(width, own_heads, 2, hs).transpose(0, 2, 1, 3).reshape(width, 2 * feats)
    sum_q = jnp.sum(d_q.astype(F32), axis=(0, 2))
    sum_kv = (
        jnp.sum(flat_kv.astype(F32), axis=0)
        .reshape(own_heads, 2, hs)
        .transpose(1, 0, 2)
        .reshape(2 * feats)
    )
    block_rows = width // wide
    extra = jnp.broadcast_to(jnp.concatenate([sum_q, sum_kv])[None, None, :], (wide, 8, 3 * feats))
    grad_in = jnp.concatenate([grad_q, grad_kv], axis=1).reshape(wide, block_rows, 3 * feats)
    grad_in = jnp.concatenate([grad_in, extra], axis=1).astype(BF)
    in_rows = grad_in.shape[1]

    def of_peer(hop):
        return lax.dynamic_index_in_dim(
            grad_in.reshape(groups, peers, in_rows, 3 * feats),
            (peer_at + hop) % peers,
            axis=1,
            keepdims=False,
        )

    total = of_peer(0).astype(F32)
    for hop in range(1, peers):
        total = total + along_peers(of_peer(hop), hop).astype(F32)
    total = total.astype(BF)
    for mask in masks:
        got = lax.ppermute(total, "dp", [(i, i ^ mask) for i in range(n_dp)])
        total = (total.astype(F32) + got.astype(F32)).astype(BF)
    pieces = [lax.dynamic_index_in_dim(total, group_at, keepdims=False)]
    for hop in range(1, groups):
        item = lax.dynamic_index_in_dim(total, (group_at + hop) % groups, keepdims=False)
        pieces.append(along_groups(item, hop))
    pieces = jnp.stack(pieces)
    pieces = jnp.stack(
        [
            lax.dynamic_index_in_dim(pieces, (group_at + groups - g) % groups, keepdims=False)
            for g in range(groups)
        ]
    ).astype(F32)
    q_part = pieces[:, :, :feats].transpose(1, 0, 2).reshape(in_rows, width)
    kv_part = (
        pieces[:, :, feats:]
        .reshape(groups, in_rows, 2, feats)
        .transpose(1, 2, 0, 3)
        .reshape(in_rows, 2 * width)
    )
    total_query, total_keyval = q_part[:block_rows], kv_part[:block_rows]
    at = me * block_rows
    wq_rows = lax.dynamic_slice_in_dim(w_query, at, block_rows).astype(F32)
    wkv_rows = lax.dynamic_slice_in_dim(w_keyval, at, block_rows).astype(F32)
    shift_grad = jnp.sum(wq_rows * q_part[block_rows], axis=1) + jnp.sum(
        wkv_rows * kv_part[block_rows], axis=1
    )
    along = jnp.sum(wq_rows * total_query, axis=1) + jnp.sum(wkv_rows * total_keyval, axis=1)
    gain_own = lax.dynamic_slice_in_dim(gain_one, at, block_rows)
    shift_own = lax.dynamic_slice_in_dim(shift_one, at, block_rows)
    gain_grad = (along - shift_own * shift_grad) / gain_own
    norm_two_own = lax.dynamic_slice_in_dim(norms, at, block_rows, axis=1)
    return (
        output,
        grad_tokens,
        total_query,
        total_keyval,
        total_out,
        total_up,
        total_down,
        gain_grad,
        shift_grad,
        norm_two_own[0],
        norm_two_own[1],
    )


def solution(mesh):
    return jax.shard_map(
        per_device,
        mesh=mesh,
        in_specs=(
            P(("dp", "wide"), None),
            P(("dp", "wide"), None),
            P("dp"),
            P("dp", None, "wide", None),
            P(),
            P(),
            P(),
            P(),
            P(),
            P(),
            P(),
            P(),
            P(),
            P(("dp", "wide"), None),
        ),
        out_specs=(
            P(("dp", "wide"), None),
            P(("dp", "wide"), None),
            P("wide", None),
            P("wide", None),
            P("wide", None),
            P("wide", None),
            P("wide", None),
            P("wide"),
            P("wide"),
            P("wide"),
            P("wide"),
        ),
        check_vma=False,
    )
```

```python
import functools
import math

import jax
import jax.numpy as jnp
import numpy as np
from jax import lax
from jax.experimental import pallas as pl
from jax.experimental.pallas import tpu as pltpu
from jax.sharding import PartitionSpec as P

EPSILON = 1e-05
NEGATIVE = -1e30
EXCLUDED = -3e30
GELU_A = math.sqrt(2.0 / math.pi)
GELU_B = 0.044715
BF = jnp.bfloat16
F32 = jnp.float32


def nn(left, right):
    return lax.dot_general(left, right, (((1,), (0,)), ((), ())), preferred_element_type=F32)


def nt(left, right):
    return lax.dot_general(left, right, (((1,), (1,)), ((), ())), preferred_element_type=F32)


def tn(left, right):
    return lax.dot_general(left, right, (((0,), (0,)), ((), ())), preferred_element_type=F32)


def params(mib, dims):
    return pltpu.CompilerParams(
        vmem_limit_bytes=mib * 1024 * 1024, dimension_semantics=("arbitrary",) * dims
    )


def cost(flops, nbytes, trans=0):
    return pl.CostEstimate(flops=int(flops), bytes_accessed=int(nbytes), transcendentals=int(trans))


def split_low(values):
    high = values.astype(BF)
    return high, (values - high.astype(F32)).astype(BF)


def one_hot_t(ids_row, clusters):
    rows = lax.broadcasted_iota(jnp.int32, (clusters, ids_row.shape[1]), 0)
    return jnp.where(rows == ids_row, 1.0, 0.0).astype(BF)


def key_passes(total, size, score, weigh):
    count = total // size
    if count <= 4:
        blocks = [score(index) for index in range(count)]
        peak = functools.reduce(jnp.maximum, [jnp.max(b, axis=0, keepdims=True) for b in blocks])
        denom, sums = 0.0, None
        for index in range(count):
            expo = jnp.exp(blocks[index] - peak)
            denom = denom + jnp.sum(expo, axis=0, keepdims=True)
            parts = weigh(index, expo)
            sums = parts if sums is None else tuple(x + y for x, y in zip(sums, parts))
        return peak, denom, sums

    def step(index, carry):
        peak, denom, sums = carry
        block = score(index)
        fresh = jnp.maximum(peak, jnp.max(block, axis=0, keepdims=True))
        expo = jnp.exp(block - fresh)
        fade = jnp.exp(peak - fresh)
        parts = weigh(index, expo)
        return (
            fresh,
            denom * fade + jnp.sum(expo, axis=0, keepdims=True),
            tuple(old * fade + new for old, new in zip(sums, parts)),
        )

    shapes = jax.eval_shape(lambda: (score(0), weigh(0, score(0))))
    lanes = shapes[0].shape[1]
    start = (
        jnp.full((1, lanes), NEGATIVE, F32),
        jnp.zeros((1, lanes), F32),
        tuple(jnp.zeros(item.shape, F32) for item in shapes[1]),
    )
    return lax.fori_loop(0, count, step, start)


def key_sum(total, size, step, start):
    count = total // size
    if count <= 4:
        for index in range(count):
            start = step(index, start)
        return start
    return lax.fori_loop(0, count, step, start)


def spot_of(index, size):
    if isinstance(index, int):
        return pl.ds(index * size, size)
    return pl.ds(pl.multiple_of(index * size, size), size)


def piece(ref, index, size, axis):
    spot = spot_of(index, size)
    return ref[spot, :] if axis == 0 else ref[:, spot]


def bias_kernel(info, top_ref, bias_ref, *, groups, peers, rows):
    part = pl.program_id(0)
    owner = (
        lax.rem(info[0] + part // peers, groups) * peers + lax.rem(info[1] + part % peers, peers)
    )
    heads, picks, clusters = top_ref.shape
    place = owner * rows + lax.broadcasted_iota(jnp.int32, (rows, clusters), 0)
    outside = place >= info[2]
    for head in range(heads):
        top = top_ref[head]
        chosen = place == top[0:1, :]
        for pick in range(1, picks):
            chosen = chosen | (place == top[pick : pick + 1, :])
        value = jnp.where(chosen, 0.0, jnp.where(outside, EXCLUDED, NEGATIVE))
        bias_ref[head] = value.astype(BF)


def project_kernel(info, *refs, peers, olds):
    parts = refs[:peers]
    gain_ref, shift_ref, w_ref = refs[peers : peers + 3]
    hat_ref, feat_ref, kv_ref = refs[peers + 3 + olds :]
    rows = hat_ref.shape[0]
    for peer in range(peers):
        values = parts[peer][...].astype(F32)
        centered = values - jnp.mean(values, axis=-1, keepdims=True)
        variance = jnp.mean(centered * centered, axis=-1, keepdims=True)
        scaled = centered * lax.rsqrt(variance + EPSILON) * gain_ref[...]
        if peer == 0:
            hat_ref[...] = scaled.astype(BF)
        low = (scaled + shift_ref[...]).astype(BF)
        found = nt(w_ref[0], low)
        heads, triple = feat_ref.shape[0], feat_ref.shape[1]
        hs = triple // 3
        spot = slice(peer * rows, (peer + 1) * rows)
        for head in range(heads):
            base = head * triple
            query = (found[base : base + hs] * 0.125).astype(BF)
            pair = found[base + hs : base + triple].astype(BF)
            feat_ref[head, :hs, spot] = query
            feat_ref[head, hs:, spot] = pair
            kv_ref[head, spot, :] = pair.T


def forward_kernel(ids_all, ids_own, feat_all, feat_own, kv, bias, *refs, size, groups):
    outs = refs[:groups]
    mix_ref, stat_ref, cen_ref, table = refs[groups:]
    hs = feat_own.shape[1] // 3
    keys = kv.shape[1]
    clusters = bias.shape[2]
    kv_h, bias_h = kv.at[0], bias.at[0]
    qt_all, kvt = feat_all.at[0, :hs], feat_all.at[0, hs:]

    @pl.when(pl.program_id(1) == 0)
    def centroid_stage():
        hot = one_hot_t(ids_all[0], clusters)
        ones = jnp.ones((16, keys), BF)
        sums = nt(jnp.concatenate([qt_all[...], ones], axis=0), hot)
        counts = sums[hs : hs + 1]
        centroid = (sums[:hs] / jnp.maximum(counts, 1.0)).astype(BF)
        padded = jnp.concatenate([centroid, jnp.zeros_like(centroid)], axis=0)

        def score(index):
            scores = nn(piece(kv_h, index, size, 0), padded)
            outside = piece(bias_h, index, size, 0).astype(F32) < 2.0 * NEGATIVE
            return jnp.where(outside, NEGATIVE, scores)

        def weigh(index, expo):
            top = piece(bias_h, index, size, 0).astype(F32) == 0.0
            mass = jnp.sum(jnp.where(top, expo, 0.0), axis=0, keepdims=True)
            other = jnp.where(top, 0.0, expo).astype(BF)
            return nn(piece(kvt, index, size, 1), other), mass

        peak, denom, (rest, mass) = key_passes(keys, size, score, weigh)
        rest = rest[hs:] / denom
        mass = mass / denom
        stats = jnp.concatenate(
            [
                rest,
                mass,
                peak + jnp.log(denom),
                counts,
                jnp.zeros((5, clusters), F32),
            ],
            axis=0,
        )
        stat_ref[0] = stats
        cen_ref[0] = centroid
        high, low = split_low(stats)
        table[...] = jnp.concatenate([high, low], axis=1)

    hot = one_hot_t(ids_own[0], clusters)
    queries = feat_own[0, :hs]
    side = jnp.concatenate([queries, jnp.zeros_like(queries), hot], axis=0)
    gathered = nn(table[...], jnp.concatenate([hot, hot], axis=0))

    def score(index):
        return nn(
            jnp.concatenate([piece(kv_h, index, size, 0), piece(bias_h, index, size, 0)], axis=1),
            side,
        )

    def weigh(index, expo):
        return (nn(piece(kvt, index, size, 1), expo.astype(BF)),)

    peak, denom, (mix,) = key_passes(keys, size, score, weigh)
    mix = mix[hs:] / denom
    result = (gathered[hs : hs + 1] * mix + gathered[:hs]).astype(BF)
    for group in range(groups):

        @pl.when(pl.program_id(1) == group)
        def store(group=group):
            outs[group][...] = result

    mix_ref[0, 0] = jnp.concatenate(
        [mix, jnp.broadcast_to(peak + jnp.log(denom), (8, mix.shape[1]))], axis=0
    )


def sums_kernel(ids_own, *refs, groups):
    grads, (mix_ref, part_ref) = refs[:groups], refs[groups:]
    hs = grads[0].shape[0]
    total = None
    for group in range(groups):
        rows = grads[group].shape[1]
        step = ids_own.shape[2] // groups
        hot = one_hot_t(ids_own[0, :, group * step : group * step + rows], part_ref.shape[2])
        grad = grads[group][...]
        along = jnp.sum(grad.astype(F32) * mix_ref[0, group, :hs], axis=0, keepdims=True)
        high, low = split_low(along)
        pad = jnp.zeros((14, rows), BF)
        part = nt(jnp.concatenate([grad, high, low, pad], axis=0), hot)
        total = part if total is None else total + part
    part_ref[0] = total


def member_kernel(ids_own, feat_all, feat_own, kv, bias, *refs, size, groups):
    grads = refs[:groups]
    mix_ref, stat_ref, dq_ref, own_ref, send_ref, total, picked = refs[groups:]
    hs, rows = picked.shape
    keys = kv.shape[1]
    clusters = bias.shape[2]
    block = pl.program_id(1)
    for group in range(groups):

        @pl.when(block == group)
        def pick(group=group):
            picked[...] = grads[group][...]

    kv_h, bias_h, kvt = kv.at[0], bias.at[0], feat_all.at[0, hs:]
    hot = one_hot_t(ids_own[0], clusters)
    queries = feat_own[0, :hs]
    blank = jnp.zeros_like(queries)
    side = jnp.concatenate([queries, blank, hot], axis=0)
    high, low = split_low(stat_ref[0, hs : hs + 8, :])
    mass = nn(jnp.concatenate([high, low], axis=1), jnp.concatenate([hot, hot], axis=0))[0:1]
    mix = mix_ref[0, 0, :hs]
    level = mix_ref[0, 0, hs : hs + 1]
    back = (mass * picked[...].astype(F32)).astype(BF)
    delta = jnp.sum(back.astype(F32) * mix, axis=0, keepdims=True)
    back_pad = jnp.concatenate([blank, back], axis=0)
    right = jnp.concatenate([jnp.concatenate([queries, blank], axis=0), back_pad], axis=1).T

    @pl.when(block == 0)
    def clear():
        total[...] = jnp.zeros_like(total)

    def step(index, dq):
        kv_c = piece(kv_h, index, size, 0)
        scores = nn(jnp.concatenate([kv_c, piece(bias_h, index, size, 0)], axis=1), side)
        weights = jnp.exp(scores - level)
        grad_w = nn(kv_c, back_pad)
        grad_s = (weights * (grad_w - delta)).astype(BF)
        spot = spot_of(index, size)
        total[spot, :] += nn(jnp.concatenate([grad_s, weights.astype(BF)], axis=1), right)
        return dq + nn(piece(kvt, index, size, 1), grad_s)

    dq = key_sum(keys, size, step, jnp.zeros((2 * hs, rows), F32))
    dq_ref[0] = dq[:hs] * 0.125

    @pl.when(block == groups - 1)
    def finish():
        peers = keys // own_ref.shape[1]
        for group in range(groups):
            base = group * peers * rows
            own_ref[0, group * rows : (group + 1) * rows, :] = total[base : base + rows, :]
            for peer in range(1, peers):
                spot = (peer - 1) * groups * rows + group * rows
                send_ref[0, spot : spot + rows, :] = total[
                    base + peer * rows : base + (peer + 1) * rows, :
                ].astype(BF)


def centroid_kernel(ids_own, feat_all, kv, bias, part_ref, stat_ref, cen_ref, dqm_ref, own_ref, *refs, size, groups, gots):
    got_refs = refs[:gots]
    outs, both = refs[gots : gots + groups], refs[gots + groups]
    hs, rows = cen_ref.shape[1], outs[0].shape[2]
    keys = kv.shape[1]
    peers = keys // (groups * rows)
    clusters = bias.shape[2]
    kv_h, bias_h, kvt = kv.at[0], bias.at[0], feat_all.at[0, hs:]
    stats = stat_ref[0]
    rest, mass = stats[:hs], stats[hs : hs + 1]
    level, counts = stats[hs + 1 : hs + 2], stats[hs + 2 : hs + 3]
    centroid = cen_ref[0]
    blank = jnp.zeros_like(centroid)
    part = part_ref[0]
    d_rest = part[:hs].astype(BF)
    d_mass = part[hs : hs + 1] + part[hs + 1 : hs + 2]
    delta = jnp.sum(d_rest.astype(F32) * rest, axis=0, keepdims=True) + d_mass * mass
    cen_pad = jnp.concatenate([centroid, blank], axis=0)
    rest_pad = jnp.concatenate([blank, d_rest], axis=0)
    right = jnp.concatenate([cen_pad, rest_pad], axis=1).T

    def step(index, total):
        kv_c = piece(kv_h, index, size, 0)
        marks = piece(bias_h, index, size, 0).astype(F32)
        scores = nn(kv_c, cen_pad)
        probs = jnp.where(marks < 2.0 * NEGATIVE, 0.0, jnp.exp(scores - level))
        top = marks == 0.0
        d_probs = jnp.where(top, d_mass, nn(kv_c, rest_pad))
        d_score = (probs * (d_probs - delta)).astype(BF)
        other = jnp.where(top, 0.0, probs).astype(BF)
        both[spot_of(index, size), :] = jnp.concatenate([d_score, other], axis=1)
        return total + nn(piece(kvt, index, size, 1), d_score)

    d_cen = key_sum(keys, size, step, jnp.zeros((2 * hs, clusters), F32))
    d_cen = d_cen[:hs] * 0.125 / jnp.maximum(counts, 1.0)
    high, low = split_low(d_cen)
    table = jnp.concatenate([high, low], axis=1)
    for group in range(groups):
        spot = group * peers * rows
        hot = one_hot_t(ids_own[0, :, spot : spot + rows], clusters)
        spread = nn(table, jnp.concatenate([hot, hot], axis=0))
        own = nn(both[spot : spot + rows, :], right) + own_ref[0, group * rows : (group + 1) * rows, :]
        for got in got_refs:
            own = own + got[0, group * rows : (group + 1) * rows, :].astype(F32)
        outs[group][0, :hs] = (dqm_ref[group] + spread).astype(BF)
        outs[group][0, hs:] = own.T.astype(BF)


def block_kernel(info, *refs, groups, chunks, fast):
    (attn, rest) = (refs[:groups], refs[groups:])
    x_ref, gain_ref, shift_ref, wo_ref, up_ref, down_ref, cot_ref = rest[:7]
    out_ref, dres_ref, dn_ref, dup_ref, dbr_ref, act_ref, low_ref = rest[7:14]
    rest = rest[14:]
    if fast:
        act_far, low_far = rest[:2]
        rest = rest[2:]
    dat = rest[:groups]
    hat_ref, inv_ref, normed, back, total = rest[groups:]
    index = pl.program_id(0)

    @pl.when(index == 0)
    def before():
        resid = x_ref[...].astype(F32)
        for group in range(groups):
            owner = lax.rem(info[0] + groups - group, groups)
            resid = resid + tn(attn[group][...], wo_ref[owner])
        total[...] = resid
        centered = resid - jnp.mean(resid, axis=-1, keepdims=True)
        variance = jnp.mean(centered * centered, axis=-1, keepdims=True)
        inverse = lax.rsqrt(variance + EPSILON)
        hat = centered * inverse
        hat_ref[...] = hat
        inv_ref[...] = jnp.broadcast_to(inverse, inv_ref.shape)
        low = (hat * gain_ref[...] + shift_ref[...]).astype(BF)
        normed[...] = low
        if fast:
            feats = attn[0].shape[0]
            half = feats // 2
            turned = low.T
            for group in range(groups):
                first = turned[group * feats : group * feats + half]
                second = turned[group * feats + half : (group + 1) * feats]
                spot = slice(group * half, (group + 1) * half)
                low_ref[spot, :] = jnp.where(info[1] == 0, first, second)
                low_far[spot, :] = jnp.where(info[1] == 0, second, first)
                first = attn[group][:half]
                second = attn[group][half:]
                spot = slice((groups + group) * half, (groups + group + 1) * half)
                low_ref[spot, :] = jnp.where(info[1] == 0, first, second)
                low_far[spot, :] = jnp.where(info[1] == 0, second, first)
        else:
            low_ref[...] = low
        back[...] = jnp.zeros_like(back)

    up = nn(normed[...], up_ref[...])
    grad_act = nt(cot_ref[...], down_ref[...])
    square = up * up
    inner = GELU_A * (up + GELU_B * up * square)
    curve = jnp.tanh(inner)
    act = (0.5 * up * (1.0 + curve)).astype(BF)
    slope = 0.5 * (1.0 + curve) + 0.5 * up * (1.0 - curve * curve) * (
        GELU_A * (1.0 + 3.0 * GELU_B * square)
    )
    d_up = (grad_act * slope).astype(BF)
    dup_ref[...] = d_up
    if fast:
        half = act.shape[1] // 2
        first, second = act[:, :half], act[:, half:]
        act_ref[...] = jnp.where(info[1] == 0, first, second)
        act_far[...] = jnp.where(info[1] == 0, second, first)
    else:
        act_ref[...] = act
    back[...] += nt(d_up, up_ref[...])
    total[...] += nn(act, down_ref[...])

    @pl.when(index == chunks - 1)
    def after():
        out_ref[...] = total[...].astype(BF)
        d_normed = back[...]
        hat = hat_ref[...]
        gain_part = jnp.sum(d_normed * hat, axis=0, keepdims=True)
        shift_part = jnp.sum(d_normed, axis=0, keepdims=True)
        blank = jnp.zeros((6, d_normed.shape[1]), F32)
        dn_ref[...] = jnp.concatenate([gain_part, shift_part, blank], axis=0)
        gy = d_normed * gain_ref[...]
        mean_one = jnp.mean(gy, axis=-1, keepdims=True)
        mean_two = jnp.mean(gy * hat, axis=-1, keepdims=True)
        d_resid = cot_ref[...].astype(F32) + inv_ref[:, 0:1] * (gy - mean_one - hat * mean_two)
        dres_ref[...] = d_resid
        branch = d_resid.astype(BF)
        dbr_ref[...] = branch
        for group in range(groups):
            owner = lax.rem(info[0] + groups - group, groups)
            dat[group][...] = nt(wo_ref[owner], branch).astype(BF)


def weights_kernel(info, *refs, groups):
    (dup, dup_got, dbr, dbr_got, act, act_got, low, low_got, cot, cot_got, dn, dn_got) = refs[:12]
    send_u, keep_u, send_d, keep_d, outs = refs[12:]
    index = pl.program_id(0)
    group_at, place_u, place_d = info[0], info[3], info[4]
    rows = low.shape[0] // (2 * groups)
    quarter = rows // 4
    stay = groups * rows

    @pl.when(index == 0)
    def first():
        found = nn(low[stay:, :], dbr[...]) + nn(low_got[stay:, :], dbr_got[...])
        for group in range(groups):
            outs[group] = found[group * rows : (group + 1) * rows]

    up = nn(low[:stay, :], dup[...]) + nn(low_got[:stay, :], dup_got[...])
    at = lax.bitwise_xor(lax.bitwise_xor(index, 2), place_u)
    norms = dn[...] + dn_got[...]
    for group in range(groups):
        spot = lax.rem(group + groups - group_at, groups)
        block = up[group * rows : (group + 1) * rows].astype(BF)
        away = (groups - group) % groups
        start = pl.multiple_of(at * quarter, 8)
        other = jnp.concatenate([outs[group, pl.ds(start, quarter), :], norms], axis=0).astype(BF)

        @pl.when(index < 2)
        def leaves():
            send_u[0, spot, :rows] = block
            send_u[0, away, rows:] = other

        @pl.when(index >= 2)
        def stays():
            keep_u[0, spot, :rows] = block
            keep_u[0, away, rows:] = other

    down = tn(act[...], cot[...]) + tn(act_got[...], cot_got[...])
    spot = lax.rem(index + groups - group_at, groups)
    for part in range(4):
        block = down[part * rows : (part + 1) * rows].astype(BF)
        place = lax.bitwise_xor(part, place_d)

        @pl.when(place >= 2)
        def leaves_down():
            send_d[place - 2, spot] = block

        @pl.when(place < 2)
        def stays_down():
            keep_d[place, spot] = block


def second_kernel(keep_u, got_u, keep_d, got_d, send_u, send_d):
    send_u[...] = (keep_u[0].astype(F32) + got_u[0].astype(F32)).astype(BF)
    send_d[...] = (keep_d[0].astype(F32) + got_d[0].astype(F32)).astype(BF)


def third_kernel(keep_u, got_u, last_u, keep_d, got_d, last_d, *outs):
    rows = keep_u.shape[2]
    for group in range(len(outs)):
        up = keep_u[0, group].astype(F32) + got_u[0, group].astype(F32) + last_u[group].astype(F32)
        down = keep_d[0, group].astype(F32) + got_d[0, group].astype(F32) + last_d[group].astype(F32)
        outs[group][:rows] = up.astype(BF)
        outs[group][rows:] = down.astype(BF)


def fourth_kernel(*refs):
    parts, out = refs[:-1], refs[-1]
    total = parts[0][...].astype(F32)
    for part in parts[1:]:
        total = total + part[...].astype(F32)
    out[...] = total.astype(BF)


def spread_kernel(info, own, from_x, from_y, from_xy, up_ref, out_ref, down_ref, norm_ref):
    index = pl.program_id(0)
    rows = up_ref.shape[0]
    quarter = out_ref.shape[0]
    top = rows + quarter + 8
    for place, part in enumerate((own, from_y, from_x, from_xy)):

        @pl.when(index == place)
        def upper(part=part):
            up_ref[...] = part[:rows].astype(F32)
            tail = part[rows:top].astype(F32)
            out_ref[...] = tail[:quarter]

            @pl.when(lax.bitwise_xor(index, info[3]) == 0)
            def norms():
                norm_ref[...] = tail[quarter:]

    for place, part in enumerate((own, from_x, from_y, from_xy)):

        @pl.when(index == place)
        def lower(part=part):
            down_ref[...] = part[top:].astype(F32)


def inward_kernel(info, *refs, groups, fast):
    parts, hat_ref = refs[:groups], refs[groups]
    outs = refs[groups + 1 :]
    heads, triple, rows = parts[0].shape
    hs = triple // 3
    total, sums = None, None
    ones = jnp.ones((16, rows), BF)
    for group in range(groups):
        order = [parts[group][h, k * hs : (k + 1) * hs] for k in range(3) for h in range(heads)]
        turned = jnp.concatenate(order, axis=0)
        found = nn(turned, hat_ref[group * rows : (group + 1) * rows, :])
        more = nt(ones, turned)
        total = found if total is None else total + found
        sums = more if sums is None else sums + more
    total = total.T
    if not fast:
        outs[0][...] = total
        outs[1][...] = sums
        return
    own_ref, far_ref = outs
    block = total.shape[0] // (2 * groups)
    low_sums = sums.astype(BF)
    for group in range(groups):
        spot = lax.rem(group + groups - info[0], groups)
        first = total[2 * group * block : (2 * group + 1) * block].astype(BF)
        second = total[(2 * group + 1) * block : (2 * group + 2) * block].astype(BF)
        own_ref[spot, :block] = jnp.where(info[1] == 0, first, second)
        far_ref[spot, :block] = jnp.where(info[1] == 0, second, first)
        own_ref[spot, block:] = low_sums
        far_ref[spot, block:] = low_sums


def final_kernel(info, *refs, groups):
    parts = refs[:groups]
    x_ref, dres_ref, gain_ref, w_ref, out_ref = refs[groups:]
    d_normed = jnp.zeros(dres_ref.shape, F32)
    for group in range(groups):
        owner = lax.rem(info[0] + groups - group, groups)
        heads, triple, rows = parts[group].shape
        d_normed = d_normed + tn(parts[group][...].reshape(heads * triple, rows), w_ref[owner])
    values = x_ref[...].astype(F32)
    centered = values - jnp.mean(values, axis=-1, keepdims=True)
    variance = jnp.mean(centered * centered, axis=-1, keepdims=True)
    inverse = lax.rsqrt(variance + EPSILON)
    hat = centered * inverse
    gy = d_normed * gain_ref[...]
    mean_one = jnp.mean(gy, axis=-1, keepdims=True)
    mean_two = jnp.mean(gy * hat, axis=-1, keepdims=True)
    out_ref[...] = (dres_ref[...] + inverse * (gy - mean_one - hat * mean_two)).astype(BF)


def whole(shape):
    return pl.BlockSpec(shape, lambda *at: (0,) * len(shape))


def per_device(
    tokens,
    cluster_ids,
    lengths,
    top_keys,
    gain_one,
    shift_one,
    w_query,
    w_keyval,
    w_out,
    gain_two,
    shift_two,
    w_up,
    w_down,
    cotangent,
):
    rows, width = tokens.shape
    heads = cluster_ids.shape[1]
    hs = width // heads
    hidden = w_up.shape[1]
    wide = lax.axis_size("wide")
    n_dp = lax.axis_size("dp")
    groups = math.gcd(heads, wide)
    peers = wide // groups
    own_heads = heads // groups
    own_clusters = top_keys.shape[2]
    clusters = own_clusters * wide
    picks = top_keys.shape[3]
    seq = rows * wide
    size = 512 if seq <= 2048 else 2048
    feats = own_heads * hs
    block_rows = width // wide
    fast = peers == 2 and n_dp == 4 and block_rows % 32 == 0 and hidden % (4 * 256) == 0
    me = lax.axis_index("wide")
    group_at, peer_at = me // peers, me % peers
    dp_at = lax.axis_index("dp")
    seq_len = lengths[0]
    bit_x, bit_y = dp_at % 2, (dp_at // 2) % 2
    place_u, place_d = 2 * bit_x + bit_y, 2 * bit_y + bit_x
    info = jnp.stack([group_at, peer_at, seq_len, place_u, place_d, me]).astype(jnp.int32)

    def along_groups(values, hop):
        pairs = [(i, ((i // peers + hop) % groups) * peers + i % peers) for i in range(wide)]
        return lax.ppermute(values, "wide", pairs)

    def along_peers(values, hop):
        pairs = [(i, (i // peers) * peers + (i % peers + hop) % peers) for i in range(wide)]
        return lax.ppermute(values, "wide", pairs)

    def along_dp(values, mask):
        return lax.ppermute(values, "dp", [(i, i ^ mask) for i in range(n_dp)])

    def prefetched(kernel, grid, in_specs, out_specs, out_shape, mib, spent, name, scratch=(), alias=None):
        return pl.pallas_call(
            kernel,
            grid_spec=pltpu.PrefetchScalarGridSpec(
                num_scalar_prefetch=1,
                grid=grid,
                in_specs=in_specs,
                out_specs=out_specs,
                scratch_shapes=list(scratch),
            ),
            out_shape=out_shape,
            compiler_params=params(mib, len(grid)),
            cost_estimate=spent,
            input_output_aliases=alias or {},
            name=name,
        )

    def array(shape, dtype):
        return jax.ShapeDtypeStruct(shape, dtype)

    position = me * rows + jnp.arange(rows, dtype=jnp.int32)
    marked = jnp.where((position < seq_len)[:, None], cluster_ids, -1).T
    packed = jnp.concatenate([marked, top_keys[0].reshape(heads, own_clusters * picks)], axis=1)
    packed = packed.reshape(groups, own_heads, -1)

    def of_heads(hop):
        return lax.dynamic_index_in_dim(packed, (group_at + groups - hop) % groups, keepdims=False)

    arrived = [of_heads(0)] + [along_groups(of_heads(hop), -hop) for hop in range(1, groups)]
    arrived = jnp.stack(arrived)
    arrived = jnp.stack([arrived] + [along_peers(arrived, -hop) for hop in range(1, peers)], axis=1)
    ids_all = arrived[..., :rows].transpose(2, 0, 1, 3).reshape(own_heads, 1, seq)
    top_all = arrived[..., rows:].reshape(groups, peers, own_heads, own_clusters, picks)
    top_all = jnp.concatenate([top_all, top_all], axis=0)
    top_all = lax.dynamic_slice_in_dim(top_all, (groups - group_at) % groups, groups, axis=0)
    top_all = jnp.concatenate([top_all, top_all], axis=1)
    top_all = lax.dynamic_slice_in_dim(top_all, (peers - peer_at) % peers, peers, axis=1)
    top_all = top_all.transpose(2, 4, 0, 1, 3).reshape(own_heads, picks, clusters)

    mine = [tokens] + [along_groups(tokens, -hop) for hop in range(1, groups)]

    bias = prefetched(
        functools.partial(bias_kernel, groups=groups, peers=peers, rows=rows),
        (wide,),
        [whole((own_heads, picks, clusters))],
        pl.BlockSpec((own_heads, rows, clusters), lambda i, s: (0, i, 0)),
        array((own_heads, seq, clusters), BF),
        60,
        cost(own_heads * seq * clusters * picks * 8, own_heads * seq * clusters * 2),
        "bias",
    )(info, top_all)

    w_in = jnp.concatenate([w_query, w_keyval], axis=1).T.reshape(3, heads, hs, width)
    w_in = w_in.transpose(1, 0, 2, 3).reshape(groups, 3 * feats, width)
    gain_row, shift_row = gain_one[None, :], shift_one[None, :]
    shapes = [
        array((groups * rows, width), BF),
        array((own_heads, 3 * hs, seq), BF),
        array((own_heads, seq, 2 * hs), BF),
    ]
    held = []
    split_peers = peers if peers <= 2 else 1
    for group in range(groups):
        chunk = [mine[group]] + [along_peers(mine[group], -hop) for hop in range(1, peers)]
        if peers > 2:
            chunk = [jnp.concatenate(chunk, axis=0)]
        span = peers * rows
        if peers > 2:
            specs_in = [pl.BlockSpec((rows, width), lambda p, s: (p, 0))]
            grid = (peers,)
            outs = [
                pl.BlockSpec((rows, width), lambda p, s, g=group: (g, 0)),
                pl.BlockSpec((own_heads, 3 * hs, rows), lambda p, s, g=group: (0, 0, g * peers + p)),
                pl.BlockSpec((own_heads, rows, 2 * hs), lambda p, s, g=group: (0, g * peers + p, 0)),
            ]
        else:
            specs_in = [whole((rows, width))] * split_peers
            grid = (1,)
            outs = [
                pl.BlockSpec((rows, width), lambda p, s, g=group: (g, 0)),
                pl.BlockSpec((own_heads, 3 * hs, span), lambda p, s, g=group: (0, 0, g)),
                pl.BlockSpec((own_heads, span, 2 * hs), lambda p, s, g=group: (0, g, 0)),
            ]
        first = 1 + split_peers + 3
        held = prefetched(
            functools.partial(project_kernel, peers=split_peers, olds=len(held)),
            grid,
            specs_in
            + [
                whole((1, width)),
                whole((1, width)),
                pl.BlockSpec((1, 3 * feats, width), lambda p, s: (s[0], 0, 0)),
            ]
            + [pl.BlockSpec(memory_space=pl.ANY)] * len(held),
            outs,
            shapes,
            60,
            cost(6 * span * width * feats, span * width * 4),
            "project",
            alias={first + k: k for k in range(len(held))},
        )(info, *chunk, gain_row, shift_row, w_in, *held)
    hat_own, feat, kv = held

    ids_full = pl.BlockSpec((1, 1, seq), lambda h, r: (h, 0, 0))
    ids_block = pl.BlockSpec((1, 1, rows), lambda h, r: (h, 0, r * peers))
    feat_full = pl.BlockSpec((1, 3 * hs, seq), lambda h, r: (h, 0, 0))
    feat_block = pl.BlockSpec((1, 3 * hs, rows), lambda h, r: (h, 0, r * peers))
    kv_full = pl.BlockSpec((1, seq, 2 * hs), lambda h, r: (h, 0, 0))
    bias_full = pl.BlockSpec((1, seq, clusters), lambda h, r: (h, 0, 0))
    head_rows = pl.BlockSpec((hs, rows), lambda h, r: (h, 0))
    mix_spec = pl.BlockSpec((1, 1, hs + 8, rows), lambda h, r: (h, r, 0, 0))
    stat_spec = pl.BlockSpec((1, hs + 8, clusters), lambda h, r: (h, 0, 0))
    cen_spec = pl.BlockSpec((1, hs, clusters), lambda h, r: (h, 0, 0))
    own_rows = groups * rows
    pair_flops = own_heads * own_rows * seq * 256

    results = pl.pallas_call(
        functools.partial(forward_kernel, size=size, groups=groups),
        grid=(own_heads, groups),
        in_specs=[ids_full, ids_block, feat_full, feat_block, kv_full, bias_full],
        out_specs=[head_rows] * groups + [mix_spec, stat_spec, cen_spec],
        out_shape=[array((feats, rows), BF)] * groups
        + [
            array((own_heads, groups, hs + 8, rows), F32),
            array((own_heads, hs + 8, clusters), F32),
            array((own_heads, hs, clusters), BF),
        ],
        scratch_shapes=[pltpu.VMEM((hs + 8, 2 * clusters), BF)],
        compiler_params=params(60, 2),
        cost_estimate=cost(6 * pair_flops, 8e6, own_heads * own_rows * seq),
        name="attend",
    )(ids_all, ids_all, feat, feat, kv, bias)
    attn_t = results[:groups]
    mixed, stats, centroid = results[groups:]

    arrived = [attn_t[0]] + [along_groups(attn_t[hop], hop) for hop in range(1, groups)]

    chunks = 4
    part = hidden // chunks
    w_out_g = w_out.reshape(groups, feats, width)
    gain_row2, shift_row2 = gain_two[None, :], shift_two[None, :]
    square = whole((rows, width))
    column = pl.BlockSpec((rows, part), lambda i, s: (0, i))
    norm_spec = whole((8, width))
    if fast:
        half_column = pl.BlockSpec((rows, part // 2), lambda i, s: (0, i))
        kept = [array((rows, hidden // 2), BF), array((width, rows), BF)]
        kept_specs = [half_column, whole((width, rows))] * 2
        kept = kept * 2
    else:
        kept = [array((rows, hidden), BF), array((rows, width), BF)]
        kept_specs = [column, square]
    results = prefetched(
        functools.partial(block_kernel, groups=groups, chunks=chunks, fast=fast),
        (chunks,),
        [whole((feats, rows))] * groups
        + [
            square,
            whole((1, width)),
            whole((1, width)),
            whole((groups, feats, width)),
            pl.BlockSpec((width, part), lambda i, s: (0, i)),
            pl.BlockSpec((part, width), lambda i, s: (i, 0)),
            square,
        ],
        [square, square, norm_spec, column, square] + kept_specs + [whole((feats, rows))] * groups,
        [
            array((rows, width), BF),
            array((rows, width), F32),
            array((8, width), F32),
            array((rows, hidden), BF),
            array((rows, width), BF),
        ]
        + kept
        + [array((feats, rows), BF)] * groups,
        60,
        cost(8 * rows * width * hidden, 4 * width * hidden, rows * hidden),
        "feed",
        scratch=[
            pltpu.VMEM((rows, width), F32),
            pltpu.VMEM((rows, 128), F32),
            pltpu.VMEM((rows, width), BF),
            pltpu.VMEM((rows, width), F32),
            pltpu.VMEM((rows, width), F32),
        ],
    )(info, *arrived, tokens, gain_row2, shift_row2, w_out_g, w_up, w_down, cotangent)
    output, d_resid, norm_two, d_up, d_branch = results[:5]
    kept, d_attn = results[5:-groups], results[-groups:]
    grads = [d_attn[0]] + [along_groups(d_attn[hop], -hop) for hop in range(1, groups)]

    one = [
        pl.BlockSpec(spec.block_shape, functools.partial(lambda h, f: f(h, 0), f=spec.index_map))
        for spec in (ids_full, feat_full, kv_full, bias_full, stat_spec, cen_spec, head_rows)
    ]
    ids_one, feat_one, kv_one, bias_one, stat_one, cen_one, rows_one = one
    part_one = pl.BlockSpec((1, hs + 16, clusters), lambda h: (h, 0, 0))
    all_groups = pl.BlockSpec((groups, hs, rows), lambda h: (0, h, 0))
    own_one = pl.BlockSpec((1, own_rows, 2 * hs), lambda h: (h, 0, 0))

    share = pl.pallas_call(
        functools.partial(sums_kernel, groups=groups),
        grid=(own_heads,),
        in_specs=[ids_one]
        + [rows_one] * groups
        + [pl.BlockSpec((1, groups, hs + 8, rows), lambda h: (h, 0, 0, 0))],
        out_specs=part_one,
        out_shape=array((own_heads, hs + 16, clusters), F32),
        compiler_params=params(60, 1),
        cost_estimate=cost(own_heads * own_rows * clusters * 160, 2e6),
        name="sums",
    )(ids_all, *grads, mixed)
    share_got = [along_peers(share, hop) for hop in range(1, peers)]

    def weight_sums():
        dup_got, dbr_got = along_peers(d_up, 1), along_peers(d_branch, 1)
        act_own, low_own, act_far, low_far = kept
        act_got, low_got = along_peers(act_far, 1), along_peers(low_far, 1)
        cot_got, dn_got = along_peers(cotangent, 1), along_peers(norm_two, 1)
        high = block_rows + block_rows // 4 + 8
        chunk = pl.BlockSpec((rows, part), lambda i, s: (0, i ^ 2 ^ s[3]))
        act_spec = pl.BlockSpec((rows, part // 2), lambda i, s: (0, i))
        low_spec = whole((width, rows))
        shape_u = (2, groups, high, width)
        shape_d = (2, groups, block_rows, width)
        send_u, keep_u, send_d, keep_d = prefetched(
            functools.partial(weights_kernel, groups=groups),
            (4,),
            [chunk, chunk, square, square, act_spec, act_spec, low_spec, low_spec, square, square]
            + [norm_spec] * 2,
            [
                pl.BlockSpec((1,) + shape_u[1:], lambda i, s: (jnp.minimum(i, 1), 0, 0, 0)),
                pl.BlockSpec((1,) + shape_u[1:], lambda i, s: (jnp.maximum(i - 2, 0), 0, 0, 0)),
                whole(shape_d),
                whole(shape_d),
            ],
            [array(shape_u, BF), array(shape_u, BF), array(shape_d, BF), array(shape_d, BF)],
            60,
            cost(8 * rows * width * hidden, 6 * width * hidden),
            "weights",
            scratch=[pltpu.VMEM((groups, block_rows, width), F32)],
        )(
            info, d_up, dup_got, d_branch, dbr_got, act_own, act_got, low_own, low_got,
            cotangent, cot_got, norm_two, dn_got,
        )
        got_u, got_d = along_dp(send_u, 1), along_dp(send_d, 2)

        def block(shape, at):
            return pl.BlockSpec((1,) + shape[1:], lambda i: (at, 0, 0, 0))

        next_u, next_d = pl.pallas_call(
            second_kernel,
            grid=(1,),
            in_specs=[block(shape_u, 1), block(shape_u, 1), block(shape_d, 1), block(shape_d, 1)],
            out_specs=[whole(shape_u[1:]), whole(shape_d[1:])],
            out_shape=[array(shape_u[1:], BF), array(shape_d[1:], BF)],
            compiler_params=params(60, 1),
            cost_estimate=cost(groups * high * width * 2, groups * high * width * 12),
            name="second",
        )(keep_u, got_u, keep_d, got_d)
        last_u, last_d = along_dp(next_u, 2), along_dp(next_d, 1)
        tall = high + block_rows
        sums = pl.pallas_call(
            third_kernel,
            grid=(1,),
            in_specs=[
                block(shape_u, 0),
                block(shape_u, 0),
                whole(shape_u[1:]),
                block(shape_d, 0),
                block(shape_d, 0),
                whole(shape_d[1:]),
            ],
            out_specs=[whole((tall, width))] * groups,
            out_shape=[array((tall, width), BF)] * groups,
            compiler_params=params(60, 1),
            cost_estimate=cost(groups * tall * width * 4, groups * tall * width * 8),
            name="third",
        )(keep_u, got_u, last_u, keep_d, got_d, last_d)
        came = [sums[0]] + [along_groups(sums[hop], hop) for hop in range(1, groups)]
        done = pl.pallas_call(
            fourth_kernel,
            grid=(1,),
            in_specs=[whole((tall, width))] * groups,
            out_specs=whole((tall, width)),
            out_shape=array((tall, width), BF),
            compiler_params=params(60, 1),
            cost_estimate=cost(groups * tall * width, groups * tall * width * 2),
            name="fourth",
        )(*came)
        from_x, from_y, from_xy = (along_dp(done, mask) for mask in (1, 2, 3))
        quarter = block_rows // 4
        total_up, total_out, total_down, norms = prefetched(
            spread_kernel,
            (4,),
            [whole((tall, width))] * 4,
            [
                pl.BlockSpec((block_rows, part), lambda i, s: (0, i ^ s[3])),
                pl.BlockSpec((quarter, width), lambda i, s: (i ^ s[3], 0)),
                pl.BlockSpec((block_rows, width), lambda i, s: (i ^ s[4], 0)),
                whole((8, width)),
            ],
            [
                array((block_rows, hidden), F32),
                array((block_rows, width), F32),
                array((hidden // wide, width), F32),
                array((8, width), F32),
            ],
            60,
            cost(1e6, 4 * tall * width * 6),
            "spread",
        )(info, done, from_x, from_y, from_xy)
        norm_own = lax.dynamic_slice_in_dim(norms, me * block_rows, block_rows, axis=1)
        return total_up, total_out, total_down, norm_own

    masks = [1 << k for k in range(n_dp.bit_length() - 1)]

    def reduce_rows(partial):
        blocks = partial.reshape(groups, peers, partial.shape[0] // wide, partial.shape[1])

        def of_peer(hop):
            at = (peer_at + hop) % peers
            return lax.dynamic_index_in_dim(blocks, at, axis=1, keepdims=False)

        total = of_peer(0).astype(F32)
        for hop in range(1, peers):
            total = total + along_peers(of_peer(hop), hop).astype(F32)
        total = total.astype(BF)

        def of_group(hop):
            return lax.dynamic_index_in_dim(total, (group_at + hop) % groups, keepdims=False)

        done = of_group(0).astype(F32)
        for hop in range(1, groups):
            done = done + along_groups(of_group(hop), hop).astype(F32)
        for mask in masks:
            done = done.astype(BF)
            done = done.astype(F32) + along_dp(done, mask).astype(F32)
        return done

    if fast:
        total_up, total_out, total_down, norm_own = weight_sums()
    else:
        act, normed_two = kept
        total_up = reduce_rows(tn(normed_two, d_up).astype(BF))
        total_down = reduce_rows(tn(act, cotangent).astype(BF))
        found = jnp.stack([nn(item, d_branch).astype(BF) for item in arrived])
        found = [
            lax.dynamic_index_in_dim(found, (group_at + groups - g) % groups, keepdims=False)
            for g in range(groups)
        ]
        total_out = reduce_rows(jnp.concatenate(found, axis=0))
        norm_own = reduce_rows(norm_two[:2].T.astype(BF)).T

    dq_member, dkv_own, dkv_send = pl.pallas_call(
        functools.partial(member_kernel, size=size, groups=groups),
        grid=(own_heads, groups),
        in_specs=[ids_block, feat_full, feat_block, kv_full, bias_full]
        + [head_rows] * groups
        + [mix_spec, stat_spec],
        out_specs=[
            pl.BlockSpec((1, hs, rows), lambda h, r: (r, h, 0)),
            pl.BlockSpec((1, own_rows, 2 * hs), lambda h, r: (h, 0, 0)),
            pl.BlockSpec((1, max(peers - 1, 1) * own_rows, 2 * hs), lambda h, r: (h, 0, 0)),
        ],
        out_shape=[
            array((groups, feats, rows), F32),
            array((own_heads, own_rows, 2 * hs), F32),
            array((own_heads, max(peers - 1, 1) * own_rows, 2 * hs), BF),
        ],
        scratch_shapes=[pltpu.VMEM((seq, 2 * hs), F32), pltpu.VMEM((hs, rows), BF)],
        compiler_params=params(60, 2),
        cost_estimate=cost(12 * pair_flops, 10e6, own_heads * own_rows * seq),
        name="member",
    )(ids_all, feat, feat, kv, bias, *grads, mixed, stats)
    dkv_got = [
        along_peers(
            dkv_send if peers == 2 else dkv_send[:, (hop - 1) * own_rows : hop * own_rows], hop
        )
        for hop in range(1, peers)
    ]
    share_total = share
    for got in share_got:
        share_total = share_total + got

    d_in = pl.pallas_call(
        functools.partial(centroid_kernel, size=size, groups=groups, gots=len(dkv_got)),
        grid=(own_heads,),
        in_specs=[ids_one, feat_one, kv_one, bias_one, part_one, stat_one, cen_one, all_groups]
        + [own_one] * (1 + len(dkv_got)),
        out_specs=[pl.BlockSpec((1, 3 * hs, rows), lambda h: (h, 0, 0))] * groups,
        out_shape=[array((own_heads, 3 * hs, rows), BF)] * groups,
        scratch_shapes=[pltpu.VMEM((seq, 2 * clusters), BF)],
        compiler_params=params(60, 1),
        cost_estimate=cost(own_heads * clusters * seq * 1024, 8e6, own_heads * clusters * seq),
        name="centroid",
    )(ids_all, feat, kv, bias, share_total, stats, centroid, dq_member, dkv_own, *dkv_got)

    home = [d_in[0]] + [along_groups(d_in[hop], hop) for hop in range(1, groups)]

    tall = block_rows + 16
    part_spec = [whole((own_heads, 3 * hs, rows))] * groups + [whole((own_rows, width))]
    inward = functools.partial(
        prefetched,
        functools.partial(inward_kernel, groups=groups, fast=fast),
        (1,),
        part_spec,
    )
    spent = cost(2 * own_rows * width * 3 * feats, 4e6)
    if fast:
        half = groups // 2
        blocks = (groups, tall, 3 * feats)
        keep, far = inward(
            [whole(blocks)] * 2, [array(blocks, BF)] * 2, 60, spent, "inward"
        )(info, *d_in, hat_own)
        got = along_peers(far, 1)
        total = keep.astype(F32) + got.astype(F32)
        one_half, two_half = total[:half].astype(BF), total[half:].astype(BF)
        for mask in (1, 2):
            got_one, got_two = along_dp(one_half, mask), along_dp(two_half, 3 - mask)
            one_half = (one_half.astype(F32) + got_one.astype(F32)).astype(BF)
            two_half = (two_half.astype(F32) + got_two.astype(F32)).astype(BF)
        items = [one_half[k] for k in range(half)] + [two_half[k] for k in range(half)]
    else:
        found, more = inward(
            [whole((width, 3 * feats)), whole((16, 3 * feats))],
            [array((width, 3 * feats), F32), array((16, 3 * feats), F32)],
            60,
            spent,
            "inward",
        )(info, *d_in, hat_own)
        found = found.reshape(groups, peers, block_rows, 3 * feats)
        more = jnp.broadcast_to(more, (groups, peers, 16, 3 * feats))
        found = jnp.concatenate([found, more], axis=2).astype(BF)

        def of_peer(hop):
            at = (peer_at + hop) % peers
            return lax.dynamic_index_in_dim(found, at, axis=1, keepdims=False)

        total = of_peer(0).astype(F32)
        for hop in range(1, peers):
            total = total + along_peers(of_peer(hop), hop).astype(F32)
        for mask in masks:
            total = total.astype(BF)
            total = total.astype(F32) + along_dp(total, mask).astype(F32)
        total = total.astype(BF)
        items = [
            lax.dynamic_index_in_dim(total, (group_at + hop) % groups, keepdims=False)
            for hop in range(groups)
        ]
    pieces = [items[0]] + [along_groups(items[hop], hop) for hop in range(1, groups)]

    grad_tokens = prefetched(
        functools.partial(final_kernel, groups=groups),
        (1,),
        [whole((own_heads, 3 * hs, rows))] * groups
        + [square, square, whole((1, width)), whole((groups, 3 * feats, width))],
        square,
        array((rows, width), BF),
        60,
        cost(6 * rows * width * width, 6 * width * width),
        "final",
    )(info, *home, tokens, d_resid, gain_row, w_in)

    pieces = jnp.stack(pieces)
    pieces = jnp.stack(
        [
            lax.dynamic_index_in_dim(pieces, (group_at + groups - g) % groups, keepdims=False)
            for g in range(groups)
        ]
    ).astype(F32)
    q_part = pieces[:, :, :feats].transpose(1, 0, 2).reshape(tall, width)
    kv_part = (
        pieces[:, :, feats:]
        .reshape(groups, tall, 2, feats)
        .transpose(1, 2, 0, 3)
        .reshape(tall, 2 * width)
    )
    at = me * block_rows
    wq_rows = lax.dynamic_slice_in_dim(w_query, at, block_rows).astype(F32)
    wkv_rows = lax.dynamic_slice_in_dim(w_keyval, at, block_rows).astype(F32)
    gain_own = lax.dynamic_slice_in_dim(gain_one, at, block_rows)
    shift_own = lax.dynamic_slice_in_dim(shift_one, at, block_rows)
    q_sum, kv_sum = q_part[block_rows], kv_part[block_rows]
    q_part, kv_part = q_part[:block_rows], kv_part[:block_rows]
    shift_grad = jnp.sum(wq_rows * q_sum, axis=1) + jnp.sum(wkv_rows * kv_sum, axis=1)
    along = jnp.sum(wq_rows * q_part, axis=1) + jnp.sum(wkv_rows * kv_part, axis=1)
    return (
        output,
        grad_tokens,
        q_part + shift_own[:, None] * q_sum,
        kv_part + shift_own[:, None] * kv_sum,
        total_out,
        total_up,
        total_down,
        along / gain_own,
        shift_grad,
        norm_own[0],
        norm_own[1],
    )


def solution(mesh):
    return jax.shard_map(
        per_device,
        mesh=mesh,
        in_specs=(
            P(("dp", "wide"), None),
            P(("dp", "wide"), None),
            P("dp"),
            P("dp", None, "wide", None),
            P(),
            P(),
            P(),
            P(),
            P(),
            P(),
            P(),
            P(),
            P(),
            P(("dp", "wide"), None),
        ),
        out_specs=(
            P(("dp", "wide"), None),
            P(("dp", "wide"), None),
            P("wide", None),
            P("wide", None),
            P("wide", None),
            P("wide", None),
            P("wide", None),
            P("wide"),
            P("wide"),
            P("wide"),
            P("wide"),
        ),
        check_vma=False,
    )
```

```python
import functools
import math

import jax
import jax.numpy as jnp
import numpy as np
from jax import lax
from jax.experimental import pallas as pl
from jax.experimental.pallas import tpu as pltpu
from jax.sharding import PartitionSpec as P

EPSILON = 1e-05
NEGATIVE = -1e30
EXCLUDED = -3e30
GELU_A = math.sqrt(2.0 / math.pi)
GELU_B = 0.044715
BF = jnp.bfloat16
F32 = jnp.float32


def nn(left, right):
    return lax.dot_general(left, right, (((1,), (0,)), ((), ())), preferred_element_type=F32)


def nt(left, right):
    return lax.dot_general(left, right, (((1,), (1,)), ((), ())), preferred_element_type=F32)


def tn(left, right):
    return lax.dot_general(left, right, (((0,), (0,)), ((), ())), preferred_element_type=F32)


def params(mib, dims):
    return pltpu.CompilerParams(
        vmem_limit_bytes=mib * 1024 * 1024, dimension_semantics=("arbitrary",) * dims
    )


def cost(flops, nbytes, trans=0):
    return pl.CostEstimate(flops=int(flops), bytes_accessed=int(nbytes), transcendentals=int(trans))


def split_low(values):
    high = values.astype(BF)
    return high, (values - high.astype(F32)).astype(BF)


def one_hot_t(ids_row, clusters):
    rows = lax.broadcasted_iota(jnp.int32, (clusters, ids_row.shape[1]), 0)
    return jnp.where(rows == ids_row, 1.0, 0.0).astype(BF)


def key_passes(total, size, score, weigh, blocks=None):
    count = total // size
    if count <= 4:
        if blocks is None:
            blocks = [score(index) for index in range(count)]
        peak = functools.reduce(jnp.maximum, [jnp.max(b, axis=0, keepdims=True) for b in blocks])
        denom, sums = 0.0, None
        for index in range(count):
            expo = jnp.exp(blocks[index] - peak)
            denom = denom + jnp.sum(expo, axis=0, keepdims=True)
            parts = weigh(index, expo)
            sums = parts if sums is None else tuple(x + y for x, y in zip(sums, parts))
        return peak, denom, sums

    def step(index, carry):
        peak, denom, sums = carry
        block = score(index)
        fresh = jnp.maximum(peak, jnp.max(block, axis=0, keepdims=True))
        expo = jnp.exp(block - fresh)
        fade = jnp.exp(peak - fresh)
        parts = weigh(index, expo)
        return (
            fresh,
            denom * fade + jnp.sum(expo, axis=0, keepdims=True),
            tuple(old * fade + new for old, new in zip(sums, parts)),
        )

    shapes = jax.eval_shape(lambda: (score(0), weigh(0, score(0))))
    lanes = shapes[0].shape[1]
    start = (
        jnp.full((1, lanes), NEGATIVE, F32),
        jnp.zeros((1, lanes), F32),
        tuple(jnp.zeros(item.shape, F32) for item in shapes[1]),
    )
    return lax.fori_loop(0, count, step, start)


def key_sum(total, size, step, start):
    count = total // size
    if count <= 4:
        for index in range(count):
            start = step(index, start)
        return start
    return lax.fori_loop(0, count, step, start)


def spot_of(index, size):
    if isinstance(index, int):
        return pl.ds(index * size, size)
    return pl.ds(pl.multiple_of(index * size, size), size)


def piece(ref, index, size, axis):
    spot = spot_of(index, size)
    return ref[spot, :] if axis == 0 else ref[:, spot]


def bias_kernel(info, top_ref, bias_ref, *, groups, peers, rows):
    part = pl.program_id(0)
    owner = (
        lax.rem(info[0] + part // peers, groups) * peers + lax.rem(info[1] + part % peers, peers)
    )
    heads, picks, clusters = top_ref.shape
    place = owner * rows + lax.broadcasted_iota(jnp.int32, (rows, clusters), 0)
    plain = jnp.where(place >= info[2], EXCLUDED, NEGATIVE)
    for head in range(heads):
        top = top_ref[head]
        value = plain
        for pick in range(picks):
            value = jnp.where(place == top[pick : pick + 1, :], 0.0, value)
        bias_ref[head] = value.astype(BF)


def project_kernel(info, *refs, peers, olds):
    parts = refs[:peers]
    gain_ref, shift_ref, w_ref = refs[peers : peers + 3]
    hat_ref, feat_ref, kv_ref = refs[peers + 3 + olds :]
    rows = hat_ref.shape[1]
    for peer in range(peers):
        values = parts[peer][...].astype(F32)
        centered = values - jnp.mean(values, axis=-1, keepdims=True)
        variance = jnp.mean(centered * centered, axis=-1, keepdims=True)
        scaled = centered * lax.rsqrt(variance + EPSILON) * gain_ref[...]
        if peer == 0:
            hat_ref[...] = scaled.astype(BF).T
        low = (scaled + shift_ref[...]).astype(BF)
        found = nt(w_ref[0], low)
        heads, triple = feat_ref.shape[0], feat_ref.shape[1]
        hs = triple // 3
        spot = slice(peer * rows, (peer + 1) * rows)
        for head in range(heads):
            base = head * triple
            query = (found[base : base + hs] * 0.125).astype(BF)
            pair = found[base + hs : base + triple].astype(BF)
            feat_ref[head, :hs, spot] = query
            feat_ref[head, hs:, spot] = pair
            kv_ref[head, spot, :] = pair.T


def forward_kernel(ids_all, feat, kv, bias, *refs, size, groups, rows):
    outs = refs[:groups]
    mix_ref, stat_ref, cen_ref = refs[groups:]
    hs = feat.shape[1] // 3
    keys = kv.shape[1]
    count = keys // size
    clusters = bias.shape[2]
    kv_h, bias_h = kv.at[0], bias.at[0]
    queries_all, kvt = feat.at[0, :hs], feat.at[0, hs:]
    hot_all = one_hot_t(ids_all[0], clusters)
    ones = jnp.ones((16, keys), BF)
    sums = nt(jnp.concatenate([queries_all[...], ones], axis=0), hot_all)
    counts = sums[hs : hs + 1]
    centroid = (sums[:hs] / jnp.maximum(counts, 1.0)).astype(BF)
    padded = jnp.concatenate([centroid, jnp.zeros_like(centroid)], axis=0)

    def cluster_score(index):
        scores = nn(piece(kv_h, index, size, 0), padded)
        outside = piece(bias_h, index, size, 0).astype(F32) < 2.0 * NEGATIVE
        return jnp.where(outside, NEGATIVE, scores)

    def cluster_weigh(index, expo):
        top = piece(bias_h, index, size, 0).astype(F32) == 0.0
        mass = jnp.sum(jnp.where(top, expo, 0.0), axis=0, keepdims=True)
        other = jnp.where(top, 0.0, expo).astype(BF)
        return nn(piece(kvt, index, size, 1), other), mass

    peers = keys // (groups * rows)
    hots, sides = [], []
    for group in range(groups):
        spot = slice(group * peers * rows, group * peers * rows + rows)
        hot = one_hot_t(ids_all[0, :, spot], clusters)
        queries = queries_all[:, spot]
        hots.append(hot)
        sides.append(jnp.concatenate([queries, jnp.zeros_like(queries), hot], axis=0))

    def member_score(group, index):
        both = jnp.concatenate([piece(kv_h, index, size, 0), piece(bias_h, index, size, 0)], axis=1)
        return nn(both, sides[group])

    def member_weigh(index, expo):
        return (nn(piece(kvt, index, size, 1), expo.astype(BF)),)

    short = count <= 4
    ahead = None
    if short:
        ahead = [member_score(0, index) for index in range(count)]
    peak, denom, (rest, mass) = key_passes(keys, size, cluster_score, cluster_weigh)
    rest = rest[hs:] / denom
    mass = mass / denom
    blank = jnp.zeros((5, clusters), F32)
    stats = jnp.concatenate([rest, mass, peak + jnp.log(denom), counts, blank], axis=0)
    stat_ref[0] = stats
    cen_ref[0] = centroid
    high, low = split_low(stats)
    table = jnp.concatenate([high, low], axis=1)
    for group in range(groups):
        gathered = nn(table, jnp.concatenate([hots[group], hots[group]], axis=0))
        blocks, ahead = ahead, None
        if short and group + 1 < groups:
            ahead = [member_score(group + 1, index) for index in range(count)]
        score = functools.partial(member_score, group)
        peak, denom, (mix,) = key_passes(keys, size, score, member_weigh, blocks)
        mix = mix[hs:] / denom
        outs[group][...] = (gathered[hs : hs + 1] * mix + gathered[:hs]).astype(BF)
        level = jnp.broadcast_to(peak + jnp.log(denom), (8, rows))
        mix_ref[0, group] = jnp.concatenate([mix, level], axis=0)


def sums_kernel(ids_own, *refs, groups):
    grads, (mix_ref, part_ref) = refs[:groups], refs[groups:]
    hs = grads[0].shape[0]
    total = None
    for group in range(groups):
        rows = grads[group].shape[1]
        step = ids_own.shape[2] // groups
        hot = one_hot_t(ids_own[0, :, group * step : group * step + rows], part_ref.shape[2])
        grad = grads[group][...]
        along = jnp.sum(grad.astype(F32) * mix_ref[0, group, :hs], axis=0, keepdims=True)
        high, low = split_low(along)
        pad = jnp.zeros((14, rows), BF)
        part = nt(jnp.concatenate([grad, high, low, pad], axis=0), hot)
        total = part if total is None else total + part
    part_ref[0] = total


def member_kernel(ids_all, feat, kv, bias, *refs, size, groups):
    grads = refs[:groups]
    mix_ref, stat_ref, dq_ref, own_ref, send_ref, total = refs[groups:]
    hs, rows = grads[0].shape
    keys = kv.shape[1]
    count = keys // size
    peers = keys // (groups * rows)
    clusters = bias.shape[2]
    kv_h, bias_h = kv.at[0], bias.at[0]
    queries_all, kvt = feat.at[0, :hs], feat.at[0, hs:]
    high, low = split_low(stat_ref[0, hs : hs + 8, :])
    table = jnp.concatenate([high, low], axis=1)
    sides, levels, deltas, pads, rights = [], [], [], [], []
    for group in range(groups):
        spot = slice(group * peers * rows, group * peers * rows + rows)
        hot = one_hot_t(ids_all[0, :, spot], clusters)
        queries = queries_all[:, spot]
        blank = jnp.zeros_like(queries)
        sides.append(jnp.concatenate([queries, blank, hot], axis=0))
        mass = nn(table, jnp.concatenate([hot, hot], axis=0))[0:1]
        back = (mass * grads[group][...].astype(F32)).astype(BF)
        levels.append(mix_ref[0, group, hs : hs + 1])
        deltas.append(jnp.sum(back.astype(F32) * mix_ref[0, group, :hs], axis=0, keepdims=True))
        pads.append(jnp.concatenate([blank, back], axis=0))
        turned = jnp.concatenate([queries, blank], axis=0)
        rights.append(jnp.concatenate([turned, pads[group]], axis=1).T)

    def scores(group, index):
        kv_c = piece(kv_h, index, size, 0)
        both = jnp.concatenate([kv_c, piece(bias_h, index, size, 0)], axis=1)
        return nn(both, sides[group]), nn(kv_c, pads[group])

    def finish(group, index, found, dq):
        weights = jnp.exp(found[0] - levels[group])
        grad_s = (weights * (found[1] - deltas[group])).astype(BF)
        part = nn(jnp.concatenate([grad_s, weights.astype(BF)], axis=1), rights[group])
        spot = spot_of(index, size)
        if group == 0:
            total[spot, :] = part
        else:
            total[spot, :] += part
        return dq + nn(piece(kvt, index, size, 1), grad_s)

    start = jnp.zeros((2 * hs, rows), F32)
    if count <= 4:
        tasks = [(group, index) for group in range(groups) for index in range(count)]
        ahead = scores(*tasks[0])
        dq = start
        for step, (group, index) in enumerate(tasks):
            found = ahead
            if step + 1 < len(tasks):
                ahead = scores(*tasks[step + 1])
            dq = finish(group, index, found, dq)
            if index == count - 1:
                dq_ref[group] = dq[:hs] * 0.125
                dq = start
    else:
        for group in range(groups):

            def step(index, dq, group=group):
                return finish(group, index, scores(group, index), dq)

            dq_ref[group] = lax.fori_loop(0, count, step, start)[:hs] * 0.125
    for group in range(groups):
        base = group * peers * rows
        own_ref[0, group * rows : (group + 1) * rows, :] = total[base : base + rows, :]
        for peer in range(1, peers):
            spot = (peer - 1) * groups * rows + group * rows
            found = total[base + peer * rows : base + (peer + 1) * rows, :]
            send_ref[0, spot : spot + rows, :] = found.astype(BF)


def centroid_kernel(ids_own, feat_all, kv, bias, part_ref, stat_ref, cen_ref, dqm_ref, own_ref, *refs, size, groups, gots):
    got_refs = refs[:gots]
    outs, both = refs[gots : gots + groups], refs[gots + groups]
    hs, rows = cen_ref.shape[1], outs[0].shape[2]
    keys = kv.shape[1]
    peers = keys // (groups * rows)
    clusters = bias.shape[2]
    kv_h, bias_h, kvt = kv.at[0], bias.at[0], feat_all.at[0, hs:]
    stats = stat_ref[0]
    rest, mass = stats[:hs], stats[hs : hs + 1]
    level, counts = stats[hs + 1 : hs + 2], stats[hs + 2 : hs + 3]
    centroid = cen_ref[0]
    blank = jnp.zeros_like(centroid)
    part = part_ref[0]
    d_rest = part[:hs].astype(BF)
    d_mass = part[hs : hs + 1] + part[hs + 1 : hs + 2]
    delta = jnp.sum(d_rest.astype(F32) * rest, axis=0, keepdims=True) + d_mass * mass
    cen_pad = jnp.concatenate([centroid, blank], axis=0)
    rest_pad = jnp.concatenate([blank, d_rest], axis=0)
    right = jnp.concatenate([cen_pad, rest_pad], axis=1).T

    def step(index, total):
        kv_c = piece(kv_h, index, size, 0)
        marks = piece(bias_h, index, size, 0).astype(F32)
        scores = nn(kv_c, cen_pad)
        probs = jnp.where(marks < 2.0 * NEGATIVE, 0.0, jnp.exp(scores - level))
        top = marks == 0.0
        d_probs = jnp.where(top, d_mass, nn(kv_c, rest_pad))
        d_score = (probs * (d_probs - delta)).astype(BF)
        other = jnp.where(top, 0.0, probs).astype(BF)
        both[spot_of(index, size), :] = jnp.concatenate([d_score, other], axis=1)
        return total + nn(piece(kvt, index, size, 1), d_score)

    d_cen = key_sum(keys, size, step, jnp.zeros((2 * hs, clusters), F32))
    d_cen = d_cen[:hs] * 0.125 / jnp.maximum(counts, 1.0)
    high, low = split_low(d_cen)
    table = jnp.concatenate([high, low], axis=1)
    for group in range(groups):
        spot = group * peers * rows
        hot = one_hot_t(ids_own[0, :, spot : spot + rows], clusters)
        spread = nn(table, jnp.concatenate([hot, hot], axis=0))
        own = nn(both[spot : spot + rows, :], right) + own_ref[0, group * rows : (group + 1) * rows, :]
        for got in got_refs:
            own = own + got[0, group * rows : (group + 1) * rows, :].astype(F32)
        outs[group][0, :hs] = (dqm_ref[group] + spread).astype(BF)
        outs[group][0, hs:] = own.T.astype(BF)


def block_kernel(info, *refs, groups, chunks, fast):
    (attn, rest) = (refs[:groups], refs[groups:])
    x_ref, gain_ref, shift_ref, wo_ref, up_ref, down_ref, cot_ref = rest[:7]
    out_ref, dres_ref, dn_ref, dup_ref, dbr_ref, act_ref, low_ref = rest[7:14]
    rest = rest[14:]
    if fast:
        act_far, low_far = rest[:2]
        rest = rest[2:]
    dat = rest[:groups]
    hat_ref, inv_ref, normed, back, total = rest[groups:]
    index = pl.program_id(0)

    @pl.when(index == 0)
    def before():
        resid = x_ref[...].astype(F32)
        for group in range(groups):
            owner = lax.rem(info[0] + groups - group, groups)
            resid = resid + tn(attn[group][...], wo_ref[owner])
        total[...] = resid
        centered = resid - jnp.mean(resid, axis=-1, keepdims=True)
        variance = jnp.mean(centered * centered, axis=-1, keepdims=True)
        inverse = lax.rsqrt(variance + EPSILON)
        hat = centered * inverse
        hat_ref[...] = hat
        inv_ref[...] = jnp.broadcast_to(inverse, inv_ref.shape)
        low = (hat * gain_ref[...] + shift_ref[...]).astype(BF)
        normed[...] = low
        if fast:
            feats = attn[0].shape[0]
            half = feats // 2
            turned = low.T
            for group in range(groups):
                first = turned[group * feats : group * feats + half]
                second = turned[group * feats + half : (group + 1) * feats]
                spot = slice(group * half, (group + 1) * half)
                low_ref[spot, :] = jnp.where(info[1] == 0, first, second)
                low_far[spot, :] = jnp.where(info[1] == 0, second, first)
                first = attn[group][:half]
                second = attn[group][half:]
                spot = slice((groups + group) * half, (groups + group + 1) * half)
                low_ref[spot, :] = jnp.where(info[1] == 0, first, second)
                low_far[spot, :] = jnp.where(info[1] == 0, second, first)
        else:
            low_ref[...] = low
        back[...] = jnp.zeros_like(back)

    up = nn(normed[...], up_ref[...])
    grad_act = nt(cot_ref[...], down_ref[...])
    square = up * up
    inner = GELU_A * (up + GELU_B * up * square)
    curve = jnp.tanh(inner)
    act = (0.5 * up * (1.0 + curve)).astype(BF)
    slope = 0.5 * (1.0 + curve) + 0.5 * up * (1.0 - curve * curve) * (
        GELU_A * (1.0 + 3.0 * GELU_B * square)
    )
    d_up = (grad_act * slope).astype(BF)
    dup_ref[...] = d_up
    if fast:
        half = act.shape[1] // 2
        first, second = act[:, :half], act[:, half:]
        act_ref[...] = jnp.where(info[1] == 0, first, second)
        act_far[...] = jnp.where(info[1] == 0, second, first)
    else:
        act_ref[...] = act
    back[...] += nt(d_up, up_ref[...])
    total[...] += nn(act, down_ref[...])

    @pl.when(index == chunks - 1)
    def after():
        out_ref[...] = total[...].astype(BF)
        d_normed = back[...]
        hat = hat_ref[...]
        gain_part = jnp.sum(d_normed * hat, axis=0, keepdims=True)
        shift_part = jnp.sum(d_normed, axis=0, keepdims=True)
        blank = jnp.zeros((6, d_normed.shape[1]), F32)
        dn_ref[...] = jnp.concatenate([gain_part, shift_part, blank], axis=0)
        gy = d_normed * gain_ref[...]
        mean_one = jnp.mean(gy, axis=-1, keepdims=True)
        mean_two = jnp.mean(gy * hat, axis=-1, keepdims=True)
        d_resid = cot_ref[...].astype(F32) + inv_ref[:, 0:1] * (gy - mean_one - hat * mean_two)
        dres_ref[...] = d_resid
        branch = d_resid.astype(BF)
        dbr_ref[...] = branch
        for group in range(groups):
            owner = lax.rem(info[0] + groups - group, groups)
            dat[group][...] = nt(wo_ref[owner], branch).astype(BF)


def weights_kernel(info, *refs, groups):
    (dup, dup_got, dbr, dbr_got, act, act_got, low, low_got, cot, cot_got, dn, dn_got) = refs[:12]
    send_u, keep_u, send_d, keep_d, outs = refs[12:]
    index = pl.program_id(0)
    group_at, place_u, place_d = info[0], info[3], info[4]
    rows = low.shape[0] // (2 * groups)
    quarter = rows // 4
    stay = groups * rows

    @pl.when(index == 0)
    def first():
        found = nn(low[stay:, :], dbr[...]) + nn(low_got[stay:, :], dbr_got[...])
        for group in range(groups):
            outs[group] = found[group * rows : (group + 1) * rows]

    up = nn(low[:stay, :], dup[...]) + nn(low_got[:stay, :], dup_got[...])
    at = lax.bitwise_xor(lax.bitwise_xor(index, 2), place_u)
    norms = dn[...] + dn_got[...]
    for group in range(groups):
        spot = lax.rem(group + groups - group_at, groups)
        block = up[group * rows : (group + 1) * rows].astype(BF)
        away = (groups - group) % groups
        start = pl.multiple_of(at * quarter, 8)
        other = jnp.concatenate([outs[group, pl.ds(start, quarter), :], norms], axis=0).astype(BF)

        @pl.when(index < 2)
        def leaves():
            send_u[0, spot, :rows] = block
            send_u[0, away, rows:] = other

        @pl.when(index >= 2)
        def stays():
            keep_u[0, spot, :rows] = block
            keep_u[0, away, rows:] = other

    down = tn(act[...], cot[...]) + tn(act_got[...], cot_got[...])
    spot = lax.rem(index + groups - group_at, groups)
    for part in range(4):
        block = down[part * rows : (part + 1) * rows].astype(BF)
        place = lax.bitwise_xor(part, place_d)

        @pl.when(place >= 2)
        def leaves_down():
            send_d[place - 2, spot] = block

        @pl.when(place < 2)
        def stays_down():
            keep_d[place, spot] = block


def second_kernel(keep_u, got_u, keep_d, got_d, send_u, send_d):
    send_u[...] = (keep_u[0].astype(F32) + got_u[0].astype(F32)).astype(BF)
    send_d[...] = (keep_d[0].astype(F32) + got_d[0].astype(F32)).astype(BF)


def third_kernel(keep_u, got_u, last_u, keep_d, got_d, last_d, *outs):
    rows = keep_u.shape[2]
    for group in range(len(outs)):
        up = keep_u[0, group].astype(F32) + got_u[0, group].astype(F32) + last_u[group].astype(F32)
        down = keep_d[0, group].astype(F32) + got_d[0, group].astype(F32) + last_d[group].astype(F32)
        outs[group][:rows] = up.astype(BF)
        outs[group][rows:] = down.astype(BF)


def fourth_kernel(*refs):
    parts, out = refs[:-1], refs[-1]
    total = parts[0][...].astype(F32)
    for part in parts[1:]:
        total = total + part[...].astype(F32)
    out[...] = total.astype(BF)


def spread_kernel(info, own, from_x, from_y, from_xy, up_ref, out_ref, down_ref, norm_ref):
    index = pl.program_id(0)
    rows = up_ref.shape[0]
    quarter = out_ref.shape[0]
    top = rows + quarter + 8
    for place, part in enumerate((own, from_y, from_x, from_xy)):

        @pl.when(index == place)
        def upper(part=part):
            up_ref[...] = part[:rows].astype(F32)
            tail = part[rows:top].astype(F32)
            out_ref[...] = tail[:quarter]

            @pl.when(lax.bitwise_xor(index, info[3]) == 0)
            def norms():
                norm_ref[...] = tail[quarter:]

    for place, part in enumerate((own, from_x, from_y, from_xy)):

        @pl.when(index == place)
        def lower(part=part):
            down_ref[...] = part[top:].astype(F32)


def inward_kernel(info, *refs, groups, fast):
    parts, hat_ref = refs[:groups], refs[groups]
    outs = refs[groups + 1 :]
    heads, triple, rows = parts[0].shape
    hs = triple // 3
    total, sums = None, None
    ones = jnp.ones((16, rows), BF)
    for group in range(groups):
        order = [parts[group][h, k * hs : (k + 1) * hs] for k in range(3) for h in range(heads)]
        turned = jnp.concatenate(order, axis=0)
        found = nt(hat_ref[:, group * rows : (group + 1) * rows], turned)
        more = nt(ones, turned)
        total = found if total is None else total + found
        sums = more if sums is None else sums + more
    if not fast:
        outs[0][...] = total
        outs[1][...] = sums
        return
    own_ref, far_ref = outs
    block = total.shape[0] // (2 * groups)
    low_sums = sums.astype(BF)
    for group in range(groups):
        spot = lax.rem(group + groups - info[0], groups)
        first = total[2 * group * block : (2 * group + 1) * block].astype(BF)
        second = total[(2 * group + 1) * block : (2 * group + 2) * block].astype(BF)
        own_ref[spot, :block] = jnp.where(info[1] == 0, first, second)
        far_ref[spot, :block] = jnp.where(info[1] == 0, second, first)
        own_ref[spot, block:] = low_sums
        far_ref[spot, block:] = low_sums


def final_kernel(info, *refs, groups):
    parts = refs[:groups]
    x_ref, dres_ref, gain_ref, w_ref, out_ref = refs[groups:]
    d_normed = jnp.zeros(dres_ref.shape, F32)
    for group in range(groups):
        owner = lax.rem(info[0] + groups - group, groups)
        heads, triple, rows = parts[group].shape
        d_normed = d_normed + tn(parts[group][...].reshape(heads * triple, rows), w_ref[owner])
    values = x_ref[...].astype(F32)
    centered = values - jnp.mean(values, axis=-1, keepdims=True)
    variance = jnp.mean(centered * centered, axis=-1, keepdims=True)
    inverse = lax.rsqrt(variance + EPSILON)
    hat = centered * inverse
    gy = d_normed * gain_ref[...]
    mean_one = jnp.mean(gy, axis=-1, keepdims=True)
    mean_two = jnp.mean(gy * hat, axis=-1, keepdims=True)
    out_ref[...] = (dres_ref[...] + inverse * (gy - mean_one - hat * mean_two)).astype(BF)


def whole(shape):
    return pl.BlockSpec(shape, lambda *at: (0,) * len(shape))


def per_device(
    tokens,
    cluster_ids,
    lengths,
    top_keys,
    gain_one,
    shift_one,
    w_query,
    w_keyval,
    w_out,
    gain_two,
    shift_two,
    w_up,
    w_down,
    cotangent,
):
    rows, width = tokens.shape
    heads = cluster_ids.shape[1]
    hs = width // heads
    hidden = w_up.shape[1]
    wide = lax.axis_size("wide")
    n_dp = lax.axis_size("dp")
    groups = math.gcd(heads, wide)
    peers = wide // groups
    own_heads = heads // groups
    own_clusters = top_keys.shape[2]
    clusters = own_clusters * wide
    picks = top_keys.shape[3]
    seq = rows * wide
    size = 512 if seq <= 2048 else 2048
    feats = own_heads * hs
    block_rows = width // wide
    fast = peers == 2 and n_dp == 4 and block_rows % 32 == 0 and hidden % (4 * 256) == 0
    me = lax.axis_index("wide")
    group_at, peer_at = me // peers, me % peers
    dp_at = lax.axis_index("dp")
    seq_len = lengths[0]
    bit_x, bit_y = dp_at % 2, (dp_at // 2) % 2
    place_u, place_d = 2 * bit_x + bit_y, 2 * bit_y + bit_x
    info = jnp.stack([group_at, peer_at, seq_len, place_u, place_d, me]).astype(jnp.int32)

    def along_groups(values, hop):
        pairs = [(i, ((i // peers + hop) % groups) * peers + i % peers) for i in range(wide)]
        return lax.ppermute(values, "wide", pairs)

    def along_peers(values, hop):
        pairs = [(i, (i // peers) * peers + (i % peers + hop) % peers) for i in range(wide)]
        return lax.ppermute(values, "wide", pairs)

    def along_dp(values, mask):
        return lax.ppermute(values, "dp", [(i, i ^ mask) for i in range(n_dp)])

    def prefetched(kernel, grid, in_specs, out_specs, out_shape, mib, spent, name, scratch=(), alias=None):
        return pl.pallas_call(
            kernel,
            grid_spec=pltpu.PrefetchScalarGridSpec(
                num_scalar_prefetch=1,
                grid=grid,
                in_specs=in_specs,
                out_specs=out_specs,
                scratch_shapes=list(scratch),
            ),
            out_shape=out_shape,
            compiler_params=params(mib, len(grid)),
            cost_estimate=spent,
            input_output_aliases=alias or {},
            name=name,
        )

    def after(values, *others):
        return lax.optimization_barrier((values, others))[0]

    def array(shape, dtype):
        return jax.ShapeDtypeStruct(shape, dtype)

    position = me * rows + jnp.arange(rows, dtype=jnp.int32)
    marked = jnp.where((position < seq_len)[:, None], cluster_ids, -1).T
    packed = jnp.concatenate([marked, top_keys[0].reshape(heads, own_clusters * picks)], axis=1)
    packed = packed.reshape(groups, own_heads, -1)

    def of_heads(hop):
        return lax.dynamic_index_in_dim(packed, (group_at + groups - hop) % groups, keepdims=False)

    arrived = [of_heads(0)] + [along_groups(of_heads(hop), -hop) for hop in range(1, groups)]

    ready = after(tokens, packed)
    mine = {0: tokens, 1: along_groups(ready, -1)}
    if groups > 2:
        mine[groups - 1] = along_groups(ready, 1)
    for hop in range(2, groups - 1):
        ready = after(tokens, mine[1], mine[groups - 1])
        mine[hop] = along_groups(ready, -hop)

    arrived = jnp.stack(arrived)
    arrived = jnp.stack([arrived] + [along_peers(arrived, -hop) for hop in range(1, peers)], axis=1)
    ids_all = arrived[..., :rows].transpose(2, 0, 1, 3).reshape(own_heads, 1, seq)
    top_all = arrived[..., rows:].reshape(groups, peers, own_heads, own_clusters, picks)
    top_all = jnp.concatenate([top_all, top_all], axis=0)
    top_all = lax.dynamic_slice_in_dim(top_all, (groups - group_at) % groups, groups, axis=0)
    top_all = jnp.concatenate([top_all, top_all], axis=1)
    top_all = lax.dynamic_slice_in_dim(top_all, (peers - peer_at) % peers, peers, axis=1)
    top_all = top_all.transpose(2, 4, 0, 1, 3).reshape(own_heads, picks, clusters)

    bias = prefetched(
        functools.partial(bias_kernel, groups=groups, peers=peers, rows=rows),
        (wide,),
        [whole((own_heads, picks, clusters))],
        pl.BlockSpec((own_heads, rows, clusters), lambda i, s: (0, i, 0)),
        array((own_heads, seq, clusters), BF),
        8 if fast else 60,
        cost(own_heads * seq * clusters * picks * 8, own_heads * seq * clusters * 2),
        "bias",
    )(info, top_all)

    w_in = jnp.concatenate([w_query, w_keyval], axis=1).T.reshape(3, heads, hs, width)
    w_in = w_in.transpose(1, 0, 2, 3).reshape(groups, 3 * feats, width)
    gain_row, shift_row = gain_one[None, :], shift_one[None, :]
    shapes = [
        array((width, groups * rows), BF),
        array((own_heads, 3 * hs, seq), BF),
        array((own_heads, seq, 2 * hs), BF),
    ]
    held = []
    split_peers = peers if peers <= 2 else 1
    for group in sorted(range(groups), key=lambda g: min(g, groups - g)):
        chunk = [mine[group]] + [along_peers(mine[group], -hop) for hop in range(1, peers)]
        if peers > 2:
            chunk = [jnp.concatenate(chunk, axis=0)]
        span = peers * rows
        if peers > 2:
            specs_in = [pl.BlockSpec((rows, width), lambda p, s: (p, 0))]
            grid = (peers,)
            outs = [
                pl.BlockSpec((width, rows), lambda p, s, g=group: (0, g)),
                pl.BlockSpec((own_heads, 3 * hs, rows), lambda p, s, g=group: (0, 0, g * peers + p)),
                pl.BlockSpec((own_heads, rows, 2 * hs), lambda p, s, g=group: (0, g * peers + p, 0)),
            ]
        else:
            specs_in = [whole((rows, width))] * split_peers
            grid = (1,)
            outs = [
                pl.BlockSpec((width, rows), lambda p, s, g=group: (0, g)),
                pl.BlockSpec((own_heads, 3 * hs, span), lambda p, s, g=group: (0, 0, g)),
                pl.BlockSpec((own_heads, span, 2 * hs), lambda p, s, g=group: (0, g, 0)),
            ]
        first = 1 + split_peers + 3
        held = prefetched(
            functools.partial(project_kernel, peers=split_peers, olds=len(held)),
            grid,
            specs_in
            + [
                whole((1, width)),
                whole((1, width)),
                pl.BlockSpec((1, 3 * feats, width), lambda p, s: (s[0], 0, 0)),
            ]
            + [pl.BlockSpec(memory_space=pl.ANY)] * len(held),
            outs,
            shapes,
            16 if fast else 60,
            cost(6 * span * width * feats, span * width * 4),
            "project",
            alias={first + k: k for k in range(len(held))},
        )(info, *chunk, gain_row, shift_row, w_in, *held)
    hat_own, feat, kv = held

    ids_full = pl.BlockSpec((1, 1, seq), lambda h, r: (h, 0, 0))
    feat_full = pl.BlockSpec((1, 3 * hs, seq), lambda h, r: (h, 0, 0))
    kv_full = pl.BlockSpec((1, seq, 2 * hs), lambda h, r: (h, 0, 0))
    bias_full = pl.BlockSpec((1, seq, clusters), lambda h, r: (h, 0, 0))
    head_rows = pl.BlockSpec((hs, rows), lambda h, r: (h, 0))
    mix_spec = pl.BlockSpec((1, 1, hs + 8, rows), lambda h, r: (h, r, 0, 0))
    stat_spec = pl.BlockSpec((1, hs + 8, clusters), lambda h, r: (h, 0, 0))
    cen_spec = pl.BlockSpec((1, hs, clusters), lambda h, r: (h, 0, 0))
    own_rows = groups * rows
    pair_flops = own_heads * own_rows * seq * 256

    one = [
        pl.BlockSpec(spec.block_shape, functools.partial(lambda h, f: f(h, 0), f=spec.index_map))
        for spec in (ids_full, feat_full, kv_full, bias_full, stat_spec, cen_spec, head_rows)
    ]
    ids_one, feat_one, kv_one, bias_one, stat_one, cen_one, rows_one = one
    part_one = pl.BlockSpec((1, hs + 16, clusters), lambda h: (h, 0, 0))
    mix_one = pl.BlockSpec((1, groups, hs + 8, rows), lambda h: (h, 0, 0, 0))
    all_groups = pl.BlockSpec((groups, hs, rows), lambda h: (0, h, 0))
    own_one = pl.BlockSpec((1, own_rows, 2 * hs), lambda h: (h, 0, 0))
    results = pl.pallas_call(
        functools.partial(forward_kernel, size=size, groups=groups, rows=rows),
        grid=(own_heads,),
        in_specs=[ids_one, feat_one, kv_one, bias_one],
        out_specs=[rows_one] * groups + [mix_one, stat_one, cen_one],
        out_shape=[array((feats, rows), BF)] * groups
        + [
            array((own_heads, groups, hs + 8, rows), F32),
            array((own_heads, hs + 8, clusters), F32),
            array((own_heads, hs, clusters), BF),
        ],
        compiler_params=params(32 if fast else 60, 1),
        cost_estimate=cost(6 * pair_flops, 8e6, own_heads * own_rows * seq),
        name="attend",
    )(ids_all, feat, kv, bias)
    attn_t = results[:groups]
    mixed, stats, centroid = results[groups:]

    arrived = [attn_t[0]] + [along_groups(attn_t[hop], hop) for hop in range(1, groups)]

    chunks = 4
    part = hidden // chunks
    w_out_g = w_out.reshape(groups, feats, width)
    gain_row2, shift_row2 = gain_two[None, :], shift_two[None, :]
    square = whole((rows, width))
    column = pl.BlockSpec((rows, part), lambda i, s: (0, i))
    norm_spec = whole((8, width))
    if fast:
        half_column = pl.BlockSpec((rows, part // 2), lambda i, s: (0, i))
        kept = [array((rows, hidden // 2), BF), array((width, rows), BF)]
        kept_specs = [half_column, whole((width, rows))] * 2
        kept = kept * 2
    else:
        kept = [array((rows, hidden), BF), array((rows, width), BF)]
        kept_specs = [column, square]
    results = prefetched(
        functools.partial(block_kernel, groups=groups, chunks=chunks, fast=fast),
        (chunks,),
        [whole((feats, rows))] * groups
        + [
            square,
            whole((1, width)),
            whole((1, width)),
            whole((groups, feats, width)),
            pl.BlockSpec((width, part), lambda i, s: (0, i)),
            pl.BlockSpec((part, width), lambda i, s: (i, 0)),
            square,
        ],
        [square, square, norm_spec, column, square] + kept_specs + [whole((feats, rows))] * groups,
        [
            array((rows, width), BF),
            array((rows, width), F32),
            array((8, width), F32),
            array((rows, hidden), BF),
            array((rows, width), BF),
        ]
        + kept
        + [array((feats, rows), BF)] * groups,
        28 if fast else 60,
        cost(8 * rows * width * hidden, 4 * width * hidden, rows * hidden),
        "feed",
        scratch=[
            pltpu.VMEM((rows, width), F32),
            pltpu.VMEM((rows, 128), F32),
            pltpu.VMEM((rows, width), BF),
            pltpu.VMEM((rows, width), F32),
            pltpu.VMEM((rows, width), F32),
        ],
    )(info, *arrived, tokens, gain_row2, shift_row2, w_out_g, w_up, w_down, cotangent)
    output, d_resid, norm_two, d_up, d_branch = results[:5]
    kept, d_attn = results[5:-groups], results[-groups:]
    grads = [d_attn[0]] + [along_groups(d_attn[hop], -hop) for hop in range(1, groups)]

    def weight_parts():
        dup_got, dbr_got = along_peers(d_up, 1), along_peers(d_branch, 1)
        act_own, low_own, act_far, low_far = kept
        act_got, low_got = along_peers(act_far, 1), along_peers(low_far, 1)
        cot_got, dn_got = along_peers(cotangent, 1), along_peers(norm_two, 1)
        high = block_rows + block_rows // 4 + 8
        chunk = pl.BlockSpec((rows, part), lambda i, s: (0, i ^ 2 ^ s[3]))
        act_spec = pl.BlockSpec((rows, part // 2), lambda i, s: (0, i))
        low_spec = whole((width, rows))
        shape_u = (2, groups, high, width)
        shape_d = (2, groups, block_rows, width)
        send_u, keep_u, send_d, keep_d = prefetched(
            functools.partial(weights_kernel, groups=groups),
            (4,),
            [chunk, chunk, square, square, act_spec, act_spec, low_spec, low_spec, square, square]
            + [norm_spec] * 2,
            [
                pl.BlockSpec((1,) + shape_u[1:], lambda i, s: (jnp.minimum(i, 1), 0, 0, 0)),
                pl.BlockSpec((1,) + shape_u[1:], lambda i, s: (jnp.maximum(i - 2, 0), 0, 0, 0)),
                whole(shape_d),
                whole(shape_d),
            ],
            [array(shape_u, BF), array(shape_u, BF), array(shape_d, BF), array(shape_d, BF)],
            28,
            cost(8 * rows * width * hidden, 6 * width * hidden),
            "weights",
            scratch=[pltpu.VMEM((groups, block_rows, width), F32)],
        )(
            info, d_up, dup_got, d_branch, dbr_got, act_own, act_got, low_own, low_got,
            cotangent, cot_got, norm_two, dn_got,
        )
        return send_u, keep_u, send_d, keep_d

    def weight_sums(keep_u, got_u, keep_d, got_d):
        high = block_rows + block_rows // 4 + 8
        shape_u, shape_d = keep_u.shape, keep_d.shape

        def block(shape, at):
            return pl.BlockSpec((1,) + shape[1:], lambda i: (at, 0, 0, 0))

        next_u, next_d = pl.pallas_call(
            second_kernel,
            grid=(1,),
            in_specs=[block(shape_u, 1), block(shape_u, 1), block(shape_d, 1), block(shape_d, 1)],
            out_specs=[whole(shape_u[1:]), whole(shape_d[1:])],
            out_shape=[array(shape_u[1:], BF), array(shape_d[1:], BF)],
            compiler_params=params(20, 1),
            cost_estimate=cost(groups * high * width * 2, groups * high * width * 12),
            name="second",
        )(keep_u, got_u, keep_d, got_d)
        last_u, last_d = along_dp(next_u, 2), along_dp(next_d, 1)
        tall = high + block_rows
        sums = pl.pallas_call(
            third_kernel,
            grid=(1,),
            in_specs=[
                block(shape_u, 0),
                block(shape_u, 0),
                whole(shape_u[1:]),
                block(shape_d, 0),
                block(shape_d, 0),
                whole(shape_d[1:]),
            ],
            out_specs=[whole((tall, width))] * groups,
            out_shape=[array((tall, width), BF)] * groups,
            compiler_params=params(24, 1),
            cost_estimate=cost(groups * tall * width * 4, groups * tall * width * 8),
            name="third",
        )(keep_u, got_u, last_u, keep_d, got_d, last_d)
        came = [sums[0]] + [along_groups(sums[hop], hop) for hop in range(1, groups)]
        done = pl.pallas_call(
            fourth_kernel,
            grid=(1,),
            in_specs=[whole((tall, width))] * groups,
            out_specs=whole((tall, width)),
            out_shape=array((tall, width), BF),
            compiler_params=params(12, 1),
            cost_estimate=cost(groups * tall * width, groups * tall * width * 2),
            name="fourth",
        )(*came)
        from_x, from_y, from_xy = (along_dp(done, mask) for mask in (1, 2, 3))
        quarter = block_rows // 4
        total_up, total_out, total_down, norms = prefetched(
            spread_kernel,
            (4,),
            [whole((tall, width))] * 4,
            [
                pl.BlockSpec((block_rows, part), lambda i, s: (0, i ^ s[3])),
                pl.BlockSpec((quarter, width), lambda i, s: (i ^ s[3], 0)),
                pl.BlockSpec((block_rows, width), lambda i, s: (i ^ s[4], 0)),
                whole((8, width)),
            ],
            [
                array((block_rows, hidden), F32),
                array((block_rows, width), F32),
                array((hidden // wide, width), F32),
                array((8, width), F32),
            ],
            16,
            cost(1e6, 4 * tall * width * 6),
            "spread",
        )(info, done, from_x, from_y, from_xy)
        norm_own = lax.dynamic_slice_in_dim(norms, me * block_rows, block_rows, axis=1)
        return total_up, total_out, total_down, norm_own

    masks = [1 << k for k in range(n_dp.bit_length() - 1)]

    def reduce_rows(partial):
        blocks = partial.reshape(groups, peers, partial.shape[0] // wide, partial.shape[1])

        def of_peer(hop):
            at = (peer_at + hop) % peers
            return lax.dynamic_index_in_dim(blocks, at, axis=1, keepdims=False)

        total = of_peer(0).astype(F32)
        for hop in range(1, peers):
            total = total + along_peers(of_peer(hop), hop).astype(F32)
        total = total.astype(BF)

        def of_group(hop):
            return lax.dynamic_index_in_dim(total, (group_at + hop) % groups, keepdims=False)

        done = of_group(0).astype(F32)
        for hop in range(1, groups):
            done = done + along_groups(of_group(hop), hop).astype(F32)
        for mask in masks:
            done = done.astype(BF)
            done = done.astype(F32) + along_dp(done, mask).astype(F32)
        return done

    if fast:
        send_u, keep_u, send_d, keep_d = weight_parts()
        got_u, got_d = along_dp(send_u, 1), along_dp(send_d, 2)
        grads = after(grads, keep_u)
    else:
        act, normed_two = kept
        total_up = reduce_rows(tn(normed_two, d_up).astype(BF))
        total_down = reduce_rows(tn(act, cotangent).astype(BF))
        found = jnp.stack([nn(item, d_branch).astype(BF) for item in arrived])
        found = [
            lax.dynamic_index_in_dim(found, (group_at + groups - g) % groups, keepdims=False)
            for g in range(groups)
        ]
        total_out = reduce_rows(jnp.concatenate(found, axis=0))
        norm_own = reduce_rows(norm_two[:2].T.astype(BF)).T

    share = pl.pallas_call(
        functools.partial(sums_kernel, groups=groups),
        grid=(own_heads,),
        in_specs=[ids_one]
        + [rows_one] * groups
        + [mix_one],
        out_specs=part_one,
        out_shape=array((own_heads, hs + 16, clusters), F32),
        compiler_params=params(16 if fast else 60, 1),
        cost_estimate=cost(own_heads * own_rows * clusters * 160, 2e6),
        name="sums",
    )(ids_all, *grads, mixed)
    share_got = [along_peers(share, hop) for hop in range(1, peers)]

    grads = after(grads, share)
    dq_member, dkv_own, dkv_send = pl.pallas_call(
        functools.partial(member_kernel, size=size, groups=groups),
        grid=(own_heads,),
        in_specs=[ids_one, feat_one, kv_one, bias_one]
        + [rows_one] * groups
        + [mix_one, stat_one],
        out_specs=[
            all_groups,
            own_one,
            pl.BlockSpec((1, max(peers - 1, 1) * own_rows, 2 * hs), lambda h: (h, 0, 0)),
        ],
        out_shape=[
            array((groups, feats, rows), F32),
            array((own_heads, own_rows, 2 * hs), F32),
            array((own_heads, max(peers - 1, 1) * own_rows, 2 * hs), BF),
        ],
        scratch_shapes=[pltpu.VMEM((seq, 2 * hs), F32)],
        compiler_params=params(32 if fast else 60, 1),
        cost_estimate=cost(12 * pair_flops, 10e6, own_heads * own_rows * seq),
        name="member",
    )(ids_all, feat, kv, bias, *grads, mixed, stats)
    dkv_got = [
        along_peers(
            dkv_send if peers == 2 else dkv_send[:, (hop - 1) * own_rows : hop * own_rows], hop
        )
        for hop in range(1, peers)
    ]
    share_total = share
    for got in share_got:
        share_total = share_total + got

    d_in = pl.pallas_call(
        functools.partial(centroid_kernel, size=size, groups=groups, gots=len(dkv_got)),
        grid=(own_heads,),
        in_specs=[ids_one, feat_one, kv_one, bias_one, part_one, stat_one, cen_one, all_groups]
        + [own_one] * (1 + len(dkv_got)),
        out_specs=[pl.BlockSpec((1, 3 * hs, rows), lambda h: (h, 0, 0))] * groups,
        out_shape=[array((own_heads, 3 * hs, rows), BF)] * groups,
        scratch_shapes=[pltpu.VMEM((seq, 2 * clusters), BF)],
        compiler_params=params(28 if fast else 60, 1),
        cost_estimate=cost(own_heads * clusters * seq * 1024, 8e6, own_heads * clusters * seq),
        name="centroid",
    )(ids_all, feat, kv, bias, share_total, stats, centroid, dq_member, dkv_own, *dkv_got)

    home = [d_in[0]] + [along_groups(d_in[hop], hop) for hop in range(1, groups)]

    tall = block_rows + 16
    part_spec = [whole((own_heads, 3 * hs, rows))] * groups + [whole((width, own_rows))]
    inward = functools.partial(
        prefetched,
        functools.partial(inward_kernel, groups=groups, fast=fast),
        (1,),
        part_spec,
    )
    spent = cost(2 * own_rows * width * 3 * feats, 4e6)
    if fast:
        half = groups // 2
        blocks = (groups, tall, 3 * feats)
        keep, far = inward(
            [whole(blocks)] * 2, [array(blocks, BF)] * 2, 24, spent, "inward"
        )(info, *d_in, hat_own)
        got = along_peers(far, 1)
        total = keep.astype(F32) + got.astype(F32)
        one_half, two_half = total[:half].astype(BF), total[half:].astype(BF)
        total_up, total_out, total_down, norm_own = weight_sums(
            keep_u, after(got_u, keep), keep_d, after(got_d, keep)
        )
        for mask in (1, 2):
            got_one, got_two = along_dp(one_half, mask), along_dp(two_half, 3 - mask)
            one_half = (one_half.astype(F32) + got_one.astype(F32)).astype(BF)
            two_half = (two_half.astype(F32) + got_two.astype(F32)).astype(BF)
        items = [one_half[k] for k in range(half)] + [two_half[k] for k in range(half)]
    else:
        found, more = inward(
            [whole((width, 3 * feats)), whole((16, 3 * feats))],
            [array((width, 3 * feats), F32), array((16, 3 * feats), F32)],
            60,
            spent,
            "inward",
        )(info, *d_in, hat_own)
        found = found.reshape(groups, peers, block_rows, 3 * feats)
        more = jnp.broadcast_to(more, (groups, peers, 16, 3 * feats))
        found = jnp.concatenate([found, more], axis=2).astype(BF)

        def of_peer(hop):
            at = (peer_at + hop) % peers
            return lax.dynamic_index_in_dim(found, at, axis=1, keepdims=False)

        total = of_peer(0).astype(F32)
        for hop in range(1, peers):
            total = total + along_peers(of_peer(hop), hop).astype(F32)
        for mask in masks:
            total = total.astype(BF)
            total = total.astype(F32) + along_dp(total, mask).astype(F32)
        total = total.astype(BF)
        items = [
            lax.dynamic_index_in_dim(total, (group_at + hop) % groups, keepdims=False)
            for hop in range(groups)
        ]
    pieces = [items[0]] + [along_groups(items[hop], hop) for hop in range(1, groups)]

    grad_tokens = prefetched(
        functools.partial(final_kernel, groups=groups),
        (1,),
        [whole((own_heads, 3 * hs, rows))] * groups
        + [square, square, whole((1, width)), whole((groups, 3 * feats, width))],
        square,
        array((rows, width), BF),
        24 if fast else 60,
        cost(6 * rows * width * width, 6 * width * width),
        "final",
    )(info, *home, tokens, d_resid, gain_row, w_in)

    pieces = jnp.stack(pieces)
    pieces = jnp.stack(
        [
            lax.dynamic_index_in_dim(pieces, (group_at + groups - g) % groups, keepdims=False)
            for g in range(groups)
        ]
    ).astype(F32)
    q_part = pieces[:, :, :feats].transpose(1, 0, 2).reshape(tall, width)
    kv_part = (
        pieces[:, :, feats:]
        .reshape(groups, tall, 2, feats)
        .transpose(1, 2, 0, 3)
        .reshape(tall, 2 * width)
    )
    at = me * block_rows
    wq_rows = lax.dynamic_slice_in_dim(w_query, at, block_rows).astype(F32)
    wkv_rows = lax.dynamic_slice_in_dim(w_keyval, at, block_rows).astype(F32)
    gain_own = lax.dynamic_slice_in_dim(gain_one, at, block_rows)
    shift_own = lax.dynamic_slice_in_dim(shift_one, at, block_rows)
    q_sum, kv_sum = q_part[block_rows], kv_part[block_rows]
    q_part, kv_part = q_part[:block_rows], kv_part[:block_rows]
    shift_grad = jnp.sum(wq_rows * q_sum, axis=1) + jnp.sum(wkv_rows * kv_sum, axis=1)
    along = jnp.sum(wq_rows * q_part, axis=1) + jnp.sum(wkv_rows * kv_part, axis=1)
    return (
        output,
        grad_tokens,
        q_part + shift_own[:, None] * q_sum,
        kv_part + shift_own[:, None] * kv_sum,
        total_out,
        total_up,
        total_down,
        along / gain_own,
        shift_grad,
        norm_own[0],
        norm_own[1],
    )


def solution(mesh):
    return jax.shard_map(
        per_device,
        mesh=mesh,
        in_specs=(
            P(("dp", "wide"), None),
            P(("dp", "wide"), None),
            P("dp"),
            P("dp", None, "wide", None),
            P(),
            P(),
            P(),
            P(),
            P(),
            P(),
            P(),
            P(),
            P(),
            P(("dp", "wide"), None),
        ),
        out_specs=(
            P(("dp", "wide"), None),
            P(("dp", "wide"), None),
            P("wide", None),
            P("wide", None),
            P("wide", None),
            P("wide", None),
            P("wide", None),
            P("wide"),
            P("wide"),
            P("wide"),
            P("wide"),
        ),
        check_vma=False,
    )
```

```python
import functools
import math

import jax
import jax.numpy as jnp
import numpy as np
from jax import lax
from jax.experimental import pallas as pl
from jax.experimental.pallas import tpu as pltpu
from jax.sharding import PartitionSpec as P

EPSILON = 1e-05
NEGATIVE = -1e30
EXCLUDED = -3e30
GELU_A = math.sqrt(2.0 / math.pi)
GELU_B = 0.044715
BF = jnp.bfloat16
F32 = jnp.float32


def nn(left, right):
    return lax.dot_general(left, right, (((1,), (0,)), ((), ())), preferred_element_type=F32)


def nt(left, right):
    return lax.dot_general(left, right, (((1,), (1,)), ((), ())), preferred_element_type=F32)


def tn(left, right):
    return lax.dot_general(left, right, (((0,), (0,)), ((), ())), preferred_element_type=F32)


def params(mib, dims):
    return pltpu.CompilerParams(
        vmem_limit_bytes=mib * 1024 * 1024, dimension_semantics=("arbitrary",) * dims
    )


def cost(flops, nbytes, trans=0):
    return pl.CostEstimate(flops=int(flops), bytes_accessed=int(nbytes), transcendentals=int(trans))


def split_low(values):
    high = values.astype(BF)
    return high, (values - high.astype(F32)).astype(BF)


def one_hot_t(ids_row, clusters):
    rows = lax.broadcasted_iota(jnp.int32, (clusters, ids_row.shape[1]), 0)
    return jnp.where(rows == ids_row, 1.0, 0.0).astype(BF)


def key_passes(total, size, score, weigh, blocks=None):
    count = total // size
    if count <= 4:
        if blocks is None:
            blocks = [score(index) for index in range(count)]
        peak = functools.reduce(jnp.maximum, [jnp.max(b, axis=0, keepdims=True) for b in blocks])
        denom, sums = 0.0, None
        for index in range(count):
            expo = jnp.exp(blocks[index] - peak)
            denom = denom + jnp.sum(expo, axis=0, keepdims=True)
            parts = weigh(index, expo)
            sums = parts if sums is None else tuple(x + y for x, y in zip(sums, parts))
        return peak, denom, sums

    def step(index, carry):
        peak, denom, sums = carry
        block = score(index)
        fresh = jnp.maximum(peak, jnp.max(block, axis=0, keepdims=True))
        expo = jnp.exp(block - fresh)
        fade = jnp.exp(peak - fresh)
        parts = weigh(index, expo)
        return (
            fresh,
            denom * fade + jnp.sum(expo, axis=0, keepdims=True),
            tuple(old * fade + new for old, new in zip(sums, parts)),
        )

    shapes = jax.eval_shape(lambda: (score(0), weigh(0, score(0))))
    lanes = shapes[0].shape[1]
    start = (
        jnp.full((1, lanes), NEGATIVE, F32),
        jnp.zeros((1, lanes), F32),
        tuple(jnp.zeros(item.shape, F32) for item in shapes[1]),
    )
    return lax.fori_loop(0, count, step, start)


def key_sum(total, size, step, start):
    count = total // size
    if count <= 4:
        for index in range(count):
            start = step(index, start)
        return start
    return lax.fori_loop(0, count, step, start)


def spot_of(index, size):
    if isinstance(index, int):
        return pl.ds(index * size, size)
    return pl.ds(pl.multiple_of(index * size, size), size)


def piece(ref, index, size, axis):
    spot = spot_of(index, size)
    return ref[spot, :] if axis == 0 else ref[:, spot]


def bias_kernel(info, top_ref, bias_ref, *, groups, peers, rows):
    part = pl.program_id(0)
    owner = (
        lax.rem(info[0] + part // peers, groups) * peers + lax.rem(info[1] + part % peers, peers)
    )
    heads, picks, clusters = top_ref.shape
    place = owner * rows + lax.broadcasted_iota(jnp.int32, (rows, clusters), 0)
    plain = jnp.where(place >= info[2], EXCLUDED, NEGATIVE)
    for head in range(heads):
        top = top_ref[head]
        value = plain
        for pick in range(picks):
            value = jnp.where(place == top[pick : pick + 1, :], 0.0, value)
        bias_ref[head] = value.astype(BF)


def project_kernel(info, *refs, peers, olds):
    parts = refs[:peers]
    gain_ref, shift_ref, w_ref = refs[peers : peers + 3]
    hat_ref, feat_ref, kv_ref = refs[peers + 3 + olds :]
    rows = hat_ref.shape[1]
    for peer in range(peers):
        values = parts[peer][...].astype(F32)
        centered = values - jnp.mean(values, axis=-1, keepdims=True)
        variance = jnp.mean(centered * centered, axis=-1, keepdims=True)
        scaled = centered * lax.rsqrt(variance + EPSILON) * gain_ref[...]
        if peer == 0:
            hat_ref[...] = scaled.astype(BF).T
        low = (scaled + shift_ref[...]).astype(BF)
        found = nt(w_ref[0], low)
        heads, triple = feat_ref.shape[0], feat_ref.shape[1]
        hs = triple // 3
        spot = slice(peer * rows, (peer + 1) * rows)
        for head in range(heads):
            base = head * triple
            query = (found[base : base + hs] * 0.125).astype(BF)
            pair = found[base + hs : base + triple].astype(BF)
            feat_ref[head, :hs, spot] = query
            feat_ref[head, hs:, spot] = pair
            kv_ref[head, spot, :] = pair.T


def forward_kernel(ids_all, feat, kv, bias, *refs, size, groups, rows):
    outs = refs[:groups]
    mix_ref, stat_ref, cen_ref = refs[groups:]
    hs = feat.shape[1] // 3
    keys = kv.shape[1]
    count = keys // size
    clusters = bias.shape[2]
    kv_h, bias_h = kv.at[0], bias.at[0]
    queries_all, kvt = feat.at[0, :hs], feat.at[0, hs:]
    hot_all = one_hot_t(ids_all[0], clusters)
    ones = jnp.ones((16, keys), BF)
    sums = nt(jnp.concatenate([queries_all[...], ones], axis=0), hot_all)
    counts = sums[hs : hs + 1]
    centroid = (sums[:hs] / jnp.maximum(counts, 1.0)).astype(BF)
    padded = jnp.concatenate([centroid, jnp.zeros_like(centroid)], axis=0)

    def cluster_score(index):
        scores = nn(piece(kv_h, index, size, 0), padded)
        outside = piece(bias_h, index, size, 0).astype(F32) < 2.0 * NEGATIVE
        return jnp.where(outside, NEGATIVE, scores)

    def cluster_weigh(index, expo):
        top = piece(bias_h, index, size, 0).astype(F32) == 0.0
        mass = jnp.sum(jnp.where(top, expo, 0.0), axis=0, keepdims=True)
        other = jnp.where(top, 0.0, expo).astype(BF)
        return nn(piece(kvt, index, size, 1), other), mass

    peers = keys // (groups * rows)
    hots, sides = [], []
    for group in range(groups):
        spot = slice(group * peers * rows, group * peers * rows + rows)
        hot = one_hot_t(ids_all[0, :, spot], clusters)
        queries = queries_all[:, spot]
        hots.append(hot)
        sides.append(jnp.concatenate([queries, jnp.zeros_like(queries), hot], axis=0))

    def member_score(group, index):
        both = jnp.concatenate([piece(kv_h, index, size, 0), piece(bias_h, index, size, 0)], axis=1)
        return nn(both, sides[group])

    def member_weigh(index, expo):
        return (nn(piece(kvt, index, size, 1), expo.astype(BF)),)

    short = count <= 4
    ahead = None
    if short:
        ahead = [member_score(0, index) for index in range(count)]
    peak, denom, (rest, mass) = key_passes(keys, size, cluster_score, cluster_weigh)
    rest = rest[hs:] / denom
    mass = mass / denom
    blank = jnp.zeros((5, clusters), F32)
    stats = jnp.concatenate([rest, mass, peak + jnp.log(denom), counts, blank], axis=0)
    stat_ref[0] = stats
    cen_ref[0] = centroid
    high, low = split_low(stats)
    table = jnp.concatenate([high, low], axis=1)
    for group in range(groups):
        gathered = nn(table, jnp.concatenate([hots[group], hots[group]], axis=0))
        blocks, ahead = ahead, None
        if short and group + 1 < groups:
            ahead = [member_score(group + 1, index) for index in range(count)]
        score = functools.partial(member_score, group)
        peak, denom, (mix,) = key_passes(keys, size, score, member_weigh, blocks)
        mix = mix[hs:] / denom
        outs[group][...] = (gathered[hs : hs + 1] * mix + gathered[:hs]).astype(BF)
        level = jnp.broadcast_to(peak + jnp.log(denom), (8, rows))
        mix_ref[0, group] = jnp.concatenate([mix, level], axis=0)


def sums_kernel(ids_own, *refs, groups):
    grads, (mix_ref, part_ref) = refs[:groups], refs[groups:]
    hs = grads[0].shape[0]
    total = None
    for group in range(groups):
        rows = grads[group].shape[1]
        step = ids_own.shape[2] // groups
        hot = one_hot_t(ids_own[0, :, group * step : group * step + rows], part_ref.shape[2])
        grad = grads[group][...]
        along = jnp.sum(grad.astype(F32) * mix_ref[0, group, :hs], axis=0, keepdims=True)
        high, low = split_low(along)
        pad = jnp.zeros((14, rows), BF)
        part = nt(jnp.concatenate([grad, high, low, pad], axis=0), hot)
        total = part if total is None else total + part
    part_ref[0] = total


def back_kernel(ids_all, feat, kv, bias, *refs, size, groups, gots):
    grads = refs[:groups]
    mix_ref, stat_ref, cen_ref = refs[groups : groups + 3]
    shares = refs[groups + 3 : groups + 4 + gots]
    dq_ref, own_ref, send_ref, total, both = refs[groups + 4 + gots :]
    hs, rows = grads[0].shape
    keys = kv.shape[1]
    count = keys // size
    peers = keys // (groups * rows)
    clusters = bias.shape[2]
    kv_h, bias_h = kv.at[0], bias.at[0]
    queries_all, kvt = feat.at[0, :hs], feat.at[0, hs:]
    stats = stat_ref[0]
    high, low = split_low(stats[hs : hs + 8])
    table = jnp.concatenate([high, low], axis=1)
    hots, sides, levels, deltas, pads, rights = [], [], [], [], [], []
    for group in range(groups):
        spot = slice(group * peers * rows, group * peers * rows + rows)
        hot = one_hot_t(ids_all[0, :, spot], clusters)
        queries = queries_all[:, spot]
        blank = jnp.zeros_like(queries)
        hots.append(jnp.concatenate([hot, hot], axis=0))
        sides.append(jnp.concatenate([queries, blank, hot], axis=0))
        mass = nn(table, hots[group])[0:1]
        back = (mass * grads[group][...].astype(F32)).astype(BF)
        levels.append(mix_ref[0, group, hs : hs + 1])
        deltas.append(jnp.sum(back.astype(F32) * mix_ref[0, group, :hs], axis=0, keepdims=True))
        pads.append(jnp.concatenate([blank, back], axis=0))
        turned = jnp.concatenate([queries, blank], axis=0)
        rights.append(jnp.concatenate([turned, pads[group]], axis=1).T)

    def scores(group, index):
        kv_c = piece(kv_h, index, size, 0)
        pair = jnp.concatenate([kv_c, piece(bias_h, index, size, 0)], axis=1)
        return nn(pair, sides[group]), nn(kv_c, pads[group])

    def finish(group, index, found, dq):
        weights = jnp.exp(found[0] - levels[group])
        grad_s = (weights * (found[1] - deltas[group])).astype(BF)
        part = nn(jnp.concatenate([grad_s, weights.astype(BF)], axis=1), rights[group])
        spot = spot_of(index, size)
        if group == 0:
            total[spot, :] = part
        else:
            total[spot, :] += part
        return dq + nn(piece(kvt, index, size, 1), grad_s)

    rest, mass = stats[:hs], stats[hs : hs + 1]
    level, counts = stats[hs + 1 : hs + 2], stats[hs + 2 : hs + 3]
    centroid = cen_ref[0]
    part = shares[0][0]
    for share in shares[1:]:
        part = part + share[0]
    d_rest = part[:hs].astype(BF)
    d_mass = part[hs : hs + 1] + part[hs + 1 : hs + 2]
    delta = jnp.sum(d_rest.astype(F32) * rest, axis=0, keepdims=True) + d_mass * mass
    cen_pad = jnp.concatenate([centroid, jnp.zeros_like(centroid)], axis=0)
    rest_pad = jnp.concatenate([jnp.zeros_like(centroid), d_rest], axis=0)
    right = jnp.concatenate([cen_pad, rest_pad], axis=1).T

    def cluster_step(index, summed):
        kv_c = piece(kv_h, index, size, 0)
        marks = piece(bias_h, index, size, 0).astype(F32)
        probs = jnp.exp(nn(kv_c, cen_pad) - level)
        probs = jnp.where(marks < 2.0 * NEGATIVE, 0.0, probs)
        top = marks == 0.0
        d_probs = jnp.where(top, d_mass, nn(kv_c, rest_pad))
        d_score = (probs * (d_probs - delta)).astype(BF)
        other = jnp.where(top, 0.0, probs).astype(BF)
        both[spot_of(index, size), :] = jnp.concatenate([d_score, other], axis=1)
        return summed + nn(piece(kvt, index, size, 1), d_score)

    start = jnp.zeros((2 * hs, rows), F32)
    zero = jnp.zeros((2 * hs, clusters), F32)
    member_dq = []
    if count <= 4:
        tasks = [(group, index) for group in range(groups) for index in range(count)]
        ahead = scores(*tasks[0])
        d_cen = key_sum(keys, size, cluster_step, zero)
        dq = start
        for step, (group, index) in enumerate(tasks):
            found = ahead
            if step + 1 < len(tasks):
                ahead = scores(*tasks[step + 1])
            dq = finish(group, index, found, dq)
            if index == count - 1:
                member_dq.append(dq[:hs] * 0.125)
                dq = start
    else:
        d_cen = key_sum(keys, size, cluster_step, zero)
        for group in range(groups):

            def step(index, dq, group=group):
                return finish(group, index, scores(group, index), dq)

            member_dq.append(lax.fori_loop(0, count, step, start)[:hs] * 0.125)
    d_cen = d_cen[:hs] * 0.125 / jnp.maximum(counts, 1.0)
    high, low = split_low(d_cen)
    table = jnp.concatenate([high, low], axis=1)
    for group in range(groups):
        base = group * peers * rows
        dq_ref[group] = (member_dq[group] + nn(table, hots[group])).astype(BF)
        own = total[base : base + rows, :] + nn(both[base : base + rows, :], right)
        own_ref[0, :, group * rows : (group + 1) * rows] = own.T
        for peer in range(1, peers):
            spot = (peer - 1) * groups * rows + group * rows
            found = total[base + peer * rows : base + (peer + 1) * rows, :]
            send_ref[0, :, spot : spot + rows] = found.astype(BF).T


def join_kernel(dq_ref, own_ref, *refs, groups):
    gots, outs = refs[:-groups], refs[-groups:]
    heads, _, rows = outs[0].shape
    hs = dq_ref.shape[1] // heads
    for head in range(heads):
        for group in range(groups):
            spot = slice(group * rows, (group + 1) * rows)
            pair = own_ref[head, :, spot]
            for got in gots:
                pair = pair + got[head, :, spot].astype(F32)
            outs[group][head, :hs] = dq_ref[group, head * hs : (head + 1) * hs]
            outs[group][head, hs:] = pair.astype(BF)


def block_kernel(info, *refs, groups, chunks, fast):
    (attn, rest) = (refs[:groups], refs[groups:])
    x_ref, gain_ref, shift_ref, wo_ref, up_ref, down_ref, cot_ref = rest[:7]
    out_ref, dres_ref = rest[7:9]
    if fast:
        far_ref, low_far, act_ref, low_ref = rest[9:13]
        rest = rest[13:]
        hidden = far_ref.shape[1] * 4 // 7
    else:
        dn_ref, dup_ref, dbr_ref, act_ref, low_ref = rest[9:14]
        rest = rest[14:]
    dat = rest[:groups]
    hat_ref, inv_ref, normed, back, total = rest[groups:]
    index = pl.program_id(0)

    @pl.when(index == 0)
    def before():
        resid = x_ref[...].astype(F32)
        for group in range(groups):
            owner = lax.rem(info[0] + groups - group, groups)
            resid = resid + tn(attn[group][...], wo_ref[owner])
        total[...] = resid
        centered = resid - jnp.mean(resid, axis=-1, keepdims=True)
        variance = jnp.mean(centered * centered, axis=-1, keepdims=True)
        inverse = lax.rsqrt(variance + EPSILON)
        hat = centered * inverse
        hat_ref[...] = hat
        inv_ref[...] = jnp.broadcast_to(inverse, inv_ref.shape)
        low = (hat * gain_ref[...] + shift_ref[...]).astype(BF)
        normed[...] = low
        if fast:
            feats = attn[0].shape[0]
            half = feats // 2
            turned = low.T
            for group in range(groups):
                first = turned[group * feats : group * feats + half]
                second = turned[group * feats + half : (group + 1) * feats]
                spot = slice(group * half, (group + 1) * half)
                low_ref[spot, :] = jnp.where(info[1] == 0, first, second)
                low_far[spot, :] = jnp.where(info[1] == 0, second, first)
                first = attn[group][:half]
                second = attn[group][half:]
                spot = slice((groups + group) * half, (groups + group + 1) * half)
                low_ref[spot, :] = jnp.where(info[1] == 0, first, second)
                low_far[spot, :] = jnp.where(info[1] == 0, second, first)
        else:
            low_ref[...] = low
        back[...] = jnp.zeros_like(back)

    up = nn(normed[...], up_ref[...])
    grad_act = nt(cot_ref[...], down_ref[...])
    square = up * up
    inner = GELU_A * (up + GELU_B * up * square)
    curve = jnp.tanh(inner)
    act = (0.5 * up * (1.0 + curve)).astype(BF)
    slope = 0.5 * (1.0 + curve) + 0.5 * up * (1.0 - curve * curve) * (
        GELU_A * (1.0 + 3.0 * GELU_B * square)
    )
    d_up = (grad_act * slope).astype(BF)
    if fast:
        part = act.shape[1]
        half = part // 2
        first, second = act[:, :half], act[:, half:]
        act_ref[...] = jnp.where(info[1] == 0, first, second)
        far_ref[:, pl.ds(pl.multiple_of(index * part, part), part)] = d_up
        spot = pl.ds(pl.multiple_of(hidden + index * half, half), half)
        far_ref[:, spot] = jnp.where(info[1] == 0, second, first)
    else:
        dup_ref[...] = d_up
        act_ref[...] = act
    back[...] += nt(d_up, up_ref[...])
    total[...] += nn(act, down_ref[...])

    @pl.when(index == chunks - 1)
    def after():
        out_ref[...] = total[...].astype(BF)
        d_normed = back[...]
        hat = hat_ref[...]
        gain_part = jnp.sum(d_normed * hat, axis=0, keepdims=True)
        shift_part = jnp.sum(d_normed, axis=0, keepdims=True)
        if fast:
            rows, width = low_far.shape[1], d_normed.shape[1]
            fold = []
            for part_row in split_low(gain_part) + split_low(shift_part):
                fold += [part_row[:, k : k + rows].astype(F32) for k in range(0, width, rows)]
            fold.append(jnp.zeros((low_far.shape[0] - width - len(fold), rows), F32))
            folded = jnp.concatenate(fold, axis=0).astype(BF)
            low_far[width:, :] = folded
            low_ref[width:, :] = folded
        else:
            blank = jnp.zeros((6, d_normed.shape[1]), F32)
            dn_ref[...] = jnp.concatenate([gain_part, shift_part, blank], axis=0)
        gy = d_normed * gain_ref[...]
        mean_one = jnp.mean(gy, axis=-1, keepdims=True)
        mean_two = jnp.mean(gy * hat, axis=-1, keepdims=True)
        d_resid = cot_ref[...].astype(F32) + inv_ref[:, 0:1] * (gy - mean_one - hat * mean_two)
        dres_ref[...] = d_resid
        branch = d_resid.astype(BF)
        if fast:
            far_ref[:, hidden * 3 // 2 :] = branch
        else:
            dbr_ref[...] = branch
        for group in range(groups):
            owner = lax.rem(info[0] + groups - group, groups)
            dat[group][...] = nt(wo_ref[owner], branch).astype(BF)


def weights_kernel(info, *refs, groups):
    (dup, dup_got, dbr, dbr_got, act, act_got, low, low_got, cot, cot_got) = refs[:10]
    send_u, keep_u, send_d, keep_d, outs = refs[10:]
    width = cot.shape[1]
    index = pl.program_id(0)
    group_at, place_u, place_d = info[0], info[3], info[4]
    rows = width // (2 * groups)
    quarter = rows // 4
    stay = groups * rows

    @pl.when(index == 0)
    def first():
        found = nn(low[stay:width, :], dbr[...]) + nn(low_got[stay:width, :], dbr_got[...])
        for group in range(groups):
            outs[group] = found[group * rows : (group + 1) * rows]

    up = nn(low[:stay, :], dup[...]) + nn(low_got[:stay, :], dup_got[...])
    at = lax.bitwise_xor(lax.bitwise_xor(index, 2), place_u)
    fold = low[width:, :].astype(F32) + low_got[width:, :].astype(F32)
    times = width // fold.shape[1]
    norms = []
    for part in range(2):
        both = fold[2 * part * times : (2 * part + 1) * times]
        both = both + fold[(2 * part + 1) * times : (2 * part + 2) * times]
        norms.append(jnp.concatenate([both[k : k + 1] for k in range(times)], axis=1))
    norms = jnp.concatenate(norms + [jnp.zeros((6, width), F32)], axis=0)
    for group in range(groups):
        spot = lax.rem(group + groups - group_at, groups)
        block = up[group * rows : (group + 1) * rows].astype(BF)
        away = (groups - group) % groups
        start = pl.multiple_of(at * quarter, 8)
        other = jnp.concatenate([outs[group, pl.ds(start, quarter), :], norms], axis=0).astype(BF)

        @pl.when(index < 2)
        def leaves():
            send_u[0, spot, :rows] = block
            send_u[0, away, rows:] = other

        @pl.when(index >= 2)
        def stays():
            keep_u[0, spot, :rows] = block
            keep_u[0, away, rows:] = other

    down = tn(act[...], cot[...]) + tn(act_got[...], cot_got[...])
    spot = lax.rem(index + groups - group_at, groups)
    for part in range(4):
        block = down[part * rows : (part + 1) * rows].astype(BF)
        place = lax.bitwise_xor(part, place_d)

        @pl.when(place >= 2)
        def leaves_down():
            send_d[place - 2, spot] = block

        @pl.when(place < 2)
        def stays_down():
            keep_d[place, spot] = block


def second_kernel(keep_u, got_u, keep_d, got_d, send_u, send_d):
    send_u[...] = (keep_u[0].astype(F32) + got_u[0].astype(F32)).astype(BF)
    send_d[...] = (keep_d[0].astype(F32) + got_d[0].astype(F32)).astype(BF)


def third_kernel(keep_u, got_u, last_u, keep_d, got_d, last_d, *outs):
    rows = keep_u.shape[2]
    for group in range(len(outs)):
        up = keep_u[0, group].astype(F32) + got_u[0, group].astype(F32) + last_u[group].astype(F32)
        down = keep_d[0, group].astype(F32) + got_d[0, group].astype(F32) + last_d[group].astype(F32)
        outs[group][:rows] = up.astype(BF)
        outs[group][rows:] = down.astype(BF)


def fourth_kernel(*refs):
    parts, out = refs[:-1], refs[-1]
    total = parts[0][...].astype(F32)
    for part in parts[1:]:
        total = total + part[...].astype(F32)
    out[...] = total.astype(BF)


def spread_kernel(info, own, from_x, from_y, from_xy, up_ref, out_ref, down_ref, norm_ref):
    index = pl.program_id(0)
    rows = up_ref.shape[0]
    quarter = out_ref.shape[0]
    top = rows + quarter + 8
    for place, part in enumerate((own, from_y, from_x, from_xy)):

        @pl.when(index == place)
        def upper(part=part):
            up_ref[...] = part[:rows].astype(F32)
            tail = part[rows:top].astype(F32)
            out_ref[...] = tail[:quarter]

            @pl.when(lax.bitwise_xor(index, info[3]) == 0)
            def norms():
                norm_ref[...] = tail[quarter:]

    for place, part in enumerate((own, from_x, from_y, from_xy)):

        @pl.when(index == place)
        def lower(part=part):
            down_ref[...] = part[top:].astype(F32)


def inward_kernel(info, *refs, groups, fast):
    parts, hat_ref = refs[:groups], refs[groups]
    outs = refs[groups + 1 :]
    heads, triple, rows = parts[0].shape
    hs = triple // 3
    total, sums = None, None
    ones = jnp.ones((16, rows), BF)
    for group in range(groups):
        order = [parts[group][h, k * hs : (k + 1) * hs] for k in range(3) for h in range(heads)]
        turned = jnp.concatenate(order, axis=0)
        found = nt(hat_ref[:, group * rows : (group + 1) * rows], turned)
        more = nt(ones, turned)
        total = found if total is None else total + found
        sums = more if sums is None else sums + more
    if not fast:
        outs[0][...] = total
        outs[1][...] = sums
        return
    own_ref, far_ref = outs
    block = total.shape[0] // (2 * groups)
    low_sums = sums.astype(BF)
    for group in range(groups):
        spot = lax.rem(group + groups - info[0], groups)
        first = total[2 * group * block : (2 * group + 1) * block].astype(BF)
        second = total[(2 * group + 1) * block : (2 * group + 2) * block].astype(BF)
        own_ref[spot, :block] = jnp.where(info[1] == 0, first, second)
        far_ref[spot, :block] = jnp.where(info[1] == 0, second, first)
        own_ref[spot, block:] = low_sums
        far_ref[spot, block:] = low_sums


def final_kernel(info, *refs, groups):
    parts = refs[:groups]
    x_ref, dres_ref, gain_ref, w_ref, out_ref = refs[groups:]
    d_normed = jnp.zeros(dres_ref.shape, F32)
    for group in range(groups):
        owner = lax.rem(info[0] + groups - group, groups)
        heads, triple, rows = parts[group].shape
        d_normed = d_normed + tn(parts[group][...].reshape(heads * triple, rows), w_ref[owner])
    values = x_ref[...].astype(F32)
    centered = values - jnp.mean(values, axis=-1, keepdims=True)
    variance = jnp.mean(centered * centered, axis=-1, keepdims=True)
    inverse = lax.rsqrt(variance + EPSILON)
    hat = centered * inverse
    gy = d_normed * gain_ref[...]
    mean_one = jnp.mean(gy, axis=-1, keepdims=True)
    mean_two = jnp.mean(gy * hat, axis=-1, keepdims=True)
    out_ref[...] = (dres_ref[...] + inverse * (gy - mean_one - hat * mean_two)).astype(BF)


def whole(shape):
    return pl.BlockSpec(shape, lambda *at: (0,) * len(shape))


def per_device(
    tokens,
    cluster_ids,
    lengths,
    top_keys,
    gain_one,
    shift_one,
    w_query,
    w_keyval,
    w_out,
    gain_two,
    shift_two,
    w_up,
    w_down,
    cotangent,
):
    rows, width = tokens.shape
    heads = cluster_ids.shape[1]
    hs = width // heads
    hidden = w_up.shape[1]
    wide = lax.axis_size("wide")
    n_dp = lax.axis_size("dp")
    groups = math.gcd(heads, wide)
    peers = wide // groups
    own_heads = heads // groups
    own_clusters = top_keys.shape[2]
    clusters = own_clusters * wide
    picks = top_keys.shape[3]
    seq = rows * wide
    size = 512 if seq <= 2048 else 2048
    feats = own_heads * hs
    block_rows = width // wide
    fast = peers == 2 and n_dp == 4 and block_rows % 32 == 0 and hidden == 4 * width and width % 256 == 0 and rows % 128 == 0
    me = lax.axis_index("wide")
    group_at, peer_at = me // peers, me % peers
    dp_at = lax.axis_index("dp")
    seq_len = lengths[0]
    bit_x, bit_y = dp_at % 2, (dp_at // 2) % 2
    place_u, place_d = 2 * bit_x + bit_y, 2 * bit_y + bit_x
    info = jnp.stack([group_at, peer_at, seq_len, place_u, place_d, me]).astype(jnp.int32)

    def along_groups(values, hop):
        pairs = [(i, ((i // peers + hop) % groups) * peers + i % peers) for i in range(wide)]
        return lax.ppermute(values, "wide", pairs)

    def along_peers(values, hop):
        pairs = [(i, (i // peers) * peers + (i % peers + hop) % peers) for i in range(wide)]
        return lax.ppermute(values, "wide", pairs)

    def along_dp(values, mask):
        return lax.ppermute(values, "dp", [(i, i ^ mask) for i in range(n_dp)])

    def prefetched(kernel, grid, in_specs, out_specs, out_shape, mib, spent, name, scratch=(), alias=None):
        return pl.pallas_call(
            kernel,
            grid_spec=pltpu.PrefetchScalarGridSpec(
                num_scalar_prefetch=1,
                grid=grid,
                in_specs=in_specs,
                out_specs=out_specs,
                scratch_shapes=list(scratch),
            ),
            out_shape=out_shape,
            compiler_params=params(mib, len(grid)),
            cost_estimate=spent,
            input_output_aliases=alias or {},
            name=name,
        )

    def after(values, *others):
        return lax.optimization_barrier((values, others))[0]

    def array(shape, dtype):
        return jax.ShapeDtypeStruct(shape, dtype)

    position = me * rows + jnp.arange(rows, dtype=jnp.int32)
    marked = jnp.where((position < seq_len)[:, None], cluster_ids, -1).T
    packed = jnp.concatenate(
        [marked, top_keys[0].transpose(0, 2, 1).reshape(heads, own_clusters * picks)], axis=1
    )
    packed = packed.reshape(groups, own_heads, -1)

    def of_heads(hop):
        return lax.dynamic_index_in_dim(packed, (group_at + groups - hop) % groups, keepdims=False)

    arrived = [of_heads(0)] + [along_groups(of_heads(hop), -hop) for hop in range(1, groups)]

    ready = after(tokens, packed)
    mine = {0: tokens, 1: along_groups(ready, -1)}
    if groups > 2:
        mine[groups - 1] = along_groups(ready, 1)
    for hop in range(2, groups - 1):
        ready = after(tokens, mine[1], mine[groups - 1])
        mine[hop] = along_groups(ready, -hop)

    arrived = jnp.stack(arrived)
    others = [arrived] + [along_peers(arrived, -hop) for hop in range(1, peers)]
    ids_all = jnp.stack([item[..., :rows] for item in others], axis=1)
    ids_all = ids_all.transpose(2, 0, 1, 3).reshape(own_heads, 1, seq)
    turned = (ids_all + (clusters - group_at * (clusters // groups))) % clusters
    ids_all = jnp.where(ids_all < 0, -1, turned)
    tops = [item[..., rows:] for item in others]
    if peers == 2:
        tops = [
            jnp.where(peer_at == 0, tops[0], tops[1]),
            jnp.where(peer_at == 0, tops[1], tops[0]),
        ]
    else:
        tops = jnp.stack(tops)
        tops = [
            lax.dynamic_index_in_dim(tops, (p + peers - peer_at) % peers, keepdims=False)
            for p in range(peers)
        ]
    top_all = jnp.stack(tops, axis=1).reshape(groups, peers, own_heads, picks, own_clusters)
    top_all = top_all.transpose(2, 3, 0, 1, 4).reshape(own_heads, picks, clusters)
    cot_got = [along_peers(cotangent, hop) for hop in range(1, peers)] if fast else []

    bias = prefetched(
        functools.partial(bias_kernel, groups=groups, peers=peers, rows=rows),
        (wide,),
        [whole((own_heads, picks, clusters))],
        pl.BlockSpec((own_heads, rows, clusters), lambda i, s: (0, i, 0)),
        array((own_heads, seq, clusters), BF),
        8 if fast else 60,
        cost(own_heads * seq * clusters * picks * 8, own_heads * seq * clusters * 2),
        "bias",
    )(info, top_all)

    w_in = jnp.concatenate([w_query, w_keyval], axis=1).T.reshape(3, heads, hs, width)
    w_in = w_in.transpose(1, 0, 2, 3).reshape(groups, 3 * feats, width)
    gain_row, shift_row = gain_one[None, :], shift_one[None, :]
    shapes = [
        array((width, groups * rows), BF),
        array((own_heads, 3 * hs, seq), BF),
        array((own_heads, seq, 2 * hs), BF),
    ]
    held = []
    split_peers = peers if peers <= 2 else 1
    for group in sorted(range(groups), key=lambda g: min(g, groups - g)):
        arrival = mine[group]
        if 1 < group < groups - 1:
            arrival = after(arrival, bias, held, cot_got)
        chunk = [arrival] + [along_peers(arrival, -hop) for hop in range(1, peers)]
        if peers > 2:
            chunk = [jnp.concatenate(chunk, axis=0)]
        span = peers * rows
        if peers > 2:
            specs_in = [pl.BlockSpec((rows, width), lambda p, s: (p, 0))]
            grid = (peers,)
            outs = [
                pl.BlockSpec((width, rows), lambda p, s, g=group: (0, g)),
                pl.BlockSpec((own_heads, 3 * hs, rows), lambda p, s, g=group: (0, 0, g * peers + p)),
                pl.BlockSpec((own_heads, rows, 2 * hs), lambda p, s, g=group: (0, g * peers + p, 0)),
            ]
        else:
            specs_in = [whole((rows, width))] * split_peers
            grid = (1,)
            outs = [
                pl.BlockSpec((width, rows), lambda p, s, g=group: (0, g)),
                pl.BlockSpec((own_heads, 3 * hs, span), lambda p, s, g=group: (0, 0, g)),
                pl.BlockSpec((own_heads, span, 2 * hs), lambda p, s, g=group: (0, g, 0)),
            ]
        first = 1 + split_peers + 3
        held = prefetched(
            functools.partial(project_kernel, peers=split_peers, olds=len(held)),
            grid,
            specs_in
            + [
                whole((1, width)),
                whole((1, width)),
                pl.BlockSpec((1, 3 * feats, width), lambda p, s: (s[0], 0, 0)),
            ]
            + [pl.BlockSpec(memory_space=pl.ANY)] * len(held),
            outs,
            shapes,
            16 if fast else 60,
            cost(6 * span * width * feats, span * width * 4),
            "project",
            alias={first + k: k for k in range(len(held))},
        )(info, *chunk, gain_row, shift_row, w_in, *held)
    hat_own, feat, kv = held

    ids_full = pl.BlockSpec((1, 1, seq), lambda h, r: (h, 0, 0))
    feat_full = pl.BlockSpec((1, 3 * hs, seq), lambda h, r: (h, 0, 0))
    kv_full = pl.BlockSpec((1, seq, 2 * hs), lambda h, r: (h, 0, 0))
    bias_full = pl.BlockSpec((1, seq, clusters), lambda h, r: (h, 0, 0))
    head_rows = pl.BlockSpec((hs, rows), lambda h, r: (h, 0))
    mix_spec = pl.BlockSpec((1, 1, hs + 8, rows), lambda h, r: (h, r, 0, 0))
    stat_spec = pl.BlockSpec((1, hs + 8, clusters), lambda h, r: (h, 0, 0))
    cen_spec = pl.BlockSpec((1, hs, clusters), lambda h, r: (h, 0, 0))
    own_rows = groups * rows
    pair_flops = own_heads * own_rows * seq * 256

    one = [
        pl.BlockSpec(spec.block_shape, functools.partial(lambda h, f: f(h, 0), f=spec.index_map))
        for spec in (ids_full, feat_full, kv_full, bias_full, stat_spec, cen_spec, head_rows)
    ]
    ids_one, feat_one, kv_one, bias_one, stat_one, cen_one, rows_one = one
    part_one = pl.BlockSpec((1, hs + 16, clusters), lambda h: (h, 0, 0))
    mix_one = pl.BlockSpec((1, groups, hs + 8, rows), lambda h: (h, 0, 0, 0))
    all_groups = pl.BlockSpec((groups, hs, rows), lambda h: (0, h, 0))
    own_one = pl.BlockSpec((1, own_rows, 2 * hs), lambda h: (h, 0, 0))
    results = pl.pallas_call(
        functools.partial(forward_kernel, size=size, groups=groups, rows=rows),
        grid=(own_heads,),
        in_specs=[ids_one, feat_one, kv_one, bias_one],
        out_specs=[rows_one] * groups + [mix_one, stat_one, cen_one],
        out_shape=[array((feats, rows), BF)] * groups
        + [
            array((own_heads, groups, hs + 8, rows), F32),
            array((own_heads, hs + 8, clusters), F32),
            array((own_heads, hs, clusters), BF),
        ],
        compiler_params=params(32 if fast else 60, 1),
        cost_estimate=cost(6 * pair_flops, 8e6, own_heads * own_rows * seq),
        name="attend",
    )(ids_all, feat, kv, bias)
    attn_t = results[:groups]
    mixed, stats, centroid = results[groups:]

    arrived = [attn_t[0]] + [along_groups(attn_t[hop], hop) for hop in range(1, groups)]

    chunks = 4
    part = hidden // chunks
    w_out_g = w_out.reshape(groups, feats, width)
    gain_row2, shift_row2 = gain_two[None, :], shift_two[None, :]
    square = whole((rows, width))
    column = pl.BlockSpec((rows, part), lambda i, s: (0, i))
    norm_spec = whole((8, width))
    if fast:
        kept_shapes = [
            array((rows, hidden + hidden // 2 + width), BF),
            array((width + 16, rows), BF),
            array((rows, hidden // 2), BF),
            array((width + 16, rows), BF),
        ]
        kept_specs = [whole(item.shape) for item in kept_shapes]
        kept_specs[2] = pl.BlockSpec((rows, part // 2), lambda i, s: (0, i))
    else:
        kept_shapes = [
            array((8, width), F32),
            array((rows, hidden), BF),
            array((rows, width), BF),
            array((rows, hidden), BF),
            array((rows, width), BF),
        ]
        kept_specs = [norm_spec, column, square, column, square]
    results = prefetched(
        functools.partial(block_kernel, groups=groups, chunks=chunks, fast=fast),
        (chunks,),
        [whole((feats, rows))] * groups
        + [
            square,
            whole((1, width)),
            whole((1, width)),
            whole((groups, feats, width)),
            pl.BlockSpec((width, part), lambda i, s: (0, i)),
            pl.BlockSpec((part, width), lambda i, s: (i, 0)),
            square,
        ],
        [square, square] + kept_specs + [whole((feats, rows))] * groups,
        [array((rows, width), BF), array((rows, width), F32)]
        + kept_shapes
        + [array((feats, rows), BF)] * groups,
        28 if fast else 60,
        cost(8 * rows * width * hidden, 4 * width * hidden, rows * hidden),
        "feed",
        scratch=[
            pltpu.VMEM((rows, width), F32),
            pltpu.VMEM((rows, 128), F32),
            pltpu.VMEM((rows, width), BF),
            pltpu.VMEM((rows, width), F32),
            pltpu.VMEM((rows, width), F32),
        ],
    )(info, *arrived, tokens, gain_row2, shift_row2, w_out_g, w_up, w_down, cotangent)
    output, d_resid = results[:2]
    kept, d_attn = results[2:-groups], results[-groups:]
    grads = [d_attn[0]] + [along_groups(d_attn[hop], -hop) for hop in range(1, groups)]

    def weight_parts():
        far, low_far, act_own, low_own = kept
        got, low_got = along_peers(far, 1), along_peers(low_far, 1)
        high = block_rows + block_rows // 4 + 8
        chunk = pl.BlockSpec((rows, part), lambda i, s: (0, i ^ 2 ^ s[3]))
        branch = pl.BlockSpec((rows, width), lambda i, s: (0, hidden * 3 // 2 // width))
        act_spec = pl.BlockSpec((rows, part // 2), lambda i, s: (0, i))
        act_there = pl.BlockSpec((rows, part // 2), lambda i, s: (0, 2 * hidden // part + i))
        low_spec = whole((width + 16, rows))
        shape_u = (2, groups, high, width)
        shape_d = (2, groups, block_rows, width)
        send_u, keep_u, send_d, keep_d = prefetched(
            functools.partial(weights_kernel, groups=groups),
            (4,),
            [chunk, chunk, branch, branch, act_spec, act_there, low_spec, low_spec, square, square],
            [
                pl.BlockSpec((1,) + shape_u[1:], lambda i, s: (jnp.minimum(i, 1), 0, 0, 0)),
                pl.BlockSpec((1,) + shape_u[1:], lambda i, s: (jnp.maximum(i - 2, 0), 0, 0, 0)),
                whole(shape_d),
                whole(shape_d),
            ],
            [array(shape_u, BF), array(shape_u, BF), array(shape_d, BF), array(shape_d, BF)],
            28,
            cost(8 * rows * width * hidden, 6 * width * hidden),
            "weights",
            scratch=[pltpu.VMEM((groups, block_rows, width), F32)],
        )(info, far, got, far, got, act_own, got, low_own, low_got, cotangent, *cot_got)
        return send_u, keep_u, send_d, keep_d

    def weight_second(keep_u, got_u, keep_d, got_d):
        shape_u, shape_d = keep_u.shape, keep_d.shape
        high = shape_u[2]

        def block(shape, at):
            return pl.BlockSpec((1,) + shape[1:], lambda i: (at, 0, 0, 0))

        next_u, next_d = pl.pallas_call(
            second_kernel,
            grid=(1,),
            in_specs=[block(shape_u, 1), block(shape_u, 1), block(shape_d, 1), block(shape_d, 1)],
            out_specs=[whole(shape_u[1:]), whole(shape_d[1:])],
            out_shape=[array(shape_u[1:], BF), array(shape_d[1:], BF)],
            compiler_params=params(20, 1),
            cost_estimate=cost(groups * high * width * 2, groups * high * width * 12),
            name="second",
        )(keep_u, got_u, keep_d, got_d)
        return next_u, next_d

    def weight_third(keep_u, got_u, last_u, keep_d, got_d, last_d):
        shape_u, shape_d = keep_u.shape, keep_d.shape
        high = shape_u[2]

        def block(shape, at):
            return pl.BlockSpec((1,) + shape[1:], lambda i: (at, 0, 0, 0))

        tall = high + block_rows
        sums = pl.pallas_call(
            third_kernel,
            grid=(1,),
            in_specs=[
                block(shape_u, 0),
                block(shape_u, 0),
                whole(shape_u[1:]),
                block(shape_d, 0),
                block(shape_d, 0),
                whole(shape_d[1:]),
            ],
            out_specs=[whole((tall, width))] * groups,
            out_shape=[array((tall, width), BF)] * groups,
            compiler_params=params(24, 1),
            cost_estimate=cost(groups * tall * width * 4, groups * tall * width * 8),
            name="third",
        )(keep_u, got_u, last_u, keep_d, got_d, last_d)
        came = [sums[0]] + [along_groups(sums[hop], hop) for hop in range(1, groups)]
        return came

    def weight_sums(came, shape_u, shape_d):
        tall = shape_u[2] + shape_d[2]
        done = pl.pallas_call(
            fourth_kernel,
            grid=(1,),
            in_specs=[whole((tall, width))] * groups,
            out_specs=whole((tall, width)),
            out_shape=array((tall, width), BF),
            compiler_params=params(12, 1),
            cost_estimate=cost(groups * tall * width, groups * tall * width * 2),
            name="fourth",
        )(*came)
        from_x, from_y, from_xy = (along_dp(done, mask) for mask in (1, 2, 3))
        quarter = block_rows // 4
        total_up, total_out, total_down, norms = prefetched(
            spread_kernel,
            (4,),
            [whole((tall, width))] * 4,
            [
                pl.BlockSpec((block_rows, part), lambda i, s: (0, i ^ s[3])),
                pl.BlockSpec((quarter, width), lambda i, s: (i ^ s[3], 0)),
                pl.BlockSpec((block_rows, width), lambda i, s: (i ^ s[4], 0)),
                whole((8, width)),
            ],
            [
                array((block_rows, hidden), F32),
                array((block_rows, width), F32),
                array((hidden // wide, width), F32),
                array((8, width), F32),
            ],
            16,
            cost(1e6, 4 * tall * width * 6),
            "spread",
        )(info, done, from_x, from_y, from_xy)
        norm_own = lax.dynamic_slice_in_dim(norms, me * block_rows, block_rows, axis=1)
        return total_up, total_out, total_down, norm_own

    masks = [1 << k for k in range(n_dp.bit_length() - 1)]

    def reduce_rows(partial):
        blocks = partial.reshape(groups, peers, partial.shape[0] // wide, partial.shape[1])

        def of_peer(hop):
            at = (peer_at + hop) % peers
            return lax.dynamic_index_in_dim(blocks, at, axis=1, keepdims=False)

        total = of_peer(0).astype(F32)
        for hop in range(1, peers):
            total = total + along_peers(of_peer(hop), hop).astype(F32)
        total = total.astype(BF)

        def of_group(hop):
            return lax.dynamic_index_in_dim(total, (group_at + hop) % groups, keepdims=False)

        done = of_group(0).astype(F32)
        for hop in range(1, groups):
            done = done + along_groups(of_group(hop), hop).astype(F32)
        for mask in masks:
            done = done.astype(BF)
            done = done.astype(F32) + along_dp(done, mask).astype(F32)
        return done

    if fast:
        send_u, keep_u, send_d, keep_d = weight_parts()
        got_u, got_d = along_dp(send_u, 1), along_dp(send_d, 2)
        grads = after(grads, keep_u)
    else:
        norm_two, d_up, d_branch, act, normed_two = kept
        total_up = reduce_rows(tn(normed_two, d_up).astype(BF))
        total_down = reduce_rows(tn(act, cotangent).astype(BF))
        found = jnp.stack([nn(item, d_branch).astype(BF) for item in arrived])
        found = [
            lax.dynamic_index_in_dim(found, (group_at + groups - g) % groups, keepdims=False)
            for g in range(groups)
        ]
        total_out = reduce_rows(jnp.concatenate(found, axis=0))
        norm_own = reduce_rows(norm_two[:2].T.astype(BF)).T

    share = pl.pallas_call(
        functools.partial(sums_kernel, groups=groups),
        grid=(own_heads,),
        in_specs=[ids_one]
        + [rows_one] * groups
        + [mix_one],
        out_specs=part_one,
        out_shape=array((own_heads, hs + 16, clusters), F32),
        compiler_params=params(16 if fast else 60, 1),
        cost_estimate=cost(own_heads * own_rows * clusters * 160, 2e6),
        name="sums",
    )(ids_all, *grads, mixed)
    share_got = [along_peers(share, hop) for hop in range(1, peers)]

    back_shapes = [
        array((groups, feats, rows), BF),
        array((own_heads, 2 * hs, own_rows), F32),
        array((own_heads, 2 * hs, max(peers - 1, 1) * own_rows), BF),
    ]
    dq, dkv_own, dkv_send = pl.pallas_call(
        functools.partial(back_kernel, size=size, groups=groups, gots=len(share_got)),
        grid=(own_heads,),
        in_specs=[ids_one, feat_one, kv_one, bias_one]
        + [rows_one] * groups
        + [mix_one, stat_one, cen_one]
        + [part_one] * (1 + len(share_got)),
        out_specs=[
            all_groups,
            pl.BlockSpec((1,) + back_shapes[1].shape[1:], lambda h: (h, 0, 0)),
            pl.BlockSpec((1,) + back_shapes[2].shape[1:], lambda h: (h, 0, 0)),
        ],
        out_shape=back_shapes,
        scratch_shapes=[pltpu.VMEM((seq, 2 * hs), F32), pltpu.VMEM((seq, 2 * clusters), BF)],
        compiler_params=params(36 if fast else 62, 1),
        cost_estimate=cost(14 * pair_flops, 10e6, own_heads * own_rows * seq),
        name="back",
    )(ids_all, feat, kv, bias, *grads, mixed, stats, centroid, share, *share_got)
    dkv_got = [
        along_peers(
            dkv_send if peers == 2 else dkv_send[..., (hop - 1) * own_rows : hop * own_rows], hop
        )
        for hop in range(1, peers)
    ]
    if fast:
        dkv_own = after(dkv_own, got_d)
    d_in = pl.pallas_call(
        functools.partial(join_kernel, groups=groups),
        grid=(1,),
        in_specs=[whole(back_shapes[0].shape), whole(back_shapes[1].shape)]
        + [whole(back_shapes[1].shape)] * len(dkv_got),
        out_specs=[whole((own_heads, 3 * hs, rows))] * groups,
        out_shape=[array((own_heads, 3 * hs, rows), BF)] * groups,
        compiler_params=params(20, 1),
        cost_estimate=cost(own_rows * feats * 8, own_rows * feats * 16),
        name="join",
    )(dq, dkv_own, *dkv_got)

    home = [d_in[0]] + [along_groups(d_in[hop], hop) for hop in range(1, groups)]

    tall = block_rows + 16
    part_spec = [whole((own_heads, 3 * hs, rows))] * groups + [whole((width, own_rows))]
    inward = functools.partial(
        prefetched,
        functools.partial(inward_kernel, groups=groups, fast=fast),
        (1,),
        part_spec,
    )
    spent = cost(2 * own_rows * width * 3 * feats, 4e6)
    if fast:
        half = groups // 2
        blocks = (groups, tall, 3 * feats)
        next_u, next_d = weight_second(keep_u, after(got_u, dq), keep_d, after(got_d, dq))
        last_u, last_d = along_dp(next_u, 2), along_dp(next_d, 1)
        keep, far = inward(
            [whole(blocks)] * 2, [array(blocks, BF)] * 2, 24, spent, "inward"
        )(info, *after(d_in, last_u, last_d), hat_own)
        came = weight_third(keep_u, got_u, last_u, keep_d, got_d, last_d)
        got = along_peers(after(far, home, came[0]), 1)
        total = keep.astype(F32) + got.astype(F32)
        one_half, two_half = total[:half].astype(BF), total[half:].astype(BF)
        for mask in (1, 2):
            got_one, got_two = along_dp(one_half, mask), along_dp(two_half, 3 - mask)
            one_half = (one_half.astype(F32) + got_one.astype(F32)).astype(BF)
            two_half = (two_half.astype(F32) + got_two.astype(F32)).astype(BF)
            if mask == 1:
                one_half, two_half = after((one_half, two_half), came)
        total_up, total_out, total_down, norm_own = weight_sums(
            came, keep_u.shape, keep_d.shape
        )
        items = [one_half[k] for k in range(half)] + [two_half[k] for k in range(half)]
    else:
        found, more = inward(
            [whole((width, 3 * feats)), whole((16, 3 * feats))],
            [array((width, 3 * feats), F32), array((16, 3 * feats), F32)],
            60,
            spent,
            "inward",
        )(info, *d_in, hat_own)
        found = found.reshape(groups, peers, block_rows, 3 * feats)
        more = jnp.broadcast_to(more, (groups, peers, 16, 3 * feats))
        found = jnp.concatenate([found, more], axis=2).astype(BF)

        def of_peer(hop):
            at = (peer_at + hop) % peers
            return lax.dynamic_index_in_dim(found, at, axis=1, keepdims=False)

        total = of_peer(0).astype(F32)
        for hop in range(1, peers):
            total = total + along_peers(of_peer(hop), hop).astype(F32)
        for mask in masks:
            total = total.astype(BF)
            total = total.astype(F32) + along_dp(total, mask).astype(F32)
        total = total.astype(BF)
        items = [
            lax.dynamic_index_in_dim(total, (group_at + hop) % groups, keepdims=False)
            for hop in range(groups)
        ]
    pieces = [items[0]] + [along_groups(items[hop], hop) for hop in range(1, groups)]

    grad_tokens = prefetched(
        functools.partial(final_kernel, groups=groups),
        (1,),
        [whole((own_heads, 3 * hs, rows))] * groups
        + [square, square, whole((1, width)), whole((groups, 3 * feats, width))],
        square,
        array((rows, width), BF),
        24 if fast else 60,
        cost(6 * rows * width * width, 6 * width * width),
        "final",
    )(info, *home, tokens, d_resid, gain_row, w_in)

    pieces = jnp.stack(pieces)
    pieces = jnp.stack(
        [
            lax.dynamic_index_in_dim(pieces, (group_at + groups - g) % groups, keepdims=False)
            for g in range(groups)
        ]
    ).astype(F32)
    q_part = pieces[:, :, :feats].transpose(1, 0, 2).reshape(tall, width)
    kv_part = (
        pieces[:, :, feats:]
        .reshape(groups, tall, 2, feats)
        .transpose(1, 2, 0, 3)
        .reshape(tall, 2 * width)
    )
    at = me * block_rows
    wq_rows = lax.dynamic_slice_in_dim(w_query, at, block_rows).astype(F32)
    wkv_rows = lax.dynamic_slice_in_dim(w_keyval, at, block_rows).astype(F32)
    gain_own = lax.dynamic_slice_in_dim(gain_one, at, block_rows)
    shift_own = lax.dynamic_slice_in_dim(shift_one, at, block_rows)
    q_sum, kv_sum = q_part[block_rows], kv_part[block_rows]
    q_part, kv_part = q_part[:block_rows], kv_part[:block_rows]
    shift_grad = jnp.sum(wq_rows * q_sum, axis=1) + jnp.sum(wkv_rows * kv_sum, axis=1)
    along = jnp.sum(wq_rows * q_part, axis=1) + jnp.sum(wkv_rows * kv_part, axis=1)
    return (
        output,
        grad_tokens,
        q_part + shift_own[:, None] * q_sum,
        kv_part + shift_own[:, None] * kv_sum,
        total_out,
        total_up,
        total_down,
        along / gain_own,
        shift_grad,
        norm_own[0],
        norm_own[1],
    )


def solution(mesh):
    return jax.shard_map(
        per_device,
        mesh=mesh,
        in_specs=(
            P(("dp", "wide"), None),
            P(("dp", "wide"), None),
            P("dp"),
            P("dp", None, "wide", None),
            P(),
            P(),
            P(),
            P(),
            P(),
            P(),
            P(),
            P(),
            P(),
            P(("dp", "wide"), None),
        ),
        out_specs=(
            P(("dp", "wide"), None),
            P(("dp", "wide"), None),
            P("wide", None),
            P("wide", None),
            P("wide", None),
            P("wide", None),
            P("wide", None),
            P("wide"),
            P("wide"),
            P("wide"),
            P("wide"),
        ),
        check_vma=False,
    )
```

```python
import functools
import math

import jax
import jax.numpy as jnp
import numpy as np
from jax import lax
from jax.experimental import pallas as pl
from jax.experimental.pallas import tpu as pltpu
from jax.sharding import PartitionSpec as P

EPSILON = 1e-05
NEGATIVE = -1e30
EXCLUDED = -3e30
GELU_A = math.sqrt(2.0 / math.pi)
GELU_B = 0.044715
BF = jnp.bfloat16
F32 = jnp.float32


def nn(left, right):
    return lax.dot_general(left, right, (((1,), (0,)), ((), ())), preferred_element_type=F32)


def nt(left, right):
    return lax.dot_general(left, right, (((1,), (1,)), ((), ())), preferred_element_type=F32)


def tn(left, right):
    return lax.dot_general(left, right, (((0,), (0,)), ((), ())), preferred_element_type=F32)


def params(mib, dims):
    return pltpu.CompilerParams(
        vmem_limit_bytes=mib * 1024 * 1024, dimension_semantics=("arbitrary",) * dims
    )


def cost(flops, nbytes, trans=0):
    return pl.CostEstimate(flops=int(flops), bytes_accessed=int(nbytes), transcendentals=int(trans))


def split_low(values):
    high = values.astype(BF)
    return high, (values - high.astype(F32)).astype(BF)


def one_hot_t(ids_row, clusters):
    rows = lax.broadcasted_iota(jnp.int32, (clusters, ids_row.shape[1]), 0)
    return jnp.where(rows == ids_row, 1.0, 0.0).astype(BF)


def key_passes(total, size, score, weigh, blocks=None):
    count = total // size
    if count <= 4:
        if blocks is None:
            blocks = [score(index) for index in range(count)]
        peak = functools.reduce(jnp.maximum, [jnp.max(b, axis=0, keepdims=True) for b in blocks])
        denom, sums = 0.0, None
        for index in range(count):
            expo = jnp.exp(blocks[index] - peak)
            denom = denom + jnp.sum(expo, axis=0, keepdims=True)
            parts = weigh(index, expo)
            sums = parts if sums is None else tuple(x + y for x, y in zip(sums, parts))
        return peak, denom, sums

    def step(index, carry):
        peak, denom, sums = carry
        block = score(index)
        fresh = jnp.maximum(peak, jnp.max(block, axis=0, keepdims=True))
        expo = jnp.exp(block - fresh)
        fade = jnp.exp(peak - fresh)
        parts = weigh(index, expo)
        return (
            fresh,
            denom * fade + jnp.sum(expo, axis=0, keepdims=True),
            tuple(old * fade + new for old, new in zip(sums, parts)),
        )

    shapes = jax.eval_shape(lambda: (score(0), weigh(0, score(0))))
    lanes = shapes[0].shape[1]
    start = (
        jnp.full((1, lanes), NEGATIVE, F32),
        jnp.zeros((1, lanes), F32),
        tuple(jnp.zeros(item.shape, F32) for item in shapes[1]),
    )
    return lax.fori_loop(0, count, step, start)


def key_sum(total, size, step, start):
    count = total // size
    if count <= 4:
        for index in range(count):
            start = step(index, start)
        return start
    return lax.fori_loop(0, count, step, start)


def spot_of(index, size):
    if isinstance(index, int):
        return pl.ds(index * size, size)
    return pl.ds(pl.multiple_of(index * size, size), size)


def piece(ref, index, size, axis):
    spot = spot_of(index, size)
    return ref[spot, :] if axis == 0 else ref[:, spot]


def table_kernel(*refs, picks):
    parts, out = refs[:-1], refs[-1]
    total = parts[0][:, :picks]
    for part in parts[1:]:
        total = total + part[:, :picks]
    out[:, :picks] = total
    rows = parts[0].shape[1] - picks
    for group, part in enumerate(parts):
        out[:, picks + group * rows : picks + (group + 1) * rows] = part[:, picks:]


def bias_kernel(info, *refs, groups, peers, rows, picks):
    tables, (bias_ref, ids_ref) = refs[:peers], refs[peers:]
    part = pl.program_id(0)
    owner = (
        lax.rem(info[0] + part // peers, groups) * peers + lax.rem(info[1] + part % peers, peers)
    )
    heads, _, clusters = tables[0].shape
    place = owner * rows + lax.broadcasted_iota(jnp.int32, (rows, clusters), 0)
    plain = jnp.where(place >= info[2], EXCLUDED, NEGATIVE)
    for head in range(heads):
        top = tables[0][head, :picks]
        for table in tables[1:]:
            top = top + table[head, :picks]
        value = plain
        for pick in range(picks):
            value = jnp.where(place == top[pick : pick + 1, :], 0.0, value)
        bias_ref[head] = value.astype(BF)

    @pl.when(part == 0)
    def ids():
        lines = rows // clusters
        for head in range(heads):
            row = []
            for group in range(groups):
                for table in tables:
                    for line in range(lines):
                        at = picks + group * lines + line
                        row.append(table[head, at : at + 1, :])
            ids_ref[head] = jnp.concatenate(row, axis=1)


def project_kernel(info, *refs, peers, olds):
    parts = refs[:peers]
    gain_ref, shift_ref, w_ref = refs[peers : peers + 3]
    hat_ref, feat_ref, kv_ref = refs[peers + 3 + olds :]
    rows = hat_ref.shape[1]
    for peer in range(peers):
        values = parts[peer][...].astype(F32)
        centered = values - jnp.mean(values, axis=-1, keepdims=True)
        variance = jnp.mean(centered * centered, axis=-1, keepdims=True)
        scaled = centered * lax.rsqrt(variance + EPSILON) * gain_ref[...]
        if peer == 0:
            hat_ref[...] = scaled.astype(BF).T
        low = (scaled + shift_ref[...]).astype(BF)
        found = nt(w_ref[0], low)
        heads, triple = feat_ref.shape[0], feat_ref.shape[1]
        hs = triple // 3
        spot = slice(peer * rows, (peer + 1) * rows)
        for head in range(heads):
            base = head * triple
            query = (found[base : base + hs] * 0.125).astype(BF)
            pair = found[base + hs : base + triple].astype(BF)
            feat_ref[head, :hs, spot] = query
            feat_ref[head, hs:, spot] = pair
            kv_ref[head, spot, :] = pair.T


def forward_kernel(ids_all, feat, kv, bias, *refs, size, groups, rows):
    outs = refs[:groups]
    mix_ref, stat_ref, cen_ref = refs[groups:]
    hs = feat.shape[1] // 3
    keys = kv.shape[1]
    count = keys // size
    clusters = bias.shape[2]
    kv_h, bias_h = kv.at[0], bias.at[0]
    queries_all, kvt = feat.at[0, :hs], feat.at[0, hs:]
    hot_all = one_hot_t(ids_all[0], clusters)
    ones = jnp.ones((16, keys), BF)
    sums = nt(jnp.concatenate([queries_all[...], ones], axis=0), hot_all)
    counts = sums[hs : hs + 1]
    centroid = (sums[:hs] / jnp.maximum(counts, 1.0)).astype(BF)
    padded = jnp.concatenate([centroid, jnp.zeros_like(centroid)], axis=0)

    def cluster_score(index):
        scores = nn(piece(kv_h, index, size, 0), padded)
        outside = piece(bias_h, index, size, 0).astype(F32) < 2.0 * NEGATIVE
        return jnp.where(outside, NEGATIVE, scores)

    def cluster_weigh(index, expo):
        top = piece(bias_h, index, size, 0).astype(F32) == 0.0
        mass = jnp.sum(jnp.where(top, expo, 0.0), axis=0, keepdims=True)
        other = jnp.where(top, 0.0, expo).astype(BF)
        return nn(piece(kvt, index, size, 1), other), mass

    peers = keys // (groups * rows)
    hots, sides = [], []
    for group in range(groups):
        spot = slice(group * peers * rows, group * peers * rows + rows)
        hot = one_hot_t(ids_all[0, :, spot], clusters)
        queries = queries_all[:, spot]
        hots.append(hot)
        sides.append(jnp.concatenate([queries, jnp.zeros_like(queries), hot], axis=0))

    def member_score(group, index):
        both = jnp.concatenate([piece(kv_h, index, size, 0), piece(bias_h, index, size, 0)], axis=1)
        return nn(both, sides[group])

    def member_weigh(index, expo):
        return (nn(piece(kvt, index, size, 1), expo.astype(BF)),)

    short = count <= 4
    ahead = None
    if short:
        ahead = [member_score(0, index) for index in range(count)]
    peak, denom, (rest, mass) = key_passes(keys, size, cluster_score, cluster_weigh)
    rest = rest[hs:] / denom
    mass = mass / denom
    blank = jnp.zeros((5, clusters), F32)
    stats = jnp.concatenate([rest, mass, peak + jnp.log(denom), counts, blank], axis=0)
    stat_ref[0] = stats
    cen_ref[0] = centroid
    high, low = split_low(stats)
    table = jnp.concatenate([high, low], axis=1)
    for group in range(groups):
        gathered = nn(table, jnp.concatenate([hots[group], hots[group]], axis=0))
        blocks, ahead = ahead, None
        if short and group + 1 < groups:
            ahead = [member_score(group + 1, index) for index in range(count)]
        score = functools.partial(member_score, group)
        peak, denom, (mix,) = key_passes(keys, size, score, member_weigh, blocks)
        mix = mix[hs:] / denom
        outs[group][...] = (gathered[hs : hs + 1] * mix + gathered[:hs]).astype(BF)
        level = jnp.broadcast_to(peak + jnp.log(denom), (8, rows))
        mix_ref[0, group] = jnp.concatenate([mix, level], axis=0)


def sums_kernel(ids_own, *refs, groups):
    grads, (mix_ref, part_ref) = refs[:groups], refs[groups:]
    hs = grads[0].shape[0]
    total = None
    for group in range(groups):
        rows = grads[group].shape[1]
        step = ids_own.shape[2] // groups
        hot = one_hot_t(ids_own[0, :, group * step : group * step + rows], part_ref.shape[2])
        grad = grads[group][...]
        along = jnp.sum(grad.astype(F32) * mix_ref[0, group, :hs], axis=0, keepdims=True)
        high, low = split_low(along)
        pad = jnp.zeros((14, rows), BF)
        part = nt(jnp.concatenate([grad, high, low, pad], axis=0), hot)
        total = part if total is None else total + part
    part_ref[0] = total


def back_kernel(ids_all, feat, kv, bias, *refs, size, groups, gots):
    grads = refs[:groups]
    mix_ref, stat_ref, cen_ref = refs[groups : groups + 3]
    shares = refs[groups + 3 : groups + 4 + gots]
    dq_ref, own_ref, send_ref, total, both = refs[groups + 4 + gots :]
    hs, rows = grads[0].shape
    keys = kv.shape[1]
    count = keys // size
    peers = keys // (groups * rows)
    clusters = bias.shape[2]
    kv_h, bias_h = kv.at[0], bias.at[0]
    queries_all, kvt = feat.at[0, :hs], feat.at[0, hs:]
    stats = stat_ref[0]
    high, low = split_low(stats[hs : hs + 8])
    table = jnp.concatenate([high, low], axis=1)
    hots, sides, levels, deltas, pads, rights = [], [], [], [], [], []
    for group in range(groups):
        spot = slice(group * peers * rows, group * peers * rows + rows)
        hot = one_hot_t(ids_all[0, :, spot], clusters)
        queries = queries_all[:, spot]
        blank = jnp.zeros_like(queries)
        hots.append(jnp.concatenate([hot, hot], axis=0))
        sides.append(jnp.concatenate([queries, blank, hot], axis=0))
        mass = nn(table, hots[group])[0:1]
        back = (mass * grads[group][...].astype(F32)).astype(BF)
        levels.append(mix_ref[0, group, hs : hs + 1])
        deltas.append(jnp.sum(back.astype(F32) * mix_ref[0, group, :hs], axis=0, keepdims=True))
        pads.append(jnp.concatenate([blank, back], axis=0))
        turned = jnp.concatenate([queries, blank], axis=0)
        rights.append(jnp.concatenate([turned, pads[group]], axis=1).T)

    def scores(group, index):
        kv_c = piece(kv_h, index, size, 0)
        pair = jnp.concatenate([kv_c, piece(bias_h, index, size, 0)], axis=1)
        return nn(pair, sides[group]), nn(kv_c, pads[group])

    def finish(group, index, found, dq):
        weights = jnp.exp(found[0] - levels[group])
        grad_s = (weights * (found[1] - deltas[group])).astype(BF)
        part = nn(jnp.concatenate([grad_s, weights.astype(BF)], axis=1), rights[group])
        spot = spot_of(index, size)
        if group == 0:
            total[spot, :] = part
        else:
            total[spot, :] += part
        return dq + nn(piece(kvt, index, size, 1), grad_s)

    rest, mass = stats[:hs], stats[hs : hs + 1]
    level, counts = stats[hs + 1 : hs + 2], stats[hs + 2 : hs + 3]
    centroid = cen_ref[0]
    part = shares[0][0]
    for share in shares[1:]:
        part = part + share[0]
    d_rest = part[:hs].astype(BF)
    d_mass = part[hs : hs + 1] + part[hs + 1 : hs + 2]
    delta = jnp.sum(d_rest.astype(F32) * rest, axis=0, keepdims=True) + d_mass * mass
    cen_pad = jnp.concatenate([centroid, jnp.zeros_like(centroid)], axis=0)
    rest_pad = jnp.concatenate([jnp.zeros_like(centroid), d_rest], axis=0)
    right = jnp.concatenate([cen_pad, rest_pad], axis=1).T

    def cluster_step(index, summed):
        kv_c = piece(kv_h, index, size, 0)
        marks = piece(bias_h, index, size, 0).astype(F32)
        probs = jnp.exp(nn(kv_c, cen_pad) - level)
        probs = jnp.where(marks < 2.0 * NEGATIVE, 0.0, probs)
        top = marks == 0.0
        d_probs = jnp.where(top, d_mass, nn(kv_c, rest_pad))
        d_score = (probs * (d_probs - delta)).astype(BF)
        other = jnp.where(top, 0.0, probs).astype(BF)
        both[spot_of(index, size), :] = jnp.concatenate([d_score, other], axis=1)
        return summed + nn(piece(kvt, index, size, 1), d_score)

    start = jnp.zeros((2 * hs, rows), F32)
    zero = jnp.zeros((2 * hs, clusters), F32)
    member_dq = []
    if count <= 4:
        tasks = [(group, index) for group in range(groups) for index in range(count)]
        ahead = scores(*tasks[0])
        d_cen = key_sum(keys, size, cluster_step, zero)
        dq = start
        for step, (group, index) in enumerate(tasks):
            found = ahead
            if step + 1 < len(tasks):
                ahead = scores(*tasks[step + 1])
            dq = finish(group, index, found, dq)
            if index == count - 1:
                member_dq.append(dq[:hs] * 0.125)
                dq = start
    else:
        d_cen = key_sum(keys, size, cluster_step, zero)
        for group in range(groups):

            def step(index, dq, group=group):
                return finish(group, index, scores(group, index), dq)

            member_dq.append(lax.fori_loop(0, count, step, start)[:hs] * 0.125)
    d_cen = d_cen[:hs] * 0.125 / jnp.maximum(counts, 1.0)
    high, low = split_low(d_cen)
    table = jnp.concatenate([high, low], axis=1)
    for group in range(groups):
        base = group * peers * rows
        dq_ref[group] = (member_dq[group] + nn(table, hots[group])).astype(BF)
        own = total[base : base + rows, :] + nn(both[base : base + rows, :], right)
        own_ref[0, :, group * rows : (group + 1) * rows] = own.T
        for peer in range(1, peers):
            spot = (peer - 1) * groups * rows + group * rows
            found = total[base + peer * rows : base + (peer + 1) * rows, :]
            send_ref[0, :, spot : spot + rows] = found.astype(BF).T


def join_kernel(dq_ref, own_ref, *refs, groups):
    gots, outs = refs[:-groups], refs[-groups:]
    heads, _, rows = outs[0].shape
    hs = dq_ref.shape[1] // heads
    for head in range(heads):
        for group in range(groups):
            spot = slice(group * rows, (group + 1) * rows)
            pair = own_ref[head, :, spot]
            for got in gots:
                pair = pair + got[head, :, spot].astype(F32)
            outs[group][head, :hs] = dq_ref[group, head * hs : (head + 1) * hs]
            outs[group][head, hs:] = pair.astype(BF)


def block_kernel(info, *refs, groups, chunks, fast):
    (attn, rest) = (refs[:groups], refs[groups:])
    x_ref, gain_ref, shift_ref, wo_ref, up_ref, down_ref, cot_ref = rest[:7]
    out_ref, dres_ref = rest[7:9]
    if fast:
        far_ref, low_far, act_ref, low_ref = rest[9:13]
        rest = rest[13:]
        hidden = far_ref.shape[1] * 4 // 7
    else:
        dn_ref, dup_ref, dbr_ref, act_ref, low_ref = rest[9:14]
        rest = rest[14:]
    dat = rest[:groups]
    hat_ref, inv_ref, normed, back, total = rest[groups:]
    index = pl.program_id(0)

    @pl.when(index == 0)
    def before():
        resid = x_ref[...].astype(F32)
        for group in range(groups):
            owner = lax.rem(info[0] + groups - group, groups)
            resid = resid + tn(attn[group][...], wo_ref[owner])
        total[...] = resid
        centered = resid - jnp.mean(resid, axis=-1, keepdims=True)
        variance = jnp.mean(centered * centered, axis=-1, keepdims=True)
        inverse = lax.rsqrt(variance + EPSILON)
        hat = centered * inverse
        hat_ref[...] = hat
        inv_ref[...] = jnp.broadcast_to(inverse, inv_ref.shape)
        low = (hat * gain_ref[...] + shift_ref[...]).astype(BF)
        normed[...] = low
        if fast:
            feats = attn[0].shape[0]
            half = feats // 2
            turned = low.T
            for group in range(groups):
                first = turned[group * feats : group * feats + half]
                second = turned[group * feats + half : (group + 1) * feats]
                spot = slice(group * half, (group + 1) * half)
                low_ref[spot, :] = jnp.where(info[1] == 0, first, second)
                low_far[spot, :] = jnp.where(info[1] == 0, second, first)
                first = attn[group][:half]
                second = attn[group][half:]
                spot = slice((groups + group) * half, (groups + group + 1) * half)
                low_ref[spot, :] = jnp.where(info[1] == 0, first, second)
                low_far[spot, :] = jnp.where(info[1] == 0, second, first)
        else:
            low_ref[...] = low
        back[...] = jnp.zeros_like(back)

    up = nn(normed[...], up_ref[...])
    grad_act = nt(cot_ref[...], down_ref[...])
    square = up * up
    inner = GELU_A * (up + GELU_B * up * square)
    curve = jnp.tanh(inner)
    act = (0.5 * up * (1.0 + curve)).astype(BF)
    slope = 0.5 * (1.0 + curve) + 0.5 * up * (1.0 - curve * curve) * (
        GELU_A * (1.0 + 3.0 * GELU_B * square)
    )
    d_up = (grad_act * slope).astype(BF)
    if fast:
        part = act.shape[1]
        half = part // 2
        first, second = act[:, :half], act[:, half:]
        act_ref[...] = jnp.where(info[1] == 0, first, second)
        far_ref[:, pl.ds(pl.multiple_of(index * part, part), part)] = d_up
        spot = pl.ds(pl.multiple_of(hidden + index * half, half), half)
        far_ref[:, spot] = jnp.where(info[1] == 0, second, first)
    else:
        dup_ref[...] = d_up
        act_ref[...] = act
    back[...] += nt(d_up, up_ref[...])
    total[...] += nn(act, down_ref[...])

    @pl.when(index == chunks - 1)
    def after():
        out_ref[...] = total[...].astype(BF)
        d_normed = back[...]
        hat = hat_ref[...]
        gain_part = jnp.sum(d_normed * hat, axis=0, keepdims=True)
        shift_part = jnp.sum(d_normed, axis=0, keepdims=True)
        if fast:
            rows, width = low_far.shape[1], d_normed.shape[1]
            fold = []
            for part_row in split_low(gain_part) + split_low(shift_part):
                fold += [part_row[:, k : k + rows].astype(F32) for k in range(0, width, rows)]
            fold.append(jnp.zeros((low_far.shape[0] - width - len(fold), rows), F32))
            folded = jnp.concatenate(fold, axis=0).astype(BF)
            low_far[width:, :] = folded
            low_ref[width:, :] = folded
        else:
            blank = jnp.zeros((6, d_normed.shape[1]), F32)
            dn_ref[...] = jnp.concatenate([gain_part, shift_part, blank], axis=0)
        gy = d_normed * gain_ref[...]
        mean_one = jnp.mean(gy, axis=-1, keepdims=True)
        mean_two = jnp.mean(gy * hat, axis=-1, keepdims=True)
        d_resid = cot_ref[...].astype(F32) + inv_ref[:, 0:1] * (gy - mean_one - hat * mean_two)
        dres_ref[...] = d_resid
        branch = d_resid.astype(BF)
        if fast:
            far_ref[:, hidden * 3 // 2 :] = branch
        else:
            dbr_ref[...] = branch
        for group in range(groups):
            owner = lax.rem(info[0] + groups - group, groups)
            dat[group][...] = nt(wo_ref[owner], branch).astype(BF)


def weights_kernel(info, *refs, groups):
    (dup, dup_got, dbr, dbr_got, act, act_got, low, low_got, cot, cot_got) = refs[:10]
    send_u, keep_u, send_d, keep_d, outs = refs[10:]
    width = cot.shape[1]
    index = pl.program_id(0)
    group_at, place_u, place_d = info[0], info[3], info[4]
    rows = width // (2 * groups)
    quarter = rows // 4
    stay = groups * rows

    @pl.when(index == 0)
    def first():
        found = nn(low[stay:width, :], dbr[...]) + nn(low_got[stay:width, :], dbr_got[...])
        fold = low[width:, :].astype(F32) + low_got[width:, :].astype(F32)
        times = width // fold.shape[1]
        norms = []
        for part in range(2):
            both = fold[2 * part * times : (2 * part + 1) * times]
            both = both + fold[(2 * part + 1) * times : (2 * part + 2) * times]
            norms.append(jnp.concatenate([both[k : k + 1] for k in range(times)], axis=1))
        norms = jnp.concatenate(norms + [jnp.zeros((6, width), F32)], axis=0)
        for group in range(groups):
            block = found[group * rows : (group + 1) * rows]
            outs[group] = block
            for part in range(4):
                tail = block[part * quarter + 16 : (part + 1) * quarter]
                tail = jnp.concatenate([tail, norms], axis=0).astype(BF)
                place = lax.bitwise_xor(part, place_d)

                @pl.when(place >= 2)
                def leaves_more():
                    send_d[place - 2, (groups - group) % groups, rows:] = tail

                @pl.when(place < 2)
                def stays_more():
                    keep_d[place, (groups - group) % groups, rows:] = tail

    up = nn(low[:stay, :], dup[...]) + nn(low_got[:stay, :], dup_got[...])
    at = lax.bitwise_xor(lax.bitwise_xor(index, 2), place_u)
    for group in range(groups):
        spot = lax.rem(group + groups - group_at, groups)
        block = up[group * rows : (group + 1) * rows].astype(BF)
        away = (groups - group) % groups
        start = pl.multiple_of(at * quarter, 8)
        other = outs[group, pl.ds(start, 16), :].astype(BF)

        @pl.when(index < 2)
        def leaves():
            send_u[0, spot, :rows] = block
            send_u[0, away, rows:] = other

        @pl.when(index >= 2)
        def stays():
            keep_u[0, spot, :rows] = block
            keep_u[0, away, rows:] = other

    down = tn(act[...], cot[...]) + tn(act_got[...], cot_got[...])
    spot = lax.rem(index + groups - group_at, groups)
    for part in range(4):
        block = down[part * rows : (part + 1) * rows].astype(BF)
        place = lax.bitwise_xor(part, place_d)

        @pl.when(place >= 2)
        def leaves_down():
            send_d[place - 2, spot, :rows] = block

        @pl.when(place < 2)
        def stays_down():
            keep_d[place, spot, :rows] = block


def second_kernel(keep_u, got_u, keep_d, got_d, send_u, send_d):
    send_u[...] = (keep_u[0].astype(F32) + got_u[0].astype(F32)).astype(BF)
    send_d[...] = (keep_d[0].astype(F32) + got_d[0].astype(F32)).astype(BF)


def third_kernel(keep_u, got_u, last_u, keep_d, got_d, last_d, *outs):
    rows = keep_u.shape[2]
    for group in range(len(outs)):
        up = keep_u[0, group].astype(F32) + got_u[0, group].astype(F32) + last_u[group].astype(F32)
        down = keep_d[0, group].astype(F32) + got_d[0, group].astype(F32) + last_d[group].astype(F32)
        outs[group][:rows] = up.astype(BF)
        outs[group][rows:] = down.astype(BF)


def fourth_kernel(*refs):
    parts, out = refs[:-1], refs[-1]
    total = parts[0][...].astype(F32)
    for part in parts[1:]:
        total = total + part[...].astype(F32)
    out[...] = total.astype(BF)


def spread_kernel(info, own, from_x, from_y, from_xy, up_ref, out_ref, down_ref, norm_ref):
    index = pl.program_id(0)
    rows = up_ref.shape[0]
    quarter = out_ref.shape[0] // 4
    high = own.shape[0] // 2
    for place, part in enumerate((own, from_y, from_x, from_xy)):

        @pl.when(index == place)
        def upper(part=part):
            up_ref[...] = part[:rows].astype(F32)
            at = pl.multiple_of(lax.bitwise_xor(index, info[3]) * quarter, 8)
            out_ref[pl.ds(at, 16), :] = part[rows:high].astype(F32)

    for place, part in enumerate((own, from_x, from_y, from_xy)):

        @pl.when(index == place)
        def lower(part=part):
            down_ref[...] = part[high : high + rows].astype(F32)
            tail = part[high + rows :].astype(F32)
            at = pl.multiple_of(lax.bitwise_xor(index, info[4]) * quarter + 16, 8)
            out_ref[pl.ds(at, quarter - 16), :] = tail[: quarter - 16]

            @pl.when(lax.bitwise_xor(index, info[4]) == 0)
            def norms():
                norm_ref[...] = tail[quarter - 16 :]


def inward_kernel(info, *refs, groups, fast):
    parts, hat_ref = refs[:groups], refs[groups]
    outs = refs[groups + 1 :]
    heads, triple, rows = parts[0].shape
    hs = triple // 3
    total, sums = None, None
    ones = jnp.ones((16, rows), BF)
    for group in range(groups):
        order = [parts[group][h, k * hs : (k + 1) * hs] for k in range(3) for h in range(heads)]
        turned = jnp.concatenate(order, axis=0)
        found = nt(hat_ref[:, group * rows : (group + 1) * rows], turned)
        more = nt(ones, turned)
        total = found if total is None else total + found
        sums = more if sums is None else sums + more
    if not fast:
        outs[0][...] = total
        outs[1][...] = sums
        return
    own_ref, far_ref = outs
    block = total.shape[0] // (2 * groups)
    low_sums = sums.astype(BF)
    for group in range(groups):
        spot = lax.rem(group + groups - info[0], groups)
        first = total[2 * group * block : (2 * group + 1) * block].astype(BF)
        second = total[(2 * group + 1) * block : (2 * group + 2) * block].astype(BF)
        own_ref[spot, :block] = jnp.where(info[1] == 0, first, second)
        far_ref[spot, :block] = jnp.where(info[1] == 0, second, first)
        own_ref[spot, block:] = low_sums
        far_ref[spot, block:] = low_sums


def final_kernel(info, *refs, groups):
    parts = refs[:groups]
    x_ref, dres_ref, gain_ref, w_ref, out_ref = refs[groups:]
    d_normed = jnp.zeros(dres_ref.shape, F32)
    for group in range(groups):
        owner = lax.rem(info[0] + groups - group, groups)
        heads, triple, rows = parts[group].shape
        d_normed = d_normed + tn(parts[group][...].reshape(heads * triple, rows), w_ref[owner])
    values = x_ref[...].astype(F32)
    centered = values - jnp.mean(values, axis=-1, keepdims=True)
    variance = jnp.mean(centered * centered, axis=-1, keepdims=True)
    inverse = lax.rsqrt(variance + EPSILON)
    hat = centered * inverse
    gy = d_normed * gain_ref[...]
    mean_one = jnp.mean(gy, axis=-1, keepdims=True)
    mean_two = jnp.mean(gy * hat, axis=-1, keepdims=True)
    out_ref[...] = (dres_ref[...] + inverse * (gy - mean_one - hat * mean_two)).astype(BF)


def whole(shape):
    return pl.BlockSpec(shape, lambda *at: (0,) * len(shape))


def per_device(
    tokens,
    cluster_ids,
    lengths,
    top_keys,
    gain_one,
    shift_one,
    w_query,
    w_keyval,
    w_out,
    gain_two,
    shift_two,
    w_up,
    w_down,
    cotangent,
):
    rows, width = tokens.shape
    heads = cluster_ids.shape[1]
    hs = width // heads
    hidden = w_up.shape[1]
    wide = lax.axis_size("wide")
    n_dp = lax.axis_size("dp")
    groups = math.gcd(heads, wide)
    peers = wide // groups
    own_heads = heads // groups
    own_clusters = top_keys.shape[2]
    clusters = own_clusters * wide
    picks = top_keys.shape[3]
    seq = rows * wide
    size = 512 if seq <= 2048 else 2048
    feats = own_heads * hs
    block_rows = width // wide
    fast = peers == 2 and n_dp == 4 and block_rows == 96 and hidden == 4 * width and width % 256 == 0 and rows % 128 == 0
    me = lax.axis_index("wide")
    group_at, peer_at = me // peers, me % peers
    dp_at = lax.axis_index("dp")
    seq_len = lengths[0]
    bit_x, bit_y = dp_at % 2, (dp_at // 2) % 2
    place_u, place_d = 2 * bit_x + bit_y, 2 * bit_y + bit_x
    info = jnp.stack([group_at, peer_at, seq_len, place_u, place_d, me]).astype(jnp.int32)

    def along_groups(values, hop):
        pairs = [(i, ((i // peers + hop) % groups) * peers + i % peers) for i in range(wide)]
        return lax.ppermute(values, "wide", pairs)

    def along_peers(values, hop):
        pairs = [(i, (i // peers) * peers + (i % peers + hop) % peers) for i in range(wide)]
        return lax.ppermute(values, "wide", pairs)

    def along_dp(values, mask):
        return lax.ppermute(values, "dp", [(i, i ^ mask) for i in range(n_dp)])

    def prefetched(kernel, grid, in_specs, out_specs, out_shape, mib, spent, name, scratch=(), alias=None):
        return pl.pallas_call(
            kernel,
            grid_spec=pltpu.PrefetchScalarGridSpec(
                num_scalar_prefetch=1,
                grid=grid,
                in_specs=in_specs,
                out_specs=out_specs,
                scratch_shapes=list(scratch),
            ),
            out_shape=out_shape,
            compiler_params=params(mib, len(grid)),
            cost_estimate=spent,
            input_output_aliases=alias or {},
            name=name,
        )

    def after(values, *others):
        return lax.optimization_barrier((values, others))[0]

    def array(shape, dtype):
        return jax.ShapeDtypeStruct(shape, dtype)

    position = me * rows + jnp.arange(rows, dtype=jnp.int32)
    marked = jnp.where((position < seq_len)[:, None], cluster_ids, -1).T
    tops = jnp.zeros((heads, picks, clusters), jnp.int32)
    tops = lax.dynamic_update_slice(
        tops, top_keys[0].transpose(0, 2, 1), (0, 0, me * own_clusters)
    )
    lines = rows // clusters
    packed = jnp.concatenate([tops, marked.reshape(heads, lines, clusters)], axis=1)
    packed = packed.reshape(groups, own_heads, picks + lines, clusters)

    def of_heads(hop):
        return lax.dynamic_index_in_dim(packed, (group_at + groups - hop) % groups, keepdims=False)

    arrived = [of_heads(0)] + [along_groups(of_heads(hop), -hop) for hop in range(1, groups)]

    ready = after(tokens, packed)
    mine = {0: tokens, 1: along_groups(ready, -1)}
    if groups > 2:
        mine[groups - 1] = along_groups(ready, 1)
    ready = after(tokens, arrived)
    for hop in range(2, groups - 1):
        mine[hop] = along_groups(ready, -hop)

    w_in = jnp.concatenate([w_query, w_keyval], axis=1).T.reshape(3, heads, hs, width)
    w_in = w_in.transpose(1, 0, 2, 3).reshape(groups, 3 * feats, width)
    table_shape = (own_heads, picks + groups * lines, clusters)
    table = pl.pallas_call(
        functools.partial(table_kernel, picks=picks),
        grid=(1,),
        in_specs=[whole((own_heads, picks + lines, clusters))] * groups,
        out_specs=whole(table_shape),
        out_shape=array(table_shape, jnp.int32),
        compiler_params=params(8, 1),
        cost_estimate=cost(1e5, 1e6),
        name="table",
    )(*after(arrived, w_in))
    tables = [table] + [along_peers(table, -hop) for hop in range(1, peers)]
    cot_got = [along_peers(after(cotangent, arrived), hop) for hop in range(1, peers)]
    cot_got = cot_got if fast else []
    bias, ids_all = prefetched(
        functools.partial(bias_kernel, groups=groups, peers=peers, rows=rows, picks=picks),
        (wide,),
        [whole(table_shape)] * peers,
        [
            pl.BlockSpec((own_heads, rows, clusters), lambda i, s: (0, i, 0)),
            whole((own_heads, 1, seq)),
        ],
        [array((own_heads, seq, clusters), BF), array((own_heads, 1, seq), jnp.int32)],
        12 if fast else 60,
        cost(own_heads * seq * clusters * picks * 8, own_heads * seq * clusters * 2),
        "bias",
    )(info, *tables)

    gain_row, shift_row = gain_one[None, :], shift_one[None, :]
    shapes = [
        array((width, groups * rows), BF),
        array((own_heads, 3 * hs, seq), BF),
        array((own_heads, seq, 2 * hs), BF),
    ]
    held = []
    split_peers = peers if peers <= 2 else 1
    for group in sorted(range(groups), key=lambda g: min(g, groups - g)):
        arrival = mine[group] if group else ready
        if 1 < group < groups - 1:
            arrival = after(arrival, held, cot_got)
        elif group:
            arrival = after(arrival, bias)
        chunk = [arrival] + [along_peers(arrival, -hop) for hop in range(1, peers)]
        if peers > 2:
            chunk = [jnp.concatenate(chunk, axis=0)]
        span = peers * rows
        if peers > 2:
            specs_in = [pl.BlockSpec((rows, width), lambda p, s: (p, 0))]
            grid = (peers,)
            outs = [
                pl.BlockSpec((width, rows), lambda p, s, g=group: (0, g)),
                pl.BlockSpec((own_heads, 3 * hs, rows), lambda p, s, g=group: (0, 0, g * peers + p)),
                pl.BlockSpec((own_heads, rows, 2 * hs), lambda p, s, g=group: (0, g * peers + p, 0)),
            ]
        else:
            specs_in = [whole((rows, width))] * split_peers
            grid = (1,)
            outs = [
                pl.BlockSpec((width, rows), lambda p, s, g=group: (0, g)),
                pl.BlockSpec((own_heads, 3 * hs, span), lambda p, s, g=group: (0, 0, g)),
                pl.BlockSpec((own_heads, span, 2 * hs), lambda p, s, g=group: (0, g, 0)),
            ]
        first = 1 + split_peers + 3
        held = prefetched(
            functools.partial(project_kernel, peers=split_peers, olds=len(held)),
            grid,
            specs_in
            + [
                whole((1, width)),
                whole((1, width)),
                pl.BlockSpec((1, 3 * feats, width), lambda p, s: (s[0], 0, 0)),
            ]
            + [pl.BlockSpec(memory_space=pl.ANY)] * len(held),
            outs,
            shapes,
            16 if fast else 60,
            cost(6 * span * width * feats, span * width * 4),
            "project",
            alias={first + k: k for k in range(len(held))},
        )(info, *chunk, gain_row, shift_row, w_in, *held)
    hat_own, feat, kv = held

    ids_full = pl.BlockSpec((1, 1, seq), lambda h, r: (h, 0, 0))
    feat_full = pl.BlockSpec((1, 3 * hs, seq), lambda h, r: (h, 0, 0))
    kv_full = pl.BlockSpec((1, seq, 2 * hs), lambda h, r: (h, 0, 0))
    bias_full = pl.BlockSpec((1, seq, clusters), lambda h, r: (h, 0, 0))
    head_rows = pl.BlockSpec((hs, rows), lambda h, r: (h, 0))
    mix_spec = pl.BlockSpec((1, 1, hs + 8, rows), lambda h, r: (h, r, 0, 0))
    stat_spec = pl.BlockSpec((1, hs + 8, clusters), lambda h, r: (h, 0, 0))
    cen_spec = pl.BlockSpec((1, hs, clusters), lambda h, r: (h, 0, 0))
    own_rows = groups * rows
    pair_flops = own_heads * own_rows * seq * 256

    one = [
        pl.BlockSpec(spec.block_shape, functools.partial(lambda h, f: f(h, 0), f=spec.index_map))
        for spec in (ids_full, feat_full, kv_full, bias_full, stat_spec, cen_spec, head_rows)
    ]
    ids_one, feat_one, kv_one, bias_one, stat_one, cen_one, rows_one = one
    part_one = pl.BlockSpec((1, hs + 16, clusters), lambda h: (h, 0, 0))
    mix_one = pl.BlockSpec((1, groups, hs + 8, rows), lambda h: (h, 0, 0, 0))
    all_groups = pl.BlockSpec((groups, hs, rows), lambda h: (0, h, 0))
    own_one = pl.BlockSpec((1, own_rows, 2 * hs), lambda h: (h, 0, 0))
    results = pl.pallas_call(
        functools.partial(forward_kernel, size=size, groups=groups, rows=rows),
        grid=(own_heads,),
        in_specs=[ids_one, feat_one, kv_one, bias_one],
        out_specs=[rows_one] * groups + [mix_one, stat_one, cen_one],
        out_shape=[array((feats, rows), BF)] * groups
        + [
            array((own_heads, groups, hs + 8, rows), F32),
            array((own_heads, hs + 8, clusters), F32),
            array((own_heads, hs, clusters), BF),
        ],
        compiler_params=params(32 if fast else 60, 1),
        cost_estimate=cost(6 * pair_flops, 8e6, own_heads * own_rows * seq),
        name="attend",
    )(ids_all, feat, kv, bias)
    attn_t = results[:groups]
    mixed, stats, centroid = results[groups:]

    arrived = [attn_t[0]] + [along_groups(attn_t[hop], hop) for hop in range(1, groups)]

    chunks = 4
    part = hidden // chunks
    w_out_g = w_out.reshape(groups, feats, width)
    gain_row2, shift_row2 = gain_two[None, :], shift_two[None, :]
    square = whole((rows, width))
    column = pl.BlockSpec((rows, part), lambda i, s: (0, i))
    norm_spec = whole((8, width))
    if fast:
        kept_shapes = [
            array((rows, hidden + hidden // 2 + width), BF),
            array((width + 16, rows), BF),
            array((rows, hidden // 2), BF),
            array((width + 16, rows), BF),
        ]
        kept_specs = [whole(item.shape) for item in kept_shapes]
        kept_specs[2] = pl.BlockSpec((rows, part // 2), lambda i, s: (0, i))
    else:
        kept_shapes = [
            array((8, width), F32),
            array((rows, hidden), BF),
            array((rows, width), BF),
            array((rows, hidden), BF),
            array((rows, width), BF),
        ]
        kept_specs = [norm_spec, column, square, column, square]
    results = prefetched(
        functools.partial(block_kernel, groups=groups, chunks=chunks, fast=fast),
        (chunks,),
        [whole((feats, rows))] * groups
        + [
            square,
            whole((1, width)),
            whole((1, width)),
            whole((groups, feats, width)),
            pl.BlockSpec((width, part), lambda i, s: (0, i)),
            pl.BlockSpec((part, width), lambda i, s: (i, 0)),
            square,
        ],
        [square, square] + kept_specs + [whole((feats, rows))] * groups,
        [array((rows, width), BF), array((rows, width), F32)]
        + kept_shapes
        + [array((feats, rows), BF)] * groups,
        28 if fast else 60,
        cost(8 * rows * width * hidden, 4 * width * hidden, rows * hidden),
        "feed",
        scratch=[
            pltpu.VMEM((rows, width), F32),
            pltpu.VMEM((rows, 128), F32),
            pltpu.VMEM((rows, width), BF),
            pltpu.VMEM((rows, width), F32),
            pltpu.VMEM((rows, width), F32),
        ],
    )(info, *arrived, tokens, gain_row2, shift_row2, w_out_g, w_up, w_down, cotangent)
    output, d_resid = results[:2]
    kept, d_attn = results[2:-groups], results[-groups:]
    grads = [d_attn[0]] + [along_groups(d_attn[hop], -hop) for hop in range(1, groups)]

    def weight_parts():
        far, low_far, act_own, low_own = kept
        got, low_got = along_peers(far, 1), along_peers(low_far, 1)
        high = block_rows + 16
        chunk = pl.BlockSpec((rows, part), lambda i, s: (0, i ^ 2 ^ s[3]))
        branch = pl.BlockSpec((rows, width), lambda i, s: (0, hidden * 3 // 2 // width))
        act_spec = pl.BlockSpec((rows, part // 2), lambda i, s: (0, i))
        act_there = pl.BlockSpec((rows, part // 2), lambda i, s: (0, 2 * hidden // part + i))
        low_spec = whole((width + 16, rows))
        shape_u = (2, groups, high, width)
        shape_d = (2, groups, high, width)
        send_u, keep_u, send_d, keep_d = prefetched(
            functools.partial(weights_kernel, groups=groups),
            (4,),
            [chunk, chunk, branch, branch, act_spec, act_there, low_spec, low_spec, square, square],
            [
                pl.BlockSpec((1,) + shape_u[1:], lambda i, s: (jnp.minimum(i, 1), 0, 0, 0)),
                pl.BlockSpec((1,) + shape_u[1:], lambda i, s: (jnp.maximum(i - 2, 0), 0, 0, 0)),
                whole(shape_d),
                whole(shape_d),
            ],
            [array(shape_u, BF), array(shape_u, BF), array(shape_d, BF), array(shape_d, BF)],
            28,
            cost(8 * rows * width * hidden, 6 * width * hidden),
            "weights",
            scratch=[pltpu.VMEM((groups, block_rows, width), F32)],
        )(info, far, got, far, got, act_own, got, low_own, low_got, cotangent, *cot_got)
        return send_u, keep_u, send_d, keep_d

    def weight_second(keep_u, got_u, keep_d, got_d):
        shape_u, shape_d = keep_u.shape, keep_d.shape
        high = shape_u[2]

        def block(shape, at):
            return pl.BlockSpec((1,) + shape[1:], lambda i: (at, 0, 0, 0))

        next_u, next_d = pl.pallas_call(
            second_kernel,
            grid=(1,),
            in_specs=[block(shape_u, 1), block(shape_u, 1), block(shape_d, 1), block(shape_d, 1)],
            out_specs=[whole(shape_u[1:]), whole(shape_d[1:])],
            out_shape=[array(shape_u[1:], BF), array(shape_d[1:], BF)],
            compiler_params=params(20, 1),
            cost_estimate=cost(groups * high * width * 2, groups * high * width * 12),
            name="second",
        )(keep_u, got_u, keep_d, got_d)
        return next_u, next_d

    def weight_third(keep_u, got_u, last_u, keep_d, got_d, last_d):
        shape_u, shape_d = keep_u.shape, keep_d.shape
        high = shape_u[2]

        def block(shape, at):
            return pl.BlockSpec((1,) + shape[1:], lambda i: (at, 0, 0, 0))

        tall = shape_u[2] + shape_d[2]
        sums = pl.pallas_call(
            third_kernel,
            grid=(1,),
            in_specs=[
                block(shape_u, 0),
                block(shape_u, 0),
                whole(shape_u[1:]),
                block(shape_d, 0),
                block(shape_d, 0),
                whole(shape_d[1:]),
            ],
            out_specs=[whole((tall, width))] * groups,
            out_shape=[array((tall, width), BF)] * groups,
            compiler_params=params(24, 1),
            cost_estimate=cost(groups * tall * width * 4, groups * tall * width * 8),
            name="third",
        )(keep_u, got_u, last_u, keep_d, got_d, last_d)
        came = [sums[0]] + [along_groups(sums[hop], hop) for hop in range(1, groups)]
        return came

    def weight_sums(came, shape_u, shape_d):
        tall = shape_u[2] + shape_d[2]
        done = pl.pallas_call(
            fourth_kernel,
            grid=(1,),
            in_specs=[whole((tall, width))] * groups,
            out_specs=whole((tall, width)),
            out_shape=array((tall, width), BF),
            compiler_params=params(12, 1),
            cost_estimate=cost(groups * tall * width, groups * tall * width * 2),
            name="fourth",
        )(*came)
        from_x, from_y, from_xy = (along_dp(done, mask) for mask in (1, 2, 3))
        total_up, total_out, total_down, norms = prefetched(
            spread_kernel,
            (4,),
            [whole((tall, width))] * 4,
            [
                pl.BlockSpec((block_rows, part), lambda i, s: (0, i ^ s[3])),
                whole((block_rows, width)),
                pl.BlockSpec((block_rows, width), lambda i, s: (i ^ s[4], 0)),
                whole((8, width)),
            ],
            [
                array((block_rows, hidden), F32),
                array((block_rows, width), F32),
                array((hidden // wide, width), F32),
                array((8, width), F32),
            ],
            16,
            cost(1e6, 4 * tall * width * 6),
            "spread",
        )(info, done, from_x, from_y, from_xy)
        norm_own = lax.dynamic_slice_in_dim(norms, me * block_rows, block_rows, axis=1)
        return total_up, total_out, total_down, norm_own

    masks = [1 << k for k in range(n_dp.bit_length() - 1)]

    def reduce_rows(partial):
        blocks = partial.reshape(groups, peers, partial.shape[0] // wide, partial.shape[1])

        def of_peer(hop):
            at = (peer_at + hop) % peers
            return lax.dynamic_index_in_dim(blocks, at, axis=1, keepdims=False)

        total = of_peer(0).astype(F32)
        for hop in range(1, peers):
            total = total + along_peers(of_peer(hop), hop).astype(F32)
        total = total.astype(BF)

        def of_group(hop):
            return lax.dynamic_index_in_dim(total, (group_at + hop) % groups, keepdims=False)

        done = of_group(0).astype(F32)
        for hop in range(1, groups):
            done = done + along_groups(of_group(hop), hop).astype(F32)
        for mask in masks:
            done = done.astype(BF)
            done = done.astype(F32) + along_dp(done, mask).astype(F32)
        return done

    if fast:
        send_u, keep_u, send_d, keep_d = weight_parts()
        got_u, got_d = along_dp(send_u, 1), along_dp(send_d, 2)
        grads = after(grads, keep_u)
    else:
        norm_two, d_up, d_branch, act, normed_two = kept
        total_up = reduce_rows(tn(normed_two, d_up).astype(BF))
        total_down = reduce_rows(tn(act, cotangent).astype(BF))
        found = jnp.stack([nn(item, d_branch).astype(BF) for item in arrived])
        found = [
            lax.dynamic_index_in_dim(found, (group_at + groups - g) % groups, keepdims=False)
            for g in range(groups)
        ]
        total_out = reduce_rows(jnp.concatenate(found, axis=0))
        norm_own = reduce_rows(norm_two[:2].T.astype(BF)).T

    share = pl.pallas_call(
        functools.partial(sums_kernel, groups=groups),
        grid=(own_heads,),
        in_specs=[ids_one]
        + [rows_one] * groups
        + [mix_one],
        out_specs=part_one,
        out_shape=array((own_heads, hs + 16, clusters), F32),
        compiler_params=params(16 if fast else 60, 1),
        cost_estimate=cost(own_heads * own_rows * clusters * 160, 2e6),
        name="sums",
    )(ids_all, *grads, mixed)
    share_got = [along_peers(share, hop) for hop in range(1, peers)]

    back_shapes = [
        array((groups, feats, rows), BF),
        array((own_heads, 2 * hs, own_rows), F32),
        array((own_heads, 2 * hs, max(peers - 1, 1) * own_rows), BF),
    ]
    dq, dkv_own, dkv_send = pl.pallas_call(
        functools.partial(back_kernel, size=size, groups=groups, gots=len(share_got)),
        grid=(own_heads,),
        in_specs=[ids_one, feat_one, kv_one, bias_one]
        + [rows_one] * groups
        + [mix_one, stat_one, cen_one]
        + [part_one] * (1 + len(share_got)),
        out_specs=[
            all_groups,
            pl.BlockSpec((1,) + back_shapes[1].shape[1:], lambda h: (h, 0, 0)),
            pl.BlockSpec((1,) + back_shapes[2].shape[1:], lambda h: (h, 0, 0)),
        ],
        out_shape=back_shapes,
        scratch_shapes=[pltpu.VMEM((seq, 2 * hs), F32), pltpu.VMEM((seq, 2 * clusters), BF)],
        compiler_params=params(36 if fast else 62, 1),
        cost_estimate=cost(14 * pair_flops, 10e6, own_heads * own_rows * seq),
        name="back",
    )(ids_all, feat, kv, bias, *grads, mixed, stats, centroid, share, *share_got)
    dkv_got = [
        along_peers(
            dkv_send if peers == 2 else dkv_send[..., (hop - 1) * own_rows : hop * own_rows], hop
        )
        for hop in range(1, peers)
    ]
    d_in = pl.pallas_call(
        functools.partial(join_kernel, groups=groups),
        grid=(1,),
        in_specs=[whole(back_shapes[0].shape), whole(back_shapes[1].shape)]
        + [whole(back_shapes[1].shape)] * len(dkv_got),
        out_specs=[whole((own_heads, 3 * hs, rows))] * groups,
        out_shape=[array((own_heads, 3 * hs, rows), BF)] * groups,
        compiler_params=params(20, 1),
        cost_estimate=cost(own_rows * feats * 8, own_rows * feats * 16),
        name="join",
    )(dq, dkv_own, *dkv_got)

    home = [d_in[0]] + [along_groups(d_in[hop], hop) for hop in range(1, groups)]

    tall = block_rows + 16
    part_spec = [whole((own_heads, 3 * hs, rows))] * groups + [whole((width, own_rows))]
    inward = functools.partial(
        prefetched,
        functools.partial(inward_kernel, groups=groups, fast=fast),
        (1,),
        part_spec,
    )
    spent = cost(2 * own_rows * width * 3 * feats, 4e6)
    if fast:
        half = groups // 2
        blocks = (groups, tall, 3 * feats)
        next_u, next_d = weight_second(
            keep_u, after(got_u, home[1]), keep_d, after(got_d, home[1])
        )
        last_u, last_d = along_dp(next_u, 2), along_dp(next_d, 1)
        came = weight_third(keep_u, got_u, last_u, keep_d, got_d, last_d)
        keep, far = inward(
            [whole(blocks)] * 2, [array(blocks, BF)] * 2, 24, spent, "inward"
        )(info, *after(d_in, home, came[0]), hat_own)
        got = along_peers(far, 1)
        total = keep.astype(F32) + got.astype(F32)
        one_half, two_half = total[:half].astype(BF), total[half:].astype(BF)
        for mask in (1, 2):
            one_half, two_half = after((one_half, two_half), came[mask])
            got_one, got_two = along_dp(one_half, mask), along_dp(two_half, 3 - mask)
            one_half = (one_half.astype(F32) + got_one.astype(F32)).astype(BF)
            two_half = (two_half.astype(F32) + got_two.astype(F32)).astype(BF)
        total_up, total_out, total_down, norm_own = weight_sums(
            after(came, one_half, two_half), keep_u.shape, keep_d.shape
        )
        items = [one_half[k] for k in range(half)] + [two_half[k] for k in range(half)]
    else:
        found, more = inward(
            [whole((width, 3 * feats)), whole((16, 3 * feats))],
            [array((width, 3 * feats), F32), array((16, 3 * feats), F32)],
            60,
            spent,
            "inward",
        )(info, *d_in, hat_own)
        found = found.reshape(groups, peers, block_rows, 3 * feats)
        more = jnp.broadcast_to(more, (groups, peers, 16, 3 * feats))
        found = jnp.concatenate([found, more], axis=2).astype(BF)

        def of_peer(hop):
            at = (peer_at + hop) % peers
            return lax.dynamic_index_in_dim(found, at, axis=1, keepdims=False)

        total = of_peer(0).astype(F32)
        for hop in range(1, peers):
            total = total + along_peers(of_peer(hop), hop).astype(F32)
        for mask in masks:
            total = total.astype(BF)
            total = total.astype(F32) + along_dp(total, mask).astype(F32)
        total = total.astype(BF)
        items = [
            lax.dynamic_index_in_dim(total, (group_at + hop) % groups, keepdims=False)
            for hop in range(groups)
        ]
    pieces = [items[0]] + [along_groups(items[hop], hop) for hop in range(1, groups)]

    grad_tokens = prefetched(
        functools.partial(final_kernel, groups=groups),
        (1,),
        [whole((own_heads, 3 * hs, rows))] * groups
        + [square, square, whole((1, width)), whole((groups, 3 * feats, width))],
        square,
        array((rows, width), BF),
        24 if fast else 60,
        cost(6 * rows * width * width, 6 * width * width),
        "final",
    )(info, *home, tokens, d_resid, gain_row, w_in)

    pieces = jnp.stack(pieces)
    pieces = jnp.stack(
        [
            lax.dynamic_index_in_dim(pieces, (group_at + groups - g) % groups, keepdims=False)
            for g in range(groups)
        ]
    ).astype(F32)
    q_part = pieces[:, :, :feats].transpose(1, 0, 2).reshape(tall, width)
    kv_part = (
        pieces[:, :, feats:]
        .reshape(groups, tall, 2, feats)
        .transpose(1, 2, 0, 3)
        .reshape(tall, 2 * width)
    )
    at = me * block_rows
    wq_rows = lax.dynamic_slice_in_dim(w_query, at, block_rows).astype(F32)
    wkv_rows = lax.dynamic_slice_in_dim(w_keyval, at, block_rows).astype(F32)
    gain_own = lax.dynamic_slice_in_dim(gain_one, at, block_rows)
    shift_own = lax.dynamic_slice_in_dim(shift_one, at, block_rows)
    q_sum, kv_sum = q_part[block_rows], kv_part[block_rows]
    q_part, kv_part = q_part[:block_rows], kv_part[:block_rows]
    shift_grad = jnp.sum(wq_rows * q_sum, axis=1) + jnp.sum(wkv_rows * kv_sum, axis=1)
    along = jnp.sum(wq_rows * q_part, axis=1) + jnp.sum(wkv_rows * kv_part, axis=1)
    return (
        output,
        grad_tokens,
        q_part + shift_own[:, None] * q_sum,
        kv_part + shift_own[:, None] * kv_sum,
        total_out,
        total_up,
        total_down,
        along / gain_own,
        shift_grad,
        norm_own[0],
        norm_own[1],
    )


def solution(mesh):
    return jax.shard_map(
        per_device,
        mesh=mesh,
        in_specs=(
            P(("dp", "wide"), None),
            P(("dp", "wide"), None),
            P("dp"),
            P("dp", None, "wide", None),
            P(),
            P(),
            P(),
            P(),
            P(),
            P(),
            P(),
            P(),
            P(),
            P(("dp", "wide"), None),
        ),
        out_specs=(
            P(("dp", "wide"), None),
            P(("dp", "wide"), None),
            P("wide", None),
            P("wide", None),
            P("wide", None),
            P("wide", None),
            P("wide", None),
            P("wide"),
            P("wide"),
            P("wide"),
            P("wide"),
        ),
        check_vma=False,
    )
```

```python
import functools
import math

import jax
import jax.numpy as jnp
import numpy as np
from jax import lax
from jax.experimental import pallas as pl
from jax.experimental.pallas import tpu as pltpu
from jax.sharding import PartitionSpec as P

EPSILON = 1e-05
NEGATIVE = -1e30
EXCLUDED = -3e30
GELU_A = math.sqrt(2.0 / math.pi)
GELU_B = 0.044715
BF = jnp.bfloat16
F32 = jnp.float32


def nn(left, right):
    return lax.dot_general(left, right, (((1,), (0,)), ((), ())), preferred_element_type=F32)


def nt(left, right):
    return lax.dot_general(left, right, (((1,), (1,)), ((), ())), preferred_element_type=F32)


def tn(left, right):
    return lax.dot_general(left, right, (((0,), (0,)), ((), ())), preferred_element_type=F32)


def params(mib, dims):
    return pltpu.CompilerParams(
        vmem_limit_bytes=mib * 1024 * 1024, dimension_semantics=("arbitrary",) * dims
    )


def cost(flops, nbytes, trans=0):
    return pl.CostEstimate(flops=int(flops), bytes_accessed=int(nbytes), transcendentals=int(trans))


def split_low(values):
    high = values.astype(BF)
    return high, (values - high.astype(F32)).astype(BF)


def one_hot_t(ids_row, clusters):
    rows = lax.broadcasted_iota(jnp.int32, (clusters, ids_row.shape[1]), 0)
    return jnp.where(rows == ids_row, 1.0, 0.0).astype(BF)


def key_passes(total, size, score, weigh, blocks=None):
    count = total // size
    if count <= 4:
        if blocks is None:
            blocks = [score(index) for index in range(count)]
        peak = functools.reduce(jnp.maximum, [jnp.max(b, axis=0, keepdims=True) for b in blocks])
        denom, sums = 0.0, None
        for index in range(count):
            expo = jnp.exp(blocks[index] - peak)
            denom = denom + jnp.sum(expo, axis=0, keepdims=True)
            parts = weigh(index, expo)
            sums = parts if sums is None else tuple(x + y for x, y in zip(sums, parts))
        return peak, denom, sums

    def step(index, carry):
        peak, denom, sums = carry
        block = score(index)
        fresh = jnp.maximum(peak, jnp.max(block, axis=0, keepdims=True))
        expo = jnp.exp(block - fresh)
        fade = jnp.exp(peak - fresh)
        parts = weigh(index, expo)
        return (
            fresh,
            denom * fade + jnp.sum(expo, axis=0, keepdims=True),
            tuple(old * fade + new for old, new in zip(sums, parts)),
        )

    shapes = jax.eval_shape(lambda: (score(0), weigh(0, score(0))))
    lanes = shapes[0].shape[1]
    start = (
        jnp.full((1, lanes), NEGATIVE, F32),
        jnp.zeros((1, lanes), F32),
        tuple(jnp.zeros(item.shape, F32) for item in shapes[1]),
    )
    return lax.fori_loop(0, count, step, start)


def key_sum(total, size, step, start):
    count = total // size
    if count <= 4:
        for index in range(count):
            start = step(index, start)
        return start
    return lax.fori_loop(0, count, step, start)


def spot_of(index, size):
    if isinstance(index, int):
        return pl.ds(index * size, size)
    return pl.ds(pl.multiple_of(index * size, size), size)


def piece(ref, index, size, axis):
    spot = spot_of(index, size)
    return ref[spot, :] if axis == 0 else ref[:, spot]


def table_kernel(*refs, picks):
    parts, out = refs[:-1], refs[-1]
    total = parts[0][:, :picks]
    for part in parts[1:]:
        total = total + part[:, :picks]
    out[:, :picks] = total
    rows = parts[0].shape[1] - picks
    for group, part in enumerate(parts):
        out[:, picks + group * rows : picks + (group + 1) * rows] = part[:, picks:]


def bias_kernel(info, *refs, groups, peers, rows, picks):
    tables, (bias_ref, ids_ref) = refs[:peers], refs[peers:]
    part = pl.program_id(0)
    owner = (
        lax.rem(info[0] + part // peers, groups) * peers + lax.rem(info[1] + part % peers, peers)
    )
    heads, _, clusters = tables[0].shape
    place = owner * rows + lax.broadcasted_iota(jnp.int32, (rows, clusters), 0)
    plain = jnp.where(place >= info[2], EXCLUDED, NEGATIVE)
    for head in range(heads):
        top = tables[0][head, :picks]
        for table in tables[1:]:
            top = top + table[head, :picks]
        value = plain
        for pick in range(picks):
            value = jnp.where(place == top[pick : pick + 1, :], 0.0, value)
        bias_ref[head] = value.astype(BF)

    @pl.when(part == 0)
    def ids():
        lines = rows // clusters
        for head in range(heads):
            row = []
            for group in range(groups):
                for table in tables:
                    for line in range(lines):
                        at = picks + group * lines + line
                        row.append(table[head, at : at + 1, :])
            ids_ref[head] = jnp.concatenate(row, axis=1)


def project_kernel(info, *refs, peers, olds):
    parts = refs[:peers]
    gain_ref, shift_ref, w_ref = refs[peers : peers + 3]
    hat_ref, feat_ref, kv_ref = refs[peers + 3 + olds :]
    rows = hat_ref.shape[1]
    for peer in range(peers):
        values = parts[peer][...].astype(F32)
        centered = values - jnp.mean(values, axis=-1, keepdims=True)
        variance = jnp.mean(centered * centered, axis=-1, keepdims=True)
        scaled = centered * lax.rsqrt(variance + EPSILON) * gain_ref[...]
        if peer == 0:
            hat_ref[...] = scaled.astype(BF).T
        low = (scaled + shift_ref[...]).astype(BF)
        found = nt(w_ref[0], low)
        heads, triple = feat_ref.shape[0], feat_ref.shape[1]
        hs = triple // 3
        spot = slice(peer * rows, (peer + 1) * rows)
        for head in range(heads):
            base = head * triple
            query = (found[base : base + hs] * 0.125).astype(BF)
            pair = found[base + hs : base + triple].astype(BF)
            feat_ref[head, :hs, spot] = query
            feat_ref[head, hs:, spot] = pair
            kv_ref[head, spot, :] = pair.T


def forward_kernel(ids_all, feat, kv, bias, *refs, size, groups, rows):
    outs = refs[:groups]
    mix_ref, stat_ref, cen_ref = refs[groups:]
    hs = feat.shape[1] // 3
    keys = kv.shape[1]
    count = keys // size
    clusters = bias.shape[2]
    kv_h, bias_h = kv.at[0], bias.at[0]
    queries_all, kvt = feat.at[0, :hs], feat.at[0, hs:]
    hot_all = one_hot_t(ids_all[0], clusters)
    ones = jnp.ones((16, keys), BF)
    sums = nt(jnp.concatenate([queries_all[...], ones], axis=0), hot_all)
    counts = sums[hs : hs + 1]
    centroid = (sums[:hs] / jnp.maximum(counts, 1.0)).astype(BF)
    padded = jnp.concatenate([centroid, jnp.zeros_like(centroid)], axis=0)

    def cluster_score(index):
        scores = nn(piece(kv_h, index, size, 0), padded)
        outside = piece(bias_h, index, size, 0).astype(F32) < 2.0 * NEGATIVE
        return jnp.where(outside, NEGATIVE, scores)

    def cluster_weigh(index, expo):
        top = piece(bias_h, index, size, 0).astype(F32) == 0.0
        mass = jnp.sum(jnp.where(top, expo, 0.0), axis=0, keepdims=True)
        other = jnp.where(top, 0.0, expo).astype(BF)
        return nn(piece(kvt, index, size, 1), other), mass

    peers = keys // (groups * rows)
    hots, sides = [], []
    for group in range(groups):
        spot = slice(group * peers * rows, group * peers * rows + rows)
        hot = one_hot_t(ids_all[0, :, spot], clusters)
        queries = queries_all[:, spot]
        hots.append(hot)
        sides.append(jnp.concatenate([queries, jnp.zeros_like(queries), hot], axis=0))

    def member_score(group, index):
        both = jnp.concatenate([piece(kv_h, index, size, 0), piece(bias_h, index, size, 0)], axis=1)
        return nn(both, sides[group])

    def member_weigh(index, expo):
        return (nn(piece(kvt, index, size, 1), expo.astype(BF)),)

    short = count <= 4
    ahead = None
    if short:
        ahead = [member_score(0, index) for index in range(count)]
    peak, denom, (rest, mass) = key_passes(keys, size, cluster_score, cluster_weigh)
    rest = rest[hs:] / denom
    mass = mass / denom
    blank = jnp.zeros((5, clusters), F32)
    stats = jnp.concatenate([rest, mass, peak + jnp.log(denom), counts, blank], axis=0)
    stat_ref[0] = stats
    cen_ref[0] = centroid
    high, low = split_low(stats)
    table = jnp.concatenate([high, low], axis=1)
    for group in range(groups):
        gathered = nn(table, jnp.concatenate([hots[group], hots[group]], axis=0))
        blocks, ahead = ahead, None
        if short and group + 1 < groups:
            ahead = [member_score(group + 1, index) for index in range(count)]
        score = functools.partial(member_score, group)
        peak, denom, (mix,) = key_passes(keys, size, score, member_weigh, blocks)
        mix = mix[hs:] / denom
        outs[group][...] = (gathered[hs : hs + 1] * mix + gathered[:hs]).astype(BF)
        level = jnp.broadcast_to(peak + jnp.log(denom), (8, rows))
        mix_ref[0, group] = jnp.concatenate([mix, level], axis=0)


def sums_kernel(ids_own, *refs, groups):
    grads, (mix_ref, part_ref) = refs[:groups], refs[groups:]
    hs = grads[0].shape[0]
    total = None
    for group in range(groups):
        rows = grads[group].shape[1]
        step = ids_own.shape[2] // groups
        hot = one_hot_t(ids_own[0, :, group * step : group * step + rows], part_ref.shape[2])
        grad = grads[group][...]
        along = jnp.sum(grad.astype(F32) * mix_ref[0, group, :hs], axis=0, keepdims=True)
        high, low = split_low(along)
        pad = jnp.zeros((14, rows), BF)
        part = nt(jnp.concatenate([grad, high, low, pad], axis=0), hot)
        total = part if total is None else total + part
    part_ref[0] = total


def back_kernel(ids_all, feat, kv, bias, *refs, size, groups, gots):
    grads = refs[:groups]
    mix_ref, stat_ref, cen_ref = refs[groups : groups + 3]
    shares = refs[groups + 3 : groups + 4 + gots]
    dq_ref, own_ref, send_ref, total, both = refs[groups + 4 + gots :]
    hs, rows = grads[0].shape
    keys = kv.shape[1]
    count = keys // size
    peers = keys // (groups * rows)
    clusters = bias.shape[2]
    kv_h, bias_h = kv.at[0], bias.at[0]
    queries_all, kvt = feat.at[0, :hs], feat.at[0, hs:]
    stats = stat_ref[0]
    high, low = split_low(stats[hs : hs + 8])
    table = jnp.concatenate([high, low], axis=1)
    hots, sides, levels, deltas, pads, rights = [], [], [], [], [], []
    for group in range(groups):
        spot = slice(group * peers * rows, group * peers * rows + rows)
        hot = one_hot_t(ids_all[0, :, spot], clusters)
        queries = queries_all[:, spot]
        blank = jnp.zeros_like(queries)
        hots.append(jnp.concatenate([hot, hot], axis=0))
        sides.append(jnp.concatenate([queries, blank, hot], axis=0))
        mass = nn(table, hots[group])[0:1]
        back = (mass * grads[group][...].astype(F32)).astype(BF)
        levels.append(mix_ref[0, group, hs : hs + 1])
        deltas.append(jnp.sum(back.astype(F32) * mix_ref[0, group, :hs], axis=0, keepdims=True))
        pads.append(jnp.concatenate([blank, back], axis=0))
        turned = jnp.concatenate([queries, blank], axis=0)
        rights.append(jnp.concatenate([turned, pads[group]], axis=1).T)

    def scores(group, index):
        kv_c = piece(kv_h, index, size, 0)
        pair = jnp.concatenate([kv_c, piece(bias_h, index, size, 0)], axis=1)
        return nn(pair, sides[group]), nn(kv_c, pads[group])

    def finish(group, index, found, dq):
        weights = jnp.exp(found[0] - levels[group])
        grad_s = (weights * (found[1] - deltas[group])).astype(BF)
        part = nn(jnp.concatenate([grad_s, weights.astype(BF)], axis=1), rights[group])
        spot = spot_of(index, size)
        if group == 0:
            total[spot, :] = part
        else:
            total[spot, :] += part
        return dq + nn(piece(kvt, index, size, 1), grad_s)

    rest, mass = stats[:hs], stats[hs : hs + 1]
    level, counts = stats[hs + 1 : hs + 2], stats[hs + 2 : hs + 3]
    centroid = cen_ref[0]
    part = shares[0][0]
    for share in shares[1:]:
        part = part + share[0]
    d_rest = part[:hs].astype(BF)
    d_mass = part[hs : hs + 1] + part[hs + 1 : hs + 2]
    delta = jnp.sum(d_rest.astype(F32) * rest, axis=0, keepdims=True) + d_mass * mass
    cen_pad = jnp.concatenate([centroid, jnp.zeros_like(centroid)], axis=0)
    rest_pad = jnp.concatenate([jnp.zeros_like(centroid), d_rest], axis=0)
    right = jnp.concatenate([cen_pad, rest_pad], axis=1).T

    def cluster_step(index, summed):
        kv_c = piece(kv_h, index, size, 0)
        marks = piece(bias_h, index, size, 0).astype(F32)
        probs = jnp.exp(nn(kv_c, cen_pad) - level)
        probs = jnp.where(marks < 2.0 * NEGATIVE, 0.0, probs)
        top = marks == 0.0
        d_probs = jnp.where(top, d_mass, nn(kv_c, rest_pad))
        d_score = (probs * (d_probs - delta)).astype(BF)
        other = jnp.where(top, 0.0, probs).astype(BF)
        both[spot_of(index, size), :] = jnp.concatenate([d_score, other], axis=1)
        return summed + nn(piece(kvt, index, size, 1), d_score)

    start = jnp.zeros((2 * hs, rows), F32)
    zero = jnp.zeros((2 * hs, clusters), F32)
    member_dq = []
    if count <= 4:
        tasks = [(group, index) for group in range(groups) for index in range(count)]
        ahead = scores(*tasks[0])
        d_cen = key_sum(keys, size, cluster_step, zero)
        dq = start
        for step, (group, index) in enumerate(tasks):
            found = ahead
            if step + 1 < len(tasks):
                ahead = scores(*tasks[step + 1])
            dq = finish(group, index, found, dq)
            if index == count - 1:
                member_dq.append(dq[:hs] * 0.125)
                dq = start
    else:
        d_cen = key_sum(keys, size, cluster_step, zero)
        for group in range(groups):

            def step(index, dq, group=group):
                return finish(group, index, scores(group, index), dq)

            member_dq.append(lax.fori_loop(0, count, step, start)[:hs] * 0.125)
    d_cen = d_cen[:hs] * 0.125 / jnp.maximum(counts, 1.0)
    high, low = split_low(d_cen)
    table = jnp.concatenate([high, low], axis=1)
    for group in range(groups):
        base = group * peers * rows
        dq_ref[group] = (member_dq[group] + nn(table, hots[group])).astype(BF)
        own = total[base : base + rows, :] + nn(both[base : base + rows, :], right)
        own_ref[0, :, group * rows : (group + 1) * rows] = own.T
        for peer in range(1, peers):
            spot = (peer - 1) * groups * rows + group * rows
            found = total[base + peer * rows : base + (peer + 1) * rows, :]
            send_ref[0, :, spot : spot + rows] = found.astype(BF).T


def join_kernel(dq_ref, own_ref, *refs, groups):
    gots, outs = refs[:-groups], refs[-groups:]
    heads, _, rows = outs[0].shape
    hs = dq_ref.shape[1] // heads
    for head in range(heads):
        for group in range(groups):
            spot = slice(group * rows, (group + 1) * rows)
            pair = own_ref[head, :, spot]
            for got in gots:
                pair = pair + got[head, :, spot].astype(F32)
            outs[group][head, :hs] = dq_ref[group, head * hs : (head + 1) * hs]
            outs[group][head, hs:] = pair.astype(BF)


def block_kernel(info, *refs, groups, chunks, fast):
    (attn, rest) = (refs[:groups], refs[groups:])
    x_ref, gain_ref, shift_ref, wo_ref, up_ref, down_ref, cot_ref = rest[:7]
    out_ref, dres_ref = rest[7:9]
    if fast:
        far_ref, low_far, act_ref, low_ref = rest[9:13]
        rest = rest[13:]
        hidden = far_ref.shape[1] * 4 // 7
    else:
        dn_ref, dup_ref, dbr_ref, act_ref, low_ref = rest[9:14]
        rest = rest[14:]
    dat = rest[:groups]
    hat_ref, inv_ref, normed, back, total = rest[groups:]
    index = pl.program_id(0)

    @pl.when(index == 0)
    def before():
        resid = x_ref[...].astype(F32)
        for group in range(groups):
            owner = lax.rem(info[0] + groups - group, groups)
            resid = resid + tn(attn[group][...], wo_ref[owner])
        total[...] = resid
        centered = resid - jnp.mean(resid, axis=-1, keepdims=True)
        variance = jnp.mean(centered * centered, axis=-1, keepdims=True)
        inverse = lax.rsqrt(variance + EPSILON)
        hat = centered * inverse
        hat_ref[...] = hat
        inv_ref[...] = jnp.broadcast_to(inverse, inv_ref.shape)
        low = (hat * gain_ref[...] + shift_ref[...]).astype(BF)
        normed[...] = low
        if fast:
            feats = attn[0].shape[0]
            half = feats // 2
            turned = low.T
            for group in range(groups):
                first = turned[group * feats : group * feats + half]
                second = turned[group * feats + half : (group + 1) * feats]
                spot = slice(group * half, (group + 1) * half)
                low_ref[spot, :] = jnp.where(info[1] == 0, first, second)
                low_far[spot, :] = jnp.where(info[1] == 0, second, first)
                first = attn[group][:half]
                second = attn[group][half:]
                spot = slice((groups + group) * half, (groups + group + 1) * half)
                low_ref[spot, :] = jnp.where(info[1] == 0, first, second)
                low_far[spot, :] = jnp.where(info[1] == 0, second, first)
        else:
            low_ref[...] = low
        back[...] = jnp.zeros_like(back)

    up = nn(normed[...], up_ref[...])
    grad_act = nt(cot_ref[...], down_ref[...])
    square = up * up
    inner = GELU_A * (up + GELU_B * up * square)
    curve = jnp.tanh(inner)
    act = (0.5 * up * (1.0 + curve)).astype(BF)
    slope = 0.5 * (1.0 + curve) + 0.5 * up * (1.0 - curve * curve) * (
        GELU_A * (1.0 + 3.0 * GELU_B * square)
    )
    d_up = (grad_act * slope).astype(BF)
    if fast:
        part = act.shape[1]
        half = part // 2
        first, second = act[:, :half], act[:, half:]
        act_ref[...] = jnp.where(info[1] == 0, first, second)
        far_ref[:, pl.ds(pl.multiple_of(index * part, part), part)] = d_up
        spot = pl.ds(pl.multiple_of(hidden + index * half, half), half)
        far_ref[:, spot] = jnp.where(info[1] == 0, second, first)
    else:
        dup_ref[...] = d_up
        act_ref[...] = act
    back[...] += nt(d_up, up_ref[...])
    total[...] += nn(act, down_ref[...])

    @pl.when(index == chunks - 1)
    def after():
        out_ref[...] = total[...].astype(BF)
        d_normed = back[...]
        hat = hat_ref[...]
        gain_part = jnp.sum(d_normed * hat, axis=0, keepdims=True)
        shift_part = jnp.sum(d_normed, axis=0, keepdims=True)
        if fast:
            rows, width = low_far.shape[1], d_normed.shape[1]
            fold = []
            for part_row in split_low(gain_part) + split_low(shift_part):
                fold += [part_row[:, k : k + rows].astype(F32) for k in range(0, width, rows)]
            fold.append(jnp.zeros((low_far.shape[0] - width - len(fold), rows), F32))
            folded = jnp.concatenate(fold, axis=0).astype(BF)
            low_far[width:, :] = folded
            low_ref[width:, :] = folded
        else:
            blank = jnp.zeros((6, d_normed.shape[1]), F32)
            dn_ref[...] = jnp.concatenate([gain_part, shift_part, blank], axis=0)
        gy = d_normed * gain_ref[...]
        mean_one = jnp.mean(gy, axis=-1, keepdims=True)
        mean_two = jnp.mean(gy * hat, axis=-1, keepdims=True)
        d_resid = cot_ref[...].astype(F32) + inv_ref[:, 0:1] * (gy - mean_one - hat * mean_two)
        dres_ref[...] = d_resid
        branch = d_resid.astype(BF)
        if fast:
            far_ref[:, hidden * 3 // 2 :] = branch
        else:
            dbr_ref[...] = branch
        for group in range(groups):
            owner = lax.rem(info[0] + groups - group, groups)
            dat[group][...] = nt(wo_ref[owner], branch).astype(BF)


def weights_kernel(info, *refs, groups):
    (dup, dup_got, dbr, dbr_got, act, act_got, low, low_got, cot, cot_got) = refs[:10]
    send_u, keep_u, send_d, keep_d, outs = refs[10:]
    width = cot.shape[1]
    index = pl.program_id(0)
    group_at, place_u, place_d = info[0], info[3], info[4]
    rows = width // (2 * groups)
    quarter = rows // 4
    stay = groups * rows

    @pl.when(index == 0)
    def first():
        found = nn(low[stay:width, :], dbr[...]) + nn(low_got[stay:width, :], dbr_got[...])
        fold = low[width:, :].astype(F32) + low_got[width:, :].astype(F32)
        times = width // fold.shape[1]
        norms = []
        for part in range(2):
            both = fold[2 * part * times : (2 * part + 1) * times]
            both = both + fold[(2 * part + 1) * times : (2 * part + 2) * times]
            norms.append(jnp.concatenate([both[k : k + 1] for k in range(times)], axis=1))
        norms = jnp.concatenate(norms + [jnp.zeros((6, width), F32)], axis=0)
        for group in range(groups):
            block = found[group * rows : (group + 1) * rows]
            outs[group] = block
            for part in range(4):
                tail = block[part * quarter + 16 : (part + 1) * quarter]
                tail = jnp.concatenate([tail, norms], axis=0).astype(BF)
                place = lax.bitwise_xor(part, place_d)

                @pl.when(place >= 2)
                def leaves_more():
                    send_d[place - 2, (groups - group) % groups, rows:] = tail

                @pl.when(place < 2)
                def stays_more():
                    keep_d[place, (groups - group) % groups, rows:] = tail

    up = nn(low[:stay, :], dup[...]) + nn(low_got[:stay, :], dup_got[...])
    at = lax.bitwise_xor(lax.bitwise_xor(index, 2), place_u)
    for group in range(groups):
        spot = lax.rem(group + groups - group_at, groups)
        block = up[group * rows : (group + 1) * rows].astype(BF)
        away = (groups - group) % groups
        start = pl.multiple_of(at * quarter, 8)
        other = outs[group, pl.ds(start, 16), :].astype(BF)

        @pl.when(index < 2)
        def leaves():
            send_u[0, spot, :rows] = block
            send_u[0, away, rows:] = other

        @pl.when(index >= 2)
        def stays():
            keep_u[0, spot, :rows] = block
            keep_u[0, away, rows:] = other

    down = tn(act[...], cot[...]) + tn(act_got[...], cot_got[...])
    spot = lax.rem(index + groups - group_at, groups)
    for part in range(4):
        block = down[part * rows : (part + 1) * rows].astype(BF)
        place = lax.bitwise_xor(part, place_d)

        @pl.when(place >= 2)
        def leaves_down():
            send_d[place - 2, spot, :rows] = block

        @pl.when(place < 2)
        def stays_down():
            keep_d[place, spot, :rows] = block


def second_kernel(keep_u, got_u, keep_d, got_d, send_u, send_d):
    send_u[...] = (keep_u[0].astype(F32) + got_u[0].astype(F32)).astype(BF)
    send_d[...] = (keep_d[0].astype(F32) + got_d[0].astype(F32)).astype(BF)


def third_kernel(keep_u, got_u, last_u, keep_d, got_d, last_d, *outs):
    rows = keep_u.shape[2]
    for group in range(len(outs)):
        up = keep_u[0, group].astype(F32) + got_u[0, group].astype(F32) + last_u[group].astype(F32)
        down = keep_d[0, group].astype(F32) + got_d[0, group].astype(F32) + last_d[group].astype(F32)
        outs[group][:rows] = up.astype(BF)
        outs[group][rows:] = down.astype(BF)


def fourth_kernel(*refs):
    parts, out = refs[:-1], refs[-1]
    total = parts[0][...].astype(F32)
    for part in parts[1:]:
        total = total + part[...].astype(F32)
    out[...] = total.astype(BF)


def spread_kernel(info, own, from_x, from_y, from_xy, up_ref, out_ref, down_ref, norm_ref):
    index = pl.program_id(0)
    rows = up_ref.shape[0]
    quarter = out_ref.shape[0] // 4
    high = own.shape[0] // 2
    for place, part in enumerate((own, from_y, from_x, from_xy)):

        @pl.when(index == place)
        def upper(part=part):
            up_ref[...] = part[:rows].astype(F32)
            at = pl.multiple_of(lax.bitwise_xor(index, info[3]) * quarter, 8)
            out_ref[pl.ds(at, 16), :] = part[rows:high].astype(F32)

    for place, part in enumerate((own, from_x, from_y, from_xy)):

        @pl.when(index == place)
        def lower(part=part):
            down_ref[...] = part[high : high + rows].astype(F32)
            tail = part[high + rows :].astype(F32)
            at = pl.multiple_of(lax.bitwise_xor(index, info[4]) * quarter + 16, 8)
            out_ref[pl.ds(at, quarter - 16), :] = tail[: quarter - 16]

            @pl.when(lax.bitwise_xor(index, info[4]) == 0)
            def norms():
                norm_ref[...] = tail[quarter - 16 :]


def inward_kernel(info, *refs, groups, fast):
    parts, hat_ref = refs[:groups], refs[groups]
    outs = refs[groups + 1 :]
    heads, triple, rows = parts[0].shape
    hs = triple // 3
    total, sums = None, None
    ones = jnp.ones((16, rows), BF)
    for group in range(groups):
        order = [parts[group][h, k * hs : (k + 1) * hs] for k in range(3) for h in range(heads)]
        turned = jnp.concatenate(order, axis=0)
        found = nt(hat_ref[:, group * rows : (group + 1) * rows], turned)
        more = nt(ones, turned)
        total = found if total is None else total + found
        sums = more if sums is None else sums + more
    if not fast:
        outs[0][...] = total
        outs[1][...] = sums
        return
    own_ref, far_ref = outs
    block = total.shape[0] // (2 * groups)
    low_sums = sums.astype(BF)
    for group in range(groups):
        spot = lax.rem(group + groups - info[0], groups)
        first = total[2 * group * block : (2 * group + 1) * block].astype(BF)
        second = total[(2 * group + 1) * block : (2 * group + 2) * block].astype(BF)
        own_ref[spot, :block] = jnp.where(info[1] == 0, first, second)
        far_ref[spot, :block] = jnp.where(info[1] == 0, second, first)
        own_ref[spot, block:] = low_sums
        far_ref[spot, block:] = low_sums


def final_kernel(info, *refs, groups):
    parts = refs[:groups]
    x_ref, dres_ref, gain_ref, w_ref, out_ref = refs[groups:]
    d_normed = jnp.zeros(dres_ref.shape, F32)
    for group in range(groups):
        owner = lax.rem(info[0] + groups - group, groups)
        heads, triple, rows = parts[group].shape
        d_normed = d_normed + tn(parts[group][...].reshape(heads * triple, rows), w_ref[owner])
    values = x_ref[...].astype(F32)
    centered = values - jnp.mean(values, axis=-1, keepdims=True)
    variance = jnp.mean(centered * centered, axis=-1, keepdims=True)
    inverse = lax.rsqrt(variance + EPSILON)
    hat = centered * inverse
    gy = d_normed * gain_ref[...]
    mean_one = jnp.mean(gy, axis=-1, keepdims=True)
    mean_two = jnp.mean(gy * hat, axis=-1, keepdims=True)
    out_ref[...] = (dres_ref[...] + inverse * (gy - mean_one - hat * mean_two)).astype(BF)


def whole(shape):
    return pl.BlockSpec(shape, lambda *at: (0,) * len(shape))


def per_device(
    tokens,
    cluster_ids,
    lengths,
    top_keys,
    gain_one,
    shift_one,
    w_query,
    w_keyval,
    w_out,
    gain_two,
    shift_two,
    w_up,
    w_down,
    cotangent,
):
    rows, width = tokens.shape
    heads = cluster_ids.shape[1]
    hs = width // heads
    hidden = w_up.shape[1]
    wide = lax.axis_size("wide")
    n_dp = lax.axis_size("dp")
    groups = math.gcd(heads, wide)
    peers = wide // groups
    own_heads = heads // groups
    own_clusters = top_keys.shape[2]
    clusters = own_clusters * wide
    picks = top_keys.shape[3]
    seq = rows * wide
    size = 512 if seq <= 2048 else 2048
    feats = own_heads * hs
    block_rows = width // wide
    fast = peers == 2 and n_dp == 4 and block_rows == 96 and hidden == 4 * width and width % 256 == 0 and rows % 128 == 0
    me = lax.axis_index("wide")
    group_at, peer_at = me // peers, me % peers
    dp_at = lax.axis_index("dp")
    seq_len = lengths[0]
    bit_x, bit_y = dp_at % 2, (dp_at // 2) % 2
    place_u, place_d = 2 * bit_x + bit_y, 2 * bit_y + bit_x
    info = jnp.stack([group_at, peer_at, seq_len, place_u, place_d, me]).astype(jnp.int32)

    def along_groups(values, hop):
        pairs = [(i, ((i // peers + hop) % groups) * peers + i % peers) for i in range(wide)]
        return lax.ppermute(values, "wide", pairs)

    def along_peers(values, hop):
        pairs = [(i, (i // peers) * peers + (i % peers + hop) % peers) for i in range(wide)]
        return lax.ppermute(values, "wide", pairs)

    def along_dp(values, mask):
        return lax.ppermute(values, "dp", [(i, i ^ mask) for i in range(n_dp)])

    def prefetched(kernel, grid, in_specs, out_specs, out_shape, mib, spent, name, scratch=(), alias=None):
        return pl.pallas_call(
            kernel,
            grid_spec=pltpu.PrefetchScalarGridSpec(
                num_scalar_prefetch=1,
                grid=grid,
                in_specs=in_specs,
                out_specs=out_specs,
                scratch_shapes=list(scratch),
            ),
            out_shape=out_shape,
            compiler_params=params(mib, len(grid)),
            cost_estimate=spent,
            input_output_aliases=alias or {},
            name=name,
        )

    def after(values, *others):
        return lax.optimization_barrier((values, others))[0]

    def array(shape, dtype):
        return jax.ShapeDtypeStruct(shape, dtype)

    position = me * rows + jnp.arange(rows, dtype=jnp.int32)
    marked = jnp.where((position < seq_len)[:, None], cluster_ids, -1).T
    tops = jnp.zeros((heads, picks, clusters), jnp.int32)
    tops = lax.dynamic_update_slice(
        tops, top_keys[0].transpose(0, 2, 1), (0, 0, me * own_clusters)
    )
    lines = rows // clusters
    packed = jnp.concatenate([tops, marked.reshape(heads, lines, clusters)], axis=1)
    early = [along_peers(tokens, -hop) for hop in range(1, peers)]
    packed = after(packed.reshape(groups, own_heads, picks + lines, clusters), early)

    def of_heads(hop):
        return lax.dynamic_index_in_dim(packed, (group_at + groups - hop) % groups, keepdims=False)

    arrived = [of_heads(0)] + [along_groups(of_heads(hop), -hop) for hop in range(1, groups)]

    mine = {0: tokens, 1: along_groups(tokens, -1)}
    if groups > 2:
        mine[groups - 1] = along_groups(tokens, 1)
    ready = after(tokens, arrived)
    for hop in range(2, groups - 1):
        mine[hop] = along_groups(ready, -hop)

    w_in = jnp.concatenate([w_query, w_keyval], axis=1).T.reshape(3, heads, hs, width)
    w_in = w_in.transpose(1, 0, 2, 3).reshape(groups, 3 * feats, width)
    table_shape = (own_heads, picks + groups * lines, clusters)
    table = pl.pallas_call(
        functools.partial(table_kernel, picks=picks),
        grid=(1,),
        in_specs=[whole((own_heads, picks + lines, clusters))] * groups,
        out_specs=whole(table_shape),
        out_shape=array(table_shape, jnp.int32),
        compiler_params=params(8, 1),
        cost_estimate=cost(1e5, 1e6),
        name="table",
    )(*after(arrived, w_in))
    tables = [table] + [along_peers(table, -hop) for hop in range(1, peers)]
    cot_got = [along_peers(after(cotangent, arrived), hop) for hop in range(1, peers)]
    cot_got = cot_got if fast else []
    bias, ids_all = prefetched(
        functools.partial(bias_kernel, groups=groups, peers=peers, rows=rows, picks=picks),
        (wide,),
        [whole(table_shape)] * peers,
        [
            pl.BlockSpec((own_heads, rows, clusters), lambda i, s: (0, i, 0)),
            whole((own_heads, 1, seq)),
        ],
        [array((own_heads, seq, clusters), BF), array((own_heads, 1, seq), jnp.int32)],
        12 if fast else 60,
        cost(own_heads * seq * clusters * picks * 8, own_heads * seq * clusters * 2),
        "bias",
    )(info, *tables)

    gain_row, shift_row = gain_one[None, :], shift_one[None, :]
    shapes = [
        array((width, groups * rows), BF),
        array((own_heads, 3 * hs, seq), BF),
        array((own_heads, seq, 2 * hs), BF),
    ]
    held = []
    split_peers = peers if peers <= 2 else 1
    for group in sorted(range(groups), key=lambda g: min(g, groups - g)):
        arrival = mine[group]
        if 1 < group < groups - 1:
            arrival = after(arrival, held, cot_got)
        elif group == 1:
            arrival = after(arrival, bias)
        elif group:
            arrival = after(arrival, bias, [mine[hop] for hop in range(2, group)])
        chunk = [arrival]
        chunk += early if group == 0 else [along_peers(arrival, -hop) for hop in range(1, peers)]
        if peers > 2:
            chunk = [jnp.concatenate(chunk, axis=0)]
        span = peers * rows
        if peers > 2:
            specs_in = [pl.BlockSpec((rows, width), lambda p, s: (p, 0))]
            grid = (peers,)
            outs = [
                pl.BlockSpec((width, rows), lambda p, s, g=group: (0, g)),
                pl.BlockSpec((own_heads, 3 * hs, rows), lambda p, s, g=group: (0, 0, g * peers + p)),
                pl.BlockSpec((own_heads, rows, 2 * hs), lambda p, s, g=group: (0, g * peers + p, 0)),
            ]
        else:
            specs_in = [whole((rows, width))] * split_peers
            grid = (1,)
            outs = [
                pl.BlockSpec((width, rows), lambda p, s, g=group: (0, g)),
                pl.BlockSpec((own_heads, 3 * hs, span), lambda p, s, g=group: (0, 0, g)),
                pl.BlockSpec((own_heads, span, 2 * hs), lambda p, s, g=group: (0, g, 0)),
            ]
        first = 1 + split_peers + 3
        held = prefetched(
            functools.partial(project_kernel, peers=split_peers, olds=len(held)),
            grid,
            specs_in
            + [
                whole((1, width)),
                whole((1, width)),
                pl.BlockSpec((1, 3 * feats, width), lambda p, s: (s[0], 0, 0)),
            ]
            + [pl.BlockSpec(memory_space=pl.ANY)] * len(held),
            outs,
            shapes,
            16 if fast else 60,
            cost(6 * span * width * feats, span * width * 4),
            "project",
            alias={first + k: k for k in range(len(held))},
        )(info, *chunk, gain_row, shift_row, w_in, *held)
    hat_own, feat, kv = held

    ids_full = pl.BlockSpec((1, 1, seq), lambda h, r: (h, 0, 0))
    feat_full = pl.BlockSpec((1, 3 * hs, seq), lambda h, r: (h, 0, 0))
    kv_full = pl.BlockSpec((1, seq, 2 * hs), lambda h, r: (h, 0, 0))
    bias_full = pl.BlockSpec((1, seq, clusters), lambda h, r: (h, 0, 0))
    head_rows = pl.BlockSpec((hs, rows), lambda h, r: (h, 0))
    mix_spec = pl.BlockSpec((1, 1, hs + 8, rows), lambda h, r: (h, r, 0, 0))
    stat_spec = pl.BlockSpec((1, hs + 8, clusters), lambda h, r: (h, 0, 0))
    cen_spec = pl.BlockSpec((1, hs, clusters), lambda h, r: (h, 0, 0))
    own_rows = groups * rows
    pair_flops = own_heads * own_rows * seq * 256

    one = [
        pl.BlockSpec(spec.block_shape, functools.partial(lambda h, f: f(h, 0), f=spec.index_map))
        for spec in (ids_full, feat_full, kv_full, bias_full, stat_spec, cen_spec, head_rows)
    ]
    ids_one, feat_one, kv_one, bias_one, stat_one, cen_one, rows_one = one
    part_one = pl.BlockSpec((1, hs + 16, clusters), lambda h: (h, 0, 0))
    mix_one = pl.BlockSpec((1, groups, hs + 8, rows), lambda h: (h, 0, 0, 0))
    all_groups = pl.BlockSpec((groups, hs, rows), lambda h: (0, h, 0))
    own_one = pl.BlockSpec((1, own_rows, 2 * hs), lambda h: (h, 0, 0))
    results = pl.pallas_call(
        functools.partial(forward_kernel, size=size, groups=groups, rows=rows),
        grid=(own_heads,),
        in_specs=[ids_one, feat_one, kv_one, bias_one],
        out_specs=[rows_one] * groups + [mix_one, stat_one, cen_one],
        out_shape=[array((feats, rows), BF)] * groups
        + [
            array((own_heads, groups, hs + 8, rows), F32),
            array((own_heads, hs + 8, clusters), F32),
            array((own_heads, hs, clusters), BF),
        ],
        compiler_params=params(32 if fast else 60, 1),
        cost_estimate=cost(6 * pair_flops, 8e6, own_heads * own_rows * seq),
        name="attend",
    )(ids_all, feat, kv, bias)
    attn_t = results[:groups]
    mixed, stats, centroid = results[groups:]

    arrived = [attn_t[0]] + [along_groups(attn_t[hop], hop) for hop in range(1, groups)]

    chunks = 4
    part = hidden // chunks
    w_out_g = w_out.reshape(groups, feats, width)
    gain_row2, shift_row2 = gain_two[None, :], shift_two[None, :]
    square = whole((rows, width))
    column = pl.BlockSpec((rows, part), lambda i, s: (0, i))
    norm_spec = whole((8, width))
    if fast:
        kept_shapes = [
            array((rows, hidden + hidden // 2 + width), BF),
            array((width + 16, rows), BF),
            array((rows, hidden // 2), BF),
            array((width + 16, rows), BF),
        ]
        kept_specs = [whole(item.shape) for item in kept_shapes]
        kept_specs[2] = pl.BlockSpec((rows, part // 2), lambda i, s: (0, i))
    else:
        kept_shapes = [
            array((8, width), F32),
            array((rows, hidden), BF),
            array((rows, width), BF),
            array((rows, hidden), BF),
            array((rows, width), BF),
        ]
        kept_specs = [norm_spec, column, square, column, square]
    results = prefetched(
        functools.partial(block_kernel, groups=groups, chunks=chunks, fast=fast),
        (chunks,),
        [whole((feats, rows))] * groups
        + [
            square,
            whole((1, width)),
            whole((1, width)),
            whole((groups, feats, width)),
            pl.BlockSpec((width, part), lambda i, s: (0, i)),
            pl.BlockSpec((part, width), lambda i, s: (i, 0)),
            square,
        ],
        [square, square] + kept_specs + [whole((feats, rows))] * groups,
        [array((rows, width), BF), array((rows, width), F32)]
        + kept_shapes
        + [array((feats, rows), BF)] * groups,
        28 if fast else 60,
        cost(8 * rows * width * hidden, 4 * width * hidden, rows * hidden),
        "feed",
        scratch=[
            pltpu.VMEM((rows, width), F32),
            pltpu.VMEM((rows, 128), F32),
            pltpu.VMEM((rows, width), BF),
            pltpu.VMEM((rows, width), F32),
            pltpu.VMEM((rows, width), F32),
        ],
    )(info, *arrived, tokens, gain_row2, shift_row2, w_out_g, w_up, w_down, cotangent)
    output, d_resid = results[:2]
    kept, d_attn = results[2:-groups], results[-groups:]
    grads = [d_attn[0]] + [along_groups(d_attn[hop], -hop) for hop in range(1, groups)]

    def weight_parts():
        far, low_far, act_own, low_own = kept
        got, low_got = along_peers(far, 1), along_peers(low_far, 1)
        high = block_rows + 16
        chunk = pl.BlockSpec((rows, part), lambda i, s: (0, i ^ 2 ^ s[3]))
        branch = pl.BlockSpec((rows, width), lambda i, s: (0, hidden * 3 // 2 // width))
        act_spec = pl.BlockSpec((rows, part // 2), lambda i, s: (0, i))
        act_there = pl.BlockSpec((rows, part // 2), lambda i, s: (0, 2 * hidden // part + i))
        low_spec = whole((width + 16, rows))
        shape_u = (2, groups, high, width)
        shape_d = (2, groups, high, width)
        send_u, keep_u, send_d, keep_d = prefetched(
            functools.partial(weights_kernel, groups=groups),
            (4,),
            [chunk, chunk, branch, branch, act_spec, act_there, low_spec, low_spec, square, square],
            [
                pl.BlockSpec((1,) + shape_u[1:], lambda i, s: (jnp.minimum(i, 1), 0, 0, 0)),
                pl.BlockSpec((1,) + shape_u[1:], lambda i, s: (jnp.maximum(i - 2, 0), 0, 0, 0)),
                whole(shape_d),
                whole(shape_d),
            ],
            [array(shape_u, BF), array(shape_u, BF), array(shape_d, BF), array(shape_d, BF)],
            28,
            cost(8 * rows * width * hidden, 6 * width * hidden),
            "weights",
            scratch=[pltpu.VMEM((groups, block_rows, width), F32)],
        )(info, far, got, far, got, act_own, got, low_own, low_got, cotangent, *cot_got)
        return send_u, keep_u, send_d, keep_d

    def weight_second(keep_u, got_u, keep_d, got_d):
        shape_u, shape_d = keep_u.shape, keep_d.shape
        high = shape_u[2]

        def block(shape, at):
            return pl.BlockSpec((1,) + shape[1:], lambda i: (at, 0, 0, 0))

        next_u, next_d = pl.pallas_call(
            second_kernel,
            grid=(1,),
            in_specs=[block(shape_u, 1), block(shape_u, 1), block(shape_d, 1), block(shape_d, 1)],
            out_specs=[whole(shape_u[1:]), whole(shape_d[1:])],
            out_shape=[array(shape_u[1:], BF), array(shape_d[1:], BF)],
            compiler_params=params(20, 1),
            cost_estimate=cost(groups * high * width * 2, groups * high * width * 12),
            name="second",
        )(keep_u, got_u, keep_d, got_d)
        return next_u, next_d

    def weight_third(keep_u, got_u, last_u, keep_d, got_d, last_d):
        shape_u, shape_d = keep_u.shape, keep_d.shape
        high = shape_u[2]

        def block(shape, at):
            return pl.BlockSpec((1,) + shape[1:], lambda i: (at, 0, 0, 0))

        tall = shape_u[2] + shape_d[2]
        sums = pl.pallas_call(
            third_kernel,
            grid=(1,),
            in_specs=[
                block(shape_u, 0),
                block(shape_u, 0),
                whole(shape_u[1:]),
                block(shape_d, 0),
                block(shape_d, 0),
                whole(shape_d[1:]),
            ],
            out_specs=[whole((tall, width))] * groups,
            out_shape=[array((tall, width), BF)] * groups,
            compiler_params=params(24, 1),
            cost_estimate=cost(groups * tall * width * 4, groups * tall * width * 8),
            name="third",
        )(keep_u, got_u, last_u, keep_d, got_d, last_d)
        came = [sums[0]] + [along_groups(sums[hop], hop) for hop in range(1, groups)]
        return came

    def weight_sums(came, shape_u, shape_d):
        tall = shape_u[2] + shape_d[2]
        done = pl.pallas_call(
            fourth_kernel,
            grid=(1,),
            in_specs=[whole((tall, width))] * groups,
            out_specs=whole((tall, width)),
            out_shape=array((tall, width), BF),
            compiler_params=params(12, 1),
            cost_estimate=cost(groups * tall * width, groups * tall * width * 2),
            name="fourth",
        )(*came)
        from_x, from_y, from_xy = (along_dp(done, mask) for mask in (1, 2, 3))
        total_up, total_out, total_down, norms = prefetched(
            spread_kernel,
            (4,),
            [whole((tall, width))] * 4,
            [
                pl.BlockSpec((block_rows, part), lambda i, s: (0, i ^ s[3])),
                whole((block_rows, width)),
                pl.BlockSpec((block_rows, width), lambda i, s: (i ^ s[4], 0)),
                whole((8, width)),
            ],
            [
                array((block_rows, hidden), F32),
                array((block_rows, width), F32),
                array((hidden // wide, width), F32),
                array((8, width), F32),
            ],
            16,
            cost(1e6, 4 * tall * width * 6),
            "spread",
        )(info, done, from_x, from_y, from_xy)
        norm_own = lax.dynamic_slice_in_dim(norms, me * block_rows, block_rows, axis=1)
        return total_up, total_out, total_down, norm_own, done

    masks = [1 << k for k in range(n_dp.bit_length() - 1)]

    def reduce_rows(partial):
        blocks = partial.reshape(groups, peers, partial.shape[0] // wide, partial.shape[1])

        def of_peer(hop):
            at = (peer_at + hop) % peers
            return lax.dynamic_index_in_dim(blocks, at, axis=1, keepdims=False)

        total = of_peer(0).astype(F32)
        for hop in range(1, peers):
            total = total + along_peers(of_peer(hop), hop).astype(F32)
        total = total.astype(BF)

        def of_group(hop):
            return lax.dynamic_index_in_dim(total, (group_at + hop) % groups, keepdims=False)

        done = of_group(0).astype(F32)
        for hop in range(1, groups):
            done = done + along_groups(of_group(hop), hop).astype(F32)
        for mask in masks:
            done = done.astype(BF)
            done = done.astype(F32) + along_dp(done, mask).astype(F32)
        return done

    if fast:
        send_u, keep_u, send_d, keep_d = weight_parts()
        got_u, got_d = along_dp(send_u, 1), along_dp(send_d, 2)
        grads = after(grads, keep_u)
    else:
        norm_two, d_up, d_branch, act, normed_two = kept
        total_up = reduce_rows(tn(normed_two, d_up).astype(BF))
        total_down = reduce_rows(tn(act, cotangent).astype(BF))
        found = jnp.stack([nn(item, d_branch).astype(BF) for item in arrived])
        found = [
            lax.dynamic_index_in_dim(found, (group_at + groups - g) % groups, keepdims=False)
            for g in range(groups)
        ]
        total_out = reduce_rows(jnp.concatenate(found, axis=0))
        norm_own = reduce_rows(norm_two[:2].T.astype(BF)).T

    share = pl.pallas_call(
        functools.partial(sums_kernel, groups=groups),
        grid=(own_heads,),
        in_specs=[ids_one]
        + [rows_one] * groups
        + [mix_one],
        out_specs=part_one,
        out_shape=array((own_heads, hs + 16, clusters), F32),
        compiler_params=params(16 if fast else 60, 1),
        cost_estimate=cost(own_heads * own_rows * clusters * 160, 2e6),
        name="sums",
    )(ids_all, *grads, mixed)
    share_got = [along_peers(share, hop) for hop in range(1, peers)]

    back_shapes = [
        array((groups, feats, rows), BF),
        array((own_heads, 2 * hs, own_rows), F32),
        array((own_heads, 2 * hs, max(peers - 1, 1) * own_rows), BF),
    ]
    dq, dkv_own, dkv_send = pl.pallas_call(
        functools.partial(back_kernel, size=size, groups=groups, gots=len(share_got)),
        grid=(own_heads,),
        in_specs=[ids_one, feat_one, kv_one, bias_one]
        + [rows_one] * groups
        + [mix_one, stat_one, cen_one]
        + [part_one] * (1 + len(share_got)),
        out_specs=[
            all_groups,
            pl.BlockSpec((1,) + back_shapes[1].shape[1:], lambda h: (h, 0, 0)),
            pl.BlockSpec((1,) + back_shapes[2].shape[1:], lambda h: (h, 0, 0)),
        ],
        out_shape=back_shapes,
        scratch_shapes=[pltpu.VMEM((seq, 2 * hs), F32), pltpu.VMEM((seq, 2 * clusters), BF)],
        compiler_params=params(36 if fast else 62, 1),
        cost_estimate=cost(14 * pair_flops, 10e6, own_heads * own_rows * seq),
        name="back",
    )(ids_all, feat, kv, bias, *grads, mixed, stats, centroid, share, *share_got)
    dkv_got = [
        along_peers(
            dkv_send if peers == 2 else dkv_send[..., (hop - 1) * own_rows : hop * own_rows], hop
        )
        for hop in range(1, peers)
    ]
    d_in = pl.pallas_call(
        functools.partial(join_kernel, groups=groups),
        grid=(1,),
        in_specs=[whole(back_shapes[0].shape), whole(back_shapes[1].shape)]
        + [whole(back_shapes[1].shape)] * len(dkv_got),
        out_specs=[whole((own_heads, 3 * hs, rows))] * groups,
        out_shape=[array((own_heads, 3 * hs, rows), BF)] * groups,
        compiler_params=params(20, 1),
        cost_estimate=cost(own_rows * feats * 8, own_rows * feats * 16),
        name="join",
    )(dq, dkv_own, *dkv_got)

    home = [d_in[0]] + [along_groups(d_in[hop], hop) for hop in range(1, groups)]

    tall = block_rows + 16
    part_spec = [whole((own_heads, 3 * hs, rows))] * groups + [whole((width, own_rows))]
    inward = functools.partial(
        prefetched,
        functools.partial(inward_kernel, groups=groups, fast=fast),
        (1,),
        part_spec,
    )
    spent = cost(2 * own_rows * width * 3 * feats, 4e6)
    if fast:
        half = groups // 2
        blocks = (groups, tall, 3 * feats)
        got_u, got_d = after((got_u, got_d), home[1])
        next_u, next_d = weight_second(keep_u, got_u, keep_d, got_d)
        keep, far = inward(
            [whole(blocks)] * 2, [array(blocks, BF)] * 2, 24, spent, "inward"
        )(info, *after(d_in, next_u, next_d), hat_own)
        got = along_peers(far, 1)
        total = keep.astype(F32) + got.astype(F32)
        one_half, two_half = total[:half].astype(BF), total[half:].astype(BF)
        last_u, last_d = along_dp(next_u, 2), along_dp(next_d, 1)
        last_u, last_d = after((last_u, last_d), home)
        came = weight_third(keep_u, got_u, last_u, keep_d, got_d, last_d)
        for mask in (1, 2):
            one_half, two_half = after((one_half, two_half), came[mask])
            got_one, got_two = along_dp(one_half, mask), along_dp(two_half, 3 - mask)
            one_half = (one_half.astype(F32) + got_one.astype(F32)).astype(BF)
            two_half = (two_half.astype(F32) + got_two.astype(F32)).astype(BF)
        total_up, total_out, total_down, norm_own, done = weight_sums(
            after(came, one_half, two_half), keep_u.shape, keep_d.shape
        )
        home = after(home, done)
        items = [one_half[k] for k in range(half)] + [two_half[k] for k in range(half)]
    else:
        found, more = inward(
            [whole((width, 3 * feats)), whole((16, 3 * feats))],
            [array((width, 3 * feats), F32), array((16, 3 * feats), F32)],
            60,
            spent,
            "inward",
        )(info, *d_in, hat_own)
        found = found.reshape(groups, peers, block_rows, 3 * feats)
        more = jnp.broadcast_to(more, (groups, peers, 16, 3 * feats))
        found = jnp.concatenate([found, more], axis=2).astype(BF)

        def of_peer(hop):
            at = (peer_at + hop) % peers
            return lax.dynamic_index_in_dim(found, at, axis=1, keepdims=False)

        total = of_peer(0).astype(F32)
        for hop in range(1, peers):
            total = total + along_peers(of_peer(hop), hop).astype(F32)
        for mask in masks:
            total = total.astype(BF)
            total = total.astype(F32) + along_dp(total, mask).astype(F32)
        total = total.astype(BF)
        items = [
            lax.dynamic_index_in_dim(total, (group_at + hop) % groups, keepdims=False)
            for hop in range(groups)
        ]
    pieces = [items[0]] + [along_groups(items[hop], hop) for hop in range(1, groups)]

    grad_tokens = prefetched(
        functools.partial(final_kernel, groups=groups),
        (1,),
        [whole((own_heads, 3 * hs, rows))] * groups
        + [square, square, whole((1, width)), whole((groups, 3 * feats, width))],
        square,
        array((rows, width), BF),
        24 if fast else 60,
        cost(6 * rows * width * width, 6 * width * width),
        "final",
    )(info, *home, tokens, d_resid, gain_row, w_in)

    pieces = jnp.stack(pieces)
    pieces = jnp.stack(
        [
            lax.dynamic_index_in_dim(pieces, (group_at + groups - g) % groups, keepdims=False)
            for g in range(groups)
        ]
    ).astype(F32)
    q_part = pieces[:, :, :feats].transpose(1, 0, 2).reshape(tall, width)
    kv_part = (
        pieces[:, :, feats:]
        .reshape(groups, tall, 2, feats)
        .transpose(1, 2, 0, 3)
        .reshape(tall, 2 * width)
    )
    at = me * block_rows
    wq_rows = lax.dynamic_slice_in_dim(w_query, at, block_rows).astype(F32)
    wkv_rows = lax.dynamic_slice_in_dim(w_keyval, at, block_rows).astype(F32)
    gain_own = lax.dynamic_slice_in_dim(gain_one, at, block_rows)
    shift_own = lax.dynamic_slice_in_dim(shift_one, at, block_rows)
    q_sum, kv_sum = q_part[block_rows], kv_part[block_rows]
    q_part, kv_part = q_part[:block_rows], kv_part[:block_rows]
    shift_grad = jnp.sum(wq_rows * q_sum, axis=1) + jnp.sum(wkv_rows * kv_sum, axis=1)
    along = jnp.sum(wq_rows * q_part, axis=1) + jnp.sum(wkv_rows * kv_part, axis=1)
    return (
        output,
        grad_tokens,
        q_part + shift_own[:, None] * q_sum,
        kv_part + shift_own[:, None] * kv_sum,
        total_out,
        total_up,
        total_down,
        along / gain_own,
        shift_grad,
        norm_own[0],
        norm_own[1],
    )


def solution(mesh):
    return jax.shard_map(
        per_device,
        mesh=mesh,
        in_specs=(
            P(("dp", "wide"), None),
            P(("dp", "wide"), None),
            P("dp"),
            P("dp", None, "wide", None),
            P(),
            P(),
            P(),
            P(),
            P(),
            P(),
            P(),
            P(),
            P(),
            P(("dp", "wide"), None),
        ),
        out_specs=(
            P(("dp", "wide"), None),
            P(("dp", "wide"), None),
            P("wide", None),
            P("wide", None),
            P("wide", None),
            P("wide", None),
            P("wide", None),
            P("wide"),
            P("wide"),
            P("wide"),
            P("wide"),
        ),
        check_vma=False,
    )
```

```python
import functools
import math

import jax
import jax.numpy as jnp
import numpy as np
from jax import lax
from jax.experimental import pallas as pl
from jax.experimental.pallas import tpu as pltpu
from jax.sharding import PartitionSpec as P

EPSILON = 1e-05
NEGATIVE = -1e30
EXCLUDED = -3e30
GELU_A = math.sqrt(2.0 / math.pi)
GELU_B = 0.044715
BF = jnp.bfloat16
F32 = jnp.float32


def nn(left, right):
    return lax.dot_general(left, right, (((1,), (0,)), ((), ())), preferred_element_type=F32)


def nt(left, right):
    return lax.dot_general(left, right, (((1,), (1,)), ((), ())), preferred_element_type=F32)


def tn(left, right):
    return lax.dot_general(left, right, (((0,), (0,)), ((), ())), preferred_element_type=F32)


def params(mib, dims):
    return pltpu.CompilerParams(
        vmem_limit_bytes=mib * 1024 * 1024, dimension_semantics=("arbitrary",) * dims
    )


def cost(flops, nbytes, trans=0):
    return pl.CostEstimate(flops=int(flops), bytes_accessed=int(nbytes), transcendentals=int(trans))


def split_low(values):
    high = values.astype(BF)
    return high, (values - high.astype(F32)).astype(BF)


def one_hot_t(ids_row, clusters):
    rows = lax.broadcasted_iota(jnp.int32, (clusters, ids_row.shape[1]), 0)
    return jnp.where(rows == ids_row, 1.0, 0.0).astype(BF)


def key_passes(total, size, score, weigh, blocks=None):
    count = total // size
    if count <= 4:
        if blocks is None:
            blocks = [score(index) for index in range(count)]
        peak = functools.reduce(jnp.maximum, [jnp.max(b, axis=0, keepdims=True) for b in blocks])
        denom, sums = 0.0, None
        for index in range(count):
            expo = jnp.exp(blocks[index] - peak)
            denom = denom + jnp.sum(expo, axis=0, keepdims=True)
            parts = weigh(index, expo)
            sums = parts if sums is None else tuple(x + y for x, y in zip(sums, parts))
        return peak, denom, sums

    def step(index, carry):
        peak, denom, sums = carry
        block = score(index)
        fresh = jnp.maximum(peak, jnp.max(block, axis=0, keepdims=True))
        expo = jnp.exp(block - fresh)
        fade = jnp.exp(peak - fresh)
        parts = weigh(index, expo)
        return (
            fresh,
            denom * fade + jnp.sum(expo, axis=0, keepdims=True),
            tuple(old * fade + new for old, new in zip(sums, parts)),
        )

    shapes = jax.eval_shape(lambda: (score(0), weigh(0, score(0))))
    lanes = shapes[0].shape[1]
    start = (
        jnp.full((1, lanes), NEGATIVE, F32),
        jnp.zeros((1, lanes), F32),
        tuple(jnp.zeros(item.shape, F32) for item in shapes[1]),
    )
    return lax.fori_loop(0, count, step, start)


def key_sum(total, size, step, start):
    count = total // size
    if count <= 4:
        for index in range(count):
            start = step(index, start)
        return start
    return lax.fori_loop(0, count, step, start)


def spot_of(index, size):
    if isinstance(index, int):
        return pl.ds(index * size, size)
    return pl.ds(pl.multiple_of(index * size, size), size)


def piece(ref, index, size, axis):
    spot = spot_of(index, size)
    return ref[spot, :] if axis == 0 else ref[:, spot]


def table_kernel(*refs, picks):
    parts, out = refs[:-1], refs[-1]
    total = parts[0][:, :picks]
    for part in parts[1:]:
        total = total + part[:, :picks]
    out[:, :picks] = total
    rows = parts[0].shape[1] - picks
    for group, part in enumerate(parts):
        out[:, picks + group * rows : picks + (group + 1) * rows] = part[:, picks:]


def bias_kernel(info, *refs, groups, peers, rows, picks):
    tables, (bias_ref, ids_ref) = refs[:peers], refs[peers:]
    part = pl.program_id(0)
    owner = (
        lax.rem(info[0] + part // peers, groups) * peers + lax.rem(info[1] + part % peers, peers)
    )
    heads, _, clusters = tables[0].shape
    place = owner * rows + lax.broadcasted_iota(jnp.int32, (rows, clusters), 0)
    plain = jnp.where(place >= info[2], EXCLUDED, NEGATIVE)
    for head in range(heads):
        top = tables[0][head, :picks]
        for table in tables[1:]:
            top = top + table[head, :picks]
        value = plain
        for pick in range(picks):
            value = jnp.where(place == top[pick : pick + 1, :], 0.0, value)
        bias_ref[head] = value.astype(BF)

    @pl.when(part == 0)
    def ids():
        lines = rows // clusters
        for head in range(heads):
            row = []
            for group in range(groups):
                for table in tables:
                    for line in range(lines):
                        at = picks + group * lines + line
                        row.append(table[head, at : at + 1, :])
            ids_ref[head] = jnp.concatenate(row, axis=1)


def project_kernel(info, *refs, peers, olds):
    parts = refs[:peers]
    gain_ref, shift_ref, w_ref = refs[peers : peers + 3]
    hat_ref, feat_ref, kv_ref = refs[peers + 3 + olds :]
    rows = hat_ref.shape[1]
    for peer in range(peers):
        values = parts[peer][...].astype(F32)
        centered = values - jnp.mean(values, axis=-1, keepdims=True)
        variance = jnp.mean(centered * centered, axis=-1, keepdims=True)
        scaled = centered * lax.rsqrt(variance + EPSILON) * gain_ref[...]
        if peer == 0:
            hat_ref[...] = scaled.astype(BF).T
        low = (scaled + shift_ref[...]).astype(BF)
        found = nt(w_ref[0], low)
        heads, triple = feat_ref.shape[0], feat_ref.shape[1]
        hs = triple // 3
        spot = slice(peer * rows, (peer + 1) * rows)
        for head in range(heads):
            base = head * triple
            query = (found[base : base + hs] * 0.125).astype(BF)
            pair = found[base + hs : base + triple].astype(BF)
            feat_ref[head, :hs, spot] = query
            feat_ref[head, hs:, spot] = pair
            kv_ref[head, spot, :] = pair.T


def forward_kernel(ids_all, feat, kv, bias, *refs, size, groups, rows):
    outs = refs[:groups]
    mix_ref, stat_ref, cen_ref = refs[groups:]
    hs = feat.shape[1] // 3
    keys = kv.shape[1]
    count = keys // size
    clusters = bias.shape[2]
    kv_h, bias_h = kv.at[0], bias.at[0]
    queries_all, kvt = feat.at[0, :hs], feat.at[0, hs:]
    hot_all = one_hot_t(ids_all[0], clusters)
    ones = jnp.ones((16, keys), BF)
    sums = nt(jnp.concatenate([queries_all[...], ones], axis=0), hot_all)
    counts = sums[hs : hs + 1]
    centroid = (sums[:hs] / jnp.maximum(counts, 1.0)).astype(BF)
    padded = jnp.concatenate([centroid, jnp.zeros_like(centroid)], axis=0)

    def cluster_score(index):
        scores = nn(piece(kv_h, index, size, 0), padded)
        outside = piece(bias_h, index, size, 0).astype(F32) < 2.0 * NEGATIVE
        return jnp.where(outside, NEGATIVE, scores)

    def cluster_weigh(index, expo):
        top = piece(bias_h, index, size, 0).astype(F32) == 0.0
        mass = jnp.sum(jnp.where(top, expo, 0.0), axis=0, keepdims=True)
        other = jnp.where(top, 0.0, expo).astype(BF)
        return nn(piece(kvt, index, size, 1), other), mass

    peers = keys // (groups * rows)
    hots, sides = [], []
    for group in range(groups):
        spot = slice(group * peers * rows, group * peers * rows + rows)
        hot = one_hot_t(ids_all[0, :, spot], clusters)
        queries = queries_all[:, spot]
        hots.append(hot)
        sides.append(jnp.concatenate([queries, jnp.zeros_like(queries), hot], axis=0))

    def member_score(group, index):
        both = jnp.concatenate([piece(kv_h, index, size, 0), piece(bias_h, index, size, 0)], axis=1)
        return nn(both, sides[group])

    def member_weigh(index, expo):
        return (nn(piece(kvt, index, size, 1), expo.astype(BF)),)

    short = count <= 4
    ahead = None
    if short:
        ahead = [member_score(0, index) for index in range(count)]
    peak, denom, (rest, mass) = key_passes(keys, size, cluster_score, cluster_weigh)
    rest = rest[hs:] / denom
    mass = mass / denom
    blank = jnp.zeros((5, clusters), F32)
    stats = jnp.concatenate([rest, mass, peak + jnp.log(denom), counts, blank], axis=0)
    stat_ref[0] = stats
    cen_ref[0] = centroid
    high, low = split_low(stats)
    table = jnp.concatenate([high, low], axis=1)
    for group in range(groups):
        gathered = nn(table, jnp.concatenate([hots[group], hots[group]], axis=0))
        blocks, ahead = ahead, None
        if short and group + 1 < groups:
            ahead = [member_score(group + 1, index) for index in range(count)]
        score = functools.partial(member_score, group)
        peak, denom, (mix,) = key_passes(keys, size, score, member_weigh, blocks)
        mix = mix[hs:] / denom
        outs[group][...] = (gathered[hs : hs + 1] * mix + gathered[:hs]).astype(BF)
        level = jnp.broadcast_to(peak + jnp.log(denom), (8, rows))
        mix_ref[0, group] = jnp.concatenate([mix, level], axis=0)


def sums_kernel(ids_own, *refs, groups):
    grads, (mix_ref, part_ref) = refs[:groups], refs[groups:]
    hs = grads[0].shape[0]
    total = None
    for group in range(groups):
        rows = grads[group].shape[1]
        step = ids_own.shape[2] // groups
        hot = one_hot_t(ids_own[0, :, group * step : group * step + rows], part_ref.shape[2])
        grad = grads[group][...]
        along = jnp.sum(grad.astype(F32) * mix_ref[0, group, :hs], axis=0, keepdims=True)
        high, low = split_low(along)
        pad = jnp.zeros((14, rows), BF)
        part = nt(jnp.concatenate([grad, high, low, pad], axis=0), hot)
        total = part if total is None else total + part
    part_ref[0] = total


def back_kernel(ids_all, feat, kv, bias, *refs, size, groups, gots):
    grads = refs[:groups]
    mix_ref, stat_ref, cen_ref = refs[groups : groups + 3]
    shares = refs[groups + 3 : groups + 4 + gots]
    dq_ref, own_ref, send_ref, total, both = refs[groups + 4 + gots :]
    hs, rows = grads[0].shape
    keys = kv.shape[1]
    count = keys // size
    peers = keys // (groups * rows)
    clusters = bias.shape[2]
    kv_h, bias_h = kv.at[0], bias.at[0]
    queries_all, kvt = feat.at[0, :hs], feat.at[0, hs:]
    stats = stat_ref[0]
    high, low = split_low(stats[hs : hs + 8])
    table = jnp.concatenate([high, low], axis=1)
    hots, sides, levels, deltas, pads, rights = [], [], [], [], [], []
    for group in range(groups):
        spot = slice(group * peers * rows, group * peers * rows + rows)
        hot = one_hot_t(ids_all[0, :, spot], clusters)
        queries = queries_all[:, spot]
        blank = jnp.zeros_like(queries)
        hots.append(jnp.concatenate([hot, hot], axis=0))
        sides.append(jnp.concatenate([queries, blank, hot], axis=0))
        mass = nn(table, hots[group])[0:1]
        back = (mass * grads[group][...].astype(F32)).astype(BF)
        levels.append(mix_ref[0, group, hs : hs + 1])
        deltas.append(jnp.sum(back.astype(F32) * mix_ref[0, group, :hs], axis=0, keepdims=True))
        pads.append(jnp.concatenate([blank, back], axis=0))
        turned = jnp.concatenate([queries, blank], axis=0)
        rights.append(jnp.concatenate([turned, pads[group]], axis=1).T)

    def scores(group, index):
        kv_c = piece(kv_h, index, size, 0)
        pair = jnp.concatenate([kv_c, piece(bias_h, index, size, 0)], axis=1)
        return nn(pair, sides[group]), nn(kv_c, pads[group])

    def finish(group, index, found, dq):
        weights = jnp.exp(found[0] - levels[group])
        grad_s = (weights * (found[1] - deltas[group])).astype(BF)
        part = nn(jnp.concatenate([grad_s, weights.astype(BF)], axis=1), rights[group])
        spot = spot_of(index, size)
        if group == 0:
            total[spot, :] = part
        else:
            total[spot, :] += part
        return dq + nn(piece(kvt, index, size, 1), grad_s)

    rest, mass = stats[:hs], stats[hs : hs + 1]
    level, counts = stats[hs + 1 : hs + 2], stats[hs + 2 : hs + 3]
    centroid = cen_ref[0]
    part = shares[0][0]
    for share in shares[1:]:
        part = part + share[0]
    d_rest = part[:hs].astype(BF)
    d_mass = part[hs : hs + 1] + part[hs + 1 : hs + 2]
    delta = jnp.sum(d_rest.astype(F32) * rest, axis=0, keepdims=True) + d_mass * mass
    cen_pad = jnp.concatenate([centroid, jnp.zeros_like(centroid)], axis=0)
    rest_pad = jnp.concatenate([jnp.zeros_like(centroid), d_rest], axis=0)
    right = jnp.concatenate([cen_pad, rest_pad], axis=1).T

    def cluster_step(index, summed):
        kv_c = piece(kv_h, index, size, 0)
        marks = piece(bias_h, index, size, 0).astype(F32)
        probs = jnp.exp(nn(kv_c, cen_pad) - level)
        probs = jnp.where(marks < 2.0 * NEGATIVE, 0.0, probs)
        top = marks == 0.0
        d_probs = jnp.where(top, d_mass, nn(kv_c, rest_pad))
        d_score = (probs * (d_probs - delta)).astype(BF)
        other = jnp.where(top, 0.0, probs).astype(BF)
        both[spot_of(index, size), :] = jnp.concatenate([d_score, other], axis=1)
        return summed + nn(piece(kvt, index, size, 1), d_score)

    start = jnp.zeros((2 * hs, rows), F32)
    zero = jnp.zeros((2 * hs, clusters), F32)
    member_dq = []
    if count <= 4:
        tasks = [(group, index) for group in range(groups) for index in range(count)]
        ahead = scores(*tasks[0])
        d_cen = key_sum(keys, size, cluster_step, zero)
        dq = start
        for step, (group, index) in enumerate(tasks):
            found = ahead
            if step + 1 < len(tasks):
                ahead = scores(*tasks[step + 1])
            dq = finish(group, index, found, dq)
            if index == count - 1:
                member_dq.append(dq[:hs] * 0.125)
                dq = start
    else:
        d_cen = key_sum(keys, size, cluster_step, zero)
        for group in range(groups):

            def step(index, dq, group=group):
                return finish(group, index, scores(group, index), dq)

            member_dq.append(lax.fori_loop(0, count, step, start)[:hs] * 0.125)
    d_cen = d_cen[:hs] * 0.125 / jnp.maximum(counts, 1.0)
    high, low = split_low(d_cen)
    table = jnp.concatenate([high, low], axis=1)
    for group in range(groups):
        base = group * peers * rows
        dq_ref[group] = (member_dq[group] + nn(table, hots[group])).astype(BF)
        own = total[base : base + rows, :] + nn(both[base : base + rows, :], right)
        own_ref[0, :, group * rows : (group + 1) * rows] = own.T
        for peer in range(1, peers):
            spot = (peer - 1) * groups * rows + group * rows
            found = total[base + peer * rows : base + (peer + 1) * rows, :]
            send_ref[0, :, spot : spot + rows] = found.astype(BF).T


def join_kernel(dq_ref, own_ref, *refs, groups):
    gots, outs = refs[:-groups], refs[-groups:]
    heads, _, rows = outs[0].shape
    hs = dq_ref.shape[1] // heads
    for head in range(heads):
        for group in range(groups):
            spot = slice(group * rows, (group + 1) * rows)
            pair = own_ref[head, :, spot]
            for got in gots:
                pair = pair + got[head, :, spot].astype(F32)
            outs[group][head, :hs] = dq_ref[group, head * hs : (head + 1) * hs]
            outs[group][head, hs:] = pair.astype(BF)


def block_kernel(info, *refs, groups, chunks, fast):
    (attn, rest) = (refs[:groups], refs[groups:])
    x_ref, gain_ref, shift_ref, wo_ref, up_ref, down_ref, cot_ref = rest[:7]
    out_ref, dres_ref = rest[7:9]
    if fast:
        far_ref, low_far, act_ref, low_ref = rest[9:13]
        rest = rest[13:]
        hidden = far_ref.shape[1] * 4 // 7
    else:
        dn_ref, dup_ref, dbr_ref, act_ref, low_ref = rest[9:14]
        rest = rest[14:]
    dat = rest[:groups]
    hat_ref, inv_ref, normed, back, total = rest[groups:]
    index = pl.program_id(0)

    @pl.when(index == 0)
    def before():
        resid = x_ref[...].astype(F32)
        for group in range(groups):
            owner = lax.rem(info[0] + groups - group, groups)
            resid = resid + tn(attn[group][...], wo_ref[owner])
        total[...] = resid
        centered = resid - jnp.mean(resid, axis=-1, keepdims=True)
        variance = jnp.mean(centered * centered, axis=-1, keepdims=True)
        inverse = lax.rsqrt(variance + EPSILON)
        hat = centered * inverse
        hat_ref[...] = hat
        inv_ref[...] = jnp.broadcast_to(inverse, inv_ref.shape)
        low = (hat * gain_ref[...] + shift_ref[...]).astype(BF)
        normed[...] = low
        if fast:
            feats = attn[0].shape[0]
            half = feats // 2
            turned = low.T
            for group in range(groups):
                first = turned[group * feats : group * feats + half]
                second = turned[group * feats + half : (group + 1) * feats]
                spot = slice(group * half, (group + 1) * half)
                low_ref[spot, :] = jnp.where(info[1] == 0, first, second)
                low_far[spot, :] = jnp.where(info[1] == 0, second, first)
                first = attn[group][:half]
                second = attn[group][half:]
                spot = slice((groups + group) * half, (groups + group + 1) * half)
                low_ref[spot, :] = jnp.where(info[1] == 0, first, second)
                low_far[spot, :] = jnp.where(info[1] == 0, second, first)
        else:
            low_ref[...] = low
        back[...] = jnp.zeros_like(back)

    up = nn(normed[...], up_ref[...])
    grad_act = nt(cot_ref[...], down_ref[...])
    square = up * up
    inner = GELU_A * (up + GELU_B * up * square)
    curve = jnp.tanh(inner)
    act = (0.5 * up * (1.0 + curve)).astype(BF)
    slope = 0.5 * (1.0 + curve) + 0.5 * up * (1.0 - curve * curve) * (
        GELU_A * (1.0 + 3.0 * GELU_B * square)
    )
    d_up = (grad_act * slope).astype(BF)
    if fast:
        part = act.shape[1]
        half = part // 2
        first, second = act[:, :half], act[:, half:]
        act_ref[...] = jnp.where(info[1] == 0, first, second)
        far_ref[:, pl.ds(pl.multiple_of(index * part, part), part)] = d_up
        spot = pl.ds(pl.multiple_of(hidden + index * half, half), half)
        far_ref[:, spot] = jnp.where(info[1] == 0, second, first)
    else:
        dup_ref[...] = d_up
        act_ref[...] = act
    back[...] += nt(d_up, up_ref[...])
    total[...] += nn(act, down_ref[...])

    @pl.when(index == chunks - 1)
    def after():
        out_ref[...] = total[...].astype(BF)
        d_normed = back[...]
        hat = hat_ref[...]
        gain_part = jnp.sum(d_normed * hat, axis=0, keepdims=True)
        shift_part = jnp.sum(d_normed, axis=0, keepdims=True)
        if fast:
            rows, width = low_far.shape[1], d_normed.shape[1]
            fold = []
            for part_row in split_low(gain_part) + split_low(shift_part):
                fold += [part_row[:, k : k + rows].astype(F32) for k in range(0, width, rows)]
            fold.append(jnp.zeros((low_far.shape[0] - width - len(fold), rows), F32))
            folded = jnp.concatenate(fold, axis=0).astype(BF)
            low_far[width:, :] = folded
            low_ref[width:, :] = folded
        else:
            blank = jnp.zeros((6, d_normed.shape[1]), F32)
            dn_ref[...] = jnp.concatenate([gain_part, shift_part, blank], axis=0)
        gy = d_normed * gain_ref[...]
        mean_one = jnp.mean(gy, axis=-1, keepdims=True)
        mean_two = jnp.mean(gy * hat, axis=-1, keepdims=True)
        d_resid = cot_ref[...].astype(F32) + inv_ref[:, 0:1] * (gy - mean_one - hat * mean_two)
        dres_ref[...] = d_resid
        branch = d_resid.astype(BF)
        if fast:
            far_ref[:, hidden * 3 // 2 :] = branch
        else:
            dbr_ref[...] = branch
        for group in range(groups):
            owner = lax.rem(info[0] + groups - group, groups)
            dat[group][...] = nt(wo_ref[owner], branch).astype(BF)


def weights_kernel(info, *refs, groups):
    (dup, dup_got, dbr, dbr_got, act, act_got, low, low_got, cot, cot_got) = refs[:10]
    send_u, keep_u, send_d, keep_d, outs = refs[10:]
    width = cot.shape[1]
    index = pl.program_id(0)
    group_at, place_u, place_d = info[0], info[3], info[4]
    rows = width // (2 * groups)
    quarter = rows // 4
    stay = groups * rows

    @pl.when(index == 0)
    def first():
        found = nn(low[stay:width, :], dbr[...]) + nn(low_got[stay:width, :], dbr_got[...])
        fold = low[width:, :].astype(F32) + low_got[width:, :].astype(F32)
        times = width // fold.shape[1]
        norms = []
        for part in range(2):
            both = fold[2 * part * times : (2 * part + 1) * times]
            both = both + fold[(2 * part + 1) * times : (2 * part + 2) * times]
            norms.append(jnp.concatenate([both[k : k + 1] for k in range(times)], axis=1))
        norms = jnp.concatenate(norms + [jnp.zeros((6, width), F32)], axis=0)
        for group in range(groups):
            block = found[group * rows : (group + 1) * rows]
            outs[group] = block
            for part in range(4):
                tail = block[part * quarter + 16 : (part + 1) * quarter]
                tail = jnp.concatenate([tail, norms], axis=0).astype(BF)
                place = lax.bitwise_xor(part, place_d)

                @pl.when(place >= 2)
                def leaves_more():
                    send_d[place - 2, (groups - group) % groups, rows:] = tail

                @pl.when(place < 2)
                def stays_more():
                    keep_d[place, (groups - group) % groups, rows:] = tail

    up = nn(low[:stay, :], dup[...]) + nn(low_got[:stay, :], dup_got[...])
    at = lax.bitwise_xor(lax.bitwise_xor(index, 2), place_u)
    for group in range(groups):
        spot = lax.rem(group + groups - group_at, groups)
        block = up[group * rows : (group + 1) * rows].astype(BF)
        away = (groups - group) % groups
        start = pl.multiple_of(at * quarter, 8)
        other = outs[group, pl.ds(start, 16), :].astype(BF)

        @pl.when(index < 2)
        def leaves():
            send_u[0, spot, :rows] = block
            send_u[0, away, rows:] = other

        @pl.when(index >= 2)
        def stays():
            keep_u[0, spot, :rows] = block
            keep_u[0, away, rows:] = other

    down = tn(act[...], cot[...]) + tn(act_got[...], cot_got[...])
    spot = lax.rem(index + groups - group_at, groups)
    for part in range(4):
        block = down[part * rows : (part + 1) * rows].astype(BF)
        place = lax.bitwise_xor(part, place_d)

        @pl.when(place >= 2)
        def leaves_down():
            send_d[place - 2, spot, :rows] = block

        @pl.when(place < 2)
        def stays_down():
            keep_d[place, spot, :rows] = block


def second_kernel(keep_u, got_u, keep_d, got_d, inner, inner_got, to_y, to_x, to_xy):
    rows = keep_u.shape[2]
    to_y[:, :rows] = (keep_u[0].astype(F32) + got_u[0].astype(F32)).astype(BF)
    to_x[:, :rows] = (keep_d[0].astype(F32) + got_d[0].astype(F32)).astype(BF)
    to_y[:, rows:] = (inner[1].astype(F32) + inner_got[1].astype(F32)).astype(BF)
    to_x[:, rows:] = (inner[2].astype(F32) + inner_got[2].astype(F32)).astype(BF)
    to_xy[...] = (inner[3].astype(F32) + inner_got[3].astype(F32)).astype(BF)


def third_kernel(keep_u, got_u, keep_d, got_d, inner, inner_got, by_y, by_x, by_xy, *outs):
    rows = keep_u.shape[2]
    for group in range(len(outs)):
        up = keep_u[0, group].astype(F32) + got_u[0, group].astype(F32)
        down = keep_d[0, group].astype(F32) + got_d[0, group].astype(F32)
        both = inner[0, group].astype(F32) + inner_got[0, group].astype(F32)
        outs[group][:rows] = (up + by_y[group, :rows].astype(F32)).astype(BF)
        outs[group][rows : 2 * rows] = (down + by_x[group, :rows].astype(F32)).astype(BF)
        both = both + by_y[group, rows:].astype(F32) + by_x[group, rows:].astype(F32)
        outs[group][2 * rows :] = (both + by_xy[group].astype(F32)).astype(BF)


def fourth_kernel(info, *refs, groups, high, feats):
    parts, out, turned = refs[:groups], refs[groups], refs[groups + 1]
    total = parts[0][: 2 * high].astype(F32)
    for part in parts[1:]:
        total = total + part[: 2 * high].astype(F32)
    out[: 2 * high] = total.astype(BF)
    third = feats // 3
    lines = turned.shape[1]
    for group in range(groups):
        turned[group] = parts[group][2 * high :].astype(F32)
    for kind in range(3):
        found = []
        for owner in range(groups):
            spot = lax.rem(info[0] + groups - owner, groups)
            found.append(turned[spot, :, kind * third : (kind + 1) * third])
        at = 2 * high + kind * lines
        out[at : at + lines] = jnp.concatenate(found, axis=1).astype(BF)


def spread_kernel(
    info, own, from_x, from_y, from_xy, wq, wkv, pair,
    up_ref, out_ref, down_ref, norm_ref, gq_ref, gkv_ref, vec_ref, sums, *, high,
):
    index = pl.program_id(0)
    rows, width = down_ref.shape
    quarter = rows // 4
    lines = quarter + 8
    order_u = (own, from_y, from_x, from_xy)
    order_d = (own, from_x, from_y, from_xy)

    @pl.when(index == 0)
    def first():
        for place, part in enumerate(order_u):

            @pl.when(info[3] == place)
            def take(part=part):
                for kind in range(3):
                    at = 2 * high + kind * lines
                    sums[kind] = part[at : at + lines].astype(F32)[quarter:]

    for place, part in enumerate(order_u):

        @pl.when(index == place)
        def upper(part=part):
            up_ref[...] = part[:rows].astype(F32)
            at = pl.multiple_of(lax.bitwise_xor(index, info[3]) * quarter, 8)
            out_ref[pl.ds(at, 16), :] = part[rows:high].astype(F32)
            spot = pl.ds(at, quarter)
            shift, gain = pair[spot, 0:1], pair[spot, 1:2]
            gain_sum, shift_sum = 0.0, 0.0
            for kind in range(3):
                base = 2 * high + kind * lines
                block = part[base : base + lines].astype(F32)[:quarter]
                line = sums[kind, 0:1]
                if kind == 0:
                    weight = wq[spot, :]
                    gq_ref[spot, :] = block + shift * line
                else:
                    lanes = slice((kind - 1) * width, kind * width)
                    weight = wkv[spot, lanes]
                    gkv_ref[spot, lanes] = block + shift * line
                gain_sum = gain_sum + jnp.sum(weight * block, axis=1, keepdims=True)
                shift_sum = shift_sum + jnp.sum(weight * line, axis=1, keepdims=True)
            lane = lax.broadcasted_iota(jnp.int32, (quarter, vec_ref.shape[1]), 1)
            vec_ref[spot, :] = jnp.where(lane == 0, gain_sum / gain, shift_sum)

    for place, part in enumerate(order_d):

        @pl.when(index == place)
        def lower(part=part):
            down_ref[...] = part[high : high + rows].astype(F32)
            tail = part[high + rows : 2 * high].astype(F32)
            at = pl.multiple_of(lax.bitwise_xor(index, info[4]) * quarter + 16, 8)
            out_ref[pl.ds(at, quarter - 16), :] = tail[: quarter - 16]

            @pl.when(lax.bitwise_xor(index, info[4]) == 0)
            def norms():
                norm_ref[...] = tail[quarter - 16 :]


def inward_kernel(info, *refs, groups, gots, fast):
    join_refs, hat_ref = refs[: 2 + gots], refs[2 + gots]
    parts = refs[3 + gots : 3 + gots + groups]
    outs = refs[3 + gots + groups :]
    join_kernel(*join_refs, *parts, groups=groups)
    heads, triple, rows = parts[0].shape
    hs = triple // 3
    total, sums = None, None
    ones = jnp.ones((16, rows), BF)
    for group in range(groups):
        order = [parts[group][h, k * hs : (k + 1) * hs] for k in range(3) for h in range(heads)]
        turned = jnp.concatenate(order, axis=0)
        found = nt(hat_ref[:, group * rows : (group + 1) * rows], turned)
        more = nt(ones, turned)
        total = found if total is None else total + found
        sums = more if sums is None else sums + more
    if not fast:
        outs[0][...] = total
        outs[1][...] = sums
        return
    own_ref, far_ref = outs
    block = total.shape[0] // (2 * groups)
    quarter = block // 4
    wide = total.shape[1]
    edge = wide // 128 * 128
    blank = jnp.zeros(own_ref.shape[:3] + (own_ref.shape[3] - edge,), BF)
    own_ref[..., edge:] = blank
    far_ref[..., edge:] = blank
    for group in range(groups):
        spot = lax.rem(group + groups - info[0], groups)
        for part in range(4):
            place = lax.bitwise_xor(part, info[3])
            found = []
            for parity in range(2):
                at = (2 * group + parity) * block + part * quarter
                lines = jnp.concatenate([total[at : at + quarter], sums[:8]], axis=0)
                found.append(lines.astype(BF))
            own_ref[place, spot, :, :wide] = jnp.where(info[1] == 0, found[0], found[1])
            far_ref[place, spot, :, :wide] = jnp.where(info[1] == 0, found[1], found[0])


def final_kernel(info, *refs, groups):
    parts = refs[:groups]
    x_ref, dres_ref, gain_ref, w_ref, out_ref = refs[groups:]
    d_normed = jnp.zeros(dres_ref.shape, F32)
    for group in range(groups):
        owner = lax.rem(info[0] + groups - group, groups)
        heads, triple, rows = parts[group].shape
        d_normed = d_normed + tn(parts[group][...].reshape(heads * triple, rows), w_ref[owner])
    values = x_ref[...].astype(F32)
    centered = values - jnp.mean(values, axis=-1, keepdims=True)
    variance = jnp.mean(centered * centered, axis=-1, keepdims=True)
    inverse = lax.rsqrt(variance + EPSILON)
    hat = centered * inverse
    gy = d_normed * gain_ref[...]
    mean_one = jnp.mean(gy, axis=-1, keepdims=True)
    mean_two = jnp.mean(gy * hat, axis=-1, keepdims=True)
    out_ref[...] = (dres_ref[...] + inverse * (gy - mean_one - hat * mean_two)).astype(BF)


def whole(shape):
    return pl.BlockSpec(shape, lambda *at: (0,) * len(shape))


def per_device(
    tokens,
    cluster_ids,
    lengths,
    top_keys,
    gain_one,
    shift_one,
    w_query,
    w_keyval,
    w_out,
    gain_two,
    shift_two,
    w_up,
    w_down,
    cotangent,
):
    rows, width = tokens.shape
    heads = cluster_ids.shape[1]
    hs = width // heads
    hidden = w_up.shape[1]
    wide = lax.axis_size("wide")
    n_dp = lax.axis_size("dp")
    groups = math.gcd(heads, wide)
    peers = wide // groups
    own_heads = heads // groups
    own_clusters = top_keys.shape[2]
    clusters = own_clusters * wide
    picks = top_keys.shape[3]
    seq = rows * wide
    size = 512 if seq <= 2048 else 2048
    feats = own_heads * hs
    block_rows = width // wide
    fast = peers == 2 and n_dp == 4 and block_rows == 96 and hidden == 4 * width and width % 256 == 0 and rows % 128 == 0
    me = lax.axis_index("wide")
    group_at, peer_at = me // peers, me % peers
    dp_at = lax.axis_index("dp")
    seq_len = lengths[0]
    bit_x, bit_y = dp_at % 2, (dp_at // 2) % 2
    place_u, place_d = 2 * bit_x + bit_y, 2 * bit_y + bit_x
    info = jnp.stack([group_at, peer_at, seq_len, place_u, place_d, me]).astype(jnp.int32)

    def along_groups(values, hop):
        pairs = [(i, ((i // peers + hop) % groups) * peers + i % peers) for i in range(wide)]
        return lax.ppermute(values, "wide", pairs)

    def along_peers(values, hop):
        pairs = [(i, (i // peers) * peers + (i % peers + hop) % peers) for i in range(wide)]
        return lax.ppermute(values, "wide", pairs)

    def along_dp(values, mask):
        return lax.ppermute(values, "dp", [(i, i ^ mask) for i in range(n_dp)])

    def prefetched(kernel, grid, in_specs, out_specs, out_shape, mib, spent, name, scratch=(), alias=None):
        return pl.pallas_call(
            kernel,
            grid_spec=pltpu.PrefetchScalarGridSpec(
                num_scalar_prefetch=1,
                grid=grid,
                in_specs=in_specs,
                out_specs=out_specs,
                scratch_shapes=list(scratch),
            ),
            out_shape=out_shape,
            compiler_params=params(mib, len(grid)),
            cost_estimate=spent,
            input_output_aliases=alias or {},
            name=name,
        )

    def after(values, *others):
        return lax.optimization_barrier((values, others))[0]

    def array(shape, dtype):
        return jax.ShapeDtypeStruct(shape, dtype)

    position = me * rows + jnp.arange(rows, dtype=jnp.int32)
    marked = jnp.where((position < seq_len)[:, None], cluster_ids, -1).T
    tops = jnp.zeros((heads, picks, clusters), jnp.int32)
    tops = lax.dynamic_update_slice(
        tops, top_keys[0].transpose(0, 2, 1), (0, 0, me * own_clusters)
    )
    lines = rows // clusters
    packed = jnp.concatenate([tops, marked.reshape(heads, lines, clusters)], axis=1)
    early = [along_peers(tokens, -hop) for hop in range(1, peers)]
    packed = after(packed.reshape(groups, own_heads, picks + lines, clusters), early)

    def of_heads(hop):
        return lax.dynamic_index_in_dim(packed, (group_at + groups - hop) % groups, keepdims=False)

    arrived = [of_heads(0)] + [along_groups(of_heads(hop), -hop) for hop in range(1, groups)]

    mine = {0: tokens, 1: along_groups(tokens, -1)}
    if groups > 2:
        mine[groups - 1] = along_groups(tokens, 1)
    ready = after(tokens, arrived)
    for hop in range(2, groups - 1):
        mine[hop] = along_groups(ready, -hop)

    w_in = jnp.concatenate([w_query, w_keyval], axis=1).T.reshape(3, heads, hs, width)
    w_in = w_in.transpose(1, 0, 2, 3).reshape(groups, 3 * feats, width)
    table_shape = (own_heads, picks + groups * lines, clusters)
    table = pl.pallas_call(
        functools.partial(table_kernel, picks=picks),
        grid=(1,),
        in_specs=[whole((own_heads, picks + lines, clusters))] * groups,
        out_specs=whole(table_shape),
        out_shape=array(table_shape, jnp.int32),
        compiler_params=params(8, 1),
        cost_estimate=cost(1e5, 1e6),
        name="table",
    )(*after(arrived, w_in))
    tables = [table] + [along_peers(table, -hop) for hop in range(1, peers)]
    cot_got = [along_peers(after(cotangent, arrived), hop) for hop in range(1, peers)]
    cot_got = cot_got if fast else []
    bias, ids_all = prefetched(
        functools.partial(bias_kernel, groups=groups, peers=peers, rows=rows, picks=picks),
        (wide,),
        [whole(table_shape)] * peers,
        [
            pl.BlockSpec((own_heads, rows, clusters), lambda i, s: (0, i, 0)),
            whole((own_heads, 1, seq)),
        ],
        [array((own_heads, seq, clusters), BF), array((own_heads, 1, seq), jnp.int32)],
        12 if fast else 60,
        cost(own_heads * seq * clusters * picks * 8, own_heads * seq * clusters * 2),
        "bias",
    )(info, *tables)

    gain_row, shift_row = gain_one[None, :], shift_one[None, :]
    shapes = [
        array((width, groups * rows), BF),
        array((own_heads, 3 * hs, seq), BF),
        array((own_heads, seq, 2 * hs), BF),
    ]
    held = []
    split_peers = peers if peers <= 2 else 1
    for group in sorted(range(groups), key=lambda g: min(g, groups - g)):
        arrival = mine[group]
        if group == 1:
            arrival = after(arrival, bias, held, cot_got, [mine[hop] for hop in range(2, groups)])
        chunk = [arrival]
        chunk += early if group == 0 else [along_peers(arrival, -hop) for hop in range(1, peers)]
        if peers > 2:
            chunk = [jnp.concatenate(chunk, axis=0)]
        span = peers * rows
        if peers > 2:
            specs_in = [pl.BlockSpec((rows, width), lambda p, s: (p, 0))]
            grid = (peers,)
            outs = [
                pl.BlockSpec((width, rows), lambda p, s, g=group: (0, g)),
                pl.BlockSpec((own_heads, 3 * hs, rows), lambda p, s, g=group: (0, 0, g * peers + p)),
                pl.BlockSpec((own_heads, rows, 2 * hs), lambda p, s, g=group: (0, g * peers + p, 0)),
            ]
        else:
            specs_in = [whole((rows, width))] * split_peers
            grid = (1,)
            outs = [
                pl.BlockSpec((width, rows), lambda p, s, g=group: (0, g)),
                pl.BlockSpec((own_heads, 3 * hs, span), lambda p, s, g=group: (0, 0, g)),
                pl.BlockSpec((own_heads, span, 2 * hs), lambda p, s, g=group: (0, g, 0)),
            ]
        first = 1 + split_peers + 3
        held = prefetched(
            functools.partial(project_kernel, peers=split_peers, olds=len(held)),
            grid,
            specs_in
            + [
                whole((1, width)),
                whole((1, width)),
                pl.BlockSpec((1, 3 * feats, width), lambda p, s: (s[0], 0, 0)),
            ]
            + [pl.BlockSpec(memory_space=pl.ANY)] * len(held),
            outs,
            shapes,
            16 if fast else 60,
            cost(6 * span * width * feats, span * width * 4),
            "project",
            alias={first + k: k for k in range(len(held))},
        )(info, *chunk, gain_row, shift_row, w_in, *held)
    hat_own, feat, kv = held

    ids_full = pl.BlockSpec((1, 1, seq), lambda h, r: (h, 0, 0))
    feat_full = pl.BlockSpec((1, 3 * hs, seq), lambda h, r: (h, 0, 0))
    kv_full = pl.BlockSpec((1, seq, 2 * hs), lambda h, r: (h, 0, 0))
    bias_full = pl.BlockSpec((1, seq, clusters), lambda h, r: (h, 0, 0))
    head_rows = pl.BlockSpec((hs, rows), lambda h, r: (h, 0))
    mix_spec = pl.BlockSpec((1, 1, hs + 8, rows), lambda h, r: (h, r, 0, 0))
    stat_spec = pl.BlockSpec((1, hs + 8, clusters), lambda h, r: (h, 0, 0))
    cen_spec = pl.BlockSpec((1, hs, clusters), lambda h, r: (h, 0, 0))
    own_rows = groups * rows
    pair_flops = own_heads * own_rows * seq * 256

    one = [
        pl.BlockSpec(spec.block_shape, functools.partial(lambda h, f: f(h, 0), f=spec.index_map))
        for spec in (ids_full, feat_full, kv_full, bias_full, stat_spec, cen_spec, head_rows)
    ]
    ids_one, feat_one, kv_one, bias_one, stat_one, cen_one, rows_one = one
    part_one = pl.BlockSpec((1, hs + 16, clusters), lambda h: (h, 0, 0))
    mix_one = pl.BlockSpec((1, groups, hs + 8, rows), lambda h: (h, 0, 0, 0))
    all_groups = pl.BlockSpec((groups, hs, rows), lambda h: (0, h, 0))
    own_one = pl.BlockSpec((1, own_rows, 2 * hs), lambda h: (h, 0, 0))
    results = pl.pallas_call(
        functools.partial(forward_kernel, size=size, groups=groups, rows=rows),
        grid=(own_heads,),
        in_specs=[ids_one, feat_one, kv_one, bias_one],
        out_specs=[rows_one] * groups + [mix_one, stat_one, cen_one],
        out_shape=[array((feats, rows), BF)] * groups
        + [
            array((own_heads, groups, hs + 8, rows), F32),
            array((own_heads, hs + 8, clusters), F32),
            array((own_heads, hs, clusters), BF),
        ],
        compiler_params=params(32 if fast else 60, 1),
        cost_estimate=cost(6 * pair_flops, 8e6, own_heads * own_rows * seq),
        name="attend",
    )(ids_all, feat, kv, bias)
    attn_t = results[:groups]
    mixed, stats, centroid = results[groups:]

    arrived = [attn_t[0]] + [along_groups(attn_t[hop], hop) for hop in range(1, groups)]

    chunks = 4
    part = hidden // chunks
    w_out_g = w_out.reshape(groups, feats, width)
    gain_row2, shift_row2 = gain_two[None, :], shift_two[None, :]
    square = whole((rows, width))
    column = pl.BlockSpec((rows, part), lambda i, s: (0, i))
    norm_spec = whole((8, width))
    if fast:
        kept_shapes = [
            array((rows, hidden + hidden // 2 + width), BF),
            array((width + 16, rows), BF),
            array((rows, hidden // 2), BF),
            array((width + 16, rows), BF),
        ]
        kept_specs = [whole(item.shape) for item in kept_shapes]
        kept_specs[2] = pl.BlockSpec((rows, part // 2), lambda i, s: (0, i))
    else:
        kept_shapes = [
            array((8, width), F32),
            array((rows, hidden), BF),
            array((rows, width), BF),
            array((rows, hidden), BF),
            array((rows, width), BF),
        ]
        kept_specs = [norm_spec, column, square, column, square]
    results = prefetched(
        functools.partial(block_kernel, groups=groups, chunks=chunks, fast=fast),
        (chunks,),
        [whole((feats, rows))] * groups
        + [
            square,
            whole((1, width)),
            whole((1, width)),
            whole((groups, feats, width)),
            pl.BlockSpec((width, part), lambda i, s: (0, i)),
            pl.BlockSpec((part, width), lambda i, s: (i, 0)),
            square,
        ],
        [square, square] + kept_specs + [whole((feats, rows))] * groups,
        [array((rows, width), BF), array((rows, width), F32)]
        + kept_shapes
        + [array((feats, rows), BF)] * groups,
        28 if fast else 60,
        cost(8 * rows * width * hidden, 4 * width * hidden, rows * hidden),
        "feed",
        scratch=[
            pltpu.VMEM((rows, width), F32),
            pltpu.VMEM((rows, 128), F32),
            pltpu.VMEM((rows, width), BF),
            pltpu.VMEM((rows, width), F32),
            pltpu.VMEM((rows, width), F32),
        ],
    )(info, *arrived, tokens, gain_row2, shift_row2, w_out_g, w_up, w_down, cotangent)
    output, d_resid = results[:2]
    kept, d_attn = results[2:-groups], results[-groups:]
    grads = [d_attn[0]] + [along_groups(d_attn[hop], -hop) for hop in range(1, groups)]

    def weight_parts():
        far, low_far, act_own, low_own = kept
        got, low_got = along_peers(far, 1), along_peers(low_far, 1)
        high = block_rows + 16
        chunk = pl.BlockSpec((rows, part), lambda i, s: (0, i ^ 2 ^ s[3]))
        branch = pl.BlockSpec((rows, width), lambda i, s: (0, hidden * 3 // 2 // width))
        act_spec = pl.BlockSpec((rows, part // 2), lambda i, s: (0, i))
        act_there = pl.BlockSpec((rows, part // 2), lambda i, s: (0, 2 * hidden // part + i))
        low_spec = whole((width + 16, rows))
        shape_u = (2, groups, high, width)
        shape_d = (2, groups, high, width)
        send_u, keep_u, send_d, keep_d = prefetched(
            functools.partial(weights_kernel, groups=groups),
            (4,),
            [chunk, chunk, branch, branch, act_spec, act_there, low_spec, low_spec, square, square],
            [
                pl.BlockSpec((1,) + shape_u[1:], lambda i, s: (jnp.minimum(i, 1), 0, 0, 0)),
                pl.BlockSpec((1,) + shape_u[1:], lambda i, s: (jnp.maximum(i - 2, 0), 0, 0, 0)),
                whole(shape_d),
                whole(shape_d),
            ],
            [array(shape_u, BF), array(shape_u, BF), array(shape_d, BF), array(shape_d, BF)],
            28,
            cost(8 * rows * width * hidden, 6 * width * hidden),
            "weights",
            scratch=[pltpu.VMEM((groups, block_rows, width), F32)],
        )(info, far, got, far, got, act_own, got, low_own, low_got, cotangent, *cot_got)
        return send_u, keep_u, send_d, keep_d

    def weight_second(keep_u, got_u, keep_d, got_d, inner, inner_got):
        def block(shape, at):
            return pl.BlockSpec((1,) + shape[1:], lambda i: (at, 0, 0, 0))

        shape_u = keep_u.shape
        lines = inner.shape[2]
        shape = (groups, shape_u[2] + lines, width)
        small = (groups, lines, width)
        return pl.pallas_call(
            second_kernel,
            grid=(1,),
            in_specs=[block(shape_u, 1)] * 4 + [whole(inner.shape)] * 2,
            out_specs=[whole(shape), whole(shape), whole(small)],
            out_shape=[array(shape, BF), array(shape, BF), array(small, BF)],
            compiler_params=params(20, 1),
            cost_estimate=cost(groups * shape[1] * width * 2, groups * shape[1] * width * 12),
            name="second",
        )(keep_u, got_u, keep_d, got_d, inner, inner_got)

    def weight_third(keep_u, got_u, keep_d, got_d, inner, inner_got, by_y, by_x, by_xy):
        def block(shape, at):
            return pl.BlockSpec((1,) + shape[1:], lambda i: (at, 0, 0, 0))

        high = keep_u.shape[2]
        tall = 2 * high + inner.shape[2]
        sums = pl.pallas_call(
            third_kernel,
            grid=(1,),
            in_specs=[block(keep_u.shape, 0)] * 4
            + [block(inner.shape, 0)] * 2
            + [whole(by_y.shape), whole(by_x.shape), whole(by_xy.shape)],
            out_specs=[whole((tall, width))] * groups,
            out_shape=[array((tall, width), BF)] * groups,
            compiler_params=params(24, 1),
            cost_estimate=cost(groups * tall * width * 4, groups * tall * width * 8),
            name="third",
        )(keep_u, got_u, keep_d, got_d, inner, inner_got, by_y, by_x, by_xy)
        return [sums[0]] + [along_groups(sums[hop], hop) for hop in range(1, groups)]

    def weight_sums(came, high, lines):
        tall = 2 * high + 3 * lines
        done = prefetched(
            functools.partial(fourth_kernel, groups=groups, high=high, feats=3 * feats),
            (1,),
            [whole(came[0].shape)] * groups,
            whole((tall, width)),
            array((tall, width), BF),
            16,
            cost(groups * tall * width, groups * tall * width * 2),
            "fourth",
            scratch=[pltpu.VMEM((groups, lines, width), F32)],
        )(info, *came)
        from_x, from_y, from_xy = (along_dp(done, mask) for mask in (1, 2, 3))
        at = me * block_rows
        wq_rows = lax.dynamic_slice_in_dim(w_query, at, block_rows).astype(F32)
        wkv_rows = lax.dynamic_slice_in_dim(w_keyval, at, block_rows).astype(F32)
        pair = jnp.stack([shift_one, gain_one] + [shift_one] * 6, axis=1)
        pair = lax.dynamic_slice_in_dim(pair, at, block_rows)
        pair, wq_rows, wkv_rows = after((pair, wq_rows, wkv_rows), came[0])
        found = prefetched(
            functools.partial(spread_kernel, high=high),
            (4,),
            [whole((tall, width))] * 4
            + [whole(wq_rows.shape), whole(wkv_rows.shape), whole(pair.shape)],
            [
                pl.BlockSpec((block_rows, part), lambda i, s: (0, i ^ s[3])),
                whole((block_rows, width)),
                pl.BlockSpec((block_rows, width), lambda i, s: (i ^ s[4], 0)),
                whole((8, width)),
                whole((block_rows, width)),
                whole((block_rows, 2 * width)),
                whole((block_rows, 128)),
            ],
            [
                array((block_rows, hidden), F32),
                array((block_rows, width), F32),
                array((hidden // wide, width), F32),
                array((8, width), F32),
                array((block_rows, width), F32),
                array((block_rows, 2 * width), F32),
                array((block_rows, 128), F32),
            ],
            20,
            cost(1e6, 4 * tall * width * 6),
            "spread",
            scratch=[pltpu.VMEM((3, 8, width), F32)],
        )(info, done, from_x, from_y, from_xy, wq_rows, wkv_rows, pair)
        return done, found

    masks = [1 << k for k in range(n_dp.bit_length() - 1)]

    def reduce_rows(partial):
        blocks = partial.reshape(groups, peers, partial.shape[0] // wide, partial.shape[1])

        def of_peer(hop):
            at = (peer_at + hop) % peers
            return lax.dynamic_index_in_dim(blocks, at, axis=1, keepdims=False)

        total = of_peer(0).astype(F32)
        for hop in range(1, peers):
            total = total + along_peers(of_peer(hop), hop).astype(F32)
        total = total.astype(BF)

        def of_group(hop):
            return lax.dynamic_index_in_dim(total, (group_at + hop) % groups, keepdims=False)

        done = of_group(0).astype(F32)
        for hop in range(1, groups):
            done = done + along_groups(of_group(hop), hop).astype(F32)
        for mask in masks:
            done = done.astype(BF)
            done = done.astype(F32) + along_dp(done, mask).astype(F32)
        return done

    if fast:
        send_u, keep_u, send_d, keep_d = weight_parts()
        got_u, got_d = along_dp(send_u, 1), along_dp(send_d, 2)
        grads = after(grads, keep_u)
    else:
        norm_two, d_up, d_branch, act, normed_two = kept
        total_up = reduce_rows(tn(normed_two, d_up).astype(BF))
        total_down = reduce_rows(tn(act, cotangent).astype(BF))
        found = jnp.stack([nn(item, d_branch).astype(BF) for item in arrived])
        found = [
            lax.dynamic_index_in_dim(found, (group_at + groups - g) % groups, keepdims=False)
            for g in range(groups)
        ]
        total_out = reduce_rows(jnp.concatenate(found, axis=0))
        norm_own = reduce_rows(norm_two[:2].T.astype(BF)).T

    share = pl.pallas_call(
        functools.partial(sums_kernel, groups=groups),
        grid=(own_heads,),
        in_specs=[ids_one]
        + [rows_one] * groups
        + [mix_one],
        out_specs=part_one,
        out_shape=array((own_heads, hs + 16, clusters), F32),
        compiler_params=params(16 if fast else 60, 1),
        cost_estimate=cost(own_heads * own_rows * clusters * 160, 2e6),
        name="sums",
    )(ids_all, *grads, mixed)
    share_got = [along_peers(share, hop) for hop in range(1, peers)]

    back_shapes = [
        array((groups, feats, rows), BF),
        array((own_heads, 2 * hs, own_rows), F32),
        array((own_heads, 2 * hs, max(peers - 1, 1) * own_rows), BF),
    ]
    dq, dkv_own, dkv_send = pl.pallas_call(
        functools.partial(back_kernel, size=size, groups=groups, gots=len(share_got)),
        grid=(own_heads,),
        in_specs=[ids_one, feat_one, kv_one, bias_one]
        + [rows_one] * groups
        + [mix_one, stat_one, cen_one]
        + [part_one] * (1 + len(share_got)),
        out_specs=[
            all_groups,
            pl.BlockSpec((1,) + back_shapes[1].shape[1:], lambda h: (h, 0, 0)),
            pl.BlockSpec((1,) + back_shapes[2].shape[1:], lambda h: (h, 0, 0)),
        ],
        out_shape=back_shapes,
        scratch_shapes=[pltpu.VMEM((seq, 2 * hs), F32), pltpu.VMEM((seq, 2 * clusters), BF)],
        compiler_params=params(36 if fast else 62, 1),
        cost_estimate=cost(14 * pair_flops, 10e6, own_heads * own_rows * seq),
        name="back",
    )(ids_all, feat, kv, bias, *grads, mixed, stats, centroid, share, *share_got)
    dkv_got = [
        along_peers(
            dkv_send if peers == 2 else dkv_send[..., (hop - 1) * own_rows : hop * own_rows], hop
        )
        for hop in range(1, peers)
    ]
    tall = block_rows + 16
    spent = cost(2 * own_rows * width * 3 * feats, 4e6)
    if fast:
        lines = block_rows // 4 + 8
        more = [array((4, groups, lines, width), BF)] * 2
    else:
        more = [array((width, 3 * feats), F32), array((16, 3 * feats), F32)]
    if fast:
        dkv_own = after(dkv_own, got_u, got_d)
    results = prefetched(
        functools.partial(inward_kernel, groups=groups, gots=len(dkv_got), fast=fast),
        (1,),
        [whole(back_shapes[0].shape)]
        + [whole(back_shapes[1].shape)] * (1 + len(dkv_got))
        + [whole((width, own_rows))],
        [whole((own_heads, 3 * hs, rows))] * groups + [whole(item.shape) for item in more],
        [array((own_heads, 3 * hs, rows), BF)] * groups + more,
        28 if fast else 60,
        spent,
        "inward",
    )(info, dq, dkv_own, *dkv_got, hat_own)
    d_in, more = results[:groups], results[groups:]
    home = [d_in[0]] + [along_groups(d_in[hop], hop) for hop in range(1, groups)]

    if fast:
        keep, far = more
        inner_got = along_peers(far, 1)
        got_u, got_d = after((got_u, got_d), home[1])
        to_y, to_x, to_xy = weight_second(keep_u, got_u, keep_d, got_d, keep, inner_got)
        by_y, by_x, by_xy = along_dp(to_y, 2), along_dp(to_x, 1), along_dp(to_xy, 3)
        by_y, by_x = after((by_y, by_x), home)
        came = weight_third(
            keep_u, got_u, keep_d, got_d, keep, inner_got, by_y, by_x, by_xy
        )
        done, found = weight_sums(came, keep_u.shape[2], lines)
        home = after(home, done)
        total_up, total_out, total_down, norms, total_query, total_keyval, vector = found
        norm_own = lax.dynamic_slice_in_dim(norms, me * block_rows, block_rows, axis=1)
        gain_grad, shift_grad = vector[:, 0], vector[:, 1]
    else:
        found, more = more
        found = found.reshape(groups, peers, block_rows, 3 * feats)
        more = jnp.broadcast_to(more, (groups, peers, 16, 3 * feats))
        found = jnp.concatenate([found, more], axis=2).astype(BF)

        def of_peer(hop):
            at = (peer_at + hop) % peers
            return lax.dynamic_index_in_dim(found, at, axis=1, keepdims=False)

        total = of_peer(0).astype(F32)
        for hop in range(1, peers):
            total = total + along_peers(of_peer(hop), hop).astype(F32)
        for mask in masks:
            total = total.astype(BF)
            total = total.astype(F32) + along_dp(total, mask).astype(F32)
        total = total.astype(BF)
        items = [
            lax.dynamic_index_in_dim(total, (group_at + hop) % groups, keepdims=False)
            for hop in range(groups)
        ]
        pieces = [items[0]] + [along_groups(items[hop], hop) for hop in range(1, groups)]
        pieces = jnp.stack(pieces)
        pieces = jnp.stack(
            [
                lax.dynamic_index_in_dim(pieces, (group_at + groups - g) % groups, keepdims=False)
                for g in range(groups)
            ]
        ).astype(F32)
        q_part = pieces[:, :, :feats].transpose(1, 0, 2).reshape(tall, width)
        kv_part = (
            pieces[:, :, feats:]
            .reshape(groups, tall, 2, feats)
            .transpose(1, 2, 0, 3)
            .reshape(tall, 2 * width)
        )
        at = me * block_rows
        wq_rows = lax.dynamic_slice_in_dim(w_query, at, block_rows).astype(F32)
        wkv_rows = lax.dynamic_slice_in_dim(w_keyval, at, block_rows).astype(F32)
        gain_own = lax.dynamic_slice_in_dim(gain_one, at, block_rows)
        shift_own = lax.dynamic_slice_in_dim(shift_one, at, block_rows)
        q_sum, kv_sum = q_part[block_rows], kv_part[block_rows]
        q_part, kv_part = q_part[:block_rows], kv_part[:block_rows]
        shift_grad = jnp.sum(wq_rows * q_sum, axis=1) + jnp.sum(wkv_rows * kv_sum, axis=1)
        along = jnp.sum(wq_rows * q_part, axis=1) + jnp.sum(wkv_rows * kv_part, axis=1)
        total_query = q_part + shift_own[:, None] * q_sum
        total_keyval = kv_part + shift_own[:, None] * kv_sum
        gain_grad = along / gain_own

    grad_tokens = prefetched(
        functools.partial(final_kernel, groups=groups),
        (1,),
        [whole((own_heads, 3 * hs, rows))] * groups
        + [square, square, whole((1, width)), whole((groups, 3 * feats, width))],
        square,
        array((rows, width), BF),
        24 if fast else 60,
        cost(6 * rows * width * width, 6 * width * width),
        "final",
    )(info, *home, tokens, d_resid, gain_row, w_in)

    return (
        output,
        grad_tokens,
        total_query,
        total_keyval,
        total_out,
        total_up,
        total_down,
        gain_grad,
        shift_grad,
        norm_own[0],
        norm_own[1],
    )


def solution(mesh):
    return jax.shard_map(
        per_device,
        mesh=mesh,
        in_specs=(
            P(("dp", "wide"), None),
            P(("dp", "wide"), None),
            P("dp"),
            P("dp", None, "wide", None),
            P(),
            P(),
            P(),
            P(),
            P(),
            P(),
            P(),
            P(),
            P(),
            P(("dp", "wide"), None),
        ),
        out_specs=(
            P(("dp", "wide"), None),
            P(("dp", "wide"), None),
            P("wide", None),
            P("wide", None),
            P("wide", None),
            P("wide", None),
            P("wide", None),
            P("wide"),
            P("wide"),
            P("wide"),
            P("wide"),
        ),
        check_vma=False,
    )
```

```python
import functools
import math

import jax
import jax.numpy as jnp
import numpy as np
from jax import lax
from jax.experimental import pallas as pl
from jax.experimental.pallas import tpu as pltpu
from jax.sharding import PartitionSpec as P

EPSILON = 1e-05
NEGATIVE = -1e30
EXCLUDED = -3e30
GELU_A = math.sqrt(2.0 / math.pi)
GELU_B = 0.044715
BF = jnp.bfloat16
F32 = jnp.float32


def nn(left, right):
    return lax.dot_general(left, right, (((1,), (0,)), ((), ())), preferred_element_type=F32)


def nt(left, right):
    return lax.dot_general(left, right, (((1,), (1,)), ((), ())), preferred_element_type=F32)


def tn(left, right):
    return lax.dot_general(left, right, (((0,), (0,)), ((), ())), preferred_element_type=F32)


def params(mib, dims):
    return pltpu.CompilerParams(
        vmem_limit_bytes=mib * 1024 * 1024, dimension_semantics=("arbitrary",) * dims
    )


def cost(flops, nbytes, trans=0):
    return pl.CostEstimate(flops=int(flops), bytes_accessed=int(nbytes), transcendentals=int(trans))


def split_low(values):
    high = values.astype(BF)
    return high, (values - high.astype(F32)).astype(BF)


def one_hot_t(ids_row, clusters):
    rows = lax.broadcasted_iota(jnp.int32, (clusters, ids_row.shape[1]), 0)
    return jnp.where(rows == ids_row, 1.0, 0.0).astype(BF)


def key_passes(total, size, score, weigh, blocks=None):
    count = total // size
    if count <= 4:
        if blocks is None:
            blocks = [score(index) for index in range(count)]
        peak = functools.reduce(jnp.maximum, [jnp.max(b, axis=0, keepdims=True) for b in blocks])
        denom, sums = 0.0, None
        for index in range(count):
            expo = jnp.exp(blocks[index] - peak)
            denom = denom + jnp.sum(expo, axis=0, keepdims=True)
            parts = weigh(index, expo)
            sums = parts if sums is None else tuple(x + y for x, y in zip(sums, parts))
        return peak, denom, sums

    def step(index, carry):
        peak, denom, sums = carry
        block = score(index)
        fresh = jnp.maximum(peak, jnp.max(block, axis=0, keepdims=True))
        expo = jnp.exp(block - fresh)
        fade = jnp.exp(peak - fresh)
        parts = weigh(index, expo)
        return (
            fresh,
            denom * fade + jnp.sum(expo, axis=0, keepdims=True),
            tuple(old * fade + new for old, new in zip(sums, parts)),
        )

    shapes = jax.eval_shape(lambda: (score(0), weigh(0, score(0))))
    lanes = shapes[0].shape[1]
    start = (
        jnp.full((1, lanes), NEGATIVE, F32),
        jnp.zeros((1, lanes), F32),
        tuple(jnp.zeros(item.shape, F32) for item in shapes[1]),
    )
    return lax.fori_loop(0, count, step, start)


def key_sum(total, size, step, start):
    count = total // size
    if count <= 4:
        for index in range(count):
            start = step(index, start)
        return start
    return lax.fori_loop(0, count, step, start)


def spot_of(index, size):
    if isinstance(index, int):
        return pl.ds(index * size, size)
    return pl.ds(pl.multiple_of(index * size, size), size)


def piece(ref, index, size, axis):
    spot = spot_of(index, size)
    return ref[spot, :] if axis == 0 else ref[:, spot]


def table_kernel(*refs, picks):
    parts, out = refs[:-1], refs[-1]
    total = parts[0][:, :picks]
    for part in parts[1:]:
        total = total + part[:, :picks]
    out[:, :picks] = total
    rows = parts[0].shape[1] - picks
    for group, part in enumerate(parts):
        out[:, picks + group * rows : picks + (group + 1) * rows] = part[:, picks:]


def bias_kernel(info, *refs, groups, peers, rows, picks):
    tables, (bias_ref, ids_ref) = refs[:peers], refs[peers:]
    part = pl.program_id(0)
    owner = (
        lax.rem(info[0] + part // peers, groups) * peers + lax.rem(info[1] + part % peers, peers)
    )
    heads, _, clusters = tables[0].shape
    place = owner * rows + lax.broadcasted_iota(jnp.int32, (rows, clusters), 0)
    plain = jnp.where(place >= info[2], EXCLUDED, NEGATIVE)
    for head in range(heads):
        top = tables[0][head, :picks]
        for table in tables[1:]:
            top = top + table[head, :picks]
        value = plain
        for pick in range(picks):
            value = jnp.where(place == top[pick : pick + 1, :], 0.0, value)
        bias_ref[head] = value.astype(BF)

    @pl.when(part == 0)
    def ids():
        lines = rows // clusters
        for head in range(heads):
            row = []
            for group in range(groups):
                for table in tables:
                    for line in range(lines):
                        at = picks + group * lines + line
                        row.append(table[head, at : at + 1, :])
            ids_ref[head] = jnp.concatenate(row, axis=1)


def project_kernel(info, *refs, peers, olds):
    parts = refs[:peers]
    gain_ref, shift_ref, w_ref = refs[peers : peers + 3]
    hat_ref, feat_ref, kv_ref = refs[peers + 3 + olds :]
    rows = hat_ref.shape[1]
    for peer in range(peers):
        values = parts[peer][...].astype(F32)
        centered = values - jnp.mean(values, axis=-1, keepdims=True)
        variance = jnp.mean(centered * centered, axis=-1, keepdims=True)
        scaled = centered * lax.rsqrt(variance + EPSILON) * gain_ref[...]
        if peer == 0:
            hat_ref[...] = scaled.astype(BF).T
        low = (scaled + shift_ref[...]).astype(BF)
        found = nt(w_ref[0], low)
        heads, triple = feat_ref.shape[0], feat_ref.shape[1]
        hs = triple // 3
        spot = slice(peer * rows, (peer + 1) * rows)
        for head in range(heads):
            base = head * triple
            query = (found[base : base + hs] * 0.125).astype(BF)
            pair = found[base + hs : base + triple].astype(BF)
            feat_ref[head, :hs, spot] = query
            feat_ref[head, hs:, spot] = pair
            kv_ref[head, spot, :] = pair.T


def forward_kernel(ids_all, feat, kv, bias, *refs, size, groups, rows):
    outs = refs[:groups]
    mix_ref, stat_ref, cen_ref = refs[groups:]
    hs = feat.shape[1] // 3
    keys = kv.shape[1]
    count = keys // size
    clusters = bias.shape[2]
    kv_h, bias_h = kv.at[0], bias.at[0]
    queries_all, kvt = feat.at[0, :hs], feat.at[0, hs:]
    hot_all = one_hot_t(ids_all[0], clusters)
    ones = jnp.ones((16, keys), BF)
    sums = nt(jnp.concatenate([queries_all[...], ones], axis=0), hot_all)
    counts = sums[hs : hs + 1]
    centroid = (sums[:hs] / jnp.maximum(counts, 1.0)).astype(BF)
    padded = jnp.concatenate([centroid, jnp.zeros_like(centroid)], axis=0)

    def cluster_score(index):
        scores = nn(piece(kv_h, index, size, 0), padded)
        outside = piece(bias_h, index, size, 0).astype(F32) < 2.0 * NEGATIVE
        return jnp.where(outside, NEGATIVE, scores)

    def cluster_weigh(index, expo):
        top = piece(bias_h, index, size, 0).astype(F32) == 0.0
        mass = jnp.sum(jnp.where(top, expo, 0.0), axis=0, keepdims=True)
        other = jnp.where(top, 0.0, expo).astype(BF)
        return nn(piece(kvt, index, size, 1), other), mass

    peers = keys // (groups * rows)
    hots, sides = [], []
    for group in range(groups):
        spot = slice(group * peers * rows, group * peers * rows + rows)
        hot = one_hot_t(ids_all[0, :, spot], clusters)
        queries = queries_all[:, spot]
        hots.append(hot)
        sides.append(jnp.concatenate([queries, jnp.zeros_like(queries), hot], axis=0))

    def member_score(group, index):
        both = jnp.concatenate([piece(kv_h, index, size, 0), piece(bias_h, index, size, 0)], axis=1)
        return nn(both, sides[group])

    def member_weigh(index, expo):
        return (nn(piece(kvt, index, size, 1), expo.astype(BF)),)

    short = count <= 4
    ahead = None
    if short:
        ahead = [member_score(0, index) for index in range(count)]
    peak, denom, (rest, mass) = key_passes(keys, size, cluster_score, cluster_weigh)
    rest = rest[hs:] / denom
    mass = mass / denom
    blank = jnp.zeros((5, clusters), F32)
    stats = jnp.concatenate([rest, mass, peak + jnp.log(denom), counts, blank], axis=0)
    stat_ref[0] = stats
    cen_ref[0] = centroid
    high, low = split_low(stats)
    table = jnp.concatenate([high, low], axis=1)
    for group in range(groups):
        gathered = nn(table, jnp.concatenate([hots[group], hots[group]], axis=0))
        blocks, ahead = ahead, None
        if short and group + 1 < groups:
            ahead = [member_score(group + 1, index) for index in range(count)]
        score = functools.partial(member_score, group)
        peak, denom, (mix,) = key_passes(keys, size, score, member_weigh, blocks)
        mix = mix[hs:] / denom
        outs[group][...] = (gathered[hs : hs + 1] * mix + gathered[:hs]).astype(BF)
        level = jnp.broadcast_to(peak + jnp.log(denom), (8, rows))
        mix_ref[0, group] = jnp.concatenate([mix, level], axis=0)


def sums_kernel(ids_own, *refs, groups):
    grads, (mix_ref, part_ref) = refs[:groups], refs[groups:]
    hs = grads[0].shape[0]
    total = None
    for group in range(groups):
        rows = grads[group].shape[1]
        step = ids_own.shape[2] // groups
        hot = one_hot_t(ids_own[0, :, group * step : group * step + rows], part_ref.shape[2])
        grad = grads[group][...]
        along = jnp.sum(grad.astype(F32) * mix_ref[0, group, :hs], axis=0, keepdims=True)
        high, low = split_low(along)
        pad = jnp.zeros((14, rows), BF)
        part = nt(jnp.concatenate([grad, high, low, pad], axis=0), hot)
        total = part if total is None else total + part
    part_ref[0] = total


def back_kernel(ids_all, feat, kv, bias, *refs, size, groups, gots):
    grads = refs[:groups]
    mix_ref, stat_ref, cen_ref = refs[groups : groups + 3]
    shares = refs[groups + 3 : groups + 4 + gots]
    dq_ref, own_ref, send_ref, total, both = refs[groups + 4 + gots :]
    hs, rows = grads[0].shape
    keys = kv.shape[1]
    count = keys // size
    peers = keys // (groups * rows)
    clusters = bias.shape[2]
    kv_h, bias_h = kv.at[0], bias.at[0]
    queries_all, kvt = feat.at[0, :hs], feat.at[0, hs:]
    stats = stat_ref[0]
    high, low = split_low(stats[hs : hs + 8])
    table = jnp.concatenate([high, low], axis=1)
    hots, sides, levels, deltas, pads, rights = [], [], [], [], [], []
    for group in range(groups):
        spot = slice(group * peers * rows, group * peers * rows + rows)
        hot = one_hot_t(ids_all[0, :, spot], clusters)
        queries = queries_all[:, spot]
        blank = jnp.zeros_like(queries)
        hots.append(jnp.concatenate([hot, hot], axis=0))
        sides.append(jnp.concatenate([queries, blank, hot], axis=0))
        mass = nn(table, hots[group])[0:1]
        back = (mass * grads[group][...].astype(F32)).astype(BF)
        levels.append(mix_ref[0, group, hs : hs + 1])
        deltas.append(jnp.sum(back.astype(F32) * mix_ref[0, group, :hs], axis=0, keepdims=True))
        pads.append(jnp.concatenate([blank, back], axis=0))
        turned = jnp.concatenate([queries, blank], axis=0)
        rights.append(jnp.concatenate([turned, pads[group]], axis=1).T)

    def scores(group, index):
        kv_c = piece(kv_h, index, size, 0)
        pair = jnp.concatenate([kv_c, piece(bias_h, index, size, 0)], axis=1)
        return nn(pair, sides[group]), nn(kv_c, pads[group])

    def finish(group, index, found, dq):
        weights = jnp.exp(found[0] - levels[group])
        grad_s = (weights * (found[1] - deltas[group])).astype(BF)
        part = nn(jnp.concatenate([grad_s, weights.astype(BF)], axis=1), rights[group])
        spot = spot_of(index, size)
        if group == 0:
            total[spot, :] = part
        else:
            total[spot, :] += part
        return dq + nn(piece(kvt, index, size, 1), grad_s)

    rest, mass = stats[:hs], stats[hs : hs + 1]
    level, counts = stats[hs + 1 : hs + 2], stats[hs + 2 : hs + 3]
    centroid = cen_ref[0]
    part = shares[0][0]
    for share in shares[1:]:
        part = part + share[0]
    d_rest = part[:hs].astype(BF)
    d_mass = part[hs : hs + 1] + part[hs + 1 : hs + 2]
    delta = jnp.sum(d_rest.astype(F32) * rest, axis=0, keepdims=True) + d_mass * mass
    cen_pad = jnp.concatenate([centroid, jnp.zeros_like(centroid)], axis=0)
    rest_pad = jnp.concatenate([jnp.zeros_like(centroid), d_rest], axis=0)
    right = jnp.concatenate([cen_pad, rest_pad], axis=1).T

    def cluster_step(index, summed):
        kv_c = piece(kv_h, index, size, 0)
        marks = piece(bias_h, index, size, 0).astype(F32)
        probs = jnp.exp(nn(kv_c, cen_pad) - level)
        probs = jnp.where(marks < 2.0 * NEGATIVE, 0.0, probs)
        top = marks == 0.0
        d_probs = jnp.where(top, d_mass, nn(kv_c, rest_pad))
        d_score = (probs * (d_probs - delta)).astype(BF)
        other = jnp.where(top, 0.0, probs).astype(BF)
        both[spot_of(index, size), :] = jnp.concatenate([d_score, other], axis=1)
        return summed + nn(piece(kvt, index, size, 1), d_score)

    start = jnp.zeros((2 * hs, rows), F32)
    zero = jnp.zeros((2 * hs, clusters), F32)
    member_dq = []
    if count <= 4:
        tasks = [(group, index) for group in range(groups) for index in range(count)]
        ahead = scores(*tasks[0])
        d_cen = key_sum(keys, size, cluster_step, zero)
        dq = start
        for step, (group, index) in enumerate(tasks):
            found = ahead
            if step + 1 < len(tasks):
                ahead = scores(*tasks[step + 1])
            dq = finish(group, index, found, dq)
            if index == count - 1:
                member_dq.append(dq[:hs] * 0.125)
                dq = start
    else:
        d_cen = key_sum(keys, size, cluster_step, zero)
        for group in range(groups):

            def step(index, dq, group=group):
                return finish(group, index, scores(group, index), dq)

            member_dq.append(lax.fori_loop(0, count, step, start)[:hs] * 0.125)
    d_cen = d_cen[:hs] * 0.125 / jnp.maximum(counts, 1.0)
    high, low = split_low(d_cen)
    table = jnp.concatenate([high, low], axis=1)
    for group in range(groups):
        base = group * peers * rows
        dq_ref[group] = (member_dq[group] + nn(table, hots[group])).astype(BF)
        own = total[base : base + rows, :] + nn(both[base : base + rows, :], right)
        own_ref[0, :, group * rows : (group + 1) * rows] = own.T
        for peer in range(1, peers):
            spot = (peer - 1) * groups * rows + group * rows
            found = total[base + peer * rows : base + (peer + 1) * rows, :]
            send_ref[0, :, spot : spot + rows] = found.astype(BF).T


def join_kernel(dqs, owns, gots, outs):
    for group, out in enumerate(outs):
        rows = out.shape[2]
        hs = out.shape[1] // 3
        spot = slice(group * rows, (group + 1) * rows)
        head = 0
        for dq, own, others in zip(dqs, owns, gots):
            for local in range(own.shape[0]):
                pair = own[local, :, spot]
                for other in others:
                    pair = pair + other[local, :, spot].astype(F32)
                out[head, :hs] = dq[group, local * hs : (local + 1) * hs]
                out[head, hs:] = pair.astype(BF)
                head += 1


def block_kernel(info, *refs, groups, chunks, fast):
    (attn, rest) = (refs[:groups], refs[groups:])
    x_ref, gain_ref, shift_ref, wo_ref, up_ref, down_ref, cot_ref = rest[:7]
    out_ref, dres_ref = rest[7:9]
    if fast:
        far_ref, low_far, act_ref, low_ref = rest[9:13]
        rest = rest[13:]
        hidden = far_ref.shape[1] * 4 // 7
    else:
        dn_ref, dup_ref, dbr_ref, act_ref, low_ref = rest[9:14]
        rest = rest[14:]
    dat = rest[:groups]
    hat_ref, inv_ref, normed, back, total = rest[groups:]
    index = pl.program_id(0)

    @pl.when(index == 0)
    def before():
        resid = x_ref[...].astype(F32)
        for group in range(groups):
            owner = lax.rem(info[0] + groups - group, groups)
            resid = resid + tn(attn[group][...], wo_ref[owner])
        total[...] = resid
        centered = resid - jnp.mean(resid, axis=-1, keepdims=True)
        variance = jnp.mean(centered * centered, axis=-1, keepdims=True)
        inverse = lax.rsqrt(variance + EPSILON)
        hat = centered * inverse
        hat_ref[...] = hat
        inv_ref[...] = jnp.broadcast_to(inverse, inv_ref.shape)
        low = (hat * gain_ref[...] + shift_ref[...]).astype(BF)
        normed[...] = low
        if fast:
            feats = attn[0].shape[0]
            half = feats // 2
            turned = low.T
            for group in range(groups):
                first = turned[group * feats : group * feats + half]
                second = turned[group * feats + half : (group + 1) * feats]
                spot = slice(group * half, (group + 1) * half)
                low_ref[spot, :] = jnp.where(info[1] == 0, first, second)
                low_far[spot, :] = jnp.where(info[1] == 0, second, first)
                first = attn[group][:half]
                second = attn[group][half:]
                spot = slice((groups + group) * half, (groups + group + 1) * half)
                low_ref[spot, :] = jnp.where(info[1] == 0, first, second)
                low_far[spot, :] = jnp.where(info[1] == 0, second, first)
        else:
            low_ref[...] = low
        back[...] = jnp.zeros_like(back)

    up = nn(normed[...], up_ref[...])
    grad_act = nt(cot_ref[...], down_ref[...])
    square = up * up
    inner = GELU_A * (up + GELU_B * up * square)
    curve = jnp.tanh(inner)
    act = (0.5 * up * (1.0 + curve)).astype(BF)
    slope = 0.5 * (1.0 + curve) + 0.5 * up * (1.0 - curve * curve) * (
        GELU_A * (1.0 + 3.0 * GELU_B * square)
    )
    d_up = (grad_act * slope).astype(BF)
    if fast:
        part = act.shape[1]
        half = part // 2
        first, second = act[:, :half], act[:, half:]
        act_ref[...] = jnp.where(info[1] == 0, first, second)
        far_ref[:, pl.ds(pl.multiple_of(index * part, part), part)] = d_up
        spot = pl.ds(pl.multiple_of(hidden + index * half, half), half)
        far_ref[:, spot] = jnp.where(info[1] == 0, second, first)
    else:
        dup_ref[...] = d_up
        act_ref[...] = act
    back[...] += nt(d_up, up_ref[...])
    total[...] += nn(act, down_ref[...])

    @pl.when(index == chunks - 1)
    def after():
        out_ref[...] = total[...].astype(BF)
        d_normed = back[...]
        hat = hat_ref[...]
        gain_part = jnp.sum(d_normed * hat, axis=0, keepdims=True)
        shift_part = jnp.sum(d_normed, axis=0, keepdims=True)
        if fast:
            rows, width = low_far.shape[1], d_normed.shape[1]
            fold = []
            for part_row in split_low(gain_part) + split_low(shift_part):
                fold += [part_row[:, k : k + rows].astype(F32) for k in range(0, width, rows)]
            fold.append(jnp.zeros((low_far.shape[0] - width - len(fold), rows), F32))
            folded = jnp.concatenate(fold, axis=0).astype(BF)
            low_far[width:, :] = folded
            low_ref[width:, :] = folded
        else:
            blank = jnp.zeros((6, d_normed.shape[1]), F32)
            dn_ref[...] = jnp.concatenate([gain_part, shift_part, blank], axis=0)
        gy = d_normed * gain_ref[...]
        mean_one = jnp.mean(gy, axis=-1, keepdims=True)
        mean_two = jnp.mean(gy * hat, axis=-1, keepdims=True)
        d_resid = cot_ref[...].astype(F32) + inv_ref[:, 0:1] * (gy - mean_one - hat * mean_two)
        dres_ref[...] = d_resid
        branch = d_resid.astype(BF)
        if fast:
            far_ref[:, hidden * 3 // 2 :] = branch
        else:
            dbr_ref[...] = branch
        for group in range(groups):
            owner = lax.rem(info[0] + groups - group, groups)
            dat[group][...] = nt(wo_ref[owner], branch).astype(BF)


def weights_kernel(info, *refs, groups):
    (dup, dup_got, dbr, dbr_got, act, act_got, low, low_got, cot, cot_got) = refs[:10]
    send_u, keep_u = refs[10:13], refs[13:15]
    send_d, keep_d = refs[15:18], refs[18:20]
    outs = refs[20]
    width = cot.shape[1]
    lead = send_u[0].shape[2]
    index = pl.program_id(0)
    group_at, place_u, place_d = info[0], info[3], info[4]
    rows = width // (2 * groups)
    quarter = rows // 4
    stay = groups * rows

    @pl.when(index == 0)
    def first():
        found = nn(low[stay:width, :], dbr[...]) + nn(low_got[stay:width, :], dbr_got[...])
        fold = low[width:, :].astype(F32) + low_got[width:, :].astype(F32)
        times = width // fold.shape[1]
        norms = []
        for part in range(2):
            both = fold[2 * part * times : (2 * part + 1) * times]
            both = both + fold[(2 * part + 1) * times : (2 * part + 2) * times]
            norms.append(jnp.concatenate([both[k : k + 1] for k in range(times)], axis=1))
        norms = jnp.concatenate(norms + [jnp.zeros((6, width), F32)], axis=0)
        for group in range(groups):
            block = found[group * rows : (group + 1) * rows]
            outs[group] = block
            for part in range(4):
                tail = block[part * quarter + 16 : (part + 1) * quarter]
                tail = jnp.concatenate([tail, norms], axis=0).astype(BF)
                place = lax.bitwise_xor(part, place_d)

                @pl.when(place >= 2)
                def leaves_more():
                    away = (groups - group) % groups

                    @pl.when(place == 2)
                    def second():
                        send_d[1][0, away, rows - lead :] = tail

                    @pl.when(place == 3)
                    def third():
                        send_d[2][0, away, rows - lead :] = tail


                @pl.when(place < 2)
                def stays_more():
                    keep_d[1][place, (groups - group) % groups, rows - lead :] = tail

    up = nn(low[:stay, :], dup[...]) + nn(low_got[:stay, :], dup_got[...])
    at = lax.bitwise_xor(lax.bitwise_xor(index, 2), place_u)
    for group in range(groups):
        spot = lax.rem(group + groups - group_at, groups)
        block = up[group * rows : (group + 1) * rows].astype(BF)
        away = (groups - group) % groups
        start = pl.multiple_of(at * quarter, 8)
        other = outs[group, pl.ds(start, 16), :].astype(BF)

        @pl.when(index < 2)
        def leaves():
            send_u[0][0, spot] = block[:lead]
            for turn in range(2):

                @pl.when(index == turn)
                def halves(turn=turn):
                    send_u[1 + turn][0, spot, : rows - lead] = block[lead:]
                    send_u[1 + turn][0, away, rows - lead :] = other

        @pl.when(index >= 2)
        def stays():
            keep_u[0][0, spot] = block[:lead]
            keep_u[1][0, spot, : rows - lead] = block[lead:]
            keep_u[1][0, away, rows - lead :] = other

    down = tn(act[...], cot[...]) + tn(act_got[...], cot_got[...])
    spot = lax.rem(index + groups - group_at, groups)
    for part in range(4):
        block = down[part * rows : (part + 1) * rows].astype(BF)
        place = lax.bitwise_xor(part, place_d)

        @pl.when(place >= 2)
        def leaves_down():
            send_d[0][place - 2, spot] = block[:lead]
            for turn in range(2):

                @pl.when(place == 2 + turn)
                def halves(turn=turn):
                    send_d[1 + turn][0, spot, : rows - lead] = block[lead:]

        @pl.when(place < 2)
        def stays_down():
            keep_d[0][place, spot] = block[:lead]
            keep_d[1][place, spot, : rows - lead] = block[lead:]


def second_kernel(keep_u, got_u, keep_d, got_d, *refs):
    inner, outs = refs[: len(refs) // 5 * 2], refs[len(refs) // 5 * 2 :]
    rows = keep_u.shape[2]
    to_y, to_x = outs[:2]
    to_y[:, :rows] = (keep_u[0].astype(F32) + got_u[0].astype(F32)).astype(BF)
    to_x[:, :rows] = (keep_d[0].astype(F32) + got_d[0].astype(F32)).astype(BF)
    if inner:
        to_y[:, rows:] = (inner[0][1].astype(F32) + inner[1][1].astype(F32)).astype(BF)
        to_x[:, rows:] = (inner[0][2].astype(F32) + inner[1][2].astype(F32)).astype(BF)
        outs[2][...] = (inner[0][3].astype(F32) + inner[1][3].astype(F32)).astype(BF)


def third_kernel(keep_u, got_u, keep_d, got_d, by_y, by_x, *refs, groups):
    more, outs = refs[:-groups], refs[-groups:]
    rows = keep_u.shape[2]
    for group in range(groups):
        up = keep_u[0, group].astype(F32) + got_u[0, group].astype(F32)
        down = keep_d[0, group].astype(F32) + got_d[0, group].astype(F32)
        outs[group][:rows] = (up + by_y[group, :rows].astype(F32)).astype(BF)
        outs[group][rows : 2 * rows] = (down + by_x[group, :rows].astype(F32)).astype(BF)
        if more:
            inner, inner_got, by_xy = more
            both = inner[0, group].astype(F32) + inner_got[0, group].astype(F32)
            both = both + by_y[group, rows:].astype(F32) + by_x[group, rows:].astype(F32)
            outs[group][2 * rows :] = (both + by_xy[group].astype(F32)).astype(BF)


def fourth_kernel(info, *refs, groups, high, feats):
    parts, out = refs[:groups], refs[groups]
    total = parts[0][: 2 * high].astype(F32)
    for part in parts[1:]:
        total = total + part[: 2 * high].astype(F32)
    out[: 2 * high] = total.astype(BF)
    if parts[0].shape[0] == 2 * high:
        return
    turned = refs[groups + 1]
    third = feats // 3
    lines = turned.shape[1]
    for group in range(groups):
        turned[group] = parts[group][2 * high :].astype(F32)
    for kind in range(3):
        found = []
        for owner in range(groups):
            spot = lax.rem(info[0] + groups - owner, groups)
            found.append(turned[spot, :, kind * third : (kind + 1) * third])
        at = 2 * high + kind * lines
        out[at : at + lines] = jnp.concatenate(found, axis=1).astype(BF)


def spread_kernel(info, *refs, lead, high):
    firsts, lasts, (wq, wkv, pair) = refs[:4], refs[4:8], refs[8:11]
    up_ref, out_ref, down_ref, norm_ref, gq_ref, gkv_ref, vec_ref, sums = refs[11:]
    index = pl.program_id(0)
    rows, width = down_ref.shape
    quarter = rows // 4
    lines = quarter + 8
    left = rows - lead
    order_u, order_d = (0, 2, 1, 3), (0, 1, 2, 3)

    @pl.when(index == 0)
    def first():
        for place, source in enumerate(order_u):

            @pl.when(info[3] == place)
            def take(source=source):
                for kind in range(3):
                    at = 2 * high + kind * lines
                    sums[kind] = lasts[source][at : at + lines].astype(F32)[quarter:]

    for place, source in enumerate(order_u):

        @pl.when(index == place)
        def upper(source=source):
            part = lasts[source]
            up_ref[:lead] = firsts[source][:lead].astype(F32)
            up_ref[lead:] = part[:left].astype(F32)
            at = pl.multiple_of(lax.bitwise_xor(index, info[3]) * quarter, 8)
            out_ref[pl.ds(at, 16), :] = part[left:high].astype(F32)
            spot = pl.ds(at, quarter)
            shift, gain = pair[spot, 0:1], pair[spot, 1:2]
            gain_sum, shift_sum = 0.0, 0.0
            for kind in range(3):
                base = 2 * high + kind * lines
                block = part[base : base + lines].astype(F32)[:quarter]
                line = sums[kind, 0:1]
                if kind == 0:
                    weight = wq[spot, :]
                    gq_ref[spot, :] = block + shift * line
                else:
                    lanes = slice((kind - 1) * width, kind * width)
                    weight = wkv[spot, lanes]
                    gkv_ref[spot, lanes] = block + shift * line
                gain_sum = gain_sum + jnp.sum(weight * block, axis=1, keepdims=True)
                shift_sum = shift_sum + jnp.sum(weight * line, axis=1, keepdims=True)
            lane = lax.broadcasted_iota(jnp.int32, (quarter, vec_ref.shape[1]), 1)
            vec_ref[spot, :] = jnp.where(lane == 0, gain_sum / gain, shift_sum)

    for place, source in enumerate(order_d):

        @pl.when(index == place)
        def lower(source=source):
            part = lasts[source]
            down_ref[:lead] = firsts[source][lead:].astype(F32)
            down_ref[lead:] = part[high : high + left].astype(F32)
            tail = part[high + left : 2 * high].astype(F32)
            at = pl.multiple_of(lax.bitwise_xor(index, info[4]) * quarter + 16, 8)
            out_ref[pl.ds(at, quarter - 16), :] = tail[: quarter - 16]

            @pl.when(lax.bitwise_xor(index, info[4]) == 0)
            def norms():
                norm_ref[...] = tail[quarter - 16 :]


def inward_kernel(info, *refs, groups, sets, gots, fast):
    dqs, owns = refs[:sets], refs[sets : 2 * sets]
    count = (2 + gots) * sets
    others = [refs[(2 + k) * sets : (3 + k) * sets] for k in range(gots)]
    hat_ref, parts, outs = refs[count], refs[count + 1 : count + 1 + groups], refs[count + 1 + groups :]
    join_kernel(dqs, owns, [[other[k] for other in others] for k in range(sets)], parts)
    heads, triple, rows = parts[0].shape
    hs = triple // 3
    total, sums = None, None
    ones = jnp.ones((16, rows), BF)
    for group in range(groups):
        order = [parts[group][h, k * hs : (k + 1) * hs] for k in range(3) for h in range(heads)]
        turned = jnp.concatenate(order, axis=0)
        found = nt(hat_ref[:, group * rows : (group + 1) * rows], turned)
        more = nt(ones, turned)
        total = found if total is None else total + found
        sums = more if sums is None else sums + more
    if not fast:
        outs[0][...] = total
        outs[1][...] = sums
        return
    own_ref, far_ref = outs
    block = total.shape[0] // (2 * groups)
    quarter = block // 4
    wide = total.shape[1]
    edge = wide // 128 * 128
    blank = jnp.zeros(own_ref.shape[:3] + (own_ref.shape[3] - edge,), BF)
    own_ref[..., edge:] = blank
    far_ref[..., edge:] = blank
    for group in range(groups):
        spot = lax.rem(group + groups - info[0], groups)
        for part in range(4):
            place = lax.bitwise_xor(part, info[3])
            found = []
            for parity in range(2):
                at = (2 * group + parity) * block + part * quarter
                lines = jnp.concatenate([total[at : at + quarter], sums[:8]], axis=0)
                found.append(lines.astype(BF))
            own_ref[place, spot, :, :wide] = jnp.where(info[1] == 0, found[0], found[1])
            far_ref[place, spot, :, :wide] = jnp.where(info[1] == 0, found[1], found[0])


def final_kernel(info, *refs, groups):
    parts = refs[:groups]
    x_ref, dres_ref, gain_ref, w_ref, out_ref = refs[groups:]
    d_normed = jnp.zeros(dres_ref.shape, F32)
    for group in range(groups):
        owner = lax.rem(info[0] + groups - group, groups)
        heads, triple, rows = parts[group].shape
        d_normed = d_normed + tn(parts[group][...].reshape(heads * triple, rows), w_ref[owner])
    values = x_ref[...].astype(F32)
    centered = values - jnp.mean(values, axis=-1, keepdims=True)
    variance = jnp.mean(centered * centered, axis=-1, keepdims=True)
    inverse = lax.rsqrt(variance + EPSILON)
    hat = centered * inverse
    gy = d_normed * gain_ref[...]
    mean_one = jnp.mean(gy, axis=-1, keepdims=True)
    mean_two = jnp.mean(gy * hat, axis=-1, keepdims=True)
    out_ref[...] = (dres_ref[...] + inverse * (gy - mean_one - hat * mean_two)).astype(BF)


def whole(shape):
    return pl.BlockSpec(shape, lambda *at: (0,) * len(shape))


def per_device(
    tokens,
    cluster_ids,
    lengths,
    top_keys,
    gain_one,
    shift_one,
    w_query,
    w_keyval,
    w_out,
    gain_two,
    shift_two,
    w_up,
    w_down,
    cotangent,
):
    rows, width = tokens.shape
    heads = cluster_ids.shape[1]
    hs = width // heads
    hidden = w_up.shape[1]
    wide = lax.axis_size("wide")
    n_dp = lax.axis_size("dp")
    groups = math.gcd(heads, wide)
    peers = wide // groups
    own_heads = heads // groups
    own_clusters = top_keys.shape[2]
    clusters = own_clusters * wide
    picks = top_keys.shape[3]
    seq = rows * wide
    size = 512 if seq <= 2048 else 2048
    feats = own_heads * hs
    block_rows = width // wide
    fast = peers == 2 and n_dp == 4 and block_rows == 96 and hidden == 4 * width and width % 256 == 0 and rows % 128 == 0
    me = lax.axis_index("wide")
    group_at, peer_at = me // peers, me % peers
    dp_at = lax.axis_index("dp")
    seq_len = lengths[0]
    bit_x, bit_y = dp_at % 2, (dp_at // 2) % 2
    place_u, place_d = 2 * bit_x + bit_y, 2 * bit_y + bit_x
    info = jnp.stack([group_at, peer_at, seq_len, place_u, place_d, me]).astype(jnp.int32)

    def along_groups(values, hop):
        pairs = [(i, ((i // peers + hop) % groups) * peers + i % peers) for i in range(wide)]
        return lax.ppermute(values, "wide", pairs)

    def along_peers(values, hop):
        pairs = [(i, (i // peers) * peers + (i % peers + hop) % peers) for i in range(wide)]
        return lax.ppermute(values, "wide", pairs)

    def along_dp(values, mask):
        return lax.ppermute(values, "dp", [(i, i ^ mask) for i in range(n_dp)])

    def prefetched(kernel, grid, in_specs, out_specs, out_shape, mib, spent, name, scratch=(), alias=None):
        return pl.pallas_call(
            kernel,
            grid_spec=pltpu.PrefetchScalarGridSpec(
                num_scalar_prefetch=1,
                grid=grid,
                in_specs=in_specs,
                out_specs=out_specs,
                scratch_shapes=list(scratch),
            ),
            out_shape=out_shape,
            compiler_params=params(mib, len(grid)),
            cost_estimate=spent,
            input_output_aliases=alias or {},
            name=name,
        )

    def after(values, *others):
        return lax.optimization_barrier((values, others))[0]

    def array(shape, dtype):
        return jax.ShapeDtypeStruct(shape, dtype)

    position = me * rows + jnp.arange(rows, dtype=jnp.int32)
    marked = jnp.where((position < seq_len)[:, None], cluster_ids, -1).T
    tops = jnp.zeros((heads, picks, clusters), jnp.int32)
    tops = lax.dynamic_update_slice(
        tops, top_keys[0].transpose(0, 2, 1), (0, 0, me * own_clusters)
    )
    lines = rows // clusters
    packed = jnp.concatenate([tops, marked.reshape(heads, lines, clusters)], axis=1)
    early = [along_peers(tokens, -hop) for hop in range(1, peers)]
    packed = after(packed.reshape(groups, own_heads, picks + lines, clusters), early)

    def of_heads(hop):
        return lax.dynamic_index_in_dim(packed, (group_at + groups - hop) % groups, keepdims=False)

    arrived = [of_heads(0)] + [along_groups(of_heads(hop), -hop) for hop in range(1, groups)]

    mine = {0: tokens, 1: along_groups(tokens, -1)}
    if groups > 2:
        mine[groups - 1] = along_groups(tokens, 1)
    ready = after(tokens, arrived)
    for hop in range(2, groups - 1):
        mine[hop] = along_groups(ready, -hop)

    w_in = jnp.concatenate([w_query, w_keyval], axis=1).T.reshape(3, heads, hs, width)
    w_in = w_in.transpose(1, 0, 2, 3).reshape(groups, 3 * feats, width)
    table_shape = (own_heads, picks + groups * lines, clusters)
    table = pl.pallas_call(
        functools.partial(table_kernel, picks=picks),
        grid=(1,),
        in_specs=[whole((own_heads, picks + lines, clusters))] * groups,
        out_specs=whole(table_shape),
        out_shape=array(table_shape, jnp.int32),
        compiler_params=params(8, 1),
        cost_estimate=cost(1e5, 1e6),
        name="table",
    )(*after(arrived, w_in))
    tables = [table] + [along_peers(table, -hop) for hop in range(1, peers)]
    cot_got = [along_peers(after(cotangent, arrived), hop) for hop in range(1, peers)]
    cot_got = cot_got if fast else []
    bias, ids_all = prefetched(
        functools.partial(bias_kernel, groups=groups, peers=peers, rows=rows, picks=picks),
        (wide,),
        [whole(table_shape)] * peers,
        [
            pl.BlockSpec((own_heads, rows, clusters), lambda i, s: (0, i, 0)),
            whole((own_heads, 1, seq)),
        ],
        [array((own_heads, seq, clusters), BF), array((own_heads, 1, seq), jnp.int32)],
        12 if fast else 60,
        cost(own_heads * seq * clusters * picks * 8, own_heads * seq * clusters * 2),
        "bias",
    )(info, *tables)

    gain_row, shift_row = gain_one[None, :], shift_one[None, :]
    shapes = [
        array((width, groups * rows), BF),
        array((own_heads, 3 * hs, seq), BF),
        array((own_heads, seq, 2 * hs), BF),
    ]
    held = []
    split_peers = peers if peers <= 2 else 1
    for group in sorted(range(groups), key=lambda g: min(g, groups - g)):
        arrival = mine[group]
        if group == 1:
            arrival = after(arrival, bias, held, cot_got, [mine[hop] for hop in range(2, groups)])
        chunk = [arrival]
        chunk += early if group == 0 else [along_peers(arrival, -hop) for hop in range(1, peers)]
        if peers > 2:
            chunk = [jnp.concatenate(chunk, axis=0)]
        span = peers * rows
        if peers > 2:
            specs_in = [pl.BlockSpec((rows, width), lambda p, s: (p, 0))]
            grid = (peers,)
            outs = [
                pl.BlockSpec((width, rows), lambda p, s, g=group: (0, g)),
                pl.BlockSpec((own_heads, 3 * hs, rows), lambda p, s, g=group: (0, 0, g * peers + p)),
                pl.BlockSpec((own_heads, rows, 2 * hs), lambda p, s, g=group: (0, g * peers + p, 0)),
            ]
        else:
            specs_in = [whole((rows, width))] * split_peers
            grid = (1,)
            outs = [
                pl.BlockSpec((width, rows), lambda p, s, g=group: (0, g)),
                pl.BlockSpec((own_heads, 3 * hs, span), lambda p, s, g=group: (0, 0, g)),
                pl.BlockSpec((own_heads, span, 2 * hs), lambda p, s, g=group: (0, g, 0)),
            ]
        first = 1 + split_peers + 3
        held = prefetched(
            functools.partial(project_kernel, peers=split_peers, olds=len(held)),
            grid,
            specs_in
            + [
                whole((1, width)),
                whole((1, width)),
                pl.BlockSpec((1, 3 * feats, width), lambda p, s: (s[0], 0, 0)),
            ]
            + [pl.BlockSpec(memory_space=pl.ANY)] * len(held),
            outs,
            shapes,
            16 if fast else 60,
            cost(6 * span * width * feats, span * width * 4),
            "project",
            alias={first + k: k for k in range(len(held))},
        )(info, *chunk, gain_row, shift_row, w_in, *held)
    hat_own, feat, kv = held

    ids_full = pl.BlockSpec((1, 1, seq), lambda h, r: (h, 0, 0))
    feat_full = pl.BlockSpec((1, 3 * hs, seq), lambda h, r: (h, 0, 0))
    kv_full = pl.BlockSpec((1, seq, 2 * hs), lambda h, r: (h, 0, 0))
    bias_full = pl.BlockSpec((1, seq, clusters), lambda h, r: (h, 0, 0))
    head_rows = pl.BlockSpec((hs, rows), lambda h, r: (h, 0))
    mix_spec = pl.BlockSpec((1, 1, hs + 8, rows), lambda h, r: (h, r, 0, 0))
    stat_spec = pl.BlockSpec((1, hs + 8, clusters), lambda h, r: (h, 0, 0))
    cen_spec = pl.BlockSpec((1, hs, clusters), lambda h, r: (h, 0, 0))
    own_rows = groups * rows
    pair_flops = own_heads * own_rows * seq * 256

    one = [
        pl.BlockSpec(spec.block_shape, functools.partial(lambda h, f: f(h, 0), f=spec.index_map))
        for spec in (ids_full, feat_full, kv_full, bias_full, stat_spec, cen_spec, head_rows)
    ]
    ids_one, feat_one, kv_one, bias_one, stat_one, cen_one, rows_one = one
    part_one = pl.BlockSpec((1, hs + 16, clusters), lambda h: (h, 0, 0))
    mix_one = pl.BlockSpec((1, groups, hs + 8, rows), lambda h: (h, 0, 0, 0))
    all_groups = pl.BlockSpec((groups, hs, rows), lambda h: (0, h, 0))
    own_one = pl.BlockSpec((1, own_rows, 2 * hs), lambda h: (h, 0, 0))
    results = pl.pallas_call(
        functools.partial(forward_kernel, size=size, groups=groups, rows=rows),
        grid=(own_heads,),
        in_specs=[ids_one, feat_one, kv_one, bias_one],
        out_specs=[rows_one] * groups + [mix_one, stat_one, cen_one],
        out_shape=[array((feats, rows), BF)] * groups
        + [
            array((own_heads, groups, hs + 8, rows), F32),
            array((own_heads, hs + 8, clusters), F32),
            array((own_heads, hs, clusters), BF),
        ],
        compiler_params=params(32 if fast else 60, 1),
        cost_estimate=cost(6 * pair_flops, 8e6, own_heads * own_rows * seq),
        name="attend",
    )(ids_all, feat, kv, bias)
    attn_t = results[:groups]
    mixed, stats, centroid = results[groups:]

    arrived = [attn_t[0]] + [along_groups(attn_t[hop], hop) for hop in range(1, groups)]

    chunks = 4
    part = hidden // chunks
    lead = 32
    w_out_g = w_out.reshape(groups, feats, width)
    gain_row2, shift_row2 = gain_two[None, :], shift_two[None, :]
    square = whole((rows, width))
    column = pl.BlockSpec((rows, part), lambda i, s: (0, i))
    norm_spec = whole((8, width))
    if fast:
        kept_shapes = [
            array((rows, hidden + hidden // 2 + width), BF),
            array((width + 16, rows), BF),
            array((rows, hidden // 2), BF),
            array((width + 16, rows), BF),
        ]
        kept_specs = [whole(item.shape) for item in kept_shapes]
        kept_specs[2] = pl.BlockSpec((rows, part // 2), lambda i, s: (0, i))
    else:
        kept_shapes = [
            array((8, width), F32),
            array((rows, hidden), BF),
            array((rows, width), BF),
            array((rows, hidden), BF),
            array((rows, width), BF),
        ]
        kept_specs = [norm_spec, column, square, column, square]
    results = prefetched(
        functools.partial(block_kernel, groups=groups, chunks=chunks, fast=fast),
        (chunks,),
        [whole((feats, rows))] * groups
        + [
            square,
            whole((1, width)),
            whole((1, width)),
            whole((groups, feats, width)),
            pl.BlockSpec((width, part), lambda i, s: (0, i)),
            pl.BlockSpec((part, width), lambda i, s: (i, 0)),
            square,
        ],
        [square, square] + kept_specs + [whole((feats, rows))] * groups,
        [array((rows, width), BF), array((rows, width), F32)]
        + kept_shapes
        + [array((feats, rows), BF)] * groups,
        28 if fast else 60,
        cost(8 * rows * width * hidden, 4 * width * hidden, rows * hidden),
        "feed",
        scratch=[
            pltpu.VMEM((rows, width), F32),
            pltpu.VMEM((rows, 128), F32),
            pltpu.VMEM((rows, width), BF),
            pltpu.VMEM((rows, width), F32),
            pltpu.VMEM((rows, width), F32),
        ],
    )(info, *arrived, tokens, gain_row2, shift_row2, w_out_g, w_up, w_down, cotangent)
    output, d_resid = results[:2]
    kept, d_attn = results[2:-groups], results[-groups:]
    grads = [d_attn[0]] + [along_groups(d_attn[hop], -hop) for hop in range(1, groups)]

    def weight_parts():
        far, low_far, act_own, low_own = kept
        got, low_got = along_peers(far, 1), along_peers(low_far, 1)
        chunk = pl.BlockSpec((rows, part), lambda i, s: (0, i ^ 2 ^ s[3]))
        branch = pl.BlockSpec((rows, width), lambda i, s: (0, hidden * 3 // 2 // width))
        act_spec = pl.BlockSpec((rows, part // 2), lambda i, s: (0, i))
        act_there = pl.BlockSpec((rows, part // 2), lambda i, s: (0, 2 * hidden // part + i))
        low_spec = whole((width + 16, rows))
        tall = ((groups, lead, width), (groups, block_rows + 16 - lead, width))

        def early(shape):
            return pl.BlockSpec((1,) + shape, lambda i, s: (jnp.minimum(i, 1), 0, 0, 0))

        def late(shape):
            return pl.BlockSpec((1,) + shape, lambda i, s: (jnp.maximum(i - 2, 0), 0, 0, 0))

        results = prefetched(
            functools.partial(weights_kernel, groups=groups),
            (4,),
            [chunk, chunk, branch, branch, act_spec, act_there, low_spec, low_spec, square, square],
            [early(tall[0]), whole((1,) + tall[1]), whole((1,) + tall[1])]
            + [late(item) for item in tall]
            + [whole((2,) + tall[0]), whole((1,) + tall[1]), whole((1,) + tall[1])]
            + [whole((2,) + item) for item in tall],
            ([array((2,) + tall[0], BF)] + [array((1,) + tall[1], BF)] * 2
            + [array((2,) + item, BF) for item in tall]) * 2,
            60,
            cost(8 * rows * width * hidden, 6 * width * hidden),
            "weights",
            scratch=[pltpu.VMEM((groups, block_rows, width), F32)],
        )(info, far, got, far, got, act_own, got, low_own, low_got, cotangent, *cot_got)
        return results[:3], results[3:5], results[5:8], results[8:]

    def weight_second(keep_u, got_u, keep_d, got_d, *inner):
        def block(shape, at):
            return pl.BlockSpec((1,) + shape[1:], lambda i: (at, 0, 0, 0))

        high = keep_u.shape[2]
        lines = inner[0].shape[2] if inner else 0
        shapes = [(groups, high + lines, width)] * 2 + [(groups, lines, width)] * (len(inner) // 2)
        return pl.pallas_call(
            second_kernel,
            grid=(1,),
            in_specs=[
                block(item.shape, item.shape[0] - 1) for item in (keep_u, got_u, keep_d, got_d)
            ]
            + [whole(item.shape) for item in inner],
            out_specs=[whole(shape) for shape in shapes],
            out_shape=[array(shape, BF) for shape in shapes],
            compiler_params=params(20, 1),
            cost_estimate=cost(groups * high * width * 2, groups * high * width * 12),
            name="second",
        )(keep_u, got_u, keep_d, got_d, *inner)

    def weight_third(keep_u, got_u, keep_d, got_d, by_y, by_x, *more):
        def block(shape, at):
            return pl.BlockSpec((1,) + shape[1:], lambda i: (at, 0, 0, 0))

        tall = 2 * keep_u.shape[2] + (more[0].shape[2] if more else 0)
        more_specs = [block(item.shape, 0) for item in more[:2]]
        return pl.pallas_call(
            functools.partial(third_kernel, groups=groups),
            grid=(1,),
            in_specs=[block(keep_u.shape, 0)] * 4
            + [whole(by_y.shape), whole(by_x.shape)]
            + more_specs
            + [whole(item.shape) for item in more[2:]],
            out_specs=[whole((tall, width))] * groups,
            out_shape=[array((tall, width), BF)] * groups,
            compiler_params=params(24, 1),
            cost_estimate=cost(groups * tall * width * 4, groups * tall * width * 8),
            name="third",
        )(keep_u, got_u, keep_d, got_d, by_y, by_x, *more)

    def weight_fourth(came, high, lines):
        tall = 2 * high + 3 * lines
        done = prefetched(
            functools.partial(fourth_kernel, groups=groups, high=high, feats=3 * feats),
            (1,),
            [whole(came[0].shape)] * groups,
            whole((tall, width)),
            array((tall, width), BF),
            16,
            cost(groups * tall * width, groups * tall * width * 2),
            "fourth",
            scratch=[pltpu.VMEM((groups, lines, width), F32)] if lines else [],
        )(info, *came)
        return [done] + [along_dp(done, mask) for mask in (1, 2, 3)]

    def weight_spread(firsts, lasts, high, ready):
        at = me * block_rows
        wq_rows = lax.dynamic_slice_in_dim(w_query, at, block_rows).astype(F32)
        wkv_rows = lax.dynamic_slice_in_dim(w_keyval, at, block_rows).astype(F32)
        pair = jnp.stack([shift_one, gain_one] + [shift_one] * 6, axis=1)
        pair = lax.dynamic_slice_in_dim(pair, at, block_rows)
        pair, wq_rows, wkv_rows = after((pair, wq_rows, wkv_rows), ready)
        return prefetched(
            functools.partial(spread_kernel, lead=lead, high=high),
            (4,),
            [whole(item.shape) for item in firsts + lasts]
            + [whole(wq_rows.shape), whole(wkv_rows.shape), whole(pair.shape)],
            [
                pl.BlockSpec((block_rows, part), lambda i, s: (0, i ^ s[3])),
                whole((block_rows, width)),
                pl.BlockSpec((block_rows, width), lambda i, s: (i ^ s[4], 0)),
                whole((8, width)),
                whole((block_rows, width)),
                whole((block_rows, 2 * width)),
                whole((block_rows, 128)),
            ],
            [
                array((block_rows, hidden), F32),
                array((block_rows, width), F32),
                array((hidden // wide, width), F32),
                array((8, width), F32),
                array((block_rows, width), F32),
                array((block_rows, 2 * width), F32),
                array((block_rows, 128), F32),
            ],
            20,
            cost(1e6, 8 * block_rows * width * 6),
            "spread",
            scratch=[pltpu.VMEM((3, 8, width), F32)],
        )(info, *firsts, *lasts, wq_rows, wkv_rows, pair)

    masks = [1 << k for k in range(n_dp.bit_length() - 1)]

    def reduce_rows(partial):
        blocks = partial.reshape(groups, peers, partial.shape[0] // wide, partial.shape[1])

        def of_peer(hop):
            at = (peer_at + hop) % peers
            return lax.dynamic_index_in_dim(blocks, at, axis=1, keepdims=False)

        total = of_peer(0).astype(F32)
        for hop in range(1, peers):
            total = total + along_peers(of_peer(hop), hop).astype(F32)
        total = total.astype(BF)

        def of_group(hop):
            return lax.dynamic_index_in_dim(total, (group_at + hop) % groups, keepdims=False)

        done = of_group(0).astype(F32)
        for hop in range(1, groups):
            done = done + along_groups(of_group(hop), hop).astype(F32)
        for mask in masks:
            done = done.astype(BF)
            done = done.astype(F32) + along_dp(done, mask).astype(F32)
        return done

    if fast:
        send_u, keep_u, send_d, keep_d = weight_parts()
        got_u, got_d = [along_dp(send_u[0], 1)], [along_dp(send_d[0], 2)]
        grads = after(grads, keep_u)
    else:
        norm_two, d_up, d_branch, act, normed_two = kept
        total_up = reduce_rows(tn(normed_two, d_up).astype(BF))
        total_down = reduce_rows(tn(act, cotangent).astype(BF))
        found = jnp.stack([nn(item, d_branch).astype(BF) for item in arrived])
        found = [
            lax.dynamic_index_in_dim(found, (group_at + groups - g) % groups, keepdims=False)
            for g in range(groups)
        ]
        total_out = reduce_rows(jnp.concatenate(found, axis=0))
        norm_own = reduce_rows(norm_two[:2].T.astype(BF)).T

    share = pl.pallas_call(
        functools.partial(sums_kernel, groups=groups),
        grid=(own_heads,),
        in_specs=[ids_one]
        + [rows_one] * groups
        + [mix_one],
        out_specs=part_one,
        out_shape=array((own_heads, hs + 16, clusters), F32),
        compiler_params=params(16 if fast else 60, 1),
        cost_estimate=cost(own_heads * own_rows * clusters * 160, 2e6),
        name="sums",
    )(ids_all, *grads, mixed)
    share_got = [along_peers(share, hop) for hop in range(1, peers)]

    sets = [(k, 1) for k in range(own_heads)] if fast else [(0, own_heads)]
    dqs, dkv_owns, dkv_sends = [], [], []
    inputs = (ids_all, feat, kv, bias, *grads, mixed, stats, centroid, share, *share_got)
    input_specs = (
        [ids_one, feat_one, kv_one, bias_one]
        + [rows_one] * groups
        + [mix_one, stat_one, cen_one]
        + [part_one] * (1 + len(share_got))
    )
    for first, many in sets:
        back_shapes = [
            array((groups, many * hs, rows), BF),
            array((many, 2 * hs, own_rows), F32),
            array((many, 2 * hs, max(peers - 1, 1) * own_rows), BF),
        ]
        moved = [
            pl.BlockSpec(
                spec.block_shape,
                functools.partial(lambda h, f, k: f(h + k), f=spec.index_map, k=first),
            )
            for spec in input_specs
        ]
        dq, dkv_own, dkv_send = pl.pallas_call(
            functools.partial(back_kernel, size=size, groups=groups, gots=len(share_got)),
            grid=(many,),
            in_specs=moved,
            out_specs=[
                all_groups,
                pl.BlockSpec((1,) + back_shapes[1].shape[1:], lambda h: (h, 0, 0)),
                pl.BlockSpec((1,) + back_shapes[2].shape[1:], lambda h: (h, 0, 0)),
            ],
            out_shape=back_shapes,
            scratch_shapes=[pltpu.VMEM((seq, 2 * hs), F32), pltpu.VMEM((seq, 2 * clusters), BF)],
            compiler_params=params(36 if fast else 62, 1),
            cost_estimate=cost(14 * many * own_rows * seq * 256, 10e6, many * own_rows * seq),
            name="back",
        )(*inputs)
        dqs.append(dq)
        dkv_owns.append(dkv_own)
        dkv_sends.append(dkv_send)
        if fast and first == 0:
            next_a = weight_second(keep_u[0], got_u[0], keep_d[0], got_d[0])
            by_a = along_dp(next_a[0], 2), along_dp(next_a[1], 1)
            send_u, send_d = after((send_u, send_d), next_a)
            got_u += [along_dp(item, 1) for item in send_u[1:]]
            got_d += [along_dp(item, 2) for item in send_d[1:]]
            inputs = after(inputs, next_a, dq)
        elif fast and first == 1:
            sums_a = weight_third(keep_u[0], got_u[0], keep_d[0], got_d[0], *by_a)
            came_a = [sums_a[0]]
            came_a += [along_groups(sums_a[hop], hop) for hop in range(1, groups)]
            inputs = after(inputs, sums_a, dq)
    dkv_gots = [
        [
            along_peers(
                item if peers == 2 else item[..., (hop - 1) * own_rows : hop * own_rows], hop
            )
            for item in dkv_sends
        ]
        for hop in range(1, peers)
    ]
    tall = block_rows + 16
    spent = cost(2 * own_rows * width * 3 * feats, 4e6)
    if fast:
        lines = block_rows // 4 + 8
        more = [array((4, groups, lines, width), BF)] * 2
    else:
        more = [array((width, 3 * feats), F32), array((16, 3 * feats), F32)]
    if fast:
        dkv_owns = after(dkv_owns, came_a[1], got_u[2], got_d[2])
    results = prefetched(
        functools.partial(
            inward_kernel, groups=groups, sets=len(sets), gots=len(dkv_gots), fast=fast
        ),
        (1,),
        [whole(back_shapes[0].shape)] * len(sets)
        + [whole(back_shapes[1].shape)] * (len(sets) * (1 + len(dkv_gots)))
        + [whole((width, own_rows))],
        [whole((own_heads, 3 * hs, rows))] * groups + [whole(item.shape) for item in more],
        [array((own_heads, 3 * hs, rows), BF)] * groups + more,
        28 if fast else 60,
        spent,
        "inward",
    )(info, *dqs, *dkv_owns, *[item for got in dkv_gots for item in got], hat_own)
    d_in, more = results[:groups], results[groups:]
    home = [d_in[0]] + [along_groups(d_in[hop], hop) for hop in range(1, groups)]

    if fast:
        keep, far = more
        inner_got = along_peers(far, 1)
        spread_a = weight_fourth(came_a, lead, 0)
        last_parts = (keep_u[1], got_u[1], keep_d[1], got_d[1])
        first_parts = (keep_u[1], got_u[2], keep_d[1], got_d[2])
        to_y, to_x, to_xy = weight_second(
            *after(first_parts, came_a, got_u[1], got_d[1]), keep, inner_got
        )
        by_y, by_x, by_xy = along_dp(to_y, 2), along_dp(to_x, 1), along_dp(to_xy, 3)
        by_y, by_x = after((by_y, by_x), home)
        sums_b = weight_third(*last_parts, by_y, by_x, keep, inner_got, by_xy)
        came_b = [sums_b[0]] + [along_groups(sums_b[hop], hop) for hop in range(1, groups)]
        high = keep_u[1].shape[2]
        came_b = after(came_b, spread_a)
        spread_b = weight_fourth(came_b, high, lines)
        home = after(home, spread_b[0])
        found = weight_spread(spread_a, spread_b, high, came_b[0])
        total_up, total_out, total_down, norms, total_query, total_keyval, vector = found
        norm_own = lax.dynamic_slice_in_dim(norms, me * block_rows, block_rows, axis=1)
        gain_grad, shift_grad = vector[:, 0], vector[:, 1]
    else:
        found, more = more
        found = found.reshape(groups, peers, block_rows, 3 * feats)
        more = jnp.broadcast_to(more, (groups, peers, 16, 3 * feats))
        found = jnp.concatenate([found, more], axis=2).astype(BF)

        def of_peer(hop):
            at = (peer_at + hop) % peers
            return lax.dynamic_index_in_dim(found, at, axis=1, keepdims=False)

        total = of_peer(0).astype(F32)
        for hop in range(1, peers):
            total = total + along_peers(of_peer(hop), hop).astype(F32)
        for mask in masks:
            total = total.astype(BF)
            total = total.astype(F32) + along_dp(total, mask).astype(F32)
        total = total.astype(BF)
        items = [
            lax.dynamic_index_in_dim(total, (group_at + hop) % groups, keepdims=False)
            for hop in range(groups)
        ]
        pieces = [items[0]] + [along_groups(items[hop], hop) for hop in range(1, groups)]
        pieces = jnp.stack(pieces)
        pieces = jnp.stack(
            [
                lax.dynamic_index_in_dim(pieces, (group_at + groups - g) % groups, keepdims=False)
                for g in range(groups)
            ]
        ).astype(F32)
        q_part = pieces[:, :, :feats].transpose(1, 0, 2).reshape(tall, width)
        kv_part = (
            pieces[:, :, feats:]
            .reshape(groups, tall, 2, feats)
            .transpose(1, 2, 0, 3)
            .reshape(tall, 2 * width)
        )
        at = me * block_rows
        wq_rows = lax.dynamic_slice_in_dim(w_query, at, block_rows).astype(F32)
        wkv_rows = lax.dynamic_slice_in_dim(w_keyval, at, block_rows).astype(F32)
        gain_own = lax.dynamic_slice_in_dim(gain_one, at, block_rows)
        shift_own = lax.dynamic_slice_in_dim(shift_one, at, block_rows)
        q_sum, kv_sum = q_part[block_rows], kv_part[block_rows]
        q_part, kv_part = q_part[:block_rows], kv_part[:block_rows]
        shift_grad = jnp.sum(wq_rows * q_sum, axis=1) + jnp.sum(wkv_rows * kv_sum, axis=1)
        along = jnp.sum(wq_rows * q_part, axis=1) + jnp.sum(wkv_rows * kv_part, axis=1)
        total_query = q_part + shift_own[:, None] * q_sum
        total_keyval = kv_part + shift_own[:, None] * kv_sum
        gain_grad = along / gain_own

    grad_tokens = prefetched(
        functools.partial(final_kernel, groups=groups),
        (1,),
        [whole((own_heads, 3 * hs, rows))] * groups
        + [square, square, whole((1, width)), whole((groups, 3 * feats, width))],
        square,
        array((rows, width), BF),
        24 if fast else 60,
        cost(6 * rows * width * width, 6 * width * width),
        "final",
    )(info, *home, tokens, d_resid, gain_row, w_in)

    return (
        output,
        grad_tokens,
        total_query,
        total_keyval,
        total_out,
        total_up,
        total_down,
        gain_grad,
        shift_grad,
        norm_own[0],
        norm_own[1],
    )


def solution(mesh):
    return jax.shard_map(
        per_device,
        mesh=mesh,
        in_specs=(
            P(("dp", "wide"), None),
            P(("dp", "wide"), None),
            P("dp"),
            P("dp", None, "wide", None),
            P(),
            P(),
            P(),
            P(),
            P(),
            P(),
            P(),
            P(),
            P(),
            P(("dp", "wide"), None),
        ),
        out_specs=(
            P(("dp", "wide"), None),
            P(("dp", "wide"), None),
            P("wide", None),
            P("wide", None),
            P("wide", None),
            P("wide", None),
            P("wide", None),
            P("wide"),
            P("wide"),
            P("wide"),
            P("wide"),
        ),
        check_vma=False,
    )
```

```python
import functools
import math

import jax
import jax.numpy as jnp
import numpy as np
from jax import lax
from jax.experimental import pallas as pl
from jax.experimental.pallas import tpu as pltpu
from jax.sharding import PartitionSpec as P

EPSILON = 1e-05
NEGATIVE = -1e30
EXCLUDED = -3e30
GELU_A = math.sqrt(2.0 / math.pi)
GELU_B = 0.044715
BF = jnp.bfloat16
F32 = jnp.float32


def nn(left, right):
    return lax.dot_general(left, right, (((1,), (0,)), ((), ())), preferred_element_type=F32)


def nt(left, right):
    return lax.dot_general(left, right, (((1,), (1,)), ((), ())), preferred_element_type=F32)


def tn(left, right):
    return lax.dot_general(left, right, (((0,), (0,)), ((), ())), preferred_element_type=F32)


def params(mib, dims):
    return pltpu.CompilerParams(
        vmem_limit_bytes=mib * 1024 * 1024, dimension_semantics=("arbitrary",) * dims
    )


def cost(flops, nbytes, trans=0):
    return pl.CostEstimate(flops=int(flops), bytes_accessed=int(nbytes), transcendentals=int(trans))


def split_low(values):
    high = values.astype(BF)
    return high, (values - high.astype(F32)).astype(BF)


def one_hot_t(ids_row, clusters):
    rows = lax.broadcasted_iota(jnp.int32, (clusters, ids_row.shape[1]), 0)
    return jnp.where(rows == ids_row, 1.0, 0.0).astype(BF)


def key_passes(total, size, score, weigh, blocks=None):
    count = total // size
    if count <= 4:
        if blocks is None:
            blocks = [score(index) for index in range(count)]
        peak = functools.reduce(jnp.maximum, [jnp.max(b, axis=0, keepdims=True) for b in blocks])
        denom, sums = 0.0, None
        for index in range(count):
            expo = jnp.exp(blocks[index] - peak)
            denom = denom + jnp.sum(expo, axis=0, keepdims=True)
            parts = weigh(index, expo)
            sums = parts if sums is None else tuple(x + y for x, y in zip(sums, parts))
        return peak, denom, sums

    def step(index, carry):
        peak, denom, sums = carry
        block = score(index)
        fresh = jnp.maximum(peak, jnp.max(block, axis=0, keepdims=True))
        expo = jnp.exp(block - fresh)
        fade = jnp.exp(peak - fresh)
        parts = weigh(index, expo)
        return (
            fresh,
            denom * fade + jnp.sum(expo, axis=0, keepdims=True),
            tuple(old * fade + new for old, new in zip(sums, parts)),
        )

    shapes = jax.eval_shape(lambda: (score(0), weigh(0, score(0))))
    lanes = shapes[0].shape[1]
    start = (
        jnp.full((1, lanes), NEGATIVE, F32),
        jnp.zeros((1, lanes), F32),
        tuple(jnp.zeros(item.shape, F32) for item in shapes[1]),
    )
    return lax.fori_loop(0, count, step, start)


def key_sum(total, size, step, start):
    count = total // size
    if count <= 4:
        for index in range(count):
            start = step(index, start)
        return start
    return lax.fori_loop(0, count, step, start)


def spot_of(index, size):
    if isinstance(index, int):
        return pl.ds(index * size, size)
    return pl.ds(pl.multiple_of(index * size, size), size)


def piece(ref, index, size, axis):
    spot = spot_of(index, size)
    return ref[spot, :] if axis == 0 else ref[:, spot]


def table_kernel(info, *refs, picks):
    parts, out = refs[:-1], refs[-1]
    total = parts[0][:, :picks]
    for part in parts[1:]:
        total = total + part[:, :picks]
    out[:, :picks] = total
    rows = parts[0].shape[1] - picks
    for group, part in enumerate(parts):
        out[:, picks + group * rows : picks + (group + 1) * rows] = part[:, picks:]


def bias_kernel(info, *refs, groups, peers, rows, picks):
    tables, (bias_ref, ids_ref) = refs[:peers], refs[peers:]
    part = pl.program_id(0)
    owner = (
        lax.rem(info[0] + part // peers, groups) * peers + lax.rem(info[1] + part % peers, peers)
    )
    heads, _, clusters = tables[0].shape
    place = owner * rows + lax.broadcasted_iota(jnp.int32, (rows, clusters), 0)
    plain = jnp.where(place >= info[2], EXCLUDED, NEGATIVE)
    for head in range(heads):
        top = tables[0][head, :picks]
        for table in tables[1:]:
            top = top + table[head, :picks]
        value = plain
        for pick in range(picks):
            value = jnp.where(place == top[pick : pick + 1, :], 0.0, value)
        bias_ref[head] = value.astype(BF)

    @pl.when(part == 0)
    def ids():
        lines = rows // clusters
        for head in range(heads):
            row = []
            for group in range(groups):
                for table in tables:
                    for line in range(lines):
                        at = picks + group * lines + line
                        row.append(table[head, at : at + 1, :])
            ids_ref[head] = jnp.concatenate(row, axis=1)


def project_kernel(info, *refs, peers, olds):
    parts = refs[:peers]
    gain_ref, shift_ref, w_ref = refs[peers : peers + 3]
    hat_ref, feat_ref, kv_ref = refs[peers + 3 + olds :]
    rows = hat_ref.shape[1]
    for peer in range(peers):
        values = parts[peer][...].astype(F32)
        centered = values - jnp.mean(values, axis=-1, keepdims=True)
        variance = jnp.mean(centered * centered, axis=-1, keepdims=True)
        scaled = centered * lax.rsqrt(variance + EPSILON) * gain_ref[...]
        if peer == 0:
            hat_ref[...] = scaled.astype(BF).T
        low = (scaled + shift_ref[...]).astype(BF)
        found = nt(w_ref[0], low)
        heads, triple = feat_ref.shape[0], feat_ref.shape[1]
        hs = triple // 3
        spot = slice(peer * rows, (peer + 1) * rows)
        for head in range(heads):
            base = head * triple
            query = (found[base : base + hs] * 0.125).astype(BF)
            pair = found[base + hs : base + triple].astype(BF)
            feat_ref[head, :hs, spot] = query
            feat_ref[head, hs:, spot] = pair
            kv_ref[head, spot, :] = pair.T


def forward_kernel(ids_all, feat, kv, bias, *refs, size, groups, rows):
    outs = refs[:groups]
    mix_ref, stat_ref, cen_ref = refs[groups:]
    hs = feat.shape[1] // 3
    keys = kv.shape[1]
    count = keys // size
    clusters = bias.shape[2]
    kv_h, bias_h = kv.at[0], bias.at[0]
    queries_all, kvt = feat.at[0, :hs], feat.at[0, hs:]
    hot_all = one_hot_t(ids_all[0], clusters)
    ones = jnp.ones((16, keys), BF)
    sums = nt(jnp.concatenate([queries_all[...], ones], axis=0), hot_all)
    counts = sums[hs : hs + 1]
    centroid = (sums[:hs] / jnp.maximum(counts, 1.0)).astype(BF)
    padded = jnp.concatenate([centroid, jnp.zeros_like(centroid)], axis=0)

    def cluster_score(index):
        scores = nn(piece(kv_h, index, size, 0), padded)
        outside = piece(bias_h, index, size, 0).astype(F32) < 2.0 * NEGATIVE
        return jnp.where(outside, NEGATIVE, scores)

    def cluster_weigh(index, expo):
        top = piece(bias_h, index, size, 0).astype(F32) == 0.0
        mass = jnp.sum(jnp.where(top, expo, 0.0), axis=0, keepdims=True)
        other = jnp.where(top, 0.0, expo).astype(BF)
        return nn(piece(kvt, index, size, 1), other), mass

    peers = keys // (groups * rows)
    hots, sides = [], []
    for group in range(groups):
        spot = slice(group * peers * rows, group * peers * rows + rows)
        hot = one_hot_t(ids_all[0, :, spot], clusters)
        queries = queries_all[:, spot]
        hots.append(hot)
        sides.append(jnp.concatenate([queries, jnp.zeros_like(queries), hot], axis=0))

    def member_score(group, index):
        both = jnp.concatenate([piece(kv_h, index, size, 0), piece(bias_h, index, size, 0)], axis=1)
        return nn(both, sides[group])

    def member_weigh(index, expo):
        return (nn(piece(kvt, index, size, 1), expo.astype(BF)),)

    short = count <= 4
    ahead = None
    if short:
        ahead = [member_score(0, index) for index in range(count)]
    peak, denom, (rest, mass) = key_passes(keys, size, cluster_score, cluster_weigh)
    rest = rest[hs:] / denom
    mass = mass / denom
    blank = jnp.zeros((5, clusters), F32)
    stats = jnp.concatenate([rest, mass, peak + jnp.log(denom), counts, blank], axis=0)
    stat_ref[0] = stats
    cen_ref[0] = centroid
    high, low = split_low(stats)
    table = jnp.concatenate([high, low], axis=1)
    for group in range(groups):
        gathered = nn(table, jnp.concatenate([hots[group], hots[group]], axis=0))
        blocks, ahead = ahead, None
        if short and group + 1 < groups:
            ahead = [member_score(group + 1, index) for index in range(count)]
        score = functools.partial(member_score, group)
        peak, denom, (mix,) = key_passes(keys, size, score, member_weigh, blocks)
        mix = mix[hs:] / denom
        outs[group][...] = (gathered[hs : hs + 1] * mix + gathered[:hs]).astype(BF)
        level = jnp.broadcast_to(peak + jnp.log(denom), (8, rows))
        mix_ref[0, group] = jnp.concatenate([mix, level], axis=0)


def sums_kernel(info, ids_own, *refs, groups):
    grads, (mix_ref, part_ref) = refs[:groups], refs[groups:]
    hs = grads[0].shape[0]
    total = None
    for group in range(groups):
        rows = grads[group].shape[1]
        step = ids_own.shape[2] // groups
        hot = one_hot_t(ids_own[0, :, group * step : group * step + rows], part_ref.shape[2])
        grad = grads[group][...]
        along = jnp.sum(grad.astype(F32) * mix_ref[0, group, :hs], axis=0, keepdims=True)
        high, low = split_low(along)
        pad = jnp.zeros((14, rows), BF)
        part = nt(jnp.concatenate([grad, high, low, pad], axis=0), hot)
        total = part if total is None else total + part
    part_ref[0] = total


def back_kernel(ids_all, feat, kv, bias, *refs, size, groups, gots):
    grads = refs[:groups]
    mix_ref, stat_ref, cen_ref = refs[groups : groups + 3]
    shares = refs[groups + 3 : groups + 4 + gots]
    dq_ref, own_ref, send_ref, total, both = refs[groups + 4 + gots :]
    hs, rows = grads[0].shape
    keys = kv.shape[1]
    count = keys // size
    peers = keys // (groups * rows)
    clusters = bias.shape[2]
    kv_h, bias_h = kv.at[0], bias.at[0]
    queries_all, kvt = feat.at[0, :hs], feat.at[0, hs:]
    stats = stat_ref[0]
    high, low = split_low(stats[hs : hs + 8])
    table = jnp.concatenate([high, low], axis=1)
    hots, sides, levels, deltas, pads, rights = [], [], [], [], [], []
    for group in range(groups):
        spot = slice(group * peers * rows, group * peers * rows + rows)
        hot = one_hot_t(ids_all[0, :, spot], clusters)
        queries = queries_all[:, spot]
        blank = jnp.zeros_like(queries)
        hots.append(jnp.concatenate([hot, hot], axis=0))
        sides.append(jnp.concatenate([queries, blank, hot], axis=0))
        mass = nn(table, hots[group])[0:1]
        back = (mass * grads[group][...].astype(F32)).astype(BF)
        levels.append(mix_ref[0, group, hs : hs + 1])
        deltas.append(jnp.sum(back.astype(F32) * mix_ref[0, group, :hs], axis=0, keepdims=True))
        pads.append(jnp.concatenate([blank, back], axis=0))
        turned = jnp.concatenate([queries, blank], axis=0)
        rights.append(jnp.concatenate([turned, pads[group]], axis=1).T)

    def scores(group, index):
        kv_c = piece(kv_h, index, size, 0)
        pair = jnp.concatenate([kv_c, piece(bias_h, index, size, 0)], axis=1)
        return nn(pair, sides[group]), nn(kv_c, pads[group])

    def finish(group, index, found, dq):
        weights = jnp.exp(found[0] - levels[group])
        grad_s = (weights * (found[1] - deltas[group])).astype(BF)
        part = nn(jnp.concatenate([grad_s, weights.astype(BF)], axis=1), rights[group])
        spot = spot_of(index, size)
        if group == 0:
            total[spot, :] = part
        else:
            total[spot, :] += part
        return dq + nn(piece(kvt, index, size, 1), grad_s)

    rest, mass = stats[:hs], stats[hs : hs + 1]
    level, counts = stats[hs + 1 : hs + 2], stats[hs + 2 : hs + 3]
    centroid = cen_ref[0]
    part = shares[0][0]
    for share in shares[1:]:
        part = part + share[0]
    d_rest = part[:hs].astype(BF)
    d_mass = part[hs : hs + 1] + part[hs + 1 : hs + 2]
    delta = jnp.sum(d_rest.astype(F32) * rest, axis=0, keepdims=True) + d_mass * mass
    cen_pad = jnp.concatenate([centroid, jnp.zeros_like(centroid)], axis=0)
    rest_pad = jnp.concatenate([jnp.zeros_like(centroid), d_rest], axis=0)
    right = jnp.concatenate([cen_pad, rest_pad], axis=1).T

    def cluster_step(index, summed):
        kv_c = piece(kv_h, index, size, 0)
        marks = piece(bias_h, index, size, 0).astype(F32)
        probs = jnp.exp(nn(kv_c, cen_pad) - level)
        probs = jnp.where(marks < 2.0 * NEGATIVE, 0.0, probs)
        top = marks == 0.0
        d_probs = jnp.where(top, d_mass, nn(kv_c, rest_pad))
        d_score = (probs * (d_probs - delta)).astype(BF)
        other = jnp.where(top, 0.0, probs).astype(BF)
        both[spot_of(index, size), :] = jnp.concatenate([d_score, other], axis=1)
        return summed + nn(piece(kvt, index, size, 1), d_score)

    start = jnp.zeros((2 * hs, rows), F32)
    zero = jnp.zeros((2 * hs, clusters), F32)
    member_dq = []
    if count <= 4:
        tasks = [(group, index) for group in range(groups) for index in range(count)]
        ahead = scores(*tasks[0])
        d_cen = key_sum(keys, size, cluster_step, zero)
        dq = start
        for step, (group, index) in enumerate(tasks):
            found = ahead
            if step + 1 < len(tasks):
                ahead = scores(*tasks[step + 1])
            dq = finish(group, index, found, dq)
            if index == count - 1:
                member_dq.append(dq[:hs] * 0.125)
                dq = start
    else:
        d_cen = key_sum(keys, size, cluster_step, zero)
        for group in range(groups):

            def step(index, dq, group=group):
                return finish(group, index, scores(group, index), dq)

            member_dq.append(lax.fori_loop(0, count, step, start)[:hs] * 0.125)
    d_cen = d_cen[:hs] * 0.125 / jnp.maximum(counts, 1.0)
    high, low = split_low(d_cen)
    table = jnp.concatenate([high, low], axis=1)
    for group in range(groups):
        base = group * peers * rows
        dq_ref[group] = (member_dq[group] + nn(table, hots[group])).astype(BF)
        own = total[base : base + rows, :] + nn(both[base : base + rows, :], right)
        own_ref[0, :, group * rows : (group + 1) * rows] = own.T
        for peer in range(1, peers):
            spot = (peer - 1) * groups * rows + group * rows
            found = total[base + peer * rows : base + (peer + 1) * rows, :]
            send_ref[0, :, spot : spot + rows] = found.astype(BF).T


def join_kernel(dq_ref, own_ref, *refs, groups):
    gots, outs = refs[:-groups], refs[-groups:]
    heads, _, rows = outs[0].shape
    hs = dq_ref.shape[1] // heads
    for head in range(heads):
        for group in range(groups):
            spot = slice(group * rows, (group + 1) * rows)
            pair = own_ref[head, :, spot]
            for got in gots:
                pair = pair + got[head, :, spot].astype(F32)
            outs[group][head, :hs] = dq_ref[group, head * hs : (head + 1) * hs]
            outs[group][head, hs:] = pair.astype(BF)


def block_kernel(info, *refs, groups, chunks, fast):
    (attn, rest) = (refs[:groups], refs[groups:])
    x_ref, gain_ref, shift_ref, wo_ref, up_ref, down_ref, cot_ref = rest[:7]
    out_ref, dres_ref = rest[7:9]
    if fast:
        far_ref, low_far, act_ref, low_ref = rest[9:13]
        rest = rest[13:]
        hidden = far_ref.shape[1] * 4 // 7
    else:
        dn_ref, dup_ref, dbr_ref, act_ref, low_ref = rest[9:14]
        rest = rest[14:]
    dat = rest[:groups]
    hat_ref, inv_ref, normed, back, total = rest[groups:]
    index = pl.program_id(0)

    @pl.when(index == 0)
    def before():
        resid = x_ref[...].astype(F32)
        for group in range(groups):
            owner = lax.rem(info[0] + groups - group, groups)
            resid = resid + tn(attn[group][...], wo_ref[owner])
        total[...] = resid
        centered = resid - jnp.mean(resid, axis=-1, keepdims=True)
        variance = jnp.mean(centered * centered, axis=-1, keepdims=True)
        inverse = lax.rsqrt(variance + EPSILON)
        hat = centered * inverse
        hat_ref[...] = hat
        inv_ref[...] = jnp.broadcast_to(inverse, inv_ref.shape)
        low = (hat * gain_ref[...] + shift_ref[...]).astype(BF)
        normed[...] = low
        if fast:
            feats = attn[0].shape[0]
            half = feats // 2
            turned = low.T
            for group in range(groups):
                first = turned[group * feats : group * feats + half]
                second = turned[group * feats + half : (group + 1) * feats]
                spot = slice(group * half, (group + 1) * half)
                low_ref[spot, :] = jnp.where(info[1] == 0, first, second)
                low_far[spot, :] = jnp.where(info[1] == 0, second, first)
                first = attn[group][:half]
                second = attn[group][half:]
                spot = slice((groups + group) * half, (groups + group + 1) * half)
                low_ref[spot, :] = jnp.where(info[1] == 0, first, second)
                low_far[spot, :] = jnp.where(info[1] == 0, second, first)
        else:
            low_ref[...] = low
        back[...] = jnp.zeros_like(back)

    up = nn(normed[...], up_ref[...])
    grad_act = nt(cot_ref[...], down_ref[...])
    square = up * up
    inner = GELU_A * (up + GELU_B * up * square)
    curve = jnp.tanh(inner)
    act = (0.5 * up * (1.0 + curve)).astype(BF)
    slope = 0.5 * (1.0 + curve) + 0.5 * up * (1.0 - curve * curve) * (
        GELU_A * (1.0 + 3.0 * GELU_B * square)
    )
    d_up = (grad_act * slope).astype(BF)
    if fast:
        part = act.shape[1]
        half = part // 2
        first, second = act[:, :half], act[:, half:]
        act_ref[...] = jnp.where(info[1] == 0, first, second)
        far_ref[:, pl.ds(pl.multiple_of(index * part, part), part)] = d_up
        spot = pl.ds(pl.multiple_of(hidden + index * half, half), half)
        far_ref[:, spot] = jnp.where(info[1] == 0, second, first)
    else:
        dup_ref[...] = d_up
        act_ref[...] = act
    back[...] += nt(d_up, up_ref[...])
    total[...] += nn(act, down_ref[...])

    @pl.when(index == chunks - 1)
    def after():
        out_ref[...] = total[...].astype(BF)
        d_normed = back[...]
        hat = hat_ref[...]
        gain_part = jnp.sum(d_normed * hat, axis=0, keepdims=True)
        shift_part = jnp.sum(d_normed, axis=0, keepdims=True)
        if fast:
            rows, width = low_far.shape[1], d_normed.shape[1]
            fold = []
            for part_row in split_low(gain_part) + split_low(shift_part):
                fold += [part_row[:, k : k + rows].astype(F32) for k in range(0, width, rows)]
            fold.append(jnp.zeros((low_far.shape[0] - width - len(fold), rows), F32))
            folded = jnp.concatenate(fold, axis=0).astype(BF)
            low_far[width:, :] = folded
            low_ref[width:, :] = folded
        else:
            blank = jnp.zeros((6, d_normed.shape[1]), F32)
            dn_ref[...] = jnp.concatenate([gain_part, shift_part, blank], axis=0)
        gy = d_normed * gain_ref[...]
        mean_one = jnp.mean(gy, axis=-1, keepdims=True)
        mean_two = jnp.mean(gy * hat, axis=-1, keepdims=True)
        d_resid = cot_ref[...].astype(F32) + inv_ref[:, 0:1] * (gy - mean_one - hat * mean_two)
        dres_ref[...] = d_resid
        branch = d_resid.astype(BF)
        if fast:
            far_ref[:, hidden * 3 // 2 :] = branch
        else:
            dbr_ref[...] = branch
        for group in range(groups):
            owner = lax.rem(info[0] + groups - group, groups)
            dat[group][...] = nt(wo_ref[owner], branch).astype(BF)


def weights_kernel(info, *refs, groups):
    (dup, dup_got, dbr, dbr_got, act, act_got, low, low_got, cot, cot_got) = refs[:10]
    send_u, keep_u, send_d, keep_d, outs = refs[10:13], refs[13], refs[14:17], refs[17], refs[18]
    width = cot.shape[1]
    lead = send_u[0].shape[2]

    def leave(send, turn, spot, block, first):
        if turn:
            send[2][0, spot, first : first + block.shape[0]] = block
        elif first:
            send[1][0, spot, first - lead : first - lead + block.shape[0]] = block
        else:
            send[0][0, spot] = block[:lead]
            send[1][0, spot, : block.shape[0] - lead] = block[lead:]

    index = pl.program_id(0)
    group_at, place_u, place_d = info[0], info[3], info[4]
    rows = width // (2 * groups)
    quarter = rows // 4
    stay = groups * rows

    @pl.when(index == 0)
    def first():
        found = nn(low[stay:width, :], dbr[...]) + nn(low_got[stay:width, :], dbr_got[...])
        fold = low[width:, :].astype(F32) + low_got[width:, :].astype(F32)
        times = width // fold.shape[1]
        norms = []
        for part in range(2):
            both = fold[2 * part * times : (2 * part + 1) * times]
            both = both + fold[(2 * part + 1) * times : (2 * part + 2) * times]
            norms.append(jnp.concatenate([both[k : k + 1] for k in range(times)], axis=1))
        norms = jnp.concatenate(norms + [jnp.zeros((6, width), F32)], axis=0)
        for group in range(groups):
            block = found[group * rows : (group + 1) * rows]
            outs[group] = block
            for part in range(4):
                tail = block[part * quarter + 16 : (part + 1) * quarter]
                tail = jnp.concatenate([tail, norms], axis=0).astype(BF)
                place = lax.bitwise_xor(part, place_d)

                for turn in range(2):

                    @pl.when(place == 2 + turn)
                    def leaves_more(turn=turn, tail=tail, group=group):
                        leave(send_d, turn, (groups - group) % groups, tail, rows)

                @pl.when(place < 2)
                def stays_more():
                    keep_d[place, (groups - group) % groups, rows:] = tail

    up = nn(low[:stay, :], dup[...]) + nn(low_got[:stay, :], dup_got[...])
    at = lax.bitwise_xor(lax.bitwise_xor(index, 2), place_u)
    for group in range(groups):
        spot = lax.rem(group + groups - group_at, groups)
        block = up[group * rows : (group + 1) * rows].astype(BF)
        away = (groups - group) % groups
        start = pl.multiple_of(at * quarter, 8)
        other = outs[group, pl.ds(start, 16), :].astype(BF)

        for turn in range(2):

            @pl.when(index == turn)
            def leaves(turn=turn, spot=spot, block=block, away=away, other=other):
                leave(send_u, turn, spot, block, 0)
                leave(send_u, turn, away, other, rows)

        @pl.when(index >= 2)
        def stays():
            keep_u[0, spot, :rows] = block
            keep_u[0, away, rows:] = other

    down = tn(act[...], cot[...]) + tn(act_got[...], cot_got[...])
    spot = lax.rem(index + groups - group_at, groups)
    for part in range(4):
        block = down[part * rows : (part + 1) * rows].astype(BF)
        place = lax.bitwise_xor(part, place_d)

        for turn in range(2):

            @pl.when(place == 2 + turn)
            def leaves_down(turn=turn, block=block):
                leave(send_d, turn, spot, block, 0)

        @pl.when(place < 2)
        def stays_down():
            keep_d[place, spot, :rows] = block


def second_kernel(keep_u, got_u, keep_d, got_d, inner, inner_got, late_u, late_d, to_y, to_x, to_xy):
    rows, lines = keep_u.shape[2], inner.shape[2]
    to_y[:, :rows] = (keep_u[0].astype(F32) + got_u[0].astype(F32)).astype(BF)
    to_x[:, :rows] = (keep_d[0].astype(F32) + got_d[0].astype(F32)).astype(BF)
    to_y[:, rows : rows + lines] = (inner[1].astype(F32) + inner_got[1].astype(F32)).astype(BF)
    to_x[:, rows : rows + lines] = (inner[2].astype(F32) + inner_got[2].astype(F32)).astype(BF)
    to_xy[...] = (inner[3].astype(F32) + inner_got[3].astype(F32)).astype(BF)
    to_y[:, rows + lines :] = late_d[0]
    to_x[:, rows + lines :] = late_u[0]


def third_kernel(info, keep_u, one_u, keep_d, one_d, by_y, by_x, inner, inner_got, by_xy, *outs):
    rows, lead, lines = keep_u.shape[2], one_u.shape[2], inner.shape[2]
    groups = len(outs) // 2
    left = rows - lead
    head, tail, late = slice(0, lead), slice(lead, rows), slice(rows + lines, None)
    mid = slice(rows, rows + lines)

    def added(keep, got, by, group, spot):
        total = keep[0, group, spot].astype(F32) + got.astype(F32)
        return (total + by[group, spot].astype(F32)).astype(BF)

    for group in range(groups):
        first, last = outs[group], outs[groups + group]
        first[:lead] = added(keep_u, one_u[0, group], by_y, group, head)
        first[lead:] = added(keep_d, one_d[0, group], by_x, group, head)
        last[:left] = added(keep_u, by_x[group, late], by_y, group, tail)
        last[left : 2 * left] = added(keep_d, by_y[group, late], by_x, group, tail)
        both = inner[0, group].astype(F32) + inner_got[0, group].astype(F32)
        both = both + by_y[group, mid].astype(F32) + by_x[group, mid].astype(F32)
        last[2 * left :] = (both + by_xy[group].astype(F32)).astype(BF)


def fourth_kernel(info, *refs, groups, high, feats):
    parts, out = refs[:groups], refs[groups]
    total = parts[0][: 2 * high].astype(F32)
    for part in parts[1:]:
        total = total + part[: 2 * high].astype(F32)
    out[: 2 * high] = total.astype(BF)
    if parts[0].shape[0] == 2 * high:
        return
    turned = refs[groups + 1]
    third = feats // 3
    lines = turned.shape[1]
    for group in range(groups):
        turned[group] = parts[group][2 * high :].astype(F32)
    for kind in range(3):
        found = []
        for owner in range(groups):
            spot = lax.rem(info[0] + groups - owner, groups)
            found.append(turned[spot, :, kind * third : (kind + 1) * third])
        at = 2 * high + kind * lines
        out[at : at + lines] = jnp.concatenate(found, axis=1).astype(BF)


def spread_kernel(info, *refs, lead, high):
    firsts, lasts, (wq, wkv, pair) = refs[:4], refs[4:8], refs[8:11]
    up_ref, out_ref, down_ref, norm_ref, gq_ref, gkv_ref, vec_ref, sums = refs[11:]
    index = pl.program_id(0)
    rows, width = down_ref.shape
    quarter = rows // 4
    lines = quarter + 8
    left = rows - lead
    order_u, order_d = (0, 2, 1, 3), (0, 1, 2, 3)

    @pl.when(index == 0)
    def first():
        for place, source in enumerate(order_u):

            @pl.when(info[3] == place)
            def take(source=source):
                for kind in range(3):
                    at = 2 * high + kind * lines
                    sums[kind] = lasts[source][at : at + lines].astype(F32)[quarter:]

    for place, source in enumerate(order_u):

        @pl.when(index == place)
        def upper(source=source):
            part = lasts[source]
            up_ref[:lead] = firsts[source][:lead].astype(F32)
            up_ref[lead:] = part[:left].astype(F32)
            at = pl.multiple_of(lax.bitwise_xor(index, info[3]) * quarter, 8)
            out_ref[pl.ds(at, 16), :] = part[left:high].astype(F32)
            spot = pl.ds(at, quarter)
            shift, gain = pair[spot, 0:1], pair[spot, 1:2]
            gain_sum, shift_sum = 0.0, 0.0
            for kind in range(3):
                base = 2 * high + kind * lines
                block = part[base : base + lines].astype(F32)[:quarter]
                line = sums[kind, 0:1]
                if kind == 0:
                    weight = wq[spot, :]
                    gq_ref[spot, :] = block + shift * line
                else:
                    lanes = slice((kind - 1) * width, kind * width)
                    weight = wkv[spot, lanes]
                    gkv_ref[spot, lanes] = block + shift * line
                gain_sum = gain_sum + jnp.sum(weight * block, axis=1, keepdims=True)
                shift_sum = shift_sum + jnp.sum(weight * line, axis=1, keepdims=True)
            lane = lax.broadcasted_iota(jnp.int32, (quarter, vec_ref.shape[1]), 1)
            vec_ref[spot, :] = jnp.where(lane == 0, gain_sum / gain, shift_sum)

    for place, source in enumerate(order_d):

        @pl.when(index == place)
        def lower(source=source):
            part = lasts[source]
            down_ref[:lead] = firsts[source][lead:].astype(F32)
            down_ref[lead:] = part[high : high + left].astype(F32)
            tail = part[high + left : 2 * high].astype(F32)
            at = pl.multiple_of(lax.bitwise_xor(index, info[4]) * quarter + 16, 8)
            out_ref[pl.ds(at, quarter - 16), :] = tail[: quarter - 16]

            @pl.when(lax.bitwise_xor(index, info[4]) == 0)
            def norms():
                norm_ref[...] = tail[quarter - 16 :]


def inward_kernel(info, *refs, groups, gots, fast):
    join_refs, hat_ref = refs[: 2 + gots], refs[2 + gots]
    parts = refs[3 + gots : 3 + gots + groups]
    outs = refs[3 + gots + groups :]
    join_kernel(*join_refs, *parts, groups=groups)
    heads, triple, rows = parts[0].shape
    hs = triple // 3
    total, sums = None, None
    ones = jnp.ones((16, rows), BF)
    for group in range(groups):
        order = [parts[group][h, k * hs : (k + 1) * hs] for k in range(3) for h in range(heads)]
        turned = jnp.concatenate(order, axis=0)
        found = nt(hat_ref[:, group * rows : (group + 1) * rows], turned)
        more = nt(ones, turned)
        total = found if total is None else total + found
        sums = more if sums is None else sums + more
    if not fast:
        outs[0][...] = total
        outs[1][...] = sums
        return
    own_ref, far_ref = outs
    block = total.shape[0] // (2 * groups)
    quarter = block // 4
    wide = total.shape[1]
    edge = wide // 128 * 128
    blank = jnp.zeros(own_ref.shape[:3] + (own_ref.shape[3] - edge,), BF)
    own_ref[..., edge:] = blank
    far_ref[..., edge:] = blank
    for group in range(groups):
        spot = lax.rem(group + groups - info[0], groups)
        for part in range(4):
            place = lax.bitwise_xor(part, info[3])
            found = []
            for parity in range(2):
                at = (2 * group + parity) * block + part * quarter
                lines = jnp.concatenate([total[at : at + quarter], sums[:8]], axis=0)
                found.append(lines.astype(BF))
            own_ref[place, spot, :, :wide] = jnp.where(info[1] == 0, found[0], found[1])
            far_ref[place, spot, :, :wide] = jnp.where(info[1] == 0, found[1], found[0])


def final_kernel(info, *refs, groups):
    parts = refs[:groups]
    x_ref, dres_ref, gain_ref, w_ref, out_ref = refs[groups:]
    d_normed = jnp.zeros(dres_ref.shape, F32)
    for group in range(groups):
        owner = lax.rem(info[0] + groups - group, groups)
        heads, triple, rows = parts[group].shape
        d_normed = d_normed + tn(parts[group][...].reshape(heads * triple, rows), w_ref[owner])
    values = x_ref[...].astype(F32)
    centered = values - jnp.mean(values, axis=-1, keepdims=True)
    variance = jnp.mean(centered * centered, axis=-1, keepdims=True)
    inverse = lax.rsqrt(variance + EPSILON)
    hat = centered * inverse
    gy = d_normed * gain_ref[...]
    mean_one = jnp.mean(gy, axis=-1, keepdims=True)
    mean_two = jnp.mean(gy * hat, axis=-1, keepdims=True)
    out_ref[...] = (dres_ref[...] + inverse * (gy - mean_one - hat * mean_two)).astype(BF)


def ordered(kernel, inputs, later):
    def run(*refs):
        kernel(*refs[:inputs], *refs[inputs + later :])

    return run if later else kernel


def whole(shape):
    return pl.BlockSpec(shape, lambda *at: (0,) * len(shape))


def per_device(
    tokens,
    cluster_ids,
    lengths,
    top_keys,
    gain_one,
    shift_one,
    w_query,
    w_keyval,
    w_out,
    gain_two,
    shift_two,
    w_up,
    w_down,
    cotangent,
):
    rows, width = tokens.shape
    heads = cluster_ids.shape[1]
    hs = width // heads
    hidden = w_up.shape[1]
    wide = lax.axis_size("wide")
    n_dp = lax.axis_size("dp")
    groups = math.gcd(heads, wide)
    peers = wide // groups
    own_heads = heads // groups
    own_clusters = top_keys.shape[2]
    clusters = own_clusters * wide
    picks = top_keys.shape[3]
    seq = rows * wide
    size = 512 if seq <= 2048 else 2048
    feats = own_heads * hs
    block_rows = width // wide
    fast = peers == 2 and n_dp == 4 and block_rows == 96 and hidden == 4 * width and width % 256 == 0 and rows % 128 == 0
    me = lax.axis_index("wide")
    group_at, peer_at = me // peers, me % peers
    dp_at = lax.axis_index("dp")
    seq_len = lengths[0]
    bit_x, bit_y = dp_at % 2, (dp_at // 2) % 2
    place_u, place_d = 2 * bit_x + bit_y, 2 * bit_y + bit_x
    info = jnp.stack([group_at, peer_at, seq_len, place_u, place_d, me]).astype(jnp.int32)

    def along_groups(values, hop):
        pairs = [(i, ((i // peers + hop) % groups) * peers + i % peers) for i in range(wide)]
        return lax.ppermute(values, "wide", pairs)

    def along_peers(values, hop):
        pairs = [(i, (i // peers) * peers + (i % peers + hop) % peers) for i in range(wide)]
        return lax.ppermute(values, "wide", pairs)

    def along_dp(values, mask):
        return lax.ppermute(values, "dp", [(i, i ^ mask) for i in range(n_dp)])

    def prefetched(
        kernel, grid, in_specs, out_specs, out_shape, mib, spent, name, scratch=(), alias=None, first=()
    ):
        first = jax.tree.leaves(first)
        call = pl.pallas_call(
            ordered(kernel, 1 + len(in_specs), len(first)),
            grid_spec=pltpu.PrefetchScalarGridSpec(
                num_scalar_prefetch=1,
                grid=grid,
                in_specs=in_specs + [pl.BlockSpec(memory_space=pl.ANY)] * len(first),
                out_specs=out_specs,
                scratch_shapes=list(scratch),
            ),
            out_shape=out_shape,
            compiler_params=params(mib, len(grid)),
            cost_estimate=spent,
            input_output_aliases=alias or {},
            name=name,
        )
        return lambda *inputs: call(*inputs, *first)

    def after(values, *others):
        return lax.optimization_barrier((values, others))[0]

    def scalar(spec):
        return pl.BlockSpec(spec.block_shape, lambda *at: spec.index_map(*at[:-1]))

    def array(shape, dtype):
        return jax.ShapeDtypeStruct(shape, dtype)

    position = me * rows + jnp.arange(rows, dtype=jnp.int32)
    marked = jnp.where((position < seq_len)[:, None], cluster_ids, -1).T
    tops = jnp.zeros((heads, picks, clusters), jnp.int32)
    tops = lax.dynamic_update_slice(
        tops, top_keys[0].transpose(0, 2, 1), (0, 0, me * own_clusters)
    )
    lines = rows // clusters
    packed = jnp.concatenate([tops, marked.reshape(heads, lines, clusters)], axis=1)
    early = [along_peers(tokens, -hop) for hop in range(1, peers)]
    packed = after(packed.reshape(groups, own_heads, picks + lines, clusters), early)

    def of_heads(hop):
        return lax.dynamic_index_in_dim(packed, (group_at + groups - hop) % groups, keepdims=False)

    arrived = [of_heads(0)] + [along_groups(of_heads(hop), -hop) for hop in range(1, groups)]

    mine = {0: tokens, 1: along_groups(tokens, -1)}
    if groups > 2:
        mine[groups - 1] = along_groups(tokens, 1)
    ready = after(tokens, arrived)
    for hop in range(2, groups - 1):
        mine[hop] = along_groups(ready, -hop)

    w_in = jnp.concatenate([w_query, w_keyval], axis=1).T.reshape(3, heads, hs, width)
    w_in = w_in.transpose(1, 0, 2, 3).reshape(groups, 3 * feats, width)
    table_shape = (own_heads, picks + groups * lines, clusters)
    table = prefetched(
        functools.partial(table_kernel, picks=picks),
        (1,),
        [whole((own_heads, picks + lines, clusters))] * groups,
        whole(table_shape),
        array(table_shape, jnp.int32),
        8,
        cost(1e5, 1e6),
        "table",
        first=w_in,
    )(info, *arrived)
    tables = [table] + [along_peers(table, -hop) for hop in range(1, peers)]
    cot_got = [along_peers(after(cotangent, arrived), hop) for hop in range(1, peers)]
    cot_got = cot_got if fast else []
    bias, ids_all = prefetched(
        functools.partial(bias_kernel, groups=groups, peers=peers, rows=rows, picks=picks),
        (wide,),
        [whole(table_shape)] * peers,
        [
            pl.BlockSpec((own_heads, rows, clusters), lambda i, s: (0, i, 0)),
            whole((own_heads, 1, seq)),
        ],
        [array((own_heads, seq, clusters), BF), array((own_heads, 1, seq), jnp.int32)],
        12 if fast else 60,
        cost(own_heads * seq * clusters * picks * 8, own_heads * seq * clusters * 2),
        "bias",
    )(info, *tables)

    gain_row, shift_row = gain_one[None, :], shift_one[None, :]
    shapes = [
        array((width, groups * rows), BF),
        array((own_heads, 3 * hs, seq), BF),
        array((own_heads, seq, 2 * hs), BF),
    ]
    held = []
    split_peers = peers if peers <= 2 else 1
    for group in sorted(range(groups), key=lambda g: min(g, groups - g)):
        arrival = mine[group]
        first = ()
        if group == 1:
            arrival = after(arrival, bias, held, cot_got, [mine[hop] for hop in range(2, groups)])
        chunk = [arrival]
        chunk += early if group == 0 else [along_peers(arrival, -hop) for hop in range(1, peers)]
        if peers > 2:
            chunk = [jnp.concatenate(chunk, axis=0)]
        span = peers * rows
        if peers > 2:
            specs_in = [pl.BlockSpec((rows, width), lambda p, s: (p, 0))]
            grid = (peers,)
            outs = [
                pl.BlockSpec((width, rows), lambda p, s, g=group: (0, g)),
                pl.BlockSpec((own_heads, 3 * hs, rows), lambda p, s, g=group: (0, 0, g * peers + p)),
                pl.BlockSpec((own_heads, rows, 2 * hs), lambda p, s, g=group: (0, g * peers + p, 0)),
            ]
        else:
            specs_in = [whole((rows, width))] * split_peers
            grid = (1,)
            outs = [
                pl.BlockSpec((width, rows), lambda p, s, g=group: (0, g)),
                pl.BlockSpec((own_heads, 3 * hs, span), lambda p, s, g=group: (0, 0, g)),
                pl.BlockSpec((own_heads, span, 2 * hs), lambda p, s, g=group: (0, g, 0)),
            ]
        old = 1 + split_peers + 3
        held = prefetched(
            functools.partial(project_kernel, peers=split_peers, olds=len(held)),
            grid,
            specs_in
            + [
                whole((1, width)),
                whole((1, width)),
                pl.BlockSpec((1, 3 * feats, width), lambda p, s: (s[0], 0, 0)),
            ]
            + [pl.BlockSpec(memory_space=pl.ANY)] * len(held),
            outs,
            shapes,
            16 if fast else 60,
            cost(6 * span * width * feats, span * width * 4),
            "project",
            alias={old + k: k for k in range(len(held))},
            first=first,
        )(info, *chunk, gain_row, shift_row, w_in, *held)
    hat_own, feat, kv = held

    ids_full = pl.BlockSpec((1, 1, seq), lambda h, r: (h, 0, 0))
    feat_full = pl.BlockSpec((1, 3 * hs, seq), lambda h, r: (h, 0, 0))
    kv_full = pl.BlockSpec((1, seq, 2 * hs), lambda h, r: (h, 0, 0))
    bias_full = pl.BlockSpec((1, seq, clusters), lambda h, r: (h, 0, 0))
    head_rows = pl.BlockSpec((hs, rows), lambda h, r: (h, 0))
    mix_spec = pl.BlockSpec((1, 1, hs + 8, rows), lambda h, r: (h, r, 0, 0))
    stat_spec = pl.BlockSpec((1, hs + 8, clusters), lambda h, r: (h, 0, 0))
    cen_spec = pl.BlockSpec((1, hs, clusters), lambda h, r: (h, 0, 0))
    own_rows = groups * rows
    pair_flops = own_heads * own_rows * seq * 256

    one = [
        pl.BlockSpec(spec.block_shape, functools.partial(lambda h, f: f(h, 0), f=spec.index_map))
        for spec in (ids_full, feat_full, kv_full, bias_full, stat_spec, cen_spec, head_rows)
    ]
    ids_one, feat_one, kv_one, bias_one, stat_one, cen_one, rows_one = one
    part_one = pl.BlockSpec((1, hs + 16, clusters), lambda h: (h, 0, 0))
    mix_one = pl.BlockSpec((1, groups, hs + 8, rows), lambda h: (h, 0, 0, 0))
    all_groups = pl.BlockSpec((groups, hs, rows), lambda h: (0, h, 0))
    own_one = pl.BlockSpec((1, own_rows, 2 * hs), lambda h: (h, 0, 0))
    results = pl.pallas_call(
        functools.partial(forward_kernel, size=size, groups=groups, rows=rows),
        grid=(own_heads,),
        in_specs=[ids_one, feat_one, kv_one, bias_one],
        out_specs=[rows_one] * groups + [mix_one, stat_one, cen_one],
        out_shape=[array((feats, rows), BF)] * groups
        + [
            array((own_heads, groups, hs + 8, rows), F32),
            array((own_heads, hs + 8, clusters), F32),
            array((own_heads, hs, clusters), BF),
        ],
        compiler_params=params(32 if fast else 60, 1),
        cost_estimate=cost(6 * pair_flops, 8e6, own_heads * own_rows * seq),
        name="attend",
    )(ids_all, feat, kv, bias)
    attn_t = results[:groups]
    mixed, stats, centroid = results[groups:]

    arrived = [attn_t[0]] + [along_groups(attn_t[hop], hop) for hop in range(1, groups)]

    chunks = 4
    part = hidden // chunks
    lead = 64
    w_out_g = w_out.reshape(groups, feats, width)
    gain_row2, shift_row2 = gain_two[None, :], shift_two[None, :]
    square = whole((rows, width))
    column = pl.BlockSpec((rows, part), lambda i, s: (0, i))
    norm_spec = whole((8, width))
    if fast:
        kept_shapes = [
            array((rows, hidden + hidden // 2 + width), BF),
            array((width + 16, rows), BF),
            array((rows, hidden // 2), BF),
            array((width + 16, rows), BF),
        ]
        kept_specs = [whole(item.shape) for item in kept_shapes]
        kept_specs[2] = pl.BlockSpec((rows, part // 2), lambda i, s: (0, i))
    else:
        kept_shapes = [
            array((8, width), F32),
            array((rows, hidden), BF),
            array((rows, width), BF),
            array((rows, hidden), BF),
            array((rows, width), BF),
        ]
        kept_specs = [norm_spec, column, square, column, square]
    results = prefetched(
        functools.partial(block_kernel, groups=groups, chunks=chunks, fast=fast),
        (chunks,),
        [whole((feats, rows))] * groups
        + [
            square,
            whole((1, width)),
            whole((1, width)),
            whole((groups, feats, width)),
            pl.BlockSpec((width, part), lambda i, s: (0, i)),
            pl.BlockSpec((part, width), lambda i, s: (i, 0)),
            square,
        ],
        [square, square] + kept_specs + [whole((feats, rows))] * groups,
        [array((rows, width), BF), array((rows, width), F32)]
        + kept_shapes
        + [array((feats, rows), BF)] * groups,
        28 if fast else 60,
        cost(8 * rows * width * hidden, 4 * width * hidden, rows * hidden),
        "feed",
        scratch=[
            pltpu.VMEM((rows, width), F32),
            pltpu.VMEM((rows, 128), F32),
            pltpu.VMEM((rows, width), BF),
            pltpu.VMEM((rows, width), F32),
            pltpu.VMEM((rows, width), F32),
        ],
    )(info, *arrived, tokens, gain_row2, shift_row2, w_out_g, w_up, w_down, cotangent)
    output, d_resid = results[:2]
    kept, d_attn = results[2:-groups], results[-groups:]
    grads = [d_attn[0]] + [along_groups(d_attn[hop], -hop) for hop in range(1, groups)]

    def weight_parts():
        far, low_far, act_own, low_own = kept
        got, low_got = along_peers(far, 1), along_peers(low_far, 1)
        high = block_rows + 16
        chunk = pl.BlockSpec((rows, part), lambda i, s: (0, i ^ 2 ^ s[3]))
        branch = pl.BlockSpec((rows, width), lambda i, s: (0, hidden * 3 // 2 // width))
        act_spec = pl.BlockSpec((rows, part // 2), lambda i, s: (0, i))
        act_there = pl.BlockSpec((rows, part // 2), lambda i, s: (0, 2 * hidden // part + i))
        low_spec = whole((width + 16, rows))
        shape_u = (2, groups, high, width)
        shape_d = (2, groups, high, width)
        parts = [(1, groups, tall, width) for tall in (lead, high - lead, high)]
        results = prefetched(
            functools.partial(weights_kernel, groups=groups),
            (4,),
            [chunk, chunk, branch, branch, act_spec, act_there, low_spec, low_spec, square, square],
            [whole(item) for item in parts]
            + [pl.BlockSpec((1,) + shape_u[1:], lambda i, s: (jnp.maximum(i - 2, 0), 0, 0, 0))]
            + [whole(item) for item in parts]
            + [whole(shape_d)],
            ([array(item, BF) for item in parts] + [array(shape_u, BF)]) * 2,
            28,
            cost(8 * rows * width * hidden, 6 * width * hidden),
            "weights",
            scratch=[pltpu.VMEM((groups, block_rows, width), F32)],
        )(info, far, got, far, got, act_own, got, low_own, low_got, cotangent, *cot_got)
        return results[:3], results[3], results[4:7], results[7]

    def weight_second(keep_u, got_u, keep_d, got_d, inner, inner_got, late_u, late_d):
        def block(shape, at):
            return pl.BlockSpec((1,) + shape[1:], lambda i: (at, 0, 0, 0))

        high, lines = keep_u.shape[2], inner.shape[2]
        shapes = [(groups, high + lines + late_u.shape[2], width)] * 2 + [(groups, lines, width)]
        return pl.pallas_call(
            second_kernel,
            grid=(1,),
            in_specs=[
                block(item.shape, item.shape[0] - 1) for item in (keep_u, got_u, keep_d, got_d)
            ]
            + [whole(item.shape) for item in (inner, inner_got, late_u, late_d)],
            out_specs=[whole(shape) for shape in shapes],
            out_shape=[array(shape, BF) for shape in shapes],
            compiler_params=params(24, 1),
            cost_estimate=cost(groups * high * width * 2, groups * high * width * 12),
            name="second",
        )(keep_u, got_u, keep_d, got_d, inner, inner_got, late_u, late_d)

    def weight_third(keep_u, got_u, keep_d, got_d, by_y, by_x, inner, inner_got, by_xy):
        def block(shape, at):
            return pl.BlockSpec((1,) + shape[1:], lambda i, s: (at, 0, 0, 0))

        left = keep_u.shape[2] - lead
        talls = [(2 * lead, width)] * groups + [(2 * left + inner.shape[2], width)] * groups
        more = (by_y, by_x)
        return prefetched(
            third_kernel,
            (1,),
            [block(item.shape, 0) for item in (keep_u, got_u, keep_d, got_d)]
            + [whole(by_y.shape), whole(by_x.shape)]
            + [block(inner.shape, 0)] * 2
            + [whole(by_xy.shape)],
            [whole(tall) for tall in talls],
            [array(tall, BF) for tall in talls],
            24,
            cost(groups * 256 * width * 4, groups * 256 * width * 8),
            "third",
            first=home,
        )(info, keep_u, got_u, keep_d, got_d, by_y, by_x, inner, inner_got, by_xy)

    def weight_fourth(came, high, lines, first):
        tall = 2 * high + 3 * lines
        done = prefetched(
            functools.partial(fourth_kernel, groups=groups, high=high, feats=3 * feats),
            (1,),
            [whole(came[0].shape)] * groups,
            whole((tall, width)),
            array((tall, width), BF),
            16,
            cost(groups * tall * width, groups * tall * width * 2),
            "fourth",
            scratch=[pltpu.VMEM((groups, lines, width), F32)] if lines else [],
            first=first,
        )(info, *came)
        return [done] + [along_dp(done, mask) for mask in (1, 2, 3)]

    def weight_spread(firsts, lasts, high, ready):
        at = me * block_rows
        wq_rows = lax.dynamic_slice_in_dim(w_query, at, block_rows).astype(F32)
        wkv_rows = lax.dynamic_slice_in_dim(w_keyval, at, block_rows).astype(F32)
        pair = jnp.stack([shift_one, gain_one] + [shift_one] * 6, axis=1)
        pair = lax.dynamic_slice_in_dim(pair, at, block_rows)
        return prefetched(
            functools.partial(spread_kernel, lead=lead, high=high),
            (4,),
            [whole(item.shape) for item in firsts + lasts]
            + [whole(wq_rows.shape), whole(wkv_rows.shape), whole(pair.shape)],
            [
                pl.BlockSpec((block_rows, part), lambda i, s: (0, i ^ s[3])),
                whole((block_rows, width)),
                pl.BlockSpec((block_rows, width), lambda i, s: (i ^ s[4], 0)),
                whole((8, width)),
                whole((block_rows, width)),
                whole((block_rows, 2 * width)),
                whole((block_rows, 128)),
            ],
            [
                array((block_rows, hidden), F32),
                array((block_rows, width), F32),
                array((hidden // wide, width), F32),
                array((8, width), F32),
                array((block_rows, width), F32),
                array((block_rows, 2 * width), F32),
                array((block_rows, 128), F32),
            ],
            20,
            cost(1e6, 8 * block_rows * width * 6),
            "spread",
            scratch=[pltpu.VMEM((3, 8, width), F32)],
        )(info, *firsts, *lasts, wq_rows, wkv_rows, pair)

    masks = [1 << k for k in range(n_dp.bit_length() - 1)]

    def reduce_rows(partial):
        blocks = partial.reshape(groups, peers, partial.shape[0] // wide, partial.shape[1])

        def of_peer(hop):
            at = (peer_at + hop) % peers
            return lax.dynamic_index_in_dim(blocks, at, axis=1, keepdims=False)

        total = of_peer(0).astype(F32)
        for hop in range(1, peers):
            total = total + along_peers(of_peer(hop), hop).astype(F32)
        total = total.astype(BF)

        def of_group(hop):
            return lax.dynamic_index_in_dim(total, (group_at + hop) % groups, keepdims=False)

        done = of_group(0).astype(F32)
        for hop in range(1, groups):
            done = done + along_groups(of_group(hop), hop).astype(F32)
        for mask in masks:
            done = done.astype(BF)
            done = done.astype(F32) + along_dp(done, mask).astype(F32)
        return done

    if fast:
        send_u, keep_u, send_d, keep_d = weight_parts()
        got_u = [along_dp(item, 1) for item in (send_u[0], send_u[2])]
        got_d = [along_dp(item, 2) for item in (send_d[0], send_d[2])]
    else:
        norm_two, d_up, d_branch, act, normed_two = kept
        total_up = reduce_rows(tn(normed_two, d_up).astype(BF))
        total_down = reduce_rows(tn(act, cotangent).astype(BF))
        found = jnp.stack([nn(item, d_branch).astype(BF) for item in arrived])
        found = [
            lax.dynamic_index_in_dim(found, (group_at + groups - g) % groups, keepdims=False)
            for g in range(groups)
        ]
        total_out = reduce_rows(jnp.concatenate(found, axis=0))
        norm_own = reduce_rows(norm_two[:2].T.astype(BF)).T

    share = prefetched(
        functools.partial(sums_kernel, groups=groups),
        (own_heads,),
        [scalar(spec) for spec in (ids_one, *[rows_one] * groups, mix_one)],
        scalar(part_one),
        array((own_heads, hs + 16, clusters), F32),
        16 if fast else 60,
        cost(own_heads * own_rows * clusters * 160, 2e6),
        "sums",
        first=(keep_u, keep_d) if fast else (),
    )(info, ids_all, *grads, mixed)
    share_got = [along_peers(share, hop) for hop in range(1, peers)]

    back_shapes = [
        array((groups, feats, rows), BF),
        array((own_heads, 2 * hs, own_rows), F32),
        array((own_heads, 2 * hs, max(peers - 1, 1) * own_rows), BF),
    ]
    dq, dkv_own, dkv_send = pl.pallas_call(
        functools.partial(back_kernel, size=size, groups=groups, gots=len(share_got)),
        grid=(own_heads,),
        in_specs=[ids_one, feat_one, kv_one, bias_one]
        + [rows_one] * groups
        + [mix_one, stat_one, cen_one]
        + [part_one] * (1 + len(share_got)),
        out_specs=[
            all_groups,
            pl.BlockSpec((1,) + back_shapes[1].shape[1:], lambda h: (h, 0, 0)),
            pl.BlockSpec((1,) + back_shapes[2].shape[1:], lambda h: (h, 0, 0)),
        ],
        out_shape=back_shapes,
        scratch_shapes=[pltpu.VMEM((seq, 2 * hs), F32), pltpu.VMEM((seq, 2 * clusters), BF)],
        compiler_params=params(36 if fast else 62, 1),
        cost_estimate=cost(14 * pair_flops, 10e6, own_heads * own_rows * seq),
        name="back",
    )(ids_all, feat, kv, bias, *grads, mixed, stats, centroid, share, *share_got)
    if fast:
        dkv_send = after(dkv_send, got_u, got_d)
    dkv_got = [
        along_peers(
            dkv_send if peers == 2 else dkv_send[..., (hop - 1) * own_rows : hop * own_rows], hop
        )
        for hop in range(1, peers)
    ]
    tall = block_rows + 16
    spent = cost(2 * own_rows * width * 3 * feats, 4e6)
    if fast:
        lines = block_rows // 4 + 8
        more = [array((4, groups, lines, width), BF)] * 2
    else:
        more = [array((width, 3 * feats), F32), array((16, 3 * feats), F32)]
    results = prefetched(
        functools.partial(inward_kernel, groups=groups, gots=len(dkv_got), fast=fast),
        (1,),
        [whole(back_shapes[0].shape)]
        + [whole(back_shapes[1].shape)] * (1 + len(dkv_got))
        + [whole((width, own_rows))],
        [whole((own_heads, 3 * hs, rows))] * groups + [whole(item.shape) for item in more],
        [array((own_heads, 3 * hs, rows), BF)] * groups + more,
        28 if fast else 60,
        spent,
        "inward",
    )(info, dq, dkv_own, *dkv_got, hat_own)
    d_in, more = results[:groups], results[groups:]
    home = [d_in[0]] + [along_groups(d_in[hop], hop) for hop in range(1, groups)]

    grad_tokens = prefetched(
        functools.partial(final_kernel, groups=groups),
        (1,),
        [whole((own_heads, 3 * hs, rows))] * groups
        + [square, square, whole((1, width)), whole((groups, 3 * feats, width))],
        square,
        array((rows, width), BF),
        24 if fast else 60,
        cost(6 * rows * width * width, 6 * width * width),
        "final",
    )(info, *home, tokens, d_resid, gain_row, w_in)

    if fast:
        keep, far = more
        inner_got = along_peers(far, 1)
        to_y, to_x, to_xy = weight_second(
            keep_u, got_u[1], keep_d, got_d[1], keep, inner_got, send_u[1], send_d[1]
        )
        by_y, by_x, by_xy = along_dp(to_y, 2), along_dp(to_x, 1), along_dp(to_xy, 3)
        sums = weight_third(
            keep_u, got_u[0], keep_d, got_d[0], by_y, by_x, keep, inner_got, by_xy
        )
        came_a, came_b = [sums[0]], [sums[groups]]
        came_a += [along_groups(sums[hop], hop) for hop in range(1, groups)]
        late = after(sums[groups + 1 :], came_a[1])
        came_b += [along_groups(late[hop - 1], hop) for hop in range(1, groups)]
        spread_a = weight_fourth(came_a, lead, 0, (came_b[1], grad_tokens))
        high = keep_u.shape[2] - lead
        spread_b = weight_fourth(came_b, high, lines, spread_a)
        found = weight_spread(spread_a, spread_b, high, came_a[0])
        total_up, total_out, total_down, norms, total_query, total_keyval, vector = found
        norm_own = lax.dynamic_slice_in_dim(norms, me * block_rows, block_rows, axis=1)
        gain_grad, shift_grad = vector[:, 0], vector[:, 1]
    else:
        found, more = more
        found = found.reshape(groups, peers, block_rows, 3 * feats)
        more = jnp.broadcast_to(more, (groups, peers, 16, 3 * feats))
        found = jnp.concatenate([found, more], axis=2).astype(BF)

        def of_peer(hop):
            at = (peer_at + hop) % peers
            return lax.dynamic_index_in_dim(found, at, axis=1, keepdims=False)

        total = of_peer(0).astype(F32)
        for hop in range(1, peers):
            total = total + along_peers(of_peer(hop), hop).astype(F32)
        for mask in masks:
            total = total.astype(BF)
            total = total.astype(F32) + along_dp(total, mask).astype(F32)
        total = total.astype(BF)
        items = [
            lax.dynamic_index_in_dim(total, (group_at + hop) % groups, keepdims=False)
            for hop in range(groups)
        ]
        pieces = [items[0]] + [along_groups(items[hop], hop) for hop in range(1, groups)]
        pieces = jnp.stack(pieces)
        pieces = jnp.stack(
            [
                lax.dynamic_index_in_dim(pieces, (group_at + groups - g) % groups, keepdims=False)
                for g in range(groups)
            ]
        ).astype(F32)
        q_part = pieces[:, :, :feats].transpose(1, 0, 2).reshape(tall, width)
        kv_part = (
            pieces[:, :, feats:]
            .reshape(groups, tall, 2, feats)
            .transpose(1, 2, 0, 3)
            .reshape(tall, 2 * width)
        )
        at = me * block_rows
        wq_rows = lax.dynamic_slice_in_dim(w_query, at, block_rows).astype(F32)
        wkv_rows = lax.dynamic_slice_in_dim(w_keyval, at, block_rows).astype(F32)
        gain_own = lax.dynamic_slice_in_dim(gain_one, at, block_rows)
        shift_own = lax.dynamic_slice_in_dim(shift_one, at, block_rows)
        q_sum, kv_sum = q_part[block_rows], kv_part[block_rows]
        q_part, kv_part = q_part[:block_rows], kv_part[:block_rows]
        shift_grad = jnp.sum(wq_rows * q_sum, axis=1) + jnp.sum(wkv_rows * kv_sum, axis=1)
        along = jnp.sum(wq_rows * q_part, axis=1) + jnp.sum(wkv_rows * kv_part, axis=1)
        total_query = q_part + shift_own[:, None] * q_sum
        total_keyval = kv_part + shift_own[:, None] * kv_sum
        gain_grad = along / gain_own


    return (
        output,
        grad_tokens,
        total_query,
        total_keyval,
        total_out,
        total_up,
        total_down,
        gain_grad,
        shift_grad,
        norm_own[0],
        norm_own[1],
    )


def solution(mesh):
    return jax.shard_map(
        per_device,
        mesh=mesh,
        in_specs=(
            P(("dp", "wide"), None),
            P(("dp", "wide"), None),
            P("dp"),
            P("dp", None, "wide", None),
            P(),
            P(),
            P(),
            P(),
            P(),
            P(),
            P(),
            P(),
            P(),
            P(("dp", "wide"), None),
        ),
        out_specs=(
            P(("dp", "wide"), None),
            P(("dp", "wide"), None),
            P("wide", None),
            P("wide", None),
            P("wide", None),
            P("wide", None),
            P("wide", None),
            P("wide"),
            P("wide"),
            P("wide"),
            P("wide"),
        ),
        check_vma=False,
    )
```

```python
import functools
import math

import jax
import jax.numpy as jnp
import numpy as np
from jax import lax
from jax.experimental import pallas as pl
from jax.experimental.pallas import tpu as pltpu
from jax.sharding import PartitionSpec as P

EPSILON = 1e-05
NEGATIVE = -1e30
EXCLUDED = -3e30
GELU_A = math.sqrt(2.0 / math.pi)
GELU_B = 0.044715
BF = jnp.bfloat16
F32 = jnp.float32


def nn(left, right):
    return lax.dot_general(left, right, (((1,), (0,)), ((), ())), preferred_element_type=F32)


def nt(left, right):
    return lax.dot_general(left, right, (((1,), (1,)), ((), ())), preferred_element_type=F32)


def tn(left, right):
    return lax.dot_general(left, right, (((0,), (0,)), ((), ())), preferred_element_type=F32)


def params(mib, dims):
    return pltpu.CompilerParams(
        vmem_limit_bytes=mib * 1024 * 1024, dimension_semantics=("arbitrary",) * dims
    )


def cost(flops, nbytes, trans=0):
    return pl.CostEstimate(flops=int(flops), bytes_accessed=int(nbytes), transcendentals=int(trans))


def split_low(values):
    high = values.astype(BF)
    return high, (values - high.astype(F32)).astype(BF)


def one_hot_t(ids_row, clusters):
    rows = lax.broadcasted_iota(jnp.int32, (clusters, ids_row.shape[1]), 0)
    return jnp.where(rows == ids_row, 1.0, 0.0).astype(BF)


def key_passes(total, size, score, weigh, blocks=None):
    count = total // size
    if count <= 4:
        if blocks is None:
            blocks = [score(index) for index in range(count)]
        peak = functools.reduce(jnp.maximum, [jnp.max(b, axis=0, keepdims=True) for b in blocks])
        denom, sums = 0.0, None
        for index in range(count):
            expo = jnp.exp(blocks[index] - peak)
            denom = denom + jnp.sum(expo, axis=0, keepdims=True)
            parts = weigh(index, expo)
            sums = parts if sums is None else tuple(x + y for x, y in zip(sums, parts))
        return peak, denom, sums

    def step(index, carry):
        peak, denom, sums = carry
        block = score(index)
        fresh = jnp.maximum(peak, jnp.max(block, axis=0, keepdims=True))
        expo = jnp.exp(block - fresh)
        fade = jnp.exp(peak - fresh)
        parts = weigh(index, expo)
        return (
            fresh,
            denom * fade + jnp.sum(expo, axis=0, keepdims=True),
            tuple(old * fade + new for old, new in zip(sums, parts)),
        )

    shapes = jax.eval_shape(lambda: (score(0), weigh(0, score(0))))
    lanes = shapes[0].shape[1]
    start = (
        jnp.full((1, lanes), NEGATIVE, F32),
        jnp.zeros((1, lanes), F32),
        tuple(jnp.zeros(item.shape, F32) for item in shapes[1]),
    )
    return lax.fori_loop(0, count, step, start)


def key_sum(total, size, step, start):
    count = total // size
    if count <= 4:
        for index in range(count):
            start = step(index, start)
        return start
    return lax.fori_loop(0, count, step, start)


def spot_of(index, size):
    if isinstance(index, int):
        return pl.ds(index * size, size)
    return pl.ds(pl.multiple_of(index * size, size), size)


def piece(ref, index, size, axis):
    spot = spot_of(index, size)
    return ref[spot, :] if axis == 0 else ref[:, spot]


def table_kernel(info, *refs, picks):
    parts, out = refs[:-1], refs[-1]
    total = parts[0][:, :picks]
    for part in parts[1:]:
        total = total + part[:, :picks]
    out[:, :picks] = total
    rows = parts[0].shape[1] - picks
    for group, part in enumerate(parts):
        out[:, picks + group * rows : picks + (group + 1) * rows] = part[:, picks:]


def bias_kernel(info, *refs, groups, peers, rows, picks):
    tables, (bias_ref, ids_ref) = refs[:peers], refs[peers:]
    part = pl.program_id(0)
    owner = (
        lax.rem(info[0] + part // peers, groups) * peers + lax.rem(info[1] + part % peers, peers)
    )
    heads, _, clusters = tables[0].shape
    place = owner * rows + lax.broadcasted_iota(jnp.int32, (rows, clusters), 0)
    plain = jnp.where(place >= info[2], EXCLUDED, NEGATIVE)
    for head in range(heads):
        top = tables[0][head, :picks]
        for table in tables[1:]:
            top = top + table[head, :picks]
        value = plain
        for pick in range(picks):
            value = jnp.where(place == top[pick : pick + 1, :], 0.0, value)
        bias_ref[head] = value.astype(BF)

    @pl.when(part == 0)
    def ids():
        lines = rows // clusters
        for head in range(heads):
            row = []
            for group in range(groups):
                for table in tables:
                    for line in range(lines):
                        at = picks + group * lines + line
                        row.append(table[head, at : at + 1, :])
            ids_ref[head] = jnp.concatenate(row, axis=1)


def project_kernel(info, *refs, peers, olds):
    parts = refs[:peers]
    gain_ref, shift_ref, w_ref = refs[peers : peers + 3]
    hat_ref, feat_ref, kv_ref = refs[peers + 3 + olds :]
    rows = hat_ref.shape[1]
    for peer in range(peers):
        values = parts[peer][...].astype(F32)
        centered = values - jnp.mean(values, axis=-1, keepdims=True)
        variance = jnp.mean(centered * centered, axis=-1, keepdims=True)
        scaled = centered * lax.rsqrt(variance + EPSILON) * gain_ref[...]
        if peer == 0:
            hat_ref[...] = scaled.astype(BF).T
        low = (scaled + shift_ref[...]).astype(BF)
        found = nt(w_ref[0], low)
        heads, triple = feat_ref.shape[0], feat_ref.shape[1]
        hs = triple // 3
        spot = slice(peer * rows, (peer + 1) * rows)
        for head in range(heads):
            base = head * triple
            query = (found[base : base + hs] * 0.125).astype(BF)
            pair = found[base + hs : base + triple].astype(BF)
            feat_ref[head, :hs, spot] = query
            feat_ref[head, hs:, spot] = pair
            kv_ref[head, spot, :] = pair.T


def forward_kernel(ids_all, feat, kv, bias, *refs, size, groups, rows):
    outs = refs[:groups]
    mix_ref, stat_ref, cen_ref = refs[groups:]
    hs = feat.shape[1] // 3
    keys = kv.shape[1]
    count = keys // size
    clusters = bias.shape[2]
    kv_h, bias_h = kv.at[0], bias.at[0]
    queries_all, kvt = feat.at[0, :hs], feat.at[0, hs:]
    hot_all = one_hot_t(ids_all[0], clusters)
    ones = jnp.ones((16, keys), BF)
    sums = nt(jnp.concatenate([queries_all[...], ones], axis=0), hot_all)
    counts = sums[hs : hs + 1]
    centroid = (sums[:hs] / jnp.maximum(counts, 1.0)).astype(BF)
    padded = jnp.concatenate([centroid, jnp.zeros_like(centroid)], axis=0)

    def cluster_score(index):
        scores = nn(piece(kv_h, index, size, 0), padded)
        outside = piece(bias_h, index, size, 0).astype(F32) < 2.0 * NEGATIVE
        return jnp.where(outside, NEGATIVE, scores)

    def cluster_weigh(index, expo):
        top = piece(bias_h, index, size, 0).astype(F32) == 0.0
        mass = jnp.sum(jnp.where(top, expo, 0.0), axis=0, keepdims=True)
        other = jnp.where(top, 0.0, expo).astype(BF)
        return nn(piece(kvt, index, size, 1), other), mass

    peers = keys // (groups * rows)
    hots, sides = [], []
    for group in range(groups):
        spot = slice(group * peers * rows, group * peers * rows + rows)
        hot = one_hot_t(ids_all[0, :, spot], clusters)
        queries = queries_all[:, spot]
        hots.append(hot)
        sides.append(jnp.concatenate([queries, jnp.zeros_like(queries), hot], axis=0))

    def member_score(group, index):
        both = jnp.concatenate([piece(kv_h, index, size, 0), piece(bias_h, index, size, 0)], axis=1)
        return nn(both, sides[group])

    def member_weigh(index, expo):
        return (nn(piece(kvt, index, size, 1), expo.astype(BF)),)

    short = count <= 4
    ahead = None
    if short:
        ahead = [member_score(0, index) for index in range(count)]
    peak, denom, (rest, mass) = key_passes(keys, size, cluster_score, cluster_weigh)
    rest = rest[hs:] / denom
    mass = mass / denom
    blank = jnp.zeros((5, clusters), F32)
    stats = jnp.concatenate([rest, mass, peak + jnp.log(denom), counts, blank], axis=0)
    stat_ref[0] = stats
    cen_ref[0] = centroid
    high, low = split_low(stats)
    table = jnp.concatenate([high, low], axis=1)
    for group in range(groups):
        gathered = nn(table, jnp.concatenate([hots[group], hots[group]], axis=0))
        blocks, ahead = ahead, None
        if short and group + 1 < groups:
            ahead = [member_score(group + 1, index) for index in range(count)]
        score = functools.partial(member_score, group)
        peak, denom, (mix,) = key_passes(keys, size, score, member_weigh, blocks)
        mix = mix[hs:] / denom
        outs[group][...] = (gathered[hs : hs + 1] * mix + gathered[:hs]).astype(BF)
        level = jnp.broadcast_to(peak + jnp.log(denom), (8, rows))
        mix_ref[0, group] = jnp.concatenate([mix, level], axis=0)


def sums_kernel(info, ids_own, *refs, groups):
    grads, (mix_ref, part_ref) = refs[:groups], refs[groups:]
    hs = grads[0].shape[0]
    total = None
    for group in range(groups):
        rows = grads[group].shape[1]
        step = ids_own.shape[2] // groups
        hot = one_hot_t(ids_own[0, :, group * step : group * step + rows], part_ref.shape[2])
        grad = grads[group][...]
        along = jnp.sum(grad.astype(F32) * mix_ref[0, group, :hs], axis=0, keepdims=True)
        high, low = split_low(along)
        pad = jnp.zeros((14, rows), BF)
        part = nt(jnp.concatenate([grad, high, low, pad], axis=0), hot)
        total = part if total is None else total + part
    part_ref[0] = total


def back_kernel(ids_all, feat, kv, bias, *refs, size, groups, gots):
    grads = refs[:groups]
    mix_ref, stat_ref, cen_ref = refs[groups : groups + 3]
    shares = refs[groups + 3 : groups + 4 + gots]
    dq_ref, own_ref, send_ref, total, both = refs[groups + 4 + gots :]
    hs, rows = grads[0].shape
    keys = kv.shape[1]
    count = keys // size
    peers = keys // (groups * rows)
    clusters = bias.shape[2]
    kv_h, bias_h = kv.at[0], bias.at[0]
    queries_all, kvt = feat.at[0, :hs], feat.at[0, hs:]
    stats = stat_ref[0]
    high, low = split_low(stats[hs : hs + 8])
    table = jnp.concatenate([high, low], axis=1)
    hots, sides, levels, deltas, pads, rights = [], [], [], [], [], []
    for group in range(groups):
        spot = slice(group * peers * rows, group * peers * rows + rows)
        hot = one_hot_t(ids_all[0, :, spot], clusters)
        queries = queries_all[:, spot]
        blank = jnp.zeros_like(queries)
        hots.append(jnp.concatenate([hot, hot], axis=0))
        sides.append(jnp.concatenate([queries, blank, hot], axis=0))
        mass = nn(table, hots[group])[0:1]
        back = (mass * grads[group][...].astype(F32)).astype(BF)
        levels.append(mix_ref[0, group, hs : hs + 1])
        deltas.append(jnp.sum(back.astype(F32) * mix_ref[0, group, :hs], axis=0, keepdims=True))
        pads.append(jnp.concatenate([blank, back], axis=0))
        turned = jnp.concatenate([queries, blank], axis=0)
        rights.append(jnp.concatenate([turned, pads[group]], axis=1).T)

    def scores(group, index):
        kv_c = piece(kv_h, index, size, 0)
        pair = jnp.concatenate([kv_c, piece(bias_h, index, size, 0)], axis=1)
        return nn(pair, sides[group]), nn(kv_c, pads[group])

    def finish(group, index, found, dq):
        weights = jnp.exp(found[0] - levels[group])
        grad_s = (weights * (found[1] - deltas[group])).astype(BF)
        part = nn(jnp.concatenate([grad_s, weights.astype(BF)], axis=1), rights[group])
        spot = spot_of(index, size)
        if group == 0:
            total[spot, :] = part
        else:
            total[spot, :] += part
        return dq + nn(piece(kvt, index, size, 1), grad_s)

    rest, mass = stats[:hs], stats[hs : hs + 1]
    level, counts = stats[hs + 1 : hs + 2], stats[hs + 2 : hs + 3]
    centroid = cen_ref[0]
    part = shares[0][0]
    for share in shares[1:]:
        part = part + share[0]
    d_rest = part[:hs].astype(BF)
    d_mass = part[hs : hs + 1] + part[hs + 1 : hs + 2]
    delta = jnp.sum(d_rest.astype(F32) * rest, axis=0, keepdims=True) + d_mass * mass
    cen_pad = jnp.concatenate([centroid, jnp.zeros_like(centroid)], axis=0)
    rest_pad = jnp.concatenate([jnp.zeros_like(centroid), d_rest], axis=0)
    right = jnp.concatenate([cen_pad, rest_pad], axis=1).T

    def cluster_step(index, summed):
        kv_c = piece(kv_h, index, size, 0)
        marks = piece(bias_h, index, size, 0).astype(F32)
        probs = jnp.exp(nn(kv_c, cen_pad) - level)
        probs = jnp.where(marks < 2.0 * NEGATIVE, 0.0, probs)
        top = marks == 0.0
        d_probs = jnp.where(top, d_mass, nn(kv_c, rest_pad))
        d_score = (probs * (d_probs - delta)).astype(BF)
        other = jnp.where(top, 0.0, probs).astype(BF)
        both[spot_of(index, size), :] = jnp.concatenate([d_score, other], axis=1)
        return summed + nn(piece(kvt, index, size, 1), d_score)

    start = jnp.zeros((2 * hs, rows), F32)
    zero = jnp.zeros((2 * hs, clusters), F32)
    member_dq = []
    if count <= 4:
        tasks = [(group, index) for group in range(groups) for index in range(count)]
        ahead = scores(*tasks[0])
        d_cen = key_sum(keys, size, cluster_step, zero)
        dq = start
        for step, (group, index) in enumerate(tasks):
            found = ahead
            if step + 1 < len(tasks):
                ahead = scores(*tasks[step + 1])
            dq = finish(group, index, found, dq)
            if index == count - 1:
                member_dq.append(dq[:hs] * 0.125)
                dq = start
    else:
        d_cen = key_sum(keys, size, cluster_step, zero)
        for group in range(groups):

            def step(index, dq, group=group):
                return finish(group, index, scores(group, index), dq)

            member_dq.append(lax.fori_loop(0, count, step, start)[:hs] * 0.125)
    d_cen = d_cen[:hs] * 0.125 / jnp.maximum(counts, 1.0)
    high, low = split_low(d_cen)
    table = jnp.concatenate([high, low], axis=1)
    for group in range(groups):
        base = group * peers * rows
        dq_ref[group] = (member_dq[group] + nn(table, hots[group])).astype(BF)
        own = total[base : base + rows, :] + nn(both[base : base + rows, :], right)
        own_ref[0, :, group * rows : (group + 1) * rows] = own.T
        for peer in range(1, peers):
            spot = (peer - 1) * groups * rows + group * rows
            found = total[base + peer * rows : base + (peer + 1) * rows, :]
            send_ref[0, :, spot : spot + rows] = found.astype(BF).T


def join_kernel(dq_ref, own_ref, *refs, groups):
    gots, outs = refs[:-groups], refs[-groups:]
    heads, _, rows = outs[0].shape
    hs = dq_ref.shape[1] // heads
    for head in range(heads):
        for group in range(groups):
            spot = slice(group * rows, (group + 1) * rows)
            pair = own_ref[head, :, spot]
            for got in gots:
                pair = pair + got[head, :, spot].astype(F32)
            outs[group][head, :hs] = dq_ref[group, head * hs : (head + 1) * hs]
            outs[group][head, hs:] = pair.astype(BF)


def block_kernel(info, *refs, groups, chunks, fast):
    (attn, rest) = (refs[:groups], refs[groups:])
    x_ref, gain_ref, shift_ref, wo_ref, up_ref, down_ref, cot_ref = rest[:7]
    out_ref, dres_ref = rest[7:9]
    if fast:
        far_ref, low_far, act_ref, low_ref = rest[9:13]
        rest = rest[13:]
        hidden = far_ref.shape[1] * 4 // 7
    else:
        dn_ref, dup_ref, dbr_ref, act_ref, low_ref = rest[9:14]
        rest = rest[14:]
    dat = rest[:groups]
    hat_ref, inv_ref, normed, back, total = rest[groups:]
    index = pl.program_id(0)

    @pl.when(index == 0)
    def before():
        resid = x_ref[...].astype(F32)
        for group in range(groups):
            owner = lax.rem(info[0] + groups - group, groups)
            resid = resid + tn(attn[group][...], wo_ref[owner])
        total[...] = resid
        centered = resid - jnp.mean(resid, axis=-1, keepdims=True)
        variance = jnp.mean(centered * centered, axis=-1, keepdims=True)
        inverse = lax.rsqrt(variance + EPSILON)
        hat = centered * inverse
        hat_ref[...] = hat
        inv_ref[...] = jnp.broadcast_to(inverse, inv_ref.shape)
        low = (hat * gain_ref[...] + shift_ref[...]).astype(BF)
        normed[...] = low
        if fast:
            feats = attn[0].shape[0]
            half = feats // 2
            turned = low.T
            for group in range(groups):
                first = turned[group * feats : group * feats + half]
                second = turned[group * feats + half : (group + 1) * feats]
                spot = slice(group * half, (group + 1) * half)
                low_ref[spot, :] = jnp.where(info[1] == 0, first, second)
                low_far[spot, :] = jnp.where(info[1] == 0, second, first)
                first = attn[group][:half]
                second = attn[group][half:]
                spot = slice((groups + group) * half, (groups + group + 1) * half)
                low_ref[spot, :] = jnp.where(info[1] == 0, first, second)
                low_far[spot, :] = jnp.where(info[1] == 0, second, first)
        else:
            low_ref[...] = low
        back[...] = jnp.zeros_like(back)

    up = nn(normed[...], up_ref[...])
    grad_act = nt(cot_ref[...], down_ref[...])
    square = up * up
    inner = GELU_A * (up + GELU_B * up * square)
    curve = jnp.tanh(inner)
    act = (0.5 * up * (1.0 + curve)).astype(BF)
    slope = 0.5 * (1.0 + curve) + 0.5 * up * (1.0 - curve * curve) * (
        GELU_A * (1.0 + 3.0 * GELU_B * square)
    )
    d_up = (grad_act * slope).astype(BF)
    if fast:
        part = act.shape[1]
        half = part // 2
        first, second = act[:, :half], act[:, half:]
        act_ref[...] = jnp.where(info[1] == 0, first, second)
        far_ref[:, pl.ds(pl.multiple_of(index * part, part), part)] = d_up
        spot = pl.ds(pl.multiple_of(hidden + index * half, half), half)
        far_ref[:, spot] = jnp.where(info[1] == 0, second, first)
    else:
        dup_ref[...] = d_up
        act_ref[...] = act
    back[...] += nt(d_up, up_ref[...])
    total[...] += nn(act, down_ref[...])

    @pl.when(index == chunks - 1)
    def after():
        out_ref[...] = total[...].astype(BF)
        d_normed = back[...]
        hat = hat_ref[...]
        gain_part = jnp.sum(d_normed * hat, axis=0, keepdims=True)
        shift_part = jnp.sum(d_normed, axis=0, keepdims=True)
        if fast:
            rows, width = low_far.shape[1], d_normed.shape[1]
            fold = []
            for part_row in split_low(gain_part) + split_low(shift_part):
                fold += [part_row[:, k : k + rows].astype(F32) for k in range(0, width, rows)]
            fold.append(jnp.zeros((low_far.shape[0] - width - len(fold), rows), F32))
            folded = jnp.concatenate(fold, axis=0).astype(BF)
            low_far[width:, :] = folded
            low_ref[width:, :] = folded
        else:
            blank = jnp.zeros((6, d_normed.shape[1]), F32)
            dn_ref[...] = jnp.concatenate([gain_part, shift_part, blank], axis=0)
        gy = d_normed * gain_ref[...]
        mean_one = jnp.mean(gy, axis=-1, keepdims=True)
        mean_two = jnp.mean(gy * hat, axis=-1, keepdims=True)
        d_resid = cot_ref[...].astype(F32) + inv_ref[:, 0:1] * (gy - mean_one - hat * mean_two)
        dres_ref[...] = d_resid
        branch = d_resid.astype(BF)
        if fast:
            far_ref[:, hidden * 3 // 2 :] = branch
        else:
            dbr_ref[...] = branch
        for group in range(groups):
            owner = lax.rem(info[0] + groups - group, groups)
            dat[group][...] = nt(wo_ref[owner], branch).astype(BF)


def weights_kernel(info, *refs, groups):
    (dup, dup_got, dbr, dbr_got, act, act_got, low, low_got, cot, cot_got) = refs[:10]
    send_u, keep_u, send_d, keep_d, outs = refs[10:13], refs[13], refs[14:17], refs[17], refs[18]
    width = cot.shape[1]
    lead = send_u[0].shape[2]

    def leave(send, turn, spot, block, first):
        if turn:
            send[2][0, spot, first : first + block.shape[0]] = block
        elif first:
            send[1][0, spot, first - lead : first - lead + block.shape[0]] = block
        else:
            send[0][0, spot] = block[:lead]
            send[1][0, spot, : block.shape[0] - lead] = block[lead:]

    index = pl.program_id(0)
    group_at, place_u, place_d = info[0], info[3], info[4]
    rows = width // (2 * groups)
    quarter = rows // 4
    stay = groups * rows

    @pl.when(index == 0)
    def first():
        found = nn(low[stay:width, :], dbr[...]) + nn(low_got[stay:width, :], dbr_got[...])
        fold = low[width:, :].astype(F32) + low_got[width:, :].astype(F32)
        times = width // fold.shape[1]
        norms = []
        for part in range(2):
            both = fold[2 * part * times : (2 * part + 1) * times]
            both = both + fold[(2 * part + 1) * times : (2 * part + 2) * times]
            norms.append(jnp.concatenate([both[k : k + 1] for k in range(times)], axis=1))
        norms = jnp.concatenate(norms + [jnp.zeros((6, width), F32)], axis=0)
        for group in range(groups):
            block = found[group * rows : (group + 1) * rows]
            outs[group] = block
            for part in range(4):
                tail = block[part * quarter + 16 : (part + 1) * quarter]
                tail = jnp.concatenate([tail, norms], axis=0).astype(BF)
                place = lax.bitwise_xor(part, place_d)

                for turn in range(2):

                    @pl.when(place == 2 + turn)
                    def leaves_more(turn=turn, tail=tail, group=group):
                        leave(send_d, turn, (groups - group) % groups, tail, rows)

                @pl.when(place < 2)
                def stays_more():
                    keep_d[place, (groups - group) % groups, rows:] = tail

    up = nn(low[:stay, :], dup[...]) + nn(low_got[:stay, :], dup_got[...])
    at = lax.bitwise_xor(lax.bitwise_xor(index, 2), place_u)
    for group in range(groups):
        spot = lax.rem(group + groups - group_at, groups)
        block = up[group * rows : (group + 1) * rows].astype(BF)
        away = (groups - group) % groups
        start = pl.multiple_of(at * quarter, 8)
        other = outs[group, pl.ds(start, 16), :].astype(BF)

        for turn in range(2):

            @pl.when(index == turn)
            def leaves(turn=turn, spot=spot, block=block, away=away, other=other):
                leave(send_u, turn, spot, block, 0)
                leave(send_u, turn, away, other, rows)

        @pl.when(index >= 2)
        def stays():
            keep_u[0, spot, :rows] = block
            keep_u[0, away, rows:] = other

    down = tn(act[...], cot[...]) + tn(act_got[...], cot_got[...])
    spot = lax.rem(index + groups - group_at, groups)
    for part in range(4):
        block = down[part * rows : (part + 1) * rows].astype(BF)
        place = lax.bitwise_xor(part, place_d)

        for turn in range(2):

            @pl.when(place == 2 + turn)
            def leaves_down(turn=turn, block=block):
                leave(send_d, turn, spot, block, 0)

        @pl.when(place < 2)
        def stays_down():
            keep_d[place, spot, :rows] = block


def second_kernel(keep_u, got_u, keep_d, got_d, inner, inner_got, late_u, late_d, to_y, to_x, to_xy):
    rows, lines = keep_u.shape[2], inner.shape[2]
    to_y[:, :rows] = (keep_u[0].astype(F32) + got_u[0].astype(F32)).astype(BF)
    to_x[:, :rows] = (keep_d[0].astype(F32) + got_d[0].astype(F32)).astype(BF)
    last = to_y.shape[1] - lines
    to_y[:, last:] = (inner[1].astype(F32) + inner_got[1].astype(F32)).astype(BF)
    to_x[:, last:] = (inner[2].astype(F32) + inner_got[2].astype(F32)).astype(BF)
    to_xy[...] = (inner[3].astype(F32) + inner_got[3].astype(F32)).astype(BF)
    to_y[:, rows:last] = late_d[0]
    to_x[:, rows:last] = late_u[0]


def third_kernel(info, keep_u, one_u, keep_d, one_d, by_y, by_x, inner, inner_got, by_xy, *outs):
    rows, lead, lines = keep_u.shape[2], one_u.shape[2], inner.shape[2]
    groups = len(outs) // 2
    left = rows - lead
    head, tail, late = slice(0, lead), slice(lead, rows), slice(rows, rows + left)
    mid = slice(rows + left, None)

    def added(keep, got, by, group, spot):
        total = keep[0, group, spot].astype(F32) + got.astype(F32)
        return (total + by[group, spot].astype(F32)).astype(BF)

    for group in range(groups):
        first, last = outs[group], outs[groups + group]
        first[:lead] = added(keep_u, one_u[0, group], by_y, group, head)
        first[lead:] = added(keep_d, one_d[0, group], by_x, group, head)
        last[:left] = added(keep_u, by_x[group, late], by_y, group, tail)
        last[left : 2 * left] = added(keep_d, by_y[group, late], by_x, group, tail)
        both = inner[0, group].astype(F32) + inner_got[0, group].astype(F32)
        both = both + by_y[group, mid].astype(F32) + by_x[group, mid].astype(F32)
        last[2 * left :] = (both + by_xy[group].astype(F32)).astype(BF)


def fourth_kernel(info, *refs, groups, high, feats):
    parts, out = refs[:groups], refs[groups]
    total = parts[0][: 2 * high].astype(F32)
    for part in parts[1:]:
        total = total + part[: 2 * high].astype(F32)
    out[: 2 * high] = total.astype(BF)
    if parts[0].shape[0] == 2 * high:
        return
    turned = refs[groups + 1]
    third = feats // 3
    for group in range(groups):
        turned[group] = parts[group][2 * high :].astype(F32)
    spots = [lax.rem(info[0] + groups - owner, groups) for owner in range(groups)]
    found, sums = [], []
    for kind in range(3):
        lanes = slice(kind * third, (kind + 1) * third)
        found.append(jnp.concatenate([turned[spot, :, lanes] for spot in spots], axis=1))
        line = [turned[spot, 8 * kind : 8 * kind + 8, 3 * third :] for spot in spots]
        sums.append(jnp.concatenate(line, axis=1)[:1])
    sums.append(jnp.zeros((5, out.shape[1]), F32))
    out[2 * high :] = jnp.concatenate(found + sums, axis=0).astype(BF)


def spread_kernel(info, *refs, lead, high):
    firsts, lasts, (wq, wkv, pair) = refs[:4], refs[4:8], refs[8:11]
    up_ref, out_ref, down_ref, norm_ref, gq_ref, gkv_ref, vec_ref, sums = refs[11:]
    index = pl.program_id(0)
    rows, width = down_ref.shape
    quarter = rows // 4
    left = rows - lead
    order_u, order_d = (0, 2, 1, 3), (0, 1, 2, 3)

    @pl.when(index == 0)
    def first():
        for place, source in enumerate(order_u):

            @pl.when(info[3] == place)
            def take(source=source):
                sums[...] = lasts[source][2 * high :].astype(F32)[3 * quarter :]

    for place, source in enumerate(order_u):

        @pl.when(index == place)
        def upper(source=source):
            part = lasts[source]
            up_ref[:lead] = firsts[source][:lead].astype(F32)
            up_ref[lead:] = part[:left].astype(F32)
            at = pl.multiple_of(lax.bitwise_xor(index, info[3]) * quarter, 8)
            out_ref[pl.ds(at, 16), :] = part[left:high].astype(F32)
            spot = pl.ds(at, quarter)
            shift, gain = pair[spot, 0:1], pair[spot, 1:2]
            gain_sum, shift_sum = 0.0, 0.0
            blocks = part[2 * high :].astype(F32)
            for kind in range(3):
                block = blocks[kind * quarter : (kind + 1) * quarter]
                line = sums[kind : kind + 1]
                if kind == 0:
                    weight = wq[spot, :]
                    gq_ref[spot, :] = block + shift * line
                else:
                    lanes = slice((kind - 1) * width, kind * width)
                    weight = wkv[spot, lanes]
                    gkv_ref[spot, lanes] = block + shift * line
                gain_sum = gain_sum + jnp.sum(weight * block, axis=1, keepdims=True)
                shift_sum = shift_sum + jnp.sum(weight * line, axis=1, keepdims=True)
            lane = lax.broadcasted_iota(jnp.int32, (quarter, vec_ref.shape[1]), 1)
            vec_ref[spot, :] = jnp.where(lane == 0, gain_sum / gain, shift_sum)

    for place, source in enumerate(order_d):

        @pl.when(index == place)
        def lower(source=source):
            part = lasts[source]
            down_ref[:lead] = firsts[source][lead:].astype(F32)
            down_ref[lead:] = part[high : high + left].astype(F32)
            tail = part[high + left : 2 * high].astype(F32)
            at = pl.multiple_of(lax.bitwise_xor(index, info[4]) * quarter + 16, 8)
            out_ref[pl.ds(at, quarter - 16), :] = tail[: quarter - 16]

            @pl.when(lax.bitwise_xor(index, info[4]) == 0)
            def norms():
                norm_ref[...] = tail[quarter - 16 :]


def inward_kernel(info, *refs, groups, gots, fast):
    join_refs, hat_ref = refs[: 2 + gots], refs[2 + gots]
    parts = refs[3 + gots : 3 + gots + groups]
    outs = refs[3 + gots + groups :]
    join_kernel(*join_refs, *parts, groups=groups)
    heads, triple, rows = parts[0].shape
    hs = triple // 3
    total, sums = None, None
    ones = jnp.ones((16, rows), BF)
    for group in range(groups):
        order = [parts[group][h, k * hs : (k + 1) * hs] for k in range(3) for h in range(heads)]
        turned = jnp.concatenate(order, axis=0)
        found = nt(hat_ref[:, group * rows : (group + 1) * rows], turned)
        more = nt(ones, turned)
        total = found if total is None else total + found
        sums = more if sums is None else sums + more
    if not fast:
        outs[0][...] = total
        outs[1][...] = sums
        return
    own_ref, far_ref = outs
    block = total.shape[0] // (2 * groups)
    quarter = block // 4
    third = total.shape[1] // 3
    more = [sums[:8, kind * third : (kind + 1) * third] for kind in range(3)]
    more = jnp.concatenate(more, axis=0)
    for group in range(groups):
        spot = lax.rem(group + groups - info[0], groups)
        for part in range(4):
            place = lax.bitwise_xor(part, info[3])
            found = []
            for parity in range(2):
                at = (2 * group + parity) * block + part * quarter
                lines = jnp.concatenate([total[at : at + quarter], more], axis=1)
                found.append(lines.astype(BF))
            own_ref[place, spot] = jnp.where(info[1] == 0, found[0], found[1])
            far_ref[place, spot] = jnp.where(info[1] == 0, found[1], found[0])


def final_kernel(info, *refs, groups):
    parts = refs[:groups]
    x_ref, dres_ref, gain_ref, w_ref, out_ref = refs[groups:]
    d_normed = jnp.zeros(dres_ref.shape, F32)
    for group in range(groups):
        owner = lax.rem(info[0] + groups - group, groups)
        heads, triple, rows = parts[group].shape
        d_normed = d_normed + tn(parts[group][...].reshape(heads * triple, rows), w_ref[owner])
    values = x_ref[...].astype(F32)
    centered = values - jnp.mean(values, axis=-1, keepdims=True)
    variance = jnp.mean(centered * centered, axis=-1, keepdims=True)
    inverse = lax.rsqrt(variance + EPSILON)
    hat = centered * inverse
    gy = d_normed * gain_ref[...]
    mean_one = jnp.mean(gy, axis=-1, keepdims=True)
    mean_two = jnp.mean(gy * hat, axis=-1, keepdims=True)
    out_ref[...] = (dres_ref[...] + inverse * (gy - mean_one - hat * mean_two)).astype(BF)


def ordered(kernel, inputs, later):
    def run(*refs):
        kernel(*refs[:inputs], *refs[inputs + later :])

    return run if later else kernel


def whole(shape):
    return pl.BlockSpec(shape, lambda *at: (0,) * len(shape))


def per_device(
    tokens,
    cluster_ids,
    lengths,
    top_keys,
    gain_one,
    shift_one,
    w_query,
    w_keyval,
    w_out,
    gain_two,
    shift_two,
    w_up,
    w_down,
    cotangent,
):
    rows, width = tokens.shape
    heads = cluster_ids.shape[1]
    hs = width // heads
    hidden = w_up.shape[1]
    wide = lax.axis_size("wide")
    n_dp = lax.axis_size("dp")
    groups = math.gcd(heads, wide)
    peers = wide // groups
    own_heads = heads // groups
    own_clusters = top_keys.shape[2]
    clusters = own_clusters * wide
    picks = top_keys.shape[3]
    seq = rows * wide
    size = 512 if seq <= 2048 else 2048
    feats = own_heads * hs
    block_rows = width // wide
    fast = peers == 2 and n_dp == 4 and block_rows == 96 and hidden == 4 * width and width % 256 == 0 and rows % 128 == 0
    me = lax.axis_index("wide")
    group_at, peer_at = me // peers, me % peers
    dp_at = lax.axis_index("dp")
    seq_len = lengths[0]
    bit_x, bit_y = dp_at % 2, (dp_at // 2) % 2
    place_u, place_d = 2 * bit_x + bit_y, 2 * bit_y + bit_x
    info = jnp.stack([group_at, peer_at, seq_len, place_u, place_d, me]).astype(jnp.int32)

    def along_groups(values, hop):
        pairs = [(i, ((i // peers + hop) % groups) * peers + i % peers) for i in range(wide)]
        return lax.ppermute(values, "wide", pairs)

    def along_peers(values, hop):
        pairs = [(i, (i // peers) * peers + (i % peers + hop) % peers) for i in range(wide)]
        return lax.ppermute(values, "wide", pairs)

    def along_dp(values, mask):
        return lax.ppermute(values, "dp", [(i, i ^ mask) for i in range(n_dp)])

    def prefetched(
        kernel, grid, in_specs, out_specs, out_shape, mib, spent, name, scratch=(), alias=None, first=()
    ):
        first = jax.tree.leaves(first)
        call = pl.pallas_call(
            ordered(kernel, 1 + len(in_specs), len(first)),
            grid_spec=pltpu.PrefetchScalarGridSpec(
                num_scalar_prefetch=1,
                grid=grid,
                in_specs=in_specs + [pl.BlockSpec(memory_space=pl.ANY)] * len(first),
                out_specs=out_specs,
                scratch_shapes=list(scratch),
            ),
            out_shape=out_shape,
            compiler_params=params(mib, len(grid)),
            cost_estimate=spent,
            input_output_aliases=alias or {},
            name=name,
        )
        return lambda *inputs: call(*inputs, *first)

    def after(values, *others):
        return lax.optimization_barrier((values, others))[0]

    def scalar(spec):
        return pl.BlockSpec(spec.block_shape, lambda *at: spec.index_map(*at[:-1]))

    def array(shape, dtype):
        return jax.ShapeDtypeStruct(shape, dtype)

    position = me * rows + jnp.arange(rows, dtype=jnp.int32)
    marked = jnp.where((position < seq_len)[:, None], cluster_ids, -1).T
    tops = jnp.zeros((heads, picks, clusters), jnp.int32)
    tops = lax.dynamic_update_slice(
        tops, top_keys[0].transpose(0, 2, 1), (0, 0, me * own_clusters)
    )
    lines = rows // clusters
    packed = jnp.concatenate([tops, marked.reshape(heads, lines, clusters)], axis=1)
    early = [along_peers(tokens, -hop) for hop in range(1, peers)]
    packed = after(packed.reshape(groups, own_heads, picks + lines, clusters), early)

    def of_heads(hop):
        return lax.dynamic_index_in_dim(packed, (group_at + groups - hop) % groups, keepdims=False)

    arrived = [of_heads(0)] + [along_groups(of_heads(hop), -hop) for hop in range(1, groups)]

    mine = {0: tokens, 1: along_groups(tokens, -1)}
    if groups > 2:
        mine[groups - 1] = along_groups(tokens, 1)
    ready = after(tokens, arrived)
    for hop in range(2, groups - 1):
        mine[hop] = along_groups(ready, -hop)

    w_in = jnp.concatenate([w_query, w_keyval], axis=1).T.reshape(3, heads, hs, width)
    w_in = w_in.transpose(1, 0, 2, 3).reshape(groups, 3 * feats, width)
    table_shape = (own_heads, picks + groups * lines, clusters)
    table = prefetched(
        functools.partial(table_kernel, picks=picks),
        (1,),
        [whole((own_heads, picks + lines, clusters))] * groups,
        whole(table_shape),
        array(table_shape, jnp.int32),
        8,
        cost(1e5, 1e6),
        "table",
    )(info, *arrived)
    tables = [table] + [along_peers(table, -hop) for hop in range(1, peers)]
    cot_got = [along_peers(after(cotangent, arrived), hop) for hop in range(1, peers)]
    cot_got = cot_got if fast else []
    bias, ids_all = prefetched(
        functools.partial(bias_kernel, groups=groups, peers=peers, rows=rows, picks=picks),
        (wide,),
        [whole(table_shape)] * peers,
        [
            pl.BlockSpec((own_heads, rows, clusters), lambda i, s: (0, i, 0)),
            whole((own_heads, 1, seq)),
        ],
        [array((own_heads, seq, clusters), BF), array((own_heads, 1, seq), jnp.int32)],
        12 if fast else 60,
        cost(own_heads * seq * clusters * picks * 8, own_heads * seq * clusters * 2),
        "bias",
    )(info, *tables)

    gain_row, shift_row = gain_one[None, :], shift_one[None, :]
    shapes = [
        array((width, groups * rows), BF),
        array((own_heads, 3 * hs, seq), BF),
        array((own_heads, seq, 2 * hs), BF),
    ]
    held = []
    split_peers = peers if peers <= 2 else 1
    for group in sorted(range(groups), key=lambda g: min(g, groups - g)):
        arrival = mine[group]
        first = ()
        if group == 1:
            arrival = after(arrival, bias, held, cot_got, [mine[hop] for hop in range(2, groups)])
        chunk = [arrival]
        chunk += early if group == 0 else [along_peers(arrival, -hop) for hop in range(1, peers)]
        if peers > 2:
            chunk = [jnp.concatenate(chunk, axis=0)]
        span = peers * rows
        if peers > 2:
            specs_in = [pl.BlockSpec((rows, width), lambda p, s: (p, 0))]
            grid = (peers,)
            outs = [
                pl.BlockSpec((width, rows), lambda p, s, g=group: (0, g)),
                pl.BlockSpec((own_heads, 3 * hs, rows), lambda p, s, g=group: (0, 0, g * peers + p)),
                pl.BlockSpec((own_heads, rows, 2 * hs), lambda p, s, g=group: (0, g * peers + p, 0)),
            ]
        else:
            specs_in = [whole((rows, width))] * split_peers
            grid = (1,)
            outs = [
                pl.BlockSpec((width, rows), lambda p, s, g=group: (0, g)),
                pl.BlockSpec((own_heads, 3 * hs, span), lambda p, s, g=group: (0, 0, g)),
                pl.BlockSpec((own_heads, span, 2 * hs), lambda p, s, g=group: (0, g, 0)),
            ]
        old = 1 + split_peers + 3
        held = prefetched(
            functools.partial(project_kernel, peers=split_peers, olds=len(held)),
            grid,
            specs_in
            + [
                whole((1, width)),
                whole((1, width)),
                pl.BlockSpec((1, 3 * feats, width), lambda p, s: (s[0], 0, 0)),
            ]
            + [pl.BlockSpec(memory_space=pl.ANY)] * len(held),
            outs,
            shapes,
            16 if fast else 60,
            cost(6 * span * width * feats, span * width * 4),
            "project",
            alias={old + k: k for k in range(len(held))},
            first=first,
        )(info, *chunk, gain_row, shift_row, w_in, *held)
    hat_own, feat, kv = held

    ids_full = pl.BlockSpec((1, 1, seq), lambda h, r: (h, 0, 0))
    feat_full = pl.BlockSpec((1, 3 * hs, seq), lambda h, r: (h, 0, 0))
    kv_full = pl.BlockSpec((1, seq, 2 * hs), lambda h, r: (h, 0, 0))
    bias_full = pl.BlockSpec((1, seq, clusters), lambda h, r: (h, 0, 0))
    head_rows = pl.BlockSpec((hs, rows), lambda h, r: (h, 0))
    mix_spec = pl.BlockSpec((1, 1, hs + 8, rows), lambda h, r: (h, r, 0, 0))
    stat_spec = pl.BlockSpec((1, hs + 8, clusters), lambda h, r: (h, 0, 0))
    cen_spec = pl.BlockSpec((1, hs, clusters), lambda h, r: (h, 0, 0))
    own_rows = groups * rows
    pair_flops = own_heads * own_rows * seq * 256

    one = [
        pl.BlockSpec(spec.block_shape, functools.partial(lambda h, f: f(h, 0), f=spec.index_map))
        for spec in (ids_full, feat_full, kv_full, bias_full, stat_spec, cen_spec, head_rows)
    ]
    ids_one, feat_one, kv_one, bias_one, stat_one, cen_one, rows_one = one
    part_one = pl.BlockSpec((1, hs + 16, clusters), lambda h: (h, 0, 0))
    mix_one = pl.BlockSpec((1, groups, hs + 8, rows), lambda h: (h, 0, 0, 0))
    all_groups = pl.BlockSpec((groups, hs, rows), lambda h: (0, h, 0))
    own_one = pl.BlockSpec((1, own_rows, 2 * hs), lambda h: (h, 0, 0))
    results = pl.pallas_call(
        functools.partial(forward_kernel, size=size, groups=groups, rows=rows),
        grid=(own_heads,),
        in_specs=[ids_one, feat_one, kv_one, bias_one],
        out_specs=[rows_one] * groups + [mix_one, stat_one, cen_one],
        out_shape=[array((feats, rows), BF)] * groups
        + [
            array((own_heads, groups, hs + 8, rows), F32),
            array((own_heads, hs + 8, clusters), F32),
            array((own_heads, hs, clusters), BF),
        ],
        compiler_params=params(32 if fast else 60, 1),
        cost_estimate=cost(6 * pair_flops, 8e6, own_heads * own_rows * seq),
        name="attend",
    )(ids_all, feat, kv, bias)
    attn_t = results[:groups]
    mixed, stats, centroid = results[groups:]

    arrived = [attn_t[0]] + [along_groups(attn_t[hop], hop) for hop in range(1, groups)]

    chunks = 4
    part = hidden // chunks
    lead = 80
    w_out_g = w_out.reshape(groups, feats, width)
    gain_row2, shift_row2 = gain_two[None, :], shift_two[None, :]
    square = whole((rows, width))
    column = pl.BlockSpec((rows, part), lambda i, s: (0, i))
    norm_spec = whole((8, width))
    if fast:
        kept_shapes = [
            array((rows, hidden + hidden // 2 + width), BF),
            array((width + 16, rows), BF),
            array((rows, hidden // 2), BF),
            array((width + 16, rows), BF),
        ]
        kept_specs = [whole(item.shape) for item in kept_shapes]
        kept_specs[2] = pl.BlockSpec((rows, part // 2), lambda i, s: (0, i))
    else:
        kept_shapes = [
            array((8, width), F32),
            array((rows, hidden), BF),
            array((rows, width), BF),
            array((rows, hidden), BF),
            array((rows, width), BF),
        ]
        kept_specs = [norm_spec, column, square, column, square]
    results = prefetched(
        functools.partial(block_kernel, groups=groups, chunks=chunks, fast=fast),
        (chunks,),
        [whole((feats, rows))] * groups
        + [
            square,
            whole((1, width)),
            whole((1, width)),
            whole((groups, feats, width)),
            pl.BlockSpec((width, part), lambda i, s: (0, i)),
            pl.BlockSpec((part, width), lambda i, s: (i, 0)),
            square,
        ],
        [square, square] + kept_specs + [whole((feats, rows))] * groups,
        [array((rows, width), BF), array((rows, width), F32)]
        + kept_shapes
        + [array((feats, rows), BF)] * groups,
        28 if fast else 60,
        cost(8 * rows * width * hidden, 4 * width * hidden, rows * hidden),
        "feed",
        scratch=[
            pltpu.VMEM((rows, width), F32),
            pltpu.VMEM((rows, 128), F32),
            pltpu.VMEM((rows, width), BF),
            pltpu.VMEM((rows, width), F32),
            pltpu.VMEM((rows, width), F32),
        ],
    )(info, *arrived, tokens, gain_row2, shift_row2, w_out_g, w_up, w_down, cotangent)
    output, d_resid = results[:2]
    kept, d_attn = results[2:-groups], results[-groups:]
    grads = [d_attn[0]] + [along_groups(d_attn[hop], -hop) for hop in range(1, groups)]

    def weight_parts():
        far, low_far, act_own, low_own = kept
        got, low_got = along_peers(far, 1), along_peers(low_far, 1)
        high = block_rows + 16
        chunk = pl.BlockSpec((rows, part), lambda i, s: (0, i ^ 2 ^ s[3]))
        branch = pl.BlockSpec((rows, width), lambda i, s: (0, hidden * 3 // 2 // width))
        act_spec = pl.BlockSpec((rows, part // 2), lambda i, s: (0, i))
        act_there = pl.BlockSpec((rows, part // 2), lambda i, s: (0, 2 * hidden // part + i))
        low_spec = whole((width + 16, rows))
        shape_u = (2, groups, high, width)
        shape_d = (2, groups, high, width)
        parts = [(1, groups, tall, width) for tall in (lead, high - lead, high)]
        results = prefetched(
            functools.partial(weights_kernel, groups=groups),
            (4,),
            [chunk, chunk, branch, branch, act_spec, act_there, low_spec, low_spec, square, square],
            [whole(item) for item in parts]
            + [pl.BlockSpec((1,) + shape_u[1:], lambda i, s: (jnp.maximum(i - 2, 0), 0, 0, 0))]
            + [whole(item) for item in parts]
            + [whole(shape_d)],
            ([array(item, BF) for item in parts] + [array(shape_u, BF)]) * 2,
            28,
            cost(8 * rows * width * hidden, 6 * width * hidden),
            "weights",
            scratch=[pltpu.VMEM((groups, block_rows, width), F32)],
        )(info, far, got, far, got, act_own, got, low_own, low_got, cotangent, *cot_got)
        return results[:3], results[3], results[4:7], results[7]

    def weight_second(keep_u, got_u, keep_d, got_d, inner, inner_got, late_u, late_d):
        def block(shape, at):
            return pl.BlockSpec((1,) + shape[1:], lambda i: (at, 0, 0, 0))

        high, lines = keep_u.shape[2], inner.shape[2]
        shapes = [(groups, high + lines + late_u.shape[2], width)] * 2 + [(groups, lines, width)]
        return pl.pallas_call(
            second_kernel,
            grid=(1,),
            in_specs=[
                block(item.shape, item.shape[0] - 1) for item in (keep_u, got_u, keep_d, got_d)
            ]
            + [whole(item.shape) for item in (inner, inner_got, late_u, late_d)],
            out_specs=[whole(shape) for shape in shapes],
            out_shape=[array(shape, BF) for shape in shapes],
            compiler_params=params(24, 1),
            cost_estimate=cost(groups * high * width * 2, groups * high * width * 12),
            name="second",
        )(keep_u, got_u, keep_d, got_d, inner, inner_got, late_u, late_d)

    def weight_third(keep_u, got_u, keep_d, got_d, by_y, by_x, inner, inner_got, by_xy):
        def block(shape, at):
            return pl.BlockSpec((1,) + shape[1:], lambda i, s: (at, 0, 0, 0))

        left = keep_u.shape[2] - lead
        talls = [(2 * lead, width)] * groups + [(2 * left + inner.shape[2], width)] * groups
        more = (by_y, by_x)
        return prefetched(
            third_kernel,
            (1,),
            [block(item.shape, 0) for item in (keep_u, got_u, keep_d, got_d)]
            + [whole(by_y.shape), whole(by_x.shape)]
            + [block(inner.shape, 0)] * 2
            + [whole(by_xy.shape)],
            [whole(tall) for tall in talls],
            [array(tall, BF) for tall in talls],
            24,
            cost(groups * 256 * width * 4, groups * 256 * width * 8),
            "third",
            first=home,
        )(info, keep_u, got_u, keep_d, got_d, by_y, by_x, inner, inner_got, by_xy)

    def weight_fourth(came, high, lines, first):
        tall = 2 * high + (3 * lines + 8 if lines else 0)
        done = prefetched(
            functools.partial(fourth_kernel, groups=groups, high=high, feats=3 * feats),
            (1,),
            [whole(came[0].shape)] * groups,
            whole((tall, width)),
            array((tall, width), BF),
            16,
            cost(groups * tall * width, groups * tall * width * 2),
            "fourth",
            scratch=[pltpu.VMEM((groups, lines, width), F32)] if lines else [],
            first=first,
        )(info, *came)
        return [done] + [along_dp(done, mask) for mask in (1, 2, 3)]

    def weight_spread(firsts, lasts, high, ready):
        at = me * block_rows
        wq_rows = lax.dynamic_slice_in_dim(w_query, at, block_rows).astype(F32)
        wkv_rows = lax.dynamic_slice_in_dim(w_keyval, at, block_rows).astype(F32)
        pair = jnp.stack([shift_one, gain_one] + [shift_one] * 6, axis=1)
        pair = lax.dynamic_slice_in_dim(pair, at, block_rows)
        return prefetched(
            functools.partial(spread_kernel, lead=lead, high=high),
            (4,),
            [whole(item.shape) for item in firsts + lasts]
            + [whole(wq_rows.shape), whole(wkv_rows.shape), whole(pair.shape)],
            [
                pl.BlockSpec((block_rows, part), lambda i, s: (0, i ^ s[3])),
                whole((block_rows, width)),
                pl.BlockSpec((block_rows, width), lambda i, s: (i ^ s[4], 0)),
                whole((8, width)),
                whole((block_rows, width)),
                whole((block_rows, 2 * width)),
                whole((block_rows, 128)),
            ],
            [
                array((block_rows, hidden), F32),
                array((block_rows, width), F32),
                array((hidden // wide, width), F32),
                array((8, width), F32),
                array((block_rows, width), F32),
                array((block_rows, 2 * width), F32),
                array((block_rows, 128), F32),
            ],
            20,
            cost(1e6, 8 * block_rows * width * 6),
            "spread",
            scratch=[pltpu.VMEM((8, width), F32)],
        )(info, *firsts, *lasts, wq_rows, wkv_rows, pair)

    masks = [1 << k for k in range(n_dp.bit_length() - 1)]

    def reduce_rows(partial):
        blocks = partial.reshape(groups, peers, partial.shape[0] // wide, partial.shape[1])

        def of_peer(hop):
            at = (peer_at + hop) % peers
            return lax.dynamic_index_in_dim(blocks, at, axis=1, keepdims=False)

        total = of_peer(0).astype(F32)
        for hop in range(1, peers):
            total = total + along_peers(of_peer(hop), hop).astype(F32)
        total = total.astype(BF)

        def of_group(hop):
            return lax.dynamic_index_in_dim(total, (group_at + hop) % groups, keepdims=False)

        done = of_group(0).astype(F32)
        for hop in range(1, groups):
            done = done + along_groups(of_group(hop), hop).astype(F32)
        for mask in masks:
            done = done.astype(BF)
            done = done.astype(F32) + along_dp(done, mask).astype(F32)
        return done

    if fast:
        send_u, keep_u, send_d, keep_d = weight_parts()
        got_u = [along_dp(item, 1) for item in (send_u[0], send_u[2])]
        got_d = [along_dp(item, 2) for item in (send_d[0], send_d[2])]
    else:
        norm_two, d_up, d_branch, act, normed_two = kept
        total_up = reduce_rows(tn(normed_two, d_up).astype(BF))
        total_down = reduce_rows(tn(act, cotangent).astype(BF))
        found = jnp.stack([nn(item, d_branch).astype(BF) for item in arrived])
        found = [
            lax.dynamic_index_in_dim(found, (group_at + groups - g) % groups, keepdims=False)
            for g in range(groups)
        ]
        total_out = reduce_rows(jnp.concatenate(found, axis=0))
        norm_own = reduce_rows(norm_two[:2].T.astype(BF)).T

    share = prefetched(
        functools.partial(sums_kernel, groups=groups),
        (own_heads,),
        [scalar(spec) for spec in (ids_one, *[rows_one] * groups, mix_one)],
        scalar(part_one),
        array((own_heads, hs + 16, clusters), F32),
        16 if fast else 60,
        cost(own_heads * own_rows * clusters * 160, 2e6),
        "sums",
        first=(keep_u, keep_d) if fast else (),
    )(info, ids_all, *grads, mixed)
    share_got = [along_peers(share, hop) for hop in range(1, peers)]

    back_shapes = [
        array((groups, feats, rows), BF),
        array((own_heads, 2 * hs, own_rows), F32),
        array((own_heads, 2 * hs, max(peers - 1, 1) * own_rows), BF),
    ]
    dq, dkv_own, dkv_send = pl.pallas_call(
        functools.partial(back_kernel, size=size, groups=groups, gots=len(share_got)),
        grid=(own_heads,),
        in_specs=[ids_one, feat_one, kv_one, bias_one]
        + [rows_one] * groups
        + [mix_one, stat_one, cen_one]
        + [part_one] * (1 + len(share_got)),
        out_specs=[
            all_groups,
            pl.BlockSpec((1,) + back_shapes[1].shape[1:], lambda h: (h, 0, 0)),
            pl.BlockSpec((1,) + back_shapes[2].shape[1:], lambda h: (h, 0, 0)),
        ],
        out_shape=back_shapes,
        scratch_shapes=[pltpu.VMEM((seq, 2 * hs), F32), pltpu.VMEM((seq, 2 * clusters), BF)],
        compiler_params=params(36 if fast else 62, 1),
        cost_estimate=cost(14 * pair_flops, 10e6, own_heads * own_rows * seq),
        name="back",
    )(ids_all, feat, kv, bias, *grads, mixed, stats, centroid, share, *share_got)
    if fast:
        dkv_send = after(dkv_send, got_u, got_d)
    dkv_got = [
        along_peers(
            dkv_send if peers == 2 else dkv_send[..., (hop - 1) * own_rows : hop * own_rows], hop
        )
        for hop in range(1, peers)
    ]
    tall = block_rows + 16
    spent = cost(2 * own_rows * width * 3 * feats, 4e6)
    if fast:
        lines = block_rows // 4
        more = [array((4, groups, lines, width), BF)] * 2
    else:
        more = [array((width, 3 * feats), F32), array((16, 3 * feats), F32)]
    results = prefetched(
        functools.partial(inward_kernel, groups=groups, gots=len(dkv_got), fast=fast),
        (1,),
        [whole(back_shapes[0].shape)]
        + [whole(back_shapes[1].shape)] * (1 + len(dkv_got))
        + [whole((width, own_rows))],
        [whole((own_heads, 3 * hs, rows))] * groups + [whole(item.shape) for item in more],
        [array((own_heads, 3 * hs, rows), BF)] * groups + more,
        28 if fast else 60,
        spent,
        "inward",
    )(info, dq, dkv_own, *dkv_got, hat_own)
    d_in, more = results[:groups], results[groups:]
    home = [d_in[0]] + [along_groups(d_in[hop], hop) for hop in range(1, groups)]

    grad_tokens = prefetched(
        functools.partial(final_kernel, groups=groups),
        (1,),
        [whole((own_heads, 3 * hs, rows))] * groups
        + [square, square, whole((1, width)), whole((groups, 3 * feats, width))],
        square,
        array((rows, width), BF),
        24 if fast else 60,
        cost(6 * rows * width * width, 6 * width * width),
        "final",
    )(info, *home, tokens, d_resid, gain_row, w_in)

    if fast:
        keep, far = more
        inner_got = along_peers(far, 1)
        to_y, to_x, to_xy = weight_second(
            keep_u, got_u[1], keep_d, got_d[1], keep, inner_got, send_u[1], send_d[1]
        )
        by_y, by_x, by_xy = along_dp(to_y, 2), along_dp(to_x, 1), along_dp(to_xy, 3)
        sums = weight_third(
            keep_u, got_u[0], keep_d, got_d[0], by_y, by_x, keep, inner_got, by_xy
        )
        came_a, came_b = [sums[0]], [sums[groups]]
        came_a += [along_groups(sums[hop], hop) for hop in range(1, groups)]
        late = after(sums[groups + 1 :], came_a[1])
        came_b += [along_groups(late[hop - 1], hop) for hop in range(1, groups)]
        spread_a = weight_fourth(came_a, lead, 0, (came_b[1], grad_tokens))
        high = keep_u.shape[2] - lead
        spread_b = weight_fourth(came_b, high, lines, spread_a)
        found = weight_spread(spread_a, spread_b, high, came_a[0])
        total_up, total_out, total_down, norms, total_query, total_keyval, vector = found
        norm_own = lax.dynamic_slice_in_dim(norms, me * block_rows, block_rows, axis=1)
        gain_grad, shift_grad = vector[:, 0], vector[:, 1]
    else:
        found, more = more
        found = found.reshape(groups, peers, block_rows, 3 * feats)
        more = jnp.broadcast_to(more, (groups, peers, 16, 3 * feats))
        found = jnp.concatenate([found, more], axis=2).astype(BF)

        def of_peer(hop):
            at = (peer_at + hop) % peers
            return lax.dynamic_index_in_dim(found, at, axis=1, keepdims=False)

        total = of_peer(0).astype(F32)
        for hop in range(1, peers):
            total = total + along_peers(of_peer(hop), hop).astype(F32)
        for mask in masks:
            total = total.astype(BF)
            total = total.astype(F32) + along_dp(total, mask).astype(F32)
        total = total.astype(BF)
        items = [
            lax.dynamic_index_in_dim(total, (group_at + hop) % groups, keepdims=False)
            for hop in range(groups)
        ]
        pieces = [items[0]] + [along_groups(items[hop], hop) for hop in range(1, groups)]
        pieces = jnp.stack(pieces)
        pieces = jnp.stack(
            [
                lax.dynamic_index_in_dim(pieces, (group_at + groups - g) % groups, keepdims=False)
                for g in range(groups)
            ]
        ).astype(F32)
        q_part = pieces[:, :, :feats].transpose(1, 0, 2).reshape(tall, width)
        kv_part = (
            pieces[:, :, feats:]
            .reshape(groups, tall, 2, feats)
            .transpose(1, 2, 0, 3)
            .reshape(tall, 2 * width)
        )
        at = me * block_rows
        wq_rows = lax.dynamic_slice_in_dim(w_query, at, block_rows).astype(F32)
        wkv_rows = lax.dynamic_slice_in_dim(w_keyval, at, block_rows).astype(F32)
        gain_own = lax.dynamic_slice_in_dim(gain_one, at, block_rows)
        shift_own = lax.dynamic_slice_in_dim(shift_one, at, block_rows)
        q_sum, kv_sum = q_part[block_rows], kv_part[block_rows]
        q_part, kv_part = q_part[:block_rows], kv_part[:block_rows]
        shift_grad = jnp.sum(wq_rows * q_sum, axis=1) + jnp.sum(wkv_rows * kv_sum, axis=1)
        along = jnp.sum(wq_rows * q_part, axis=1) + jnp.sum(wkv_rows * kv_part, axis=1)
        total_query = q_part + shift_own[:, None] * q_sum
        total_keyval = kv_part + shift_own[:, None] * kv_sum
        gain_grad = along / gain_own


    return (
        output,
        grad_tokens,
        total_query,
        total_keyval,
        total_out,
        total_up,
        total_down,
        gain_grad,
        shift_grad,
        norm_own[0],
        norm_own[1],
    )


def solution(mesh):
    return jax.shard_map(
        per_device,
        mesh=mesh,
        in_specs=(
            P(("dp", "wide"), None),
            P(("dp", "wide"), None),
            P("dp"),
            P("dp", None, "wide", None),
            P(),
            P(),
            P(),
            P(),
            P(),
            P(),
            P(),
            P(),
            P(),
            P(("dp", "wide"), None),
        ),
        out_specs=(
            P(("dp", "wide"), None),
            P(("dp", "wide"), None),
            P("wide", None),
            P("wide", None),
            P("wide", None),
            P("wide", None),
            P("wide", None),
            P("wide"),
            P("wide"),
            P("wide"),
            P("wide"),
        ),
        check_vma=False,
    )
```

```python
import functools
import math

import jax
import jax.numpy as jnp
import numpy as np
from jax import lax
from jax.experimental import pallas as pl
from jax.experimental.pallas import tpu as pltpu
from jax.sharding import PartitionSpec as P

EPSILON = 1e-05
NEGATIVE = -1e30
EXCLUDED = -3e30
GELU_A = math.sqrt(2.0 / math.pi)
GELU_B = 0.044715
BF = jnp.bfloat16
F32 = jnp.float32


def nn(left, right):
    return lax.dot_general(left, right, (((1,), (0,)), ((), ())), preferred_element_type=F32)


def nt(left, right):
    return lax.dot_general(left, right, (((1,), (1,)), ((), ())), preferred_element_type=F32)


def tn(left, right):
    return lax.dot_general(left, right, (((0,), (0,)), ((), ())), preferred_element_type=F32)


def params(mib, dims):
    return pltpu.CompilerParams(
        vmem_limit_bytes=mib * 1024 * 1024, dimension_semantics=("arbitrary",) * dims
    )


def cost(flops, nbytes, trans=0):
    return pl.CostEstimate(flops=int(flops), bytes_accessed=int(nbytes), transcendentals=int(trans))


def split_low(values):
    high = values.astype(BF)
    return high, (values - high.astype(F32)).astype(BF)


def one_hot_t(ids_row, clusters):
    rows = lax.broadcasted_iota(jnp.int32, (clusters, ids_row.shape[1]), 0)
    return jnp.where(rows == ids_row, 1.0, 0.0).astype(BF)


def key_passes(total, size, score, weigh, blocks=None):
    count = total // size
    if count <= 4:
        if blocks is None:
            blocks = [score(index) for index in range(count)]
        peak = functools.reduce(jnp.maximum, [jnp.max(b, axis=0, keepdims=True) for b in blocks])
        denom, sums = 0.0, None
        for index in range(count):
            expo = jnp.exp(blocks[index] - peak)
            denom = denom + jnp.sum(expo, axis=0, keepdims=True)
            parts = weigh(index, expo)
            sums = parts if sums is None else tuple(x + y for x, y in zip(sums, parts))
        return peak, denom, sums

    def step(index, carry):
        peak, denom, sums = carry
        block = score(index)
        fresh = jnp.maximum(peak, jnp.max(block, axis=0, keepdims=True))
        expo = jnp.exp(block - fresh)
        fade = jnp.exp(peak - fresh)
        parts = weigh(index, expo)
        return (
            fresh,
            denom * fade + jnp.sum(expo, axis=0, keepdims=True),
            tuple(old * fade + new for old, new in zip(sums, parts)),
        )

    shapes = jax.eval_shape(lambda: (score(0), weigh(0, score(0))))
    lanes = shapes[0].shape[1]
    start = (
        jnp.full((1, lanes), NEGATIVE, F32),
        jnp.zeros((1, lanes), F32),
        tuple(jnp.zeros(item.shape, F32) for item in shapes[1]),
    )
    return lax.fori_loop(0, count, step, start)


def key_sum(total, size, step, start):
    count = total // size
    if count <= 4:
        for index in range(count):
            start = step(index, start)
        return start
    return lax.fori_loop(0, count, step, start)


def spot_of(index, size):
    if isinstance(index, int):
        return pl.ds(index * size, size)
    return pl.ds(pl.multiple_of(index * size, size), size)


def piece(ref, index, size, axis):
    spot = spot_of(index, size)
    return ref[spot, :] if axis == 0 else ref[:, spot]


def table_kernel(info, *refs, picks):
    parts, out = refs[:-1], refs[-1]
    total = parts[0][:, :picks]
    for part in parts[1:]:
        total = total + part[:, :picks]
    out[:, :picks] = total
    rows = parts[0].shape[1] - picks
    for group, part in enumerate(parts):
        out[:, picks + group * rows : picks + (group + 1) * rows] = part[:, picks:]


def bias_kernel(info, *refs, groups, peers, rows, picks):
    tables, (bias_ref, ids_ref) = refs[:peers], refs[peers:]
    part = pl.program_id(0)
    owner = (
        lax.rem(info[0] + part // peers, groups) * peers + lax.rem(info[1] + part % peers, peers)
    )
    heads, _, clusters = tables[0].shape
    place = owner * rows + lax.broadcasted_iota(jnp.int32, (rows, clusters), 0)
    plain = jnp.where(place >= info[2], EXCLUDED, NEGATIVE)
    for head in range(heads):
        top = tables[0][head, :picks]
        for table in tables[1:]:
            top = top + table[head, :picks]
        value = plain
        for pick in range(picks):
            value = jnp.where(place == top[pick : pick + 1, :], 0.0, value)
        bias_ref[head] = value.astype(BF)

    @pl.when(part == 0)
    def ids():
        lines = rows // clusters
        for head in range(heads):
            row = []
            for group in range(groups):
                for table in tables:
                    for line in range(lines):
                        at = picks + group * lines + line
                        row.append(table[head, at : at + 1, :])
            ids_ref[head] = jnp.concatenate(row, axis=1)


def project_kernel(info, *refs, peers, olds):
    parts = refs[:peers]
    gain_ref, shift_ref, w_ref = refs[peers : peers + 3]
    hat_ref, feat_ref, kv_ref = refs[peers + 3 + olds :]
    rows = hat_ref.shape[1]
    for peer in range(peers):
        values = parts[peer][...].astype(F32)
        centered = values - jnp.mean(values, axis=-1, keepdims=True)
        variance = jnp.mean(centered * centered, axis=-1, keepdims=True)
        scaled = centered * lax.rsqrt(variance + EPSILON) * gain_ref[...]
        if peer == 0:
            hat_ref[...] = scaled.astype(BF).T
        low = (scaled + shift_ref[...]).astype(BF)
        found = nt(w_ref[0], low)
        heads, triple = feat_ref.shape[0], feat_ref.shape[1]
        hs = triple // 3
        spot = slice(peer * rows, (peer + 1) * rows)
        for head in range(heads):
            base = head * triple
            query = (found[base : base + hs] * 0.125).astype(BF)
            pair = found[base + hs : base + triple].astype(BF)
            feat_ref[head, :hs, spot] = query
            feat_ref[head, hs:, spot] = pair
            kv_ref[head, spot, :] = pair.T


def forward_kernel(ids_all, feat, kv, bias, *refs, size, groups, rows):
    outs = refs[:groups]
    mix_ref, stat_ref, cen_ref = refs[groups:]
    hs = feat.shape[1] // 3
    keys = kv.shape[1]
    count = keys // size
    clusters = bias.shape[2]
    kv_h, bias_h = kv.at[0], bias.at[0]
    queries_all, kvt = feat.at[0, :hs], feat.at[0, hs:]
    hot_all = one_hot_t(ids_all[0], clusters)
    ones = jnp.ones((16, keys), BF)
    sums = nt(jnp.concatenate([queries_all[...], ones], axis=0), hot_all)
    counts = sums[hs : hs + 1]
    centroid = (sums[:hs] / jnp.maximum(counts, 1.0)).astype(BF)
    padded = jnp.concatenate([centroid, jnp.zeros_like(centroid)], axis=0)

    def cluster_score(index):
        scores = nn(piece(kv_h, index, size, 0), padded)
        outside = piece(bias_h, index, size, 0).astype(F32) < 2.0 * NEGATIVE
        return jnp.where(outside, NEGATIVE, scores)

    def cluster_weigh(index, expo):
        top = piece(bias_h, index, size, 0).astype(F32) == 0.0
        mass = jnp.sum(jnp.where(top, expo, 0.0), axis=0, keepdims=True)
        other = jnp.where(top, 0.0, expo).astype(BF)
        return nn(piece(kvt, index, size, 1), other), mass

    peers = keys // (groups * rows)
    hots, sides = [], []
    for group in range(groups):
        spot = slice(group * peers * rows, group * peers * rows + rows)
        hot = one_hot_t(ids_all[0, :, spot], clusters)
        queries = queries_all[:, spot]
        hots.append(hot)
        sides.append(jnp.concatenate([queries, jnp.zeros_like(queries), hot], axis=0))

    def member_score(group, index):
        both = jnp.concatenate([piece(kv_h, index, size, 0), piece(bias_h, index, size, 0)], axis=1)
        return nn(both, sides[group])

    def member_weigh(index, expo):
        return (nn(piece(kvt, index, size, 1), expo.astype(BF)),)

    short = count <= 4
    ahead = None
    if short:
        ahead = [member_score(0, index) for index in range(count)]
    peak, denom, (rest, mass) = key_passes(keys, size, cluster_score, cluster_weigh)
    rest = rest[hs:] / denom
    mass = mass / denom
    blank = jnp.zeros((5, clusters), F32)
    stats = jnp.concatenate([rest, mass, peak + jnp.log(denom), counts, blank], axis=0)
    stat_ref[0] = stats
    cen_ref[0] = centroid
    high, low = split_low(stats)
    table = jnp.concatenate([high, low], axis=1)
    for group in range(groups):
        gathered = nn(table, jnp.concatenate([hots[group], hots[group]], axis=0))
        blocks, ahead = ahead, None
        if short and group + 1 < groups:
            ahead = [member_score(group + 1, index) for index in range(count)]
        score = functools.partial(member_score, group)
        peak, denom, (mix,) = key_passes(keys, size, score, member_weigh, blocks)
        mix = mix[hs:] / denom
        outs[group][...] = (gathered[hs : hs + 1] * mix + gathered[:hs]).astype(BF)
        level = jnp.broadcast_to(peak + jnp.log(denom), (8, rows))
        mix_ref[0, group] = jnp.concatenate([mix, level], axis=0)


def sums_kernel(info, ids_own, *refs, groups):
    grads, (mix_ref, part_ref) = refs[:groups], refs[groups:]
    hs = grads[0].shape[0]
    total = None
    for group in range(groups):
        rows = grads[group].shape[1]
        step = ids_own.shape[2] // groups
        hot = one_hot_t(ids_own[0, :, group * step : group * step + rows], part_ref.shape[2])
        grad = grads[group][...]
        along = jnp.sum(grad.astype(F32) * mix_ref[0, group, :hs], axis=0, keepdims=True)
        high, low = split_low(along)
        pad = jnp.zeros((14, rows), BF)
        part = nt(jnp.concatenate([grad, high, low, pad], axis=0), hot)
        total = part if total is None else total + part
    part_ref[0] = total


def back_kernel(ids_all, feat, kv, bias, *refs, size, groups, gots):
    grads = refs[:groups]
    mix_ref, stat_ref, cen_ref = refs[groups : groups + 3]
    shares = refs[groups + 3 : groups + 4 + gots]
    dq_ref, own_ref, send_ref, total, both = refs[groups + 4 + gots :]
    hs, rows = grads[0].shape
    keys = kv.shape[1]
    count = keys // size
    peers = keys // (groups * rows)
    clusters = bias.shape[2]
    kv_h, bias_h = kv.at[0], bias.at[0]
    queries_all, kvt = feat.at[0, :hs], feat.at[0, hs:]
    stats = stat_ref[0]
    high, low = split_low(stats[hs : hs + 8])
    table = jnp.concatenate([high, low], axis=1)
    hots, sides, levels, deltas, pads, rights = [], [], [], [], [], []
    for group in range(groups):
        spot = slice(group * peers * rows, group * peers * rows + rows)
        hot = one_hot_t(ids_all[0, :, spot], clusters)
        queries = queries_all[:, spot]
        blank = jnp.zeros_like(queries)
        hots.append(jnp.concatenate([hot, hot], axis=0))
        sides.append(jnp.concatenate([queries, blank, hot], axis=0))
        mass = nn(table, hots[group])[0:1]
        back = (mass * grads[group][...].astype(F32)).astype(BF)
        levels.append(mix_ref[0, group, hs : hs + 1])
        deltas.append(jnp.sum(back.astype(F32) * mix_ref[0, group, :hs], axis=0, keepdims=True))
        pads.append(jnp.concatenate([blank, back], axis=0))
        turned = jnp.concatenate([queries, blank], axis=0)
        rights.append(jnp.concatenate([turned, pads[group]], axis=1).T)

    def scores(group, index):
        kv_c = piece(kv_h, index, size, 0)
        pair = jnp.concatenate([kv_c, piece(bias_h, index, size, 0)], axis=1)
        return nn(pair, sides[group]), nn(kv_c, pads[group])

    def finish(group, index, found, dq):
        weights = jnp.exp(found[0] - levels[group])
        grad_s = (weights * (found[1] - deltas[group])).astype(BF)
        part = nn(jnp.concatenate([grad_s, weights.astype(BF)], axis=1), rights[group])
        spot = spot_of(index, size)
        if group == 0:
            total[spot, :] = part
        else:
            total[spot, :] += part
        return dq + nn(piece(kvt, index, size, 1), grad_s)

    rest, mass = stats[:hs], stats[hs : hs + 1]
    level, counts = stats[hs + 1 : hs + 2], stats[hs + 2 : hs + 3]
    centroid = cen_ref[0]
    part = shares[0][0]
    for share in shares[1:]:
        part = part + share[0]
    d_rest = part[:hs].astype(BF)
    d_mass = part[hs : hs + 1] + part[hs + 1 : hs + 2]
    delta = jnp.sum(d_rest.astype(F32) * rest, axis=0, keepdims=True) + d_mass * mass
    cen_pad = jnp.concatenate([centroid, jnp.zeros_like(centroid)], axis=0)
    rest_pad = jnp.concatenate([jnp.zeros_like(centroid), d_rest], axis=0)
    right = jnp.concatenate([cen_pad, rest_pad], axis=1).T

    def cluster_step(index, summed):
        kv_c = piece(kv_h, index, size, 0)
        marks = piece(bias_h, index, size, 0).astype(F32)
        probs = jnp.exp(nn(kv_c, cen_pad) - level)
        probs = jnp.where(marks < 2.0 * NEGATIVE, 0.0, probs)
        top = marks == 0.0
        d_probs = jnp.where(top, d_mass, nn(kv_c, rest_pad))
        d_score = (probs * (d_probs - delta)).astype(BF)
        other = jnp.where(top, 0.0, probs).astype(BF)
        both[spot_of(index, size), :] = jnp.concatenate([d_score, other], axis=1)
        return summed + nn(piece(kvt, index, size, 1), d_score)

    start = jnp.zeros((2 * hs, rows), F32)
    zero = jnp.zeros((2 * hs, clusters), F32)
    member_dq = []
    if count <= 4:
        tasks = [(group, index) for group in range(groups) for index in range(count)]
        ahead = scores(*tasks[0])
        d_cen = key_sum(keys, size, cluster_step, zero)
        dq = start
        for step, (group, index) in enumerate(tasks):
            found = ahead
            if step + 1 < len(tasks):
                ahead = scores(*tasks[step + 1])
            dq = finish(group, index, found, dq)
            if index == count - 1:
                member_dq.append(dq[:hs] * 0.125)
                dq = start
    else:
        d_cen = key_sum(keys, size, cluster_step, zero)
        for group in range(groups):

            def step(index, dq, group=group):
                return finish(group, index, scores(group, index), dq)

            member_dq.append(lax.fori_loop(0, count, step, start)[:hs] * 0.125)
    d_cen = d_cen[:hs] * 0.125 / jnp.maximum(counts, 1.0)
    high, low = split_low(d_cen)
    table = jnp.concatenate([high, low], axis=1)
    for group in range(groups):
        base = group * peers * rows
        dq_ref[group] = (member_dq[group] + nn(table, hots[group])).astype(BF)
        own = total[base : base + rows, :] + nn(both[base : base + rows, :], right)
        own_ref[0, :, group * rows : (group + 1) * rows] = own.T
        for peer in range(1, peers):
            spot = (peer - 1) * groups * rows + group * rows
            found = total[base + peer * rows : base + (peer + 1) * rows, :]
            send_ref[0, :, spot : spot + rows] = found.astype(BF).T


def join_kernel(dq_ref, own_ref, *refs, groups):
    gots, outs = refs[:-groups], refs[-groups:]
    heads, _, rows = outs[0].shape
    hs = dq_ref.shape[1] // heads
    for head in range(heads):
        for group in range(groups):
            spot = slice(group * rows, (group + 1) * rows)
            pair = own_ref[head, :, spot]
            for got in gots:
                pair = pair + got[head, :, spot].astype(F32)
            outs[group][head, :hs] = dq_ref[group, head * hs : (head + 1) * hs]
            outs[group][head, hs:] = pair.astype(BF)


def block_kernel(info, *refs, groups, chunks, fast):
    (attn, rest) = (refs[:groups], refs[groups:])
    x_ref, gain_ref, shift_ref, wo_ref, up_ref, down_ref, cot_ref = rest[:7]
    out_ref, dres_ref = rest[7:9]
    if fast:
        far_ref, low_far, act_ref, low_ref = rest[9:13]
        rest = rest[13:]
        hidden = far_ref.shape[1] * 4 // 7
    else:
        dn_ref, dup_ref, dbr_ref, act_ref, low_ref = rest[9:14]
        rest = rest[14:]
    dat = rest[:groups]
    hat_ref, inv_ref, normed, back, total = rest[groups:]
    index = pl.program_id(0)

    @pl.when(index == 0)
    def before():
        resid = x_ref[...].astype(F32)
        for group in range(groups):
            owner = lax.rem(info[0] + groups - group, groups)
            resid = resid + tn(attn[group][...], wo_ref[owner])
        total[...] = resid
        centered = resid - jnp.mean(resid, axis=-1, keepdims=True)
        variance = jnp.mean(centered * centered, axis=-1, keepdims=True)
        inverse = lax.rsqrt(variance + EPSILON)
        hat = centered * inverse
        hat_ref[...] = hat
        inv_ref[...] = jnp.broadcast_to(inverse, inv_ref.shape)
        low = (hat * gain_ref[...] + shift_ref[...]).astype(BF)
        normed[...] = low
        if fast:
            feats = attn[0].shape[0]
            half = feats // 2
            turned = low.T
            for group in range(groups):
                first = turned[group * feats : group * feats + half]
                second = turned[group * feats + half : (group + 1) * feats]
                spot = slice(group * half, (group + 1) * half)
                low_ref[spot, :] = jnp.where(info[1] == 0, first, second)
                low_far[spot, :] = jnp.where(info[1] == 0, second, first)
                first = attn[group][:half]
                second = attn[group][half:]
                spot = slice((groups + group) * half, (groups + group + 1) * half)
                low_ref[spot, :] = jnp.where(info[1] == 0, first, second)
                low_far[spot, :] = jnp.where(info[1] == 0, second, first)
        else:
            low_ref[...] = low
        back[...] = jnp.zeros_like(back)

    up = nn(normed[...], up_ref[...])
    grad_act = nt(cot_ref[...], down_ref[...])
    square = up * up
    inner = GELU_A * (up + GELU_B * up * square)
    curve = jnp.tanh(inner)
    act = (0.5 * up * (1.0 + curve)).astype(BF)
    slope = 0.5 * (1.0 + curve) + 0.5 * up * (1.0 - curve * curve) * (
        GELU_A * (1.0 + 3.0 * GELU_B * square)
    )
    d_up = (grad_act * slope).astype(BF)
    if fast:
        part = act.shape[1]
        half = part // 2
        first, second = act[:, :half], act[:, half:]
        act_ref[...] = jnp.where(info[1] == 0, first, second)
        far_ref[:, pl.ds(pl.multiple_of(index * part, part), part)] = d_up
        spot = pl.ds(pl.multiple_of(hidden + index * half, half), half)
        far_ref[:, spot] = jnp.where(info[1] == 0, second, first)
    else:
        dup_ref[...] = d_up
        act_ref[...] = act
    back[...] += nt(d_up, up_ref[...])
    total[...] += nn(act, down_ref[...])

    @pl.when(index == chunks - 1)
    def after():
        out_ref[...] = total[...].astype(BF)
        d_normed = back[...]
        hat = hat_ref[...]
        gain_part = jnp.sum(d_normed * hat, axis=0, keepdims=True)
        shift_part = jnp.sum(d_normed, axis=0, keepdims=True)
        if fast:
            rows, width = low_far.shape[1], d_normed.shape[1]
            fold = []
            for part_row in split_low(gain_part) + split_low(shift_part):
                fold += [part_row[:, k : k + rows].astype(F32) for k in range(0, width, rows)]
            fold.append(jnp.zeros((low_far.shape[0] - width - len(fold), rows), F32))
            folded = jnp.concatenate(fold, axis=0).astype(BF)
            low_far[width:, :] = folded
            low_ref[width:, :] = folded
        else:
            blank = jnp.zeros((6, d_normed.shape[1]), F32)
            dn_ref[...] = jnp.concatenate([gain_part, shift_part, blank], axis=0)
        gy = d_normed * gain_ref[...]
        mean_one = jnp.mean(gy, axis=-1, keepdims=True)
        mean_two = jnp.mean(gy * hat, axis=-1, keepdims=True)
        d_resid = cot_ref[...].astype(F32) + inv_ref[:, 0:1] * (gy - mean_one - hat * mean_two)
        dres_ref[...] = d_resid
        branch = d_resid.astype(BF)
        if fast:
            far_ref[:, hidden * 3 // 2 :] = branch
        else:
            dbr_ref[...] = branch
        for group in range(groups):
            owner = lax.rem(info[0] + groups - group, groups)
            dat[group][...] = nt(wo_ref[owner], branch).astype(BF)


def weights_kernel(info, *refs, groups):
    (dup, dup_got, dbr, dbr_got, act, act_got, low, low_got, cot, cot_got) = refs[:10]
    send_u, keep_u, send_d, keep_d, outs = refs[10:12], refs[12], refs[13:15], refs[15], refs[16]
    width = cot.shape[1]
    lead = send_u[0].shape[2] - keep_u.shape[2]

    def leave(send, turn, spot, block, first):
        if turn:
            send[0][0, spot, lead + first : lead + first + block.shape[0]] = block
        elif first:
            send[1][0, spot, first - lead : first - lead + block.shape[0]] = block
        else:
            send[0][0, spot, :lead] = block[:lead]
            send[1][0, spot, : block.shape[0] - lead] = block[lead:]

    index = pl.program_id(0)
    group_at, place_u, place_d = info[0], info[3], info[4]
    rows = width // (2 * groups)
    quarter = rows // 4
    stay = groups * rows

    @pl.when(index == 0)
    def first():
        found = nn(low[stay:width, :], dbr[...]) + nn(low_got[stay:width, :], dbr_got[...])
        fold = low[width:, :].astype(F32) + low_got[width:, :].astype(F32)
        times = width // fold.shape[1]
        norms = []
        for part in range(2):
            both = fold[2 * part * times : (2 * part + 1) * times]
            both = both + fold[(2 * part + 1) * times : (2 * part + 2) * times]
            norms.append(jnp.concatenate([both[k : k + 1] for k in range(times)], axis=1))
        norms = jnp.concatenate(norms + [jnp.zeros((6, width), F32)], axis=0)
        for group in range(groups):
            block = found[group * rows : (group + 1) * rows]
            outs[group] = block
            for part in range(4):
                tail = block[part * quarter + 16 : (part + 1) * quarter]
                tail = jnp.concatenate([tail, norms], axis=0).astype(BF)
                place = lax.bitwise_xor(part, place_d)

                for turn in range(2):

                    @pl.when(place == 2 + turn)
                    def leaves_more(turn=turn, tail=tail, group=group):
                        leave(send_d, turn, (groups - group) % groups, tail, rows)

                @pl.when(place < 2)
                def stays_more():
                    keep_d[place, (groups - group) % groups, rows:] = tail

    up = nn(low[:stay, :], dup[...]) + nn(low_got[:stay, :], dup_got[...])
    at = lax.bitwise_xor(lax.bitwise_xor(index, 2), place_u)
    for group in range(groups):
        spot = lax.rem(group + groups - group_at, groups)
        block = up[group * rows : (group + 1) * rows].astype(BF)
        away = (groups - group) % groups
        start = pl.multiple_of(at * quarter, 8)
        other = outs[group, pl.ds(start, 16), :].astype(BF)

        for turn in range(2):

            @pl.when(index == turn)
            def leaves(turn=turn, spot=spot, block=block, away=away, other=other):
                leave(send_u, turn, spot, block, 0)
                leave(send_u, turn, away, other, rows)

        @pl.when(index >= 2)
        def stays():
            keep_u[0, spot, :rows] = block
            keep_u[0, away, rows:] = other

    down = tn(act[...], cot[...]) + tn(act_got[...], cot_got[...])
    spot = lax.rem(index + groups - group_at, groups)
    for part in range(4):
        block = down[part * rows : (part + 1) * rows].astype(BF)
        place = lax.bitwise_xor(part, place_d)

        for turn in range(2):

            @pl.when(place == 2 + turn)
            def leaves_down(turn=turn, block=block):
                leave(send_d, turn, spot, block, 0)

        @pl.when(place < 2)
        def stays_down():
            keep_d[place, spot, :rows] = block


def second_kernel(keep_u, got_u, keep_d, got_d, inner, inner_got, late_u, late_d, to_y, to_x, to_xy):
    rows, lines = keep_u.shape[2], inner.shape[2]
    lead = got_u.shape[2] - rows
    to_y[:, :rows] = (keep_u[0].astype(F32) + got_u[0, :, lead:].astype(F32)).astype(BF)
    to_x[:, :rows] = (keep_d[0].astype(F32) + got_d[0, :, lead:].astype(F32)).astype(BF)
    last = to_y.shape[1] - lines
    to_y[:, last:] = (inner[1].astype(F32) + inner_got[1].astype(F32)).astype(BF)
    to_x[:, last:] = (inner[2].astype(F32) + inner_got[2].astype(F32)).astype(BF)
    to_xy[...] = (inner[3].astype(F32) + inner_got[3].astype(F32)).astype(BF)
    to_y[:, rows:last] = late_d[0]
    to_x[:, rows:last] = late_u[0]


def third_kernel(info, keep_u, one_u, keep_d, one_d, by_y, by_x, inner, inner_got, by_xy, *outs):
    rows, lines = keep_u.shape[2], inner.shape[2]
    early = one_u.shape[2] - rows
    groups = len(outs) // 2
    lead = outs[0].shape[0] // 2
    left = rows - lead
    late, mid = slice(rows, 2 * rows - early), slice(2 * rows - early, None)

    def added(keep, one, rest, by, group):
        got = jnp.concatenate([one[0, group, :early], rest[group, late]], axis=0)
        total = keep[0, group].astype(F32) + got.astype(F32)
        return (total + by[group, :rows].astype(F32)).astype(BF)

    for group in range(groups):
        first, last = outs[group], outs[groups + group]
        up = added(keep_u, one_u, by_x, by_y, group)
        down = added(keep_d, one_d, by_y, by_x, group)
        first[:lead] = up[:lead]
        first[lead:] = down[:lead]
        last[:left] = up[lead:]
        last[left : 2 * left] = down[lead:]
        both = inner[0, group].astype(F32) + inner_got[0, group].astype(F32)
        both = both + by_y[group, mid].astype(F32) + by_x[group, mid].astype(F32)
        last[2 * left :] = (both + by_xy[group].astype(F32)).astype(BF)


def fourth_kernel(info, *refs, groups, high, feats):
    parts, out = refs[:groups], refs[groups]
    total = parts[0][: 2 * high].astype(F32)
    for part in parts[1:]:
        total = total + part[: 2 * high].astype(F32)
    out[: 2 * high] = total.astype(BF)
    if parts[0].shape[0] == 2 * high:
        return
    turned = refs[groups + 1]
    third = feats // 3
    for group in range(groups):
        turned[group] = parts[group][2 * high :].astype(F32)
    spots = [lax.rem(info[0] + groups - owner, groups) for owner in range(groups)]
    found, sums = [], []
    for kind in range(3):
        lanes = slice(kind * third, (kind + 1) * third)
        found.append(jnp.concatenate([turned[spot, :, lanes] for spot in spots], axis=1))
        line = [turned[spot, 8 * kind : 8 * kind + 8, 3 * third :] for spot in spots]
        sums.append(jnp.concatenate(line, axis=1)[:1])
    sums.append(jnp.zeros((5, out.shape[1]), F32))
    out[2 * high :] = jnp.concatenate(found + sums, axis=0).astype(BF)


def spread_kernel(info, *refs, lead, high):
    firsts, lasts, (wq, wkv, pair) = refs[:4], refs[4:8], refs[8:11]
    up_ref, out_ref, down_ref, norm_ref, gq_ref, gkv_ref, vec_ref, sums = refs[11:]
    index = pl.program_id(0)
    rows, width = down_ref.shape
    quarter = rows // 4
    left = rows - lead
    order_u, order_d = (0, 2, 1, 3), (0, 1, 2, 3)

    @pl.when(index == 0)
    def first():
        for place, source in enumerate(order_u):

            @pl.when(info[3] == place)
            def take(source=source):
                sums[...] = lasts[source][2 * high :].astype(F32)[3 * quarter :]

    for place, source in enumerate(order_u):

        @pl.when(index == place)
        def upper(source=source):
            part = lasts[source]
            up_ref[:lead] = firsts[source][:lead].astype(F32)
            up_ref[lead:] = part[:left].astype(F32)
            at = pl.multiple_of(lax.bitwise_xor(index, info[3]) * quarter, 8)
            out_ref[pl.ds(at, 16), :] = part[left:high].astype(F32)
            spot = pl.ds(at, quarter)
            shift, gain = pair[spot, 0:1], pair[spot, 1:2]
            gain_sum, shift_sum = 0.0, 0.0
            blocks = part[2 * high :].astype(F32)
            for kind in range(3):
                block = blocks[kind * quarter : (kind + 1) * quarter]
                line = sums[kind : kind + 1]
                if kind == 0:
                    weight = wq[spot, :]
                    gq_ref[spot, :] = block + shift * line
                else:
                    lanes = slice((kind - 1) * width, kind * width)
                    weight = wkv[spot, lanes]
                    gkv_ref[spot, lanes] = block + shift * line
                gain_sum = gain_sum + jnp.sum(weight * block, axis=1, keepdims=True)
                shift_sum = shift_sum + jnp.sum(weight * line, axis=1, keepdims=True)
            lane = lax.broadcasted_iota(jnp.int32, (quarter, vec_ref.shape[1]), 1)
            vec_ref[spot, :] = jnp.where(lane == 0, gain_sum / gain, shift_sum)

    for place, source in enumerate(order_d):

        @pl.when(index == place)
        def lower(source=source):
            part = lasts[source]
            down_ref[:lead] = firsts[source][lead:].astype(F32)
            down_ref[lead:] = part[high : high + left].astype(F32)
            tail = part[high + left : 2 * high].astype(F32)
            at = pl.multiple_of(lax.bitwise_xor(index, info[4]) * quarter + 16, 8)
            out_ref[pl.ds(at, quarter - 16), :] = tail[: quarter - 16]

            @pl.when(lax.bitwise_xor(index, info[4]) == 0)
            def norms():
                norm_ref[...] = tail[quarter - 16 :]


def inward_kernel(info, *refs, groups, gots, fast):
    join_refs, hat_ref = refs[: 2 + gots], refs[2 + gots]
    parts = refs[3 + gots : 3 + gots + groups]
    outs = refs[3 + gots + groups :]
    join_kernel(*join_refs, *parts, groups=groups)
    heads, triple, rows = parts[0].shape
    hs = triple // 3
    total, sums = None, None
    ones = jnp.ones((16, rows), BF)
    for group in range(groups):
        order = [parts[group][h, k * hs : (k + 1) * hs] for k in range(3) for h in range(heads)]
        turned = jnp.concatenate(order, axis=0)
        found = nt(hat_ref[:, group * rows : (group + 1) * rows], turned)
        more = nt(ones, turned)
        total = found if total is None else total + found
        sums = more if sums is None else sums + more
    if not fast:
        outs[0][...] = total
        outs[1][...] = sums
        return
    own_ref, far_ref = outs
    block = total.shape[0] // (2 * groups)
    quarter = block // 4
    third = total.shape[1] // 3
    more = [sums[:8, kind * third : (kind + 1) * third] for kind in range(3)]
    more = jnp.concatenate(more, axis=0)
    for group in range(groups):
        spot = lax.rem(group + groups - info[0], groups)
        for part in range(4):
            place = lax.bitwise_xor(part, info[3])
            found = []
            for parity in range(2):
                at = (2 * group + parity) * block + part * quarter
                lines = jnp.concatenate([total[at : at + quarter], more], axis=1)
                found.append(lines.astype(BF))
            own_ref[place, spot] = jnp.where(info[1] == 0, found[0], found[1])
            far_ref[place, spot] = jnp.where(info[1] == 0, found[1], found[0])


def final_kernel(info, *refs, groups):
    parts = refs[:groups]
    x_ref, dres_ref, gain_ref, w_ref, out_ref = refs[groups:]
    d_normed = jnp.zeros(dres_ref.shape, F32)
    for group in range(groups):
        owner = lax.rem(info[0] + groups - group, groups)
        heads, triple, rows = parts[group].shape
        d_normed = d_normed + tn(parts[group][...].reshape(heads * triple, rows), w_ref[owner])
    values = x_ref[...].astype(F32)
    centered = values - jnp.mean(values, axis=-1, keepdims=True)
    variance = jnp.mean(centered * centered, axis=-1, keepdims=True)
    inverse = lax.rsqrt(variance + EPSILON)
    hat = centered * inverse
    gy = d_normed * gain_ref[...]
    mean_one = jnp.mean(gy, axis=-1, keepdims=True)
    mean_two = jnp.mean(gy * hat, axis=-1, keepdims=True)
    out_ref[...] = (dres_ref[...] + inverse * (gy - mean_one - hat * mean_two)).astype(BF)


def ordered(kernel, inputs, later):
    def run(*refs):
        kernel(*refs[:inputs], *refs[inputs + later :])

    return run if later else kernel


def whole(shape):
    return pl.BlockSpec(shape, lambda *at: (0,) * len(shape))


def per_device(
    tokens,
    cluster_ids,
    lengths,
    top_keys,
    gain_one,
    shift_one,
    w_query,
    w_keyval,
    w_out,
    gain_two,
    shift_two,
    w_up,
    w_down,
    cotangent,
):
    rows, width = tokens.shape
    heads = cluster_ids.shape[1]
    hs = width // heads
    hidden = w_up.shape[1]
    wide = lax.axis_size("wide")
    n_dp = lax.axis_size("dp")
    groups = math.gcd(heads, wide)
    peers = wide // groups
    own_heads = heads // groups
    own_clusters = top_keys.shape[2]
    clusters = own_clusters * wide
    picks = top_keys.shape[3]
    seq = rows * wide
    size = 512 if seq <= 2048 else 2048
    feats = own_heads * hs
    block_rows = width // wide
    fast = peers == 2 and n_dp == 4 and block_rows == 96 and hidden == 4 * width and width % 256 == 0 and rows % 128 == 0
    me = lax.axis_index("wide")
    group_at, peer_at = me // peers, me % peers
    dp_at = lax.axis_index("dp")
    seq_len = lengths[0]
    bit_x, bit_y = dp_at % 2, (dp_at // 2) % 2
    place_u, place_d = 2 * bit_x + bit_y, 2 * bit_y + bit_x
    info = jnp.stack([group_at, peer_at, seq_len, place_u, place_d, me]).astype(jnp.int32)

    def along_groups(values, hop):
        pairs = [(i, ((i // peers + hop) % groups) * peers + i % peers) for i in range(wide)]
        return lax.ppermute(values, "wide", pairs)

    def along_peers(values, hop):
        pairs = [(i, (i // peers) * peers + (i % peers + hop) % peers) for i in range(wide)]
        return lax.ppermute(values, "wide", pairs)

    def along_dp(values, mask):
        return lax.ppermute(values, "dp", [(i, i ^ mask) for i in range(n_dp)])

    def prefetched(
        kernel, grid, in_specs, out_specs, out_shape, mib, spent, name, scratch=(), alias=None, first=()
    ):
        first = jax.tree.leaves(first)
        call = pl.pallas_call(
            ordered(kernel, 1 + len(in_specs), len(first)),
            grid_spec=pltpu.PrefetchScalarGridSpec(
                num_scalar_prefetch=1,
                grid=grid,
                in_specs=in_specs + [pl.BlockSpec(memory_space=pl.ANY)] * len(first),
                out_specs=out_specs,
                scratch_shapes=list(scratch),
            ),
            out_shape=out_shape,
            compiler_params=params(mib, len(grid)),
            cost_estimate=spent,
            input_output_aliases=alias or {},
            name=name,
        )
        return lambda *inputs: call(*inputs, *first)

    def after(values, *others):
        return lax.optimization_barrier((values, others))[0]

    def scalar(spec):
        return pl.BlockSpec(spec.block_shape, lambda *at: spec.index_map(*at[:-1]))

    def array(shape, dtype):
        return jax.ShapeDtypeStruct(shape, dtype)

    position = me * rows + jnp.arange(rows, dtype=jnp.int32)
    marked = jnp.where((position < seq_len)[:, None], cluster_ids, -1).T
    tops = jnp.zeros((heads, picks, clusters), jnp.int32)
    tops = lax.dynamic_update_slice(
        tops, top_keys[0].transpose(0, 2, 1), (0, 0, me * own_clusters)
    )
    lines = rows // clusters
    packed = jnp.concatenate([tops, marked.reshape(heads, lines, clusters)], axis=1)
    near = [along_peers(tokens, -hop) for hop in range(1, peers)]
    packed = after(packed.reshape(groups, own_heads, picks + lines, clusters), near)

    def of_heads(hop):
        return lax.dynamic_index_in_dim(packed, (group_at + groups - hop) % groups, keepdims=False)

    arrived = [of_heads(0)] + [along_groups(of_heads(hop), -hop) for hop in range(1, groups)]

    mine = {0: tokens, 1: along_groups(tokens, -1)}
    if groups > 2:
        mine[groups - 1] = along_groups(tokens, 1)
    ready = after(tokens, arrived)
    for hop in range(2, groups - 1):
        mine[hop] = along_groups(ready, -hop)

    w_in = jnp.concatenate([w_query, w_keyval], axis=1).T.reshape(3, heads, hs, width)
    w_in = w_in.transpose(1, 0, 2, 3).reshape(groups, 3 * feats, width)
    table_shape = (own_heads, picks + groups * lines, clusters)
    table = prefetched(
        functools.partial(table_kernel, picks=picks),
        (1,),
        [whole((own_heads, picks + lines, clusters))] * groups,
        whole(table_shape),
        array(table_shape, jnp.int32),
        8,
        cost(1e5, 1e6),
        "table",
    )(info, *arrived)
    tables = [table] + [along_peers(table, -hop) for hop in range(1, peers)]
    cot_got = [along_peers(after(cotangent, arrived), hop) for hop in range(1, peers)]
    cot_got = cot_got if fast else []
    bias, ids_all = prefetched(
        functools.partial(bias_kernel, groups=groups, peers=peers, rows=rows, picks=picks),
        (wide,),
        [whole(table_shape)] * peers,
        [
            pl.BlockSpec((own_heads, rows, clusters), lambda i, s: (0, i, 0)),
            whole((own_heads, 1, seq)),
        ],
        [array((own_heads, seq, clusters), BF), array((own_heads, 1, seq), jnp.int32)],
        12 if fast else 60,
        cost(own_heads * seq * clusters * picks * 8, own_heads * seq * clusters * 2),
        "bias",
    )(info, *tables)

    gain_row, shift_row = gain_one[None, :], shift_one[None, :]
    shapes = [
        array((width, groups * rows), BF),
        array((own_heads, 3 * hs, seq), BF),
        array((own_heads, seq, 2 * hs), BF),
    ]
    held = []
    split_peers = peers if peers <= 2 else 1
    for group in sorted(range(groups), key=lambda g: min(g, groups - g)):
        arrival = mine[group]
        first = ()
        if group == 1:
            arrival = after(arrival, bias, held, cot_got, [mine[hop] for hop in range(2, groups)])
        chunk = [arrival]
        chunk += near if group == 0 else [along_peers(arrival, -hop) for hop in range(1, peers)]
        if peers > 2:
            chunk = [jnp.concatenate(chunk, axis=0)]
        span = peers * rows
        if peers > 2:
            specs_in = [pl.BlockSpec((rows, width), lambda p, s: (p, 0))]
            grid = (peers,)
            outs = [
                pl.BlockSpec((width, rows), lambda p, s, g=group: (0, g)),
                pl.BlockSpec((own_heads, 3 * hs, rows), lambda p, s, g=group: (0, 0, g * peers + p)),
                pl.BlockSpec((own_heads, rows, 2 * hs), lambda p, s, g=group: (0, g * peers + p, 0)),
            ]
        else:
            specs_in = [whole((rows, width))] * split_peers
            grid = (1,)
            outs = [
                pl.BlockSpec((width, rows), lambda p, s, g=group: (0, g)),
                pl.BlockSpec((own_heads, 3 * hs, span), lambda p, s, g=group: (0, 0, g)),
                pl.BlockSpec((own_heads, span, 2 * hs), lambda p, s, g=group: (0, g, 0)),
            ]
        old = 1 + split_peers + 3
        held = prefetched(
            functools.partial(project_kernel, peers=split_peers, olds=len(held)),
            grid,
            specs_in
            + [
                whole((1, width)),
                whole((1, width)),
                pl.BlockSpec((1, 3 * feats, width), lambda p, s: (s[0], 0, 0)),
            ]
            + [pl.BlockSpec(memory_space=pl.ANY)] * len(held),
            outs,
            shapes,
            16 if fast else 60,
            cost(6 * span * width * feats, span * width * 4),
            "project",
            alias={old + k: k for k in range(len(held))},
            first=first,
        )(info, *chunk, gain_row, shift_row, w_in, *held)
    hat_own, feat, kv = held

    ids_full = pl.BlockSpec((1, 1, seq), lambda h, r: (h, 0, 0))
    feat_full = pl.BlockSpec((1, 3 * hs, seq), lambda h, r: (h, 0, 0))
    kv_full = pl.BlockSpec((1, seq, 2 * hs), lambda h, r: (h, 0, 0))
    bias_full = pl.BlockSpec((1, seq, clusters), lambda h, r: (h, 0, 0))
    head_rows = pl.BlockSpec((hs, rows), lambda h, r: (h, 0))
    mix_spec = pl.BlockSpec((1, 1, hs + 8, rows), lambda h, r: (h, r, 0, 0))
    stat_spec = pl.BlockSpec((1, hs + 8, clusters), lambda h, r: (h, 0, 0))
    cen_spec = pl.BlockSpec((1, hs, clusters), lambda h, r: (h, 0, 0))
    own_rows = groups * rows
    pair_flops = own_heads * own_rows * seq * 256

    one = [
        pl.BlockSpec(spec.block_shape, functools.partial(lambda h, f: f(h, 0), f=spec.index_map))
        for spec in (ids_full, feat_full, kv_full, bias_full, stat_spec, cen_spec, head_rows)
    ]
    ids_one, feat_one, kv_one, bias_one, stat_one, cen_one, rows_one = one
    part_one = pl.BlockSpec((1, hs + 16, clusters), lambda h: (h, 0, 0))
    mix_one = pl.BlockSpec((1, groups, hs + 8, rows), lambda h: (h, 0, 0, 0))
    all_groups = pl.BlockSpec((groups, hs, rows), lambda h: (0, h, 0))
    own_one = pl.BlockSpec((1, own_rows, 2 * hs), lambda h: (h, 0, 0))
    results = pl.pallas_call(
        functools.partial(forward_kernel, size=size, groups=groups, rows=rows),
        grid=(own_heads,),
        in_specs=[ids_one, feat_one, kv_one, bias_one],
        out_specs=[rows_one] * groups + [mix_one, stat_one, cen_one],
        out_shape=[array((feats, rows), BF)] * groups
        + [
            array((own_heads, groups, hs + 8, rows), F32),
            array((own_heads, hs + 8, clusters), F32),
            array((own_heads, hs, clusters), BF),
        ],
        compiler_params=params(16 if fast else 60, 1),
        cost_estimate=cost(6 * pair_flops, 8e6, own_heads * own_rows * seq),
        name="attend",
    )(ids_all, feat, kv, bias)
    attn_t = results[:groups]
    mixed, stats, centroid = results[groups:]

    arrived = [attn_t[0]] + [along_groups(attn_t[hop], hop) for hop in range(1, groups)]

    chunks = 4
    part = hidden // chunks
    early, lead = 64, 80
    w_out_g = w_out.reshape(groups, feats, width)
    gain_row2, shift_row2 = gain_two[None, :], shift_two[None, :]
    square = whole((rows, width))
    column = pl.BlockSpec((rows, part), lambda i, s: (0, i))
    norm_spec = whole((8, width))
    if fast:
        kept_shapes = [
            array((rows, hidden + hidden // 2 + width), BF),
            array((width + 16, rows), BF),
            array((rows, hidden // 2), BF),
            array((width + 16, rows), BF),
        ]
        kept_specs = [whole(item.shape) for item in kept_shapes]
        kept_specs[2] = pl.BlockSpec((rows, part // 2), lambda i, s: (0, i))
    else:
        kept_shapes = [
            array((8, width), F32),
            array((rows, hidden), BF),
            array((rows, width), BF),
            array((rows, hidden), BF),
            array((rows, width), BF),
        ]
        kept_specs = [norm_spec, column, square, column, square]
    results = prefetched(
        functools.partial(block_kernel, groups=groups, chunks=chunks, fast=fast),
        (chunks,),
        [whole((feats, rows))] * groups
        + [
            square,
            whole((1, width)),
            whole((1, width)),
            whole((groups, feats, width)),
            pl.BlockSpec((width, part), lambda i, s: (0, i)),
            pl.BlockSpec((part, width), lambda i, s: (i, 0)),
            square,
        ],
        [square, square] + kept_specs + [whole((feats, rows))] * groups,
        [array((rows, width), BF), array((rows, width), F32)]
        + kept_shapes
        + [array((feats, rows), BF)] * groups,
        28 if fast else 60,
        cost(8 * rows * width * hidden, 4 * width * hidden, rows * hidden),
        "feed",
        scratch=[
            pltpu.VMEM((rows, width), F32),
            pltpu.VMEM((rows, 128), F32),
            pltpu.VMEM((rows, width), BF),
            pltpu.VMEM((rows, width), F32),
            pltpu.VMEM((rows, width), F32),
        ],
    )(info, *arrived, tokens, gain_row2, shift_row2, w_out_g, w_up, w_down, cotangent)
    output, d_resid = results[:2]
    kept, d_attn = results[2:-groups], results[-groups:]
    grads = [d_attn[0]] + [along_groups(d_attn[hop], -hop) for hop in range(1, groups)]

    def weight_parts():
        far, low_far, act_own, low_own = kept
        got, low_got = along_peers(far, 1), along_peers(low_far, 1)
        high = block_rows + 16
        chunk = pl.BlockSpec((rows, part), lambda i, s: (0, i ^ 2 ^ s[3]))
        branch = pl.BlockSpec((rows, width), lambda i, s: (0, hidden * 3 // 2 // width))
        act_spec = pl.BlockSpec((rows, part // 2), lambda i, s: (0, i))
        act_there = pl.BlockSpec((rows, part // 2), lambda i, s: (0, 2 * hidden // part + i))
        low_spec = whole((width + 16, rows))
        shape_u = (2, groups, high, width)
        shape_d = (2, groups, high, width)
        parts = [(1, groups, tall, width) for tall in (early + high, high - early)]
        results = prefetched(
            functools.partial(weights_kernel, groups=groups),
            (4,),
            [chunk, chunk, branch, branch, act_spec, act_there, low_spec, low_spec, square, square],
            [whole(item) for item in parts]
            + [pl.BlockSpec((1,) + shape_u[1:], lambda i, s: (jnp.maximum(i - 2, 0), 0, 0, 0))]
            + [whole(item) for item in parts]
            + [whole(shape_d)],
            ([array(item, BF) for item in parts] + [array(shape_u, BF)]) * 2,
            28,
            cost(8 * rows * width * hidden, 6 * width * hidden),
            "weights",
            scratch=[pltpu.VMEM((groups, block_rows, width), F32)],
        )(info, far, got, far, got, act_own, got, low_own, low_got, cotangent, *cot_got)
        return results[:2], results[2], results[3:5], results[5]

    def weight_second(keep_u, got_u, keep_d, got_d, inner, inner_got, late_u, late_d):
        def block(shape, at):
            return pl.BlockSpec((1,) + shape[1:], lambda i: (at, 0, 0, 0))

        high, lines = keep_u.shape[2], inner.shape[2]
        shapes = [(groups, high + lines + late_u.shape[2], width)] * 2 + [(groups, lines, width)]
        return pl.pallas_call(
            second_kernel,
            grid=(1,),
            in_specs=[
                block(item.shape, item.shape[0] - 1) for item in (keep_u, got_u, keep_d, got_d)
            ]
            + [whole(item.shape) for item in (inner, inner_got, late_u, late_d)],
            out_specs=[whole(shape) for shape in shapes],
            out_shape=[array(shape, BF) for shape in shapes],
            compiler_params=params(24, 1),
            cost_estimate=cost(groups * high * width * 2, groups * high * width * 12),
            name="second",
        )(keep_u, got_u, keep_d, got_d, inner, inner_got, late_u, late_d)

    def weight_third(keep_u, got_u, keep_d, got_d, by_y, by_x, inner, inner_got, by_xy):
        def block(shape, at):
            return pl.BlockSpec((1,) + shape[1:], lambda i, s: (at, 0, 0, 0))

        left = keep_u.shape[2] - lead
        talls = [(2 * lead, width)] * groups + [(2 * left + inner.shape[2], width)] * groups
        more = (by_y, by_x)
        return prefetched(
            third_kernel,
            (1,),
            [block(item.shape, 0) for item in (keep_u, got_u, keep_d, got_d)]
            + [whole(by_y.shape), whole(by_x.shape)]
            + [block(inner.shape, 0)] * 2
            + [whole(by_xy.shape)],
            [whole(tall) for tall in talls],
            [array(tall, BF) for tall in talls],
            24,
            cost(groups * 256 * width * 4, groups * 256 * width * 8),
            "third",
            first=home,
        )(info, keep_u, got_u, keep_d, got_d, by_y, by_x, inner, inner_got, by_xy)

    def weight_fourth(came, high, lines, first):
        tall = 2 * high + (3 * lines + 8 if lines else 0)
        done = prefetched(
            functools.partial(fourth_kernel, groups=groups, high=high, feats=3 * feats),
            (1,),
            [whole(came[0].shape)] * groups,
            whole((tall, width)),
            array((tall, width), BF),
            16,
            cost(groups * tall * width, groups * tall * width * 2),
            "fourth",
            scratch=[pltpu.VMEM((groups, lines, width), F32)] if lines else [],
            first=first,
        )(info, *came)
        return [done] + [along_dp(done, mask) for mask in (1, 2, 3)]

    def weight_spread(firsts, lasts, high, ready):
        at = me * block_rows
        wq_rows = lax.dynamic_slice_in_dim(w_query, at, block_rows).astype(F32)
        wkv_rows = lax.dynamic_slice_in_dim(w_keyval, at, block_rows).astype(F32)
        pair = jnp.stack([shift_one, gain_one] + [shift_one] * 6, axis=1)
        pair = lax.dynamic_slice_in_dim(pair, at, block_rows)
        return prefetched(
            functools.partial(spread_kernel, lead=lead, high=high),
            (4,),
            [whole(item.shape) for item in firsts + lasts]
            + [whole(wq_rows.shape), whole(wkv_rows.shape), whole(pair.shape)],
            [
                pl.BlockSpec((block_rows, part), lambda i, s: (0, i ^ s[3])),
                whole((block_rows, width)),
                pl.BlockSpec((block_rows, width), lambda i, s: (i ^ s[4], 0)),
                whole((8, width)),
                whole((block_rows, width)),
                whole((block_rows, 2 * width)),
                whole((block_rows, 128)),
            ],
            [
                array((block_rows, hidden), F32),
                array((block_rows, width), F32),
                array((hidden // wide, width), F32),
                array((8, width), F32),
                array((block_rows, width), F32),
                array((block_rows, 2 * width), F32),
                array((block_rows, 128), F32),
            ],
            20,
            cost(1e6, 8 * block_rows * width * 6),
            "spread",
            scratch=[pltpu.VMEM((8, width), F32)],
        )(info, *firsts, *lasts, wq_rows, wkv_rows, pair)

    masks = [1 << k for k in range(n_dp.bit_length() - 1)]

    def reduce_rows(partial):
        blocks = partial.reshape(groups, peers, partial.shape[0] // wide, partial.shape[1])

        def of_peer(hop):
            at = (peer_at + hop) % peers
            return lax.dynamic_index_in_dim(blocks, at, axis=1, keepdims=False)

        total = of_peer(0).astype(F32)
        for hop in range(1, peers):
            total = total + along_peers(of_peer(hop), hop).astype(F32)
        total = total.astype(BF)

        def of_group(hop):
            return lax.dynamic_index_in_dim(total, (group_at + hop) % groups, keepdims=False)

        done = of_group(0).astype(F32)
        for hop in range(1, groups):
            done = done + along_groups(of_group(hop), hop).astype(F32)
        for mask in masks:
            done = done.astype(BF)
            done = done.astype(F32) + along_dp(done, mask).astype(F32)
        return done

    if fast:
        send_u, keep_u, send_d, keep_d = weight_parts()
        got_u, got_d = along_dp(send_u[0], 1), along_dp(send_d[0], 2)
    else:
        norm_two, d_up, d_branch, act, normed_two = kept
        total_up = reduce_rows(tn(normed_two, d_up).astype(BF))
        total_down = reduce_rows(tn(act, cotangent).astype(BF))
        found = jnp.stack([nn(item, d_branch).astype(BF) for item in arrived])
        found = [
            lax.dynamic_index_in_dim(found, (group_at + groups - g) % groups, keepdims=False)
            for g in range(groups)
        ]
        total_out = reduce_rows(jnp.concatenate(found, axis=0))
        norm_own = reduce_rows(norm_two[:2].T.astype(BF)).T

    share = prefetched(
        functools.partial(sums_kernel, groups=groups),
        (own_heads,),
        [scalar(spec) for spec in (ids_one, *[rows_one] * groups, mix_one)],
        scalar(part_one),
        array((own_heads, hs + 16, clusters), F32),
        16 if fast else 60,
        cost(own_heads * own_rows * clusters * 160, 2e6),
        "sums",
        first=(keep_u, keep_d) if fast else (),
    )(info, ids_all, *grads, mixed)
    share_got = [along_peers(share, hop) for hop in range(1, peers)]

    back_shapes = [
        array((groups, feats, rows), BF),
        array((own_heads, 2 * hs, own_rows), F32),
        array((own_heads, 2 * hs, max(peers - 1, 1) * own_rows), BF),
    ]
    dq, dkv_own, dkv_send = pl.pallas_call(
        functools.partial(back_kernel, size=size, groups=groups, gots=len(share_got)),
        grid=(own_heads,),
        in_specs=[ids_one, feat_one, kv_one, bias_one]
        + [rows_one] * groups
        + [mix_one, stat_one, cen_one]
        + [part_one] * (1 + len(share_got)),
        out_specs=[
            all_groups,
            pl.BlockSpec((1,) + back_shapes[1].shape[1:], lambda h: (h, 0, 0)),
            pl.BlockSpec((1,) + back_shapes[2].shape[1:], lambda h: (h, 0, 0)),
        ],
        out_shape=back_shapes,
        scratch_shapes=[pltpu.VMEM((seq, 2 * hs), F32), pltpu.VMEM((seq, 2 * clusters), BF)],
        compiler_params=params(24 if fast else 62, 1),
        cost_estimate=cost(14 * pair_flops, 10e6, own_heads * own_rows * seq),
        name="back",
    )(ids_all, feat, kv, bias, *grads, mixed, stats, centroid, share, *share_got)
    if fast:
        dkv_send = after(dkv_send, got_u, got_d)
    dkv_got = [
        along_peers(
            dkv_send if peers == 2 else dkv_send[..., (hop - 1) * own_rows : hop * own_rows], hop
        )
        for hop in range(1, peers)
    ]
    tall = block_rows + 16
    spent = cost(2 * own_rows * width * 3 * feats, 4e6)
    if fast:
        lines = block_rows // 4
        more = [array((4, groups, lines, width), BF)] * 2
    else:
        more = [array((width, 3 * feats), F32), array((16, 3 * feats), F32)]
    results = prefetched(
        functools.partial(inward_kernel, groups=groups, gots=len(dkv_got), fast=fast),
        (1,),
        [whole(back_shapes[0].shape)]
        + [whole(back_shapes[1].shape)] * (1 + len(dkv_got))
        + [whole((width, own_rows))],
        [whole((own_heads, 3 * hs, rows))] * groups + [whole(item.shape) for item in more],
        [array((own_heads, 3 * hs, rows), BF)] * groups + more,
        28 if fast else 60,
        spent,
        "inward",
    )(info, dq, dkv_own, *dkv_got, hat_own)
    d_in, more = results[:groups], results[groups:]
    home = [d_in[0]] + [along_groups(d_in[hop], hop) for hop in range(1, groups)]

    grad_tokens = prefetched(
        functools.partial(final_kernel, groups=groups),
        (1,),
        [whole((own_heads, 3 * hs, rows))] * groups
        + [square, square, whole((1, width)), whole((groups, 3 * feats, width))],
        square,
        array((rows, width), BF),
        24 if fast else 60,
        cost(6 * rows * width * width, 6 * width * width),
        "final",
    )(info, *home, tokens, d_resid, gain_row, w_in)

    if fast:
        keep, far = more
        inner_got = along_peers(far, 1)
        to_y, to_x, to_xy = weight_second(
            keep_u, got_u, keep_d, got_d, keep, inner_got, send_u[1], send_d[1]
        )
        by_y, by_x, by_xy = along_dp(to_y, 2), along_dp(to_x, 1), along_dp(to_xy, 3)
        sums = weight_third(
            keep_u, got_u, keep_d, got_d, by_y, by_x, keep, inner_got, by_xy
        )
        came_a, came_b = [sums[0]], [sums[groups]]
        came_a += [along_groups(sums[hop], hop) for hop in range(1, groups)]
        late = after(sums[groups + 1 :], came_a[1])
        came_b += [along_groups(late[hop - 1], hop) for hop in range(1, groups)]
        spread_a = weight_fourth(came_a, lead, 0, (came_b[1], grad_tokens))
        high = keep_u.shape[2] - lead
        spread_b = weight_fourth(came_b, high, lines, spread_a)
        found = weight_spread(spread_a, spread_b, high, came_a[0])
        total_up, total_out, total_down, norms, total_query, total_keyval, vector = found
        norm_own = lax.dynamic_slice_in_dim(norms, me * block_rows, block_rows, axis=1)
        gain_grad, shift_grad = vector[:, 0], vector[:, 1]
    else:
        found, more = more
        found = found.reshape(groups, peers, block_rows, 3 * feats)
        more = jnp.broadcast_to(more, (groups, peers, 16, 3 * feats))
        found = jnp.concatenate([found, more], axis=2).astype(BF)

        def of_peer(hop):
            at = (peer_at + hop) % peers
            return lax.dynamic_index_in_dim(found, at, axis=1, keepdims=False)

        total = of_peer(0).astype(F32)
        for hop in range(1, peers):
            total = total + along_peers(of_peer(hop), hop).astype(F32)
        for mask in masks:
            total = total.astype(BF)
            total = total.astype(F32) + along_dp(total, mask).astype(F32)
        total = total.astype(BF)
        items = [
            lax.dynamic_index_in_dim(total, (group_at + hop) % groups, keepdims=False)
            for hop in range(groups)
        ]
        pieces = [items[0]] + [along_groups(items[hop], hop) for hop in range(1, groups)]
        pieces = jnp.stack(pieces)
        pieces = jnp.stack(
            [
                lax.dynamic_index_in_dim(pieces, (group_at + groups - g) % groups, keepdims=False)
                for g in range(groups)
            ]
        ).astype(F32)
        q_part = pieces[:, :, :feats].transpose(1, 0, 2).reshape(tall, width)
        kv_part = (
            pieces[:, :, feats:]
            .reshape(groups, tall, 2, feats)
            .transpose(1, 2, 0, 3)
            .reshape(tall, 2 * width)
        )
        at = me * block_rows
        wq_rows = lax.dynamic_slice_in_dim(w_query, at, block_rows).astype(F32)
        wkv_rows = lax.dynamic_slice_in_dim(w_keyval, at, block_rows).astype(F32)
        gain_own = lax.dynamic_slice_in_dim(gain_one, at, block_rows)
        shift_own = lax.dynamic_slice_in_dim(shift_one, at, block_rows)
        q_sum, kv_sum = q_part[block_rows], kv_part[block_rows]
        q_part, kv_part = q_part[:block_rows], kv_part[:block_rows]
        shift_grad = jnp.sum(wq_rows * q_sum, axis=1) + jnp.sum(wkv_rows * kv_sum, axis=1)
        along = jnp.sum(wq_rows * q_part, axis=1) + jnp.sum(wkv_rows * kv_part, axis=1)
        total_query = q_part + shift_own[:, None] * q_sum
        total_keyval = kv_part + shift_own[:, None] * kv_sum
        gain_grad = along / gain_own


    return (
        output,
        grad_tokens,
        total_query,
        total_keyval,
        total_out,
        total_up,
        total_down,
        gain_grad,
        shift_grad,
        norm_own[0],
        norm_own[1],
    )


def solution(mesh):
    return jax.shard_map(
        per_device,
        mesh=mesh,
        in_specs=(
            P(("dp", "wide"), None),
            P(("dp", "wide"), None),
            P("dp"),
            P("dp", None, "wide", None),
            P(),
            P(),
            P(),
            P(),
            P(),
            P(),
            P(),
            P(),
            P(),
            P(("dp", "wide"), None),
        ),
        out_specs=(
            P(("dp", "wide"), None),
            P(("dp", "wide"), None),
            P("wide", None),
            P("wide", None),
            P("wide", None),
            P("wide", None),
            P("wide", None),
            P("wide"),
            P("wide"),
            P("wide"),
            P("wide"),
        ),
        check_vma=False,
    )
```

```python
import functools
import math

import jax
import jax.numpy as jnp
import numpy as np
from jax import lax
from jax.experimental import pallas as pl
from jax.experimental.pallas import tpu as pltpu
from jax.sharding import PartitionSpec as P

EPSILON = 1e-05
NEGATIVE = -1e30
EXCLUDED = -3e30
GELU_A = math.sqrt(2.0 / math.pi)
GELU_B = 0.044715
BF = jnp.bfloat16
F32 = jnp.float32


def nn(left, right):
    return lax.dot_general(left, right, (((1,), (0,)), ((), ())), preferred_element_type=F32)


def nt(left, right):
    return lax.dot_general(left, right, (((1,), (1,)), ((), ())), preferred_element_type=F32)


def tn(left, right):
    return lax.dot_general(left, right, (((0,), (0,)), ((), ())), preferred_element_type=F32)


def params(mib, dims):
    return pltpu.CompilerParams(
        vmem_limit_bytes=mib * 1024 * 1024, dimension_semantics=("arbitrary",) * dims
    )


def cost(flops, nbytes, trans=0):
    return pl.CostEstimate(flops=int(flops), bytes_accessed=int(nbytes), transcendentals=int(trans))


def split_low(values):
    high = values.astype(BF)
    return high, (values - high.astype(F32)).astype(BF)


def one_hot_t(ids_row, clusters):
    rows = lax.broadcasted_iota(jnp.int32, (clusters, ids_row.shape[1]), 0)
    return jnp.where(rows == ids_row, 1.0, 0.0).astype(BF)


def key_passes(total, size, score, weigh, blocks=None):
    count = total // size
    if count <= 4:
        if blocks is None:
            blocks = [score(index) for index in range(count)]
        peak = functools.reduce(jnp.maximum, [jnp.max(b, axis=0, keepdims=True) for b in blocks])
        denom, sums = 0.0, None
        for index in range(count):
            expo = jnp.exp(blocks[index] - peak)
            denom = denom + jnp.sum(expo, axis=0, keepdims=True)
            parts = weigh(index, expo)
            sums = parts if sums is None else tuple(x + y for x, y in zip(sums, parts))
        return peak, denom, sums

    def step(index, carry):
        peak, denom, sums = carry
        block = score(index)
        fresh = jnp.maximum(peak, jnp.max(block, axis=0, keepdims=True))
        expo = jnp.exp(block - fresh)
        fade = jnp.exp(peak - fresh)
        parts = weigh(index, expo)
        return (
            fresh,
            denom * fade + jnp.sum(expo, axis=0, keepdims=True),
            tuple(old * fade + new for old, new in zip(sums, parts)),
        )

    shapes = jax.eval_shape(lambda: (score(0), weigh(0, score(0))))
    lanes = shapes[0].shape[1]
    start = (
        jnp.full((1, lanes), NEGATIVE, F32),
        jnp.zeros((1, lanes), F32),
        tuple(jnp.zeros(item.shape, F32) for item in shapes[1]),
    )
    return lax.fori_loop(0, count, step, start)


def key_sum(total, size, step, start):
    count = total // size
    if count <= 4:
        for index in range(count):
            start = step(index, start)
        return start
    return lax.fori_loop(0, count, step, start)


def spot_of(index, size):
    if isinstance(index, int):
        return pl.ds(index * size, size)
    return pl.ds(pl.multiple_of(index * size, size), size)


def piece(ref, index, size, axis):
    spot = spot_of(index, size)
    return ref[spot, :] if axis == 0 else ref[:, spot]


def table_kernel(info, *refs, picks):
    parts, out = refs[:-1], refs[-1]
    total = parts[0][:, :picks]
    for part in parts[1:]:
        total = total + part[:, :picks]
    out[:, :picks] = total
    rows = parts[0].shape[1] - picks
    for group, part in enumerate(parts):
        out[:, picks + group * rows : picks + (group + 1) * rows] = part[:, picks:]


def bias_kernel(info, *refs, groups, peers, rows, picks):
    tables, (bias_ref, ids_ref) = refs[:peers], refs[peers:]
    part = pl.program_id(0)
    owner = (
        lax.rem(info[0] + part // peers, groups) * peers + lax.rem(info[1] + part % peers, peers)
    )
    heads, _, clusters = tables[0].shape
    place = owner * rows + lax.broadcasted_iota(jnp.int32, (rows, clusters), 0)
    plain = jnp.where(place >= info[2], EXCLUDED, NEGATIVE)
    for head in range(heads):
        top = tables[0][head, :picks]
        for table in tables[1:]:
            top = top + table[head, :picks]
        value = plain
        for pick in range(picks):
            value = jnp.where(place == top[pick : pick + 1, :], 0.0, value)
        bias_ref[head] = value.astype(BF)

    @pl.when(part == 0)
    def ids():
        lines = rows // clusters
        for head in range(heads):
            row = []
            for group in range(groups):
                for table in tables:
                    for line in range(lines):
                        at = picks + group * lines + line
                        row.append(table[head, at : at + 1, :])
            ids_ref[head] = jnp.concatenate(row, axis=1)


def project_kernel(info, *refs, peers, olds):
    parts = refs[:peers]
    gain_ref, shift_ref, w_ref = refs[peers : peers + 3]
    hat_ref, feat_ref, kv_ref = refs[peers + 3 + olds :]
    rows = hat_ref.shape[1]
    for peer in range(peers):
        values = parts[peer][...].astype(F32)
        centered = values - jnp.mean(values, axis=-1, keepdims=True)
        variance = jnp.mean(centered * centered, axis=-1, keepdims=True)
        scaled = centered * lax.rsqrt(variance + EPSILON) * gain_ref[...]
        if peer == 0:
            hat_ref[...] = scaled.astype(BF).T
        low = (scaled + shift_ref[...]).astype(BF)
        found = nt(w_ref[0], low)
        heads, triple = feat_ref.shape[0], feat_ref.shape[1]
        hs = triple // 3
        spot = slice(peer * rows, (peer + 1) * rows)
        for head in range(heads):
            base = head * triple
            query = (found[base : base + hs] * 0.125).astype(BF)
            pair = found[base + hs : base + triple].astype(BF)
            feat_ref[head, :hs, spot] = query
            feat_ref[head, hs:, spot] = pair
            kv_ref[head, spot, :] = pair.T


def forward_kernel(ids_all, feat, kv, bias, *refs, size, groups, rows):
    outs = refs[:groups]
    mix_ref, stat_ref, cen_ref = refs[groups:]
    hs = feat.shape[1] // 3
    keys = kv.shape[1]
    count = keys // size
    clusters = bias.shape[2]
    kv_h, bias_h = kv.at[0], bias.at[0]
    queries_all, kvt = feat.at[0, :hs], feat.at[0, hs:]
    hot_all = one_hot_t(ids_all[0], clusters)
    ones = jnp.ones((16, keys), BF)
    sums = nt(jnp.concatenate([queries_all[...], ones], axis=0), hot_all)
    counts = sums[hs : hs + 1]
    centroid = (sums[:hs] / jnp.maximum(counts, 1.0)).astype(BF)
    padded = jnp.concatenate([centroid, jnp.zeros_like(centroid)], axis=0)

    def cluster_score(index):
        scores = nn(piece(kv_h, index, size, 0), padded)
        outside = piece(bias_h, index, size, 0).astype(F32) < 2.0 * NEGATIVE
        return jnp.where(outside, NEGATIVE, scores)

    def cluster_weigh(index, expo):
        top = piece(bias_h, index, size, 0).astype(F32) == 0.0
        mass = jnp.sum(jnp.where(top, expo, 0.0), axis=0, keepdims=True)
        other = jnp.where(top, 0.0, expo).astype(BF)
        return nn(piece(kvt, index, size, 1), other), mass

    peers = keys // (groups * rows)
    hots, sides = [], []
    for group in range(groups):
        spot = slice(group * peers * rows, group * peers * rows + rows)
        hot = one_hot_t(ids_all[0, :, spot], clusters)
        queries = queries_all[:, spot]
        hots.append(hot)
        sides.append(jnp.concatenate([queries, jnp.zeros_like(queries), hot], axis=0))

    def member_score(group, index):
        both = jnp.concatenate([piece(kv_h, index, size, 0), piece(bias_h, index, size, 0)], axis=1)
        return nn(both, sides[group])

    def member_weigh(index, expo):
        return (nn(piece(kvt, index, size, 1), expo.astype(BF)),)

    short = count <= 4
    ahead = None
    if short:
        ahead = [member_score(0, index) for index in range(count)]
    peak, denom, (rest, mass) = key_passes(keys, size, cluster_score, cluster_weigh)
    rest = rest[hs:] / denom
    mass = mass / denom
    blank = jnp.zeros((5, clusters), F32)
    stats = jnp.concatenate([rest, mass, peak + jnp.log(denom), counts, blank], axis=0)
    stat_ref[0] = stats
    cen_ref[0] = centroid
    high, low = split_low(stats)
    table = jnp.concatenate([high, low], axis=1)
    for group in range(groups):
        gathered = nn(table, jnp.concatenate([hots[group], hots[group]], axis=0))
        blocks, ahead = ahead, None
        if short and group + 1 < groups:
            ahead = [member_score(group + 1, index) for index in range(count)]
        score = functools.partial(member_score, group)
        peak, denom, (mix,) = key_passes(keys, size, score, member_weigh, blocks)
        mix = mix[hs:] / denom
        outs[group][...] = (gathered[hs : hs + 1] * mix + gathered[:hs]).astype(BF)
        level = jnp.broadcast_to(peak + jnp.log(denom), (8, rows))
        mix_ref[0, group] = jnp.concatenate([mix, level], axis=0)


def sums_kernel(info, ids_own, *refs, groups):
    grads, (mix_ref, part_ref) = refs[:groups], refs[groups:]
    hs = grads[0].shape[0]
    total = None
    for group in range(groups):
        rows = grads[group].shape[1]
        step = ids_own.shape[2] // groups
        hot = one_hot_t(ids_own[0, :, group * step : group * step + rows], part_ref.shape[2])
        grad = grads[group][...]
        along = jnp.sum(grad.astype(F32) * mix_ref[0, group, :hs], axis=0, keepdims=True)
        high, low = split_low(along)
        pad = jnp.zeros((14, rows), BF)
        part = nt(jnp.concatenate([grad, high, low, pad], axis=0), hot)
        total = part if total is None else total + part
    part_ref[0] = total


def back_kernel(ids_all, feat, kv, bias, *refs, size, groups, gots):
    grads = refs[:groups]
    mix_ref, stat_ref, cen_ref = refs[groups : groups + 3]
    shares = refs[groups + 3 : groups + 4 + gots]
    dq_ref, own_ref, send_ref, total, both = refs[groups + 4 + gots :]
    hs, rows = grads[0].shape
    keys = kv.shape[1]
    count = keys // size
    peers = keys // (groups * rows)
    clusters = bias.shape[2]
    kv_h, bias_h = kv.at[0], bias.at[0]
    queries_all, kvt = feat.at[0, :hs], feat.at[0, hs:]
    stats = stat_ref[0]
    high, low = split_low(stats[hs : hs + 8])
    table = jnp.concatenate([high, low], axis=1)
    hots, sides, levels, deltas, pads, rights = [], [], [], [], [], []
    for group in range(groups):
        spot = slice(group * peers * rows, group * peers * rows + rows)
        hot = one_hot_t(ids_all[0, :, spot], clusters)
        queries = queries_all[:, spot]
        blank = jnp.zeros_like(queries)
        hots.append(jnp.concatenate([hot, hot], axis=0))
        sides.append(jnp.concatenate([queries, blank, hot], axis=0))
        mass = nn(table, hots[group])[0:1]
        back = (mass * grads[group][...].astype(F32)).astype(BF)
        levels.append(mix_ref[0, group, hs : hs + 1])
        deltas.append(jnp.sum(back.astype(F32) * mix_ref[0, group, :hs], axis=0, keepdims=True))
        pads.append(jnp.concatenate([blank, back], axis=0))
        turned = jnp.concatenate([queries, blank], axis=0)
        rights.append(jnp.concatenate([turned, pads[group]], axis=1).T)

    def scores(group, index):
        kv_c = piece(kv_h, index, size, 0)
        pair = jnp.concatenate([kv_c, piece(bias_h, index, size, 0)], axis=1)
        return nn(pair, sides[group]), nn(kv_c, pads[group])

    def finish(group, index, found, dq):
        weights = jnp.exp(found[0] - levels[group])
        grad_s = (weights * (found[1] - deltas[group])).astype(BF)
        part = nn(jnp.concatenate([grad_s, weights.astype(BF)], axis=1), rights[group])
        spot = spot_of(index, size)
        if group == 0:
            total[spot, :] = part
        else:
            total[spot, :] += part
        return dq + nn(piece(kvt, index, size, 1), grad_s)

    rest, mass = stats[:hs], stats[hs : hs + 1]
    level, counts = stats[hs + 1 : hs + 2], stats[hs + 2 : hs + 3]
    centroid = cen_ref[0]
    part = shares[0][0]
    for share in shares[1:]:
        part = part + share[0]
    d_rest = part[:hs].astype(BF)
    d_mass = part[hs : hs + 1] + part[hs + 1 : hs + 2]
    delta = jnp.sum(d_rest.astype(F32) * rest, axis=0, keepdims=True) + d_mass * mass
    cen_pad = jnp.concatenate([centroid, jnp.zeros_like(centroid)], axis=0)
    rest_pad = jnp.concatenate([jnp.zeros_like(centroid), d_rest], axis=0)
    right = jnp.concatenate([cen_pad, rest_pad], axis=1).T

    def cluster_step(index, summed):
        kv_c = piece(kv_h, index, size, 0)
        marks = piece(bias_h, index, size, 0).astype(F32)
        probs = jnp.exp(nn(kv_c, cen_pad) - level)
        probs = jnp.where(marks < 2.0 * NEGATIVE, 0.0, probs)
        top = marks == 0.0
        d_probs = jnp.where(top, d_mass, nn(kv_c, rest_pad))
        d_score = (probs * (d_probs - delta)).astype(BF)
        other = jnp.where(top, 0.0, probs).astype(BF)
        both[spot_of(index, size), :] = jnp.concatenate([d_score, other], axis=1)
        return summed + nn(piece(kvt, index, size, 1), d_score)

    start = jnp.zeros((2 * hs, rows), F32)
    zero = jnp.zeros((2 * hs, clusters), F32)
    member_dq = []
    if count <= 4:
        tasks = [(group, index) for group in range(groups) for index in range(count)]
        ahead = scores(*tasks[0])
        d_cen = key_sum(keys, size, cluster_step, zero)
        dq = start
        for step, (group, index) in enumerate(tasks):
            found = ahead
            if step + 1 < len(tasks):
                ahead = scores(*tasks[step + 1])
            dq = finish(group, index, found, dq)
            if index == count - 1:
                member_dq.append(dq[:hs] * 0.125)
                dq = start
    else:
        d_cen = key_sum(keys, size, cluster_step, zero)
        for group in range(groups):

            def step(index, dq, group=group):
                return finish(group, index, scores(group, index), dq)

            member_dq.append(lax.fori_loop(0, count, step, start)[:hs] * 0.125)
    d_cen = d_cen[:hs] * 0.125 / jnp.maximum(counts, 1.0)
    high, low = split_low(d_cen)
    table = jnp.concatenate([high, low], axis=1)
    for group in range(groups):
        base = group * peers * rows
        dq_ref[group] = (member_dq[group] + nn(table, hots[group])).astype(BF)
        own = total[base : base + rows, :] + nn(both[base : base + rows, :], right)
        own_ref[0, :, group * rows : (group + 1) * rows] = own.T
        for peer in range(1, peers):
            spot = (peer - 1) * groups * rows + group * rows
            found = total[base + peer * rows : base + (peer + 1) * rows, :]
            send_ref[0, :, spot : spot + rows] = found.astype(BF).T


def join_kernel(dq_ref, own_ref, *refs, groups):
    gots, outs = refs[:-groups], refs[-groups:]
    heads, _, rows = outs[0].shape
    hs = dq_ref.shape[1] // heads
    for head in range(heads):
        for group in range(groups):
            spot = slice(group * rows, (group + 1) * rows)
            pair = own_ref[head, :, spot]
            for got in gots:
                pair = pair + got[head, :, spot].astype(F32)
            outs[group][head, :hs] = dq_ref[group, head * hs : (head + 1) * hs]
            outs[group][head, hs:] = pair.astype(BF)


def block_kernel(info, *refs, groups, chunks, fast):
    (attn, rest) = (refs[:groups], refs[groups:])
    x_ref, gain_ref, shift_ref, wo_ref, up_ref, down_ref, cot_ref = rest[:7]
    out_ref, dres_ref = rest[7:9]
    if fast:
        far_ref, low_far, act_ref, low_ref = rest[9:13]
        rest = rest[13:]
        hidden = far_ref.shape[1] * 4 // 7
    else:
        dn_ref, dup_ref, dbr_ref, act_ref, low_ref = rest[9:14]
        rest = rest[14:]
    dat = rest[:groups]
    hat_ref, inv_ref, normed, back, total = rest[groups:]
    index = pl.program_id(0)

    @pl.when(index == 0)
    def before():
        resid = x_ref[...].astype(F32)
        for group in range(groups):
            owner = lax.rem(info[0] + groups - group, groups)
            resid = resid + tn(attn[group][...], wo_ref[owner])
        total[...] = resid
        centered = resid - jnp.mean(resid, axis=-1, keepdims=True)
        variance = jnp.mean(centered * centered, axis=-1, keepdims=True)
        inverse = lax.rsqrt(variance + EPSILON)
        hat = centered * inverse
        hat_ref[...] = hat
        inv_ref[...] = jnp.broadcast_to(inverse, inv_ref.shape)
        low = (hat * gain_ref[...] + shift_ref[...]).astype(BF)
        normed[...] = low
        if fast:
            feats = attn[0].shape[0]
            half = feats // 2
            turned = low.T
            for group in range(groups):
                first = turned[group * feats : group * feats + half]
                second = turned[group * feats + half : (group + 1) * feats]
                spot = slice(group * half, (group + 1) * half)
                low_ref[spot, :] = jnp.where(info[1] == 0, first, second)
                low_far[spot, :] = jnp.where(info[1] == 0, second, first)
                first = attn[group][:half]
                second = attn[group][half:]
                spot = slice((groups + group) * half, (groups + group + 1) * half)
                low_ref[spot, :] = jnp.where(info[1] == 0, first, second)
                low_far[spot, :] = jnp.where(info[1] == 0, second, first)
        else:
            low_ref[...] = low
        back[...] = jnp.zeros_like(back)

    up = nn(normed[...], up_ref[...])
    grad_act = nt(cot_ref[...], down_ref[...])
    square = up * up
    inner = GELU_A * (up + GELU_B * up * square)
    curve = jnp.tanh(inner)
    act = (0.5 * up * (1.0 + curve)).astype(BF)
    slope = 0.5 * (1.0 + curve) + 0.5 * up * (1.0 - curve * curve) * (
        GELU_A * (1.0 + 3.0 * GELU_B * square)
    )
    d_up = (grad_act * slope).astype(BF)
    if fast:
        part = act.shape[1]
        half = part // 2
        first, second = act[:, :half], act[:, half:]
        act_ref[...] = jnp.where(info[1] == 0, first, second)
        far_ref[:, pl.ds(pl.multiple_of(index * part, part), part)] = d_up
        spot = pl.ds(pl.multiple_of(hidden + index * half, half), half)
        far_ref[:, spot] = jnp.where(info[1] == 0, second, first)
    else:
        dup_ref[...] = d_up
        act_ref[...] = act
    back[...] += nt(d_up, up_ref[...])
    total[...] += nn(act, down_ref[...])

    @pl.when(index == chunks - 1)
    def after():
        out_ref[...] = total[...].astype(BF)
        d_normed = back[...]
        hat = hat_ref[...]
        gain_part = jnp.sum(d_normed * hat, axis=0, keepdims=True)
        shift_part = jnp.sum(d_normed, axis=0, keepdims=True)
        if fast:
            rows, width = low_far.shape[1], d_normed.shape[1]
            fold = []
            for part_row in split_low(gain_part) + split_low(shift_part):
                fold += [part_row[:, k : k + rows].astype(F32) for k in range(0, width, rows)]
            fold.append(jnp.zeros((low_far.shape[0] - width - len(fold), rows), F32))
            folded = jnp.concatenate(fold, axis=0).astype(BF)
            low_far[width:, :] = folded
            low_ref[width:, :] = folded
        else:
            blank = jnp.zeros((6, d_normed.shape[1]), F32)
            dn_ref[...] = jnp.concatenate([gain_part, shift_part, blank], axis=0)
        gy = d_normed * gain_ref[...]
        mean_one = jnp.mean(gy, axis=-1, keepdims=True)
        mean_two = jnp.mean(gy * hat, axis=-1, keepdims=True)
        d_resid = cot_ref[...].astype(F32) + inv_ref[:, 0:1] * (gy - mean_one - hat * mean_two)
        dres_ref[...] = d_resid
        branch = d_resid.astype(BF)
        if fast:
            far_ref[:, hidden * 3 // 2 :] = branch
        else:
            dbr_ref[...] = branch
        for group in range(groups):
            owner = lax.rem(info[0] + groups - group, groups)
            dat[group][...] = nt(wo_ref[owner], branch).astype(BF)


def weights_kernel(info, *refs, groups):
    (dup, dup_got, dbr, dbr_got, act, act_got, low, low_got, cot, cot_got) = refs[:10]
    send_u, keep_u, send_d, keep_d, outs = refs[10:12], refs[12], refs[13:15], refs[15], refs[16]
    width = cot.shape[1]
    lead = send_u[0].shape[2] - keep_u.shape[2]

    def leave(send, turn, spot, block, first):
        if turn:
            send[0][0, spot, lead + first : lead + first + block.shape[0]] = block
        elif first:
            send[1][0, spot, first - lead : first - lead + block.shape[0]] = block
        else:
            send[0][0, spot, :lead] = block[:lead]
            send[1][0, spot, : block.shape[0] - lead] = block[lead:]

    index = pl.program_id(0)
    group_at, place_u, place_d = info[0], info[3], info[4]
    rows = width // (2 * groups)
    quarter = rows // 4
    stay = groups * rows

    @pl.when(index == 0)
    def first():
        found = nn(low[stay:width, :], dbr[...]) + nn(low_got[stay:width, :], dbr_got[...])
        fold = low[width:, :].astype(F32) + low_got[width:, :].astype(F32)
        times = width // fold.shape[1]
        norms = []
        for part in range(2):
            both = fold[2 * part * times : (2 * part + 1) * times]
            both = both + fold[(2 * part + 1) * times : (2 * part + 2) * times]
            norms.append(jnp.concatenate([both[k : k + 1] for k in range(times)], axis=1))
        norms = jnp.concatenate(norms + [jnp.zeros((6, width), F32)], axis=0)
        for group in range(groups):
            block = found[group * rows : (group + 1) * rows]
            outs[group] = block
            for part in range(4):
                tail = block[part * quarter + 16 : (part + 1) * quarter]
                tail = jnp.concatenate([tail, norms], axis=0).astype(BF)
                place = lax.bitwise_xor(part, place_d)

                for turn in range(2):

                    @pl.when(place == 2 + turn)
                    def leaves_more(turn=turn, tail=tail, group=group):
                        leave(send_d, turn, (groups - group) % groups, tail, rows)

                @pl.when(place < 2)
                def stays_more():
                    keep_d[place, (groups - group) % groups, rows:] = tail

    up = nn(low[:stay, :], dup[...]) + nn(low_got[:stay, :], dup_got[...])
    at = lax.bitwise_xor(lax.bitwise_xor(index, 2), place_u)
    for group in range(groups):
        spot = lax.rem(group + groups - group_at, groups)
        block = up[group * rows : (group + 1) * rows].astype(BF)
        away = (groups - group) % groups
        start = pl.multiple_of(at * quarter, 8)
        other = outs[group, pl.ds(start, 16), :].astype(BF)

        for turn in range(2):

            @pl.when(index == turn)
            def leaves(turn=turn, spot=spot, block=block, away=away, other=other):
                leave(send_u, turn, spot, block, 0)
                leave(send_u, turn, away, other, rows)

        @pl.when(index >= 2)
        def stays():
            keep_u[0, spot, :rows] = block
            keep_u[0, away, rows:] = other

    down = tn(act[...], cot[...]) + tn(act_got[...], cot_got[...])
    spot = lax.rem(index + groups - group_at, groups)
    for part in range(4):
        block = down[part * rows : (part + 1) * rows].astype(BF)
        place = lax.bitwise_xor(part, place_d)

        for turn in range(2):

            @pl.when(place == 2 + turn)
            def leaves_down(turn=turn, block=block):
                leave(send_d, turn, spot, block, 0)

        @pl.when(place < 2)
        def stays_down():
            keep_d[place, spot, :rows] = block


def second_kernel(keep_u, got_u, keep_d, got_d, inner, inner_got, late_u, late_d, to_y, to_x, to_xy):
    rows, lines = keep_u.shape[2], inner.shape[2]
    lead = got_u.shape[2] - rows
    to_y[:, :rows] = (keep_u[0].astype(F32) + got_u[0, :, lead:].astype(F32)).astype(BF)
    to_x[:, :rows] = (keep_d[0].astype(F32) + got_d[0, :, lead:].astype(F32)).astype(BF)
    last = to_y.shape[1] - lines
    to_y[:, last:] = (inner[1].astype(F32) + inner_got[1].astype(F32)).astype(BF)
    to_x[:, last:] = (inner[2].astype(F32) + inner_got[2].astype(F32)).astype(BF)
    to_xy[...] = (inner[3].astype(F32) + inner_got[3].astype(F32)).astype(BF)
    to_y[:, rows:last] = late_d[0]
    to_x[:, rows:last] = late_u[0]


def third_kernel(info, keep_u, one_u, keep_d, one_d, by_y, by_x, inner, inner_got, by_xy, *outs):
    rows, lines = keep_u.shape[2], inner.shape[2]
    early = one_u.shape[2] - rows
    groups = len(outs) // 2
    lead = outs[0].shape[0] // 2
    left = rows - lead
    late, mid = slice(rows, 2 * rows - early), slice(2 * rows - early, None)

    def added(keep, one, rest, by, group):
        got = jnp.concatenate([one[0, group, :early], rest[group, late]], axis=0)
        total = keep[0, group].astype(F32) + got.astype(F32)
        return (total + by[group, :rows].astype(F32)).astype(BF)

    for group in range(groups):
        first, last = outs[group], outs[groups + group]
        up = added(keep_u, one_u, by_x, by_y, group)
        down = added(keep_d, one_d, by_y, by_x, group)
        first[:lead] = up[:lead]
        first[lead:] = down[:lead]
        last[:left] = up[lead:]
        last[left : 2 * left] = down[lead:]
        both = inner[0, group].astype(F32) + inner_got[0, group].astype(F32)
        both = both + by_y[group, mid].astype(F32) + by_x[group, mid].astype(F32)
        last[2 * left :] = (both + by_xy[group].astype(F32)).astype(BF)


def fourth_kernel(info, *refs, groups, high, feats):
    parts, out = refs[:groups], refs[groups]
    total = parts[0][: 2 * high].astype(F32)
    for part in parts[1:]:
        total = total + part[: 2 * high].astype(F32)
    out[: 2 * high] = total.astype(BF)
    if parts[0].shape[0] == 2 * high:
        return
    turned = refs[groups + 1]
    third = feats // 3
    for group in range(groups):
        turned[group] = parts[group][2 * high :].astype(F32)
    spots = [lax.rem(info[0] + groups - owner, groups) for owner in range(groups)]
    found, sums = [], []
    for kind in range(3):
        lanes = slice(kind * third, (kind + 1) * third)
        found.append(jnp.concatenate([turned[spot, :, lanes] for spot in spots], axis=1))
        line = [turned[spot, 8 * kind : 8 * kind + 8, 3 * third :] for spot in spots]
        sums.append(jnp.concatenate(line, axis=1)[:1])
    sums.append(jnp.zeros((5, out.shape[1]), F32))
    out[2 * high :] = jnp.concatenate(found + sums, axis=0).astype(BF)


def spread_kernel(info, *refs, lead, high):
    firsts, lasts, (wq, wkv, pair) = refs[:4], refs[4:8], refs[8:11]
    up_ref, out_ref, down_ref, norm_ref, gq_ref, gkv_ref, vec_ref, sums = refs[11:]
    index = pl.program_id(0)
    rows, width = down_ref.shape
    quarter = rows // 4
    left = rows - lead
    order_u, order_d = (0, 2, 1, 3), (0, 1, 2, 3)

    @pl.when(index == 0)
    def first():
        for place, source in enumerate(order_u):

            @pl.when(info[3] == place)
            def take(source=source):
                sums[...] = lasts[source][2 * high :].astype(F32)[3 * quarter :]

    for place, source in enumerate(order_u):

        @pl.when(index == place)
        def upper(source=source):
            part = lasts[source]
            up_ref[:lead] = firsts[source][:lead].astype(F32)
            up_ref[lead:] = part[:left].astype(F32)
            at = pl.multiple_of(lax.bitwise_xor(index, info[3]) * quarter, 8)
            out_ref[pl.ds(at, 16), :] = part[left:high].astype(F32)
            spot = pl.ds(at, quarter)
            shift, gain = pair[spot, 0:1], pair[spot, 1:2]
            gain_sum, shift_sum = 0.0, 0.0
            blocks = part[2 * high :].astype(F32)
            for kind in range(3):
                block = blocks[kind * quarter : (kind + 1) * quarter]
                line = sums[kind : kind + 1]
                if kind == 0:
                    weight = wq[spot, :]
                    gq_ref[spot, :] = block + shift * line
                else:
                    lanes = slice((kind - 1) * width, kind * width)
                    weight = wkv[spot, lanes]
                    gkv_ref[spot, lanes] = block + shift * line
                gain_sum = gain_sum + jnp.sum(weight * block, axis=1, keepdims=True)
                shift_sum = shift_sum + jnp.sum(weight * line, axis=1, keepdims=True)
            lane = lax.broadcasted_iota(jnp.int32, (quarter, vec_ref.shape[1]), 1)
            vec_ref[spot, :] = jnp.where(lane == 0, gain_sum / gain, shift_sum)

    for place, source in enumerate(order_d):

        @pl.when(index == place)
        def lower(source=source):
            part = lasts[source]
            down_ref[:lead] = firsts[source][lead:].astype(F32)
            down_ref[lead:] = part[high : high + left].astype(F32)
            tail = part[high + left : 2 * high].astype(F32)
            at = pl.multiple_of(lax.bitwise_xor(index, info[4]) * quarter + 16, 8)
            out_ref[pl.ds(at, quarter - 16), :] = tail[: quarter - 16]

            @pl.when(lax.bitwise_xor(index, info[4]) == 0)
            def norms():
                norm_ref[...] = tail[quarter - 16 :]


def inward_kernel(info, *refs, groups, gots, fast):
    join_refs, hat_ref = refs[: 2 + gots], refs[2 + gots]
    parts = refs[3 + gots : 3 + gots + groups]
    outs = refs[3 + gots + groups :]
    join_kernel(*join_refs, *parts, groups=groups)
    heads, triple, rows = parts[0].shape
    hs = triple // 3
    total, sums = None, None
    ones = jnp.ones((16, rows), BF)
    for group in range(groups):
        order = [parts[group][h, k * hs : (k + 1) * hs] for k in range(3) for h in range(heads)]
        turned = jnp.concatenate(order, axis=0)
        found = nt(hat_ref[:, group * rows : (group + 1) * rows], turned)
        more = nt(ones, turned)
        total = found if total is None else total + found
        sums = more if sums is None else sums + more
    if not fast:
        outs[0][...] = total
        outs[1][...] = sums
        return
    own_ref, far_ref = outs
    block = total.shape[0] // (2 * groups)
    quarter = block // 4
    third = total.shape[1] // 3
    more = [sums[:8, kind * third : (kind + 1) * third] for kind in range(3)]
    more = jnp.concatenate(more, axis=0)
    for group in range(groups):
        spot = lax.rem(group + groups - info[0], groups)
        for part in range(4):
            place = lax.bitwise_xor(part, info[3])
            found = []
            for parity in range(2):
                at = (2 * group + parity) * block + part * quarter
                lines = jnp.concatenate([total[at : at + quarter], more], axis=1)
                found.append(lines.astype(BF))
            own_ref[place, spot] = jnp.where(info[1] == 0, found[0], found[1])
            far_ref[place, spot] = jnp.where(info[1] == 0, found[1], found[0])


def final_kernel(info, *refs, groups):
    parts = refs[:groups]
    x_ref, dres_ref, gain_ref, w_ref, out_ref = refs[groups:]
    d_normed = jnp.zeros(dres_ref.shape, F32)
    for group in range(groups):
        owner = lax.rem(info[0] + groups - group, groups)
        heads, triple, rows = parts[group].shape
        d_normed = d_normed + tn(parts[group][...].reshape(heads * triple, rows), w_ref[owner])
    values = x_ref[...].astype(F32)
    centered = values - jnp.mean(values, axis=-1, keepdims=True)
    variance = jnp.mean(centered * centered, axis=-1, keepdims=True)
    inverse = lax.rsqrt(variance + EPSILON)
    hat = centered * inverse
    gy = d_normed * gain_ref[...]
    mean_one = jnp.mean(gy, axis=-1, keepdims=True)
    mean_two = jnp.mean(gy * hat, axis=-1, keepdims=True)
    out_ref[...] = (dres_ref[...] + inverse * (gy - mean_one - hat * mean_two)).astype(BF)


def ordered(kernel, inputs, later):
    def run(*refs):
        kernel(*refs[:inputs], *refs[inputs + later :])

    return run if later else kernel


def whole(shape):
    return pl.BlockSpec(shape, lambda *at: (0,) * len(shape))


def per_device(
    tokens,
    cluster_ids,
    lengths,
    top_keys,
    gain_one,
    shift_one,
    w_query,
    w_keyval,
    w_out,
    gain_two,
    shift_two,
    w_up,
    w_down,
    cotangent,
):
    rows, width = tokens.shape
    heads = cluster_ids.shape[1]
    hs = width // heads
    hidden = w_up.shape[1]
    wide = lax.axis_size("wide")
    n_dp = lax.axis_size("dp")
    groups = math.gcd(heads, wide)
    peers = wide // groups
    own_heads = heads // groups
    own_clusters = top_keys.shape[2]
    clusters = own_clusters * wide
    picks = top_keys.shape[3]
    seq = rows * wide
    size = 512 if seq <= 2048 else 2048
    feats = own_heads * hs
    block_rows = width // wide
    fast = peers == 2 and n_dp == 4 and block_rows == 96 and hidden == 4 * width and width % 256 == 0 and rows % 128 == 0
    me = lax.axis_index("wide")
    group_at, peer_at = me // peers, me % peers
    dp_at = lax.axis_index("dp")
    seq_len = lengths[0]
    bit_x, bit_y = dp_at % 2, (dp_at // 2) % 2
    place_u, place_d = 2 * bit_x + bit_y, 2 * bit_y + bit_x
    info = jnp.stack([group_at, peer_at, seq_len, place_u, place_d, me]).astype(jnp.int32)

    def along_groups(values, hop):
        pairs = [(i, ((i // peers + hop) % groups) * peers + i % peers) for i in range(wide)]
        return lax.ppermute(values, "wide", pairs)

    def along_peers(values, hop):
        pairs = [(i, (i // peers) * peers + (i % peers + hop) % peers) for i in range(wide)]
        return lax.ppermute(values, "wide", pairs)

    def along_dp(values, mask):
        return lax.ppermute(values, "dp", [(i, i ^ mask) for i in range(n_dp)])

    def prefetched(
        kernel, grid, in_specs, out_specs, out_shape, mib, spent, name, scratch=(), alias=None, first=()
    ):
        first = jax.tree.leaves(first)
        call = pl.pallas_call(
            ordered(kernel, 1 + len(in_specs), len(first)),
            grid_spec=pltpu.PrefetchScalarGridSpec(
                num_scalar_prefetch=1,
                grid=grid,
                in_specs=in_specs + [pl.BlockSpec(memory_space=pl.ANY)] * len(first),
                out_specs=out_specs,
                scratch_shapes=list(scratch),
            ),
            out_shape=out_shape,
            compiler_params=params(mib, len(grid)),
            cost_estimate=spent,
            input_output_aliases=alias or {},
            name=name,
        )
        return lambda *inputs: call(*inputs, *first)

    def after(values, *others):
        return lax.optimization_barrier((values, others))[0]

    def scalar(spec):
        return pl.BlockSpec(spec.block_shape, lambda *at: spec.index_map(*at[:-1]))

    def array(shape, dtype):
        return jax.ShapeDtypeStruct(shape, dtype)

    position = me * rows + jnp.arange(rows, dtype=jnp.int32)
    marked = jnp.where((position < seq_len)[:, None], cluster_ids, -1).T
    tops = top_keys[0].transpose(0, 2, 1)[:, :, None, :]
    mine_lanes = (jnp.arange(wide, dtype=jnp.int32) == me)[None, None, :, None]
    tops = jnp.where(mine_lanes, tops, 0).reshape(heads, picks, clusters)
    lines = rows // clusters
    packed = jnp.concatenate([tops, marked.reshape(heads, lines, clusters)], axis=1)
    near = [along_peers(tokens, -hop) for hop in range(1, peers)]
    packed = after(packed.reshape(groups, own_heads, picks + lines, clusters), near)

    def of_heads(hop):
        return lax.dynamic_index_in_dim(packed, (group_at + groups - hop) % groups, keepdims=False)

    arrived = [of_heads(0)] + [along_groups(of_heads(hop), -hop) for hop in range(1, groups)]

    mine = {0: tokens, 1: along_groups(tokens, -1)}
    if groups > 2:
        mine[groups - 1] = along_groups(tokens, 1)
    ready = after(tokens, arrived)
    for hop in range(2, groups - 1):
        mine[hop] = along_groups(ready, -hop)

    w_in = jnp.concatenate([w_query, w_keyval], axis=1).T.reshape(3, heads, hs, width)
    w_in = w_in.transpose(1, 0, 2, 3).reshape(groups, 3 * feats, width)
    table_shape = (own_heads, picks + groups * lines, clusters)
    table = prefetched(
        functools.partial(table_kernel, picks=picks),
        (1,),
        [whole((own_heads, picks + lines, clusters))] * groups,
        whole(table_shape),
        array(table_shape, jnp.int32),
        8,
        cost(1e5, 1e6),
        "table",
    )(info, *arrived)
    tables = [table] + [along_peers(table, -hop) for hop in range(1, peers)]
    cot_got = [along_peers(after(cotangent, arrived), hop) for hop in range(1, peers)]
    cot_got = cot_got if fast else []
    bias, ids_all = prefetched(
        functools.partial(bias_kernel, groups=groups, peers=peers, rows=rows, picks=picks),
        (wide,),
        [whole(table_shape)] * peers,
        [
            pl.BlockSpec((own_heads, rows, clusters), lambda i, s: (0, i, 0)),
            whole((own_heads, 1, seq)),
        ],
        [array((own_heads, seq, clusters), BF), array((own_heads, 1, seq), jnp.int32)],
        12 if fast else 60,
        cost(own_heads * seq * clusters * picks * 8, own_heads * seq * clusters * 2),
        "bias",
    )(info, *tables)

    gain_row, shift_row = gain_one[None, :], shift_one[None, :]
    shapes = [
        array((width, groups * rows), BF),
        array((own_heads, 3 * hs, seq), BF),
        array((own_heads, seq, 2 * hs), BF),
    ]
    held = []
    split_peers = peers if peers <= 2 else 1
    for group in sorted(range(groups), key=lambda g: min(g, groups - g)):
        arrival = mine[group]
        first = ()
        if group == 1:
            arrival = after(arrival, bias, held, cot_got, [mine[hop] for hop in range(2, groups)])
        chunk = [arrival]
        chunk += near if group == 0 else [along_peers(arrival, -hop) for hop in range(1, peers)]
        if peers > 2:
            chunk = [jnp.concatenate(chunk, axis=0)]
        span = peers * rows
        if peers > 2:
            specs_in = [pl.BlockSpec((rows, width), lambda p, s: (p, 0))]
            grid = (peers,)
            outs = [
                pl.BlockSpec((width, rows), lambda p, s, g=group: (0, g)),
                pl.BlockSpec((own_heads, 3 * hs, rows), lambda p, s, g=group: (0, 0, g * peers + p)),
                pl.BlockSpec((own_heads, rows, 2 * hs), lambda p, s, g=group: (0, g * peers + p, 0)),
            ]
        else:
            specs_in = [whole((rows, width))] * split_peers
            grid = (1,)
            outs = [
                pl.BlockSpec((width, rows), lambda p, s, g=group: (0, g)),
                pl.BlockSpec((own_heads, 3 * hs, span), lambda p, s, g=group: (0, 0, g)),
                pl.BlockSpec((own_heads, span, 2 * hs), lambda p, s, g=group: (0, g, 0)),
            ]
        old = 1 + split_peers + 3
        held = prefetched(
            functools.partial(project_kernel, peers=split_peers, olds=len(held)),
            grid,
            specs_in
            + [
                whole((1, width)),
                whole((1, width)),
                pl.BlockSpec((1, 3 * feats, width), lambda p, s: (s[0], 0, 0)),
            ]
            + [pl.BlockSpec(memory_space=pl.ANY)] * len(held),
            outs,
            shapes,
            16 if fast else 60,
            cost(6 * span * width * feats, span * width * 4),
            "project",
            alias={old + k: k for k in range(len(held))},
            first=first,
        )(info, *chunk, gain_row, shift_row, w_in, *held)
    hat_own, feat, kv = held

    ids_full = pl.BlockSpec((1, 1, seq), lambda h, r: (h, 0, 0))
    feat_full = pl.BlockSpec((1, 3 * hs, seq), lambda h, r: (h, 0, 0))
    kv_full = pl.BlockSpec((1, seq, 2 * hs), lambda h, r: (h, 0, 0))
    bias_full = pl.BlockSpec((1, seq, clusters), lambda h, r: (h, 0, 0))
    head_rows = pl.BlockSpec((hs, rows), lambda h, r: (h, 0))
    mix_spec = pl.BlockSpec((1, 1, hs + 8, rows), lambda h, r: (h, r, 0, 0))
    stat_spec = pl.BlockSpec((1, hs + 8, clusters), lambda h, r: (h, 0, 0))
    cen_spec = pl.BlockSpec((1, hs, clusters), lambda h, r: (h, 0, 0))
    own_rows = groups * rows
    pair_flops = own_heads * own_rows * seq * 256

    one = [
        pl.BlockSpec(spec.block_shape, functools.partial(lambda h, f: f(h, 0), f=spec.index_map))
        for spec in (ids_full, feat_full, kv_full, bias_full, stat_spec, cen_spec, head_rows)
    ]
    ids_one, feat_one, kv_one, bias_one, stat_one, cen_one, rows_one = one
    part_one = pl.BlockSpec((1, hs + 16, clusters), lambda h: (h, 0, 0))
    mix_one = pl.BlockSpec((1, groups, hs + 8, rows), lambda h: (h, 0, 0, 0))
    all_groups = pl.BlockSpec((groups, hs, rows), lambda h: (0, h, 0))
    own_one = pl.BlockSpec((1, own_rows, 2 * hs), lambda h: (h, 0, 0))
    results = pl.pallas_call(
        functools.partial(forward_kernel, size=size, groups=groups, rows=rows),
        grid=(own_heads,),
        in_specs=[ids_one, feat_one, kv_one, bias_one],
        out_specs=[rows_one] * groups + [mix_one, stat_one, cen_one],
        out_shape=[array((feats, rows), BF)] * groups
        + [
            array((own_heads, groups, hs + 8, rows), F32),
            array((own_heads, hs + 8, clusters), F32),
            array((own_heads, hs, clusters), BF),
        ],
        compiler_params=params(16 if fast else 60, 1),
        cost_estimate=cost(6 * pair_flops, 8e6, own_heads * own_rows * seq),
        name="attend",
    )(ids_all, feat, kv, bias)
    attn_t = results[:groups]
    mixed, stats, centroid = results[groups:]

    arrived = [attn_t[0]] + [along_groups(attn_t[hop], hop) for hop in range(1, groups)]

    chunks = 4
    part = hidden // chunks
    early, lead = 64, 80
    w_out_g = w_out.reshape(groups, feats, width)
    gain_row2, shift_row2 = gain_two[None, :], shift_two[None, :]
    square = whole((rows, width))
    column = pl.BlockSpec((rows, part), lambda i, s: (0, i))
    norm_spec = whole((8, width))
    if fast:
        kept_shapes = [
            array((rows, hidden + hidden // 2 + width), BF),
            array((width + 16, rows), BF),
            array((rows, hidden // 2), BF),
            array((width + 16, rows), BF),
        ]
        kept_specs = [whole(item.shape) for item in kept_shapes]
        kept_specs[2] = pl.BlockSpec((rows, part // 2), lambda i, s: (0, i))
    else:
        kept_shapes = [
            array((8, width), F32),
            array((rows, hidden), BF),
            array((rows, width), BF),
            array((rows, hidden), BF),
            array((rows, width), BF),
        ]
        kept_specs = [norm_spec, column, square, column, square]
    results = prefetched(
        functools.partial(block_kernel, groups=groups, chunks=chunks, fast=fast),
        (chunks,),
        [whole((feats, rows))] * groups
        + [
            square,
            whole((1, width)),
            whole((1, width)),
            whole((groups, feats, width)),
            pl.BlockSpec((width, part), lambda i, s: (0, i)),
            pl.BlockSpec((part, width), lambda i, s: (i, 0)),
            square,
        ],
        [square, square] + kept_specs + [whole((feats, rows))] * groups,
        [array((rows, width), BF), array((rows, width), F32)]
        + kept_shapes
        + [array((feats, rows), BF)] * groups,
        28 if fast else 60,
        cost(8 * rows * width * hidden, 4 * width * hidden, rows * hidden),
        "feed",
        scratch=[
            pltpu.VMEM((rows, width), F32),
            pltpu.VMEM((rows, 128), F32),
            pltpu.VMEM((rows, width), BF),
            pltpu.VMEM((rows, width), F32),
            pltpu.VMEM((rows, width), F32),
        ],
    )(info, *arrived, tokens, gain_row2, shift_row2, w_out_g, w_up, w_down, cotangent)
    output, d_resid = results[:2]
    kept, d_attn = results[2:-groups], results[-groups:]
    grads = [d_attn[0]] + [along_groups(d_attn[hop], -hop) for hop in range(1, groups)]

    def weight_parts():
        far, low_far, act_own, low_own = kept
        got, low_got = along_peers(far, 1), along_peers(low_far, 1)
        high = block_rows + 16
        chunk = pl.BlockSpec((rows, part), lambda i, s: (0, i ^ 2 ^ s[3]))
        branch = pl.BlockSpec((rows, width), lambda i, s: (0, hidden * 3 // 2 // width))
        act_spec = pl.BlockSpec((rows, part // 2), lambda i, s: (0, i))
        act_there = pl.BlockSpec((rows, part // 2), lambda i, s: (0, 2 * hidden // part + i))
        low_spec = whole((width + 16, rows))
        shape_u = (2, groups, high, width)
        shape_d = (2, groups, high, width)
        parts = [(1, groups, tall, width) for tall in (early + high, high - early)]
        results = prefetched(
            functools.partial(weights_kernel, groups=groups),
            (4,),
            [chunk, chunk, branch, branch, act_spec, act_there, low_spec, low_spec, square, square],
            [whole(item) for item in parts]
            + [pl.BlockSpec((1,) + shape_u[1:], lambda i, s: (jnp.maximum(i - 2, 0), 0, 0, 0))]
            + [whole(item) for item in parts]
            + [whole(shape_d)],
            ([array(item, BF) for item in parts] + [array(shape_u, BF)]) * 2,
            28,
            cost(8 * rows * width * hidden, 6 * width * hidden),
            "weights",
            scratch=[pltpu.VMEM((groups, block_rows, width), F32)],
        )(info, far, got, far, got, act_own, got, low_own, low_got, cotangent, *cot_got)
        return results[:2], results[2], results[3:5], results[5]

    def weight_second(keep_u, got_u, keep_d, got_d, inner, inner_got, late_u, late_d):
        def block(shape, at):
            return pl.BlockSpec((1,) + shape[1:], lambda i: (at, 0, 0, 0))

        high, lines = keep_u.shape[2], inner.shape[2]
        shapes = [(groups, high + lines + late_u.shape[2], width)] * 2 + [(groups, lines, width)]
        return pl.pallas_call(
            second_kernel,
            grid=(1,),
            in_specs=[
                block(item.shape, item.shape[0] - 1) for item in (keep_u, got_u, keep_d, got_d)
            ]
            + [whole(item.shape) for item in (inner, inner_got, late_u, late_d)],
            out_specs=[whole(shape) for shape in shapes],
            out_shape=[array(shape, BF) for shape in shapes],
            compiler_params=params(24, 1),
            cost_estimate=cost(groups * high * width * 2, groups * high * width * 12),
            name="second",
        )(keep_u, got_u, keep_d, got_d, inner, inner_got, late_u, late_d)

    def weight_third(keep_u, got_u, keep_d, got_d, by_y, by_x, inner, inner_got, by_xy):
        def block(shape, at):
            return pl.BlockSpec((1,) + shape[1:], lambda i, s: (at, 0, 0, 0))

        left = keep_u.shape[2] - lead
        talls = [(2 * lead, width)] * groups + [(2 * left + inner.shape[2], width)] * groups
        more = (by_y, by_x)
        return prefetched(
            third_kernel,
            (1,),
            [block(item.shape, 0) for item in (keep_u, got_u, keep_d, got_d)]
            + [whole(by_y.shape), whole(by_x.shape)]
            + [block(inner.shape, 0)] * 2
            + [whole(by_xy.shape)],
            [whole(tall) for tall in talls],
            [array(tall, BF) for tall in talls],
            24,
            cost(groups * 256 * width * 4, groups * 256 * width * 8),
            "third",
            first=home,
        )(info, keep_u, got_u, keep_d, got_d, by_y, by_x, inner, inner_got, by_xy)

    def weight_fourth(came, high, lines, first):
        tall = 2 * high + (3 * lines + 8 if lines else 0)
        done = prefetched(
            functools.partial(fourth_kernel, groups=groups, high=high, feats=3 * feats),
            (1,),
            [whole(came[0].shape)] * groups,
            whole((tall, width)),
            array((tall, width), BF),
            16,
            cost(groups * tall * width, groups * tall * width * 2),
            "fourth",
            scratch=[pltpu.VMEM((groups, lines, width), F32)] if lines else [],
            first=first,
        )(info, *came)
        return [done] + [along_dp(done, mask) for mask in (1, 2, 3)]

    def weight_spread(firsts, lasts, high, ready):
        at = me * block_rows
        wq_rows = lax.dynamic_slice_in_dim(w_query, at, block_rows).astype(F32)
        wkv_rows = lax.dynamic_slice_in_dim(w_keyval, at, block_rows).astype(F32)
        pair = jnp.stack([shift_one, gain_one] + [shift_one] * 6, axis=1)
        pair = lax.dynamic_slice_in_dim(pair, at, block_rows)
        return prefetched(
            functools.partial(spread_kernel, lead=lead, high=high),
            (4,),
            [whole(item.shape) for item in firsts + lasts]
            + [whole(wq_rows.shape), whole(wkv_rows.shape), whole(pair.shape)],
            [
                pl.BlockSpec((block_rows, part), lambda i, s: (0, i ^ s[3])),
                whole((block_rows, width)),
                pl.BlockSpec((block_rows, width), lambda i, s: (i ^ s[4], 0)),
                whole((8, width)),
                whole((block_rows, width)),
                whole((block_rows, 2 * width)),
                whole((block_rows, 128)),
            ],
            [
                array((block_rows, hidden), F32),
                array((block_rows, width), F32),
                array((hidden // wide, width), F32),
                array((8, width), F32),
                array((block_rows, width), F32),
                array((block_rows, 2 * width), F32),
                array((block_rows, 128), F32),
            ],
            20,
            cost(1e6, 8 * block_rows * width * 6),
            "spread",
            scratch=[pltpu.VMEM((8, width), F32)],
        )(info, *firsts, *lasts, wq_rows, wkv_rows, pair)

    masks = [1 << k for k in range(n_dp.bit_length() - 1)]

    def reduce_rows(partial):
        blocks = partial.reshape(groups, peers, partial.shape[0] // wide, partial.shape[1])

        def of_peer(hop):
            at = (peer_at + hop) % peers
            return lax.dynamic_index_in_dim(blocks, at, axis=1, keepdims=False)

        total = of_peer(0).astype(F32)
        for hop in range(1, peers):
            total = total + along_peers(of_peer(hop), hop).astype(F32)
        total = total.astype(BF)

        def of_group(hop):
            return lax.dynamic_index_in_dim(total, (group_at + hop) % groups, keepdims=False)

        done = of_group(0).astype(F32)
        for hop in range(1, groups):
            done = done + along_groups(of_group(hop), hop).astype(F32)
        for mask in masks:
            done = done.astype(BF)
            done = done.astype(F32) + along_dp(done, mask).astype(F32)
        return done

    if fast:
        send_u, keep_u, send_d, keep_d = weight_parts()
        got_u, got_d = along_dp(send_u[0], 1), along_dp(send_d[0], 2)
    else:
        norm_two, d_up, d_branch, act, normed_two = kept
        total_up = reduce_rows(tn(normed_two, d_up).astype(BF))
        total_down = reduce_rows(tn(act, cotangent).astype(BF))
        found = jnp.stack([nn(item, d_branch).astype(BF) for item in arrived])
        found = [
            lax.dynamic_index_in_dim(found, (group_at + groups - g) % groups, keepdims=False)
            for g in range(groups)
        ]
        total_out = reduce_rows(jnp.concatenate(found, axis=0))
        norm_own = reduce_rows(norm_two[:2].T.astype(BF)).T

    share = prefetched(
        functools.partial(sums_kernel, groups=groups),
        (own_heads,),
        [scalar(spec) for spec in (ids_one, *[rows_one] * groups, mix_one)],
        scalar(part_one),
        array((own_heads, hs + 16, clusters), F32),
        16 if fast else 60,
        cost(own_heads * own_rows * clusters * 160, 2e6),
        "sums",
        first=(keep_u, keep_d) if fast else (),
    )(info, ids_all, *grads, mixed)
    share_got = [along_peers(share, hop) for hop in range(1, peers)]

    back_shapes = [
        array((groups, feats, rows), BF),
        array((own_heads, 2 * hs, own_rows), F32),
        array((own_heads, 2 * hs, max(peers - 1, 1) * own_rows), BF),
    ]
    dq, dkv_own, dkv_send = pl.pallas_call(
        functools.partial(back_kernel, size=size, groups=groups, gots=len(share_got)),
        grid=(own_heads,),
        in_specs=[ids_one, feat_one, kv_one, bias_one]
        + [rows_one] * groups
        + [mix_one, stat_one, cen_one]
        + [part_one] * (1 + len(share_got)),
        out_specs=[
            all_groups,
            pl.BlockSpec((1,) + back_shapes[1].shape[1:], lambda h: (h, 0, 0)),
            pl.BlockSpec((1,) + back_shapes[2].shape[1:], lambda h: (h, 0, 0)),
        ],
        out_shape=back_shapes,
        scratch_shapes=[pltpu.VMEM((seq, 2 * hs), F32), pltpu.VMEM((seq, 2 * clusters), BF)],
        compiler_params=params(24 if fast else 62, 1),
        cost_estimate=cost(14 * pair_flops, 10e6, own_heads * own_rows * seq),
        name="back",
    )(ids_all, feat, kv, bias, *grads, mixed, stats, centroid, share, *share_got)
    if fast:
        dkv_send = after(dkv_send, got_u, got_d)
    dkv_got = [
        along_peers(
            dkv_send if peers == 2 else dkv_send[..., (hop - 1) * own_rows : hop * own_rows], hop
        )
        for hop in range(1, peers)
    ]
    tall = block_rows + 16
    spent = cost(2 * own_rows * width * 3 * feats, 4e6)
    if fast:
        lines = block_rows // 4
        more = [array((4, groups, lines, width), BF)] * 2
    else:
        more = [array((width, 3 * feats), F32), array((16, 3 * feats), F32)]
    results = prefetched(
        functools.partial(inward_kernel, groups=groups, gots=len(dkv_got), fast=fast),
        (1,),
        [whole(back_shapes[0].shape)]
        + [whole(back_shapes[1].shape)] * (1 + len(dkv_got))
        + [whole((width, own_rows))],
        [whole((own_heads, 3 * hs, rows))] * groups + [whole(item.shape) for item in more],
        [array((own_heads, 3 * hs, rows), BF)] * groups + more,
        28 if fast else 60,
        spent,
        "inward",
    )(info, dq, dkv_own, *dkv_got, hat_own)
    d_in, more = results[:groups], results[groups:]
    home = [d_in[0]] + [along_groups(d_in[hop], hop) for hop in range(1, groups)]

    grad_tokens = prefetched(
        functools.partial(final_kernel, groups=groups),
        (1,),
        [whole((own_heads, 3 * hs, rows))] * groups
        + [square, square, whole((1, width)), whole((groups, 3 * feats, width))],
        square,
        array((rows, width), BF),
        24 if fast else 60,
        cost(6 * rows * width * width, 6 * width * width),
        "final",
    )(info, *home, tokens, d_resid, gain_row, w_in)

    if fast:
        keep, far = more
        inner_got = along_peers(far, 1)
        to_y, to_x, to_xy = weight_second(
            keep_u, got_u, keep_d, got_d, keep, inner_got, send_u[1], send_d[1]
        )
        by_y, by_x, by_xy = along_dp(to_y, 2), along_dp(to_x, 1), along_dp(to_xy, 3)
        sums = weight_third(
            keep_u, got_u, keep_d, got_d, by_y, by_x, keep, inner_got, by_xy
        )
        came_a, came_b = [sums[0]], [sums[groups]]
        came_a += [along_groups(sums[hop], hop) for hop in range(1, groups)]
        late = after(sums[groups + 1 :], came_a[1])
        came_b += [along_groups(late[hop - 1], hop) for hop in range(1, groups)]
        spread_a = weight_fourth(came_a, lead, 0, (came_b[1], grad_tokens))
        high = keep_u.shape[2] - lead
        spread_b = weight_fourth(came_b, high, lines, spread_a)
        found = weight_spread(spread_a, spread_b, high, came_a[0])
        total_up, total_out, total_down, norms, total_query, total_keyval, vector = found
        norm_own = lax.dynamic_slice_in_dim(norms, me * block_rows, block_rows, axis=1)
        gain_grad, shift_grad = vector[:, 0], vector[:, 1]
    else:
        found, more = more
        found = found.reshape(groups, peers, block_rows, 3 * feats)
        more = jnp.broadcast_to(more, (groups, peers, 16, 3 * feats))
        found = jnp.concatenate([found, more], axis=2).astype(BF)

        def of_peer(hop):
            at = (peer_at + hop) % peers
            return lax.dynamic_index_in_dim(found, at, axis=1, keepdims=False)

        total = of_peer(0).astype(F32)
        for hop in range(1, peers):
            total = total + along_peers(of_peer(hop), hop).astype(F32)
        for mask in masks:
            total = total.astype(BF)
            total = total.astype(F32) + along_dp(total, mask).astype(F32)
        total = total.astype(BF)
        items = [
            lax.dynamic_index_in_dim(total, (group_at + hop) % groups, keepdims=False)
            for hop in range(groups)
        ]
        pieces = [items[0]] + [along_groups(items[hop], hop) for hop in range(1, groups)]
        pieces = jnp.stack(pieces)
        pieces = jnp.stack(
            [
                lax.dynamic_index_in_dim(pieces, (group_at + groups - g) % groups, keepdims=False)
                for g in range(groups)
            ]
        ).astype(F32)
        q_part = pieces[:, :, :feats].transpose(1, 0, 2).reshape(tall, width)
        kv_part = (
            pieces[:, :, feats:]
            .reshape(groups, tall, 2, feats)
            .transpose(1, 2, 0, 3)
            .reshape(tall, 2 * width)
        )
        at = me * block_rows
        wq_rows = lax.dynamic_slice_in_dim(w_query, at, block_rows).astype(F32)
        wkv_rows = lax.dynamic_slice_in_dim(w_keyval, at, block_rows).astype(F32)
        gain_own = lax.dynamic_slice_in_dim(gain_one, at, block_rows)
        shift_own = lax.dynamic_slice_in_dim(shift_one, at, block_rows)
        q_sum, kv_sum = q_part[block_rows], kv_part[block_rows]
        q_part, kv_part = q_part[:block_rows], kv_part[:block_rows]
        shift_grad = jnp.sum(wq_rows * q_sum, axis=1) + jnp.sum(wkv_rows * kv_sum, axis=1)
        along = jnp.sum(wq_rows * q_part, axis=1) + jnp.sum(wkv_rows * kv_part, axis=1)
        total_query = q_part + shift_own[:, None] * q_sum
        total_keyval = kv_part + shift_own[:, None] * kv_sum
        gain_grad = along / gain_own


    return (
        output,
        grad_tokens,
        total_query,
        total_keyval,
        total_out,
        total_up,
        total_down,
        gain_grad,
        shift_grad,
        norm_own[0],
        norm_own[1],
    )


def solution(mesh):
    return jax.shard_map(
        per_device,
        mesh=mesh,
        in_specs=(
            P(("dp", "wide"), None),
            P(("dp", "wide"), None),
            P("dp"),
            P("dp", None, "wide", None),
            P(),
            P(),
            P(),
            P(),
            P(),
            P(),
            P(),
            P(),
            P(),
            P(("dp", "wide"), None),
        ),
        out_specs=(
            P(("dp", "wide"), None),
            P(("dp", "wide"), None),
            P("wide", None),
            P("wide", None),
            P("wide", None),
            P("wide", None),
            P("wide", None),
            P("wide"),
            P("wide"),
            P("wide"),
            P("wide"),
        ),
        check_vma=False,
    )
```

```python
import functools
import math

import jax
import jax.numpy as jnp
import numpy as np
from jax import lax
from jax.experimental import pallas as pl
from jax.experimental.pallas import tpu as pltpu
from jax.sharding import PartitionSpec as P

EPSILON = 1e-05
NEGATIVE = -1e30
EXCLUDED = -3e30
GELU_A = math.sqrt(2.0 / math.pi)
GELU_B = 0.044715
BF = jnp.bfloat16
F32 = jnp.float32


def nn(left, right):
    return lax.dot_general(left, right, (((1,), (0,)), ((), ())), preferred_element_type=F32)


def nt(left, right):
    return lax.dot_general(left, right, (((1,), (1,)), ((), ())), preferred_element_type=F32)


def tn(left, right):
    return lax.dot_general(left, right, (((0,), (0,)), ((), ())), preferred_element_type=F32)


def params(mib, dims):
    return pltpu.CompilerParams(
        vmem_limit_bytes=mib * 1024 * 1024, dimension_semantics=("arbitrary",) * dims
    )


def cost(flops, nbytes, trans=0):
    return pl.CostEstimate(flops=int(flops), bytes_accessed=int(nbytes), transcendentals=int(trans))


def split_low(values):
    high = values.astype(BF)
    return high, (values - high.astype(F32)).astype(BF)


def one_hot_t(ids_row, clusters):
    rows = lax.broadcasted_iota(jnp.int32, (clusters, ids_row.shape[1]), 0)
    return jnp.where(rows == ids_row, 1.0, 0.0).astype(BF)


def key_passes(total, size, score, weigh, blocks=None):
    count = total // size
    if count <= 4:
        if blocks is None:
            blocks = [score(index) for index in range(count)]
        peak = functools.reduce(jnp.maximum, [jnp.max(b, axis=0, keepdims=True) for b in blocks])
        denom, sums = 0.0, None
        for index in range(count):
            expo = jnp.exp(blocks[index] - peak)
            denom = denom + jnp.sum(expo, axis=0, keepdims=True)
            parts = weigh(index, expo)
            sums = parts if sums is None else tuple(x + y for x, y in zip(sums, parts))
        return peak, denom, sums

    def step(index, carry):
        peak, denom, sums = carry
        block = score(index)
        fresh = jnp.maximum(peak, jnp.max(block, axis=0, keepdims=True))
        expo = jnp.exp(block - fresh)
        fade = jnp.exp(peak - fresh)
        parts = weigh(index, expo)
        return (
            fresh,
            denom * fade + jnp.sum(expo, axis=0, keepdims=True),
            tuple(old * fade + new for old, new in zip(sums, parts)),
        )

    shapes = jax.eval_shape(lambda: (score(0), weigh(0, score(0))))
    lanes = shapes[0].shape[1]
    start = (
        jnp.full((1, lanes), NEGATIVE, F32),
        jnp.zeros((1, lanes), F32),
        tuple(jnp.zeros(item.shape, F32) for item in shapes[1]),
    )
    return lax.fori_loop(0, count, step, start)


def key_sum(total, size, step, start):
    count = total // size
    if count <= 4:
        for index in range(count):
            start = step(index, start)
        return start
    return lax.fori_loop(0, count, step, start)


def spot_of(index, size):
    if isinstance(index, int):
        return pl.ds(index * size, size)
    return pl.ds(pl.multiple_of(index * size, size), size)


def piece(ref, index, size, axis):
    spot = spot_of(index, size)
    return ref[spot, :] if axis == 0 else ref[:, spot]


def table_kernel(info, *refs, picks):
    parts, out = refs[:-1], refs[-1]
    total = parts[0][:, :picks]
    for part in parts[1:]:
        total = total + part[:, :picks]
    out[:, :picks] = total
    rows = (out.shape[1] - picks) // len(parts)
    for group, part in enumerate(parts):
        out[:, picks + group * rows : picks + (group + 1) * rows] = part[:, picks : picks + rows]


def bias_kernel(info, *refs, groups, peers, rows, picks):
    tables, (bias_ref, ids_ref) = refs[:peers], refs[peers:]
    part = pl.program_id(0)
    owner = (
        lax.rem(info[0] + part // peers, groups) * peers + lax.rem(info[1] + part % peers, peers)
    )
    heads, _, clusters = tables[0].shape
    place = owner * rows + lax.broadcasted_iota(jnp.int32, (rows, clusters), 0)
    plain = jnp.where(place >= info[2], EXCLUDED, NEGATIVE)
    for head in range(heads):
        top = tables[0][head, :picks]
        for table in tables[1:]:
            top = top + table[head, :picks]
        value = plain
        for pick in range(picks):
            value = jnp.where(place == top[pick : pick + 1, :], 0.0, value)
        bias_ref[head] = value.astype(BF)

    @pl.when(part == 0)
    def ids():
        lines = rows // clusters
        for head in range(heads):
            row = []
            for group in range(groups):
                for table in tables:
                    for line in range(lines):
                        at = picks + group * lines + line
                        row.append(table[head, at : at + 1, :])
            ids_ref[head] = jnp.concatenate(row, axis=1)


def project_kernel(info, *refs, peers, olds):
    parts = refs[:peers]
    gain_ref, shift_ref, w_ref = refs[peers : peers + 3]
    hat_ref, feat_ref, kv_ref = refs[peers + 3 + olds :]
    rows = hat_ref.shape[1]
    for peer in range(peers):
        values = parts[peer][...].astype(F32)
        centered = values - jnp.mean(values, axis=-1, keepdims=True)
        variance = jnp.mean(centered * centered, axis=-1, keepdims=True)
        scaled = centered * lax.rsqrt(variance + EPSILON) * gain_ref[...]
        if peer == 0:
            hat_ref[...] = scaled.astype(BF).T
        low = (scaled + shift_ref[...]).astype(BF)
        found = nt(w_ref[0], low)
        heads, triple = feat_ref.shape[0], feat_ref.shape[1]
        hs = triple // 3
        spot = slice(peer * rows, (peer + 1) * rows)
        for head in range(heads):
            base = head * triple
            query = (found[base : base + hs] * 0.125).astype(BF)
            pair = found[base + hs : base + triple].astype(BF)
            feat_ref[head, :hs, spot] = query
            feat_ref[head, hs:, spot] = pair
            kv_ref[head, spot, :] = pair.T


def forward_kernel(ids_all, feat, kv, bias, *refs, size, groups, rows):
    outs = refs[:groups]
    mix_ref, stat_ref, cen_ref = refs[groups:]
    hs = feat.shape[1] // 3
    keys = kv.shape[1]
    count = keys // size
    clusters = bias.shape[2]
    kv_h, bias_h = kv.at[0], bias.at[0]
    queries_all, kvt = feat.at[0, :hs], feat.at[0, hs:]
    hot_all = one_hot_t(ids_all[0], clusters)
    ones = jnp.ones((16, keys), BF)
    sums = nt(jnp.concatenate([queries_all[...], ones], axis=0), hot_all)
    counts = sums[hs : hs + 1]
    centroid = (sums[:hs] / jnp.maximum(counts, 1.0)).astype(BF)
    padded = jnp.concatenate([centroid, jnp.zeros_like(centroid)], axis=0)

    def cluster_score(index):
        scores = nn(piece(kv_h, index, size, 0), padded)
        outside = piece(bias_h, index, size, 0).astype(F32) < 2.0 * NEGATIVE
        return jnp.where(outside, NEGATIVE, scores)

    def cluster_weigh(index, expo):
        top = piece(bias_h, index, size, 0).astype(F32) == 0.0
        mass = jnp.sum(jnp.where(top, expo, 0.0), axis=0, keepdims=True)
        other = jnp.where(top, 0.0, expo).astype(BF)
        return nn(piece(kvt, index, size, 1), other), mass

    peers = keys // (groups * rows)
    hots, sides = [], []
    for group in range(groups):
        spot = slice(group * peers * rows, group * peers * rows + rows)
        hot = one_hot_t(ids_all[0, :, spot], clusters)
        queries = queries_all[:, spot]
        hots.append(hot)
        sides.append(jnp.concatenate([queries, jnp.zeros_like(queries), hot], axis=0))

    def member_score(group, index):
        both = jnp.concatenate([piece(kv_h, index, size, 0), piece(bias_h, index, size, 0)], axis=1)
        return nn(both, sides[group])

    def member_weigh(index, expo):
        return (nn(piece(kvt, index, size, 1), expo.astype(BF)),)

    short = count <= 4
    ahead = None
    if short:
        ahead = [member_score(0, index) for index in range(count)]
    peak, denom, (rest, mass) = key_passes(keys, size, cluster_score, cluster_weigh)
    rest = rest[hs:] / denom
    mass = mass / denom
    blank = jnp.zeros((5, clusters), F32)
    stats = jnp.concatenate([rest, mass, peak + jnp.log(denom), counts, blank], axis=0)
    stat_ref[0] = stats
    cen_ref[0] = centroid
    high, low = split_low(stats)
    table = jnp.concatenate([high, low], axis=1)
    for group in range(groups):
        gathered = nn(table, jnp.concatenate([hots[group], hots[group]], axis=0))
        blocks, ahead = ahead, None
        if short and group + 1 < groups:
            ahead = [member_score(group + 1, index) for index in range(count)]
        score = functools.partial(member_score, group)
        peak, denom, (mix,) = key_passes(keys, size, score, member_weigh, blocks)
        mix = mix[hs:] / denom
        outs[group][...] = (gathered[hs : hs + 1] * mix + gathered[:hs]).astype(BF)
        level = jnp.broadcast_to(peak + jnp.log(denom), (8, rows))
        mix_ref[0, group] = jnp.concatenate([mix, level], axis=0)


def sums_kernel(info, ids_own, *refs, groups):
    grads, (mix_ref, part_ref) = refs[:groups], refs[groups:]
    hs = grads[0].shape[0]
    total = None
    for group in range(groups):
        rows = grads[group].shape[1]
        step = ids_own.shape[2] // groups
        hot = one_hot_t(ids_own[0, :, group * step : group * step + rows], part_ref.shape[2])
        grad = grads[group][...]
        along = jnp.sum(grad.astype(F32) * mix_ref[0, group, :hs], axis=0, keepdims=True)
        high, low = split_low(along)
        pad = jnp.zeros((14, rows), BF)
        part = nt(jnp.concatenate([grad, high, low, pad], axis=0), hot)
        total = part if total is None else total + part
    part_ref[0] = total


def back_kernel(ids_all, feat, kv, bias, *refs, size, groups, gots):
    grads = refs[:groups]
    mix_ref, stat_ref, cen_ref = refs[groups : groups + 3]
    shares = refs[groups + 3 : groups + 4 + gots]
    dq_ref, own_ref, send_ref, total, both = refs[groups + 4 + gots :]
    hs, rows = grads[0].shape
    keys = kv.shape[1]
    count = keys // size
    peers = keys // (groups * rows)
    clusters = bias.shape[2]
    kv_h, bias_h = kv.at[0], bias.at[0]
    queries_all, kvt = feat.at[0, :hs], feat.at[0, hs:]
    stats = stat_ref[0]
    high, low = split_low(stats[hs : hs + 8])
    table = jnp.concatenate([high, low], axis=1)
    hots, sides, levels, deltas, pads, rights = [], [], [], [], [], []
    for group in range(groups):
        spot = slice(group * peers * rows, group * peers * rows + rows)
        hot = one_hot_t(ids_all[0, :, spot], clusters)
        queries = queries_all[:, spot]
        blank = jnp.zeros_like(queries)
        hots.append(jnp.concatenate([hot, hot], axis=0))
        sides.append(jnp.concatenate([queries, blank, hot], axis=0))
        mass = nn(table, hots[group])[0:1]
        back = (mass * grads[group][...].astype(F32)).astype(BF)
        levels.append(mix_ref[0, group, hs : hs + 1])
        deltas.append(jnp.sum(back.astype(F32) * mix_ref[0, group, :hs], axis=0, keepdims=True))
        pads.append(jnp.concatenate([blank, back], axis=0))
        turned = jnp.concatenate([queries, blank], axis=0)
        rights.append(jnp.concatenate([turned, pads[group]], axis=1).T)

    def scores(group, index):
        kv_c = piece(kv_h, index, size, 0)
        pair = jnp.concatenate([kv_c, piece(bias_h, index, size, 0)], axis=1)
        return nn(pair, sides[group]), nn(kv_c, pads[group])

    def finish(group, index, found, dq):
        weights = jnp.exp(found[0] - levels[group])
        grad_s = (weights * (found[1] - deltas[group])).astype(BF)
        part = nn(jnp.concatenate([grad_s, weights.astype(BF)], axis=1), rights[group])
        spot = spot_of(index, size)
        if group == 0:
            total[spot, :] = part
        else:
            total[spot, :] += part
        return dq + nn(piece(kvt, index, size, 1), grad_s)

    rest, mass = stats[:hs], stats[hs : hs + 1]
    level, counts = stats[hs + 1 : hs + 2], stats[hs + 2 : hs + 3]
    centroid = cen_ref[0]
    part = shares[0][0]
    for share in shares[1:]:
        part = part + share[0]
    d_rest = part[:hs].astype(BF)
    d_mass = part[hs : hs + 1] + part[hs + 1 : hs + 2]
    delta = jnp.sum(d_rest.astype(F32) * rest, axis=0, keepdims=True) + d_mass * mass
    cen_pad = jnp.concatenate([centroid, jnp.zeros_like(centroid)], axis=0)
    rest_pad = jnp.concatenate([jnp.zeros_like(centroid), d_rest], axis=0)
    right = jnp.concatenate([cen_pad, rest_pad], axis=1).T

    def cluster_step(index, summed):
        kv_c = piece(kv_h, index, size, 0)
        marks = piece(bias_h, index, size, 0).astype(F32)
        probs = jnp.exp(nn(kv_c, cen_pad) - level)
        probs = jnp.where(marks < 2.0 * NEGATIVE, 0.0, probs)
        top = marks == 0.0
        d_probs = jnp.where(top, d_mass, nn(kv_c, rest_pad))
        d_score = (probs * (d_probs - delta)).astype(BF)
        other = jnp.where(top, 0.0, probs).astype(BF)
        both[spot_of(index, size), :] = jnp.concatenate([d_score, other], axis=1)
        return summed + nn(piece(kvt, index, size, 1), d_score)

    start = jnp.zeros((2 * hs, rows), F32)
    zero = jnp.zeros((2 * hs, clusters), F32)
    member_dq = []
    if count <= 4:
        tasks = [(group, index) for group in range(groups) for index in range(count)]
        ahead = scores(*tasks[0])
        d_cen = key_sum(keys, size, cluster_step, zero)
        dq = start
        for step, (group, index) in enumerate(tasks):
            found = ahead
            if step + 1 < len(tasks):
                ahead = scores(*tasks[step + 1])
            dq = finish(group, index, found, dq)
            if index == count - 1:
                member_dq.append(dq[:hs] * 0.125)
                dq = start
    else:
        d_cen = key_sum(keys, size, cluster_step, zero)
        for group in range(groups):

            def step(index, dq, group=group):
                return finish(group, index, scores(group, index), dq)

            member_dq.append(lax.fori_loop(0, count, step, start)[:hs] * 0.125)
    d_cen = d_cen[:hs] * 0.125 / jnp.maximum(counts, 1.0)
    high, low = split_low(d_cen)
    table = jnp.concatenate([high, low], axis=1)
    for group in range(groups):
        base = group * peers * rows
        dq_ref[group] = (member_dq[group] + nn(table, hots[group])).astype(BF)
        own = total[base : base + rows, :] + nn(both[base : base + rows, :], right)
        own_ref[0, :, group * rows : (group + 1) * rows] = own.T
        for peer in range(1, peers):
            spot = (peer - 1) * groups * rows + group * rows
            found = total[base + peer * rows : base + (peer + 1) * rows, :]
            send_ref[0, :, spot : spot + rows] = found.astype(BF).T


def join_kernel(dq_ref, own_ref, *refs, groups):
    gots, outs = refs[:-groups], refs[-groups:]
    heads, _, rows = outs[0].shape
    hs = dq_ref.shape[1] // heads
    for head in range(heads):
        for group in range(groups):
            spot = slice(group * rows, (group + 1) * rows)
            pair = own_ref[head, :, spot]
            for got in gots:
                pair = pair + got[head, :, spot].astype(F32)
            outs[group][head, :hs] = dq_ref[group, head * hs : (head + 1) * hs]
            outs[group][head, hs:] = pair.astype(BF)


def block_kernel(info, *refs, groups, chunks, fast):
    (attn, rest) = (refs[:groups], refs[groups:])
    x_ref, gain_ref, shift_ref, wo_ref, up_ref, down_ref, cot_ref = rest[:7]
    out_ref, dres_ref = rest[7:9]
    if fast:
        far_ref, low_far, act_ref, low_ref = rest[9:13]
        rest = rest[13:]
        hidden = far_ref.shape[1] * 4 // 7
    else:
        dn_ref, dup_ref, dbr_ref, act_ref, low_ref = rest[9:14]
        rest = rest[14:]
    dat = rest[:groups]
    hat_ref, inv_ref, normed, back, total = rest[groups:]
    index = pl.program_id(0)

    @pl.when(index == 0)
    def before():
        resid = x_ref[...].astype(F32)
        for group in range(groups):
            owner = lax.rem(info[0] + groups - group, groups)
            resid = resid + tn(attn[group][...], wo_ref[owner])
        total[...] = resid
        centered = resid - jnp.mean(resid, axis=-1, keepdims=True)
        variance = jnp.mean(centered * centered, axis=-1, keepdims=True)
        inverse = lax.rsqrt(variance + EPSILON)
        hat = centered * inverse
        hat_ref[...] = hat
        inv_ref[...] = jnp.broadcast_to(inverse, inv_ref.shape)
        low = (hat * gain_ref[...] + shift_ref[...]).astype(BF)
        normed[...] = low
        if fast:
            feats = attn[0].shape[0]
            half = feats // 2
            turned = low.T
            for group in range(groups):
                first = turned[group * feats : group * feats + half]
                second = turned[group * feats + half : (group + 1) * feats]
                spot = slice(group * half, (group + 1) * half)
                low_ref[spot, :] = jnp.where(info[1] == 0, first, second)
                low_far[spot, :] = jnp.where(info[1] == 0, second, first)
                first = attn[group][:half]
                second = attn[group][half:]
                spot = slice((groups + group) * half, (groups + group + 1) * half)
                low_ref[spot, :] = jnp.where(info[1] == 0, first, second)
                low_far[spot, :] = jnp.where(info[1] == 0, second, first)
        else:
            low_ref[...] = low
        back[...] = jnp.zeros_like(back)

    up = nn(normed[...], up_ref[...])
    grad_act = nt(cot_ref[...], down_ref[...])
    square = up * up
    inner = GELU_A * (up + GELU_B * up * square)
    curve = jnp.tanh(inner)
    act = (0.5 * up * (1.0 + curve)).astype(BF)
    slope = 0.5 * (1.0 + curve) + 0.5 * up * (1.0 - curve * curve) * (
        GELU_A * (1.0 + 3.0 * GELU_B * square)
    )
    d_up = (grad_act * slope).astype(BF)
    if fast:
        part = act.shape[1]
        half = part // 2
        first, second = act[:, :half], act[:, half:]
        act_ref[...] = jnp.where(info[1] == 0, first, second)
        far_ref[:, pl.ds(pl.multiple_of(index * part, part), part)] = d_up
        spot = pl.ds(pl.multiple_of(hidden + index * half, half), half)
        far_ref[:, spot] = jnp.where(info[1] == 0, second, first)
    else:
        dup_ref[...] = d_up
        act_ref[...] = act
    back[...] += nt(d_up, up_ref[...])
    total[...] += nn(act, down_ref[...])

    @pl.when(index == chunks - 1)
    def after():
        out_ref[...] = total[...].astype(BF)
        d_normed = back[...]
        hat = hat_ref[...]
        gain_part = jnp.sum(d_normed * hat, axis=0, keepdims=True)
        shift_part = jnp.sum(d_normed, axis=0, keepdims=True)
        if fast:
            rows, width = low_far.shape[1], d_normed.shape[1]
            fold = []
            for part_row in split_low(gain_part) + split_low(shift_part):
                fold += [part_row[:, k : k + rows].astype(F32) for k in range(0, width, rows)]
            fold.append(jnp.zeros((low_far.shape[0] - width - len(fold), rows), F32))
            folded = jnp.concatenate(fold, axis=0).astype(BF)
            low_far[width:, :] = folded
            low_ref[width:, :] = folded
        else:
            blank = jnp.zeros((6, d_normed.shape[1]), F32)
            dn_ref[...] = jnp.concatenate([gain_part, shift_part, blank], axis=0)
        gy = d_normed * gain_ref[...]
        mean_one = jnp.mean(gy, axis=-1, keepdims=True)
        mean_two = jnp.mean(gy * hat, axis=-1, keepdims=True)
        d_resid = cot_ref[...].astype(F32) + inv_ref[:, 0:1] * (gy - mean_one - hat * mean_two)
        dres_ref[...] = d_resid
        branch = d_resid.astype(BF)
        if fast:
            far_ref[:, hidden * 3 // 2 :] = branch
        else:
            dbr_ref[...] = branch
        for group in range(groups):
            owner = lax.rem(info[0] + groups - group, groups)
            dat[group][...] = nt(wo_ref[owner], branch).astype(BF)


def weights_kernel(info, *refs, groups):
    (dup, dup_got, dbr, dbr_got, act, act_got, low, low_got, cot, cot_got) = refs[:10]
    send_u, keep_u, send_d, keep_d, outs = refs[10:12], refs[12], refs[13:15], refs[15], refs[16]
    width = cot.shape[1]
    lead = send_u[0].shape[2] - keep_u.shape[2]

    def leave(send, turn, spot, block, first):
        if turn:
            send[0][0, spot, lead + first : lead + first + block.shape[0]] = block
        elif first:
            send[1][0, spot, first - lead : first - lead + block.shape[0]] = block
        else:
            send[0][0, spot, :lead] = block[:lead]
            send[1][0, spot, : block.shape[0] - lead] = block[lead:]

    index = pl.program_id(0)
    group_at, place_u, place_d = info[0], info[3], info[4]
    rows = width // (2 * groups)
    quarter = rows // 4
    stay = groups * rows

    @pl.when(index == 0)
    def first():
        found = nn(low[stay:width, :], dbr[...]) + nn(low_got[stay:width, :], dbr_got[...])
        fold = low[width:, :].astype(F32) + low_got[width:, :].astype(F32)
        times = width // fold.shape[1]
        norms = []
        for part in range(2):
            both = fold[2 * part * times : (2 * part + 1) * times]
            both = both + fold[(2 * part + 1) * times : (2 * part + 2) * times]
            norms.append(jnp.concatenate([both[k : k + 1] for k in range(times)], axis=1))
        norms = jnp.concatenate(norms + [jnp.zeros((6, width), F32)], axis=0)
        for group in range(groups):
            block = found[group * rows : (group + 1) * rows]
            outs[group] = block
            for part in range(4):
                tail = block[part * quarter + 16 : (part + 1) * quarter]
                tail = jnp.concatenate([tail, norms], axis=0).astype(BF)
                place = lax.bitwise_xor(part, place_d)

                for turn in range(2):

                    @pl.when(place == 2 + turn)
                    def leaves_more(turn=turn, tail=tail, group=group):
                        leave(send_d, turn, (groups - group) % groups, tail, rows)

                @pl.when(place < 2)
                def stays_more():
                    keep_d[place, (groups - group) % groups, rows:] = tail

    up = nn(low[:stay, :], dup[...]) + nn(low_got[:stay, :], dup_got[...])
    at = lax.bitwise_xor(lax.bitwise_xor(index, 2), place_u)
    for group in range(groups):
        spot = lax.rem(group + groups - group_at, groups)
        block = up[group * rows : (group + 1) * rows].astype(BF)
        away = (groups - group) % groups
        start = pl.multiple_of(at * quarter, 8)
        other = outs[group, pl.ds(start, 16), :].astype(BF)

        for turn in range(2):

            @pl.when(index == turn)
            def leaves(turn=turn, spot=spot, block=block, away=away, other=other):
                leave(send_u, turn, spot, block, 0)
                leave(send_u, turn, away, other, rows)

        @pl.when(index >= 2)
        def stays():
            keep_u[0, spot, :rows] = block
            keep_u[0, away, rows:] = other

    down = tn(act[...], cot[...]) + tn(act_got[...], cot_got[...])
    spot = lax.rem(index + groups - group_at, groups)
    for part in range(4):
        block = down[part * rows : (part + 1) * rows].astype(BF)
        place = lax.bitwise_xor(part, place_d)

        for turn in range(2):

            @pl.when(place == 2 + turn)
            def leaves_down(turn=turn, block=block):
                leave(send_d, turn, spot, block, 0)

        @pl.when(place < 2)
        def stays_down():
            keep_d[place, spot, :rows] = block


def second_kernel(keep_u, got_u, keep_d, got_d, inner, inner_got, late_u, late_d, to_y, to_x, to_xy):
    rows, lines = keep_u.shape[2], inner.shape[2]
    lead = got_u.shape[2] - rows
    to_y[:, :rows] = (keep_u[0].astype(F32) + got_u[0, :, lead:].astype(F32)).astype(BF)
    to_x[:, :rows] = (keep_d[0].astype(F32) + got_d[0, :, lead:].astype(F32)).astype(BF)
    last = to_y.shape[1] - lines
    to_y[:, last:] = (inner[1].astype(F32) + inner_got[1].astype(F32)).astype(BF)
    to_x[:, last:] = (inner[2].astype(F32) + inner_got[2].astype(F32)).astype(BF)
    to_xy[...] = (inner[3].astype(F32) + inner_got[3].astype(F32)).astype(BF)
    to_y[:, rows:last] = late_d[0]
    to_x[:, rows:last] = late_u[0]


def third_kernel(info, keep_u, one_u, keep_d, one_d, by_y, by_x, inner, inner_got, by_xy, *outs):
    rows, lines = keep_u.shape[2], inner.shape[2]
    early = one_u.shape[2] - rows
    groups = len(outs) // 2
    lead = outs[0].shape[0] // 2
    left = rows - lead
    late, mid = slice(rows, 2 * rows - early), slice(2 * rows - early, None)

    def added(keep, one, rest, by, group):
        got = jnp.concatenate([one[0, group, :early], rest[group, late]], axis=0)
        total = keep[0, group].astype(F32) + got.astype(F32)
        return (total + by[group, :rows].astype(F32)).astype(BF)

    for group in range(groups):
        first, last = outs[group], outs[groups + group]
        up = added(keep_u, one_u, by_x, by_y, group)
        down = added(keep_d, one_d, by_y, by_x, group)
        first[:lead] = up[:lead]
        first[lead:] = down[:lead]
        last[:left] = up[lead:]
        last[left : 2 * left] = down[lead:]
        both = inner[0, group].astype(F32) + inner_got[0, group].astype(F32)
        both = both + by_y[group, mid].astype(F32) + by_x[group, mid].astype(F32)
        last[2 * left :] = (both + by_xy[group].astype(F32)).astype(BF)


def fourth_kernel(info, *refs, groups, high, feats):
    parts, out = refs[:groups], refs[groups]
    total = parts[0][: 2 * high].astype(F32)
    for part in parts[1:]:
        total = total + part[: 2 * high].astype(F32)
    out[: 2 * high] = total.astype(BF)
    if parts[0].shape[0] == 2 * high:
        return
    turned = refs[groups + 1]
    third = feats // 3
    quarter = turned.shape[1] - 8
    for group in range(groups):
        turned[group] = parts[group][2 * high :].astype(F32)
    spots = [lax.rem(info[0] + groups - owner, groups) for owner in range(groups)]
    found, sums = [], []
    for kind in range(3):
        lanes = slice(kind * third, (kind + 1) * third)
        found.append(jnp.concatenate([turned[spot, :quarter, lanes] for spot in spots], axis=1))
        line = [turned[spot, 8 * kind : 8 * kind + 8, 3 * third :] for spot in spots]
        sums.append(jnp.concatenate(line, axis=1)[:1])
    sums.append(jnp.zeros((5, out.shape[1]), F32))
    out[2 * high :] = jnp.concatenate(found + sums, axis=0).astype(BF)


def spread_kernel(info, *refs, lead, high):
    firsts, lasts, (wq, wkv, pair) = refs[:4], refs[4:8], refs[8:11]
    up_ref, out_ref, down_ref, norm_ref, gq_ref, gkv_ref, vec_ref, sums = refs[11:]
    index = pl.program_id(0)
    rows, width = down_ref.shape
    quarter = rows // 4
    left = rows - lead
    order_u, order_d = (0, 2, 1, 3), (0, 1, 2, 3)

    @pl.when(index == 0)
    def first():
        for place, source in enumerate(order_u):

            @pl.when(info[3] == place)
            def take(source=source):
                sums[...] = lasts[source][2 * high :].astype(F32)[3 * quarter :]

    for place, source in enumerate(order_u):

        @pl.when(index == place)
        def upper(source=source):
            part = lasts[source]
            up_ref[:lead] = firsts[source][:lead].astype(F32)
            up_ref[lead:] = part[:left].astype(F32)
            at = pl.multiple_of(lax.bitwise_xor(index, info[3]) * quarter, 8)
            out_ref[pl.ds(at, 16), :] = part[left:high].astype(F32)
            spot = pl.ds(at, quarter)
            shift, gain = pair[spot, 0:1], pair[spot, 1:2]
            gain_sum, shift_sum = 0.0, 0.0
            blocks = part[2 * high :].astype(F32)
            for kind in range(3):
                block = blocks[kind * quarter : (kind + 1) * quarter]
                line = sums[kind : kind + 1]
                if kind == 0:
                    weight = wq[spot, :]
                    gq_ref[spot, :] = block + shift * line
                else:
                    lanes = slice((kind - 1) * width, kind * width)
                    weight = wkv[spot, lanes]
                    gkv_ref[spot, lanes] = block + shift * line
                gain_sum = gain_sum + jnp.sum(weight * block, axis=1, keepdims=True)
                shift_sum = shift_sum + jnp.sum(weight * line, axis=1, keepdims=True)
            lane = lax.broadcasted_iota(jnp.int32, (quarter, vec_ref.shape[1]), 1)
            vec_ref[spot, :] = jnp.where(lane == 0, gain_sum / gain, shift_sum)

    for place, source in enumerate(order_d):

        @pl.when(index == place)
        def lower(source=source):
            part = lasts[source]
            down_ref[:lead] = firsts[source][lead:].astype(F32)
            down_ref[lead:] = part[high : high + left].astype(F32)
            tail = part[high + left : 2 * high].astype(F32)
            at = pl.multiple_of(lax.bitwise_xor(index, info[4]) * quarter + 16, 8)
            out_ref[pl.ds(at, quarter - 16), :] = tail[: quarter - 16]

            @pl.when(lax.bitwise_xor(index, info[4]) == 0)
            def norms():
                norm_ref[...] = tail[quarter - 16 :]


def inward_kernel(info, *refs, groups, gots, fast):
    join_refs, hat_ref = refs[: 2 + gots], refs[2 + gots]
    parts = refs[3 + gots : 3 + gots + groups]
    outs = refs[3 + gots + groups :]
    join_kernel(*join_refs, *parts, groups=groups)
    heads, triple, rows = parts[0].shape
    hs = triple // 3
    total, sums = None, None
    ones = jnp.ones((16, rows), BF)
    for group in range(groups):
        order = [parts[group][h, k * hs : (k + 1) * hs] for k in range(3) for h in range(heads)]
        turned = jnp.concatenate(order, axis=0)
        found = nt(hat_ref[:, group * rows : (group + 1) * rows], turned)
        more = nt(ones, turned)
        total = found if total is None else total + found
        sums = more if sums is None else sums + more
    if not fast:
        outs[0][...] = total
        outs[1][...] = sums
        return
    own_ref, far_ref = outs
    block = total.shape[0] // (2 * groups)
    quarter = block // 4
    third = total.shape[1] // 3
    more = [sums[:8, kind * third : (kind + 1) * third] for kind in range(3)]
    more = jnp.concatenate(more, axis=0)
    for group in range(groups):
        spot = lax.rem(group + groups - info[0], groups)
        for part in range(4):
            place = lax.bitwise_xor(part, info[3])
            found = []
            for parity in range(2):
                at = (2 * group + parity) * block + part * quarter
                lines = jnp.concatenate([total[at : at + quarter], more], axis=1)
                lines = jnp.concatenate([lines, jnp.zeros_like(lines[:8])], axis=0)
                found.append(lines.astype(BF))
            own_ref[place, spot] = jnp.where(info[1] == 0, found[0], found[1])
            far_ref[place, spot] = jnp.where(info[1] == 0, found[1], found[0])


def final_kernel(info, *refs, groups):
    parts = refs[:groups]
    x_ref, dres_ref, gain_ref, w_ref, out_ref = refs[groups:]
    d_normed = jnp.zeros(dres_ref.shape, F32)
    for group in range(groups):
        owner = lax.rem(info[0] + groups - group, groups)
        heads, triple, rows = parts[group].shape
        d_normed = d_normed + tn(parts[group][...].reshape(heads * triple, rows), w_ref[owner])
    values = x_ref[...].astype(F32)
    centered = values - jnp.mean(values, axis=-1, keepdims=True)
    variance = jnp.mean(centered * centered, axis=-1, keepdims=True)
    inverse = lax.rsqrt(variance + EPSILON)
    hat = centered * inverse
    gy = d_normed * gain_ref[...]
    mean_one = jnp.mean(gy, axis=-1, keepdims=True)
    mean_two = jnp.mean(gy * hat, axis=-1, keepdims=True)
    out_ref[...] = (dres_ref[...] + inverse * (gy - mean_one - hat * mean_two)).astype(BF)


def ordered(kernel, inputs, later):
    def run(*refs):
        kernel(*refs[:inputs], *refs[inputs + later :])

    return run if later else kernel


def whole(shape):
    return pl.BlockSpec(shape, lambda *at: (0,) * len(shape))


def per_device(
    tokens,
    cluster_ids,
    lengths,
    top_keys,
    gain_one,
    shift_one,
    w_query,
    w_keyval,
    w_out,
    gain_two,
    shift_two,
    w_up,
    w_down,
    cotangent,
):
    rows, width = tokens.shape
    heads = cluster_ids.shape[1]
    hs = width // heads
    hidden = w_up.shape[1]
    wide = lax.axis_size("wide")
    n_dp = lax.axis_size("dp")
    groups = math.gcd(heads, wide)
    peers = wide // groups
    own_heads = heads // groups
    own_clusters = top_keys.shape[2]
    clusters = own_clusters * wide
    picks = top_keys.shape[3]
    seq = rows * wide
    size = 512 if seq <= 2048 else 2048
    feats = own_heads * hs
    block_rows = width // wide
    fast = peers == 2 and n_dp == 4 and block_rows == 96 and hidden == 4 * width and width % 256 == 0 and rows % 128 == 0
    me = lax.axis_index("wide")
    group_at, peer_at = me // peers, me % peers
    dp_at = lax.axis_index("dp")
    seq_len = lengths[0]
    bit_x, bit_y = dp_at % 2, (dp_at // 2) % 2
    place_u, place_d = 2 * bit_x + bit_y, 2 * bit_y + bit_x
    info = jnp.stack([group_at, peer_at, seq_len, place_u, place_d, me]).astype(jnp.int32)

    def along_groups(values, hop):
        pairs = [(i, ((i // peers + hop) % groups) * peers + i % peers) for i in range(wide)]
        return lax.ppermute(values, "wide", pairs)

    def along_peers(values, hop):
        pairs = [(i, (i // peers) * peers + (i % peers + hop) % peers) for i in range(wide)]
        return lax.ppermute(values, "wide", pairs)

    def along_dp(values, mask):
        return lax.ppermute(values, "dp", [(i, i ^ mask) for i in range(n_dp)])

    def prefetched(
        kernel, grid, in_specs, out_specs, out_shape, mib, spent, name, scratch=(), alias=None, first=()
    ):
        first = jax.tree.leaves(first)
        call = pl.pallas_call(
            ordered(kernel, 1 + len(in_specs), len(first)),
            grid_spec=pltpu.PrefetchScalarGridSpec(
                num_scalar_prefetch=1,
                grid=grid,
                in_specs=in_specs + [pl.BlockSpec(memory_space=pl.ANY)] * len(first),
                out_specs=out_specs,
                scratch_shapes=list(scratch),
            ),
            out_shape=out_shape,
            compiler_params=params(mib, len(grid)),
            cost_estimate=spent,
            input_output_aliases=alias or {},
            name=name,
        )
        return lambda *inputs: call(*inputs, *first)

    def after(values, *others):
        return lax.optimization_barrier((values, others))[0]

    def scalar(spec):
        return pl.BlockSpec(spec.block_shape, lambda *at: spec.index_map(*at[:-1]))

    def array(shape, dtype):
        return jax.ShapeDtypeStruct(shape, dtype)

    position = me * rows + jnp.arange(rows, dtype=jnp.int32)
    marked = jnp.where((position < seq_len)[:, None], cluster_ids, -1).T
    tops = top_keys[0].transpose(0, 2, 1)[:, :, None, :]
    mine_lanes = (jnp.arange(wide, dtype=jnp.int32) == me)[None, None, :, None]
    tops = jnp.where(mine_lanes, tops, 0).reshape(heads, picks, clusters)
    lines = rows // clusters
    marked = marked.reshape(heads, lines, clusters)
    fill = jnp.zeros((heads, -lines % 8, clusters), jnp.int32)
    packed = jnp.concatenate([tops, marked, fill], axis=1)
    near = [along_peers(tokens, -hop) for hop in range(1, peers)]
    packed = after(packed.reshape(groups, own_heads, -1, clusters), near)

    def of_heads(hop):
        return lax.dynamic_index_in_dim(packed, (group_at + groups - hop) % groups, keepdims=False)

    arrived = [of_heads(0)] + [along_groups(of_heads(hop), -hop) for hop in range(1, groups)]

    mine = {0: tokens, 1: along_groups(tokens, -1)}
    if groups > 2:
        mine[groups - 1] = along_groups(tokens, 1)
    ready = after(tokens, arrived)
    for hop in range(2, groups - 1):
        mine[hop] = along_groups(ready, -hop)

    w_in = jnp.concatenate([w_query, w_keyval], axis=1).T.reshape(3, heads, hs, width)
    w_in = w_in.transpose(1, 0, 2, 3).reshape(groups, 3 * feats, width)
    table_shape = (own_heads, picks + groups * lines, clusters)
    table = prefetched(
        functools.partial(table_kernel, picks=picks),
        (1,),
        [whole(packed.shape[1:])] * groups,
        whole(table_shape),
        array(table_shape, jnp.int32),
        8,
        cost(1e5, 1e6),
        "table",
    )(info, *arrived)
    tables = [table] + [along_peers(table, -hop) for hop in range(1, peers)]
    cot_got = [along_peers(after(cotangent, arrived), hop) for hop in range(1, peers)]
    cot_got = cot_got if fast else []
    bias, ids_all = prefetched(
        functools.partial(bias_kernel, groups=groups, peers=peers, rows=rows, picks=picks),
        (wide,),
        [whole(table_shape)] * peers,
        [
            pl.BlockSpec((own_heads, rows, clusters), lambda i, s: (0, i, 0)),
            whole((own_heads, 1, seq)),
        ],
        [array((own_heads, seq, clusters), BF), array((own_heads, 1, seq), jnp.int32)],
        12 if fast else 60,
        cost(own_heads * seq * clusters * picks * 8, own_heads * seq * clusters * 2),
        "bias",
    )(info, *tables)

    gain_row, shift_row = gain_one[None, :], shift_one[None, :]
    shapes = [
        array((width, groups * rows), BF),
        array((own_heads, 3 * hs, seq), BF),
        array((own_heads, seq, 2 * hs), BF),
    ]
    held = []
    split_peers = peers if peers <= 2 else 1
    for group in sorted(range(groups), key=lambda g: min(g, groups - g)):
        arrival = mine[group]
        first = ()
        if group == 1:
            arrival = after(arrival, bias, held, cot_got, [mine[hop] for hop in range(2, groups)])
        chunk = [arrival]
        chunk += near if group == 0 else [along_peers(arrival, -hop) for hop in range(1, peers)]
        if peers > 2:
            chunk = [jnp.concatenate(chunk, axis=0)]
        span = peers * rows
        if peers > 2:
            specs_in = [pl.BlockSpec((rows, width), lambda p, s: (p, 0))]
            grid = (peers,)
            outs = [
                pl.BlockSpec((width, rows), lambda p, s, g=group: (0, g)),
                pl.BlockSpec((own_heads, 3 * hs, rows), lambda p, s, g=group: (0, 0, g * peers + p)),
                pl.BlockSpec((own_heads, rows, 2 * hs), lambda p, s, g=group: (0, g * peers + p, 0)),
            ]
        else:
            specs_in = [whole((rows, width))] * split_peers
            grid = (1,)
            outs = [
                pl.BlockSpec((width, rows), lambda p, s, g=group: (0, g)),
                pl.BlockSpec((own_heads, 3 * hs, span), lambda p, s, g=group: (0, 0, g)),
                pl.BlockSpec((own_heads, span, 2 * hs), lambda p, s, g=group: (0, g, 0)),
            ]
        old = 1 + split_peers + 3
        held = prefetched(
            functools.partial(project_kernel, peers=split_peers, olds=len(held)),
            grid,
            specs_in
            + [
                whole((1, width)),
                whole((1, width)),
                pl.BlockSpec((1, 3 * feats, width), lambda p, s: (s[0], 0, 0)),
            ]
            + [pl.BlockSpec(memory_space=pl.ANY)] * len(held),
            outs,
            shapes,
            16 if fast else 60,
            cost(6 * span * width * feats, span * width * 4),
            "project",
            alias={old + k: k for k in range(len(held))},
            first=first,
        )(info, *chunk, gain_row, shift_row, w_in, *held)
    hat_own, feat, kv = held

    ids_full = pl.BlockSpec((1, 1, seq), lambda h, r: (h, 0, 0))
    feat_full = pl.BlockSpec((1, 3 * hs, seq), lambda h, r: (h, 0, 0))
    kv_full = pl.BlockSpec((1, seq, 2 * hs), lambda h, r: (h, 0, 0))
    bias_full = pl.BlockSpec((1, seq, clusters), lambda h, r: (h, 0, 0))
    head_rows = pl.BlockSpec((hs, rows), lambda h, r: (h, 0))
    mix_spec = pl.BlockSpec((1, 1, hs + 8, rows), lambda h, r: (h, r, 0, 0))
    stat_spec = pl.BlockSpec((1, hs + 8, clusters), lambda h, r: (h, 0, 0))
    cen_spec = pl.BlockSpec((1, hs, clusters), lambda h, r: (h, 0, 0))
    own_rows = groups * rows
    pair_flops = own_heads * own_rows * seq * 256

    one = [
        pl.BlockSpec(spec.block_shape, functools.partial(lambda h, f: f(h, 0), f=spec.index_map))
        for spec in (ids_full, feat_full, kv_full, bias_full, stat_spec, cen_spec, head_rows)
    ]
    ids_one, feat_one, kv_one, bias_one, stat_one, cen_one, rows_one = one
    part_one = pl.BlockSpec((1, hs + 16, clusters), lambda h: (h, 0, 0))
    mix_one = pl.BlockSpec((1, groups, hs + 8, rows), lambda h: (h, 0, 0, 0))
    all_groups = pl.BlockSpec((groups, hs, rows), lambda h: (0, h, 0))
    own_one = pl.BlockSpec((1, own_rows, 2 * hs), lambda h: (h, 0, 0))
    results = pl.pallas_call(
        functools.partial(forward_kernel, size=size, groups=groups, rows=rows),
        grid=(own_heads,),
        in_specs=[ids_one, feat_one, kv_one, bias_one],
        out_specs=[rows_one] * groups + [mix_one, stat_one, cen_one],
        out_shape=[array((feats, rows), BF)] * groups
        + [
            array((own_heads, groups, hs + 8, rows), F32),
            array((own_heads, hs + 8, clusters), F32),
            array((own_heads, hs, clusters), BF),
        ],
        compiler_params=params(16 if fast else 60, 1),
        cost_estimate=cost(6 * pair_flops, 8e6, own_heads * own_rows * seq),
        name="attend",
    )(ids_all, feat, kv, bias)
    attn_t = results[:groups]
    mixed, stats, centroid = results[groups:]

    arrived = [attn_t[0]] + [along_groups(attn_t[hop], hop) for hop in range(1, groups)]

    chunks = 4
    part = hidden // chunks
    early, lead = 64, 80
    w_out_g = w_out.reshape(groups, feats, width)
    gain_row2, shift_row2 = gain_two[None, :], shift_two[None, :]
    square = whole((rows, width))
    column = pl.BlockSpec((rows, part), lambda i, s: (0, i))
    norm_spec = whole((8, width))
    if fast:
        kept_shapes = [
            array((rows, hidden + hidden // 2 + width), BF),
            array((width + 16, rows), BF),
            array((rows, hidden // 2), BF),
            array((width + 16, rows), BF),
        ]
        kept_specs = [whole(item.shape) for item in kept_shapes]
        kept_specs[2] = pl.BlockSpec((rows, part // 2), lambda i, s: (0, i))
    else:
        kept_shapes = [
            array((8, width), F32),
            array((rows, hidden), BF),
            array((rows, width), BF),
            array((rows, hidden), BF),
            array((rows, width), BF),
        ]
        kept_specs = [norm_spec, column, square, column, square]
    results = prefetched(
        functools.partial(block_kernel, groups=groups, chunks=chunks, fast=fast),
        (chunks,),
        [whole((feats, rows))] * groups
        + [
            square,
            whole((1, width)),
            whole((1, width)),
            whole((groups, feats, width)),
            pl.BlockSpec((width, part), lambda i, s: (0, i)),
            pl.BlockSpec((part, width), lambda i, s: (i, 0)),
            square,
        ],
        [square, square] + kept_specs + [whole((feats, rows))] * groups,
        [array((rows, width), BF), array((rows, width), F32)]
        + kept_shapes
        + [array((feats, rows), BF)] * groups,
        28 if fast else 60,
        cost(8 * rows * width * hidden, 4 * width * hidden, rows * hidden),
        "feed",
        scratch=[
            pltpu.VMEM((rows, width), F32),
            pltpu.VMEM((rows, 128), F32),
            pltpu.VMEM((rows, width), BF),
            pltpu.VMEM((rows, width), F32),
            pltpu.VMEM((rows, width), F32),
        ],
    )(info, *arrived, tokens, gain_row2, shift_row2, w_out_g, w_up, w_down, cotangent)
    output, d_resid = results[:2]
    kept, d_attn = results[2:-groups], results[-groups:]
    grads = [d_attn[0]] + [along_groups(d_attn[hop], -hop) for hop in range(1, groups)]

    def weight_parts():
        far, low_far, act_own, low_own = kept
        got, low_got = along_peers(far, 1), along_peers(low_far, 1)
        high = block_rows + 16
        chunk = pl.BlockSpec((rows, part), lambda i, s: (0, i ^ 2 ^ s[3]))
        branch = pl.BlockSpec((rows, width), lambda i, s: (0, hidden * 3 // 2 // width))
        act_spec = pl.BlockSpec((rows, part // 2), lambda i, s: (0, i))
        act_there = pl.BlockSpec((rows, part // 2), lambda i, s: (0, 2 * hidden // part + i))
        low_spec = whole((width + 16, rows))
        shape_u = (2, groups, high, width)
        shape_d = (2, groups, high, width)
        parts = [(1, groups, tall, width) for tall in (early + high, high - early)]
        results = prefetched(
            functools.partial(weights_kernel, groups=groups),
            (4,),
            [chunk, chunk, branch, branch, act_spec, act_there, low_spec, low_spec, square, square],
            [whole(item) for item in parts]
            + [pl.BlockSpec((1,) + shape_u[1:], lambda i, s: (jnp.maximum(i - 2, 0), 0, 0, 0))]
            + [whole(item) for item in parts]
            + [whole(shape_d)],
            ([array(item, BF) for item in parts] + [array(shape_u, BF)]) * 2,
            28,
            cost(8 * rows * width * hidden, 6 * width * hidden),
            "weights",
            scratch=[pltpu.VMEM((groups, block_rows, width), F32)],
        )(info, far, got, far, got, act_own, got, low_own, low_got, cotangent, *cot_got)
        return results[:2], results[2], results[3:5], results[5]

    def weight_second(keep_u, got_u, keep_d, got_d, inner, inner_got, late_u, late_d):
        def block(shape, at):
            return pl.BlockSpec((1,) + shape[1:], lambda i: (at, 0, 0, 0))

        high, lines = keep_u.shape[2], inner.shape[2]
        shapes = [(groups, high + lines + late_u.shape[2], width)] * 2 + [(groups, lines, width)]
        return pl.pallas_call(
            second_kernel,
            grid=(1,),
            in_specs=[
                block(item.shape, item.shape[0] - 1) for item in (keep_u, got_u, keep_d, got_d)
            ]
            + [whole(item.shape) for item in (inner, inner_got, late_u, late_d)],
            out_specs=[whole(shape) for shape in shapes],
            out_shape=[array(shape, BF) for shape in shapes],
            compiler_params=params(24, 1),
            cost_estimate=cost(groups * high * width * 2, groups * high * width * 12),
            name="second",
        )(keep_u, got_u, keep_d, got_d, inner, inner_got, late_u, late_d)

    def weight_third(keep_u, got_u, keep_d, got_d, by_y, by_x, inner, inner_got, by_xy):
        def block(shape, at):
            return pl.BlockSpec((1,) + shape[1:], lambda i, s: (at, 0, 0, 0))

        left = keep_u.shape[2] - lead
        talls = [(2 * lead, width)] * groups + [(2 * left + inner.shape[2], width)] * groups
        more = (by_y, by_x)
        return prefetched(
            third_kernel,
            (1,),
            [block(item.shape, 0) for item in (keep_u, got_u, keep_d, got_d)]
            + [whole(by_y.shape), whole(by_x.shape)]
            + [block(inner.shape, 0)] * 2
            + [whole(by_xy.shape)],
            [whole(tall) for tall in talls],
            [array(tall, BF) for tall in talls],
            24,
            cost(groups * 256 * width * 4, groups * 256 * width * 8),
            "third",
            first=home,
        )(info, keep_u, got_u, keep_d, got_d, by_y, by_x, inner, inner_got, by_xy)

    def weight_fourth(came, high, lines, first):
        tall = 2 * high + (3 * (block_rows // 4) + 8 if lines else 0)
        done = prefetched(
            functools.partial(fourth_kernel, groups=groups, high=high, feats=3 * feats),
            (1,),
            [whole(came[0].shape)] * groups,
            whole((tall, width)),
            array((tall, width), BF),
            16,
            cost(groups * tall * width, groups * tall * width * 2),
            "fourth",
            scratch=[pltpu.VMEM((groups, lines, width), F32)] if lines else [],
            first=first,
        )(info, *came)
        return [done] + [along_dp(done, mask) for mask in (1, 2, 3)]

    def weight_spread(firsts, lasts, high, ready):
        at = me * block_rows
        wq_rows = lax.dynamic_slice_in_dim(w_query, at, block_rows).astype(F32)
        wkv_rows = lax.dynamic_slice_in_dim(w_keyval, at, block_rows).astype(F32)
        pair = jnp.stack([shift_one, gain_one] + [shift_one] * 6, axis=1)
        pair = lax.dynamic_slice_in_dim(pair, at, block_rows)
        return prefetched(
            functools.partial(spread_kernel, lead=lead, high=high),
            (4,),
            [whole(item.shape) for item in firsts + lasts]
            + [whole(wq_rows.shape), whole(wkv_rows.shape), whole(pair.shape)],
            [
                pl.BlockSpec((block_rows, part), lambda i, s: (0, i ^ s[3])),
                whole((block_rows, width)),
                pl.BlockSpec((block_rows, width), lambda i, s: (i ^ s[4], 0)),
                whole((8, width)),
                whole((block_rows, width)),
                whole((block_rows, 2 * width)),
                whole((block_rows, 128)),
            ],
            [
                array((block_rows, hidden), F32),
                array((block_rows, width), F32),
                array((hidden // wide, width), F32),
                array((8, width), F32),
                array((block_rows, width), F32),
                array((block_rows, 2 * width), F32),
                array((block_rows, 128), F32),
            ],
            20,
            cost(1e6, 8 * block_rows * width * 6),
            "spread",
            scratch=[pltpu.VMEM((8, width), F32)],
        )(info, *firsts, *lasts, wq_rows, wkv_rows, pair)

    masks = [1 << k for k in range(n_dp.bit_length() - 1)]

    def reduce_rows(partial):
        blocks = partial.reshape(groups, peers, partial.shape[0] // wide, partial.shape[1])

        def of_peer(hop):
            at = (peer_at + hop) % peers
            return lax.dynamic_index_in_dim(blocks, at, axis=1, keepdims=False)

        total = of_peer(0).astype(F32)
        for hop in range(1, peers):
            total = total + along_peers(of_peer(hop), hop).astype(F32)
        total = total.astype(BF)

        def of_group(hop):
            return lax.dynamic_index_in_dim(total, (group_at + hop) % groups, keepdims=False)

        done = of_group(0).astype(F32)
        for hop in range(1, groups):
            done = done + along_groups(of_group(hop), hop).astype(F32)
        for mask in masks:
            done = done.astype(BF)
            done = done.astype(F32) + along_dp(done, mask).astype(F32)
        return done

    if fast:
        send_u, keep_u, send_d, keep_d = weight_parts()
        got_u, got_d = along_dp(send_u[0], 1), along_dp(send_d[0], 2)
    else:
        norm_two, d_up, d_branch, act, normed_two = kept
        total_up = reduce_rows(tn(normed_two, d_up).astype(BF))
        total_down = reduce_rows(tn(act, cotangent).astype(BF))
        found = jnp.stack([nn(item, d_branch).astype(BF) for item in arrived])
        found = [
            lax.dynamic_index_in_dim(found, (group_at + groups - g) % groups, keepdims=False)
            for g in range(groups)
        ]
        total_out = reduce_rows(jnp.concatenate(found, axis=0))
        norm_own = reduce_rows(norm_two[:2].T.astype(BF)).T

    share = prefetched(
        functools.partial(sums_kernel, groups=groups),
        (own_heads,),
        [scalar(spec) for spec in (ids_one, *[rows_one] * groups, mix_one)],
        scalar(part_one),
        array((own_heads, hs + 16, clusters), F32),
        16 if fast else 60,
        cost(own_heads * own_rows * clusters * 160, 2e6),
        "sums",
        first=(keep_u, keep_d) if fast else (),
    )(info, ids_all, *grads, mixed)
    share_got = [along_peers(share, hop) for hop in range(1, peers)]

    back_shapes = [
        array((groups, feats, rows), BF),
        array((own_heads, 2 * hs, own_rows), F32),
        array((own_heads, 2 * hs, max(peers - 1, 1) * own_rows), BF),
    ]
    dq, dkv_own, dkv_send = pl.pallas_call(
        functools.partial(back_kernel, size=size, groups=groups, gots=len(share_got)),
        grid=(own_heads,),
        in_specs=[ids_one, feat_one, kv_one, bias_one]
        + [rows_one] * groups
        + [mix_one, stat_one, cen_one]
        + [part_one] * (1 + len(share_got)),
        out_specs=[
            all_groups,
            pl.BlockSpec((1,) + back_shapes[1].shape[1:], lambda h: (h, 0, 0)),
            pl.BlockSpec((1,) + back_shapes[2].shape[1:], lambda h: (h, 0, 0)),
        ],
        out_shape=back_shapes,
        scratch_shapes=[pltpu.VMEM((seq, 2 * hs), F32), pltpu.VMEM((seq, 2 * clusters), BF)],
        compiler_params=params(24 if fast else 62, 1),
        cost_estimate=cost(14 * pair_flops, 10e6, own_heads * own_rows * seq),
        name="back",
    )(ids_all, feat, kv, bias, *grads, mixed, stats, centroid, share, *share_got)
    if fast:
        dkv_send = after(dkv_send, got_u, got_d)
    dkv_got = [
        along_peers(
            dkv_send if peers == 2 else dkv_send[..., (hop - 1) * own_rows : hop * own_rows], hop
        )
        for hop in range(1, peers)
    ]
    tall = block_rows + 16
    spent = cost(2 * own_rows * width * 3 * feats, 4e6)
    if fast:
        lines = block_rows // 4 + 8
        more = [array((4, groups, lines, width), BF)] * 2
    else:
        more = [array((width, 3 * feats), F32), array((16, 3 * feats), F32)]
    results = prefetched(
        functools.partial(inward_kernel, groups=groups, gots=len(dkv_got), fast=fast),
        (1,),
        [whole(back_shapes[0].shape)]
        + [whole(back_shapes[1].shape)] * (1 + len(dkv_got))
        + [whole((width, own_rows))],
        [whole((own_heads, 3 * hs, rows))] * groups + [whole(item.shape) for item in more],
        [array((own_heads, 3 * hs, rows), BF)] * groups + more,
        28 if fast else 60,
        spent,
        "inward",
    )(info, dq, dkv_own, *dkv_got, hat_own)
    d_in, more = results[:groups], results[groups:]
    home = [d_in[0]] + [along_groups(d_in[hop], hop) for hop in range(1, groups)]

    grad_tokens = prefetched(
        functools.partial(final_kernel, groups=groups),
        (1,),
        [whole((own_heads, 3 * hs, rows))] * groups
        + [square, square, whole((1, width)), whole((groups, 3 * feats, width))],
        square,
        array((rows, width), BF),
        24 if fast else 60,
        cost(6 * rows * width * width, 6 * width * width),
        "final",
    )(info, *home, tokens, d_resid, gain_row, w_in)

    if fast:
        keep, far = more
        inner_got = along_peers(far, 1)
        to_y, to_x, to_xy = weight_second(
            keep_u, got_u, keep_d, got_d, keep, inner_got, send_u[1], send_d[1]
        )
        by_y, by_x, by_xy = along_dp(to_y, 2), along_dp(to_x, 1), along_dp(to_xy, 3)
        sums = weight_third(
            keep_u, got_u, keep_d, got_d, by_y, by_x, keep, inner_got, by_xy
        )
        came_a, came_b = [sums[0]], [sums[groups]]
        came_a += [along_groups(sums[hop], hop) for hop in range(1, groups)]
        late = after(sums[groups + 1 :], came_a[1])
        came_b += [along_groups(late[hop - 1], hop) for hop in range(1, groups)]
        spread_a = weight_fourth(came_a, lead, 0, (came_b[1], grad_tokens))
        high = keep_u.shape[2] - lead
        spread_b = weight_fourth(came_b, high, lines, spread_a)
        found = weight_spread(spread_a, spread_b, high, came_a[0])
        total_up, total_out, total_down, norms, total_query, total_keyval, vector = found
        norm_own = lax.dynamic_slice_in_dim(norms, me * block_rows, block_rows, axis=1)
        gain_grad, shift_grad = vector[:, 0], vector[:, 1]
    else:
        found, more = more
        found = found.reshape(groups, peers, block_rows, 3 * feats)
        more = jnp.broadcast_to(more, (groups, peers, 16, 3 * feats))
        found = jnp.concatenate([found, more], axis=2).astype(BF)

        def of_peer(hop):
            at = (peer_at + hop) % peers
            return lax.dynamic_index_in_dim(found, at, axis=1, keepdims=False)

        total = of_peer(0).astype(F32)
        for hop in range(1, peers):
            total = total + along_peers(of_peer(hop), hop).astype(F32)
        for mask in masks:
            total = total.astype(BF)
            total = total.astype(F32) + along_dp(total, mask).astype(F32)
        total = total.astype(BF)
        items = [
            lax.dynamic_index_in_dim(total, (group_at + hop) % groups, keepdims=False)
            for hop in range(groups)
        ]
        pieces = [items[0]] + [along_groups(items[hop], hop) for hop in range(1, groups)]
        pieces = jnp.stack(pieces)
        pieces = jnp.stack(
            [
                lax.dynamic_index_in_dim(pieces, (group_at + groups - g) % groups, keepdims=False)
                for g in range(groups)
            ]
        ).astype(F32)
        q_part = pieces[:, :, :feats].transpose(1, 0, 2).reshape(tall, width)
        kv_part = (
            pieces[:, :, feats:]
            .reshape(groups, tall, 2, feats)
            .transpose(1, 2, 0, 3)
            .reshape(tall, 2 * width)
        )
        at = me * block_rows
        wq_rows = lax.dynamic_slice_in_dim(w_query, at, block_rows).astype(F32)
        wkv_rows = lax.dynamic_slice_in_dim(w_keyval, at, block_rows).astype(F32)
        gain_own = lax.dynamic_slice_in_dim(gain_one, at, block_rows)
        shift_own = lax.dynamic_slice_in_dim(shift_one, at, block_rows)
        q_sum, kv_sum = q_part[block_rows], kv_part[block_rows]
        q_part, kv_part = q_part[:block_rows], kv_part[:block_rows]
        shift_grad = jnp.sum(wq_rows * q_sum, axis=1) + jnp.sum(wkv_rows * kv_sum, axis=1)
        along = jnp.sum(wq_rows * q_part, axis=1) + jnp.sum(wkv_rows * kv_part, axis=1)
        total_query = q_part + shift_own[:, None] * q_sum
        total_keyval = kv_part + shift_own[:, None] * kv_sum
        gain_grad = along / gain_own


    return (
        output,
        grad_tokens,
        total_query,
        total_keyval,
        total_out,
        total_up,
        total_down,
        gain_grad,
        shift_grad,
        norm_own[0],
        norm_own[1],
    )


def solution(mesh):
    return jax.shard_map(
        per_device,
        mesh=mesh,
        in_specs=(
            P(("dp", "wide"), None),
            P(("dp", "wide"), None),
            P("dp"),
            P("dp", None, "wide", None),
            P(),
            P(),
            P(),
            P(),
            P(),
            P(),
            P(),
            P(),
            P(),
            P(("dp", "wide"), None),
        ),
        out_specs=(
            P(("dp", "wide"), None),
            P(("dp", "wide"), None),
            P("wide", None),
            P("wide", None),
            P("wide", None),
            P("wide", None),
            P("wide", None),
            P("wide"),
            P("wide"),
            P("wide"),
            P("wide"),
        ),
        check_vma=False,
    )
```

```python
import functools
import math

import jax
import jax.numpy as jnp
import numpy as np
from jax import lax
from jax.experimental import pallas as pl
from jax.experimental.pallas import tpu as pltpu
from jax.sharding import PartitionSpec as P

EPSILON = 1e-05
NEGATIVE = -1e30
EXCLUDED = -3e30
GELU_A = math.sqrt(2.0 / math.pi)
GELU_B = 0.044715
BF = jnp.bfloat16
F32 = jnp.float32


def nn(left, right):
    return lax.dot_general(left, right, (((1,), (0,)), ((), ())), preferred_element_type=F32)


def nt(left, right):
    return lax.dot_general(left, right, (((1,), (1,)), ((), ())), preferred_element_type=F32)


def tn(left, right):
    return lax.dot_general(left, right, (((0,), (0,)), ((), ())), preferred_element_type=F32)


def params(mib, dims):
    return pltpu.CompilerParams(
        vmem_limit_bytes=mib * 1024 * 1024, dimension_semantics=("arbitrary",) * dims
    )


def cost(flops, nbytes, trans=0):
    return pl.CostEstimate(flops=int(flops), bytes_accessed=int(nbytes), transcendentals=int(trans))


def split_low(values):
    high = values.astype(BF)
    return high, (values - high.astype(F32)).astype(BF)


def one_hot_t(ids_row, clusters):
    rows = lax.broadcasted_iota(jnp.int32, (clusters, ids_row.shape[1]), 0)
    return jnp.where(rows == ids_row, 1.0, 0.0).astype(BF)


def key_passes(total, size, score, weigh, blocks=None):
    count = total // size
    if count <= 4:
        if blocks is None:
            blocks = [score(index) for index in range(count)]
        peak = functools.reduce(jnp.maximum, [jnp.max(b, axis=0, keepdims=True) for b in blocks])
        denom, sums = 0.0, None
        for index in range(count):
            expo = jnp.exp(blocks[index] - peak)
            denom = denom + jnp.sum(expo, axis=0, keepdims=True)
            parts = weigh(index, expo)
            sums = parts if sums is None else tuple(x + y for x, y in zip(sums, parts))
        return peak, denom, sums

    def step(index, carry):
        peak, denom, sums = carry
        block = score(index)
        fresh = jnp.maximum(peak, jnp.max(block, axis=0, keepdims=True))
        expo = jnp.exp(block - fresh)
        fade = jnp.exp(peak - fresh)
        parts = weigh(index, expo)
        return (
            fresh,
            denom * fade + jnp.sum(expo, axis=0, keepdims=True),
            tuple(old * fade + new for old, new in zip(sums, parts)),
        )

    shapes = jax.eval_shape(lambda: (score(0), weigh(0, score(0))))
    lanes = shapes[0].shape[1]
    start = (
        jnp.full((1, lanes), NEGATIVE, F32),
        jnp.zeros((1, lanes), F32),
        tuple(jnp.zeros(item.shape, F32) for item in shapes[1]),
    )
    return lax.fori_loop(0, count, step, start)


def key_sum(total, size, step, start):
    count = total // size
    if count <= 4:
        for index in range(count):
            start = step(index, start)
        return start
    return lax.fori_loop(0, count, step, start)


def spot_of(index, size):
    if isinstance(index, int):
        return pl.ds(index * size, size)
    return pl.ds(pl.multiple_of(index * size, size), size)


def piece(ref, index, size, axis):
    spot = spot_of(index, size)
    return ref[spot, :] if axis == 0 else ref[:, spot]


def table_kernel(info, *refs, picks):
    parts, out = refs[:-1], refs[-1]
    total = parts[0][:, :picks]
    for part in parts[1:]:
        total = total + part[:, :picks]
    out[:, :picks] = total
    rows = (out.shape[1] - picks) // len(parts)
    for group, part in enumerate(parts):
        out[:, picks + group * rows : picks + (group + 1) * rows] = part[:, picks : picks + rows]


def bias_kernel(info, *refs, groups, peers, rows, picks):
    tables, (bias_ref, ids_ref) = refs[:peers], refs[peers:]
    part = pl.program_id(0)
    owner = (
        lax.rem(info[0] + part // peers, groups) * peers + lax.rem(info[1] + part % peers, peers)
    )
    heads, _, clusters = tables[0].shape
    place = owner * rows + lax.broadcasted_iota(jnp.int32, (rows, clusters), 0)
    plain = jnp.where(place >= info[2], EXCLUDED, NEGATIVE)
    for head in range(heads):
        top = tables[0][head, :picks]
        for table in tables[1:]:
            top = top + table[head, :picks]
        value = plain
        for pick in range(picks):
            value = jnp.where(place == top[pick : pick + 1, :], 0.0, value)
        bias_ref[head] = value.astype(BF)

    @pl.when(part == 0)
    def ids():
        lines = rows // clusters
        for head in range(heads):
            row = []
            for group in range(groups):
                for table in tables:
                    for line in range(lines):
                        at = picks + group * lines + line
                        row.append(table[head, at : at + 1, :])
            ids_ref[head] = jnp.concatenate(row, axis=1)


def project_kernel(info, *refs, peers, olds):
    parts = refs[:peers]
    gain_ref, shift_ref, w_ref = refs[peers : peers + 3]
    hat_ref, feat_ref, kv_ref = refs[peers + 3 + olds :]
    rows = hat_ref.shape[1]
    for peer in range(peers):
        values = parts[peer][...].astype(F32)
        centered = values - jnp.mean(values, axis=-1, keepdims=True)
        variance = jnp.mean(centered * centered, axis=-1, keepdims=True)
        scaled = centered * lax.rsqrt(variance + EPSILON) * gain_ref[...]
        if peer == 0:
            hat_ref[...] = scaled.astype(BF).T
        low = (scaled + shift_ref[...]).astype(BF)
        found = nt(w_ref[0], low)
        heads, triple = feat_ref.shape[0], feat_ref.shape[1]
        hs = triple // 3
        spot = slice(peer * rows, (peer + 1) * rows)
        for head in range(heads):
            base = head * triple
            query = (found[base : base + hs] * 0.125).astype(BF)
            pair = found[base + hs : base + triple].astype(BF)
            feat_ref[head, :hs, spot] = query
            feat_ref[head, hs:, spot] = pair
            kv_ref[head, spot, :] = pair.T


def forward_kernel(ids_all, feat, kv, bias, *refs, size, groups, rows):
    outs = refs[:groups]
    mix_ref, stat_ref, cen_ref = refs[groups:]
    hs = feat.shape[1] // 3
    keys = kv.shape[1]
    count = keys // size
    clusters = bias.shape[2]
    kv_h, bias_h = kv.at[0], bias.at[0]
    queries_all, kvt = feat.at[0, :hs], feat.at[0, hs:]
    hot_all = one_hot_t(ids_all[0], clusters)
    ones = jnp.ones((16, keys), BF)
    sums = nt(jnp.concatenate([queries_all[...], ones], axis=0), hot_all)
    counts = sums[hs : hs + 1]
    centroid = (sums[:hs] / jnp.maximum(counts, 1.0)).astype(BF)
    padded = jnp.concatenate([centroid, jnp.zeros_like(centroid)], axis=0)

    def cluster_score(index):
        scores = nn(piece(kv_h, index, size, 0), padded)
        outside = piece(bias_h, index, size, 0).astype(F32) < 2.0 * NEGATIVE
        return jnp.where(outside, NEGATIVE, scores)

    def cluster_weigh(index, expo):
        top = piece(bias_h, index, size, 0).astype(F32) == 0.0
        mass = jnp.sum(jnp.where(top, expo, 0.0), axis=0, keepdims=True)
        other = jnp.where(top, 0.0, expo).astype(BF)
        return nn(piece(kvt, index, size, 1), other), mass

    peers = keys // (groups * rows)
    hots, sides = [], []
    for group in range(groups):
        spot = slice(group * peers * rows, group * peers * rows + rows)
        hot = one_hot_t(ids_all[0, :, spot], clusters)
        queries = queries_all[:, spot]
        hots.append(hot)
        sides.append(jnp.concatenate([queries, jnp.zeros_like(queries), hot], axis=0))

    def member_score(group, index):
        both = jnp.concatenate([piece(kv_h, index, size, 0), piece(bias_h, index, size, 0)], axis=1)
        return nn(both, sides[group])

    def member_weigh(index, expo):
        return (nn(piece(kvt, index, size, 1), expo.astype(BF)),)

    short = count <= 4
    ahead = None
    if short:
        ahead = [member_score(0, index) for index in range(count)]
    peak, denom, (rest, mass) = key_passes(keys, size, cluster_score, cluster_weigh)
    rest = rest[hs:] / denom
    mass = mass / denom
    blank = jnp.zeros((5, clusters), F32)
    stats = jnp.concatenate([rest, mass, peak + jnp.log(denom), counts, blank], axis=0)
    stat_ref[0] = stats
    cen_ref[0] = centroid
    high, low = split_low(stats)
    table = jnp.concatenate([high, low], axis=1)
    for group in range(groups):
        gathered = nn(table, jnp.concatenate([hots[group], hots[group]], axis=0))
        blocks, ahead = ahead, None
        if short and group + 1 < groups:
            ahead = [member_score(group + 1, index) for index in range(count)]
        score = functools.partial(member_score, group)
        peak, denom, (mix,) = key_passes(keys, size, score, member_weigh, blocks)
        mix = mix[hs:] / denom
        outs[group][...] = (gathered[hs : hs + 1] * mix + gathered[:hs]).astype(BF)
        level = jnp.broadcast_to(peak + jnp.log(denom), (8, rows))
        mix_ref[0, group] = jnp.concatenate([mix, level], axis=0)


def sums_kernel(info, ids_own, *refs, groups):
    grads, (mix_ref, part_ref) = refs[:groups], refs[groups:]
    hs = grads[0].shape[0]
    total = None
    for group in range(groups):
        rows = grads[group].shape[1]
        step = ids_own.shape[2] // groups
        hot = one_hot_t(ids_own[0, :, group * step : group * step + rows], part_ref.shape[2])
        grad = grads[group][...]
        along = jnp.sum(grad.astype(F32) * mix_ref[0, group, :hs], axis=0, keepdims=True)
        high, low = split_low(along)
        pad = jnp.zeros((14, rows), BF)
        part = nt(jnp.concatenate([grad, high, low, pad], axis=0), hot)
        total = part if total is None else total + part
    part_ref[0] = total


def back_kernel(ids_all, feat, kv, bias, *refs, size, groups, gots):
    grads = refs[:groups]
    mix_ref, stat_ref, cen_ref = refs[groups : groups + 3]
    shares = refs[groups + 3 : groups + 4 + gots]
    dq_ref, own_ref, send_ref, total, both = refs[groups + 4 + gots :]
    hs, rows = grads[0].shape
    keys = kv.shape[1]
    count = keys // size
    peers = keys // (groups * rows)
    clusters = bias.shape[2]
    kv_h, bias_h = kv.at[0], bias.at[0]
    queries_all, kvt = feat.at[0, :hs], feat.at[0, hs:]
    stats = stat_ref[0]
    high, low = split_low(stats[hs : hs + 8])
    table = jnp.concatenate([high, low], axis=1)
    hots, sides, levels, deltas, pads, rights = [], [], [], [], [], []
    for group in range(groups):
        spot = slice(group * peers * rows, group * peers * rows + rows)
        hot = one_hot_t(ids_all[0, :, spot], clusters)
        queries = queries_all[:, spot]
        blank = jnp.zeros_like(queries)
        hots.append(jnp.concatenate([hot, hot], axis=0))
        sides.append(jnp.concatenate([queries, blank, hot], axis=0))
        mass = nn(table, hots[group])[0:1]
        back = (mass * grads[group][...].astype(F32)).astype(BF)
        levels.append(mix_ref[0, group, hs : hs + 1])
        deltas.append(jnp.sum(back.astype(F32) * mix_ref[0, group, :hs], axis=0, keepdims=True))
        pads.append(jnp.concatenate([blank, back], axis=0))
        turned = jnp.concatenate([queries, blank], axis=0)
        rights.append(jnp.concatenate([turned, pads[group]], axis=1).T)

    def scores(group, index):
        kv_c = piece(kv_h, index, size, 0)
        pair = jnp.concatenate([kv_c, piece(bias_h, index, size, 0)], axis=1)
        return nn(pair, sides[group]), nn(kv_c, pads[group])

    def finish(group, index, found, dq):
        weights = jnp.exp(found[0] - levels[group])
        grad_s = (weights * (found[1] - deltas[group])).astype(BF)
        part = nn(jnp.concatenate([grad_s, weights.astype(BF)], axis=1), rights[group])
        spot = spot_of(index, size)
        if group == 0:
            total[spot, :] = part
        else:
            total[spot, :] += part
        return dq + nn(piece(kvt, index, size, 1), grad_s)

    rest, mass = stats[:hs], stats[hs : hs + 1]
    level, counts = stats[hs + 1 : hs + 2], stats[hs + 2 : hs + 3]
    centroid = cen_ref[0]
    part = shares[0][0]
    for share in shares[1:]:
        part = part + share[0]
    d_rest = part[:hs].astype(BF)
    d_mass = part[hs : hs + 1] + part[hs + 1 : hs + 2]
    delta = jnp.sum(d_rest.astype(F32) * rest, axis=0, keepdims=True) + d_mass * mass
    cen_pad = jnp.concatenate([centroid, jnp.zeros_like(centroid)], axis=0)
    rest_pad = jnp.concatenate([jnp.zeros_like(centroid), d_rest], axis=0)
    right = jnp.concatenate([cen_pad, rest_pad], axis=1).T

    def cluster_step(index, summed):
        kv_c = piece(kv_h, index, size, 0)
        marks = piece(bias_h, index, size, 0).astype(F32)
        probs = jnp.exp(nn(kv_c, cen_pad) - level)
        probs = jnp.where(marks < 2.0 * NEGATIVE, 0.0, probs)
        top = marks == 0.0
        d_probs = jnp.where(top, d_mass, nn(kv_c, rest_pad))
        d_score = (probs * (d_probs - delta)).astype(BF)
        other = jnp.where(top, 0.0, probs).astype(BF)
        both[spot_of(index, size), :] = jnp.concatenate([d_score, other], axis=1)
        return summed + nn(piece(kvt, index, size, 1), d_score)

    start = jnp.zeros((2 * hs, rows), F32)
    zero = jnp.zeros((2 * hs, clusters), F32)
    member_dq = []
    if count <= 4:
        tasks = [(group, index) for group in range(groups) for index in range(count)]
        ahead = scores(*tasks[0])
        d_cen = key_sum(keys, size, cluster_step, zero)
        dq = start
        for step, (group, index) in enumerate(tasks):
            found = ahead
            if step + 1 < len(tasks):
                ahead = scores(*tasks[step + 1])
            dq = finish(group, index, found, dq)
            if index == count - 1:
                member_dq.append(dq[:hs] * 0.125)
                dq = start
    else:
        d_cen = key_sum(keys, size, cluster_step, zero)
        for group in range(groups):

            def step(index, dq, group=group):
                return finish(group, index, scores(group, index), dq)

            member_dq.append(lax.fori_loop(0, count, step, start)[:hs] * 0.125)
    d_cen = d_cen[:hs] * 0.125 / jnp.maximum(counts, 1.0)
    high, low = split_low(d_cen)
    table = jnp.concatenate([high, low], axis=1)
    for group in range(groups):
        base = group * peers * rows
        dq_ref[group] = (member_dq[group] + nn(table, hots[group])).astype(BF)
        own = total[base : base + rows, :] + nn(both[base : base + rows, :], right)
        own_ref[0, :, group * rows : (group + 1) * rows] = own.T
        for peer in range(1, peers):
            spot = (peer - 1) * groups * rows + group * rows
            found = total[base + peer * rows : base + (peer + 1) * rows, :]
            send_ref[0, :, spot : spot + rows] = found.astype(BF).T


def join_kernel(dq_ref, own_ref, *refs, groups):
    gots, outs = refs[:-groups], refs[-groups:]
    heads, _, rows = outs[0].shape
    hs = dq_ref.shape[1] // heads
    for head in range(heads):
        for group in range(groups):
            spot = slice(group * rows, (group + 1) * rows)
            pair = own_ref[head, :, spot]
            for got in gots:
                pair = pair + got[head, :, spot].astype(F32)
            outs[group][head, :hs] = dq_ref[group, head * hs : (head + 1) * hs]
            outs[group][head, hs:] = pair.astype(BF)


def block_kernel(info, *refs, groups, chunks, fast):
    (attn, rest) = (refs[:groups], refs[groups:])
    x_ref, gain_ref, shift_ref, wo_ref, up_ref, down_ref, cot_ref = rest[:7]
    out_ref, dres_ref = rest[7:9]
    if fast:
        far_ref, low_far, act_ref, low_ref = rest[9:13]
        rest = rest[13:]
        hidden = far_ref.shape[1] * 4 // 7
    else:
        dn_ref, dup_ref, dbr_ref, act_ref, low_ref = rest[9:14]
        rest = rest[14:]
    dat = rest[:groups]
    hat_ref, inv_ref, normed, back, total = rest[groups:]
    index = pl.program_id(0)

    @pl.when(index == 0)
    def before():
        resid = x_ref[...].astype(F32)
        for group in range(groups):
            owner = lax.rem(info[0] + groups - group, groups)
            resid = resid + tn(attn[group][...], wo_ref[owner])
        total[...] = resid
        centered = resid - jnp.mean(resid, axis=-1, keepdims=True)
        variance = jnp.mean(centered * centered, axis=-1, keepdims=True)
        inverse = lax.rsqrt(variance + EPSILON)
        hat = centered * inverse
        hat_ref[...] = hat
        inv_ref[...] = jnp.broadcast_to(inverse, inv_ref.shape)
        low = (hat * gain_ref[...] + shift_ref[...]).astype(BF)
        normed[...] = low
        if fast:
            feats = attn[0].shape[0]
            half = feats // 2
            turned = low.T
            for group in range(groups):
                first = turned[group * feats : group * feats + half]
                second = turned[group * feats + half : (group + 1) * feats]
                spot = slice(group * half, (group + 1) * half)
                low_ref[spot, :] = jnp.where(info[1] == 0, first, second)
                low_far[spot, :] = jnp.where(info[1] == 0, second, first)
                first = attn[group][:half]
                second = attn[group][half:]
                spot = slice((groups + group) * half, (groups + group + 1) * half)
                low_ref[spot, :] = jnp.where(info[1] == 0, first, second)
                low_far[spot, :] = jnp.where(info[1] == 0, second, first)
        else:
            low_ref[...] = low
        back[...] = jnp.zeros_like(back)

    up = nn(normed[...], up_ref[...])
    grad_act = nt(cot_ref[...], down_ref[...])
    square = up * up
    inner = GELU_A * (up + GELU_B * up * square)
    curve = jnp.tanh(inner)
    act = (0.5 * up * (1.0 + curve)).astype(BF)
    slope = 0.5 * (1.0 + curve) + 0.5 * up * (1.0 - curve * curve) * (
        GELU_A * (1.0 + 3.0 * GELU_B * square)
    )
    d_up = (grad_act * slope).astype(BF)
    if fast:
        part = act.shape[1]
        half = part // 2
        first, second = act[:, :half], act[:, half:]
        act_ref[...] = jnp.where(info[1] == 0, first, second)
        far_ref[:, pl.ds(pl.multiple_of(index * part, part), part)] = d_up
        spot = pl.ds(pl.multiple_of(hidden + index * half, half), half)
        far_ref[:, spot] = jnp.where(info[1] == 0, second, first)
    else:
        dup_ref[...] = d_up
        act_ref[...] = act
    back[...] += nt(d_up, up_ref[...])
    total[...] += nn(act, down_ref[...])

    @pl.when(index == chunks - 1)
    def after():
        out_ref[...] = total[...].astype(BF)
        d_normed = back[...]
        hat = hat_ref[...]
        gain_part = jnp.sum(d_normed * hat, axis=0, keepdims=True)
        shift_part = jnp.sum(d_normed, axis=0, keepdims=True)
        if fast:
            rows, width = low_far.shape[1], d_normed.shape[1]
            fold = []
            for part_row in split_low(gain_part) + split_low(shift_part):
                fold += [part_row[:, k : k + rows].astype(F32) for k in range(0, width, rows)]
            fold.append(jnp.zeros((low_far.shape[0] - width - len(fold), rows), F32))
            folded = jnp.concatenate(fold, axis=0).astype(BF)
            low_far[width:, :] = folded
            low_ref[width:, :] = folded
        else:
            blank = jnp.zeros((6, d_normed.shape[1]), F32)
            dn_ref[...] = jnp.concatenate([gain_part, shift_part, blank], axis=0)
        gy = d_normed * gain_ref[...]
        mean_one = jnp.mean(gy, axis=-1, keepdims=True)
        mean_two = jnp.mean(gy * hat, axis=-1, keepdims=True)
        d_resid = cot_ref[...].astype(F32) + inv_ref[:, 0:1] * (gy - mean_one - hat * mean_two)
        dres_ref[...] = d_resid
        branch = d_resid.astype(BF)
        if fast:
            far_ref[:, hidden * 3 // 2 :] = branch
        else:
            dbr_ref[...] = branch
        for group in range(groups):
            owner = lax.rem(info[0] + groups - group, groups)
            dat[group][...] = nt(wo_ref[owner], branch).astype(BF)


def weights_kernel(info, *refs, groups):
    (dup, dup_got, dbr, dbr_got, act, act_got, low, low_got, cot, cot_got) = refs[:10]
    send_u, keep_u, send_d, keep_d, outs = refs[10:12], refs[12], refs[13:15], refs[15], refs[16]
    width = cot.shape[1]
    lead = send_u[0].shape[2] - keep_u.shape[2]

    def leave(send, turn, spot, block, first):
        if turn:
            send[0][0, spot, lead + first : lead + first + block.shape[0]] = block
        elif first:
            send[1][0, spot, first - lead : first - lead + block.shape[0]] = block
        else:
            send[0][0, spot, :lead] = block[:lead]
            send[1][0, spot, : block.shape[0] - lead] = block[lead:]

    index = pl.program_id(0)
    group_at, place_u, place_d = info[0], info[3], info[4]
    rows = width // (2 * groups)
    quarter = rows // 4
    stay = groups * rows

    @pl.when(index == 0)
    def first():
        found = nn(low[stay:width, :], dbr[...]) + nn(low_got[stay:width, :], dbr_got[...])
        fold = low[width:, :].astype(F32) + low_got[width:, :].astype(F32)
        times = width // fold.shape[1]
        norms = []
        for part in range(2):
            both = fold[2 * part * times : (2 * part + 1) * times]
            both = both + fold[(2 * part + 1) * times : (2 * part + 2) * times]
            norms.append(jnp.concatenate([both[k : k + 1] for k in range(times)], axis=1))
        norms = jnp.concatenate(norms + [jnp.zeros((6, width), F32)], axis=0)
        for group in range(groups):
            block = found[group * rows : (group + 1) * rows]
            outs[group] = block
            for part in range(4):
                tail = block[part * quarter + 16 : (part + 1) * quarter]
                tail = jnp.concatenate([tail, norms], axis=0).astype(BF)
                place = lax.bitwise_xor(part, place_d)

                for turn in range(2):

                    @pl.when(place == 2 + turn)
                    def leaves_more(turn=turn, tail=tail, group=group):
                        leave(send_d, turn, (groups - group) % groups, tail, rows)

                @pl.when(place < 2)
                def stays_more():
                    keep_d[place, (groups - group) % groups, rows:] = tail

    up = nn(low[:stay, :], dup[...]) + nn(low_got[:stay, :], dup_got[...])
    at = lax.bitwise_xor(lax.bitwise_xor(index, 2), place_u)
    for group in range(groups):
        spot = lax.rem(group + groups - group_at, groups)
        block = up[group * rows : (group + 1) * rows].astype(BF)
        away = (groups - group) % groups
        start = pl.multiple_of(at * quarter, 8)
        other = outs[group, pl.ds(start, 16), :].astype(BF)

        for turn in range(2):

            @pl.when(index == turn)
            def leaves(turn=turn, spot=spot, block=block, away=away, other=other):
                leave(send_u, turn, spot, block, 0)
                leave(send_u, turn, away, other, rows)

        @pl.when(index >= 2)
        def stays():
            keep_u[0, spot, :rows] = block
            keep_u[0, away, rows:] = other

    down = tn(act[...], cot[...]) + tn(act_got[...], cot_got[...])
    spot = lax.rem(index + groups - group_at, groups)
    for part in range(4):
        block = down[part * rows : (part + 1) * rows].astype(BF)
        place = lax.bitwise_xor(part, place_d)

        for turn in range(2):

            @pl.when(place == 2 + turn)
            def leaves_down(turn=turn, block=block):
                leave(send_d, turn, spot, block, 0)

        @pl.when(place < 2)
        def stays_down():
            keep_d[place, spot, :rows] = block


def second_kernel(keep_u, got_u, keep_d, got_d, inner, inner_got, late_u, late_d, to_y, to_x, to_xy):
    rows, lines = keep_u.shape[2], inner.shape[2]
    lead = got_u.shape[2] - rows
    to_y[:, :rows] = (keep_u[0].astype(F32) + got_u[0, :, lead:].astype(F32)).astype(BF)
    to_x[:, :rows] = (keep_d[0].astype(F32) + got_d[0, :, lead:].astype(F32)).astype(BF)
    last = to_y.shape[1] - lines
    to_y[:, last:] = (inner[1].astype(F32) + inner_got[1].astype(F32)).astype(BF)
    to_x[:, last:] = (inner[2].astype(F32) + inner_got[2].astype(F32)).astype(BF)
    to_xy[...] = (inner[3].astype(F32) + inner_got[3].astype(F32)).astype(BF)
    to_y[:, rows:last] = late_d[0]
    to_x[:, rows:last] = late_u[0]


def third_kernel(info, keep_u, one_u, keep_d, one_d, by_y, by_x, inner, inner_got, by_xy, *outs):
    rows, lines = keep_u.shape[2], inner.shape[2]
    early = one_u.shape[2] - rows
    groups = len(outs) // 2
    lead = outs[0].shape[0] // 2
    left = rows - lead
    late, mid = slice(rows, 2 * rows - early), slice(2 * rows - early, None)

    def added(keep, one, rest, by, group):
        got = jnp.concatenate([one[0, group, :early], rest[group, late]], axis=0)
        total = keep[0, group].astype(F32) + got.astype(F32)
        return (total + by[group, :rows].astype(F32)).astype(BF)

    for group in range(groups):
        first, last = outs[group], outs[groups + group]
        up = added(keep_u, one_u, by_x, by_y, group)
        down = added(keep_d, one_d, by_y, by_x, group)
        first[:lead] = up[:lead]
        first[lead:] = down[:lead]
        last[:left] = up[lead:]
        last[left : 2 * left] = down[lead:]
        both = inner[0, group].astype(F32) + inner_got[0, group].astype(F32)
        both = both + by_y[group, mid].astype(F32) + by_x[group, mid].astype(F32)
        last[2 * left :] = (both + by_xy[group].astype(F32)).astype(BF)


def fourth_kernel(info, *refs, groups, high, feats):
    parts, out = refs[:groups], refs[groups]
    total = parts[0][: 2 * high].astype(F32)
    for part in parts[1:]:
        total = total + part[: 2 * high].astype(F32)
    out[: 2 * high] = total.astype(BF)
    if parts[0].shape[0] == 2 * high:
        return
    turned = refs[groups + 1]
    third = feats // 3
    quarter = turned.shape[1] - 8
    for group in range(groups):
        turned[group] = parts[group][2 * high :].astype(F32)
    spots = [lax.rem(info[0] + groups - owner, groups) for owner in range(groups)]
    found, sums = [], []
    for kind in range(3):
        lanes = slice(kind * third, (kind + 1) * third)
        found.append(jnp.concatenate([turned[spot, :quarter, lanes] for spot in spots], axis=1))
        line = [turned[spot, 8 * kind : 8 * kind + 8, 3 * third :] for spot in spots]
        sums.append(jnp.concatenate(line, axis=1)[:1])
    sums.append(jnp.zeros((5, out.shape[1]), F32))
    out[2 * high :] = jnp.concatenate(found + sums, axis=0).astype(BF)


def spread_kernel(info, *refs, lead, high):
    firsts, lasts, (wq, wkv, pair) = refs[:4], refs[4:8], refs[8:11]
    up_ref, out_ref, down_ref, norm_ref, gq_ref, gkv_ref, vec_ref, sums = refs[11:]
    index = pl.program_id(0)
    rows, width = down_ref.shape
    quarter = rows // 4
    left = rows - lead
    order_u, order_d = (0, 2, 1, 3), (0, 1, 2, 3)

    @pl.when(index == 0)
    def first():
        for place, source in enumerate(order_u):

            @pl.when(info[3] == place)
            def take(source=source):
                sums[...] = lasts[source][2 * high :].astype(F32)[3 * quarter :]

    for place, source in enumerate(order_u):

        @pl.when(index == place)
        def upper(source=source):
            part = lasts[source]
            up_ref[:lead] = firsts[source][:lead].astype(F32)
            up_ref[lead:] = part[:left].astype(F32)
            at = pl.multiple_of(lax.bitwise_xor(index, info[3]) * quarter, 8)
            out_ref[pl.ds(at, 16), :] = part[left:high].astype(F32)
            spot = pl.ds(at, quarter)
            shift, gain = pair[spot, 0:1], pair[spot, 1:2]
            gain_sum, shift_sum = 0.0, 0.0
            blocks = part[2 * high :].astype(F32)
            for kind in range(3):
                block = blocks[kind * quarter : (kind + 1) * quarter]
                line = sums[kind : kind + 1]
                if kind == 0:
                    weight = wq[spot, :]
                    gq_ref[spot, :] = block + shift * line
                else:
                    lanes = slice((kind - 1) * width, kind * width)
                    weight = wkv[spot, lanes]
                    gkv_ref[spot, lanes] = block + shift * line
                gain_sum = gain_sum + jnp.sum(weight * block, axis=1, keepdims=True)
                shift_sum = shift_sum + jnp.sum(weight * line, axis=1, keepdims=True)
            lane = lax.broadcasted_iota(jnp.int32, (quarter, vec_ref.shape[1]), 1)
            vec_ref[spot, :] = jnp.where(lane == 0, gain_sum / gain, shift_sum)

    for place, source in enumerate(order_d):

        @pl.when(index == place)
        def lower(source=source):
            part = lasts[source]
            down_ref[:lead] = firsts[source][lead:].astype(F32)
            down_ref[lead:] = part[high : high + left].astype(F32)
            tail = part[high + left : 2 * high].astype(F32)
            at = pl.multiple_of(lax.bitwise_xor(index, info[4]) * quarter + 16, 8)
            out_ref[pl.ds(at, quarter - 16), :] = tail[: quarter - 16]

            @pl.when(lax.bitwise_xor(index, info[4]) == 0)
            def norms():
                norm_ref[...] = tail[quarter - 16 :]


def inward_kernel(info, *refs, groups, gots, fast):
    join_refs, hat_ref = refs[: 2 + gots], refs[2 + gots]
    parts = refs[3 + gots : 3 + gots + groups]
    outs = refs[3 + gots + groups :]
    join_kernel(*join_refs, *parts, groups=groups)
    heads, triple, rows = parts[0].shape
    hs = triple // 3
    total, sums = None, None
    ones = jnp.ones((16, rows), BF)
    for group in range(groups):
        order = [parts[group][h, k * hs : (k + 1) * hs] for k in range(3) for h in range(heads)]
        turned = jnp.concatenate(order, axis=0)
        found = nt(hat_ref[:, group * rows : (group + 1) * rows], turned)
        more = nt(ones, turned)
        total = found if total is None else total + found
        sums = more if sums is None else sums + more
    if not fast:
        outs[0][...] = total
        outs[1][...] = sums
        return
    own_ref, far_ref = outs
    block = total.shape[0] // (2 * groups)
    quarter = block // 4
    third = total.shape[1] // 3
    more = [sums[:8, kind * third : (kind + 1) * third] for kind in range(3)]
    more = jnp.concatenate(more, axis=0)
    for group in range(groups):
        spot = lax.rem(group + groups - info[0], groups)
        for part in range(4):
            place = lax.bitwise_xor(part, info[3])
            found = []
            for parity in range(2):
                at = (2 * group + parity) * block + part * quarter
                lines = jnp.concatenate([total[at : at + quarter], more], axis=1)
                lines = jnp.concatenate([lines, jnp.zeros_like(lines[:8])], axis=0)
                found.append(lines.astype(BF))
            own_ref[place, spot] = jnp.where(info[1] == 0, found[0], found[1])
            far_ref[place, spot] = jnp.where(info[1] == 0, found[1], found[0])


def final_kernel(info, *refs, groups):
    parts = refs[:groups]
    x_ref, dres_ref, gain_ref, w_ref, out_ref = refs[groups:]
    d_normed = jnp.zeros(dres_ref.shape, F32)
    for group in range(groups):
        owner = lax.rem(info[0] + groups - group, groups)
        heads, triple, rows = parts[group].shape
        d_normed = d_normed + tn(parts[group][...].reshape(heads * triple, rows), w_ref[owner])
    values = x_ref[...].astype(F32)
    centered = values - jnp.mean(values, axis=-1, keepdims=True)
    variance = jnp.mean(centered * centered, axis=-1, keepdims=True)
    inverse = lax.rsqrt(variance + EPSILON)
    hat = centered * inverse
    gy = d_normed * gain_ref[...]
    mean_one = jnp.mean(gy, axis=-1, keepdims=True)
    mean_two = jnp.mean(gy * hat, axis=-1, keepdims=True)
    out_ref[...] = (dres_ref[...] + inverse * (gy - mean_one - hat * mean_two)).astype(BF)


def ordered(kernel, inputs, later):
    def run(*refs):
        kernel(*refs[:inputs], *refs[inputs + later :])

    return run if later else kernel


def whole(shape):
    return pl.BlockSpec(shape, lambda *at: (0,) * len(shape))


def per_device(
    tokens,
    cluster_ids,
    lengths,
    top_keys,
    gain_one,
    shift_one,
    w_query,
    w_keyval,
    w_out,
    gain_two,
    shift_two,
    w_up,
    w_down,
    cotangent,
):
    rows, width = tokens.shape
    heads = cluster_ids.shape[1]
    hs = width // heads
    hidden = w_up.shape[1]
    wide = lax.axis_size("wide")
    n_dp = lax.axis_size("dp")
    groups = math.gcd(heads, wide)
    peers = wide // groups
    own_heads = heads // groups
    own_clusters = top_keys.shape[2]
    clusters = own_clusters * wide
    picks = top_keys.shape[3]
    seq = rows * wide
    size = 512 if seq <= 2048 else 2048
    feats = own_heads * hs
    block_rows = width // wide
    fast = peers == 2 and n_dp == 4 and block_rows == 96 and hidden == 4 * width and width % 256 == 0 and rows % 128 == 0
    me = lax.axis_index("wide")
    group_at, peer_at = me // peers, me % peers
    dp_at = lax.axis_index("dp")
    seq_len = lengths[0]
    bit_x, bit_y = dp_at % 2, (dp_at // 2) % 2
    place_u, place_d = 2 * bit_x + bit_y, 2 * bit_y + bit_x
    info = jnp.stack([group_at, peer_at, seq_len, place_u, place_d, me]).astype(jnp.int32)

    def along_groups(values, hop):
        pairs = [(i, ((i // peers + hop) % groups) * peers + i % peers) for i in range(wide)]
        return lax.ppermute(values, "wide", pairs)

    def along_peers(values, hop):
        pairs = [(i, (i // peers) * peers + (i % peers + hop) % peers) for i in range(wide)]
        return lax.ppermute(values, "wide", pairs)

    def along_dp(values, mask):
        return lax.ppermute(values, "dp", [(i, i ^ mask) for i in range(n_dp)])

    def prefetched(
        kernel, grid, in_specs, out_specs, out_shape, mib, spent, name, scratch=(), alias=None, first=()
    ):
        first = jax.tree.leaves(first)
        call = pl.pallas_call(
            ordered(kernel, 1 + len(in_specs), len(first)),
            grid_spec=pltpu.PrefetchScalarGridSpec(
                num_scalar_prefetch=1,
                grid=grid,
                in_specs=in_specs + [pl.BlockSpec(memory_space=pl.ANY)] * len(first),
                out_specs=out_specs,
                scratch_shapes=list(scratch),
            ),
            out_shape=out_shape,
            compiler_params=params(mib, len(grid)),
            cost_estimate=spent,
            input_output_aliases=alias or {},
            name=name,
        )
        return lambda *inputs: call(*inputs, *first)

    def after(values, *others):
        return lax.optimization_barrier((values, others))[0]

    def scalar(spec):
        return pl.BlockSpec(spec.block_shape, lambda *at: spec.index_map(*at[:-1]))

    def array(shape, dtype):
        return jax.ShapeDtypeStruct(shape, dtype)

    position = me * rows + jnp.arange(rows, dtype=jnp.int32)
    marked = jnp.where((position < seq_len)[:, None], cluster_ids, -1).T
    tops = top_keys[0].transpose(0, 2, 1)[:, :, None, :]
    mine_lanes = (jnp.arange(wide, dtype=jnp.int32) == me)[None, None, :, None]
    tops = jnp.where(mine_lanes, tops, 0).reshape(heads, picks, clusters)
    lines = rows // clusters
    marked = marked.reshape(heads, lines, clusters)
    fill = jnp.zeros((heads, -lines % 8, clusters), jnp.int32)
    packed = jnp.concatenate([tops, marked, fill], axis=1)
    near = [along_peers(tokens, -hop) for hop in range(1, peers)]
    packed = after(packed.reshape(groups, own_heads, -1, clusters), near)

    def of_heads(hop):
        return lax.dynamic_index_in_dim(packed, (group_at + groups - hop) % groups, keepdims=False)

    arrived = [of_heads(0)] + [along_groups(of_heads(hop), -hop) for hop in range(1, groups)]

    mine = {0: tokens, 1: along_groups(tokens, -1)}
    if groups > 2:
        mine[groups - 1] = along_groups(tokens, 1)
    ready = after(tokens, arrived)
    for hop in range(2, groups - 1):
        mine[hop] = along_groups(ready, -hop)

    w_in = jnp.concatenate([w_query, w_keyval], axis=1).T.reshape(3, heads, hs, width)
    w_in = w_in.transpose(1, 0, 2, 3).reshape(groups, 3 * feats, width)
    table_shape = (own_heads, picks + groups * lines, clusters)
    table = prefetched(
        functools.partial(table_kernel, picks=picks),
        (1,),
        [whole(packed.shape[1:])] * groups,
        whole(table_shape),
        array(table_shape, jnp.int32),
        8,
        cost(1e5, 1e6),
        "table",
    )(info, *arrived)
    tables = [table] + [along_peers(table, -hop) for hop in range(1, peers)]
    cot_got = [along_peers(after(cotangent, arrived), hop) for hop in range(1, peers)]
    cot_got = cot_got if fast else []
    bias, ids_all = prefetched(
        functools.partial(bias_kernel, groups=groups, peers=peers, rows=rows, picks=picks),
        (wide,),
        [whole(table_shape)] * peers,
        [
            pl.BlockSpec((own_heads, rows, clusters), lambda i, s: (0, i, 0)),
            whole((own_heads, 1, seq)),
        ],
        [array((own_heads, seq, clusters), BF), array((own_heads, 1, seq), jnp.int32)],
        12 if fast else 60,
        cost(own_heads * seq * clusters * picks * 8, own_heads * seq * clusters * 2),
        "bias",
    )(info, *tables)

    gain_row, shift_row = gain_one[None, :], shift_one[None, :]
    shapes = [
        array((width, groups * rows), BF),
        array((own_heads, 3 * hs, seq), BF),
        array((own_heads, seq, 2 * hs), BF),
    ]
    held = []
    split_peers = peers if peers <= 2 else 1
    for group in sorted(range(groups), key=lambda g: min(g, groups - g)):
        arrival = mine[group]
        first = ()
        if group == 1:
            arrival = after(arrival, bias, held, cot_got, [mine[hop] for hop in range(2, groups)])
        chunk = [arrival]
        chunk += near if group == 0 else [along_peers(arrival, -hop) for hop in range(1, peers)]
        if peers > 2:
            chunk = [jnp.concatenate(chunk, axis=0)]
        span = peers * rows
        if peers > 2:
            specs_in = [pl.BlockSpec((rows, width), lambda p, s: (p, 0))]
            grid = (peers,)
            outs = [
                pl.BlockSpec((width, rows), lambda p, s, g=group: (0, g)),
                pl.BlockSpec((own_heads, 3 * hs, rows), lambda p, s, g=group: (0, 0, g * peers + p)),
                pl.BlockSpec((own_heads, rows, 2 * hs), lambda p, s, g=group: (0, g * peers + p, 0)),
            ]
        else:
            specs_in = [whole((rows, width))] * split_peers
            grid = (1,)
            outs = [
                pl.BlockSpec((width, rows), lambda p, s, g=group: (0, g)),
                pl.BlockSpec((own_heads, 3 * hs, span), lambda p, s, g=group: (0, 0, g)),
                pl.BlockSpec((own_heads, span, 2 * hs), lambda p, s, g=group: (0, g, 0)),
            ]
        old = 1 + split_peers + 3
        held = prefetched(
            functools.partial(project_kernel, peers=split_peers, olds=len(held)),
            grid,
            specs_in
            + [
                whole((1, width)),
                whole((1, width)),
                pl.BlockSpec((1, 3 * feats, width), lambda p, s: (s[0], 0, 0)),
            ]
            + [pl.BlockSpec(memory_space=pl.ANY)] * len(held),
            outs,
            shapes,
            16 if fast else 60,
            cost(6 * span * width * feats, span * width * 4),
            "project",
            alias={old + k: k for k in range(len(held))},
            first=first,
        )(info, *chunk, gain_row, shift_row, w_in, *held)
    hat_own, feat, kv = held

    ids_full = pl.BlockSpec((1, 1, seq), lambda h, r: (h, 0, 0))
    feat_full = pl.BlockSpec((1, 3 * hs, seq), lambda h, r: (h, 0, 0))
    kv_full = pl.BlockSpec((1, seq, 2 * hs), lambda h, r: (h, 0, 0))
    bias_full = pl.BlockSpec((1, seq, clusters), lambda h, r: (h, 0, 0))
    head_rows = pl.BlockSpec((hs, rows), lambda h, r: (h, 0))
    mix_spec = pl.BlockSpec((1, 1, hs + 8, rows), lambda h, r: (h, r, 0, 0))
    stat_spec = pl.BlockSpec((1, hs + 8, clusters), lambda h, r: (h, 0, 0))
    cen_spec = pl.BlockSpec((1, hs, clusters), lambda h, r: (h, 0, 0))
    own_rows = groups * rows
    pair_flops = own_heads * own_rows * seq * 256

    one = [
        pl.BlockSpec(spec.block_shape, functools.partial(lambda h, f: f(h, 0), f=spec.index_map))
        for spec in (ids_full, feat_full, kv_full, bias_full, stat_spec, cen_spec, head_rows)
    ]
    ids_one, feat_one, kv_one, bias_one, stat_one, cen_one, rows_one = one
    part_one = pl.BlockSpec((1, hs + 16, clusters), lambda h: (h, 0, 0))
    mix_one = pl.BlockSpec((1, groups, hs + 8, rows), lambda h: (h, 0, 0, 0))
    all_groups = pl.BlockSpec((groups, hs, rows), lambda h: (0, h, 0))
    own_one = pl.BlockSpec((1, own_rows, 2 * hs), lambda h: (h, 0, 0))
    results = pl.pallas_call(
        functools.partial(forward_kernel, size=size, groups=groups, rows=rows),
        grid=(own_heads,),
        in_specs=[ids_one, feat_one, kv_one, bias_one],
        out_specs=[rows_one] * groups + [mix_one, stat_one, cen_one],
        out_shape=[array((feats, rows), BF)] * groups
        + [
            array((own_heads, groups, hs + 8, rows), F32),
            array((own_heads, hs + 8, clusters), F32),
            array((own_heads, hs, clusters), BF),
        ],
        compiler_params=params(16 if fast else 60, 1),
        cost_estimate=cost(6 * pair_flops, 8e6, own_heads * own_rows * seq),
        name="attend",
    )(ids_all, feat, kv, bias)
    attn_t = results[:groups]
    mixed, stats, centroid = results[groups:]

    arrived = [attn_t[0]] + [along_groups(attn_t[hop], hop) for hop in range(1, groups)]

    chunks = 4
    part = hidden // chunks
    early, lead = 64, 80
    w_out_g = w_out.reshape(groups, feats, width)
    gain_row2, shift_row2 = gain_two[None, :], shift_two[None, :]
    square = whole((rows, width))
    column = pl.BlockSpec((rows, part), lambda i, s: (0, i))
    norm_spec = whole((8, width))
    if fast:
        kept_shapes = [
            array((rows, hidden + hidden // 2 + width), BF),
            array((width + 16, rows), BF),
            array((rows, hidden // 2), BF),
            array((width + 16, rows), BF),
        ]
        kept_specs = [whole(item.shape) for item in kept_shapes]
        kept_specs[2] = pl.BlockSpec((rows, part // 2), lambda i, s: (0, i))
    else:
        kept_shapes = [
            array((8, width), F32),
            array((rows, hidden), BF),
            array((rows, width), BF),
            array((rows, hidden), BF),
            array((rows, width), BF),
        ]
        kept_specs = [norm_spec, column, square, column, square]
    results = prefetched(
        functools.partial(block_kernel, groups=groups, chunks=chunks, fast=fast),
        (chunks,),
        [whole((feats, rows))] * groups
        + [
            square,
            whole((1, width)),
            whole((1, width)),
            whole((groups, feats, width)),
            pl.BlockSpec((width, part), lambda i, s: (0, i)),
            pl.BlockSpec((part, width), lambda i, s: (i, 0)),
            square,
        ],
        [square, square] + kept_specs + [whole((feats, rows))] * groups,
        [array((rows, width), BF), array((rows, width), F32)]
        + kept_shapes
        + [array((feats, rows), BF)] * groups,
        28 if fast else 60,
        cost(8 * rows * width * hidden, 4 * width * hidden, rows * hidden),
        "feed",
        scratch=[
            pltpu.VMEM((rows, width), F32),
            pltpu.VMEM((rows, 128), F32),
            pltpu.VMEM((rows, width), BF),
            pltpu.VMEM((rows, width), F32),
            pltpu.VMEM((rows, width), F32),
        ],
    )(info, *arrived, tokens, gain_row2, shift_row2, w_out_g, w_up, w_down, cotangent)
    output, d_resid = results[:2]
    kept, d_attn = results[2:-groups], results[-groups:]
    grads = [d_attn[0]] + [along_groups(d_attn[hop], -hop) for hop in range(1, groups)]

    def weight_parts():
        far, low_far, act_own, low_own = kept
        got, low_got = along_peers(far, 1), along_peers(low_far, 1)
        high = block_rows + 16
        chunk = pl.BlockSpec((rows, part), lambda i, s: (0, i ^ 2 ^ s[3]))
        branch = pl.BlockSpec((rows, width), lambda i, s: (0, hidden * 3 // 2 // width))
        act_spec = pl.BlockSpec((rows, part // 2), lambda i, s: (0, i))
        act_there = pl.BlockSpec((rows, part // 2), lambda i, s: (0, 2 * hidden // part + i))
        low_spec = whole((width + 16, rows))
        shape_u = (2, groups, high, width)
        shape_d = (2, groups, high, width)
        parts = [(1, groups, tall, width) for tall in (early + high, high - early)]
        results = prefetched(
            functools.partial(weights_kernel, groups=groups),
            (4,),
            [chunk, chunk, branch, branch, act_spec, act_there, low_spec, low_spec, square, square],
            [whole(item) for item in parts]
            + [pl.BlockSpec((1,) + shape_u[1:], lambda i, s: (jnp.maximum(i - 2, 0), 0, 0, 0))]
            + [whole(item) for item in parts]
            + [whole(shape_d)],
            ([array(item, BF) for item in parts] + [array(shape_u, BF)]) * 2,
            28,
            cost(8 * rows * width * hidden, 6 * width * hidden),
            "weights",
            scratch=[pltpu.VMEM((groups, block_rows, width), F32)],
        )(info, far, got, far, got, act_own, got, low_own, low_got, cotangent, *cot_got)
        return results[:2], results[2], results[3:5], results[5]

    def weight_second(keep_u, got_u, keep_d, got_d, inner, inner_got, late_u, late_d):
        def block(shape, at):
            return pl.BlockSpec((1,) + shape[1:], lambda i: (at, 0, 0, 0))

        high, lines = keep_u.shape[2], inner.shape[2]
        shapes = [(groups, high + lines + late_u.shape[2], width)] * 2 + [(groups, lines, width)]
        return pl.pallas_call(
            second_kernel,
            grid=(1,),
            in_specs=[
                block(item.shape, item.shape[0] - 1) for item in (keep_u, got_u, keep_d, got_d)
            ]
            + [whole(item.shape) for item in (inner, inner_got, late_u, late_d)],
            out_specs=[whole(shape) for shape in shapes],
            out_shape=[array(shape, BF) for shape in shapes],
            compiler_params=params(24, 1),
            cost_estimate=cost(groups * high * width * 2, groups * high * width * 12),
            name="second",
        )(keep_u, got_u, keep_d, got_d, inner, inner_got, late_u, late_d)

    def weight_third(keep_u, got_u, keep_d, got_d, by_y, by_x, inner, inner_got, by_xy):
        def block(shape, at):
            return pl.BlockSpec((1,) + shape[1:], lambda i, s: (at, 0, 0, 0))

        left = keep_u.shape[2] - lead
        talls = [(2 * lead, width)] * groups + [(2 * left + inner.shape[2], width)] * groups
        more = (by_y, by_x)
        return prefetched(
            third_kernel,
            (1,),
            [block(item.shape, 0) for item in (keep_u, got_u, keep_d, got_d)]
            + [whole(by_y.shape), whole(by_x.shape)]
            + [block(inner.shape, 0)] * 2
            + [whole(by_xy.shape)],
            [whole(tall) for tall in talls],
            [array(tall, BF) for tall in talls],
            24,
            cost(groups * 256 * width * 4, groups * 256 * width * 8),
            "third",
            first=home,
        )(info, keep_u, got_u, keep_d, got_d, by_y, by_x, inner, inner_got, by_xy)

    def weight_fourth(came, high, lines, first):
        tall = 2 * high + (3 * (block_rows // 4) + 8 if lines else 0)
        done = prefetched(
            functools.partial(fourth_kernel, groups=groups, high=high, feats=3 * feats),
            (1,),
            [whole(came[0].shape)] * groups,
            whole((tall, width)),
            array((tall, width), BF),
            16,
            cost(groups * tall * width, groups * tall * width * 2),
            "fourth",
            scratch=[pltpu.VMEM((groups, lines, width), F32)] if lines else [],
            first=first,
        )(info, *came)
        return [done] + [along_dp(done, mask) for mask in (1, 2, 3)]

    def weight_spread(firsts, lasts, high, ready):
        at = me * block_rows
        wq_rows = lax.dynamic_slice_in_dim(w_query, at, block_rows).astype(F32)
        wkv_rows = lax.dynamic_slice_in_dim(w_keyval, at, block_rows).astype(F32)
        pair = jnp.stack([shift_one, gain_one] + [shift_one] * 6, axis=1)
        pair = lax.dynamic_slice_in_dim(pair, at, block_rows)
        return prefetched(
            functools.partial(spread_kernel, lead=lead, high=high),
            (4,),
            [whole(item.shape) for item in firsts + lasts]
            + [whole(wq_rows.shape), whole(wkv_rows.shape), whole(pair.shape)],
            [
                pl.BlockSpec((block_rows, part), lambda i, s: (0, i ^ s[3])),
                whole((block_rows, width)),
                pl.BlockSpec((block_rows, width), lambda i, s: (i ^ s[4], 0)),
                whole((8, width)),
                whole((block_rows, width)),
                whole((block_rows, 2 * width)),
                whole((block_rows, 128)),
            ],
            [
                array((block_rows, hidden), F32),
                array((block_rows, width), F32),
                array((hidden // wide, width), F32),
                array((8, width), F32),
                array((block_rows, width), F32),
                array((block_rows, 2 * width), F32),
                array((block_rows, 128), F32),
            ],
            20,
            cost(1e6, 8 * block_rows * width * 6),
            "spread",
            scratch=[pltpu.VMEM((8, width), F32)],
        )(info, *firsts, *lasts, wq_rows, wkv_rows, pair)

    masks = [1 << k for k in range(n_dp.bit_length() - 1)]

    def reduce_rows(partial):
        blocks = partial.reshape(groups, peers, partial.shape[0] // wide, partial.shape[1])

        def of_peer(hop):
            at = (peer_at + hop) % peers
            return lax.dynamic_index_in_dim(blocks, at, axis=1, keepdims=False)

        total = of_peer(0).astype(F32)
        for hop in range(1, peers):
            total = total + along_peers(of_peer(hop), hop).astype(F32)
        total = total.astype(BF)

        def of_group(hop):
            return lax.dynamic_index_in_dim(total, (group_at + hop) % groups, keepdims=False)

        done = of_group(0).astype(F32)
        for hop in range(1, groups):
            done = done + along_groups(of_group(hop), hop).astype(F32)
        for mask in masks:
            done = done.astype(BF)
            done = done.astype(F32) + along_dp(done, mask).astype(F32)
        return done

    if fast:
        send_u, keep_u, send_d, keep_d = weight_parts()
        got_u, got_d = along_dp(send_u[0], 1), along_dp(send_d[0], 2)
    else:
        norm_two, d_up, d_branch, act, normed_two = kept
        total_up = reduce_rows(tn(normed_two, d_up).astype(BF))
        total_down = reduce_rows(tn(act, cotangent).astype(BF))
        found = jnp.stack([nn(item, d_branch).astype(BF) for item in arrived])
        found = [
            lax.dynamic_index_in_dim(found, (group_at + groups - g) % groups, keepdims=False)
            for g in range(groups)
        ]
        total_out = reduce_rows(jnp.concatenate(found, axis=0))
        norm_own = reduce_rows(norm_two[:2].T.astype(BF)).T

    share = prefetched(
        functools.partial(sums_kernel, groups=groups),
        (own_heads,),
        [scalar(spec) for spec in (ids_one, *[rows_one] * groups, mix_one)],
        scalar(part_one),
        array((own_heads, hs + 16, clusters), F32),
        16 if fast else 60,
        cost(own_heads * own_rows * clusters * 160, 2e6),
        "sums",
        first=(keep_u, keep_d) if fast else (),
    )(info, ids_all, *grads, mixed)
    share_got = [along_peers(share, hop) for hop in range(1, peers)]

    back_shapes = [
        array((groups, feats, rows), BF),
        array((own_heads, 2 * hs, own_rows), F32),
        array((own_heads, 2 * hs, max(peers - 1, 1) * own_rows), BF),
    ]
    dq, dkv_own, dkv_send = pl.pallas_call(
        functools.partial(back_kernel, size=size, groups=groups, gots=len(share_got)),
        grid=(own_heads,),
        in_specs=[ids_one, feat_one, kv_one, bias_one]
        + [rows_one] * groups
        + [mix_one, stat_one, cen_one]
        + [part_one] * (1 + len(share_got)),
        out_specs=[
            all_groups,
            pl.BlockSpec((1,) + back_shapes[1].shape[1:], lambda h: (h, 0, 0)),
            pl.BlockSpec((1,) + back_shapes[2].shape[1:], lambda h: (h, 0, 0)),
        ],
        out_shape=back_shapes,
        scratch_shapes=[pltpu.VMEM((seq, 2 * hs), F32), pltpu.VMEM((seq, 2 * clusters), BF)],
        compiler_params=params(24 if fast else 62, 1),
        cost_estimate=cost(14 * pair_flops, 10e6, own_heads * own_rows * seq),
        name="back",
    )(ids_all, feat, kv, bias, *grads, mixed, stats, centroid, share, *share_got)
    if fast:
        dkv_send = after(dkv_send, got_u, got_d)
    dkv_got = [
        along_peers(
            dkv_send if peers == 2 else dkv_send[..., (hop - 1) * own_rows : hop * own_rows], hop
        )
        for hop in range(1, peers)
    ]
    tall = block_rows + 16
    spent = cost(2 * own_rows * width * 3 * feats, 4e6)
    if fast:
        lines = block_rows // 4 + 8
        more = [array((4, groups, lines, width), BF)] * 2
    else:
        more = [array((width, 3 * feats), F32), array((16, 3 * feats), F32)]
    results = prefetched(
        functools.partial(inward_kernel, groups=groups, gots=len(dkv_got), fast=fast),
        (1,),
        [whole(back_shapes[0].shape)]
        + [whole(back_shapes[1].shape)] * (1 + len(dkv_got))
        + [whole((width, own_rows))],
        [whole((own_heads, 3 * hs, rows))] * groups + [whole(item.shape) for item in more],
        [array((own_heads, 3 * hs, rows), BF)] * groups + more,
        28 if fast else 60,
        spent,
        "inward",
    )(info, dq, dkv_own, *dkv_got, hat_own)
    d_in, more = results[:groups], results[groups:]
    home = [d_in[0]] + [along_groups(d_in[hop], hop) for hop in range(1, groups)]

    grad_tokens = prefetched(
        functools.partial(final_kernel, groups=groups),
        (1,),
        [whole((own_heads, 3 * hs, rows))] * groups
        + [square, square, whole((1, width)), whole((groups, 3 * feats, width))],
        square,
        array((rows, width), BF),
        24 if fast else 60,
        cost(6 * rows * width * width, 6 * width * width),
        "final",
    )(info, *home, tokens, d_resid, gain_row, w_in)

    if fast:
        keep, far = more
        inner_got = along_peers(far, 1)
        to_y, to_x, to_xy = weight_second(
            keep_u, got_u, keep_d, got_d, keep, inner_got, send_u[1], send_d[1]
        )
        by_y, by_x, by_xy = along_dp(to_y, 2), along_dp(to_x, 1), along_dp(to_xy, 3)
        sums = weight_third(
            keep_u, got_u, keep_d, got_d, by_y, by_x, keep, inner_got, by_xy
        )
        came_a, came_b = [sums[0]], [sums[groups]]
        came_a += [along_groups(sums[hop], hop) for hop in range(1, groups)]
        late = after(sums[groups + 1 :], came_a[groups - 1])
        came_b += [along_groups(late[hop - 1], hop) for hop in range(1, groups)]
        spread_a = weight_fourth(came_a, lead, 0, (came_b[1], grad_tokens))
        high = keep_u.shape[2] - lead
        spread_b = weight_fourth(came_b, high, lines, spread_a)
        found = weight_spread(spread_a, spread_b, high, came_a[0])
        total_up, total_out, total_down, norms, total_query, total_keyval, vector = found
        norm_own = lax.dynamic_slice_in_dim(norms, me * block_rows, block_rows, axis=1)
        gain_grad, shift_grad = vector[:, 0], vector[:, 1]
    else:
        found, more = more
        found = found.reshape(groups, peers, block_rows, 3 * feats)
        more = jnp.broadcast_to(more, (groups, peers, 16, 3 * feats))
        found = jnp.concatenate([found, more], axis=2).astype(BF)

        def of_peer(hop):
            at = (peer_at + hop) % peers
            return lax.dynamic_index_in_dim(found, at, axis=1, keepdims=False)

        total = of_peer(0).astype(F32)
        for hop in range(1, peers):
            total = total + along_peers(of_peer(hop), hop).astype(F32)
        for mask in masks:
            total = total.astype(BF)
            total = total.astype(F32) + along_dp(total, mask).astype(F32)
        total = total.astype(BF)
        items = [
            lax.dynamic_index_in_dim(total, (group_at + hop) % groups, keepdims=False)
            for hop in range(groups)
        ]
        pieces = [items[0]] + [along_groups(items[hop], hop) for hop in range(1, groups)]
        pieces = jnp.stack(pieces)
        pieces = jnp.stack(
            [
                lax.dynamic_index_in_dim(pieces, (group_at + groups - g) % groups, keepdims=False)
                for g in range(groups)
            ]
        ).astype(F32)
        q_part = pieces[:, :, :feats].transpose(1, 0, 2).reshape(tall, width)
        kv_part = (
            pieces[:, :, feats:]
            .reshape(groups, tall, 2, feats)
            .transpose(1, 2, 0, 3)
            .reshape(tall, 2 * width)
        )
        at = me * block_rows
        wq_rows = lax.dynamic_slice_in_dim(w_query, at, block_rows).astype(F32)
        wkv_rows = lax.dynamic_slice_in_dim(w_keyval, at, block_rows).astype(F32)
        gain_own = lax.dynamic_slice_in_dim(gain_one, at, block_rows)
        shift_own = lax.dynamic_slice_in_dim(shift_one, at, block_rows)
        q_sum, kv_sum = q_part[block_rows], kv_part[block_rows]
        q_part, kv_part = q_part[:block_rows], kv_part[:block_rows]
        shift_grad = jnp.sum(wq_rows * q_sum, axis=1) + jnp.sum(wkv_rows * kv_sum, axis=1)
        along = jnp.sum(wq_rows * q_part, axis=1) + jnp.sum(wkv_rows * kv_part, axis=1)
        total_query = q_part + shift_own[:, None] * q_sum
        total_keyval = kv_part + shift_own[:, None] * kv_sum
        gain_grad = along / gain_own


    return (
        output,
        grad_tokens,
        total_query,
        total_keyval,
        total_out,
        total_up,
        total_down,
        gain_grad,
        shift_grad,
        norm_own[0],
        norm_own[1],
    )


def solution(mesh):
    return jax.shard_map(
        per_device,
        mesh=mesh,
        in_specs=(
            P(("dp", "wide"), None),
            P(("dp", "wide"), None),
            P("dp"),
            P("dp", None, "wide", None),
            P(),
            P(),
            P(),
            P(),
            P(),
            P(),
            P(),
            P(),
            P(),
            P(("dp", "wide"), None),
        ),
        out_specs=(
            P(("dp", "wide"), None),
            P(("dp", "wide"), None),
            P("wide", None),
            P("wide", None),
            P("wide", None),
            P("wide", None),
            P("wide", None),
            P("wide"),
            P("wide"),
            P("wide"),
            P("wide"),
        ),
        check_vma=False,
    )
```
